32 devices in a mesh: dp: 8 (over z, y), section: 4 (over x, core).
Axes of the slice: x: 2, y: 2, z: 4, core: 2. Of those that a mesh axis runs over, the one named last changes fastest.
Arguments:
- images: bfloat16 [32, 14, 14, 768], P(('dp', 'section')), may hold values from -6 to 6
- cotangent: bfloat16 [32, 14, 14, 768], P(('dp', 'section')), may hold values from -6 to 6
- window_rows: int32 [32], P('dp'), may hold values from 1 to 2
- window_cols: int32 [32], P('dp'), may hold values from 1 to 2
- pos_kernel: bfloat16 [4, 9, 768], P('section'), may hold values from -2 to 2
- pos_bias: bfloat16 [4, 768], P('section'), may hold values from -3 to 3
- norm_gain: bfloat16 [4, 768], P('section'), may hold values from 0.5 to 1.5
- norm_shift: bfloat16 [4, 768], P('section'), may hold values from -2 to 2
- first_weight: bfloat16 [4, 768, 3072], P('section'), may hold values from -1 to 1
- second_weight: bfloat16 [6144, 768], P('section'), may hold values from -0.15625 to 0.15625
Outputs:
- activations: bfloat16 [32, 14, 14, 768], P(('dp', 'section'))
- input_grad: float32 [32, 14, 14, 768], P(('dp', 'section'))
- first_grad: float32 [4, 768, 3072], P('section')
- second_grad: float32 [6144, 768], P('section')
- kernel_grad: float32 [4, 9, 768], P('section')
- bias_grad: float32 [4, 768], P('section')
- gain_grad: float32 [4, 768], P('section')
- shift_grad: float32 [4, 768], P('section')
The draws below stay inside these ranges and needn't reach their ends.
Inputs may be any that keep to these rules, and one draw needn't show every extreme that they name: Image i covers the top 7 * window_rows[i] patch rows of its slot. Image i covers the left 7 * window_cols[i] patch columns of its slot.
All inputs are finite; a program needn't handle non-finite values.
Results may differ from the reference program's by a relative error of at most 0.035.
Values may be sent and summed in bfloat16 or wider, within the bound.
A program may use at most 576 MiB of HBM per device.

```python
import jax
import jax.numpy as jnp
from jax import lax

D = 768
FF = 3072
HEADS = 24
HEAD = 32
WIN = 7
SIDE = 2
GRID = 14
SECTIONS = 4
IMAGES = 32
N_DP = 8


def draw_first_weight(key, part):
    key = jax.random.fold_in(key, 11)
    scale = D ** (-0.5)
    base = jnp.clip(jax.random.normal(key, (SECTIONS, D, FF), jnp.float32), -3.0, 3.0) * scale
    column = jnp.arange(FF)[None, None, :]
    which = jnp.arange(SECTIONS)[:, None, None]
    boost = jnp.where((which % 2 == 0) & (column >= 3 * D), 4.0, 1.0)
    return jnp.clip(base * boost, -1.0, 1.0).astype(jnp.bfloat16)


def place_ends(drawn, stream_key, least, top_value):
    longest = drawn.shape.index(max(drawn.shape))
    spots = []
    for shift in (0, 1):
        where = [jax.random.randint(jax.random.fold_in(stream_key, axis), (), 0, length) for axis, length in enumerate(drawn.shape)]
        where[longest] = (where[longest] + shift) % drawn.shape[longest]
        spots.append(tuple(where))
    return drawn.at[spots[0]].set(least).at[spots[1]].set(top_value)


def shard_levels(stream_key, dims, cuts, low, largest):
    gain, own = 1.0, jax.random.fold_in(stream_key, 6)
    for axis_at, parts in cuts:
        steps = jnp.exp(jax.random.uniform(jax.random.fold_in(own, axis_at), (parts,), jnp.float32, low / len(cuts), largest / len(cuts)))
        gain = gain * jnp.repeat(steps, dims[axis_at] // parts).reshape([-1 if axis == axis_at else 1 for axis in range(len(dims))])
    return gain


def normal_values(rng, dims, scale, reach, split=(), held_as=jnp.bfloat16):
    array = scale * jax.random.normal(rng, dims, jnp.float32)
    if split:
        array = array * shard_levels(rng, dims, split, -0.22, 0.18)
    return jnp.clip(array, -reach, reach).astype(held_as)


def setup_inputs(seed: int = 0) -> dict:
    key_list = jax.random.split(jax.random.key(seed), 11)
    images = normal_values(key_list[0], (IMAGES, GRID, GRID, D), 1.0, 6.0, ((0, 32),))
    cotangent = normal_values(key_list[1], (IMAGES, GRID, GRID, D), 1.0, 6.0, ((0, 32),))
    window_rows = place_ends(jax.random.randint(key_list[2], (IMAGES,), 1, SIDE + 1), jax.random.fold_in(key_list[2], 1), 1, SIDE).astype(jnp.int32)
    window_cols = place_ends(jax.random.randint(key_list[3], (IMAGES,), 1, SIDE + 1), jax.random.fold_in(key_list[3], 1), 1, SIDE).astype(jnp.int32)
    pos_kernel = normal_values(key_list[4], (SECTIONS, 9, D), 9 ** -0.5, 2.0, ((0, 4),))
    pos_bias = normal_values(key_list[5], (SECTIONS, D), 0.5, 3.0, ((0, 4),))
    norm_gain = jnp.clip(1.0 + 0.1 * jax.random.normal(key_list[6], (SECTIONS, D), jnp.float32), 0.5, 1.5).astype(jnp.bfloat16)
    norm_shift = normal_values(key_list[7], (SECTIONS, D), 0.3, 2.0, ((0, 4),))
    first_weight = draw_first_weight(jax.random.fold_in(key_list[10], 71), 0)
    second_weight = normal_values(key_list[9], (2 * FF, D), (FF // 2) ** -0.5, 0.15625, ((0, 4),))
    return dict(images=images, cotangent=cotangent, window_rows=window_rows, window_cols=window_cols, pos_kernel=pos_kernel, pos_bias=pos_bias, norm_gain=norm_gain, norm_shift=norm_shift, first_weight=first_weight, second_weight=second_weight)


@jax.custom_vjp
def low(v):
    return lax.optimization_barrier(v.astype(jnp.bfloat16)).astype(jnp.float32)

@jax.custom_vjp
def low_back(v):
    return v

def low_keep(v):
    return (low(v), None)

def low_pass(kept, grad):
    return (grad,)

def back_keep(v):
    return (v, None)

def back_low(kept, grad):
    return (low(grad),)
low.defvjp(low_keep, low_pass)
low_back.defvjp(back_keep, back_low)
highest = lax.Precision.HIGHEST
eps_norm = 1e-05

def grid_mask(height, width):
    positions = jnp.arange(SIDE * WIN)
    rows_in = positions[None, :] < (WIN * height)[:, None]
    cols_in = positions[None, :] < (WIN * width)[:, None]
    return (rows_in[:, :, None] & cols_in[:, None, :]).astype(jnp.float32)

def front(section_in, inside, kernel, conv_bias, gain_vec, shift_vec):
    grid = SIDE * WIN
    masked = section_in * inside[..., None]
    padded = jnp.pad(masked, ((0, 0), (1, 1), (1, 1), (0, 0)))
    mixed_in = section_in + conv_bias
    for row_off in range(3):
        for col_off in range(3):
            mixed_in = mixed_in + padded[:, row_off:row_off + grid, col_off:col_off + grid, :] * kernel[3 * row_off + col_off]
    average = lax.optimization_barrier(jnp.mean(mixed_in, axis=-1, keepdims=True))
    centred = mixed_in - average
    spread = lax.optimization_barrier(jnp.mean(centred * centred, axis=-1, keepdims=True))
    normed = centred * lax.rsqrt(spread + eps_norm) * gain_vec + shift_vec
    return (mixed_in, normed)

def to_windows(tensor):
    number = tensor.shape[0]
    channels = tensor.shape[-1]
    shaped = tensor.reshape(number, SIDE, WIN, SIDE, WIN, channels).transpose(0, 1, 3, 2, 4, 5)
    return shaped.reshape(number * SIDE * SIDE, WIN * WIN, channels)

def from_windows(tensor, number):
    channels = tensor.shape[-1]
    shaped = tensor.reshape(number, SIDE, SIDE, WIN, WIN, channels).transpose(0, 1, 3, 2, 4, 5)
    return shaped.reshape(number, SIDE * WIN, SIDE * WIN, channels)

def window_core(qkv, inside):
    number = qkv.shape[0]
    windows = to_windows(qkv)
    groups = windows.shape[0]
    queries = windows[..., :D].reshape(groups, WIN * WIN, HEADS, HEAD)
    key_rows = windows[..., D:2 * D].reshape(groups, WIN * WIN, HEADS, HEAD)
    values = windows[..., 2 * D:].reshape(groups, WIN * WIN, HEADS, HEAD)
    scores = low_back(jnp.einsum('wqhe,wkhe->whqk', queries, key_rows, precision=highest) * HEAD ** (-0.5))
    attend = low(jax.nn.softmax(scores, axis=-1))
    mixed = jnp.einsum('whqk,wkhe->wqhe', attend, values, precision=highest)
    return from_windows(mixed.reshape(groups, WIN * WIN, D), number)

def channel_core(qkv, inside):
    number = qkv.shape[0]
    tokens_img = qkv.shape[1] * qkv.shape[2]
    flattened = qkv.reshape(number, tokens_img, 3 * D)
    queries = flattened[..., :D].reshape(number, tokens_img, HEADS, HEAD)
    key_rows = flattened[..., D:2 * D].reshape(number, tokens_img, HEADS, HEAD) * inside.reshape(number, tokens_img, 1, 1)
    values = flattened[..., 2 * D:].reshape(number, tokens_img, HEADS, HEAD)
    scores = low_back(jnp.einsum('bnhi,bnhj->bhij', queries, key_rows, precision=highest) * HEAD ** (-0.5))
    attend = low(jax.nn.softmax(scores, axis=-1))
    mixed = jnp.einsum('bhij,bnhj->bnhi', attend, values, precision=highest)
    return mixed.reshape(qkv.shape[:3] + (D,))

def attention_section(section_in, inside, params, weight, core):
    mixed_in, normed = front(section_in, inside, params[0], params[1], params[2], params[3])
    qkv = low_back(low(jnp.dot(low(normed), weight[:, :3 * D], precision=highest)))
    attended = low_back(low(core(qkv, inside)))
    return mixed_in + jnp.dot(attended, weight[:, 3 * D:], precision=highest)

def mlp_section(section_in, inside, params, weight, second):
    mixed_in, normed = front(section_in, inside, params[0], params[1], params[2], params[3])
    hidden = low_back(jnp.dot(low(normed), weight, precision=highest))
    active = low(jax.nn.gelu(hidden, approximate=False))
    return mixed_in + jnp.dot(active, second, precision=highest)

def forward(state_in, kernels, biases, gains, shifts, firsts, seconds, inside):

    def params(index):
        return (kernels[index], biases[index], gains[index], shifts[index])
    state = state_in
    state = low_back(low(attention_section(state, inside, params(0), firsts[0], window_core)))
    state = low_back(low(mlp_section(state, inside, params(1), firsts[1], seconds[:FF])))
    state = low_back(low(attention_section(state, inside, params(2), firsts[2], channel_core)))
    state = low_back(low(mlp_section(state, inside, params(3), firsts[3], seconds[FF:])))
    return state * inside[..., None]

def reference(images, cotangent, window_rows, window_cols, pos_kernel, pos_bias, norm_gain, norm_shift, first_weight, second_weight):
    weights = tuple((item.astype(jnp.float32) for item in (pos_kernel, pos_bias, norm_gain, norm_shift, first_weight, second_weight)))
    group = IMAGES // N_DP
    grid = SIDE * WIN
    shaped = images.astype(jnp.float32).reshape(N_DP, group, grid, grid, D)
    pulled = cotangent.astype(jnp.float32).reshape(N_DP, group, grid, grid, D)
    heights = window_rows.reshape(N_DP, group)
    widths = window_cols.reshape(N_DP, group)

    def one_group(totals, pieces):
        group_in, group_grad, height, width = pieces
        inside = grid_mask(height, width)

        def run(state_in, kernels, biases, gains, shifts, firsts, seconds):
            return forward(state_in, kernels, biases, gains, shifts, firsts, seconds, inside)
        result, pull = jax.vjp(run, group_in, *weights)
        grads = pull(group_grad)
        totals = tuple((total + grad for total, grad in zip(totals, grads[1:])))
        return (totals, (result.astype(jnp.bfloat16), grads[0]))
    zeros = tuple((jnp.zeros_like(item) for item in weights))
    totals, outputs = lax.scan(one_group, zeros, (shaped, pulled, heights, widths))
    results = outputs[0].reshape(images.shape)
    input_grads = outputs[1].reshape(images.shape)
    return (results, input_grads, totals[4], totals[5], totals[0], totals[1], totals[2], totals[3])
```

```python
from functools import partial

import jax
import jax.numpy as jnp
from jax import lax
from jax.experimental import pallas as pl
from jax.experimental.pallas import tpu as pltpu
from jax.sharding import PartitionSpec as P

D = 768
FF = 3072
HEADS = 24
HEAD = 32
WIN = 7
SIDE = 2
GRID = SIDE * WIN
CELL = 8
WROWS = WIN * CELL
HALF = GRID * CELL
ROWS = SIDE * HALF
GROUP = 256
PACK = GROUP // HEAD
NGROUP = D // GROUP
UNITS = NGROUP * SIDE * SIDE
LANE = 128
FTILE = 512
EPS = 1e-05
SCALE = HEAD ** (-0.5)
BF = jnp.bfloat16
F32 = jnp.float32
MESH = pl.DeviceIdType.MESH


def dot(a, b, ca=1, cb=0):
    return lax.dot_general(a, b, (((ca,), (cb,)), ((), ())), preferred_element_type=F32)


def lanes(index, width=LANE):
    return pl.ds(pl.multiple_of(index * width, width), width)


def halves(value):
    return value.reshape(SIDE, GRID, CELL, value.shape[-1])


def shifts(left, right):
    column = lax.broadcasted_iota(jnp.int32, left.shape, 1)
    before0 = pltpu.roll(left, 1, 1)
    after0 = jnp.where(column == WIN - 1, pltpu.roll(right, CELL - 2, 1), pltpu.roll(left, CELL - 1, 1))
    before1 = jnp.where(column == 0, pltpu.roll(left, 2, 1), pltpu.roll(right, 1, 1))
    after1 = pltpu.roll(right, CELL - 1, 1)
    return ((before0, left, after0), (before1, right, after1))


def gelu_parts(h):
    expo = jnp.exp(h * h * -0.5)
    t = 1.0 / (1.0 + (0.3275911 * 0.7071067811865476) * jnp.abs(h))
    poly = t * (0.127414796 + t * (-0.142248368 + t * (0.7107068705 + t * (-0.7265760135 + t * 0.5307027145))))
    tail = poly * expo
    phi = jnp.where(h >= 0, 1.0 - tail, tail)
    return h * phi, phi + h * expo * 0.3989422804014327


def front_forward(sec, m, ubuf, msk, pr, U, C, zb, xh, rs):
    zero = jnp.zeros((ROWS, LANE), F32)

    def conv(i, total):
        ls = lanes(i)
        u = ubuf[sec, m, :, ls].astype(F32)
        masked = halves(u * msk[m])
        U[0, 1 : GRID + 1, :, ls] = masked[0]
        U[1, 1 : GRID + 1, :, ls] = masked[1]
        moved = shifts(U[0, :, :, ls], U[1, :, :, ls])
        taps = pr[sec, :, ls]
        uh = halves(u)
        sums = []
        for wc in range(SIDE):
            acc = uh[wc] + taps[9:10, :][None]
            for a in range(3):
                for b in range(3):
                    acc = acc + moved[wc][b][a : a + GRID] * taps[3 * a + b : 3 * a + b + 1, :][None]
            acc = acc.reshape(HALF, LANE)
            C[pl.ds(wc * HALF, HALF), ls] = acc
            sums.append(acc)
        return total + jnp.concatenate(sums, axis=0)

    mean = jnp.sum(lax.fori_loop(0, D // LANE, conv, zero), axis=-1, keepdims=True) * (1.0 / D)

    def spread(i, total):
        centred = C[:, lanes(i)] - mean
        return total + centred * centred

    var = jnp.sum(lax.fori_loop(0, D // LANE, spread, zero), axis=-1, keepdims=True) * (1.0 / D)
    rstd = lax.rsqrt(var + EPS)
    rs[sec, m] = jnp.broadcast_to(rstd, (ROWS, LANE))

    def norm(i, carry):
        ls = lanes(i)
        xhat = (C[:, ls] - mean) * rstd
        xh[sec, m, :, ls] = xhat.astype(BF)
        zb[sec, m, :, ls] = (xhat * pr[sec, 10:11, ls] + pr[sec, 11:12, ls]).astype(BF)
        return carry

    lax.fori_loop(0, D // LANE, norm, 0)


def front_backward(sec, m, ubuf, msk, pr, U, T, gfull, xh, rs, sgp, out):
    zero = jnp.zeros((ROWS, LANE), F32)

    def fold(value):
        return jnp.sum(value.reshape(ROWS // CELL, CELL, LANE), axis=0)

    def sums(i, carry):
        s1, s2 = carry
        ls = lanes(i)
        dz = T[:, ls]
        xhat = xh[sec, m, :, ls].astype(F32)
        both = xhat * dz
        sgp[sec, 10, :, ls] += fold(both)
        sgp[sec, 11, :, ls] += fold(dz)
        gain = pr[sec, 10:11, ls]
        return s1 + dz * gain, s2 + both * gain

    s1, s2 = lax.fori_loop(0, D // LANE, sums, (zero, zero))
    m1 = jnp.sum(s1, axis=-1, keepdims=True) * (1.0 / D)
    m2 = jnp.sum(s2, axis=-1, keepdims=True) * (1.0 / D)

    def back(i, carry):
        ls = lanes(i)
        xhat = xh[sec, m, :, ls].astype(F32)
        inner = T[:, ls] * pr[sec, 10:11, ls] - m1 - xhat * m2
        gc = gfull[m, :, ls].astype(F32) + rs[sec, m] * inner
        sgp[sec, 9, :, ls] += fold(gc)
        gh = halves(gc)
        U[0, 1 : GRID + 1, :, ls] = gh[0]
        U[1, 1 : GRID + 1, :, ls] = gh[1]
        moved = shifts(U[0, :, :, ls], U[1, :, :, ls])
        taps = pr[sec, :, ls]
        mask = halves(msk[m])
        um = halves(ubuf[sec, m, :, ls].astype(F32) * msk[m])
        accs = [jnp.zeros((GRID, CELL, LANE), F32) for _ in range(SIDE)]
        for a in range(3):
            for b in range(3):
                tap = 3 * a + b
                kg = jnp.zeros((CELL, LANE), F32)
                for wc in range(SIDE):
                    gs = moved[wc][2 - b][2 - a : 2 - a + GRID]
                    accs[wc] = accs[wc] + gs * taps[tap : tap + 1, :][None]
                    kg = kg + jnp.sum(gs * um[wc], axis=0)
                sgp[sec, tap, :, ls] += kg
        du = [(gh[wc] + mask[wc] * accs[wc]).reshape(HALF, LANE) for wc in range(SIDE)]
        out[m, :, ls] = jnp.concatenate(du, axis=0).astype(BF)
        return carry

    lax.fori_loop(0, D // LANE, back, 0)


def spread_heads(value, head_of_lane):
    parts = [jnp.where(head_of_lane == h, value, 0.0) for h in range(PACK)]
    return jnp.concatenate(parts, axis=0).astype(BF)


def gather_heads(value, rows, head_of_lane):
    out = jnp.zeros((rows, GROUP), F32)
    for h in range(PACK):
        out = jnp.where(head_of_lane == h, value[h * rows : (h + 1) * rows], out)
    return out


def unit_slices(unit):
    window, group = unit // NGROUP, lax.rem(unit, NGROUP)
    rows = pl.ds(pl.multiple_of(window * WROWS, 8), WROWS)
    cols = [pl.ds(pl.multiple_of(part * D + group * GROUP, LANE), GROUP) for part in range(3)]
    return rows, cols


def window_forward(m, qkv, pw, T):
    def unit(i, carry):
        rows, cols = unit_slices(i)
        head_of_lane = lax.broadcasted_iota(jnp.int32, (WROWS, GROUP), 1) // HEAD
        q = qkv[m, rows, cols[0]].astype(BF)
        kd = spread_heads(qkv[m, rows, cols[1]], head_of_lane)
        vd = spread_heads(qkv[m, rows, cols[2]], head_of_lane)
        s = dot(kd, q, 1, 1) * SCALE
        s = s.reshape(PACK, WROWS, WROWS)
        key = lax.broadcasted_iota(jnp.int32, s.shape, 1)
        s = jnp.where(lax.rem(key, CELL) == WIN, -1e30, s)
        p = jnp.exp(s - jnp.max(s, axis=1, keepdims=True))
        p = p * (1.0 / jnp.sum(p, axis=1, keepdims=True))
        p = p.reshape(PACK * WROWS, WROWS)
        pw[m, i] = p
        T[rows, cols[0]] = dot(p.astype(BF), vd, 0, 0)
        return carry

    lax.fori_loop(0, UNITS, unit, 0)


def window_backward(m, qkv, pw, T, Q):
    def unit(i, carry):
        rows, cols = unit_slices(i)
        head_of_lane = lax.broadcasted_iota(jnp.int32, (WROWS, GROUP), 1) // HEAD
        q = qkv[m, rows, cols[0]].astype(BF)
        kd = spread_heads(qkv[m, rows, cols[1]], head_of_lane)
        vd = spread_heads(qkv[m, rows, cols[2]], head_of_lane)
        g = T[rows, cols[0]].astype(BF)
        p = pw[m, i]
        dp = dot(vd, g, 1, 1).reshape(PACK, WROWS, WROWS)
        pf = p.reshape(PACK, WROWS, WROWS)
        ds = pf * (dp - jnp.sum(pf * dp, axis=1, keepdims=True))
        ds = ds.reshape(PACK * WROWS, WROWS).astype(BF)
        Q[rows, cols[0]] = dot(ds, kd, 0, 0) * SCALE
        Q[rows, cols[1]] = gather_heads(dot(ds, q), WROWS, head_of_lane) * SCALE
        Q[rows, cols[2]] = gather_heads(dot(p.astype(BF), g), WROWS, head_of_lane)
        return carry

    lax.fori_loop(0, UNITS, unit, 0)


def group_slices(group):
    return [pl.ds(pl.multiple_of(part * D + group * GROUP, LANE), GROUP) for part in range(3)]


def channel_forward(m, qkv, pc, T, msk):
    def unit(i, carry):
        cols = group_slices(i)
        mask = msk[m][:, :1]
        q = qkv[m, :, cols[0]].astype(BF)
        k = (qkv[m, :, cols[1]] * mask).astype(BF)
        v = qkv[m, :, cols[2]].astype(BF)
        s = dot(q, k, 0, 0) * SCALE
        same = (lax.broadcasted_iota(jnp.int32, s.shape, 0) // HEAD) == (lax.broadcasted_iota(jnp.int32, s.shape, 1) // HEAD)
        s = jnp.where(same, s, -1e30)
        p = jnp.exp(s - jnp.max(s, axis=1, keepdims=True))
        p = p * (1.0 / jnp.sum(p, axis=1, keepdims=True))
        pc[m, i] = p
        T[:, cols[0]] = dot(v, p.astype(BF), 1, 1)
        return carry

    lax.fori_loop(0, NGROUP, unit, 0)


def channel_backward(m, qkv, pc, T, Q, msk):
    def unit(i, carry):
        cols = group_slices(i)
        mask = msk[m][:, :1]
        q = qkv[m, :, cols[0]].astype(BF)
        k = (qkv[m, :, cols[1]] * mask).astype(BF)
        v = qkv[m, :, cols[2]].astype(BF)
        g = T[:, cols[0]].astype(BF)
        p = pc[m, i]
        dp = dot(g, v, 0, 0)
        ds = (p * (dp - jnp.sum(p * dp, axis=1, keepdims=True))).astype(BF)
        Q[:, cols[0]] = dot(k, ds, 1, 1) * SCALE
        Q[:, cols[1]] = dot(q, ds) * (SCALE * mask)
        Q[:, cols[2]] = dot(g, p.astype(BF))
        return carry

    lax.fori_loop(0, NGROUP, unit, 0)


def relay_kernel(
    img, cot, msk, prm, first, second,
    act, ing, fa, fb, fr, f2, fg, sg_own, sg_mate,
    wf, w2, pr, ubuf, gin, gatt, gout, uout, zb, xh, rs, qkv, ob, ab, db, hb, dqk, pw, pc, U, C, T, Q, sgp, sgs,
    wl, ws, wr, pl_, usem, gsem, hs, ls, ss, rsem, es, er, sgsem,
):
    s = lax.axis_index("section")
    dp = lax.axis_index("dp")
    stage, c = s // 2, lax.rem(s, 2)
    mate = (dp, stage * 2 + (1 - c))
    opposite = (dp, (1 - stage) * 2 + c)
    early = stage == 0

    barrier = pltpu.get_barrier_semaphore()
    for peer in (mate, opposite):
        pl.semaphore_signal(barrier, inc=1, device_id=peer, device_id_type=MESH)
    pl.semaphore_wait(barrier, 2)

    def remote(src, dst, send, recv, peer):
        return pltpu.make_async_remote_copy(
            src_ref=src, dst_ref=dst, send_sem=send, recv_sem=recv, device_id=peer, device_id_type=MESH
        )

    half = second.shape[0]

    def weight_parts(k):
        parts = []
        for i in range(4):
            parts.append((first.at[:, pl.ds(i * D, D)], wf.at[k, :, pl.ds(i * D, D)]))
        parts.append((second, w2.at[pl.ds(k * half, half), :]))
        parts.append((prm, pr.at[k]))
        return parts

    def weight_copies(k):
        local = [pltpu.make_async_copy(a, b, wl.at[i]) for i, (a, b) in enumerate(weight_parts(k))]
        sent = [remote(a, b, ws.at[i], wr.at[i], mate) for i, (a, b) in enumerate(weight_parts(k))]
        return local, sent

    order = (5, 0, 1, 2, 3, 4)
    for k in range(2):

        @pl.when(c == k)
        def _():
            local, sent = weight_copies(k)
            for i in order:
                local[i].start()
                sent[i].start()

    def wait_weight(k, i):
        @pl.when(c == k)
        def _():
            weight_copies(k)[0][i].wait()

        @pl.when(c != k)
        def _():
            weight_copies(k)[1][i].wait_recv()

    img_out = remote(img, ubuf.at[0, 1], pl_.at[0], usem.at[1], opposite)
    cot_out = remote(cot, gin.at[0], pl_.at[1], gsem.at[0], opposite)

    @pl.when(early)
    def _():
        cot_out.start()
        ubuf[0, 0] = img[...]

    @pl.when(jnp.logical_not(early))
    def _():
        img_out.start()
        gin[1] = cot[...]

    for wc in range(SIDE):
        U[wc, 0] = jnp.zeros((CELL, D), F32)
        U[wc, GRID + 1] = jnp.zeros((CELL, D), F32)
    sgp[...] = jnp.zeros(sgp.shape, F32)

    def u_hop(m):
        return remote(uout.at[m], ubuf.at[0, m], hs.at[m], usem.at[m], opposite)

    def g_hop(m):
        return remote(gout.at[m], gin.at[m], hs.at[m], gsem.at[m], opposite)

    def factor_copies(k, m, local):
        slot = m if local else 2 + m
        rows = pl.ds(pl.multiple_of(slot * ROWS, 16), ROWS)
        if k == 0:
            parts = [
                ("F", zb.at[0, m], fa.at[rows, :]),
                ("F", ob.at[m], fb.at[rows, :]),
                ("F", ab.at[m, :, pl.ds(0, FF // 2)], f2.at[rows, :]),
                ("M", gin.at[m], fg.at[rows, :]),
                ("G", gatt.at[m], fr.at[rows, pl.ds(3 * D, D)]),
                ("A", dqk.at[m], fr.at[rows, pl.ds(0, 3 * D)]),
            ]
        else:
            parts = [
                ("F", zb.at[1, m], fa.at[rows, :]),
                ("F", ab.at[m, :, pl.ds(FF // 2, FF // 2)], f2.at[rows, :]),
                ("M", gin.at[m], fg.at[rows, :]),
                ("M", hb.at[m], fr.at[rows, :]),
            ]
        made = []
        for i, (when, src, dst) in enumerate(parts):
            if local:
                made.append((when, pltpu.make_async_copy(src, dst, ls.at[m, i])))
            else:
                made.append((when, remote(src, dst, ss.at[m, i], rsem.at[m, i], mate)))
        return made

    def start_factors(m, which):
        for k in range(2):
            for local in (True, False):

                @pl.when((c == k) if local else (c != k))
                def _():
                    for when, copy in factor_copies(k, m, local):
                        if when == which:
                            copy.start()

    def forward(m, p):
        @pl.when(jnp.logical_not(early))
        def _():
            u_hop(m).wait_recv()

        @pl.when(early & (m == 1))
        def _():
            img_out.wait_recv()

        once = p == 0

        def first_time(k, i):
            @pl.when(once)
            def _():
                wait_weight(k, i)

        first_time(0, 5)
        front_forward(0, m, ubuf, msk, pr, U, C, zb, xh, rs)
        for i in range(3):
            first_time(0, i)
            qkv[m, :, pl.ds(i * D, D)] = dot(zb[0, m], wf[0, :, pl.ds(i * D, D)]).astype(BF).astype(F32)

        @pl.when(early)
        def _():
            window_forward(m, qkv, pw, T)

        @pl.when(jnp.logical_not(early))
        def _():
            channel_forward(m, qkv, pc, T, msk)

        first_time(0, 3)
        ob[m] = T[...].astype(BF)
        ubuf[1, m] = (C[...] + dot(ob[m], wf[0, :, pl.ds(3 * D, D)])).astype(BF)

        first_time(1, 5)
        front_forward(1, m, ubuf, msk, pr, U, C, zb, xh, rs)
        for i in range(4):
            first_time(1, i)
        first_time(0, 4)
        first_time(1, 4)

        def mlp(t, carry):
            cols = lanes(t, FTILE)
            h = dot(zb[1, m], wf[1, :, cols])
            a, d = gelu_parts(h)
            a = a.astype(BF)
            ab[m, :, cols] = a
            db[m, :, cols] = d.astype(BF)
            C[...] += dot(a, w2[cols, :])
            return carry

        lax.fori_loop(0, FF // FTILE, mlp, 0)

        @pl.when(early)
        def _():
            uout[m] = C[...].astype(BF)
            u_hop(m).start()

        @pl.when(jnp.logical_not(early))
        def _():
            for l in range(D // LANE):
                cols = pl.ds(l * LANE, LANE)
                uout[m, :, cols] = (C[:, cols].astype(BF).astype(F32) * msk[m]).astype(BF)

        @pl.when(jnp.logical_not(early) & (m == 0))
        def _():
            remote(uout.at[0], act, es.at[0], er.at[0], opposite).start()

        @pl.when(jnp.logical_not(early) & (m == 1))
        def _():
            pltpu.make_async_copy(uout.at[1], act, es.at[0]).start()

        start_factors(m, "F")

    def backward(m):
        @pl.when(early)
        def _():
            g_hop(m).wait_recv()

        @pl.when(jnp.logical_not(early))
        def _():
            @pl.when(m == 0)
            def _():
                cot_out.wait_recv()

            for l in range(D // LANE):
                cols = pl.ds(l * LANE, LANE)
                gin[m, :, cols] = (gin[m, :, cols].astype(F32) * msk[m]).astype(BF)

        def mlp(t, carry):
            cols = lanes(t, FTILE)
            da = dot(gin[m], w2[cols, :], 1, 1)
            h = (da * db[m, :, cols].astype(F32)).astype(BF)
            hb[m, :, cols] = h
            part = dot(h, wf[1, :, cols], 1, 1)

            @pl.when(t == 0)
            def _():
                T[...] = part

            @pl.when(t > 0)
            def _():
                T[...] += part

            return carry

        lax.fori_loop(0, FF // FTILE, mlp, 0)
        start_factors(m, "M")
        front_backward(1, m, ubuf, msk, pr, U, T, gin, xh, rs, sgp, gatt)
        start_factors(m, "G")
        T[...] = dot(gatt[m], wf[0, :, pl.ds(3 * D, D)], 1, 1)

        @pl.when(early)
        def _():
            window_backward(m, qkv, pw, T, Q)

        @pl.when(jnp.logical_not(early))
        def _():
            channel_backward(m, qkv, pc, T, Q, msk)

        for i in range(3):
            cols = pl.ds(i * D, D)
            dqk[m, :, cols] = Q[:, cols].astype(BF)
        start_factors(m, "A")
        for i in range(3):
            cols = pl.ds(i * D, D)
            part = dot(dqk[m, :, cols], wf[0, :, cols], 1, 1)
            if i == 0:
                T[...] = part
            else:
                T[...] += part
        front_backward(0, m, ubuf, msk, pr, U, T, gatt, xh, rs, sgp, gout)

        @pl.when(jnp.logical_not(early))
        def _():
            g_hop(m).start()

        @pl.when(early & (m == 0))
        def _():
            pltpu.make_async_copy(gout.at[0], ing, es.at[1]).start()

        @pl.when(early & (m == 1))
        def _():
            remote(gout.at[1], ing, es.at[1], er.at[1], opposite).start()

    def phase(p, carry):
        m = jnp.where(early, lax.rem(p, 2), p // 2)
        ahead = jnp.where(early, p < 2, lax.rem(p, 2) == 0)

        @pl.when(ahead)
        def _():
            forward(m, p)

        @pl.when(jnp.logical_not(ahead))
        def _():
            backward(m)

        return carry

    lax.fori_loop(0, 4, phase, 0)

    for sec in range(2):
        for j in range(12):
            sgs[sec, j : j + 1, :] = jnp.sum(sgp[sec, j], axis=0, keepdims=True)
        sgs[sec, 12:16, :] = jnp.zeros((4, D), F32)
    keep = pltpu.make_async_copy(sgs.at[c], sg_own, sgsem.at[0])
    give = remote(sgs.at[1 - c], sg_mate, sgsem.at[1], sgsem.at[2], mate)
    keep.start()
    give.start()

    for k in range(2):

        @pl.when(c == k)
        def _():
            for copy in weight_copies(k)[1]:
                copy.wait_send()
            for m in range(2):
                for _when, copy in factor_copies(k, m, True):
                    copy.wait()
                for _when, copy in factor_copies(1 - k, m, False):
                    copy.wait_send()
                for _when, copy in factor_copies(k, m, False):
                    copy.wait_recv()

    keep.wait()
    give.wait()

    @pl.when(early)
    def _():
        cot_out.wait_send()
        for m in range(2):
            u_hop(m).wait_send()
        pltpu.make_async_copy(gout.at[0], ing, es.at[1]).wait()
        remote(gout.at[1], ing, es.at[1], er.at[1], opposite).wait_send()
        remote(uout.at[0], act, es.at[0], er.at[0], opposite).wait_recv()

    @pl.when(jnp.logical_not(early))
    def _():
        img_out.wait_send()
        for m in range(2):
            g_hop(m).wait_send()
        remote(uout.at[0], act, es.at[0], er.at[0], opposite).wait_send()
        pltpu.make_async_copy(uout.at[1], act, es.at[0]).wait()
        remote(gout.at[1], ing, es.at[1], er.at[1], opposite).wait_recv()


def relay(img, cot, msk, prm, first, second):
    shape = jax.ShapeDtypeStruct
    vmem = pl.BlockSpec(memory_space=pltpu.VMEM)
    anywhere = pl.BlockSpec(memory_space=pl.ANY)
    dma = pltpu.SemaphoreType.DMA
    image = (ROWS, D)
    return pl.pallas_call(
        relay_kernel,
        out_shape=[
            shape(image, BF),
            shape(image, BF),
            shape((4 * ROWS, D), BF),
            shape((4 * ROWS, D), BF),
            shape((4 * ROWS, FF), BF),
            shape((4 * ROWS, FF // 2), BF),
            shape((4 * ROWS, D), BF),
            shape((16, D), F32),
            shape((16, D), F32),
        ],
        in_specs=[vmem, vmem, vmem, vmem, anywhere, anywhere],
        out_specs=[anywhere] * 9,
        scratch_shapes=[
            pltpu.VMEM((2, D, FF), BF),
            pltpu.VMEM((FF, D), BF),
            pltpu.VMEM((2, 16, D), F32),
            pltpu.VMEM((2, 2) + image, BF),
            pltpu.VMEM((2,) + image, BF),
            pltpu.VMEM((2,) + image, BF),
            pltpu.VMEM((2,) + image, BF),
            pltpu.VMEM((2,) + image, BF),
            pltpu.VMEM((2, 2) + image, BF),
            pltpu.VMEM((2, 2) + image, BF),
            pltpu.VMEM((2, 2, ROWS, LANE), F32),
            pltpu.VMEM((2, ROWS, 3 * D), F32),
            pltpu.VMEM((2,) + image, BF),
            pltpu.VMEM((2, ROWS, FF), BF),
            pltpu.VMEM((2, ROWS, FF), BF),
            pltpu.VMEM((2, ROWS, FF), BF),
            pltpu.VMEM((2, ROWS, 3 * D), BF),
            pltpu.VMEM((2, UNITS, PACK * WROWS, WROWS), F32),
            pltpu.VMEM((2, NGROUP, GROUP, GROUP), F32),
            pltpu.VMEM((SIDE, GRID + 2, CELL, D), F32),
            pltpu.VMEM(image, F32),
            pltpu.VMEM(image, F32),
            pltpu.VMEM((ROWS, 3 * D), F32),
            pltpu.VMEM((2, 12, CELL, D), F32),
            pltpu.VMEM((2, 16, D), F32),
            dma((6,)),
            dma((6,)),
            dma((6,)),
            dma((2,)),
            dma((2,)),
            dma((2,)),
            dma((2,)),
            dma((2, 6)),
            dma((2, 6)),
            dma((2, 6)),
            dma((2,)),
            dma((2,)),
            dma((3,)),
        ],
        name="relay",
        compiler_params=pltpu.CompilerParams(
            collective_id=1, has_side_effects=True, vmem_limit_bytes=60 * 2**20
        ),
    )(img, cot, msk, prm, first, second)


RING = 8
COLS = FF // RING
TAIL = FF // 2 // RING


def ring_kernel(
    n, fa, fb, fr, f2, fg, sg_own, sg_mate,
    out1, out2, outs,
    la, r1, a2, g2, lt, at, buf, ag, acc, got,
    lsem, ss, rs, os_, sms, smr,
):
    s = lax.axis_index("section")
    dp = lax.axis_index("dp")
    c = lax.rem(s, 2)
    tokens = la.shape[1]

    def place(pos):
        pos = lax.rem(pos + 2 * n, n)
        return jnp.where(pos < n // 2, 2 * pos, 2 * (n - 1 - pos) + 1)

    me = jnp.where(lax.rem(dp, 2) == 0, dp // 2, n - 1 - dp // 2)
    nexts = (place(me + 1), place(me - 1))
    rounds = n.bit_length() - 1
    partners = []
    for r in range(rounds):
        bit = 1 << r
        partners.append(jnp.where(lax.rem(dp // bit, 2) == 0, dp + bit, dp - bit))

    barrier = pltpu.get_barrier_semaphore()
    peers = list(nexts) + partners
    for peer in peers:
        pl.semaphore_signal(barrier, inc=1, device_id=(peer, s), device_id_type=MESH)

    loads = [
        pltpu.make_async_copy(fa, la.at[0], lsem.at[0]),
        pltpu.make_async_copy(fr, r1, lsem.at[1]),
        pltpu.make_async_copy(f2, a2, lsem.at[2]),
        pltpu.make_async_copy(fg, g2, lsem.at[3]),
        pltpu.make_async_copy(fb, la.at[1], lsem.at[4]),
    ]
    for copy in loads[:4]:
        copy.start()

    @pl.when(c == 0)
    def _():
        loads[4].start()

    def turn(src, dst, count):
        def body(i, carry):
            dst[lanes(i), :] = src[:, lanes(i)].T
            return carry

        lax.fori_loop(0, count, body, 0)

    def shard(k):
        return lax.rem(k + 2 * n, n)

    def tile1(h, j):
        sel = jnp.where((c == 0) & (j >= (3 * n) // 4), 1, 0)
        return dot(lt[sel, pl.ds(h * COLS, COLS), :], r1[:, lanes(j, COLS)])

    def tile2(h, j):
        rows = pl.ds(pl.multiple_of(j * TAIL, 16), TAIL)
        return dot(at[rows, :], g2[:, pl.ds(h * COLS, COLS)])

    parts = (pl.ds(0, COLS), pl.ds(COLS, TAIL))
    tiles = (tile1, tile2)

    def scatter(h, t, sub):
        return pltpu.make_async_remote_copy(
            src_ref=buf.at[h, t, parts[sub], :],
            dst_ref=buf.at[h, t + 1, parts[sub], :],
            send_sem=ss.at[h, t, sub],
            recv_sem=rs.at[h, t + 1, sub],
            device_id=(nexts[h], s),
            device_id_type=MESH,
        )

    def spread(h, t, sub, j):
        return pltpu.make_async_remote_copy(
            src_ref=ag.at[h, j, parts[sub], :],
            dst_ref=ag.at[h, j, parts[sub], :],
            send_sem=ss.at[h, n - 1 + t, sub],
            recv_sem=rs.at[h, n + t, sub],
            device_id=(nexts[h], s),
            device_id_type=MESH,
        )

    def write(h, j, sub):
        cols = lanes(j, COLS)
        if sub == 0:
            dst = out1.at[pl.ds(h * COLS, COLS), cols]
        else:
            dst = out2.at[pl.ds(pl.multiple_of(j * TAIL, 16), TAIL), pl.ds(h * COLS, COLS)]
        return pltpu.make_async_copy(ag.at[h, j, parts[sub], :], dst, os_.at[h, j, sub])

    def sign(h):
        return 1 if h == 0 else -1

    loads[0].wait()
    turn(la.at[0], lt.at[0], D // LANE)

    @pl.when(c == 0)
    def _():
        loads[4].wait()
        turn(la.at[1], lt.at[1], D // LANE)

    loads[1].wait()
    pl.semaphore_wait(barrier, len(peers))
    for h in range(2):
        buf[h, 0, parts[0], :] = tile1(h, me).astype(BF)
        scatter(h, 0, 0).start()
    loads[2].wait()
    loads[3].wait()
    turn(a2, at, FF // 2 // LANE)
    for h in range(2):
        buf[h, 0, parts[1], :] = tile2(h, me).astype(BF)
        scatter(h, 0, 1).start()

    acc[0] = sg_own[...] + sg_mate[...]

    def reduce_step(t, carry):
        for sub in range(2):
            for h in range(2):
                own = tiles[sub](h, shard(me - sign(h) * t))
                scatter(h, t - 1, sub).wait_recv()
                buf[h, t, parts[sub], :] = (own + buf[h, t, parts[sub], :].astype(F32)).astype(BF)
                scatter(h, t, sub).start()
        return carry

    lax.fori_loop(1, n - 1, reduce_step, 0)

    def home(h, t):
        return shard(me + sign(h) - sign(h) * t)

    for sub in range(2):
        for h in range(2):
            j = home(h, 0)
            own = tiles[sub](h, j)
            scatter(h, n - 2, sub).wait_recv()
            ag[h, j, parts[sub], :] = (own + buf[h, n - 1, parts[sub], :].astype(F32)).astype(BF)
            spread(h, 0, sub, j).start()
            write(h, j, sub).start()

    def small(r):
        return pltpu.make_async_remote_copy(
            src_ref=acc.at[r],
            dst_ref=got.at[r],
            send_sem=sms.at[r],
            recv_sem=smr.at[r],
            device_id=(partners[r], s),
            device_id_type=MESH,
        )

    small(0).start()
    for t in range(1, n):
        for sub in range(2):
            for h in range(2):
                j = home(h, t)
                spread(h, t - 1, sub, j).wait_recv()
                if t < n - 1:
                    spread(h, t, sub, j).start()
                write(h, j, sub).start()
        if t % 2 == 0 and t // 2 <= rounds:
            r = t // 2 - 1
            small(r).wait_recv()
            acc[r + 1] = acc[r] + got[r]
            if r + 1 < rounds:
                small(r + 1).start()
    outs[...] = acc[rounds]

    def drain(t, carry):
        for sub in range(2):
            for h in range(2):
                scatter(h, t, sub).wait_send()
        return carry

    lax.fori_loop(0, n - 1, drain, 0)
    for t in range(n - 1):
        for sub in range(2):
            for h in range(2):
                spread(h, t, sub, home(h, t)).wait_send()
    for j in range(n):
        for sub in range(2):
            for h in range(2):
                write(h, j, sub).wait()
    for r in range(rounds):
        small(r).wait_send()


def ring_reduce(n, fa, fb, fr, f2, fg, sg_own, sg_mate):
    shape = jax.ShapeDtypeStruct
    vmem = pl.BlockSpec(memory_space=pltpu.VMEM)
    anywhere = pl.BlockSpec(memory_space=pl.ANY)
    dma = pltpu.SemaphoreType.DMA
    tokens = fa.shape[0]
    rounds = n.bit_length() - 1
    block = (COLS + TAIL, COLS)
    return pl.pallas_call(
        partial(ring_kernel, n),
        out_shape=[shape((D, FF), BF), shape((FF // 2, D), BF), shape((16, D), F32)],
        in_specs=[anywhere] * 5 + [vmem] * 2,
        out_specs=[anywhere, anywhere, vmem],
        scratch_shapes=[
            pltpu.VMEM((2, tokens, D), BF),
            pltpu.VMEM((tokens, FF), BF),
            pltpu.VMEM((tokens, FF // 2), BF),
            pltpu.VMEM((tokens, D), BF),
            pltpu.VMEM((2, D, tokens), BF),
            pltpu.VMEM((FF // 2, tokens), BF),
            pltpu.VMEM((2, n) + block, BF),
            pltpu.VMEM((2, n) + block, BF),
            pltpu.VMEM((rounds + 1, 16, D), F32),
            pltpu.VMEM((rounds, 16, D), F32),
            dma((5,)),
            dma((2, 2 * n, 2)),
            dma((2, 2 * n, 2)),
            dma((2, n, 2)),
            dma((rounds,)),
            dma((rounds,)),
        ],
        name="ring",
        compiler_params=pltpu.CompilerParams(
            collective_id=2, has_side_effects=True, vmem_limit_bytes=60 * 2**20
        ),
    )(fa, fb, fr, f2, fg, sg_own, sg_mate)


def plain_reduce(fa, fb, fr, f2, fg, sg_own, sg_mate):
    even = lax.rem(lax.axis_index("section"), 2) == 0
    left = jnp.where(even, fb, fa)
    qkv = dot(fa, fr[:, : 3 * D], 0, 0)
    last = dot(left, fr[:, 3 * D :], 0, 0)
    out1 = jnp.concatenate([qkv, last], axis=1)
    out2 = dot(f2, fg, 0, 0)
    return lax.psum((out1.astype(BF), out2.astype(BF), sg_own + sg_mate), "dp")


def to_rows(images):
    shaped = images.reshape(GRID, SIDE, WIN, images.shape[-1]).transpose(1, 0, 2, 3)
    return jnp.pad(shaped, ((0, 0), (0, 0), (0, CELL - WIN), (0, 0))).reshape(ROWS, images.shape[-1])


def from_rows(rows):
    shaped = rows.reshape(SIDE, GRID, CELL, rows.shape[-1])[:, :, :WIN].transpose(1, 0, 2, 3)
    return shaped.reshape(1, GRID, GRID, rows.shape[-1])


def masks(window_rows, window_cols, c):
    places = jnp.stack([c, c + 2])
    height = (WIN * window_rows[places])[:, None]
    width = (WIN * window_cols[places])[:, None]
    index = jnp.arange(ROWS)[None, :]
    row = (index % HALF) // CELL
    cell = index % CELL
    column = (index // HALF) * WIN + cell
    inside = (row < height) & (column < width) & (cell < WIN)
    return jnp.broadcast_to(inside.astype(F32)[:, :, None], (2, ROWS, LANE))


def per_device(
    images, cotangent, window_rows, window_cols, pos_kernel, pos_bias, norm_gain, norm_shift, first_weight, second_weight
):
    s = lax.axis_index("section")
    prm = jnp.concatenate(
        [pos_kernel[0], pos_bias, norm_gain, norm_shift, jnp.zeros((4, D), pos_bias.dtype)], axis=0
    ).astype(F32)
    msk = masks(window_rows, window_cols, lax.rem(s, 2))
    act, ing, fa, fb, fr, f2, fg, sg_own, sg_mate = relay(
        to_rows(images), to_rows(cotangent), msk, prm, first_weight[0], second_weight
    )
    n = lax.axis_size("dp")
    reduce = partial(ring_reduce, n) if n == RING else plain_reduce
    out1, out2, outs = reduce(fa, fb, fr, f2, fg, sg_own, sg_mate)
    return (
        from_rows(act),
        from_rows(ing).astype(F32),
        out1.astype(F32)[None],
        out2.astype(F32),
        outs[None, :9],
        outs[9:10],
        outs[10:11],
        outs[11:12],
    )


def solution(mesh):
    in_specs = (
        P(("dp", "section"), None, None, None),
        P(("dp", "section"), None, None, None),
        P("dp"),
        P("dp"),
        P("section", None, None),
        P("section", None),
        P("section", None),
        P("section", None),
        P("section", None, None),
        P("section", None),
    )
    out_specs = (
        P(("dp", "section"), None, None, None),
        P(("dp", "section"), None, None, None),
        P("section", None, None),
        P("section", None),
        P("section", None, None),
        P("section", None),
        P("section", None),
        P("section", None),
    )
    return jax.shard_map(per_device, mesh=mesh, in_specs=in_specs, out_specs=out_specs, check_vma=False)
```

```python
from functools import partial

import jax
import jax.numpy as jnp
from jax import lax
from jax.experimental import pallas as pl
from jax.experimental.pallas import tpu as pltpu
from jax.sharding import PartitionSpec as P

D = 768
FF = 3072
HEADS = 24
HEAD = 32
WIN = 7
SIDE = 2
GRID = SIDE * WIN
CELL = 8
WROWS = WIN * CELL
HALF = GRID * CELL
ROWS = SIDE * HALF
GROUP = 256
PACK = GROUP // HEAD
NGROUP = D // GROUP
UNITS = NGROUP * SIDE * SIDE
LANE = 128
FTILE = 1024
EPS = 1e-05
SCALE = HEAD ** (-0.5)
BF = jnp.bfloat16
F32 = jnp.float32
MESH = pl.DeviceIdType.MESH


def dot(a, b, ca=1, cb=0):
    return lax.dot_general(a, b, (((ca,), (cb,)), ((), ())), preferred_element_type=F32)


def lanes(index, width=LANE):
    return pl.ds(pl.multiple_of(index * width, width), width)


def halves(value):
    return value.reshape(SIDE, GRID, CELL, value.shape[-1])


def shifts(left, right):
    column = lax.broadcasted_iota(jnp.int32, left.shape, 1)
    before0 = pltpu.roll(left, 1, 1)
    after0 = jnp.where(column == WIN - 1, pltpu.roll(right, CELL - 2, 1), pltpu.roll(left, CELL - 1, 1))
    before1 = jnp.where(column == 0, pltpu.roll(left, 2, 1), pltpu.roll(right, 1, 1))
    after1 = pltpu.roll(right, CELL - 1, 1)
    return ((before0, left, after0), (before1, right, after1))


def gelu_parts(h):
    expo = jnp.exp(h * h * -0.5)
    t = 1.0 / (1.0 + (0.3275911 * 0.7071067811865476) * jnp.abs(h))
    poly = t * (0.127414796 + t * (-0.142248368 + t * (0.7107068705 + t * (-0.7265760135 + t * 0.5307027145))))
    tail = poly * expo
    phi = jnp.where(h >= 0, 1.0 - tail, tail)
    return h * phi, phi + h * expo * 0.3989422804014327


def front_forward(sec, m, ubuf, msk, pr, U, C, zb, xh, rs):
    zero = jnp.zeros((ROWS, LANE), F32)

    def conv(i, total):
        ls = lanes(i)
        u = ubuf[sec, m, :, ls].astype(F32)
        masked = halves(u * msk[m])
        U[0, 1 : GRID + 1, :, ls] = masked[0]
        U[1, 1 : GRID + 1, :, ls] = masked[1]
        moved = shifts(U[0, :, :, ls], U[1, :, :, ls])
        taps = pr[sec, :, ls]
        uh = halves(u)
        sums = []
        for wc in range(SIDE):
            acc = uh[wc] + taps[9:10, :][None]
            for a in range(3):
                for b in range(3):
                    acc = acc + moved[wc][b][a : a + GRID] * taps[3 * a + b : 3 * a + b + 1, :][None]
            acc = acc.reshape(HALF, LANE)
            C[pl.ds(wc * HALF, HALF), ls] = acc
            sums.append(acc)
        return total + jnp.concatenate(sums, axis=0)

    mean = jnp.sum(lax.fori_loop(0, D // LANE, conv, zero), axis=-1, keepdims=True) * (1.0 / D)

    def spread(i, total):
        centred = C[:, lanes(i)] - mean
        return total + centred * centred

    var = jnp.sum(lax.fori_loop(0, D // LANE, spread, zero), axis=-1, keepdims=True) * (1.0 / D)
    rstd = lax.rsqrt(var + EPS)
    rs[sec, m] = jnp.broadcast_to(rstd, (ROWS, LANE))

    def norm(i, carry):
        ls = lanes(i)
        xhat = (C[:, ls] - mean) * rstd
        xh[sec, m, :, ls] = xhat.astype(BF)
        zb[sec, m, :, ls] = (xhat * pr[sec, 10:11, ls] + pr[sec, 11:12, ls]).astype(BF)
        return carry

    lax.fori_loop(0, D // LANE, norm, 0)


def front_backward(sec, m, ubuf, msk, pr, U, T, gfull, xh, rs, sgp, out):
    zero = jnp.zeros((ROWS, LANE), F32)

    def fold(value):
        return jnp.sum(value.reshape(ROWS // CELL, CELL, LANE), axis=0)

    def sums(i, carry):
        s1, s2 = carry
        ls = lanes(i)
        dz = T[:, ls]
        xhat = xh[sec, m, :, ls].astype(F32)
        both = xhat * dz
        sgp[sec, 10, :, ls] += fold(both)
        sgp[sec, 11, :, ls] += fold(dz)
        gain = pr[sec, 10:11, ls]
        return s1 + dz * gain, s2 + both * gain

    s1, s2 = lax.fori_loop(0, D // LANE, sums, (zero, zero))
    m1 = jnp.sum(s1, axis=-1, keepdims=True) * (1.0 / D)
    m2 = jnp.sum(s2, axis=-1, keepdims=True) * (1.0 / D)

    def back(i, carry):
        ls = lanes(i)
        xhat = xh[sec, m, :, ls].astype(F32)
        inner = T[:, ls] * pr[sec, 10:11, ls] - m1 - xhat * m2
        gc = gfull[m, :, ls].astype(F32) + rs[sec, m] * inner
        sgp[sec, 9, :, ls] += fold(gc)
        gh = halves(gc)
        U[0, 1 : GRID + 1, :, ls] = gh[0]
        U[1, 1 : GRID + 1, :, ls] = gh[1]
        moved = shifts(U[0, :, :, ls], U[1, :, :, ls])
        taps = pr[sec, :, ls]
        mask = halves(msk[m])
        um = halves(ubuf[sec, m, :, ls].astype(F32) * msk[m])
        accs = [jnp.zeros((GRID, CELL, LANE), F32) for _ in range(SIDE)]
        for a in range(3):
            for b in range(3):
                tap = 3 * a + b
                kg = jnp.zeros((CELL, LANE), F32)
                for wc in range(SIDE):
                    gs = moved[wc][2 - b][2 - a : 2 - a + GRID]
                    accs[wc] = accs[wc] + gs * taps[tap : tap + 1, :][None]
                    kg = kg + jnp.sum(gs * um[wc], axis=0)
                sgp[sec, tap, :, ls] += kg
        du = [(gh[wc] + mask[wc] * accs[wc]).reshape(HALF, LANE) for wc in range(SIDE)]
        out[m, :, ls] = jnp.concatenate(du, axis=0).astype(BF)
        return carry

    lax.fori_loop(0, D // LANE, back, 0)


def spread_heads(value, head_of_lane):
    parts = [jnp.where(head_of_lane == h, value, 0.0) for h in range(PACK)]
    return jnp.concatenate(parts, axis=0).astype(BF)


def gather_heads(value, rows, head_of_lane):
    out = jnp.zeros((rows, GROUP), F32)
    for h in range(PACK):
        out = jnp.where(head_of_lane == h, value[h * rows : (h + 1) * rows], out)
    return out


def unit_slices(unit):
    pair, group = unit // NGROUP, lax.rem(unit, NGROUP)
    rows = [pl.ds(pl.multiple_of((2 * pair + w) * WROWS, 8), WROWS) for w in range(2)]
    cols = [pl.ds(pl.multiple_of(part * D + group * GROUP, LANE), GROUP) for part in range(3)]
    return rows, cols


def window_parts(m, i, qkv):
    rows, cols = unit_slices(i)
    head_of_lane = lax.broadcasted_iota(jnp.int32, (WROWS, GROUP), 1) // HEAD
    q = [qkv[m, r, cols[0]].astype(BF) for r in rows]
    kd = [spread_heads(qkv[m, r, cols[1]], head_of_lane) for r in rows]
    vd = [spread_heads(qkv[m, r, cols[2]], head_of_lane) for r in rows]
    return rows, cols, head_of_lane, q, kd, vd


def window_forward(m, qkv, pw, T):
    def unit(i, carry):
        rows, cols, head_of_lane, q, kd, vd = window_parts(m, i, qkv)
        s = [(dot(b, a, 1, 1) * SCALE).reshape(PACK, WROWS, WROWS) for a, b in zip(q, kd)]
        key = lax.broadcasted_iota(jnp.int32, s[0].shape, 1)
        real = lax.rem(key, CELL) < WIN
        s = [jnp.where(real, x, -1e30) for x in s]
        p = [jnp.exp(x - jnp.max(x, axis=1, keepdims=True)) for x in s]
        p = [x * (1.0 / jnp.sum(x, axis=1, keepdims=True)) for x in p]
        p = [x.reshape(PACK * WROWS, WROWS) for x in p]
        for w in range(2):
            pw[m, 2 * i + w] = p[w]
        out = [dot(x.astype(BF), v, 0, 0) for x, v in zip(p, vd)]
        for w in range(2):
            T[rows[w], cols[0]] = out[w]
        return carry

    lax.fori_loop(0, UNITS // 2, unit, 0)


def window_backward(m, qkv, pw, T, Q):
    def unit(i, carry):
        rows, cols, head_of_lane, q, kd, vd = window_parts(m, i, qkv)
        g = [T[r, cols[0]].astype(BF) for r in rows]
        p = [pw[m, 2 * i + w].reshape(PACK, WROWS, WROWS) for w in range(2)]
        dp = [dot(v, x, 1, 1).reshape(PACK, WROWS, WROWS) for v, x in zip(vd, g)]
        ds = [x * (y - jnp.sum(x * y, axis=1, keepdims=True)) for x, y in zip(p, dp)]
        ds = [x.reshape(PACK * WROWS, WROWS).astype(BF) for x in ds]
        pb = [x.reshape(PACK * WROWS, WROWS).astype(BF) for x in p]
        dv = [gather_heads(dot(x, y), WROWS, head_of_lane) for x, y in zip(pb, g)]
        dk = [gather_heads(dot(x, y), WROWS, head_of_lane) * SCALE for x, y in zip(ds, q)]
        dq = [dot(x, y, 0, 0) * SCALE for x, y in zip(ds, kd)]
        for w in range(2):
            Q[rows[w], cols[0]] = dq[w]
            Q[rows[w], cols[1]] = dk[w]
            Q[rows[w], cols[2]] = dv[w]
        return carry

    lax.fori_loop(0, UNITS // 2, unit, 0)


def group_slices(group):
    return [pl.ds(pl.multiple_of(part * D + group * GROUP, LANE), GROUP) for part in range(3)]


def channel_forward(m, qkv, pc, T, msk):
    def unit(i, carry):
        cols = group_slices(i)
        mask = msk[m][:, :1]
        q = qkv[m, :, cols[0]].astype(BF)
        k = (qkv[m, :, cols[1]] * mask).astype(BF)
        v = qkv[m, :, cols[2]].astype(BF)
        s = dot(q, k, 0, 0) * SCALE
        same = (lax.broadcasted_iota(jnp.int32, s.shape, 0) // HEAD) == (lax.broadcasted_iota(jnp.int32, s.shape, 1) // HEAD)
        s = jnp.where(same, s, -1e30)
        p = jnp.exp(s - jnp.max(s, axis=1, keepdims=True))
        p = p * (1.0 / jnp.sum(p, axis=1, keepdims=True))
        pc[m, i] = p
        T[:, cols[0]] = dot(v, p.astype(BF), 1, 1)
        return carry

    lax.fori_loop(0, NGROUP, unit, 0, unroll=True)


def channel_backward(m, qkv, pc, T, Q, msk):
    def unit(i, carry):
        cols = group_slices(i)
        mask = msk[m][:, :1]
        q = qkv[m, :, cols[0]].astype(BF)
        k = (qkv[m, :, cols[1]] * mask).astype(BF)
        v = qkv[m, :, cols[2]].astype(BF)
        g = T[:, cols[0]].astype(BF)
        p = pc[m, i]
        dp = dot(g, v, 0, 0)
        ds = (p * (dp - jnp.sum(p * dp, axis=1, keepdims=True))).astype(BF)
        Q[:, cols[0]] = dot(k, ds, 1, 1) * SCALE
        Q[:, cols[1]] = dot(q, ds) * (SCALE * mask)
        Q[:, cols[2]] = dot(g, p.astype(BF))
        return carry

    lax.fori_loop(0, NGROUP, unit, 0, unroll=True)


def relay_kernel(
    wrows, wcols, img, cot, kern, bias, gain, move, first, second,
    act, ing, fa, fb, fr, f2, fg, sg_own, sg_mate,
    wf, w2, pr, msk, raw, flat, ubuf, gin, gatt, gout, uout, zb, xh, rs, qkv, ob, ab, db, hb, dqk, pw, pc, U, C, T, Q, sgp, sgs,
    wl, ws, wr, pl_, usem, gsem, hs, ls, ss, rsem, es, er, sgsem,
):
    s = lax.axis_index("section")
    dp = lax.axis_index("dp")
    stage, c = s // 2, lax.rem(s, 2)
    mate = (dp, stage * 2 + (1 - c))
    opposite = (dp, (1 - stage) * 2 + c)
    early = stage == 0

    barrier = pltpu.get_barrier_semaphore()
    for peer in (mate, opposite):
        pl.semaphore_signal(barrier, inc=1, device_id=peer, device_id_type=MESH)
    pl.semaphore_wait(barrier, 2)

    def remote(src, dst, send, recv, peer):
        return pltpu.make_async_remote_copy(
            src_ref=src, dst_ref=dst, send_sem=send, recv_sem=recv, device_id=peer, device_id_type=MESH
        )

    half = second.shape[0]

    def weight_parts(k):
        parts = []
        for i in range(4):
            parts.append((first.at[:, pl.ds(i * D, D)], wf.at[k, :, pl.ds(i * D, D)]))
        parts.append((second, w2.at[pl.ds(k * half, half), :]))
        return parts

    def weight_copies(k):
        local = [pltpu.make_async_copy(a, b, wl.at[i]) for i, (a, b) in enumerate(weight_parts(k))]
        sent = [remote(a, b, ws.at[i], wr.at[i], mate) for i, (a, b) in enumerate(weight_parts(k))]
        return local, sent

    def params_copy(k):
        return remote(pr.at[k], pr.at[k], ws.at[5], wr.at[5], mate)

    pr[c, 0:9, :] = kern[...].astype(F32)
    pr[c, 9:10, :] = bias[...].astype(F32)
    pr[c, 10:11, :] = gain[...].astype(F32)
    pr[c, 11:12, :] = move[...].astype(F32)
    params_copy(c).start()
    for k in range(2):

        @pl.when(c == k)
        def _():
            local, sent = weight_copies(k)
            for i in range(5):
                local[i].start()
                sent[i].start()

    def wait_weight(k, i):
        if i < 5:

            @pl.when(c == k)
            def _():
                weight_copies(k)[0][i].wait()

        @pl.when(c != k)
        def _():
            (weight_copies(k)[1][i] if i < 5 else params_copy(k)).wait_recv()

    img_out = remote(img, raw, pl_.at[0], pl_.at[1], opposite)
    cot_out = remote(cot, raw, pl_.at[0], pl_.at[1], opposite)

    def pad(src, dst):
        blank = jnp.zeros((CELL - WIN, D), F32)
        for r in range(GRID):
            line = src[r].astype(F32)
            for wc in range(SIDE):
                cells = jnp.concatenate([line[wc * WIN : (wc + 1) * WIN], blank], axis=0)
                C[pl.ds(wc * HALF + r * CELL, CELL), :] = cells
        dst[...] = C[...].astype(BF)

    def unpad(dst):
        for r in range(GRID):
            sides = [C[pl.ds(wc * HALF + r * CELL, CELL), :][:WIN] for wc in range(SIDE)]
            dst[r] = jnp.concatenate(sides, axis=0).astype(BF)

    @pl.when(early)
    def _():
        cot_out.start()
        pad(img, ubuf.at[0, 0])

    @pl.when(jnp.logical_not(early))
    def _():
        img_out.start()
        pad(cot, gin.at[1])

    index = lax.broadcasted_iota(jnp.int32, (ROWS, LANE), 0)
    cell = lax.rem(index, CELL)
    row = lax.rem(index, HALF) // CELL
    column = (index // HALF) * WIN + cell
    for m in range(2):
        inside = (row < WIN * wrows[c + 2 * m]) & (column < WIN * wcols[c + 2 * m]) & (cell < WIN)
        msk[m] = jnp.where(inside, 1.0, 0.0)

    for wc in range(SIDE):
        U[wc, 0] = jnp.zeros((CELL, D), F32)
        U[wc, GRID + 1] = jnp.zeros((CELL, D), F32)
    sgp[...] = jnp.zeros(sgp.shape, F32)

    def u_hop(m):
        return remote(uout.at[m], ubuf.at[0, m], hs.at[m], usem.at[m], opposite)

    def g_hop(m):
        return remote(gout.at[m], gin.at[m], hs.at[m], gsem.at[m], opposite)

    def factor_copies(k, m, local):
        slot = m if local else 2 + m
        rows = pl.ds(pl.multiple_of(slot * ROWS, 16), ROWS)
        if k == 0:
            parts = [
                ("F", zb.at[0, m], fa.at[rows, :]),
                ("F", ob.at[m], fb.at[rows, :]),
                ("F", ab.at[m, :, pl.ds(0, FF // 2)], f2.at[rows, :]),
                ("M", gin.at[m], fg.at[rows, :]),
                ("G", gatt.at[m], fr.at[rows, pl.ds(3 * D, D)]),
                ("A", dqk.at[m], fr.at[rows, pl.ds(0, 3 * D)]),
            ]
        else:
            parts = [
                ("F", zb.at[1, m], fa.at[rows, :]),
                ("F", ab.at[m, :, pl.ds(FF // 2, FF // 2)], f2.at[rows, :]),
                ("M", gin.at[m], fg.at[rows, :]),
                ("M", hb.at[m], fr.at[rows, :]),
            ]
        made = []
        for i, (when, src, dst) in enumerate(parts):
            if local:
                made.append((when, pltpu.make_async_copy(src, dst, ls.at[m, i])))
            else:
                made.append((when, remote(src, dst, ss.at[m, i], rsem.at[m, i], mate)))
        return made

    def start_factors(m, which):
        for k in range(2):
            for local in (True, False):

                @pl.when((c == k) if local else (c != k))
                def _():
                    for when, copy in factor_copies(k, m, local):
                        if when == which:
                            copy.start()

    def forward(m, p):
        @pl.when(jnp.logical_not(early))
        def _():
            u_hop(m).wait_recv()

        @pl.when(early & (m == 1))
        def _():
            img_out.wait_recv()
            pad(raw, ubuf.at[0, 1])

        once = p == 0

        def first_time(k, i):
            @pl.when(once)
            def _():
                wait_weight(k, i)

        first_time(0, 5)
        front_forward(0, m, ubuf, msk, pr, U, C, zb, xh, rs)
        for i in range(3):
            first_time(0, i)
            qkv[m, :, pl.ds(i * D, D)] = dot(zb[0, m], wf[0, :, pl.ds(i * D, D)]).astype(BF).astype(F32)

        @pl.when(early)
        def _():
            window_forward(m, qkv, pw, T)

        @pl.when(jnp.logical_not(early))
        def _():
            channel_forward(m, qkv, pc, T, msk)

        first_time(0, 3)
        ob[m] = T[...].astype(BF)
        ubuf[1, m] = (C[...] + dot(ob[m], wf[0, :, pl.ds(3 * D, D)])).astype(BF)

        first_time(1, 5)
        front_forward(1, m, ubuf, msk, pr, U, C, zb, xh, rs)
        for i in range(4):
            first_time(1, i)
        first_time(0, 4)
        first_time(1, 4)

        for t in range(FF // FTILE):
            cols = pl.ds(t * FTILE, FTILE)
            a, d = gelu_parts(dot(zb[1, m], wf[1, :, cols]))
            ab[m, :, cols] = a.astype(BF)
            db[m, :, cols] = d.astype(BF)
        uout[m] = (C[...] + dot(ab[m], w2[...])).astype(BF)

        @pl.when(early)
        def _():
            u_hop(m).start()

        @pl.when(jnp.logical_not(early))
        def _():
            for l in range(D // LANE):
                cols = pl.ds(l * LANE, LANE)
                C[:, cols] = uout[m, :, cols].astype(F32) * msk[m]
            unpad(flat.at[m])

        @pl.when(jnp.logical_not(early) & (m == 0))
        def _():
            remote(flat.at[0], act, es.at[0], er.at[0], opposite).start()

        @pl.when(jnp.logical_not(early) & (m == 1))
        def _():
            pltpu.make_async_copy(flat.at[1], act, es.at[0]).start()

        start_factors(m, "F")

    def backward(m):
        @pl.when(early)
        def _():
            g_hop(m).wait_recv()

        @pl.when(jnp.logical_not(early))
        def _():
            @pl.when(m == 0)
            def _():
                cot_out.wait_recv()
                pad(raw, gin.at[0])

            for l in range(D // LANE):
                cols = pl.ds(l * LANE, LANE)
                gin[m, :, cols] = (gin[m, :, cols].astype(F32) * msk[m]).astype(BF)

        for t in range(FF // FTILE):
            cols = pl.ds(t * FTILE, FTILE)
            da = dot(gin[m], w2[cols, :], 1, 1)
            hb[m, :, cols] = (da * db[m, :, cols].astype(F32)).astype(BF)
        T[...] = dot(hb[m], wf[1], 1, 1)
        start_factors(m, "M")
        front_backward(1, m, ubuf, msk, pr, U, T, gin, xh, rs, sgp, gatt)
        start_factors(m, "G")
        T[...] = dot(gatt[m], wf[0, :, pl.ds(3 * D, D)], 1, 1)

        @pl.when(early)
        def _():
            window_backward(m, qkv, pw, T, Q)

        @pl.when(jnp.logical_not(early))
        def _():
            channel_backward(m, qkv, pc, T, Q, msk)

        for i in range(3):
            cols = pl.ds(i * D, D)
            dqk[m, :, cols] = Q[:, cols].astype(BF)
        start_factors(m, "A")
        T[...] = dot(dqk[m], wf[0, :, pl.ds(0, 3 * D)], 1, 1)
        front_backward(0, m, ubuf, msk, pr, U, T, gatt, xh, rs, sgp, gout)

        @pl.when(jnp.logical_not(early))
        def _():
            g_hop(m).start()

        @pl.when(early)
        def _():
            C[...] = gout[m].astype(F32)
            unpad(flat.at[m])

        @pl.when(early & (m == 0))
        def _():
            pltpu.make_async_copy(flat.at[0], ing, es.at[1]).start()

        @pl.when(early & (m == 1))
        def _():
            remote(flat.at[1], ing, es.at[1], er.at[1], opposite).start()

    def phase(p, carry):
        m = jnp.where(early, lax.rem(p, 2), p // 2)
        ahead = jnp.where(early, p < 2, lax.rem(p, 2) == 0)

        @pl.when(ahead)
        def _():
            forward(m, p)

        @pl.when(jnp.logical_not(ahead))
        def _():
            backward(m)

        return carry

    lax.fori_loop(0, 4, phase, 0)

    for sec in range(2):
        for j in range(12):
            sgs[sec, j : j + 1, :] = jnp.sum(sgp[sec, j], axis=0, keepdims=True)
        sgs[sec, 12:16, :] = jnp.zeros((4, D), F32)
    keep = pltpu.make_async_copy(sgs.at[c], sg_own, sgsem.at[0])
    give = remote(sgs.at[1 - c], sg_mate, sgsem.at[1], sgsem.at[2], mate)
    keep.start()
    give.start()

    for k in range(2):

        @pl.when(c == k)
        def _():
            for copy in weight_copies(k)[1]:
                copy.wait_send()
            params_copy(k).wait_send()
            for m in range(2):
                for _when, copy in factor_copies(k, m, True):
                    copy.wait()
                for _when, copy in factor_copies(1 - k, m, False):
                    copy.wait_send()
                for _when, copy in factor_copies(k, m, False):
                    copy.wait_recv()

    keep.wait()
    give.wait()

    @pl.when(early)
    def _():
        cot_out.wait_send()
        for m in range(2):
            u_hop(m).wait_send()
        pltpu.make_async_copy(flat.at[0], ing, es.at[1]).wait()
        remote(flat.at[1], ing, es.at[1], er.at[1], opposite).wait_send()
        remote(flat.at[0], act, es.at[0], er.at[0], opposite).wait_recv()

    @pl.when(jnp.logical_not(early))
    def _():
        img_out.wait_send()
        for m in range(2):
            g_hop(m).wait_send()
        remote(flat.at[0], act, es.at[0], er.at[0], opposite).wait_send()
        pltpu.make_async_copy(flat.at[1], act, es.at[0]).wait()
        remote(flat.at[1], ing, es.at[1], er.at[1], opposite).wait_recv()


def relay(wrows, wcols, img, cot, kern, bias, gain, move, first, second):
    shape = jax.ShapeDtypeStruct
    vmem = pl.BlockSpec(memory_space=pltpu.VMEM)
    anywhere = pl.BlockSpec(memory_space=pl.ANY)
    dma = pltpu.SemaphoreType.DMA
    smem = pl.BlockSpec(memory_space=pltpu.SMEM)
    image = (ROWS, D)
    slot = img.shape
    return pl.pallas_call(
        relay_kernel,
        out_shape=[
            shape(slot, BF),
            shape(slot, BF),
            shape((4 * ROWS, D), BF),
            shape((4 * ROWS, D), BF),
            shape((4 * ROWS, FF), BF),
            shape((4 * ROWS, FF // 2), BF),
            shape((4 * ROWS, D), BF),
            shape((16, D), F32),
            shape((16, D), F32),
        ],
        in_specs=[smem] * 2 + [vmem] * 6 + [anywhere] * 2,
        out_specs=[anywhere] * 9,
        scratch_shapes=[
            pltpu.VMEM((2, D, FF), BF),
            pltpu.VMEM((FF, D), BF),
            pltpu.VMEM((2, 16, D), F32),
            pltpu.VMEM((2, ROWS, LANE), F32),
            pltpu.VMEM(slot, BF),
            pltpu.VMEM((2,) + slot, BF),
            pltpu.VMEM((2, 2) + image, BF),
            pltpu.VMEM((2,) + image, BF),
            pltpu.VMEM((2,) + image, BF),
            pltpu.VMEM((2,) + image, BF),
            pltpu.VMEM((2,) + image, BF),
            pltpu.VMEM((2, 2) + image, BF),
            pltpu.VMEM((2, 2) + image, BF),
            pltpu.VMEM((2, 2, ROWS, LANE), F32),
            pltpu.VMEM((2, ROWS, 3 * D), F32),
            pltpu.VMEM((2,) + image, BF),
            pltpu.VMEM((2, ROWS, FF), BF),
            pltpu.VMEM((2, ROWS, FF), BF),
            pltpu.VMEM((2, ROWS, FF), BF),
            pltpu.VMEM((2, ROWS, 3 * D), BF),
            pltpu.VMEM((2, UNITS, PACK * WROWS, WROWS), F32),
            pltpu.VMEM((2, NGROUP, GROUP, GROUP), F32),
            pltpu.VMEM((SIDE, GRID + 2, CELL, D), F32),
            pltpu.VMEM(image, F32),
            pltpu.VMEM(image, F32),
            pltpu.VMEM((ROWS, 3 * D), F32),
            pltpu.VMEM((2, 12, CELL, D), F32),
            pltpu.VMEM((2, 16, D), F32),
            dma((6,)),
            dma((6,)),
            dma((6,)),
            dma((2,)),
            dma((2,)),
            dma((2,)),
            dma((2,)),
            dma((2, 6)),
            dma((2, 6)),
            dma((2, 6)),
            dma((2,)),
            dma((2,)),
            dma((3,)),
        ],
        name="relay",
        compiler_params=pltpu.CompilerParams(
            collective_id=1, has_side_effects=True, vmem_limit_bytes=60 * 2**20
        ),
    )(wrows, wcols, img, cot, kern, bias, gain, move, first, second)


RING = 8
COLS = FF // RING
TAIL = FF // 2 // RING


def ring_kernel(
    n, fa, fb, fr, f2, fg, sg_own, sg_mate,
    out1, out2, outs,
    la, r1, a2, g2, lt, at, buf, ag, acc, got,
    lsem, ss, rs, os_, sms, smr,
):
    s = lax.axis_index("section")
    dp = lax.axis_index("dp")
    c = lax.rem(s, 2)
    tokens = la.shape[1]

    def place(pos):
        pos = lax.rem(pos + 2 * n, n)
        return jnp.where(pos < n // 2, 2 * pos, 2 * (n - 1 - pos) + 1)

    me = jnp.where(lax.rem(dp, 2) == 0, dp // 2, n - 1 - dp // 2)
    nexts = (place(me + 1), place(me - 1))
    rounds = n.bit_length() - 1
    partners = []
    for r in range(rounds):
        bit = 1 << r
        partners.append(jnp.where(lax.rem(dp // bit, 2) == 0, dp + bit, dp - bit))

    barrier = pltpu.get_barrier_semaphore()
    peers = list(nexts) + partners
    for peer in peers:
        pl.semaphore_signal(barrier, inc=1, device_id=(peer, s), device_id_type=MESH)

    loads = [
        pltpu.make_async_copy(fa, la.at[0], lsem.at[0]),
        pltpu.make_async_copy(fr, r1, lsem.at[1]),
        pltpu.make_async_copy(f2, a2, lsem.at[2]),
        pltpu.make_async_copy(fg, g2, lsem.at[3]),
        pltpu.make_async_copy(fb, la.at[1], lsem.at[4]),
    ]
    for copy in loads[:4]:
        copy.start()

    @pl.when(c == 0)
    def _():
        loads[4].start()

    def turn(src, dst, count):
        def body(i, carry):
            dst[lanes(i), :] = src[:, lanes(i)].T
            return carry

        lax.fori_loop(0, count, body, 0)

    def shard(k):
        return lax.rem(k + 2 * n, n)

    def tile1(h, j):
        sel = jnp.where((c == 0) & (j >= (3 * n) // 4), 1, 0)
        return dot(lt[sel, pl.ds(h * COLS, COLS), :], r1[:, lanes(j, COLS)])

    def tile2(h, j):
        rows = pl.ds(pl.multiple_of(j * TAIL, 16), TAIL)
        return dot(at[rows, :], g2[:, pl.ds(h * COLS, COLS)])

    parts = (pl.ds(0, COLS), pl.ds(COLS, TAIL))
    tiles = (tile1, tile2)

    def scatter(h, t, sub):
        return pltpu.make_async_remote_copy(
            src_ref=buf.at[h, t, parts[sub], :],
            dst_ref=buf.at[h, t + 1, parts[sub], :],
            send_sem=ss.at[h, t, sub],
            recv_sem=rs.at[h, t + 1, sub],
            device_id=(nexts[h], s),
            device_id_type=MESH,
        )

    def spread(h, t, sub, j):
        return pltpu.make_async_remote_copy(
            src_ref=ag.at[h, j, parts[sub], :],
            dst_ref=ag.at[h, j, parts[sub], :],
            send_sem=ss.at[h, n - 1 + t, sub],
            recv_sem=rs.at[h, n + t, sub],
            device_id=(nexts[h], s),
            device_id_type=MESH,
        )

    def write(h, j, sub):
        cols = lanes(j, COLS)
        if sub == 0:
            dst = out1.at[pl.ds(h * COLS, COLS), cols]
        else:
            dst = out2.at[pl.ds(pl.multiple_of(j * TAIL, 16), TAIL), pl.ds(h * COLS, COLS)]
        return pltpu.make_async_copy(ag.at[h, j, parts[sub], :], dst, os_.at[h, j, sub])

    def sign(h):
        return 1 if h == 0 else -1

    loads[0].wait()
    turn(la.at[0], lt.at[0], D // LANE)

    @pl.when(c == 0)
    def _():
        loads[4].wait()
        turn(la.at[1], lt.at[1], D // LANE)

    loads[1].wait()
    pl.semaphore_wait(barrier, len(peers))
    for h in range(2):
        buf[h, 0, parts[0], :] = tile1(h, me).astype(BF)
        scatter(h, 0, 0).start()
    loads[2].wait()
    loads[3].wait()
    turn(a2, at, FF // 2 // LANE)
    for h in range(2):
        buf[h, 0, parts[1], :] = tile2(h, me).astype(BF)
        scatter(h, 0, 1).start()

    acc[0] = sg_own[...] + sg_mate[...]

    def reduce_step(t, carry):
        for sub in range(2):
            for h in range(2):
                own = tiles[sub](h, shard(me - sign(h) * t))
                scatter(h, t - 1, sub).wait_recv()
                buf[h, t, parts[sub], :] = (own + buf[h, t, parts[sub], :].astype(F32)).astype(BF)
                scatter(h, t, sub).start()
        return carry

    lax.fori_loop(1, n - 1, reduce_step, 0)

    def home(h, t):
        return shard(me + sign(h) - sign(h) * t)

    for sub in range(2):
        for h in range(2):
            j = home(h, 0)
            own = tiles[sub](h, j)
            scatter(h, n - 2, sub).wait_recv()
            ag[h, j, parts[sub], :] = (own + buf[h, n - 1, parts[sub], :].astype(F32)).astype(BF)
            spread(h, 0, sub, j).start()
            write(h, j, sub).start()

    def small(r):
        return pltpu.make_async_remote_copy(
            src_ref=acc.at[r],
            dst_ref=got.at[r],
            send_sem=sms.at[r],
            recv_sem=smr.at[r],
            device_id=(partners[r], s),
            device_id_type=MESH,
        )

    small(0).start()
    for t in range(1, n):
        for sub in range(2):
            for h in range(2):
                j = home(h, t)
                spread(h, t - 1, sub, j).wait_recv()
                if t < n - 1:
                    spread(h, t, sub, j).start()
                write(h, j, sub).start()
        if t % 2 == 0 and t // 2 <= rounds:
            r = t // 2 - 1
            small(r).wait_recv()
            acc[r + 1] = acc[r] + got[r]
            if r + 1 < rounds:
                small(r + 1).start()
    outs[...] = acc[rounds]

    def drain(t, carry):
        for sub in range(2):
            for h in range(2):
                scatter(h, t, sub).wait_send()
        return carry

    lax.fori_loop(0, n - 1, drain, 0)
    for t in range(n - 1):
        for sub in range(2):
            for h in range(2):
                spread(h, t, sub, home(h, t)).wait_send()
    for j in range(n):
        for sub in range(2):
            for h in range(2):
                write(h, j, sub).wait()
    for r in range(rounds):
        small(r).wait_send()


def ring_reduce(n, fa, fb, fr, f2, fg, sg_own, sg_mate):
    shape = jax.ShapeDtypeStruct
    vmem = pl.BlockSpec(memory_space=pltpu.VMEM)
    anywhere = pl.BlockSpec(memory_space=pl.ANY)
    dma = pltpu.SemaphoreType.DMA
    tokens = fa.shape[0]
    rounds = n.bit_length() - 1
    block = (COLS + TAIL, COLS)
    return pl.pallas_call(
        partial(ring_kernel, n),
        out_shape=[shape((D, FF), BF), shape((FF // 2, D), BF), shape((16, D), F32)],
        in_specs=[anywhere] * 5 + [vmem] * 2,
        out_specs=[anywhere, anywhere, vmem],
        scratch_shapes=[
            pltpu.VMEM((2, tokens, D), BF),
            pltpu.VMEM((tokens, FF), BF),
            pltpu.VMEM((tokens, FF // 2), BF),
            pltpu.VMEM((tokens, D), BF),
            pltpu.VMEM((2, D, tokens), BF),
            pltpu.VMEM((FF // 2, tokens), BF),
            pltpu.VMEM((2, n) + block, BF),
            pltpu.VMEM((2, n) + block, BF),
            pltpu.VMEM((rounds + 1, 16, D), F32),
            pltpu.VMEM((rounds, 16, D), F32),
            dma((5,)),
            dma((2, 2 * n, 2)),
            dma((2, 2 * n, 2)),
            dma((2, n, 2)),
            dma((rounds,)),
            dma((rounds,)),
        ],
        name="ring",
        compiler_params=pltpu.CompilerParams(
            collective_id=2, has_side_effects=True, vmem_limit_bytes=60 * 2**20
        ),
    )(fa, fb, fr, f2, fg, sg_own, sg_mate)


def plain_reduce(fa, fb, fr, f2, fg, sg_own, sg_mate):
    even = lax.rem(lax.axis_index("section"), 2) == 0
    left = jnp.where(even, fb, fa)
    qkv = dot(fa, fr[:, : 3 * D], 0, 0)
    last = dot(left, fr[:, 3 * D :], 0, 0)
    out1 = jnp.concatenate([qkv, last], axis=1)
    out2 = dot(f2, fg, 0, 0)
    return lax.psum((out1.astype(BF), out2.astype(BF), sg_own + sg_mate), "dp")


def per_device(
    images, cotangent, window_rows, window_cols, pos_kernel, pos_bias, norm_gain, norm_shift, first_weight, second_weight
):
    act, ing, fa, fb, fr, f2, fg, sg_own, sg_mate = relay(
        window_rows, window_cols, images[0], cotangent[0], pos_kernel[0], pos_bias, norm_gain, norm_shift,
        first_weight[0], second_weight,
    )
    n = lax.axis_size("dp")
    reduce = partial(ring_reduce, n) if n == RING else plain_reduce
    out1, out2, outs = reduce(fa, fb, fr, f2, fg, sg_own, sg_mate)
    return (
        act[None],
        ing.astype(F32)[None],
        out1.astype(F32)[None],
        out2.astype(F32),
        outs[None, :9],
        outs[9:10],
        outs[10:11],
        outs[11:12],
    )


def solution(mesh):
    in_specs = (
        P(("dp", "section"), None, None, None),
        P(("dp", "section"), None, None, None),
        P("dp"),
        P("dp"),
        P("section", None, None),
        P("section", None),
        P("section", None),
        P("section", None),
        P("section", None, None),
        P("section", None),
    )
    out_specs = (
        P(("dp", "section"), None, None, None),
        P(("dp", "section"), None, None, None),
        P("section", None, None),
        P("section", None),
        P("section", None, None),
        P("section", None),
        P("section", None),
        P("section", None),
    )
    return jax.shard_map(per_device, mesh=mesh, in_specs=in_specs, out_specs=out_specs, check_vma=False)
```

```python
from functools import partial

import jax
import jax.numpy as jnp
from jax import lax
from jax.experimental import pallas as pl
from jax.experimental.pallas import tpu as pltpu
from jax.sharding import PartitionSpec as P

D = 768
FF = 3072
HEADS = 24
HEAD = 32
WIN = 7
SIDE = 2
GRID = SIDE * WIN
CELL = 8
WROWS = WIN * CELL
HALF = GRID * CELL
ROWS = SIDE * HALF
GROUP = 256
PACK = GROUP // HEAD
NGROUP = D // GROUP
UNITS = NGROUP * SIDE * SIDE
LANE = 128
FTILE = 1024
EPS = 1e-05
SCALE = HEAD ** (-0.5)
BF = jnp.bfloat16
F32 = jnp.float32
MESH = pl.DeviceIdType.MESH


def dot(a, b, ca=1, cb=0):
    return lax.dot_general(a, b, (((ca,), (cb,)), ((), ())), preferred_element_type=F32)


def lanes(index, width=LANE):
    return pl.ds(pl.multiple_of(index * width, width), width)


def halves(value):
    return value.reshape(SIDE, GRID, CELL, value.shape[-1])


def shifts(left, right):
    column = lax.broadcasted_iota(jnp.int32, left.shape, 1)
    before0 = pltpu.roll(left, 1, 1)
    after0 = jnp.where(column == WIN - 1, pltpu.roll(right, CELL - 2, 1), pltpu.roll(left, CELL - 1, 1))
    before1 = jnp.where(column == 0, pltpu.roll(left, 2, 1), pltpu.roll(right, 1, 1))
    after1 = pltpu.roll(right, CELL - 1, 1)
    return ((before0, left, after0), (before1, right, after1))


def gelu_parts(h):
    expo = jnp.exp(h * h * -0.5)
    t = 1.0 / (1.0 + (0.3275911 * 0.7071067811865476) * jnp.abs(h))
    poly = t * (0.127414796 + t * (-0.142248368 + t * (0.7107068705 + t * (-0.7265760135 + t * 0.5307027145))))
    tail = poly * expo
    phi = jnp.where(h >= 0, 1.0 - tail, tail)
    return h * phi, phi + h * expo * 0.3989422804014327


def front_forward(sec, m, ubuf, msk, pr, U, C, zz, xh, rs):
    zero = jnp.zeros((ROWS, LANE), F32)

    def conv(i, total):
        ls = lanes(i)
        u = ubuf[sec, m, :, ls].astype(F32)
        masked = halves(u * msk[m])
        U[0, 1 : GRID + 1, :, ls] = masked[0]
        U[1, 1 : GRID + 1, :, ls] = masked[1]
        moved = shifts(U[0, :, :, ls], U[1, :, :, ls])
        taps = pr[sec, :, ls]
        uh = halves(u)
        sums = []
        for wc in range(SIDE):
            acc = uh[wc] + taps[9:10, :][None]
            for a in range(3):
                for b in range(3):
                    acc = acc + moved[wc][b][a : a + GRID] * taps[3 * a + b : 3 * a + b + 1, :][None]
            acc = acc.reshape(HALF, LANE)
            C[pl.ds(wc * HALF, HALF), ls] = acc
            sums.append(acc)
        return total + jnp.concatenate(sums, axis=0)

    mean = jnp.sum(lax.fori_loop(0, D // LANE, conv, zero), axis=-1, keepdims=True) * (1.0 / D)

    def spread(i, total):
        centred = C[:, lanes(i)] - mean
        return total + centred * centred

    var = jnp.sum(lax.fori_loop(0, D // LANE, spread, zero), axis=-1, keepdims=True) * (1.0 / D)
    rstd = lax.rsqrt(var + EPS)
    rs[sec, m] = jnp.broadcast_to(rstd, (ROWS, LANE))

    def norm(i, carry):
        ls = lanes(i)
        xhat = (C[:, ls] - mean) * rstd
        xh[sec, m, :, ls] = xhat.astype(BF)
        zz[m, 2 * sec, :, ls] = (xhat * pr[sec, 10:11, ls] + pr[sec, 11:12, ls]).astype(BF)
        return carry

    lax.fori_loop(0, D // LANE, norm, 0)


def front_backward(sec, m, ubuf, msk, pr, U, T, gfull, xh, rs, sgp, out):
    zero = jnp.zeros((ROWS, LANE), F32)

    def fold(value):
        return jnp.sum(value.reshape(ROWS // CELL, CELL, LANE), axis=0)

    def sums(i, carry):
        s1, s2 = carry
        ls = lanes(i)
        dz = T[:, ls]
        xhat = xh[sec, m, :, ls].astype(F32)
        both = xhat * dz
        sgp[sec, 10, :, ls] += fold(both)
        sgp[sec, 11, :, ls] += fold(dz)
        gain = pr[sec, 10:11, ls]
        return s1 + dz * gain, s2 + both * gain

    s1, s2 = lax.fori_loop(0, D // LANE, sums, (zero, zero))
    m1 = jnp.sum(s1, axis=-1, keepdims=True) * (1.0 / D)
    m2 = jnp.sum(s2, axis=-1, keepdims=True) * (1.0 / D)

    def back(i, carry):
        ls = lanes(i)
        xhat = xh[sec, m, :, ls].astype(F32)
        inner = T[:, ls] * pr[sec, 10:11, ls] - m1 - xhat * m2
        gc = gfull(i)[...].astype(F32) + rs[sec, m] * inner
        sgp[sec, 9, :, ls] += fold(gc)
        gh = halves(gc)
        U[0, 1 : GRID + 1, :, ls] = gh[0]
        U[1, 1 : GRID + 1, :, ls] = gh[1]
        moved = shifts(U[0, :, :, ls], U[1, :, :, ls])
        taps = pr[sec, :, ls]
        mask = halves(msk[m])
        um = halves(ubuf[sec, m, :, ls].astype(F32) * msk[m])
        accs = [jnp.zeros((GRID, CELL, LANE), F32) for _ in range(SIDE)]
        for a in range(3):
            for b in range(3):
                tap = 3 * a + b
                kg = jnp.zeros((CELL, LANE), F32)
                for wc in range(SIDE):
                    gs = moved[wc][2 - b][2 - a : 2 - a + GRID]
                    accs[wc] = accs[wc] + gs * taps[tap : tap + 1, :][None]
                    kg = kg + jnp.sum(gs * um[wc], axis=0)
                sgp[sec, tap, :, ls] += kg
        du = [(gh[wc] + mask[wc] * accs[wc]).reshape(HALF, LANE) for wc in range(SIDE)]
        out(i)[...] = jnp.concatenate(du, axis=0).astype(BF)
        return carry

    lax.fori_loop(0, D // LANE, back, 0)


def spread_heads(value, head_of_lane):
    parts = [jnp.where(head_of_lane == h, value, 0.0) for h in range(PACK)]
    return jnp.concatenate(parts, axis=0).astype(BF)


def gather_heads(value, rows, head_of_lane):
    out = jnp.zeros((rows, GROUP), F32)
    for h in range(PACK):
        out = jnp.where(head_of_lane == h, value[h * rows : (h + 1) * rows], out)
    return out


def unit_slices(unit):
    pair, group = unit // NGROUP, lax.rem(unit, NGROUP)
    rows = [pl.ds(pl.multiple_of((2 * pair + w) * WROWS, 8), WROWS) for w in range(2)]
    cols = [pl.ds(pl.multiple_of(part * D + group * GROUP, LANE), GROUP) for part in range(3)]
    return rows, cols


def window_parts(m, i, qkv):
    rows, cols = unit_slices(i)
    head_of_lane = lax.broadcasted_iota(jnp.int32, (WROWS, GROUP), 1) // HEAD
    q = [qkv[m, r, cols[0]].astype(BF) for r in rows]
    kd = [spread_heads(qkv[m, r, cols[1]], head_of_lane) for r in rows]
    vd = [spread_heads(qkv[m, r, cols[2]], head_of_lane) for r in rows]
    return rows, cols, head_of_lane, q, kd, vd


def window_forward(m, qkv, pw, T):
    def unit(i, carry):
        rows, cols, head_of_lane, q, kd, vd = window_parts(m, i, qkv)
        s = [(dot(b, a, 1, 1) * SCALE).reshape(PACK, WROWS, WROWS) for a, b in zip(q, kd)]
        key = lax.broadcasted_iota(jnp.int32, s[0].shape, 1)
        real = lax.rem(key, CELL) < WIN
        s = [jnp.where(real, x, -1e30) for x in s]
        p = [jnp.exp(x - jnp.max(x, axis=1, keepdims=True)) for x in s]
        p = [x * (1.0 / jnp.sum(x, axis=1, keepdims=True)) for x in p]
        p = [x.reshape(PACK * WROWS, WROWS) for x in p]
        for w in range(2):
            pw[m, 2 * i + w] = p[w]
        out = [dot(x.astype(BF), v, 0, 0) for x, v in zip(p, vd)]
        for w in range(2):
            T[rows[w], cols[0]] = out[w]
        return carry

    lax.fori_loop(0, UNITS // 2, unit, 0)


def window_backward(m, qkv, pw, T, Q):
    def unit(i, carry):
        rows, cols, head_of_lane, q, kd, vd = window_parts(m, i, qkv)
        g = [T[r, cols[0]].astype(BF) for r in rows]
        p = [pw[m, 2 * i + w].reshape(PACK, WROWS, WROWS) for w in range(2)]
        dp = [dot(v, x, 1, 1).reshape(PACK, WROWS, WROWS) for v, x in zip(vd, g)]
        ds = [x * (y - jnp.sum(x * y, axis=1, keepdims=True)) for x, y in zip(p, dp)]
        ds = [x.reshape(PACK * WROWS, WROWS).astype(BF) for x in ds]
        pb = [x.reshape(PACK * WROWS, WROWS).astype(BF) for x in p]
        dv = [gather_heads(dot(x, y), WROWS, head_of_lane) for x, y in zip(pb, g)]
        dk = [gather_heads(dot(x, y), WROWS, head_of_lane) * SCALE for x, y in zip(ds, q)]
        dq = [dot(x, y, 0, 0) * SCALE for x, y in zip(ds, kd)]
        for w in range(2):
            Q[rows[w], cols[0]] = dq[w]
            Q[rows[w], cols[1]] = dk[w]
            Q[rows[w], cols[2]] = dv[w]
        return carry

    lax.fori_loop(0, UNITS // 2, unit, 0)


def group_slices(group):
    return [pl.ds(pl.multiple_of(part * D + group * GROUP, LANE), GROUP) for part in range(3)]


def channel_forward(m, qkv, pc, T, msk):
    def unit(i, carry):
        cols = group_slices(i)
        mask = msk[m][:, :1]
        q = qkv[m, :, cols[0]].astype(BF)
        k = (qkv[m, :, cols[1]] * mask).astype(BF)
        v = qkv[m, :, cols[2]].astype(BF)
        s = dot(q, k, 0, 0) * SCALE
        same = (lax.broadcasted_iota(jnp.int32, s.shape, 0) // HEAD) == (lax.broadcasted_iota(jnp.int32, s.shape, 1) // HEAD)
        s = jnp.where(same, s, -1e30)
        p = jnp.exp(s - jnp.max(s, axis=1, keepdims=True))
        p = p * (1.0 / jnp.sum(p, axis=1, keepdims=True))
        pc[m, i] = p
        T[:, cols[0]] = dot(v, p.astype(BF), 1, 1)
        return carry

    lax.fori_loop(0, NGROUP, unit, 0, unroll=True)


def channel_backward(m, qkv, pc, T, Q, msk):
    def unit(i, carry):
        cols = group_slices(i)
        mask = msk[m][:, :1]
        q = qkv[m, :, cols[0]].astype(BF)
        k = (qkv[m, :, cols[1]] * mask).astype(BF)
        v = qkv[m, :, cols[2]].astype(BF)
        g = T[:, cols[0]].astype(BF)
        p = pc[m, i]
        dp = dot(g, v, 0, 0)
        ds = (p * (dp - jnp.sum(p * dp, axis=1, keepdims=True))).astype(BF)
        Q[:, cols[0]] = dot(k, ds, 1, 1) * SCALE
        Q[:, cols[1]] = dot(q, ds) * (SCALE * mask)
        Q[:, cols[2]] = dot(g, p.astype(BF))
        return carry

    lax.fori_loop(0, NGROUP, unit, 0, unroll=True)


RING = 8
COLS = FF // RING
TAIL = FF // 2 // RING
EARLY = 2


def relay_kernel(
    wrows, wcols, img, cot, kern, bias, gain, move, first, second,
    act, ing, out1, out2, outs,
    wf, w2, pr, msk, raw, flat, ubuf, gin, gout, uout, zz, xh, rs, qkv, ab, rr, pw, pc, U, C, T, Q, sgp, sgs, sgm,
    rL, rR, rA, rG, buf, acc, got,
    wl, ws, wr, pl_, usem, gsem, us, gs, ss, rsem, es, er, sgsem, ssem, rcem, osem, sms, smr, free,
):
    n = RING
    s = lax.axis_index("section")
    dp = lax.axis_index("dp")
    stage, c = s // 2, lax.rem(s, 2)
    mate = (dp, stage * 2 + (1 - c))
    opposite = (dp, (1 - stage) * 2 + c)
    early = stage == 0

    spot = lax.rem(dp, n)
    base = dp - spot
    me = jnp.where(lax.rem(spot, 2) == 0, spot // 2, n - 1 - spot // 2)

    def place(pos):
        pos = lax.rem(pos + 2 * n, n)
        return (base + jnp.where(pos < n // 2, 2 * pos, 2 * (n - 1 - pos) + 1), s)

    nexts = (place(me + 1), place(me - 1))
    rounds = n.bit_length() - 1
    partners = []
    for r in range(rounds):
        bit = 1 << r
        partners.append((jnp.where(lax.rem(spot // bit, 2) == 0, dp + bit, dp - bit), s))

    barrier = pltpu.get_barrier_semaphore()
    peers = [mate, opposite, *nexts, *partners]
    for peer in peers:
        pl.semaphore_signal(barrier, inc=1, device_id=peer, device_id_type=MESH)
    pl.semaphore_wait(barrier, len(peers))

    def remote(src, dst, send, recv, peer):
        return pltpu.make_async_remote_copy(
            src_ref=src, dst_ref=dst, send_sem=send, recv_sem=recv, device_id=peer, device_id_type=MESH
        )

    half = second.shape[0]

    def weight_parts(k):
        parts = []
        for i in range(4):
            parts.append((first.at[:, pl.ds(i * D, D)], wf.at[k, :, pl.ds(i * D, D)]))
        parts.append((second, w2.at[pl.ds(k * half, half), :]))
        return parts

    def weight_copies(k):
        local = [pltpu.make_async_copy(a, b, wl.at[i]) for i, (a, b) in enumerate(weight_parts(k))]
        sent = [remote(a, b, ws.at[i], wr.at[i], mate) for i, (a, b) in enumerate(weight_parts(k))]
        return local, sent

    def params_copy(k):
        return remote(pr.at[k], pr.at[k], ws.at[5], wr.at[5], mate)

    pr[c, 0:9, :] = kern[...].astype(F32)
    pr[c, 9:10, :] = bias[...].astype(F32)
    pr[c, 10:11, :] = gain[...].astype(F32)
    pr[c, 11:12, :] = move[...].astype(F32)
    params_copy(c).start()
    for k in range(2):

        @pl.when(c == k)
        def _():
            local, sent = weight_copies(k)
            for i in range(5):
                local[i].start()
                sent[i].start()

    def wait_weight(k, i):
        if i < 5:

            @pl.when(c == k)
            def _():
                weight_copies(k)[0][i].wait()

        @pl.when(c != k)
        def _():
            (weight_copies(k)[1][i] if i < 5 else params_copy(k)).wait_recv()

    img_out = remote(img, raw, pl_.at[0], pl_.at[1], opposite)
    cot_out = remote(cot, raw, pl_.at[0], pl_.at[1], opposite)

    def pad(src, dst):
        blank = jnp.zeros((CELL - WIN, D), F32)
        for r in range(GRID):
            line = src[r].astype(F32)
            for wc in range(SIDE):
                cells = jnp.concatenate([line[wc * WIN : (wc + 1) * WIN], blank], axis=0)
                C[pl.ds(wc * HALF + r * CELL, CELL), :] = cells
        dst[...] = C[...].astype(BF)

    def unpad(dst):
        for r in range(GRID):
            sides = [C[pl.ds(wc * HALF + r * CELL, CELL), :][:WIN] for wc in range(SIDE)]
            dst[r] = jnp.concatenate(sides, axis=0).astype(BF)

    @pl.when(early)
    def _():
        cot_out.start()
        pad(img, ubuf.at[0, 0])

    @pl.when(jnp.logical_not(early))
    def _():
        img_out.start()
        pad(cot, gin.at[1])

    index = lax.broadcasted_iota(jnp.int32, (ROWS, LANE), 0)
    cell = lax.rem(index, CELL)
    row = lax.rem(index, HALF) // CELL
    column = (index // HALF) * WIN + cell
    for m in range(2):
        inside = (row < WIN * wrows[c + 2 * m]) & (column < WIN * wcols[c + 2 * m]) & (cell < WIN)
        msk[m] = jnp.where(inside, 1.0, 0.0)

    for wc in range(SIDE):
        U[wc, 0] = jnp.zeros((CELL, D), F32)
        U[wc, GRID + 1] = jnp.zeros((CELL, D), F32)
    sgp[...] = jnp.zeros(sgp.shape, F32)

    def u_hop(m):
        return remote(uout.at[m], ubuf.at[0, m], us.at[m], usem.at[m], opposite)

    def g_hop(m):
        return remote(gout.at[m], gin.at[m], gs.at[m], gsem.at[m], opposite)

    def factor_copies(k, m):
        if k == 0:
            parts = [
                ("F", zz.at[m, 0], rL.at[m, 0]),
                ("F", zz.at[m, 1], rL.at[m, 1]),
                ("F", ab.at[m, :, pl.ds(0, FF // 2)], rA.at[m]),
                ("M", gin.at[m], rG.at[m]),
                ("G", rr.at[m, 0, :, pl.ds(3 * D, D)], rR.at[m, :, pl.ds(3 * D, D)]),
                ("A", rr.at[m, 0, :, pl.ds(0, 3 * D)], rR.at[m, :, pl.ds(0, 3 * D)]),
            ]
        else:
            parts = [
                ("F", zz.at[m, 2], rL.at[m, 0]),
                ("F", ab.at[m, :, pl.ds(FF // 2, FF // 2)], rA.at[m]),
                ("M", gin.at[m], rG.at[m]),
                ("M", rr.at[m, 1], rR.at[m]),
            ]
        return [(w, remote(a, b, ss.at[m, i], rsem.at[m, i], mate)) for i, (w, a, b) in enumerate(parts)]

    def start_factors(m, which):
        for k in range(2):

            @pl.when(c != k)
            def _():
                for when, copy in factor_copies(k, m):
                    if when == which:
                        copy.start()

    def wait_factors(which):
        for k in range(2):

            @pl.when(c == k)
            def _():
                for m in range(2):
                    for when, copy in factor_copies(k, m):
                        if when in which:
                            copy.wait_recv()

    def shard(k):
        return lax.rem(k + 4 * n, n)

    def sign(h):
        return 1 if h == 0 else -1

    def home(h, t):
        return shard(me + sign(h) - sign(h) * t)

    def tile(sub, h, j):
        side = pl.ds(h * COLS, COLS)
        if sub == 0:
            last = jnp.where(j >= (3 * n) // 4, 1, 0)
            own = jnp.where(c == 1, 2, last)
            other = jnp.where(c == 1, 0, last)
            cols = lanes(j, COLS)
            terms = [(zz.at[m, own, :, side], rr.at[m, c, :, cols]) for m in range(2)]
            terms += [(rL.at[m, other, :, side], rR.at[m, :, cols]) for m in range(2)]
        else:
            mine = pl.ds(pl.multiple_of(c * (FF // 2) + (j // 2) * 2 * TAIL, LANE), 2 * TAIL)
            cols = lanes(j // 2, 2 * TAIL)
            terms = [(ab.at[m, :, mine], gin.at[m, :, side]) for m in range(2)]
            terms += [(rA.at[m, :, cols], rG.at[m, :, side]) for m in range(2)]
        total = None
        for a, b in terms:
            part = dot(a[...], b[...], 0, 0)
            total = part if total is None else total + part
        if sub == 1:
            total = jnp.where(lax.rem(j, 2) == 1, total[TAIL:], total[:TAIL])
        return total

    parts = (pl.ds(0, COLS), pl.ds(COLS, TAIL))

    def gathered(sub, h, j):
        if sub == 0:
            return wf.at[0, pl.ds(h * COLS, COLS), lanes(j, COLS)]
        return w2.at[pl.ds(pl.multiple_of(j * TAIL, 16), TAIL), pl.ds(h * COLS, COLS)]

    def scatter(h, t, sub):
        src, dst = buf.at[h, t, parts[sub], :], buf.at[h, t + 1, parts[sub], :]
        return remote(src, dst, ssem.at[h, t, sub], rcem.at[h, t + 1, sub], nexts[h])

    def spread(h, t, sub, j):
        ref = gathered(sub, h, j)
        return remote(ref, ref, ssem.at[h, n - 1 + t, sub], rcem.at[h, n + t, sub], nexts[h])

    def write(h, j, sub):
        if sub == 0:
            dst = out1.at[pl.ds(h * COLS, COLS), lanes(j, COLS)]
        else:
            dst = out2.at[pl.ds(pl.multiple_of(j * TAIL, 16), TAIL), pl.ds(h * COLS, COLS)]
        return pltpu.make_async_copy(gathered(sub, h, j), dst, osem.at[h, j, sub])

    def reduce_event(sub, h, e):
        total = tile(sub, h, shard(me - sign(h) * e))

        @pl.when(e == 0)
        def _():
            buf[h, 0, parts[sub], :] = total.astype(BF)
            scatter(h, 0, sub).start()

        @pl.when((e > 0) & (e < n - 1))
        def _():
            scatter(h, e - 1, sub).wait_recv()
            buf[h, e, parts[sub], :] = (total + buf[h, e, parts[sub], :].astype(F32)).astype(BF)
            scatter(h, e, sub).start()

        @pl.when(e == n - 1)
        def _():
            j = home(h, 0)
            scatter(h, n - 2, sub).wait_recv()
            gathered(sub, h, j)[...] = (total + buf[h, n - 1, parts[sub], :].astype(F32)).astype(BF)
            pl.semaphore_wait(free.at[h, sub], 1)
            spread(h, 0, sub, j).start()
            write(h, j, sub).start()

    def event(sub, e):
        for h in range(2):

            @pl.when(e < n)
            def _():
                reduce_event(sub, h, e)

            @pl.when((e >= n) & (e < 2 * n - 1))
            def _():
                t = e - (n - 1)
                j = home(h, t)
                spread(h, t - 1, sub, j).wait_recv()

                @pl.when(t < n - 1)
                def _():
                    spread(h, t, sub, j).start()

                write(h, j, sub).start()

    def early_event(e):
        event(1, e)

        @pl.when(c == 1)
        def _():
            event(0, e)

    def small(r):
        return remote(acc.at[r], got.at[r], sms.at[r], smr.at[r], partners[r])

    def forward(m, p):
        @pl.when(jnp.logical_not(early))
        def _():
            u_hop(m).wait_recv()

        @pl.when(early & (m == 1))
        def _():
            img_out.wait_recv()
            pad(raw, ubuf.at[0, 1])

        once = p == 0

        def first_time(k, i):
            @pl.when(once)
            def _():
                wait_weight(k, i)

        first_time(0, 5)
        front_forward(0, m, ubuf, msk, pr, U, C, zz, xh, rs)
        for i in range(3):
            first_time(0, i)
            qkv[m, :, pl.ds(i * D, D)] = dot(zz[m, 0], wf[0, :, pl.ds(i * D, D)]).astype(BF).astype(F32)

        @pl.when(early)
        def _():
            window_forward(m, qkv, pw, T)

        @pl.when(jnp.logical_not(early))
        def _():
            channel_forward(m, qkv, pc, T, msk)

        first_time(0, 3)
        zz[m, 1] = T[...].astype(BF)
        ubuf[1, m] = (C[...] + dot(zz[m, 1], wf[0, :, pl.ds(3 * D, D)])).astype(BF)

        first_time(1, 5)
        front_forward(1, m, ubuf, msk, pr, U, C, zz, xh, rs)
        for i in range(4):
            first_time(1, i)
        first_time(0, 4)
        first_time(1, 4)

        for t in range(FF // FTILE):
            cols = pl.ds(t * FTILE, FTILE)
            a, d = gelu_parts(dot(zz[m, 2], wf[1, :, cols]))
            ab[m, :, cols] = a.astype(BF)
            rr[m, 1, :, cols] = d.astype(BF)
        uout[m] = (C[...] + dot(ab[m], w2[...])).astype(BF)

        @pl.when(early)
        def _():
            u_hop(m).start()

        @pl.when(jnp.logical_not(early))
        def _():
            for l in range(D // LANE):
                cols = pl.ds(l * LANE, LANE)
                C[:, cols] = uout[m, :, cols].astype(F32) * msk[m]
            unpad(flat.at[m])

        @pl.when(jnp.logical_not(early) & (m == 0))
        def _():
            remote(flat.at[0], act, es.at[0], er.at[0], opposite).start()

        @pl.when(jnp.logical_not(early) & (m == 1))
        def _():
            pltpu.make_async_copy(flat.at[1], act, es.at[0]).start()

        start_factors(m, "F")

    def backward(m):
        @pl.when(early)
        def _():
            g_hop(m).wait_recv()

        @pl.when(jnp.logical_not(early))
        def _():
            @pl.when(m == 0)
            def _():
                cot_out.wait_recv()
                pad(raw, gin.at[0])

            for l in range(D // LANE):
                cols = pl.ds(l * LANE, LANE)
                gin[m, :, cols] = (gin[m, :, cols].astype(F32) * msk[m]).astype(BF)

        for t in range(FF // FTILE):
            cols = pl.ds(t * FTILE, FTILE)
            da = dot(gin[m], w2[cols, :], 1, 1)
            rr[m, 1, :, cols] = (da * rr[m, 1, :, cols].astype(F32)).astype(BF)
        T[...] = dot(rr[m, 1], wf[1], 1, 1)
        start_factors(m, "M")
        last = pl.ds(3 * D, D)

        def tail_lanes(i):
            return rr.at[m, 0, :, pl.ds(pl.multiple_of(3 * D + i * LANE, LANE), LANE)]

        front_backward(1, m, ubuf, msk, pr, U, T, lambda i: gin.at[m, :, lanes(i)], xh, rs, sgp, tail_lanes)
        start_factors(m, "G")

        @pl.when(m == 1)
        def _():
            wait_factors("FM")
            early_event(0)

        T[...] = dot(rr[m, 0, :, last], wf[0, :, last], 1, 1)

        @pl.when(early)
        def _():
            window_backward(m, qkv, pw, T, Q)

        @pl.when(jnp.logical_not(early))
        def _():
            channel_backward(m, qkv, pc, T, Q, msk)

        for i in range(3):
            cols = pl.ds(i * D, D)
            rr[m, 0, :, cols] = Q[:, cols].astype(BF)
        start_factors(m, "A")

        @pl.when(m == 1)
        def _():
            for e in range(1, EARLY):
                early_event(e)

        T[...] = dot(rr[m, 0, :, pl.ds(0, 3 * D)], wf[0, :, pl.ds(0, 3 * D)], 1, 1)
        front_backward(0, m, ubuf, msk, pr, U, T, tail_lanes, xh, rs, sgp, lambda i: gout.at[m, :, lanes(i)])

        @pl.when(jnp.logical_not(early))
        def _():
            g_hop(m).start()

        @pl.when(early)
        def _():
            C[...] = gout[m].astype(F32)
            unpad(flat.at[m])

        @pl.when(early & (m == 0))
        def _():
            pltpu.make_async_copy(flat.at[0], ing, es.at[1]).start()

        @pl.when(early & (m == 1))
        def _():
            remote(flat.at[1], ing, es.at[1], er.at[1], opposite).start()

    def phase(p, carry):
        m = jnp.where(early, lax.rem(p, 2), p // 2)
        ahead = jnp.where(early, p < 2, lax.rem(p, 2) == 0)

        @pl.when(ahead)
        def _():
            forward(m, p)

        @pl.when(jnp.logical_not(ahead))
        def _():
            backward(m)

        return carry

    lax.fori_loop(0, 4, phase, 0)

    for h in range(2):
        for sub in range(2):
            pl.semaphore_signal(free.at[h, sub], inc=1, device_id=nexts[1 - h], device_id_type=MESH)

    for sec in range(2):
        for j in range(12):
            sgs[sec, j : j + 1, :] = jnp.sum(sgp[sec, j], axis=0, keepdims=True)
        sgs[sec, 12:16, :] = jnp.zeros((4, D), F32)
    give = remote(sgs.at[1 - c], sgm, sgsem.at[0], sgsem.at[1], mate)
    give.start()
    wait_factors("GA")

    def ring_step(t, carry):
        event(1, t + EARLY)
        event(0, t + jnp.where(c == 1, EARLY, 0))
        for r in range(rounds + 1):

            @pl.when(t == 1 + 3 * r)
            def _():
                if r == 0:
                    give.wait_recv()
                    acc[0] = sgs[c] + sgm[...]
                else:
                    small(r - 1).wait_recv()
                    acc[r] = acc[r - 1] + got[r - 1]
                if r < rounds:
                    small(r).start()

        return carry

    lax.fori_loop(0, 2 * n - 1, ring_step, 0)
    outs[...] = acc[rounds]

    for k in range(2):

        @pl.when(c == k)
        def _():
            for copy in weight_copies(k)[1]:
                copy.wait_send()
            params_copy(k).wait_send()
            for m in range(2):
                for _when, copy in factor_copies(1 - k, m):
                    copy.wait_send()

    give.wait_send()
    for r in range(rounds):
        small(r).wait_send()

    def drain(t, carry):
        for sub in range(2):
            for h in range(2):
                scatter(h, t, sub).wait_send()
                spread(h, t, sub, home(h, t)).wait_send()
        return carry

    lax.fori_loop(0, n - 1, drain, 0)

    def written(j, carry):
        for sub in range(2):
            for h in range(2):
                write(h, j, sub).wait()
        return carry

    lax.fori_loop(0, n, written, 0)

    @pl.when(early)
    def _():
        cot_out.wait_send()
        for m in range(2):
            u_hop(m).wait_send()
        pltpu.make_async_copy(flat.at[0], ing, es.at[1]).wait()
        remote(flat.at[1], ing, es.at[1], er.at[1], opposite).wait_send()
        remote(flat.at[0], act, es.at[0], er.at[0], opposite).wait_recv()

    @pl.when(jnp.logical_not(early))
    def _():
        img_out.wait_send()
        for m in range(2):
            g_hop(m).wait_send()
        remote(flat.at[0], act, es.at[0], er.at[0], opposite).wait_send()
        pltpu.make_async_copy(flat.at[1], act, es.at[0]).wait()
        remote(flat.at[1], ing, es.at[1], er.at[1], opposite).wait_recv()


def relay(wrows, wcols, img, cot, kern, bias, gain, move, first, second):
    shape = jax.ShapeDtypeStruct
    vmem = pl.BlockSpec(memory_space=pltpu.VMEM)
    anywhere = pl.BlockSpec(memory_space=pl.ANY)
    dma = pltpu.SemaphoreType.DMA
    smem = pl.BlockSpec(memory_space=pltpu.SMEM)
    image = (ROWS, D)
    slot = img.shape
    rounds = RING.bit_length() - 1
    return pl.pallas_call(
        relay_kernel,
        out_shape=[
            shape(slot, BF),
            shape(slot, BF),
            shape((D, FF), BF),
            shape((FF // 2, D), BF),
            shape((16, D), F32),
        ],
        in_specs=[smem] * 2 + [vmem] * 6 + [anywhere] * 2,
        out_specs=[anywhere] * 4 + [vmem],
        scratch_shapes=[
            pltpu.VMEM((2, D, FF), BF),
            pltpu.VMEM((FF, D), BF),
            pltpu.VMEM((2, 16, D), F32),
            pltpu.VMEM((2, ROWS, LANE), F32),
            pltpu.VMEM(slot, BF),
            pltpu.VMEM((2,) + slot, BF),
            pltpu.VMEM((2, 2) + image, BF),
            pltpu.VMEM((2,) + image, BF),
            pltpu.VMEM((2,) + image, BF),
            pltpu.VMEM((2,) + image, BF),
            pltpu.VMEM((2, 3) + image, BF),
            pltpu.VMEM((2, 2) + image, BF),
            pltpu.VMEM((2, 2, ROWS, LANE), F32),
            pltpu.VMEM((2, ROWS, 3 * D), F32),
            pltpu.VMEM((2, ROWS, FF), BF),
            pltpu.VMEM((2, 2, ROWS, FF), BF),
            pltpu.VMEM((2, UNITS, PACK * WROWS, WROWS), F32),
            pltpu.VMEM((2, NGROUP, GROUP, GROUP), F32),
            pltpu.VMEM((SIDE, GRID + 2, CELL, D), F32),
            pltpu.VMEM(image, F32),
            pltpu.VMEM(image, F32),
            pltpu.VMEM((ROWS, 3 * D), F32),
            pltpu.VMEM((2, 12, CELL, D), F32),
            pltpu.VMEM((2, 16, D), F32),
            pltpu.VMEM((16, D), F32),
            pltpu.VMEM((2, 2) + image, BF),
            pltpu.VMEM((2, ROWS, FF), BF),
            pltpu.VMEM((2, ROWS, FF // 2), BF),
            pltpu.VMEM((2,) + image, BF),
            pltpu.VMEM((2, RING, COLS + TAIL, COLS), BF),
            pltpu.VMEM((rounds + 1, 16, D), F32),
            pltpu.VMEM((rounds, 16, D), F32),
            dma((5,)),
            dma((6,)),
            dma((6,)),
            dma((2,)),
            dma((2,)),
            dma((2,)),
            dma((2,)),
            dma((2,)),
            dma((2, 6)),
            dma((2, 6)),
            dma((2,)),
            dma((2,)),
            dma((2,)),
            dma((2, 2 * RING, 2)),
            dma((2, 2 * RING, 2)),
            dma((2, RING, 2)),
            dma((rounds,)),
            dma((rounds,)),
            pltpu.SemaphoreType.REGULAR((2, 2)),
        ],
        name="relay",
        compiler_params=pltpu.CompilerParams(
            collective_id=1, has_side_effects=True, vmem_limit_bytes=62 * 2**20
        ),
    )(wrows, wcols, img, cot, kern, bias, gain, move, first, second)


def per_device(
    images, cotangent, window_rows, window_cols, pos_kernel, pos_bias, norm_gain, norm_shift, first_weight, second_weight
):
    act, ing, out1, out2, outs = relay(
        window_rows, window_cols, images[0], cotangent[0], pos_kernel[0], pos_bias, norm_gain, norm_shift,
        first_weight[0], second_weight,
    )
    out1, out2 = out1.astype(F32), out2.astype(F32)
    if lax.axis_size("dp") > RING:
        out1, out2, outs = lax.psum((out1 / RING, out2 / RING, outs / RING), "dp")
    return (
        act[None],
        ing.astype(F32)[None],
        out1[None],
        out2,
        outs[None, :9],
        outs[9:10],
        outs[10:11],
        outs[11:12],
    )


def solution(mesh):
    in_specs = (
        P(("dp", "section"), None, None, None),
        P(("dp", "section"), None, None, None),
        P("dp"),
        P("dp"),
        P("section", None, None),
        P("section", None),
        P("section", None),
        P("section", None),
        P("section", None, None),
        P("section", None),
    )
    out_specs = (
        P(("dp", "section"), None, None, None),
        P(("dp", "section"), None, None, None),
        P("section", None, None),
        P("section", None),
        P("section", None, None),
        P("section", None),
        P("section", None),
        P("section", None),
    )
    return jax.shard_map(per_device, mesh=mesh, in_specs=in_specs, out_specs=out_specs, check_vma=False)
```

```python
from functools import partial

import jax
import jax.numpy as jnp
from jax import lax
from jax.experimental import pallas as pl
from jax.experimental.pallas import tpu as pltpu
from jax.sharding import PartitionSpec as P

D = 768
FF = 3072
HEADS = 24
HEAD = 32
WIN = 7
SIDE = 2
GRID = SIDE * WIN
CELL = 8
WROWS = WIN * CELL
HALF = GRID * CELL
ROWS = SIDE * HALF
GROUP = 256
PACK = GROUP // HEAD
NGROUP = D // GROUP
UNITS = NGROUP * SIDE * SIDE
LANE = 128
FTILE = 1024
EPS = 1e-05
SCALE = HEAD ** (-0.5)
BF = jnp.bfloat16
F32 = jnp.float32
MESH = pl.DeviceIdType.MESH


def dot(a, b, ca=1, cb=0):
    return lax.dot_general(a, b, (((ca,), (cb,)), ((), ())), preferred_element_type=F32)


def lanes(index, width=LANE):
    return pl.ds(pl.multiple_of(index * width, width), width)


def halves(value):
    return value.reshape(SIDE, GRID, CELL, value.shape[-1])


def shifts(left, right):
    column = lax.broadcasted_iota(jnp.int32, left.shape, 1)
    before0 = pltpu.roll(left, 1, 1)
    after0 = jnp.where(column == WIN - 1, pltpu.roll(right, CELL - 2, 1), pltpu.roll(left, CELL - 1, 1))
    before1 = jnp.where(column == 0, pltpu.roll(left, 2, 1), pltpu.roll(right, 1, 1))
    after1 = pltpu.roll(right, CELL - 1, 1)
    return ((before0, left, after0), (before1, right, after1))


def gelu_parts(h):
    expo = jnp.exp(h * h * -0.5)
    t = 1.0 / (1.0 + (0.3275911 * 0.7071067811865476) * jnp.abs(h))
    poly = t * (0.127414796 + t * (-0.142248368 + t * (0.7107068705 + t * (-0.7265760135 + t * 0.5307027145))))
    tail = poly * expo
    phi = jnp.where(h >= 0, 1.0 - tail, tail)
    return h * phi, phi + h * expo * 0.3989422804014327


def front_forward(sec, m, ubuf, msk, pr, U, C, zz, xh, rs):
    zero = jnp.zeros((ROWS, LANE), F32)

    def conv(i, total):
        ls = lanes(i)
        u = ubuf[sec, m, :, ls].astype(F32)
        masked = halves(u * msk[m])
        U[0, 1 : GRID + 1, :, ls] = masked[0]
        U[1, 1 : GRID + 1, :, ls] = masked[1]
        moved = shifts(U[0, :, :, ls], U[1, :, :, ls])
        taps = pr[sec, :, ls]
        uh = halves(u)
        sums = []
        for wc in range(SIDE):
            acc = uh[wc] + taps[9:10, :][None]
            for a in range(3):
                for b in range(3):
                    acc = acc + moved[wc][b][a : a + GRID] * taps[3 * a + b : 3 * a + b + 1, :][None]
            acc = acc.reshape(HALF, LANE)
            C[pl.ds(wc * HALF, HALF), ls] = acc
            sums.append(acc)
        return total + jnp.concatenate(sums, axis=0)

    mean = jnp.sum(lax.fori_loop(0, D // LANE, conv, zero), axis=-1, keepdims=True) * (1.0 / D)

    def spread(i, total):
        centred = C[:, lanes(i)] - mean
        return total + centred * centred

    var = jnp.sum(lax.fori_loop(0, D // LANE, spread, zero), axis=-1, keepdims=True) * (1.0 / D)
    rstd = lax.rsqrt(var + EPS)
    rs[sec, m] = jnp.broadcast_to(rstd, (ROWS, LANE))

    def norm(i, carry):
        ls = lanes(i)
        xhat = (C[:, ls] - mean) * rstd
        xh[sec, m, :, ls] = xhat.astype(BF)
        zz[m, 2 * sec, :, ls] = (xhat * pr[sec, 10:11, ls] + pr[sec, 11:12, ls]).astype(BF)
        return carry

    lax.fori_loop(0, D // LANE, norm, 0)


def front_backward(sec, m, ubuf, msk, pr, U, T, gfull, xh, rs, sgp, out):
    zero = jnp.zeros((ROWS, LANE), F32)

    def fold(value):
        return jnp.sum(value.reshape(ROWS // CELL, CELL, LANE), axis=0)

    def sums(i, carry):
        s1, s2 = carry
        ls = lanes(i)
        dz = T[:, ls]
        xhat = xh[sec, m, :, ls].astype(F32)
        both = xhat * dz
        sgp[sec, 10, :, ls] += fold(both)
        sgp[sec, 11, :, ls] += fold(dz)
        gain = pr[sec, 10:11, ls]
        return s1 + dz * gain, s2 + both * gain

    s1, s2 = lax.fori_loop(0, D // LANE, sums, (zero, zero))
    m1 = jnp.sum(s1, axis=-1, keepdims=True) * (1.0 / D)
    m2 = jnp.sum(s2, axis=-1, keepdims=True) * (1.0 / D)

    def back(i, carry):
        ls = lanes(i)
        xhat = xh[sec, m, :, ls].astype(F32)
        inner = T[:, ls] * pr[sec, 10:11, ls] - m1 - xhat * m2
        gc = gfull(i)[...].astype(F32) + rs[sec, m] * inner
        sgp[sec, 9, :, ls] += fold(gc)
        gh = halves(gc)
        U[0, 1 : GRID + 1, :, ls] = gh[0]
        U[1, 1 : GRID + 1, :, ls] = gh[1]
        moved = shifts(U[0, :, :, ls], U[1, :, :, ls])
        taps = pr[sec, :, ls]
        mask = halves(msk[m])
        um = halves(ubuf[sec, m, :, ls].astype(F32) * msk[m])
        accs = [jnp.zeros((GRID, CELL, LANE), F32) for _ in range(SIDE)]
        for a in range(3):
            for b in range(3):
                tap = 3 * a + b
                kg = jnp.zeros((CELL, LANE), F32)
                for wc in range(SIDE):
                    gs = moved[wc][2 - b][2 - a : 2 - a + GRID]
                    accs[wc] = accs[wc] + gs * taps[tap : tap + 1, :][None]
                    kg = kg + jnp.sum(gs * um[wc], axis=0)
                sgp[sec, tap, :, ls] += kg
        du = [(gh[wc] + mask[wc] * accs[wc]).reshape(HALF, LANE) for wc in range(SIDE)]
        out(i)[...] = jnp.concatenate(du, axis=0).astype(BF)
        return carry

    lax.fori_loop(0, D // LANE, back, 0)


def spread_heads(value, head_of_lane):
    parts = [jnp.where(head_of_lane == h, value, 0.0) for h in range(PACK)]
    return jnp.concatenate(parts, axis=0).astype(BF)


def gather_heads(value, rows, head_of_lane):
    out = jnp.zeros((rows, GROUP), F32)
    for h in range(PACK):
        out = jnp.where(head_of_lane == h, value[h * rows : (h + 1) * rows], out)
    return out


def unit_slices(unit):
    pair, group = unit // NGROUP, lax.rem(unit, NGROUP)
    rows = [pl.ds(pl.multiple_of((2 * pair + w) * WROWS, 8), WROWS) for w in range(2)]
    cols = [pl.ds(pl.multiple_of(part * D + group * GROUP, LANE), GROUP) for part in range(3)]
    return rows, cols


def window_parts(m, i, qkv):
    rows, cols = unit_slices(i)
    head_of_lane = lax.broadcasted_iota(jnp.int32, (WROWS, GROUP), 1) // HEAD
    q = [qkv[m, r, cols[0]].astype(BF) for r in rows]
    kd = [spread_heads(qkv[m, r, cols[1]], head_of_lane) for r in rows]
    vd = [spread_heads(qkv[m, r, cols[2]], head_of_lane) for r in rows]
    return rows, cols, head_of_lane, q, kd, vd


def window_forward(m, qkv, pw, T):
    def unit(i, carry):
        rows, cols, head_of_lane, q, kd, vd = window_parts(m, i, qkv)
        s = [(dot(b, a, 1, 1) * SCALE).reshape(PACK, WROWS, WROWS) for a, b in zip(q, kd)]
        key = lax.broadcasted_iota(jnp.int32, s[0].shape, 1)
        real = lax.rem(key, CELL) < WIN
        s = [jnp.where(real, x, -1e30) for x in s]
        p = [jnp.exp(x - jnp.max(x, axis=1, keepdims=True)) for x in s]
        p = [x * (1.0 / jnp.sum(x, axis=1, keepdims=True)) for x in p]
        p = [x.reshape(PACK * WROWS, WROWS) for x in p]
        for w in range(2):
            pw[m, 2 * i + w] = p[w]
        out = [dot(x.astype(BF), v, 0, 0) for x, v in zip(p, vd)]
        for w in range(2):
            T[rows[w], cols[0]] = out[w]
        return carry

    lax.fori_loop(0, UNITS // 2, unit, 0)


def window_backward(m, qkv, pw, T):
    def unit(i, carry):
        rows, cols, head_of_lane, q, kd, vd = window_parts(m, i, qkv)
        g = [T[r, cols[0]].astype(BF) for r in rows]
        p = [pw[m, 2 * i + w].reshape(PACK, WROWS, WROWS) for w in range(2)]
        dp = [dot(v, x, 1, 1).reshape(PACK, WROWS, WROWS) for v, x in zip(vd, g)]
        ds = [x * (y - jnp.sum(x * y, axis=1, keepdims=True)) for x, y in zip(p, dp)]
        ds = [x.reshape(PACK * WROWS, WROWS).astype(BF) for x in ds]
        pb = [x.reshape(PACK * WROWS, WROWS).astype(BF) for x in p]
        dv = [gather_heads(dot(x, y), WROWS, head_of_lane) for x, y in zip(pb, g)]
        dk = [gather_heads(dot(x, y), WROWS, head_of_lane) * SCALE for x, y in zip(ds, q)]
        dq = [dot(x, y, 0, 0) * SCALE for x, y in zip(ds, kd)]
        for w in range(2):
            qkv[m, rows[w], cols[0]] = dq[w]
            qkv[m, rows[w], cols[1]] = dk[w]
            qkv[m, rows[w], cols[2]] = dv[w]
        return carry

    lax.fori_loop(0, UNITS // 2, unit, 0)


def group_slices(group):
    return [pl.ds(pl.multiple_of(part * D + group * GROUP, LANE), GROUP) for part in range(3)]


def channel_forward(m, qkv, pc, T, msk):
    def unit(i, carry):
        cols = group_slices(i)
        mask = msk[m][:, :1]
        q = qkv[m, :, cols[0]].astype(BF)
        k = (qkv[m, :, cols[1]] * mask).astype(BF)
        v = qkv[m, :, cols[2]].astype(BF)
        s = dot(q, k, 0, 0) * SCALE
        same = (lax.broadcasted_iota(jnp.int32, s.shape, 0) // HEAD) == (lax.broadcasted_iota(jnp.int32, s.shape, 1) // HEAD)
        s = jnp.where(same, s, -1e30)
        p = jnp.exp(s - jnp.max(s, axis=1, keepdims=True))
        p = p * (1.0 / jnp.sum(p, axis=1, keepdims=True))
        pc[m, i] = p
        T[:, cols[0]] = dot(v, p.astype(BF), 1, 1)
        return carry

    lax.fori_loop(0, NGROUP, unit, 0, unroll=True)


def channel_backward(m, qkv, pc, T, msk):
    def unit(i, carry):
        cols = group_slices(i)
        mask = msk[m][:, :1]
        q = qkv[m, :, cols[0]].astype(BF)
        k = (qkv[m, :, cols[1]] * mask).astype(BF)
        v = qkv[m, :, cols[2]].astype(BF)
        g = T[:, cols[0]].astype(BF)
        p = pc[m, i]
        dp = dot(g, v, 0, 0)
        ds = (p * (dp - jnp.sum(p * dp, axis=1, keepdims=True))).astype(BF)
        qkv[m, :, cols[0]] = dot(k, ds, 1, 1) * SCALE
        qkv[m, :, cols[1]] = dot(q, ds) * (SCALE * mask)
        qkv[m, :, cols[2]] = dot(g, p.astype(BF))
        return carry

    lax.fori_loop(0, NGROUP, unit, 0, unroll=True)


RING = 8
COLS = FF // RING
TAIL = FF // 3 // RING
REST = FF // 6 // RING
LATER = FF // 3
EARLY = 2


def relay_kernel(
    wrows, wcols, img, cot, kern, bias, gain, move, first, second,
    act, ing, out1, out2, outs,
    wf, w2, pr, msk, raw, flat, ubuf, gin, gout, zz, xh, rs, qkv, ab, rr, pw, pc, U, C, T, sgp, sgs, sgm,
    rL, rR, rA, rG, xA, xG, buf, acc, got,
    wl, ws, wr, pl_, usem, gsem, us, gs, ss, rsem, es, er, sgsem, ssem, rcem, osem, sms, smr, xs, xr, ys, yr, bs, br, free,
):
    n = RING
    s = lax.axis_index("section")
    dp = lax.axis_index("dp")
    stage, c = s // 2, lax.rem(s, 2)
    mate = (dp, stage * 2 + (1 - c))
    opposite = (dp, (1 - stage) * 2 + c)
    early = stage == 0

    spot = lax.rem(dp, n)
    base = dp - spot
    me = jnp.where(lax.rem(spot, 2) == 0, spot // 2, n - 1 - spot // 2)

    def place(pos):
        pos = lax.rem(pos + 2 * n, n)
        return (base + jnp.where(pos < n // 2, 2 * pos, 2 * (n - 1 - pos) + 1), s)

    nexts = (place(me + 1), place(me - 1))
    rounds = n.bit_length() - 1
    partners = []
    for r in range(rounds):
        bit = 1 << r
        partners.append((jnp.where(lax.rem(spot // bit, 2) == 0, dp + bit, dp - bit), s))

    barrier = pltpu.get_barrier_semaphore()
    peers = [mate, opposite, *nexts, *partners]
    for peer in peers:
        pl.semaphore_signal(barrier, inc=1, device_id=peer, device_id_type=MESH)
    pl.semaphore_wait(barrier, len(peers))

    def remote(src, dst, send, recv, peer):
        return pltpu.make_async_remote_copy(
            src_ref=src, dst_ref=dst, send_sem=send, recv_sem=recv, device_id=peer, device_id_type=MESH
        )

    half = second.shape[0]

    def weight_parts(k):
        parts = []
        for i in range(4):
            parts.append((first.at[:, pl.ds(i * D, D)], wf.at[k, :, pl.ds(i * D, D)]))
        parts.append((second, w2.at[pl.ds(k * half, half), :]))
        return parts

    def weight_copies(k):
        local = [pltpu.make_async_copy(a, b, wl.at[i]) for i, (a, b) in enumerate(weight_parts(k))]
        sent = [remote(a, b, ws.at[i], wr.at[i], mate) for i, (a, b) in enumerate(weight_parts(k))]
        return local, sent

    def params_copy(k):
        return remote(pr.at[k], pr.at[k], ws.at[5], wr.at[5], mate)

    pr[c, 0:9, :] = kern[...].astype(F32)
    pr[c, 9:10, :] = bias[...].astype(F32)
    pr[c, 10:11, :] = gain[...].astype(F32)
    pr[c, 11:12, :] = move[...].astype(F32)
    params_copy(c).start()
    for k in range(2):

        @pl.when(c == k)
        def _():
            local, sent = weight_copies(k)
            for i in range(5):
                local[i].start()
                sent[i].start()

    def wait_weight(k, i):
        if i < 5:

            @pl.when(c == k)
            def _():
                weight_copies(k)[0][i].wait()

        @pl.when(c != k)
        def _():
            (weight_copies(k)[1][i] if i < 5 else params_copy(k)).wait_recv()

    img_out = remote(img, raw, pl_.at[0], pl_.at[1], opposite)
    cot_out = remote(cot, raw, pl_.at[0], pl_.at[1], opposite)

    def pad(src, dst):
        blank = jnp.zeros((CELL - WIN, D), F32)
        for r in range(GRID):
            line = src[r].astype(F32)
            for wc in range(SIDE):
                cells = jnp.concatenate([line[wc * WIN : (wc + 1) * WIN], blank], axis=0)
                C[pl.ds(wc * HALF + r * CELL, CELL), :] = cells
        dst[...] = C[...].astype(BF)

    def unpad(dst):
        for r in range(GRID):
            sides = [C[pl.ds(wc * HALF + r * CELL, CELL), :][:WIN] for wc in range(SIDE)]
            dst[r] = jnp.concatenate(sides, axis=0).astype(BF)

    @pl.when(early)
    def _():
        cot_out.start()
        pad(img, ubuf.at[0, 0])

    @pl.when(jnp.logical_not(early))
    def _():
        img_out.start()
        pad(cot, gin.at[1])

    index = lax.broadcasted_iota(jnp.int32, (ROWS, LANE), 0)
    cell = lax.rem(index, CELL)
    row = lax.rem(index, HALF) // CELL
    column = (index // HALF) * WIN + cell
    for m in range(2):
        inside = (row < WIN * wrows[c + 2 * m]) & (column < WIN * wcols[c + 2 * m]) & (cell < WIN)
        msk[m] = jnp.where(inside, 1.0, 0.0)

    for wc in range(SIDE):
        U[wc, 0] = jnp.zeros((CELL, D), F32)
        U[wc, GRID + 1] = jnp.zeros((CELL, D), F32)
    sgp[...] = jnp.zeros(sgp.shape, F32)

    def u_hop(m):
        return remote(gout.at[m], ubuf.at[0, m], us.at[m], usem.at[m], opposite)

    def g_hop(m):
        return remote(gout.at[m], gin.at[m], gs.at[m], gsem.at[m], opposite)

    def factor_copies(k, m):
        if k == 0:
            parts = [
                ("F", zz.at[m, 0], rL.at[m, 0]),
                ("F", zz.at[m, 1], rL.at[m, 1]),
                ("F", ab.at[m, :, pl.ds(0, FF // 2)], rA.at[m]),
                ("M", gin.at[m], rG.at[m]),
                ("G", rr.at[m, 0, :, pl.ds(3 * D, D)], rR.at[m, :, pl.ds(3 * D, D)]),
                ("A", rr.at[m, 0, :, pl.ds(0, 3 * D)], rR.at[m, :, pl.ds(0, 3 * D)]),
            ]
        else:
            parts = [
                ("F", zz.at[m, 2], rL.at[m, 0]),
                ("F", ab.at[m, :, pl.ds(FF // 2, FF // 2)], rA.at[m]),
                ("M", gin.at[m], rG.at[m]),
                ("M", rr.at[m, 1], rR.at[m]),
            ]
        return [(w, remote(a, b, ss.at[m, i], rsem.at[m, i], mate)) for i, (w, a, b) in enumerate(parts)]

    def start_factors(m, which):
        for k in range(2):

            @pl.when(c != k)
            def _():
                for when, copy in factor_copies(k, m):
                    if when == which:
                        copy.start()

    def wait_factors(which):
        for k in range(2):

            @pl.when(c == k)
            def _():
                for m in range(2):
                    for when, copy in factor_copies(k, m):
                        if when in which:
                            copy.wait_recv()

    def shard(k):
        return lax.rem(k + 4 * n, n)

    def sign(h):
        return 1 if h == 0 else -1

    def home(h, t):
        return shard(me + sign(h) - sign(h) * t)

    def products(terms):
        total = None
        for a, b in terms:
            part = dot(a[...], b[...], 0, 0)
            total = part if total is None else total + part
        return total

    def pick(total, j):
        return jnp.where(lax.rem(j, 2) == 1, total[REST:], total[:REST])

    def tile(sub, h, j):
        side = pl.ds(h * COLS, COLS)
        if sub == 0:
            last = jnp.where(j >= (3 * n) // 4, 1, 0)
            own = jnp.where(c == 1, 2, last)
            other = jnp.where(c == 1, 0, last)
            cols = lanes(j, COLS)
            terms = [(zz.at[m, own, :, side], rr.at[m, c, :, cols]) for m in range(2)]
            terms += [(rL.at[m, other, :, side], rR.at[m, :, cols]) for m in range(2)]
        elif sub == 1:
            mine = pl.ds(pl.multiple_of(c * (FF // 2) + j * TAIL, LANE), TAIL)
            cols = lanes(j, TAIL)
            terms = [(ab.at[m, :, mine], gin.at[m, :, side]) for m in range(2)]
            terms += [(rA.at[m, :, cols], rG.at[m, :, side]) for m in range(2)]
        else:
            block = j // 2 * 2 * REST
            mine = pl.ds(pl.multiple_of(c * (FF // 2) + LATER + block, LANE), 2 * REST)
            cols = pl.ds(pl.multiple_of(LATER + block, LANE), 2 * REST)
            sent = pl.ds(pl.multiple_of(block, LANE), 2 * REST)
            terms = [(ab.at[m, :, mine], gin.at[m, :, side]) for m in range(2)]
            terms += [(rA.at[m, :, cols], rG.at[m, :, side]) for m in range(2)]
            own = pick(products(terms), j)
            terms = [(xA.at[m, :, sent], gout.at[m, :, side]) for m in range(2)]
            terms += [(xA.at[2 + m, :, sent], xG.at[m, :, side]) for m in range(2)]
            return jnp.concatenate([own, pick(products(terms), j)], axis=0)
        return products(terms)

    parts = (pl.ds(0, COLS), pl.ds(COLS, TAIL), pl.ds(COLS + TAIL, 2 * REST))

    def gathered(sub, h, j):
        if sub == 0:
            return wf.at[0, pl.ds(h * COLS, COLS), lanes(j, COLS)]
        start = j * TAIL if sub == 1 else 2 * LATER + j * 2 * REST
        return w2.at[pl.ds(pl.multiple_of(start, 16), TAIL if sub == 1 else 2 * REST), pl.ds(h * COLS, COLS)]

    def scatter(h, t, sub):
        src, dst = buf.at[h, t, parts[sub], :], buf.at[h, t + 1, parts[sub], :]
        return remote(src, dst, ssem.at[h, t, sub], rcem.at[h, t + 1, sub], nexts[h])

    def spread(h, t, sub, j):
        ref = gathered(sub, h, j)
        return remote(ref, ref, ssem.at[h, n - 1 + t, sub], rcem.at[h, n + t, sub], nexts[h])

    def write(h, j, sub):
        if sub == 0:
            dst = out1.at[pl.ds(h * COLS, COLS), lanes(j, COLS)]
        elif sub == 1:
            dst = out2.at[pl.ds(pl.multiple_of(j * TAIL, 16), TAIL), pl.ds(h * COLS, COLS)]
        else:
            dst = out2.at[pl.ds(pl.multiple_of(LATER + j * REST, 16), REST), pl.ds(h * COLS, COLS)]
            return pltpu.make_async_copy(gathered(sub, h, j).at[pl.ds(0, REST), :], dst, osem.at[h, j, sub])
        return pltpu.make_async_copy(gathered(sub, h, j), dst, osem.at[h, j, sub])

    def give_back(h, j):
        src = w2.at[pl.ds(pl.multiple_of(2 * LATER + j * 2 * REST + REST, 16), REST), pl.ds(h * COLS, COLS)]
        dst = out2.at[pl.ds(pl.multiple_of(LATER + j * REST, 16), REST), pl.ds(h * COLS, COLS)]
        return remote(src, dst, bs.at[h, j], br.at[h, j], opposite)

    def deliver(h, j, sub):
        write(h, j, sub).start()
        if sub == 2:
            give_back(h, j).start()

    def lend(m):
        own = ab.at[m, :, pl.ds(pl.multiple_of(c * (FF // 2) + LATER, LANE), FF // 2 - LATER)]
        other = rA.at[m, :, pl.ds(LATER, FF // 2 - LATER)]
        return (
            remote(own, xA.at[m], xs.at[m], xr.at[m], opposite),
            remote(other, xA.at[2 + m], xs.at[2 + m], xr.at[2 + m], opposite),
        )

    def share(m):
        return remote(gout.at[m], xG.at[m], ys.at[m], yr.at[m], mate)

    def reduce_event(sub, h, e):
        total = tile(sub, h, shard(me - sign(h) * e))

        @pl.when(e == 0)
        def _():
            buf[h, 0, parts[sub], :] = total.astype(BF)
            scatter(h, 0, sub).start()

        @pl.when((e > 0) & (e < n - 1))
        def _():
            scatter(h, e - 1, sub).wait_recv()
            buf[h, e, parts[sub], :] = (total + buf[h, e, parts[sub], :].astype(F32)).astype(BF)
            scatter(h, e, sub).start()

        @pl.when(e == n - 1)
        def _():
            j = home(h, 0)
            scatter(h, n - 2, sub).wait_recv()
            gathered(sub, h, j)[...] = (total + buf[h, n - 1, parts[sub], :].astype(F32)).astype(BF)
            pl.semaphore_wait(free.at[h, sub], 1)
            spread(h, 0, sub, j).start()
            deliver(h, j, sub)

    def event(sub, e):
        for h in range(2):

            @pl.when(e < n)
            def _():
                reduce_event(sub, h, e)

            @pl.when((e >= n) & (e < 2 * n - 1))
            def _():
                t = e - (n - 1)
                j = home(h, t)
                spread(h, t - 1, sub, j).wait_recv()

                @pl.when(t < n - 1)
                def _():
                    spread(h, t, sub, j).start()

                deliver(h, j, sub)

    def early_event(e):
        event(1, e)

        @pl.when(c == 1)
        def _():
            event(0, e)

    def small(r):
        return remote(acc.at[r], got.at[r], sms.at[r], smr.at[r], partners[r])

    def forward(m, p):
        @pl.when(jnp.logical_not(early))
        def _():
            u_hop(m).wait_recv()

        @pl.when(early & (m == 1))
        def _():
            img_out.wait_recv()
            pad(raw, ubuf.at[0, 1])

        once = p == 0

        def first_time(k, i):
            @pl.when(once)
            def _():
                wait_weight(k, i)

        first_time(0, 5)
        front_forward(0, m, ubuf, msk, pr, U, C, zz, xh, rs)
        for i in range(3):
            first_time(0, i)
            qkv[m, :, pl.ds(i * D, D)] = dot(zz[m, 0], wf[0, :, pl.ds(i * D, D)]).astype(BF).astype(F32)

        @pl.when(early)
        def _():
            window_forward(m, qkv, pw, T)

        @pl.when(jnp.logical_not(early))
        def _():
            channel_forward(m, qkv, pc, T, msk)

        first_time(0, 3)
        zz[m, 1] = T[...].astype(BF)
        ubuf[1, m] = (C[...] + dot(zz[m, 1], wf[0, :, pl.ds(3 * D, D)])).astype(BF)

        first_time(1, 5)
        front_forward(1, m, ubuf, msk, pr, U, C, zz, xh, rs)
        for i in range(4):
            first_time(1, i)
        first_time(0, 4)
        first_time(1, 4)

        for t in range(FF // FTILE):
            cols = pl.ds(t * FTILE, FTILE)
            a, d = gelu_parts(dot(zz[m, 2], wf[1, :, cols]))
            ab[m, :, cols] = a.astype(BF)
            rr[m, 1, :, cols] = d.astype(BF)
        gout[m] = (C[...] + dot(ab[m], w2[...])).astype(BF)

        @pl.when(early)
        def _():
            u_hop(m).start()

        @pl.when(jnp.logical_not(early))
        def _():
            for l in range(D // LANE):
                cols = pl.ds(l * LANE, LANE)
                C[:, cols] = gout[m, :, cols].astype(F32) * msk[m]
            unpad(flat.at[m])

        @pl.when(jnp.logical_not(early) & (m == 0))
        def _():
            remote(flat.at[0], act, es.at[0], er.at[0], opposite).start()

        @pl.when(jnp.logical_not(early) & (m == 1))
        def _():
            pltpu.make_async_copy(flat.at[1], act, es.at[0]).start()

        start_factors(m, "F")

        @pl.when(early & (m == 1))
        def _():
            wait_factors("F")
            for i in range(2):
                for copy in lend(i):
                    copy.start()

    def backward(m):
        @pl.when(early)
        def _():
            g_hop(m).wait_recv()

        @pl.when(jnp.logical_not(early))
        def _():
            @pl.when(m == 0)
            def _():
                cot_out.wait_recv()
                pad(raw, gin.at[0])

            for l in range(D // LANE):
                cols = pl.ds(l * LANE, LANE)
                gin[m, :, cols] = (gin[m, :, cols].astype(F32) * msk[m]).astype(BF)

        for t in range(FF // FTILE):
            cols = pl.ds(t * FTILE, FTILE)
            da = dot(gin[m], w2[cols, :], 1, 1)
            rr[m, 1, :, cols] = (da * rr[m, 1, :, cols].astype(F32)).astype(BF)
        T[...] = dot(rr[m, 1], wf[1], 1, 1)
        start_factors(m, "M")
        last = pl.ds(3 * D, D)

        @pl.when(early)
        def _():
            u_hop(m).wait_send()

        def tail_lanes(i):
            return rr.at[m, 0, :, pl.ds(pl.multiple_of(3 * D + i * LANE, LANE), LANE)]

        front_backward(1, m, ubuf, msk, pr, U, T, lambda i: gin.at[m, :, lanes(i)], xh, rs, sgp, tail_lanes)
        start_factors(m, "G")

        @pl.when(m == 1)
        def _():
            @pl.when(jnp.logical_not(early))
            def _():
                wait_factors("F")

            wait_factors("M")
            early_event(0)

        T[...] = dot(rr[m, 0, :, last], wf[0, :, last], 1, 1)

        @pl.when(early)
        def _():
            window_backward(m, qkv, pw, T)

        @pl.when(jnp.logical_not(early))
        def _():
            channel_backward(m, qkv, pc, T, msk)

        for i in range(3):
            cols = pl.ds(i * D, D)
            rr[m, 0, :, cols] = qkv[m, :, cols].astype(BF)
        start_factors(m, "A")

        @pl.when(m == 1)
        def _():
            for e in range(1, EARLY):
                early_event(e)

        T[...] = dot(rr[m, 0, :, pl.ds(0, 3 * D)], wf[0, :, pl.ds(0, 3 * D)], 1, 1)
        front_backward(0, m, ubuf, msk, pr, U, T, tail_lanes, xh, rs, sgp, lambda i: gout.at[m, :, lanes(i)])

        @pl.when(jnp.logical_not(early))
        def _():
            g_hop(m).start()
            share(m).start()

        @pl.when(early)
        def _():
            C[...] = gout[m].astype(F32)
            unpad(flat.at[m])

        @pl.when(early & (m == 0))
        def _():
            pltpu.make_async_copy(flat.at[0], ing, es.at[1]).start()

        @pl.when(early & (m == 1))
        def _():
            remote(flat.at[1], ing, es.at[1], er.at[1], opposite).start()

    def phase(p, carry):
        m = jnp.where(early, lax.rem(p, 2), p // 2)
        ahead = jnp.where(early, p < 2, lax.rem(p, 2) == 0)

        @pl.when(ahead)
        def _():
            forward(m, p)

        @pl.when(jnp.logical_not(ahead))
        def _():
            backward(m)

        return carry

    lax.fori_loop(0, 4, phase, 0)

    for h in range(2):
        for sub in range(2):
            pl.semaphore_signal(free.at[h, sub], inc=1, device_id=nexts[1 - h], device_id_type=MESH)

        @pl.when(jnp.logical_not(early))
        def _():
            pl.semaphore_signal(free.at[h, 2], inc=1, device_id=nexts[1 - h], device_id_type=MESH)

    for sec in range(2):
        for j in range(12):
            sgs[sec, j : j + 1, :] = jnp.sum(sgp[sec, j], axis=0, keepdims=True)
        sgs[sec, 12:16, :] = jnp.zeros((4, D), F32)
    give = remote(sgs.at[1 - c], sgm, sgsem.at[0], sgsem.at[1], mate)
    give.start()
    wait_factors("GA")

    @pl.when(jnp.logical_not(early))
    def _():
        for m in range(2):
            for copy in lend(m):
                copy.wait_recv()
            share(m).wait_recv()

    def ring_step(t, carry):
        event(1, t + EARLY)

        @pl.when(jnp.logical_not(early))
        def _():
            event(2, t)

        event(0, t + jnp.where(c == 1, EARLY, 0))
        for r in range(rounds + 1):

            @pl.when(t == 1 + 3 * r)
            def _():
                if r == 0:
                    give.wait_recv()
                    acc[0] = sgs[c] + sgm[...]
                else:
                    small(r - 1).wait_recv()
                    acc[r] = acc[r - 1] + got[r - 1]
                if r < rounds:
                    small(r).start()

        return carry

    lax.fori_loop(0, 2 * n - 1, ring_step, 0)
    outs[...] = acc[rounds]

    for k in range(2):

        @pl.when(c == k)
        def _():
            for copy in weight_copies(k)[1]:
                copy.wait_send()
            params_copy(k).wait_send()
            for m in range(2):
                for _when, copy in factor_copies(1 - k, m):
                    copy.wait_send()

    give.wait_send()
    for r in range(rounds):
        small(r).wait_send()

    def drain(t, carry):
        for h in range(2):
            for sub in range(2):
                scatter(h, t, sub).wait_send()
                spread(h, t, sub, home(h, t)).wait_send()

            @pl.when(jnp.logical_not(early))
            def _():
                scatter(h, t, 2).wait_send()
                spread(h, t, 2, home(h, t)).wait_send()

        return carry

    lax.fori_loop(0, n - 1, drain, 0)

    def written(j, carry):
        for h in range(2):
            for sub in range(2):
                write(h, j, sub).wait()

            @pl.when(early)
            def _():
                give_back(h, j).wait_recv()

            @pl.when(jnp.logical_not(early))
            def _():
                write(h, j, 2).wait()
                give_back(h, j).wait_send()

        return carry

    lax.fori_loop(0, n, written, 0)

    @pl.when(early)
    def _():
        cot_out.wait_send()
        for m in range(2):
            for copy in lend(m):
                copy.wait_send()
        pltpu.make_async_copy(flat.at[0], ing, es.at[1]).wait()
        remote(flat.at[1], ing, es.at[1], er.at[1], opposite).wait_send()
        remote(flat.at[0], act, es.at[0], er.at[0], opposite).wait_recv()

    @pl.when(jnp.logical_not(early))
    def _():
        img_out.wait_send()
        for m in range(2):
            g_hop(m).wait_send()
            share(m).wait_send()
        remote(flat.at[0], act, es.at[0], er.at[0], opposite).wait_send()
        pltpu.make_async_copy(flat.at[1], act, es.at[0]).wait()
        remote(flat.at[1], ing, es.at[1], er.at[1], opposite).wait_recv()


def relay(wrows, wcols, img, cot, kern, bias, gain, move, first, second):
    shape = jax.ShapeDtypeStruct
    vmem = pl.BlockSpec(memory_space=pltpu.VMEM)
    anywhere = pl.BlockSpec(memory_space=pl.ANY)
    dma = pltpu.SemaphoreType.DMA
    smem = pl.BlockSpec(memory_space=pltpu.SMEM)
    image = (ROWS, D)
    slot = img.shape
    rounds = RING.bit_length() - 1
    return pl.pallas_call(
        relay_kernel,
        out_shape=[
            shape(slot, BF),
            shape(slot, BF),
            shape((D, FF), BF),
            shape((FF // 2, D), BF),
            shape((16, D), F32),
        ],
        in_specs=[smem] * 2 + [vmem] * 6 + [anywhere] * 2,
        out_specs=[anywhere] * 4 + [vmem],
        scratch_shapes=[
            pltpu.VMEM((2, D, FF), BF),
            pltpu.VMEM((FF, D), BF),
            pltpu.VMEM((2, 16, D), F32),
            pltpu.VMEM((2, ROWS, LANE), F32),
            pltpu.VMEM(slot, BF),
            pltpu.VMEM((2,) + slot, BF),
            pltpu.VMEM((2, 2) + image, BF),
            pltpu.VMEM((2,) + image, BF),
            pltpu.VMEM((2,) + image, BF),
            pltpu.VMEM((2, 3) + image, BF),
            pltpu.VMEM((2, 2) + image, BF),
            pltpu.VMEM((2, 2, ROWS, LANE), F32),
            pltpu.VMEM((2, ROWS, 3 * D), F32),
            pltpu.VMEM((2, ROWS, FF), BF),
            pltpu.VMEM((2, 2, ROWS, FF), BF),
            pltpu.VMEM((2, UNITS, PACK * WROWS, WROWS), F32),
            pltpu.VMEM((2, NGROUP, GROUP, GROUP), F32),
            pltpu.VMEM((SIDE, GRID + 2, CELL, D), F32),
            pltpu.VMEM(image, F32),
            pltpu.VMEM(image, F32),
            pltpu.VMEM((2, 12, CELL, D), F32),
            pltpu.VMEM((2, 16, D), F32),
            pltpu.VMEM((16, D), F32),
            pltpu.VMEM((2, 2) + image, BF),
            pltpu.VMEM((2, ROWS, FF), BF),
            pltpu.VMEM((2, ROWS, FF // 2), BF),
            pltpu.VMEM((2,) + image, BF),
            pltpu.VMEM((4, ROWS, FF // 2 - LATER), BF),
            pltpu.VMEM((2,) + image, BF),
            pltpu.VMEM((2, RING, COLS + TAIL + 2 * REST, COLS), BF),
            pltpu.VMEM((rounds + 1, 16, D), F32),
            pltpu.VMEM((rounds, 16, D), F32),
            dma((5,)),
            dma((6,)),
            dma((6,)),
            dma((2,)),
            dma((2,)),
            dma((2,)),
            dma((2,)),
            dma((2,)),
            dma((2, 6)),
            dma((2, 6)),
            dma((2,)),
            dma((2,)),
            dma((2,)),
            dma((2, 2 * RING, 3)),
            dma((2, 2 * RING, 3)),
            dma((2, RING, 3)),
            dma((rounds,)),
            dma((rounds,)),
            dma((4,)),
            dma((4,)),
            dma((2,)),
            dma((2,)),
            dma((2, RING)),
            dma((2, RING)),
            pltpu.SemaphoreType.REGULAR((2, 3)),
        ],
        name="relay",
        compiler_params=pltpu.CompilerParams(
            collective_id=1, has_side_effects=True, vmem_limit_bytes=62 * 2**20
        ),
    )(wrows, wcols, img, cot, kern, bias, gain, move, first, second)


def per_device(
    images, cotangent, window_rows, window_cols, pos_kernel, pos_bias, norm_gain, norm_shift, first_weight, second_weight
):
    act, ing, out1, out2, outs = relay(
        window_rows, window_cols, images[0], cotangent[0], pos_kernel[0], pos_bias, norm_gain, norm_shift,
        first_weight[0], second_weight,
    )
    out1, out2 = out1.astype(F32), out2.astype(F32)
    if lax.axis_size("dp") > RING:
        out1, out2, outs = lax.psum((out1 / RING, out2 / RING, outs / RING), "dp")
    return (
        act[None],
        ing.astype(F32)[None],
        out1[None],
        out2,
        outs[None, :9],
        outs[9:10],
        outs[10:11],
        outs[11:12],
    )


def solution(mesh):
    in_specs = (
        P(("dp", "section"), None, None, None),
        P(("dp", "section"), None, None, None),
        P("dp"),
        P("dp"),
        P("section", None, None),
        P("section", None),
        P("section", None),
        P("section", None),
        P("section", None, None),
        P("section", None),
    )
    out_specs = (
        P(("dp", "section"), None, None, None),
        P(("dp", "section"), None, None, None),
        P("section", None, None),
        P("section", None),
        P("section", None, None),
        P("section", None),
        P("section", None),
        P("section", None),
    )
    return jax.shard_map(per_device, mesh=mesh, in_specs=in_specs, out_specs=out_specs, check_vma=False)
```

```python
from functools import partial

import jax
import jax.numpy as jnp
from jax import lax
from jax.experimental import pallas as pl
from jax.experimental.pallas import tpu as pltpu
from jax.sharding import PartitionSpec as P

D = 768
FF = 3072
HEADS = 24
HEAD = 32
WIN = 7
SIDE = 2
GRID = SIDE * WIN
CELL = 8
WROWS = WIN * CELL
HALF = GRID * CELL
ROWS = SIDE * HALF
GROUP = 256
PACK = GROUP // HEAD
NGROUP = D // GROUP
UNITS = NGROUP * SIDE * SIDE
LANE = 128
FTILE = 1024
EPS = 1e-05
SCALE = HEAD ** (-0.5)
BF = jnp.bfloat16
F32 = jnp.float32
MESH = pl.DeviceIdType.MESH


def dot(a, b, ca=1, cb=0):
    return lax.dot_general(a, b, (((ca,), (cb,)), ((), ())), preferred_element_type=F32)


def lanes(index, width=LANE):
    return pl.ds(pl.multiple_of(index * width, width), width)


def halves(value):
    return value.reshape(SIDE, GRID, CELL, value.shape[-1])


def shifts(left, right):
    column = lax.broadcasted_iota(jnp.int32, left.shape, 1)
    before0 = pltpu.roll(left, 1, 1)
    after0 = jnp.where(column == WIN - 1, pltpu.roll(right, CELL - 2, 1), pltpu.roll(left, CELL - 1, 1))
    before1 = jnp.where(column == 0, pltpu.roll(left, 2, 1), pltpu.roll(right, 1, 1))
    after1 = pltpu.roll(right, CELL - 1, 1)
    return ((before0, left, after0), (before1, right, after1))


def gelu_parts(h):
    expo = jnp.exp(h * h * -0.5)
    t = 1.0 / (1.0 + (0.3275911 * 0.7071067811865476) * jnp.abs(h))
    poly = t * (0.127414796 + t * (-0.142248368 + t * (0.7107068705 + t * (-0.7265760135 + t * 0.5307027145))))
    tail = poly * expo
    phi = jnp.where(h >= 0, 1.0 - tail, tail)
    return h * phi, phi + h * expo * 0.3989422804014327


def front_forward(sec, m, ubuf, msk, pr, U, C, zz, xh, rs):
    zero = jnp.zeros((ROWS, LANE), F32)

    def conv(i, total):
        ls = lanes(i)
        u = ubuf[sec, m, :, ls].astype(F32)
        masked = halves(u * msk[m])
        U[0, 1 : GRID + 1, :, ls] = masked[0]
        U[1, 1 : GRID + 1, :, ls] = masked[1]
        moved = shifts(U[0, :, :, ls], U[1, :, :, ls])
        taps = pr[sec, :, ls]
        uh = halves(u)
        sums = []
        for wc in range(SIDE):
            acc = uh[wc] + taps[9:10, :][None]
            for a in range(3):
                for b in range(3):
                    acc = acc + moved[wc][b][a : a + GRID] * taps[3 * a + b : 3 * a + b + 1, :][None]
            acc = acc.reshape(HALF, LANE)
            C[pl.ds(wc * HALF, HALF), ls] = acc
            sums.append(acc)
        return total + jnp.concatenate(sums, axis=0)

    mean = jnp.sum(lax.fori_loop(0, D // LANE, conv, zero), axis=-1, keepdims=True) * (1.0 / D)

    def spread(i, total):
        centred = C[:, lanes(i)] - mean
        return total + centred * centred

    var = jnp.sum(lax.fori_loop(0, D // LANE, spread, zero), axis=-1, keepdims=True) * (1.0 / D)
    rstd = lax.rsqrt(var + EPS)
    rs[sec, m] = jnp.broadcast_to(rstd, (ROWS, LANE))

    def norm(i, carry):
        ls = lanes(i)
        xhat = (C[:, ls] - mean) * rstd
        xh[sec, m, :, ls] = xhat.astype(BF)
        zz[m, 2 * sec, :, ls] = (xhat * pr[sec, 10:11, ls] + pr[sec, 11:12, ls]).astype(BF)
        return carry

    lax.fori_loop(0, D // LANE, norm, 0)


def front_backward(sec, m, ubuf, msk, pr, U, T, gfull, xh, rs, sgp, out):
    zero = jnp.zeros((ROWS, LANE), F32)

    def fold(value):
        return jnp.sum(value.reshape(ROWS // CELL, CELL, LANE), axis=0)

    def sums(i, carry):
        s1, s2 = carry
        ls = lanes(i)
        dz = T[:, ls]
        xhat = xh[sec, m, :, ls].astype(F32)
        both = xhat * dz
        sgp[sec, 10, :, ls] += fold(both)
        sgp[sec, 11, :, ls] += fold(dz)
        gain = pr[sec, 10:11, ls]
        return s1 + dz * gain, s2 + both * gain

    s1, s2 = lax.fori_loop(0, D // LANE, sums, (zero, zero))
    m1 = jnp.sum(s1, axis=-1, keepdims=True) * (1.0 / D)
    m2 = jnp.sum(s2, axis=-1, keepdims=True) * (1.0 / D)

    def back(i, carry):
        ls = lanes(i)
        xhat = xh[sec, m, :, ls].astype(F32)
        inner = T[:, ls] * pr[sec, 10:11, ls] - m1 - xhat * m2
        gc = gfull(i)[...].astype(F32) + rs[sec, m] * inner
        sgp[sec, 9, :, ls] += fold(gc)
        gh = halves(gc)
        U[0, 1 : GRID + 1, :, ls] = gh[0]
        U[1, 1 : GRID + 1, :, ls] = gh[1]
        moved = shifts(U[0, :, :, ls], U[1, :, :, ls])
        taps = pr[sec, :, ls]
        mask = halves(msk[m])
        um = halves(ubuf[sec, m, :, ls].astype(F32) * msk[m])
        accs = [jnp.zeros((GRID, CELL, LANE), F32) for _ in range(SIDE)]
        for a in range(3):
            for b in range(3):
                tap = 3 * a + b
                kg = jnp.zeros((CELL, LANE), F32)
                for wc in range(SIDE):
                    gs = moved[wc][2 - b][2 - a : 2 - a + GRID]
                    accs[wc] = accs[wc] + gs * taps[tap : tap + 1, :][None]
                    kg = kg + jnp.sum(gs * um[wc], axis=0)
                sgp[sec, tap, :, ls] += kg
        du = [(gh[wc] + mask[wc] * accs[wc]).reshape(HALF, LANE) for wc in range(SIDE)]
        out(i)[...] = jnp.concatenate(du, axis=0).astype(BF)
        return carry

    lax.fori_loop(0, D // LANE, back, 0)


def spread_heads(value, head_of_lane):
    parts = [jnp.where(head_of_lane == h, value, 0.0) for h in range(PACK)]
    return jnp.concatenate(parts, axis=0).astype(BF)


def gather_heads(value, rows, head_of_lane):
    out = jnp.zeros((rows, GROUP), F32)
    for h in range(PACK):
        out = jnp.where(head_of_lane == h, value[h * rows : (h + 1) * rows], out)
    return out


def unit_slices(unit):
    pair, group = unit // NGROUP, lax.rem(unit, NGROUP)
    rows = [pl.ds(pl.multiple_of((2 * pair + w) * WROWS, 8), WROWS) for w in range(2)]
    cols = [pl.ds(pl.multiple_of(part * D + group * GROUP, LANE), GROUP) for part in range(3)]
    return rows, cols


def window_parts(m, i, qkv):
    rows, cols = unit_slices(i)
    head_of_lane = lax.broadcasted_iota(jnp.int32, (WROWS, GROUP), 1) // HEAD
    q = [qkv[m, r, cols[0]].astype(BF) for r in rows]
    kd = [spread_heads(qkv[m, r, cols[1]], head_of_lane) for r in rows]
    vd = [spread_heads(qkv[m, r, cols[2]], head_of_lane) for r in rows]
    return rows, cols, head_of_lane, q, kd, vd


def window_forward(m, qkv, pw, T):
    def unit(i, carry):
        rows, cols, head_of_lane, q, kd, vd = window_parts(m, i, qkv)
        s = [(dot(b, a, 1, 1) * SCALE).reshape(PACK, WROWS, WROWS) for a, b in zip(q, kd)]
        key = lax.broadcasted_iota(jnp.int32, s[0].shape, 1)
        real = lax.rem(key, CELL) < WIN
        s = [jnp.where(real, x, -1e30) for x in s]
        p = [jnp.exp(x - jnp.max(x, axis=1, keepdims=True)) for x in s]
        p = [x * (1.0 / jnp.sum(x, axis=1, keepdims=True)) for x in p]
        p = [x.reshape(PACK * WROWS, WROWS) for x in p]
        for w in range(2):
            pw[m, 2 * i + w] = p[w]
        out = [dot(x.astype(BF), v, 0, 0) for x, v in zip(p, vd)]
        for w in range(2):
            T[rows[w], cols[0]] = out[w]
        return carry

    lax.fori_loop(0, UNITS // 2, unit, 0)


def window_backward(m, qkv, pw, T):
    def unit(i, carry):
        rows, cols, head_of_lane, q, kd, vd = window_parts(m, i, qkv)
        g = [T[r, cols[0]].astype(BF) for r in rows]
        p = [pw[m, 2 * i + w].reshape(PACK, WROWS, WROWS) for w in range(2)]
        dp = [dot(v, x, 1, 1).reshape(PACK, WROWS, WROWS) for v, x in zip(vd, g)]
        ds = [x * (y - jnp.sum(x * y, axis=1, keepdims=True)) for x, y in zip(p, dp)]
        ds = [x.reshape(PACK * WROWS, WROWS).astype(BF) for x in ds]
        pb = [x.reshape(PACK * WROWS, WROWS).astype(BF) for x in p]
        dv = [gather_heads(dot(x, y), WROWS, head_of_lane) for x, y in zip(pb, g)]
        dk = [gather_heads(dot(x, y), WROWS, head_of_lane) * SCALE for x, y in zip(ds, q)]
        dq = [dot(x, y, 0, 0) * SCALE for x, y in zip(ds, kd)]
        for w in range(2):
            qkv[m, rows[w], cols[0]] = dq[w]
            qkv[m, rows[w], cols[1]] = dk[w]
            qkv[m, rows[w], cols[2]] = dv[w]
        return carry

    lax.fori_loop(0, UNITS // 2, unit, 0)


def group_slices(group):
    return [pl.ds(pl.multiple_of(part * D + group * GROUP, LANE), GROUP) for part in range(3)]


def channel_forward(m, qkv, pc, T, msk):
    def unit(i, carry):
        cols = group_slices(i)
        mask = msk[m][:, :1]
        q = qkv[m, :, cols[0]].astype(BF)
        k = (qkv[m, :, cols[1]] * mask).astype(BF)
        v = qkv[m, :, cols[2]].astype(BF)
        s = dot(q, k, 0, 0) * SCALE
        same = (lax.broadcasted_iota(jnp.int32, s.shape, 0) // HEAD) == (lax.broadcasted_iota(jnp.int32, s.shape, 1) // HEAD)
        s = jnp.where(same, s, -1e30)
        p = jnp.exp(s - jnp.max(s, axis=1, keepdims=True))
        p = p * (1.0 / jnp.sum(p, axis=1, keepdims=True))
        pc[m, i] = p
        T[:, cols[0]] = dot(v, p.astype(BF), 1, 1)
        return carry

    lax.fori_loop(0, NGROUP, unit, 0, unroll=True)


def channel_backward(m, qkv, pc, T, msk):
    def unit(i, carry):
        cols = group_slices(i)
        mask = msk[m][:, :1]
        q = qkv[m, :, cols[0]].astype(BF)
        k = (qkv[m, :, cols[1]] * mask).astype(BF)
        v = qkv[m, :, cols[2]].astype(BF)
        g = T[:, cols[0]].astype(BF)
        p = pc[m, i]
        dp = dot(g, v, 0, 0)
        ds = (p * (dp - jnp.sum(p * dp, axis=1, keepdims=True))).astype(BF)
        qkv[m, :, cols[0]] = dot(k, ds, 1, 1) * SCALE
        qkv[m, :, cols[1]] = dot(q, ds) * (SCALE * mask)
        qkv[m, :, cols[2]] = dot(g, p.astype(BF))
        return carry

    lax.fori_loop(0, NGROUP, unit, 0, unroll=True)


RING = 8
COLS = FF // RING
TAIL = FF // 3 // RING
REST = FF // 6 // RING
LATER = FF // 3
EARLY = 2


def relay_kernel(
    wrows, wcols, img, cot, kern, bias, gain, move, first, second,
    act, ing, out1, out2, outs,
    wf, w2, pr, msk, raw, flat, ubuf, gin, gout, zz, xh, rs, qkv, ab, rr, pw, pc, U, C, T, sgp, sgs, sgm,
    rL, rR, rA, rG, xA, xG, buf, acc, got,
    wl, ws, wr, pl_, usem, gsem, us, gs, ss, rsem, es, er, sgsem, ssem, rcem, osem, sms, smr, xs, xr, ys, yr, bs, br, free,
):
    n = RING
    s = lax.axis_index("section")
    dp = lax.axis_index("dp")
    stage, c = s // 2, lax.rem(s, 2)
    mate = (dp, stage * 2 + (1 - c))
    opposite = (dp, (1 - stage) * 2 + c)
    diagonal = (dp, 3 - s)
    lender, helper = s == 0, s == 3
    early = stage == 0

    spot = lax.rem(dp, n)
    base = dp - spot
    me = jnp.where(lax.rem(spot, 2) == 0, spot // 2, n - 1 - spot // 2)

    def place(pos):
        pos = lax.rem(pos + 2 * n, n)
        return (base + jnp.where(pos < n // 2, 2 * pos, 2 * (n - 1 - pos) + 1), s)

    nexts = (place(me + 1), place(me - 1))
    rounds = n.bit_length() - 1
    partners = []
    for r in range(rounds):
        bit = 1 << r
        partners.append((jnp.where(lax.rem(spot // bit, 2) == 0, dp + bit, dp - bit), s))

    barrier = pltpu.get_barrier_semaphore()
    peers = [mate, opposite, diagonal, *nexts, *partners]
    for peer in peers:
        pl.semaphore_signal(barrier, inc=1, device_id=peer, device_id_type=MESH)
    pl.semaphore_wait(barrier, len(peers))

    def remote(src, dst, send, recv, peer):
        return pltpu.make_async_remote_copy(
            src_ref=src, dst_ref=dst, send_sem=send, recv_sem=recv, device_id=peer, device_id_type=MESH
        )

    half = second.shape[0]

    def weight_parts(k):
        parts = []
        for i in range(4):
            parts.append((first.at[:, pl.ds(i * D, D)], wf.at[k, :, pl.ds(i * D, D)]))
        parts.append((second, w2.at[pl.ds(k * half, half), :]))
        return parts

    def weight_copies(k):
        local = [pltpu.make_async_copy(a, b, wl.at[i]) for i, (a, b) in enumerate(weight_parts(k))]
        sent = [remote(a, b, ws.at[i], wr.at[i], mate) for i, (a, b) in enumerate(weight_parts(k))]
        return local, sent

    def params_copy(k):
        return remote(pr.at[k], pr.at[k], ws.at[5], wr.at[5], mate)

    pr[c, 0:9, :] = kern[...].astype(F32)
    pr[c, 9:10, :] = bias[...].astype(F32)
    pr[c, 10:11, :] = gain[...].astype(F32)
    pr[c, 11:12, :] = move[...].astype(F32)
    params_copy(c).start()
    for k in range(2):

        @pl.when(c == k)
        def _():
            local, sent = weight_copies(k)
            for i in range(5):
                local[i].start()
                sent[i].start()

    def wait_weight(k, i):
        if i < 5:

            @pl.when(c == k)
            def _():
                weight_copies(k)[0][i].wait()

        @pl.when(c != k)
        def _():
            (weight_copies(k)[1][i] if i < 5 else params_copy(k)).wait_recv()

    img_out = remote(img, raw, pl_.at[0], pl_.at[1], opposite)
    cot_out = remote(cot, raw, pl_.at[0], pl_.at[1], opposite)

    def pad(src, dst):
        blank = jnp.zeros((CELL - WIN, D), F32)
        for r in range(GRID):
            line = src[r].astype(F32)
            for wc in range(SIDE):
                cells = jnp.concatenate([line[wc * WIN : (wc + 1) * WIN], blank], axis=0)
                C[pl.ds(wc * HALF + r * CELL, CELL), :] = cells
        dst[...] = C[...].astype(BF)

    def unpad(dst):
        for r in range(GRID):
            sides = [C[pl.ds(wc * HALF + r * CELL, CELL), :][:WIN] for wc in range(SIDE)]
            dst[r] = jnp.concatenate(sides, axis=0).astype(BF)

    @pl.when(early)
    def _():
        cot_out.start()
        pad(img, ubuf.at[0, 0])

    @pl.when(jnp.logical_not(early))
    def _():
        img_out.start()
        pad(cot, gin.at[1])

    index = lax.broadcasted_iota(jnp.int32, (ROWS, LANE), 0)
    cell = lax.rem(index, CELL)
    row = lax.rem(index, HALF) // CELL
    column = (index // HALF) * WIN + cell
    for m in range(2):
        inside = (row < WIN * wrows[c + 2 * m]) & (column < WIN * wcols[c + 2 * m]) & (cell < WIN)
        msk[m] = jnp.where(inside, 1.0, 0.0)

    for wc in range(SIDE):
        U[wc, 0] = jnp.zeros((CELL, D), F32)
        U[wc, GRID + 1] = jnp.zeros((CELL, D), F32)
    sgp[...] = jnp.zeros(sgp.shape, F32)

    def u_hop(m):
        return remote(gout.at[m], ubuf.at[0, m], us.at[m], usem.at[m], opposite)

    def g_hop(m):
        return remote(gout.at[m], gin.at[m], gs.at[m], gsem.at[m], opposite)

    def factor_copies(k, m):
        if k == 0:
            parts = [
                ("F", zz.at[m, 0], rL.at[m, 0]),
                ("F", zz.at[m, 1], rL.at[m, 1]),
                ("F", ab.at[m, :, pl.ds(0, FF // 2)], rA.at[m]),
                ("M", gin.at[m], rG.at[m]),
                ("G", rr.at[m, 0, :, pl.ds(3 * D, D)], rR.at[m, :, pl.ds(3 * D, D)]),
                ("A", rr.at[m, 0, :, pl.ds(0, 3 * D)], rR.at[m, :, pl.ds(0, 3 * D)]),
            ]
        else:
            parts = [
                ("F", zz.at[m, 2], rL.at[m, 0]),
                ("F", ab.at[m, :, pl.ds(FF // 2, FF // 2)], rA.at[m]),
                ("M", gin.at[m], rG.at[m]),
                ("M", rr.at[m, 1], rR.at[m]),
            ]
        return [(w, remote(a, b, ss.at[m, i], rsem.at[m, i], mate)) for i, (w, a, b) in enumerate(parts)]

    def start_factors(m, which):
        for k in range(2):

            @pl.when(c != k)
            def _():
                for when, copy in factor_copies(k, m):
                    if when == which:
                        copy.start()

    def wait_factors(which):
        for k in range(2):

            @pl.when(c == k)
            def _():
                for m in range(2):
                    for when, copy in factor_copies(k, m):
                        if when in which:
                            copy.wait_recv()

    def shard(k):
        return lax.rem(k + 4 * n, n)

    def sign(h):
        return 1 if h == 0 else -1

    def home(h, t):
        return shard(me + sign(h) - sign(h) * t)

    def products(terms):
        total = None
        for a, b in terms:
            part = dot(a[...], b[...], 0, 0)
            total = part if total is None else total + part
        return total

    def pick(total, j):
        return jnp.where(lax.rem(j, 2) == 1, total[REST:], total[:REST])

    def tile(sub, h, j):
        side = pl.ds(h * COLS, COLS)
        if sub == 0:
            last = jnp.where(j >= (3 * n) // 4, 1, 0)
            own = jnp.where(c == 1, 2, last)
            other = jnp.where(c == 1, 0, last)
            cols = lanes(j, COLS)
            terms = [(zz.at[m, own, :, side], rr.at[m, c, :, cols]) for m in range(2)]
            terms += [(rL.at[m, other, :, side], rR.at[m, :, cols]) for m in range(2)]
        elif sub == 1:
            mine = pl.ds(pl.multiple_of(c * (FF // 2) + j * TAIL, LANE), TAIL)
            cols = lanes(j, TAIL)
            terms = [(ab.at[m, :, mine], gin.at[m, :, side]) for m in range(2)]
            terms += [(rA.at[m, :, cols], rG.at[m, :, side]) for m in range(2)]
        elif sub == 2:
            block = j // 2 * 2 * REST
            mine = pl.ds(pl.multiple_of(c * (FF // 2) + LATER + block, LANE), 2 * REST)
            cols = pl.ds(pl.multiple_of(LATER + block, LANE), 2 * REST)
            terms = [(ab.at[m, :, mine], gin.at[m, :, side]) for m in range(2)]
            terms += [(rA.at[m, :, cols], rG.at[m, :, side]) for m in range(2)]
            return pick(products(terms), j)
        else:
            cols = lanes(j // 2, 2 * REST)
            terms = [(xA.at[m, :, cols], xG.at[m, :, side]) for m in range(2)]
            terms += [(xA.at[2 + m, :, cols], gout.at[m, :, side]) for m in range(2)]
            return pick(products(terms), j)
        return products(terms)

    parts = (pl.ds(0, COLS), pl.ds(COLS, TAIL), pl.ds(COLS + TAIL, REST), pl.ds(COLS + TAIL + REST, REST))
    active = (None, None, jnp.logical_not(lender), helper)

    def where_active(sub, run):
        if active[sub] is None:
            run()
        else:
            pl.when(active[sub])(run)


    def gathered(sub, h, j):
        if sub == 0:
            return wf.at[0, pl.ds(h * COLS, COLS), lanes(j, COLS)]
        first_row, count = ((0, TAIL), (LATER, REST), (2 * LATER, REST))[sub - 1]
        return w2.at[pl.ds(pl.multiple_of(first_row + j * count, 16), count), pl.ds(h * COLS, COLS)]

    def scatter(h, t, sub):
        src, dst = buf.at[h, t, parts[sub], :], buf.at[h, t + 1, parts[sub], :]
        return remote(src, dst, ssem.at[h, t, sub], rcem.at[h, t + 1, sub], nexts[h])

    def spread(h, t, sub, j):
        ref = gathered(sub, h, j)
        return remote(ref, ref, ssem.at[h, n - 1 + t, sub], rcem.at[h, n + t, sub], nexts[h])

    def write(h, j, sub):
        if sub == 0:
            dst = out1.at[pl.ds(h * COLS, COLS), lanes(j, COLS)]
        else:
            first_row, count = ((0, TAIL), (LATER, REST), (LATER, REST))[sub - 1]
            dst = out2.at[pl.ds(pl.multiple_of(first_row + j * count, 16), count), pl.ds(h * COLS, COLS)]
        if sub == 3:
            return remote(gathered(sub, h, j), dst, bs.at[h, j], br.at[h, j], diagonal)
        return pltpu.make_async_copy(gathered(sub, h, j), dst, osem.at[h, j, sub])

    def lend(m):
        own = ab.at[m, :, pl.ds(LATER, FF // 2 - LATER)]
        other = rA.at[m, :, pl.ds(LATER, FF // 2 - LATER)]
        return (
            remote(own, xA.at[m], xs.at[m], xr.at[m], diagonal),
            remote(other, xA.at[2 + m], xs.at[2 + m], xr.at[2 + m], diagonal),
        )

    def share(m):
        return remote(gout.at[m], xG.at[m], ys.at[m], yr.at[m], mate)

    def reduce_event(sub, h, e):
        total = tile(sub, h, shard(me - sign(h) * e))

        @pl.when(e == 0)
        def _():
            buf[h, 0, parts[sub], :] = total.astype(BF)
            scatter(h, 0, sub).start()

        @pl.when((e > 0) & (e < n - 1))
        def _():
            scatter(h, e - 1, sub).wait_recv()
            buf[h, e, parts[sub], :] = (total + buf[h, e, parts[sub], :].astype(F32)).astype(BF)
            scatter(h, e, sub).start()

        @pl.when(e == n - 1)
        def _():
            j = home(h, 0)
            scatter(h, n - 2, sub).wait_recv()
            gathered(sub, h, j)[...] = (total + buf[h, n - 1, parts[sub], :].astype(F32)).astype(BF)
            pl.semaphore_wait(free.at[h, sub], 1)
            spread(h, 0, sub, j).start()
            write(h, j, sub).start()

    def event(sub, e):
        for h in range(2):

            @pl.when(e < n)
            def _():
                reduce_event(sub, h, e)

            @pl.when((e >= n) & (e < 2 * n - 1))
            def _():
                t = e - (n - 1)
                j = home(h, t)
                spread(h, t - 1, sub, j).wait_recv()

                @pl.when(t < n - 1)
                def _():
                    spread(h, t, sub, j).start()

                write(h, j, sub).start()

    def early_event(e):
        event(1, e)
        where_active(2, lambda: event(2, e))

        @pl.when(c == 1)
        def _():
            event(0, e)

    def small(r):
        return remote(acc.at[r], got.at[r], sms.at[r], smr.at[r], partners[r])

    def forward(m, p):
        @pl.when(jnp.logical_not(early))
        def _():
            u_hop(m).wait_recv()

        @pl.when(early & (m == 1))
        def _():
            img_out.wait_recv()
            pad(raw, ubuf.at[0, 1])

        once = p == 0

        def first_time(k, i):
            @pl.when(once)
            def _():
                wait_weight(k, i)

        first_time(0, 5)
        front_forward(0, m, ubuf, msk, pr, U, C, zz, xh, rs)
        for i in range(3):
            first_time(0, i)
            qkv[m, :, pl.ds(i * D, D)] = dot(zz[m, 0], wf[0, :, pl.ds(i * D, D)]).astype(BF).astype(F32)

        @pl.when(early)
        def _():
            window_forward(m, qkv, pw, T)

        @pl.when(jnp.logical_not(early))
        def _():
            channel_forward(m, qkv, pc, T, msk)

        first_time(0, 3)
        zz[m, 1] = T[...].astype(BF)
        ubuf[1, m] = (C[...] + dot(zz[m, 1], wf[0, :, pl.ds(3 * D, D)])).astype(BF)

        first_time(1, 5)
        front_forward(1, m, ubuf, msk, pr, U, C, zz, xh, rs)
        for i in range(4):
            first_time(1, i)
        first_time(0, 4)
        first_time(1, 4)

        for t in range(FF // FTILE):
            cols = pl.ds(t * FTILE, FTILE)
            a, d = gelu_parts(dot(zz[m, 2], wf[1, :, cols]))
            ab[m, :, cols] = a.astype(BF)
            rr[m, 1, :, cols] = d.astype(BF)
        gout[m] = (C[...] + dot(ab[m], w2[...])).astype(BF)

        @pl.when(early)
        def _():
            u_hop(m).start()

        @pl.when(jnp.logical_not(early))
        def _():
            for l in range(D // LANE):
                cols = pl.ds(l * LANE, LANE)
                C[:, cols] = gout[m, :, cols].astype(F32) * msk[m]
            unpad(flat.at[m])

        @pl.when(jnp.logical_not(early) & (m == 0))
        def _():
            remote(flat.at[0], act, es.at[0], er.at[0], opposite).start()

        @pl.when(jnp.logical_not(early) & (m == 1))
        def _():
            pltpu.make_async_copy(flat.at[1], act, es.at[0]).start()

        start_factors(m, "F")

        @pl.when(early & (m == 1))
        def _():
            wait_factors("F")

        @pl.when(lender & (m == 1))
        def _():
            for i in range(2):
                for copy in lend(i):
                    copy.start()

    def backward(m):
        @pl.when(early)
        def _():
            g_hop(m).wait_recv()

        @pl.when(jnp.logical_not(early))
        def _():
            @pl.when(m == 0)
            def _():
                cot_out.wait_recv()
                pad(raw, gin.at[0])

            for l in range(D // LANE):
                cols = pl.ds(l * LANE, LANE)
                gin[m, :, cols] = (gin[m, :, cols].astype(F32) * msk[m]).astype(BF)

        for t in range(FF // FTILE):
            cols = pl.ds(t * FTILE, FTILE)
            da = dot(gin[m], w2[cols, :], 1, 1)
            rr[m, 1, :, cols] = (da * rr[m, 1, :, cols].astype(F32)).astype(BF)
        T[...] = dot(rr[m, 1], wf[1], 1, 1)
        start_factors(m, "M")
        last = pl.ds(3 * D, D)

        @pl.when(early)
        def _():
            u_hop(m).wait_send()

        def tail_lanes(i):
            return rr.at[m, 0, :, pl.ds(pl.multiple_of(3 * D + i * LANE, LANE), LANE)]

        front_backward(1, m, ubuf, msk, pr, U, T, lambda i: gin.at[m, :, lanes(i)], xh, rs, sgp, tail_lanes)
        start_factors(m, "G")

        @pl.when(m == 1)
        def _():
            @pl.when(jnp.logical_not(early))
            def _():
                wait_factors("F")

            wait_factors("M")
            early_event(0)

        T[...] = dot(rr[m, 0, :, last], wf[0, :, last], 1, 1)

        @pl.when(early)
        def _():
            window_backward(m, qkv, pw, T)

        @pl.when(jnp.logical_not(early))
        def _():
            channel_backward(m, qkv, pc, T, msk)

        for i in range(3):
            cols = pl.ds(i * D, D)
            rr[m, 0, :, cols] = qkv[m, :, cols].astype(BF)
        start_factors(m, "A")

        @pl.when(m == 1)
        def _():
            for e in range(1, EARLY):
                early_event(e)

        T[...] = dot(rr[m, 0, :, pl.ds(0, 3 * D)], wf[0, :, pl.ds(0, 3 * D)], 1, 1)
        front_backward(0, m, ubuf, msk, pr, U, T, tail_lanes, xh, rs, sgp, lambda i: gout.at[m, :, lanes(i)])

        @pl.when(jnp.logical_not(early))
        def _():
            g_hop(m).start()

        @pl.when(s == 2)
        def _():
            share(m).start()

        @pl.when(early)
        def _():
            C[...] = gout[m].astype(F32)
            unpad(flat.at[m])

        @pl.when(early & (m == 0))
        def _():
            pltpu.make_async_copy(flat.at[0], ing, es.at[1]).start()

        @pl.when(early & (m == 1))
        def _():
            remote(flat.at[1], ing, es.at[1], er.at[1], opposite).start()

    def phase(p, carry):
        m = jnp.where(early, lax.rem(p, 2), p // 2)
        ahead = jnp.where(early, p < 2, lax.rem(p, 2) == 0)

        @pl.when(ahead)
        def _():
            forward(m, p)

        @pl.when(jnp.logical_not(ahead))
        def _():
            backward(m)

        return carry

    lax.fori_loop(0, 4, phase, 0)

    for h in range(2):
        for sub in range(4):

            def ready():
                pl.semaphore_signal(free.at[h, sub], inc=1, device_id=nexts[1 - h], device_id_type=MESH)

            where_active(sub, ready)

    for sec in range(2):
        for j in range(12):
            sgs[sec, j : j + 1, :] = jnp.sum(sgp[sec, j], axis=0, keepdims=True)
        sgs[sec, 12:16, :] = jnp.zeros((4, D), F32)
    give = remote(sgs.at[1 - c], sgm, sgsem.at[0], sgsem.at[1], mate)
    give.start()
    wait_factors("GA")

    @pl.when(helper)
    def _():
        for m in range(2):
            for copy in lend(m):
                copy.wait_recv()
            share(m).wait_recv()

    def ring_step(t, carry):
        event(1, t + EARLY)
        where_active(2, lambda: event(2, t + EARLY))
        where_active(3, lambda: event(3, t))
        event(0, t + jnp.where(c == 1, EARLY, 0))
        for r in range(rounds + 1):

            @pl.when(t == 1 + 3 * r)
            def _():
                if r == 0:
                    give.wait_recv()
                    acc[0] = sgs[c] + sgm[...]
                else:
                    small(r - 1).wait_recv()
                    acc[r] = acc[r - 1] + got[r - 1]
                if r < rounds:
                    small(r).start()

        return carry

    lax.fori_loop(0, 2 * n - 1, ring_step, 0)
    outs[...] = acc[rounds]

    for k in range(2):

        @pl.when(c == k)
        def _():
            for copy in weight_copies(k)[1]:
                copy.wait_send()
            params_copy(k).wait_send()
            for m in range(2):
                for _when, copy in factor_copies(1 - k, m):
                    copy.wait_send()

    give.wait_send()
    for r in range(rounds):
        small(r).wait_send()

    def drain(t, carry):
        for h in range(2):
            for sub in range(4):

                def sent():
                    scatter(h, t, sub).wait_send()
                    spread(h, t, sub, home(h, t)).wait_send()

                where_active(sub, sent)

        return carry

    lax.fori_loop(0, n - 1, drain, 0)

    def written(j, carry):
        for h in range(2):
            for sub in range(3):
                where_active(sub, lambda: write(h, j, sub).wait())

            @pl.when(helper)
            def _():
                write(h, j, 3).wait_send()

            @pl.when(lender)
            def _():
                write(h, j, 3).wait_recv()

        return carry

    lax.fori_loop(0, n, written, 0)

    @pl.when(lender)
    def _():
        for m in range(2):
            for copy in lend(m):
                copy.wait_send()

    @pl.when(s == 2)
    def _():
        for m in range(2):
            share(m).wait_send()

    @pl.when(early)
    def _():
        cot_out.wait_send()
        pltpu.make_async_copy(flat.at[0], ing, es.at[1]).wait()
        remote(flat.at[1], ing, es.at[1], er.at[1], opposite).wait_send()
        remote(flat.at[0], act, es.at[0], er.at[0], opposite).wait_recv()

    @pl.when(jnp.logical_not(early))
    def _():
        img_out.wait_send()
        for m in range(2):
            g_hop(m).wait_send()
        remote(flat.at[0], act, es.at[0], er.at[0], opposite).wait_send()
        pltpu.make_async_copy(flat.at[1], act, es.at[0]).wait()
        remote(flat.at[1], ing, es.at[1], er.at[1], opposite).wait_recv()


def relay(wrows, wcols, img, cot, kern, bias, gain, move, first, second):
    shape = jax.ShapeDtypeStruct
    vmem = pl.BlockSpec(memory_space=pltpu.VMEM)
    anywhere = pl.BlockSpec(memory_space=pl.ANY)
    dma = pltpu.SemaphoreType.DMA
    smem = pl.BlockSpec(memory_space=pltpu.SMEM)
    image = (ROWS, D)
    slot = img.shape
    rounds = RING.bit_length() - 1
    return pl.pallas_call(
        relay_kernel,
        out_shape=[
            shape(slot, BF),
            shape(slot, BF),
            shape((D, FF), BF),
            shape((FF // 2, D), BF),
            shape((16, D), F32),
        ],
        in_specs=[smem] * 2 + [vmem] * 6 + [anywhere] * 2,
        out_specs=[anywhere] * 4 + [vmem],
        scratch_shapes=[
            pltpu.VMEM((2, D, FF), BF),
            pltpu.VMEM((FF, D), BF),
            pltpu.VMEM((2, 16, D), F32),
            pltpu.VMEM((2, ROWS, LANE), F32),
            pltpu.VMEM(slot, BF),
            pltpu.VMEM((2,) + slot, BF),
            pltpu.VMEM((2, 2) + image, BF),
            pltpu.VMEM((2,) + image, BF),
            pltpu.VMEM((2,) + image, BF),
            pltpu.VMEM((2, 3) + image, BF),
            pltpu.VMEM((2, 2) + image, BF),
            pltpu.VMEM((2, 2, ROWS, LANE), F32),
            pltpu.VMEM((2, ROWS, 3 * D), F32),
            pltpu.VMEM((2, ROWS, FF), BF),
            pltpu.VMEM((2, 2, ROWS, FF), BF),
            pltpu.VMEM((2, UNITS, PACK * WROWS, WROWS), F32),
            pltpu.VMEM((2, NGROUP, GROUP, GROUP), F32),
            pltpu.VMEM((SIDE, GRID + 2, CELL, D), F32),
            pltpu.VMEM(image, F32),
            pltpu.VMEM(image, F32),
            pltpu.VMEM((2, 12, CELL, D), F32),
            pltpu.VMEM((2, 16, D), F32),
            pltpu.VMEM((16, D), F32),
            pltpu.VMEM((2, 2) + image, BF),
            pltpu.VMEM((2, ROWS, FF), BF),
            pltpu.VMEM((2, ROWS, FF // 2), BF),
            pltpu.VMEM((2,) + image, BF),
            pltpu.VMEM((4, ROWS, FF // 2 - LATER), BF),
            pltpu.VMEM((2,) + image, BF),
            pltpu.VMEM((2, RING, COLS + TAIL + 2 * REST, COLS), BF),
            pltpu.VMEM((rounds + 1, 16, D), F32),
            pltpu.VMEM((rounds, 16, D), F32),
            dma((5,)),
            dma((6,)),
            dma((6,)),
            dma((2,)),
            dma((2,)),
            dma((2,)),
            dma((2,)),
            dma((2,)),
            dma((2, 6)),
            dma((2, 6)),
            dma((2,)),
            dma((2,)),
            dma((2,)),
            dma((2, 2 * RING, 4)),
            dma((2, 2 * RING, 4)),
            dma((2, RING, 3)),
            dma((rounds,)),
            dma((rounds,)),
            dma((4,)),
            dma((4,)),
            dma((2,)),
            dma((2,)),
            dma((2, RING)),
            dma((2, RING)),
            pltpu.SemaphoreType.REGULAR((2, 4)),
        ],
        name="relay",
        compiler_params=pltpu.CompilerParams(
            collective_id=1, has_side_effects=True, vmem_limit_bytes=62 * 2**20
        ),
    )(wrows, wcols, img, cot, kern, bias, gain, move, first, second)


STEPS = 8


def finish_kernel(out1, out2, act, ing, outs, first, second, acts, ings, kern, bias, gain, move, sem):
    first[...] = out1[...].astype(F32)
    second[...] = out2[...].astype(F32)
    step = pl.program_id(0)
    copy = pltpu.make_async_copy(act, acts, sem.at[0])

    @pl.when(step == 0)
    def _():
        copy.start()
        for k in range(9):
            kern[k] = outs[k : k + 1, :]
        bias[...] = outs[9:10, :]
        gain[...] = outs[10:11, :]
        move[...] = outs[11:12, :]
        for r in range(GRID):
            line = ing[r].astype(F32)
            for k in range(GRID):
                ings[r, k] = line[k : k + 1, :]

    @pl.when(step == STEPS - 1)
    def _():
        copy.wait()


def finish(out1, out2, act, ing, outs):
    shape = jax.ShapeDtypeStruct
    slot = act.shape

    def split(like):
        return pl.BlockSpec((like.shape[0] // STEPS,) + like.shape[1:], lambda i: (i, 0))

    def whole(dims):
        return pl.BlockSpec(dims, lambda i: (0,) * len(dims))

    anywhere = pl.BlockSpec(memory_space=pl.ANY)
    line = (1, D)
    spread = slot[:2] + line
    return pl.pallas_call(
        finish_kernel,
        grid=(STEPS,),
        out_shape=[
            shape(out1.shape, F32),
            shape(out2.shape, F32),
            shape(slot, BF),
            shape(spread, F32),
            shape((9,) + line, F32),
            shape(line, F32),
            shape(line, F32),
            shape(line, F32),
        ],
        in_specs=[split(out1), split(out2), anywhere, whole(slot), whole(outs.shape)],
        out_specs=[split(out1), split(out2), anywhere, whole(spread), whole((9,) + line)] + [whole(line)] * 3,
        scratch_shapes=[pltpu.SemaphoreType.DMA((1,))],
        name="finish",
        compiler_params=pltpu.CompilerParams(vmem_limit_bytes=60 * 2**20),
    )(out1, out2, act, ing, outs)


def per_device(
    images, cotangent, window_rows, window_cols, pos_kernel, pos_bias, norm_gain, norm_shift, first_weight, second_weight
):
    act, ing, out1, out2, outs = relay(
        window_rows, window_cols, images[0], cotangent[0], pos_kernel[0], pos_bias, norm_gain, norm_shift,
        first_weight[0], second_weight,
    )
    if lax.axis_size("dp") > RING:
        out1, out2, outs = lax.psum((out1.astype(F32) / RING, out2.astype(F32) / RING, outs / RING), "dp")
    out1, out2, act, ing, kern, bias, gain, move = finish(out1, out2, act, ing, outs)
    return (
        act[None],
        ing.transpose(2, 0, 1, 3),
        out1[None],
        out2,
        kern.transpose(1, 0, 2),
        bias,
        gain,
        move,
    )


def solution(mesh):
    in_specs = (
        P(("dp", "section"), None, None, None),
        P(("dp", "section"), None, None, None),
        P("dp"),
        P("dp"),
        P("section", None, None),
        P("section", None),
        P("section", None),
        P("section", None),
        P("section", None, None),
        P("section", None),
    )
    out_specs = (
        P(("dp", "section"), None, None, None),
        P(("dp", "section"), None, None, None),
        P("section", None, None),
        P("section", None),
        P("section", None, None),
        P("section", None),
        P("section", None),
        P("section", None),
    )
    return jax.shard_map(per_device, mesh=mesh, in_specs=in_specs, out_specs=out_specs, check_vma=False)
```

```python
from functools import partial

import jax
import jax.numpy as jnp
from jax import lax
from jax.experimental import pallas as pl
from jax.experimental.pallas import tpu as pltpu
from jax.sharding import PartitionSpec as P

D = 768
FF = 3072
HEADS = 24
HEAD = 32
WIN = 7
SIDE = 2
GRID = SIDE * WIN
CELL = 8
WROWS = WIN * CELL
HALF = GRID * CELL
ROWS = SIDE * HALF
GROUP = 256
PACK = GROUP // HEAD
NGROUP = D // GROUP
UNITS = NGROUP * SIDE * SIDE
LANE = 128
FTILE = 1024
EPS = 1e-05
SCALE = HEAD ** (-0.5)
BF = jnp.bfloat16
F32 = jnp.float32
MESH = pl.DeviceIdType.MESH


def dot(a, b, ca=1, cb=0):
    return lax.dot_general(a, b, (((ca,), (cb,)), ((), ())), preferred_element_type=F32)


def lanes(index, width=LANE):
    return pl.ds(pl.multiple_of(index * width, width), width)


def halves(value):
    return value.reshape(SIDE, GRID, CELL, value.shape[-1])


def shifts(left, right):
    column = lax.broadcasted_iota(jnp.int32, left.shape, 1)
    before0 = pltpu.roll(left, 1, 1)
    after0 = jnp.where(column == WIN - 1, pltpu.roll(right, CELL - 2, 1), pltpu.roll(left, CELL - 1, 1))
    before1 = jnp.where(column == 0, pltpu.roll(left, 2, 1), pltpu.roll(right, 1, 1))
    after1 = pltpu.roll(right, CELL - 1, 1)
    return ((before0, left, after0), (before1, right, after1))


def gelu_parts(h):
    expo = jnp.exp(h * h * -0.5)
    t = 1.0 / (1.0 + (0.3275911 * 0.7071067811865476) * jnp.abs(h))
    poly = t * (0.127414796 + t * (-0.142248368 + t * (0.7107068705 + t * (-0.7265760135 + t * 0.5307027145))))
    tail = poly * expo
    phi = jnp.where(h >= 0, 1.0 - tail, tail)
    return h * phi, phi + h * expo * 0.3989422804014327


def front_forward(sec, m, ubuf, msk, pr, U, C, zz, xh, rs):
    zero = jnp.zeros((ROWS, LANE), F32)

    def conv(i, total):
        ls = lanes(i)
        u = ubuf[sec, m, :, ls].astype(F32)
        masked = halves(u * msk[m])
        U[0, 1 : GRID + 1, :, ls] = masked[0]
        U[1, 1 : GRID + 1, :, ls] = masked[1]
        moved = shifts(U[0, :, :, ls], U[1, :, :, ls])
        taps = pr[sec, :, ls]
        uh = halves(u)
        sums = []
        for wc in range(SIDE):
            acc = uh[wc] + taps[9:10, :][None]
            for a in range(3):
                for b in range(3):
                    acc = acc + moved[wc][b][a : a + GRID] * taps[3 * a + b : 3 * a + b + 1, :][None]
            acc = acc.reshape(HALF, LANE)
            C[pl.ds(wc * HALF, HALF), ls] = acc
            sums.append(acc)
        return total + jnp.concatenate(sums, axis=0)

    mean = jnp.sum(lax.fori_loop(0, D // LANE, conv, zero), axis=-1, keepdims=True) * (1.0 / D)

    def spread(i, total):
        centred = C[:, lanes(i)] - mean
        return total + centred * centred

    var = jnp.sum(lax.fori_loop(0, D // LANE, spread, zero), axis=-1, keepdims=True) * (1.0 / D)
    rstd = lax.rsqrt(var + EPS)
    rs[sec, m] = jnp.broadcast_to(rstd, (ROWS, LANE))

    def norm(i, carry):
        ls = lanes(i)
        xhat = (C[:, ls] - mean) * rstd
        xh[sec, m, :, ls] = xhat.astype(BF)
        zz[m, 2 * sec, :, ls] = (xhat * pr[sec, 10:11, ls] + pr[sec, 11:12, ls]).astype(BF)
        return carry

    lax.fori_loop(0, D // LANE, norm, 0)


def front_backward(sec, m, ubuf, msk, pr, U, T, gfull, xh, rs, sgp, out):
    zero = jnp.zeros((ROWS, LANE), F32)

    def fold(value):
        return jnp.sum(value.reshape(ROWS // CELL, CELL, LANE), axis=0)

    def sums(i, carry):
        s1, s2 = carry
        ls = lanes(i)
        dz = T[:, ls]
        xhat = xh[sec, m, :, ls].astype(F32)
        both = xhat * dz
        sgp[sec, 10, :, ls] += fold(both)
        sgp[sec, 11, :, ls] += fold(dz)
        gain = pr[sec, 10:11, ls]
        return s1 + dz * gain, s2 + both * gain

    s1, s2 = lax.fori_loop(0, D // LANE, sums, (zero, zero))
    m1 = jnp.sum(s1, axis=-1, keepdims=True) * (1.0 / D)
    m2 = jnp.sum(s2, axis=-1, keepdims=True) * (1.0 / D)

    def back(i, carry):
        ls = lanes(i)
        xhat = xh[sec, m, :, ls].astype(F32)
        inner = T[:, ls] * pr[sec, 10:11, ls] - m1 - xhat * m2
        gc = gfull(i)[...].astype(F32) + rs[sec, m] * inner
        sgp[sec, 9, :, ls] += fold(gc)
        gh = halves(gc)
        U[0, 1 : GRID + 1, :, ls] = gh[0]
        U[1, 1 : GRID + 1, :, ls] = gh[1]
        moved = shifts(U[0, :, :, ls], U[1, :, :, ls])
        taps = pr[sec, :, ls]
        mask = halves(msk[m])
        um = halves(ubuf[sec, m, :, ls].astype(F32) * msk[m])
        accs = [jnp.zeros((GRID, CELL, LANE), F32) for _ in range(SIDE)]
        for a in range(3):
            for b in range(3):
                tap = 3 * a + b
                kg = jnp.zeros((CELL, LANE), F32)
                for wc in range(SIDE):
                    gs = moved[wc][2 - b][2 - a : 2 - a + GRID]
                    accs[wc] = accs[wc] + gs * taps[tap : tap + 1, :][None]
                    kg = kg + jnp.sum(gs * um[wc], axis=0)
                sgp[sec, tap, :, ls] += kg
        du = [(gh[wc] + mask[wc] * accs[wc]).reshape(HALF, LANE) for wc in range(SIDE)]
        out(i)[...] = jnp.concatenate(du, axis=0).astype(BF)
        return carry

    lax.fori_loop(0, D // LANE, back, 0)


def spread_heads(value, head_of_lane):
    parts = [jnp.where(head_of_lane == h, value, 0.0) for h in range(PACK)]
    return jnp.concatenate(parts, axis=0).astype(BF)


def gather_heads(value, rows, head_of_lane):
    out = jnp.zeros((rows, GROUP), F32)
    for h in range(PACK):
        out = jnp.where(head_of_lane == h, value[h * rows : (h + 1) * rows], out)
    return out


def unit_slices(unit):
    pair, group = unit // NGROUP, lax.rem(unit, NGROUP)
    rows = [pl.ds(pl.multiple_of((2 * pair + w) * WROWS, 8), WROWS) for w in range(2)]
    cols = [pl.ds(pl.multiple_of(part * D + group * GROUP, LANE), GROUP) for part in range(3)]
    return rows, cols


def window_parts(m, i, qkv):
    rows, cols = unit_slices(i)
    head_of_lane = lax.broadcasted_iota(jnp.int32, (WROWS, GROUP), 1) // HEAD
    q = [qkv[m, r, cols[0]].astype(BF) for r in rows]
    kd = [spread_heads(qkv[m, r, cols[1]], head_of_lane) for r in rows]
    vd = [spread_heads(qkv[m, r, cols[2]], head_of_lane) for r in rows]
    return rows, cols, head_of_lane, q, kd, vd


def window_forward(m, qkv, pw, T):
    def unit(i, carry):
        rows, cols, head_of_lane, q, kd, vd = window_parts(m, i, qkv)
        s = [(dot(b, a, 1, 1) * SCALE).reshape(PACK, WROWS, WROWS) for a, b in zip(q, kd)]
        key = lax.broadcasted_iota(jnp.int32, s[0].shape, 1)
        real = lax.rem(key, CELL) < WIN
        s = [jnp.where(real, x, -1e30) for x in s]
        p = [jnp.exp(x - jnp.max(x, axis=1, keepdims=True)) for x in s]
        p = [x * (1.0 / jnp.sum(x, axis=1, keepdims=True)) for x in p]
        p = [x.reshape(PACK * WROWS, WROWS) for x in p]
        for w in range(2):
            pw[m, 2 * i + w, :, 0:WROWS] = p[w]
        out = [dot(x.astype(BF), v, 0, 0) for x, v in zip(p, vd)]
        for w in range(2):
            T[rows[w], cols[0]] = out[w]
        return carry

    lax.fori_loop(0, UNITS // 2, unit, 0)


def window_backward(m, qkv, pw, T):
    def unit(i, carry):
        rows, cols, head_of_lane, q, kd, vd = window_parts(m, i, qkv)
        g = [T[r, cols[0]].astype(BF) for r in rows]
        p = [pw[m, 2 * i + w, :, 0:WROWS].reshape(PACK, WROWS, WROWS) for w in range(2)]
        dp = [dot(v, x, 1, 1).reshape(PACK, WROWS, WROWS) for v, x in zip(vd, g)]
        ds = [x * (y - jnp.sum(x * y, axis=1, keepdims=True)) for x, y in zip(p, dp)]
        ds = [x.reshape(PACK * WROWS, WROWS).astype(BF) for x in ds]
        pb = [x.reshape(PACK * WROWS, WROWS).astype(BF) for x in p]
        dv = [gather_heads(dot(x, y), WROWS, head_of_lane) for x, y in zip(pb, g)]
        dk = [gather_heads(dot(x, y), WROWS, head_of_lane) * SCALE for x, y in zip(ds, q)]
        dq = [dot(x, y, 0, 0) * SCALE for x, y in zip(ds, kd)]
        for w in range(2):
            qkv[m, rows[w], cols[0]] = dq[w]
            qkv[m, rows[w], cols[1]] = dk[w]
            qkv[m, rows[w], cols[2]] = dv[w]
        return carry

    lax.fori_loop(0, UNITS // 2, unit, 0)


def group_slices(group):
    return [pl.ds(pl.multiple_of(part * D + group * GROUP, LANE), GROUP) for part in range(3)]


def channel_forward(m, qkv, pw, T, msk):
    def unit(i, carry):
        cols = group_slices(i)
        mask = msk[m][:, :1]
        q = qkv[m, :, cols[0]].astype(BF)
        k = (qkv[m, :, cols[1]] * mask).astype(BF)
        v = qkv[m, :, cols[2]].astype(BF)
        s = dot(q, k, 0, 0) * SCALE
        same = (lax.broadcasted_iota(jnp.int32, s.shape, 0) // HEAD) == (lax.broadcasted_iota(jnp.int32, s.shape, 1) // HEAD)
        s = jnp.where(same, s, -1e30)
        p = jnp.exp(s - jnp.max(s, axis=1, keepdims=True))
        p = p * (1.0 / jnp.sum(p, axis=1, keepdims=True))
        for k in range(GROUP // LANE):
            pw[m, 2 * i + k, 0:GROUP, :] = p[:, k * LANE : (k + 1) * LANE]
        T[:, cols[0]] = dot(v, p.astype(BF), 1, 1)
        return carry

    lax.fori_loop(0, NGROUP, unit, 0, unroll=True)


def channel_backward(m, qkv, pw, T, msk):
    def unit(i, carry):
        cols = group_slices(i)
        mask = msk[m][:, :1]
        q = qkv[m, :, cols[0]].astype(BF)
        k = (qkv[m, :, cols[1]] * mask).astype(BF)
        v = qkv[m, :, cols[2]].astype(BF)
        g = T[:, cols[0]].astype(BF)
        p = jnp.concatenate([pw[m, 2 * i + k, 0:GROUP, :] for k in range(GROUP // LANE)], axis=1)
        dp = dot(g, v, 0, 0)
        ds = (p * (dp - jnp.sum(p * dp, axis=1, keepdims=True))).astype(BF)
        qkv[m, :, cols[0]] = dot(k, ds, 1, 1) * SCALE
        qkv[m, :, cols[1]] = dot(q, ds) * (SCALE * mask)
        qkv[m, :, cols[2]] = dot(g, p.astype(BF))
        return carry

    lax.fori_loop(0, NGROUP, unit, 0, unroll=True)


RING = 8
COLS = FF // RING
WIDE = FF // 12 * 8 // RING
REST = FF // 6 // RING
FIFTH, SIXTH = FF // 6 * 4, FF // 6 * 5
EARLY = 2


def relay_kernel(
    wrows, wcols, img, cot, kern, bias, gain, move, first, second,
    act, ing, out1, out2, outs,
    wf, w2, pr, msk, flat, ubuf, gin, gout, zz, xh, rs, qkv, ab, rr, pw, U, C, T, sgp, sgs, sgm,
    rL, rR, rA, rG, xA, xG, buf, acc, got,
    wl, ws, wr, pl_, usem, gsem, us, gs, ss, rsem, es, er, sgsem, ssem, rcem, osem, sms, smr, xs, xr, ys, yr, bs, br, hs, hr, free,
):
    n = RING
    s = lax.axis_index("section")
    dp = lax.axis_index("dp")
    stage, c = s // 2, lax.rem(s, 2)
    mate = (dp, stage * 2 + (1 - c))
    opposite = (dp, (1 - stage) * 2 + c)
    lender, helper = s == 1, s == 3
    early = stage == 0

    spot = lax.rem(dp, n)
    base = dp - spot
    me = jnp.where(lax.rem(spot, 2) == 0, spot // 2, n - 1 - spot // 2)

    def place(pos):
        pos = lax.rem(pos + 2 * n, n)
        return (base + jnp.where(pos < n // 2, 2 * pos, 2 * (n - 1 - pos) + 1), s)

    nexts = (place(me + 1), place(me - 1))
    rounds = n.bit_length() - 1
    partners = []
    for r in range(rounds):
        bit = 1 << r
        partners.append((jnp.where(lax.rem(spot // bit, 2) == 0, dp + bit, dp - bit), s))

    barrier = pltpu.get_barrier_semaphore()
    peers = [mate, opposite, *nexts, *partners]
    for peer in peers:
        pl.semaphore_signal(barrier, inc=1, device_id=peer, device_id_type=MESH)
    pl.semaphore_wait(barrier, len(peers))

    def remote(src, dst, send, recv, peer):
        return pltpu.make_async_remote_copy(
            src_ref=src, dst_ref=dst, send_sem=send, recv_sem=recv, device_id=peer, device_id_type=MESH
        )

    half = second.shape[0]

    def weight_parts(k):
        parts = []
        for i in range(4):
            parts.append((first.at[:, pl.ds(i * D, D)], wf.at[k, :, pl.ds(i * D, D)]))
        parts.append((second, w2.at[pl.ds(k * half, half), :]))
        return parts

    def weight_copies(k):
        local = [pltpu.make_async_copy(a, b, wl.at[i]) for i, (a, b) in enumerate(weight_parts(k))]
        sent = [remote(a, b, ws.at[i], wr.at[i], mate) for i, (a, b) in enumerate(weight_parts(k))]
        return local, sent

    def params_copy(k):
        return remote(pr.at[k], pr.at[k], ws.at[5], wr.at[5], mate)

    pr[c, 0:9, :] = kern[...].astype(F32)
    pr[c, 9:10, :] = bias[...].astype(F32)
    pr[c, 10:11, :] = gain[...].astype(F32)
    pr[c, 11:12, :] = move[...].astype(F32)
    params_copy(c).start()
    for k in range(2):

        @pl.when(c == k)
        def _():
            local, sent = weight_copies(k)
            for i in range(5):
                local[i].start()
                sent[i].start()

    def wait_weight(k, i):
        if i < 5:

            @pl.when(c == k)
            def _():
                weight_copies(k)[0][i].wait()

        @pl.when(c != k)
        def _():
            (weight_copies(k)[1][i] if i < 5 else params_copy(k)).wait_recv()

    raw = flat.at[0]
    img_out = remote(img, raw, pl_.at[0], pl_.at[1], opposite)
    cot_out = remote(cot, raw, pl_.at[0], pl_.at[1], opposite)

    def pad(src, dst):
        blank = jnp.zeros((CELL - WIN, D), F32)
        for r in range(GRID):
            line = src[r].astype(F32)
            for wc in range(SIDE):
                cells = jnp.concatenate([line[wc * WIN : (wc + 1) * WIN], blank], axis=0)
                C[pl.ds(wc * HALF + r * CELL, CELL), :] = cells
        dst[...] = C[...].astype(BF)

    def unpad(dst):
        for r in range(GRID):
            sides = [C[pl.ds(wc * HALF + r * CELL, CELL), :][:WIN] for wc in range(SIDE)]
            dst[r] = jnp.concatenate(sides, axis=0).astype(BF)

    @pl.when(early)
    def _():
        cot_out.start()
        pad(img, ubuf.at[0, 0])

    @pl.when(jnp.logical_not(early))
    def _():
        img_out.start()
        pad(cot, gin.at[1])

    index = lax.broadcasted_iota(jnp.int32, (ROWS, LANE), 0)
    cell = lax.rem(index, CELL)
    row = lax.rem(index, HALF) // CELL
    column = (index // HALF) * WIN + cell
    for m in range(2):
        inside = (row < WIN * wrows[c + 2 * m]) & (column < WIN * wcols[c + 2 * m]) & (cell < WIN)
        msk[m] = jnp.where(inside, 1.0, 0.0)

    @pl.when(jnp.logical_not(early))
    def _():
        cot_out.wait_recv()
        pad(raw, gin.at[0])
        for m in range(2):
            for l in range(D // LANE):
                cols = pl.ds(l * LANE, LANE)
                gin[m, :, cols] = (gin[m, :, cols].astype(F32) * msk[m]).astype(BF)

    for wc in range(SIDE):
        U[wc, 0] = jnp.zeros((CELL, D), F32)
        U[wc, GRID + 1] = jnp.zeros((CELL, D), F32)
    sgp[...] = jnp.zeros(sgp.shape, F32)

    def u_hop(m):
        return remote(gout.at[m], ubuf.at[0, m], us.at[m], usem.at[m], opposite)

    def g_hop(m):
        return remote(gout.at[m], gin.at[m], gs.at[m], gsem.at[m], opposite)

    def factor_copies(k, m):
        if k == 0:
            parts = [
                ("F", zz.at[m, 0], rL.at[m, 0]),
                ("F", zz.at[m, 1], rL.at[m, 1]),
                ("G", rr.at[m, 0, :, pl.ds(3 * D, D)], rR.at[m, :, pl.ds(3 * D, D)]),
                ("A", rr.at[m, 0, :, pl.ds(0, 3 * D)], rR.at[m, :, pl.ds(0, 3 * D)]),
            ]
        else:
            parts = [
                ("F", zz.at[m, 2], rL.at[m, 0]),
                ("F", ab.at[m], rA.at[m]),
                ("M", gin.at[m], rG.at[m]),
                ("M", rr.at[m, 1], rR.at[m]),
            ]
        return [(w, remote(a, b, ss.at[m, i], rsem.at[m, i], mate)) for i, (w, a, b) in enumerate(parts)]

    def start_factors(m, which):
        for k in range(2):

            @pl.when(c != k)
            def _():
                for when, copy in factor_copies(k, m):
                    if when == which:
                        copy.start()

    def wait_factors(which):
        for k in range(2):

            @pl.when(c == k)
            def _():
                for m in range(2):
                    for when, copy in factor_copies(k, m):
                        if when in which:
                            copy.wait_recv()

    def shard(k):
        return lax.rem(k + 4 * n, n)

    def sign(h):
        return 1 if h == 0 else -1

    def home(h, t):
        return shard(me + sign(h) - sign(h) * t)

    def products(terms):
        total = None
        for a, b in terms:
            part = dot(a[...], b[...], 0, 0)
            total = part if total is None else total + part
        return total

    def pick(total, j):
        return jnp.where(lax.rem(j, 2) == 1, total[REST:], total[:REST])

    def tile(sub, h, j):
        side = pl.ds(h * COLS, COLS)
        if sub == 0:
            last = jnp.where(j >= (3 * n) // 4, 1, 0)
            own = jnp.where(c == 1, 2, last)
            other = jnp.where(c == 1, 0, last)
            cols = lanes(j, COLS)
            terms = [(zz.at[m, own, :, side], rr.at[m, c, :, cols]) for m in range(2)]
            terms += [(rL.at[m, other, :, side], rR.at[m, :, cols]) for m in range(2)]
        elif sub == 1:
            cols = lanes(j, WIDE)
            terms = [(ab.at[m, :, cols], gin.at[m, :, side]) for m in range(2)]
            terms += [(rA.at[m, :, cols], rG.at[m, :, side]) for m in range(2)]
        else:
            start = (FIFTH if sub == 2 else SIXTH) + j // 2 * 2 * REST
            cols = pl.ds(pl.multiple_of(start, LANE), 2 * REST)
            terms = [(ab.at[m, :, cols], gin.at[m, :, side]) for m in range(2)]
            terms += [(rA.at[m, :, cols], rG.at[m, :, side]) for m in range(2)]
            own = pick(products(terms), j)
            if sub == 2:
                return own
            cols = lanes(j // 2, 2 * REST)
            terms = [(xA.at[m, :, cols], gout.at[m, :, side]) for m in range(2)]
            terms += [(xA.at[2 + m, :, cols], xG.at[m, :, side]) for m in range(2)]
            return jnp.concatenate([own, pick(products(terms), j)], axis=0)
        return products(terms)

    sizes = (COLS, WIDE, REST, 2 * REST)
    parts = [pl.ds(sum(sizes[:i]), size) for i, size in enumerate(sizes)]
    odd = c == 1
    active = (None, odd, odd, helper)

    def where_active(sub, run):
        if active[sub] is None:
            run()
        else:
            pl.when(active[sub])(run)


    def gathered(sub, h, j):
        if sub == 0:
            return wf.at[0, pl.ds(h * COLS, COLS), lanes(j, COLS)]
        if sub == 3:
            rows = pl.ds(pl.multiple_of(lax.rem(j, n // 2) * sizes[3], 16), sizes[3])
            return wf.at[1, rows, lanes(2 * (j // (n // 2)) + h, COLS)]
        first_row = 0 if sub == 1 else FIFTH
        return w2.at[pl.ds(pl.multiple_of(first_row + j * sizes[sub], 16), sizes[sub]), pl.ds(h * COLS, COLS)]

    def scatter(h, t, sub):
        src, dst = buf.at[h, t, parts[sub], :], buf.at[h, t + 1, parts[sub], :]
        return remote(src, dst, ssem.at[h, t, sub], rcem.at[h, t + 1, sub], nexts[h])

    def spread(h, t, sub, j):
        ref = gathered(sub, h, j)
        return remote(ref, ref, ssem.at[h, n - 1 + t, sub], rcem.at[h, n + t, sub], nexts[h])

    half_shards = n * 3 // 4

    def write(h, j, sub, part=0):
        src, side = gathered(sub, h, j), pl.ds(h * COLS, COLS)
        if sub == 0:
            dst = out1.at[side, lanes(j, COLS)]
        elif sub == 1:
            dst = out2.at[pl.ds(pl.multiple_of((j - half_shards) * WIDE, 16), WIDE), side]
        else:
            first_row = (FIFTH if sub == 2 else SIXTH) - FF // 2
            dst = out2.at[pl.ds(pl.multiple_of(first_row + j * REST, 16), REST), side]
            src = src.at[pl.ds(part * REST, REST), :]
        if part == 1:
            return remote(src, dst, bs.at[h, j], br.at[h, j], opposite)
        return pltpu.make_async_copy(src, dst, osem.at[h, j, sub])

    def hand_over(h, j):
        dst = out2.at[pl.ds(pl.multiple_of(j * WIDE, 16), WIDE), pl.ds(h * COLS, COLS)]
        return remote(gathered(1, h, j), dst, hs.at[h, j], hr.at[h, j], mate)

    def deliver(h, j, sub):
        if sub == 1:

            @pl.when(j < half_shards)
            def _():
                hand_over(h, j).start()

            @pl.when(j >= half_shards)
            def _():
                write(h, j, sub).start()

        else:
            write(h, j, sub).start()
            if sub == 3:
                write(h, j, sub, 1).start()

    def lend(m):
        cols = pl.ds(SIXTH, FF - SIXTH)
        return (
            remote(ab.at[m, :, cols], xA.at[m], xs.at[m], xr.at[m], opposite),
            remote(rA.at[m, :, cols], xA.at[2 + m], xs.at[2 + m], xr.at[2 + m], opposite),
        )

    def share(m):
        return remote(gout.at[m], xG.at[m], ys.at[m], yr.at[m], mate)

    def reduce_event(sub, h, e):
        total = tile(sub, h, shard(me - sign(h) * e))

        @pl.when(e == 0)
        def _():
            buf[h, 0, parts[sub], :] = total.astype(BF)
            scatter(h, 0, sub).start()

        @pl.when((e > 0) & (e < n - 1))
        def _():
            scatter(h, e - 1, sub).wait_recv()
            buf[h, e, parts[sub], :] = (total + buf[h, e, parts[sub], :].astype(F32)).astype(BF)
            scatter(h, e, sub).start()

        @pl.when(e == n - 1)
        def _():
            j = home(h, 0)
            scatter(h, n - 2, sub).wait_recv()
            gathered(sub, h, j)[...] = (total + buf[h, n - 1, parts[sub], :].astype(F32)).astype(BF)
            pl.semaphore_wait(free.at[h, sub], 1)
            spread(h, 0, sub, j).start()
            deliver(h, j, sub)

    def event(sub, e):
        for h in range(2):

            @pl.when(e < n)
            def _():
                reduce_event(sub, h, e)

            @pl.when((e >= n) & (e < 2 * n - 1))
            def _():
                t = e - (n - 1)
                j = home(h, t)
                spread(h, t - 1, sub, j).wait_recv()

                @pl.when(t < n - 1)
                def _():
                    spread(h, t, sub, j).start()

                deliver(h, j, sub)

    def early_event(e):
        @pl.when(odd)
        def _():
            for sub in range(3):
                event(sub, e)

    def small(r):
        return remote(acc.at[r], got.at[r], sms.at[r], smr.at[r], partners[r])

    def forward(m, p):
        @pl.when(jnp.logical_not(early))
        def _():
            u_hop(m).wait_recv()

        @pl.when(early & (m == 1))
        def _():
            img_out.wait_recv()
            pad(raw, ubuf.at[0, 1])

        once = p == 0

        def first_time(k, i):
            @pl.when(once)
            def _():
                wait_weight(k, i)

        first_time(0, 5)
        front_forward(0, m, ubuf, msk, pr, U, C, zz, xh, rs)
        for i in range(3):
            first_time(0, i)
            qkv[m, :, pl.ds(i * D, D)] = dot(zz[m, 0], wf[0, :, pl.ds(i * D, D)]).astype(BF).astype(F32)

        @pl.when(early)
        def _():
            window_forward(m, qkv, pw, T)

        @pl.when(jnp.logical_not(early))
        def _():
            channel_forward(m, qkv, pw, T, msk)

        first_time(0, 3)
        zz[m, 1] = T[...].astype(BF)
        ubuf[1, m] = (C[...] + dot(zz[m, 1], wf[0, :, pl.ds(3 * D, D)])).astype(BF)

        first_time(1, 5)
        front_forward(1, m, ubuf, msk, pr, U, C, zz, xh, rs)
        for i in range(4):
            first_time(1, i)
        first_time(0, 4)
        first_time(1, 4)

        for t in range(FF // FTILE):
            cols = pl.ds(t * FTILE, FTILE)
            a, d = gelu_parts(dot(zz[m, 2], wf[1, :, cols]))
            ab[m, :, cols] = a.astype(BF)
            rr[m, 1, :, cols] = d.astype(BF)
        gout[m] = (C[...] + dot(ab[m], w2[...])).astype(BF)

        @pl.when(early)
        def _():
            u_hop(m).start()

        @pl.when(jnp.logical_not(early))
        def _():
            for l in range(D // LANE):
                cols = pl.ds(l * LANE, LANE)
                C[:, cols] = gout[m, :, cols].astype(F32) * msk[m]
            unpad(flat.at[m])

        @pl.when(jnp.logical_not(early) & (m == 0))
        def _():
            remote(flat.at[0], act, es.at[0], er.at[0], opposite).start()

        @pl.when(jnp.logical_not(early) & (m == 1))
        def _():
            pltpu.make_async_copy(flat.at[1], act, es.at[0]).start()

        start_factors(m, "F")

        @pl.when(early & (m == 1))
        def _():
            wait_factors("F")

        @pl.when(lender & (m == 1))
        def _():
            for i in range(2):
                for copy in lend(i):
                    copy.start()

    def backward(m):
        @pl.when(early)
        def _():
            g_hop(m).wait_recv()

        for t in range(FF // FTILE):
            cols = pl.ds(t * FTILE, FTILE)
            da = dot(gin[m], w2[cols, :], 1, 1)
            rr[m, 1, :, cols] = (da * rr[m, 1, :, cols].astype(F32)).astype(BF)
        T[...] = dot(rr[m, 1], wf[1], 1, 1)
        start_factors(m, "M")
        last = pl.ds(3 * D, D)

        @pl.when(early)
        def _():
            u_hop(m).wait_send()

        def tail_lanes(i):
            return rr.at[m, 0, :, pl.ds(pl.multiple_of(3 * D + i * LANE, LANE), LANE)]

        front_backward(1, m, ubuf, msk, pr, U, T, lambda i: gin.at[m, :, lanes(i)], xh, rs, sgp, tail_lanes)
        start_factors(m, "G")

        @pl.when(m == 1)
        def _():
            @pl.when(jnp.logical_not(early))
            def _():
                wait_factors("F")

            wait_factors("M")
            early_event(0)

        T[...] = dot(rr[m, 0, :, last], wf[0, :, last], 1, 1)

        @pl.when(early)
        def _():
            window_backward(m, qkv, pw, T)

        @pl.when(jnp.logical_not(early))
        def _():
            channel_backward(m, qkv, pw, T, msk)

        for i in range(3):
            cols = pl.ds(i * D, D)
            rr[m, 0, :, cols] = qkv[m, :, cols].astype(BF)
        start_factors(m, "A")

        @pl.when(m == 1)
        def _():
            for e in range(1, EARLY):
                early_event(e)

        T[...] = dot(rr[m, 0, :, pl.ds(0, 3 * D)], wf[0, :, pl.ds(0, 3 * D)], 1, 1)
        front_backward(0, m, ubuf, msk, pr, U, T, tail_lanes, xh, rs, sgp, lambda i: gout.at[m, :, lanes(i)])

        @pl.when(jnp.logical_not(early))
        def _():
            g_hop(m).start()

        @pl.when(s == 2)
        def _():
            share(m).start()

        @pl.when(early)
        def _():
            C[...] = gout[m].astype(F32)
            unpad(flat.at[m])

        @pl.when(early & (m == 0))
        def _():
            pltpu.make_async_copy(flat.at[0], ing, es.at[1]).start()

        @pl.when(early & (m == 1))
        def _():
            remote(flat.at[1], ing, es.at[1], er.at[1], opposite).start()

    def phase(p, carry):
        m = jnp.where(early, lax.rem(p, 2), p // 2)
        ahead = jnp.where(early, p < 2, lax.rem(p, 2) == 0)

        @pl.when(ahead)
        def _():
            forward(m, p)

        @pl.when(jnp.logical_not(ahead))
        def _():
            backward(m)

        return carry

    lax.fori_loop(0, 4, phase, 0)

    for h in range(2):
        for sub in range(4):

            def ready():
                pl.semaphore_signal(free.at[h, sub], inc=1, device_id=nexts[1 - h], device_id_type=MESH)

            where_active(sub, ready)

    for sec in range(2):
        for j in range(12):
            sgs[sec, j : j + 1, :] = jnp.sum(sgp[sec, j], axis=0, keepdims=True)
        sgs[sec, 12:16, :] = jnp.zeros((4, D), F32)
    give = remote(sgs.at[1 - c], sgm, sgsem.at[0], sgsem.at[1], mate)
    give.start()
    wait_factors("GA")

    @pl.when(helper)
    def _():
        for m in range(2):
            for copy in lend(m):
                copy.wait_recv()
            share(m).wait_recv()

    def ring_step(t, carry):
        event(0, t + jnp.where(odd, EARLY, 0))
        where_active(1, lambda: event(1, t + EARLY))
        where_active(2, lambda: event(2, t + EARLY))
        where_active(3, lambda: event(3, t))
        for r in range(rounds + 1):

            @pl.when(t == 1 + 3 * r)
            def _():
                if r == 0:
                    give.wait_recv()
                    acc[0] = sgs[c] + sgm[...]
                else:
                    small(r - 1).wait_recv()
                    acc[r] = acc[r - 1] + got[r - 1]
                if r < rounds:
                    small(r).start()

        return carry

    lax.fori_loop(0, 2 * n - 1, ring_step, 0)
    outs[...] = acc[rounds]

    for k in range(2):

        @pl.when(c == k)
        def _():
            for copy in weight_copies(k)[1]:
                copy.wait_send()
            params_copy(k).wait_send()
            for m in range(2):
                for _when, copy in factor_copies(1 - k, m):
                    copy.wait_send()

    give.wait_send()
    for r in range(rounds):
        small(r).wait_send()

    def drain(t, carry):
        for h in range(2):
            for sub in range(4):

                def sent():
                    scatter(h, t, sub).wait_send()
                    spread(h, t, sub, home(h, t)).wait_send()

                where_active(sub, sent)

        return carry

    lax.fori_loop(0, n - 1, drain, 0)

    def written(j, carry):
        for h in range(2):
            write(h, j, 0).wait()

            @pl.when(odd)
            def _():
                write(h, j, 2).wait()

                @pl.when(j < half_shards)
                def _():
                    hand_over(h, j).wait_send()

                @pl.when(j >= half_shards)
                def _():
                    write(h, j, 1).wait()

            @pl.when(jnp.logical_not(odd) & (j < half_shards))
            def _():
                hand_over(h, j).wait_recv()

            @pl.when(helper)
            def _():
                write(h, j, 3).wait()
                write(h, j, 3, 1).wait_send()

            @pl.when(lender)
            def _():
                write(h, j, 3, 1).wait_recv()

        return carry

    lax.fori_loop(0, n, written, 0)

    @pl.when(lender)
    def _():
        for m in range(2):
            for copy in lend(m):
                copy.wait_send()

    @pl.when(s == 2)
    def _():
        for m in range(2):
            share(m).wait_send()

    @pl.when(early)
    def _():
        cot_out.wait_send()
        pltpu.make_async_copy(flat.at[0], ing, es.at[1]).wait()
        remote(flat.at[1], ing, es.at[1], er.at[1], opposite).wait_send()
        remote(flat.at[0], act, es.at[0], er.at[0], opposite).wait_recv()

    @pl.when(jnp.logical_not(early))
    def _():
        img_out.wait_send()
        for m in range(2):
            g_hop(m).wait_send()
        remote(flat.at[0], act, es.at[0], er.at[0], opposite).wait_send()
        pltpu.make_async_copy(flat.at[1], act, es.at[0]).wait()
        remote(flat.at[1], ing, es.at[1], er.at[1], opposite).wait_recv()


def relay(wrows, wcols, img, cot, kern, bias, gain, move, first, second):
    shape = jax.ShapeDtypeStruct
    vmem = pl.BlockSpec(memory_space=pltpu.VMEM)
    anywhere = pl.BlockSpec(memory_space=pl.ANY)
    dma = pltpu.SemaphoreType.DMA
    smem = pl.BlockSpec(memory_space=pltpu.SMEM)
    image = (ROWS, D)
    slot = img.shape
    rounds = RING.bit_length() - 1
    return pl.pallas_call(
        relay_kernel,
        out_shape=[
            shape(slot, BF),
            shape(slot, BF),
            shape((D, FF), BF),
            shape((FF // 2, D), BF),
            shape((16, D), F32),
        ],
        in_specs=[smem] * 2 + [vmem] * 6 + [anywhere] * 2,
        out_specs=[anywhere] * 4 + [vmem],
        scratch_shapes=[
            pltpu.VMEM((2, D, FF), BF),
            pltpu.VMEM((FF, D), BF),
            pltpu.VMEM((2, 16, D), F32),
            pltpu.VMEM((2, ROWS, LANE), F32),
            pltpu.VMEM((2,) + slot, BF),
            pltpu.VMEM((2, 2) + image, BF),
            pltpu.VMEM((2,) + image, BF),
            pltpu.VMEM((2,) + image, BF),
            pltpu.VMEM((2, 3) + image, BF),
            pltpu.VMEM((2, 2) + image, BF),
            pltpu.VMEM((2, 2, ROWS, LANE), F32),
            pltpu.VMEM((2, ROWS, 3 * D), F32),
            pltpu.VMEM((2, ROWS, FF), BF),
            pltpu.VMEM((2, 2, ROWS, FF), BF),
            pltpu.VMEM((2, UNITS, PACK * WROWS, LANE), F32),
            pltpu.VMEM((SIDE, GRID + 2, CELL, D), F32),
            pltpu.VMEM(image, F32),
            pltpu.VMEM(image, F32),
            pltpu.VMEM((2, 12, CELL, D), F32),
            pltpu.VMEM((2, 16, D), F32),
            pltpu.VMEM((16, D), F32),
            pltpu.VMEM((2, 2) + image, BF),
            pltpu.VMEM((2, ROWS, FF), BF),
            pltpu.VMEM((2, ROWS, FF), BF),
            pltpu.VMEM((2,) + image, BF),
            pltpu.VMEM((4, ROWS, FF - SIXTH), BF),
            pltpu.VMEM((2,) + image, BF),
            pltpu.VMEM((2, RING, COLS + WIDE + 3 * REST, COLS), BF),
            pltpu.VMEM((rounds + 1, 16, D), F32),
            pltpu.VMEM((rounds, 16, D), F32),
            dma((5,)),
            dma((6,)),
            dma((6,)),
            dma((2,)),
            dma((2,)),
            dma((2,)),
            dma((2,)),
            dma((2,)),
            dma((2, 6)),
            dma((2, 6)),
            dma((2,)),
            dma((2,)),
            dma((2,)),
            dma((2, 2 * RING, 4)),
            dma((2, 2 * RING, 4)),
            dma((2, RING, 4)),
            dma((rounds,)),
            dma((rounds,)),
            dma((4,)),
            dma((4,)),
            dma((2,)),
            dma((2,)),
            dma((2, RING)),
            dma((2, RING)),
            dma((2, RING)),
            dma((2, RING)),
            pltpu.SemaphoreType.REGULAR((2, 4)),
        ],
        name="relay",
        compiler_params=pltpu.CompilerParams(
            collective_id=1, has_side_effects=True, vmem_limit_bytes=63 * 2**20
        ),
    )(wrows, wcols, img, cot, kern, bias, gain, move, first, second)


def finish_kernel(
    out1, out2, act, ing, outs, first, second, acts, ings, kern, bias, gain, move,
    raw1, raw2, full1, full2, acted, graded, wide, small, kernels, rsem, wsem,
):
    steps = rsem.shape[0] - 3

    loads = [
        pltpu.make_async_copy(act, acted, rsem.at[steps]),
        pltpu.make_async_copy(ing, graded, rsem.at[steps + 1]),
        pltpu.make_async_copy(outs, small, rsem.at[steps + 2]),
    ]
    for copy in loads:
        copy.start()
    reads, writes = [], []
    for i in range(steps):
        pair = ((out1, raw1, full1, first), (out2, raw2, full2, second))[i % 2]
        src, raw, full, dst = pair
        half = steps // 2
        rows = pl.ds(i // 2 * (src.shape[0] // half), src.shape[0] // half)
        reads.append((pltpu.make_async_copy(src.at[rows, :], raw.at[rows, :], rsem.at[i]), raw, full, rows))
        writes.append(pltpu.make_async_copy(full.at[rows, :], dst.at[rows, :], wsem.at[i]))
    for copy, *_ in reads:
        copy.start()
    for (copy, raw, full, rows), back in zip(reads, writes):
        copy.wait()
        full[rows, :] = raw[rows, :].astype(F32)
        back.start()
    for copy in loads:
        copy.wait()
    for k in range(9):
        kernels[k] = small[k : k + 1, :]
    for r in range(GRID):
        line = graded[r].astype(F32)
        for k in range(GRID):
            wide[r, k] = line[k : k + 1, :]
    last = [
        pltpu.make_async_copy(acted, acts, wsem.at[steps]),
        pltpu.make_async_copy(wide, ings, wsem.at[steps + 1]),
        pltpu.make_async_copy(kernels, kern, wsem.at[steps + 2]),
    ]
    for i, dst in enumerate((bias, gain, move)):
        last.append(pltpu.make_async_copy(small.at[pl.ds(9 + i, 1), :], dst, wsem.at[steps + 3 + i]))
    for copy in last:
        copy.start()
    for copy in writes + last:
        copy.wait()


def finish(out1, out2, act, ing, outs):
    shape = jax.ShapeDtypeStruct
    slot = act.shape
    anywhere = pl.BlockSpec(memory_space=pl.ANY)
    line = (1, D)
    spread = slot[:2] + line
    steps = 16
    return pl.pallas_call(
        finish_kernel,
        out_shape=[
            shape(out1.shape, F32),
            shape(out2.shape, F32),
            shape(slot, BF),
            shape(spread, F32),
            shape((9,) + line, F32),
            shape(line, F32),
            shape(line, F32),
            shape(line, F32),
        ],
        in_specs=[anywhere] * 5,
        out_specs=[anywhere] * 8,
        scratch_shapes=[
            pltpu.VMEM(out1.shape, out1.dtype),
            pltpu.VMEM(out2.shape, out2.dtype),
            pltpu.VMEM(out1.shape, F32),
            pltpu.VMEM(out2.shape, F32),
            pltpu.VMEM(slot, BF),
            pltpu.VMEM(slot, BF),
            pltpu.VMEM(spread, F32),
            pltpu.VMEM(outs.shape, F32),
            pltpu.VMEM((9,) + line, F32),
            pltpu.SemaphoreType.DMA((steps + 3,)),
            pltpu.SemaphoreType.DMA((steps + 6,)),
        ],
        name="finish",
        compiler_params=pltpu.CompilerParams(vmem_limit_bytes=60 * 2**20),
    )(out1, out2, act, ing, outs)


def per_device(
    images, cotangent, window_rows, window_cols, pos_kernel, pos_bias, norm_gain, norm_shift, first_weight, second_weight
):
    act, ing, out1, out2, outs = relay(
        window_rows, window_cols, images[0], cotangent[0], pos_kernel[0], pos_bias, norm_gain, norm_shift,
        first_weight[0], second_weight,
    )
    if lax.axis_size("dp") > RING:
        out1, out2, outs = lax.psum((out1.astype(F32) / RING, out2.astype(F32) / RING, outs / RING), "dp")
    out1, out2, act, ing, kern, bias, gain, move = finish(out1, out2, act, ing, outs)
    return (
        act[None],
        ing.transpose(2, 0, 1, 3),
        out1[None],
        out2,
        kern.transpose(1, 0, 2),
        bias,
        gain,
        move,
    )


def solution(mesh):
    in_specs = (
        P(("dp", "section"), None, None, None),
        P(("dp", "section"), None, None, None),
        P("dp"),
        P("dp"),
        P("section", None, None),
        P("section", None),
        P("section", None),
        P("section", None),
        P("section", None, None),
        P("section", None),
    )
    out_specs = (
        P(("dp", "section"), None, None, None),
        P(("dp", "section"), None, None, None),
        P("section", None, None),
        P("section", None),
        P("section", None, None),
        P("section", None),
        P("section", None),
        P("section", None),
    )
    return jax.shard_map(per_device, mesh=mesh, in_specs=in_specs, out_specs=out_specs, check_vma=False)
```

```python
from functools import partial

import jax
import jax.numpy as jnp
from jax import lax
from jax.experimental import pallas as pl
from jax.experimental.pallas import tpu as pltpu
from jax.sharding import PartitionSpec as P

D = 768
FF = 3072
HEADS = 24
HEAD = 32
WIN = 7
SIDE = 2
GRID = SIDE * WIN
CELL = 8
WROWS = WIN * CELL
HALF = GRID * CELL
ROWS = SIDE * HALF
GROUP = 256
PACK = GROUP // HEAD
NGROUP = D // GROUP
UNITS = NGROUP * SIDE * SIDE
LANE = 128
FTILE = 512
EPS = 1e-05
SCALE = HEAD ** (-0.5)
BF = jnp.bfloat16
F32 = jnp.float32
MESH = pl.DeviceIdType.MESH


def dot(a, b, ca=1, cb=0):
    return lax.dot_general(a, b, (((ca,), (cb,)), ((), ())), preferred_element_type=F32)


def lanes(index, width=LANE):
    return pl.ds(pl.multiple_of(index * width, width), width)


def halves(value):
    return value.reshape(SIDE, GRID, CELL, value.shape[-1])


def shifts(left, right):
    column = lax.broadcasted_iota(jnp.int32, left.shape, 1)
    before0 = pltpu.roll(left, 1, 1)
    after0 = jnp.where(column == WIN - 1, pltpu.roll(right, CELL - 2, 1), pltpu.roll(left, CELL - 1, 1))
    before1 = jnp.where(column == 0, pltpu.roll(left, 2, 1), pltpu.roll(right, 1, 1))
    after1 = pltpu.roll(right, CELL - 1, 1)
    return ((before0, left, after0), (before1, right, after1))


def gelu_parts(h):
    expo = jnp.exp(h * h * -0.5)
    t = 1.0 / (1.0 + (0.3275911 * 0.7071067811865476) * jnp.abs(h))
    poly = t * (0.127414796 + t * (-0.142248368 + t * (0.7107068705 + t * (-0.7265760135 + t * 0.5307027145))))
    tail = poly * expo
    phi = jnp.where(h >= 0, 1.0 - tail, tail)
    return h * phi, phi + h * expo * 0.3989422804014327


def front_forward(sec, m, ubuf, msk, pr, U, C, zz, xh, rs):
    zero = jnp.zeros((ROWS, LANE), F32)

    def conv(i, total):
        ls = lanes(i)
        u = ubuf[sec, m, :, ls].astype(F32)
        masked = halves(u * msk[m])
        U[0, 1 : GRID + 1, :, ls] = masked[0]
        U[1, 1 : GRID + 1, :, ls] = masked[1]
        moved = shifts(U[0, :, :, ls], U[1, :, :, ls])
        taps = pr[sec, :, ls]
        uh = halves(u)
        sums = []
        for wc in range(SIDE):
            acc = uh[wc] + taps[9:10, :][None]
            for a in range(3):
                for b in range(3):
                    acc = acc + moved[wc][b][a : a + GRID] * taps[3 * a + b : 3 * a + b + 1, :][None]
            acc = acc.reshape(HALF, LANE)
            C[pl.ds(wc * HALF, HALF), ls] = acc
            sums.append(acc)
        return total + jnp.concatenate(sums, axis=0)

    mean = jnp.sum(lax.fori_loop(0, D // LANE, conv, zero), axis=-1, keepdims=True) * (1.0 / D)

    def spread(i, total):
        centred = C[:, lanes(i)] - mean
        return total + centred * centred

    var = jnp.sum(lax.fori_loop(0, D // LANE, spread, zero), axis=-1, keepdims=True) * (1.0 / D)
    rstd = lax.rsqrt(var + EPS)
    rs[sec, m] = jnp.broadcast_to(rstd, (ROWS, LANE))

    def norm(i, carry):
        ls = lanes(i)
        xhat = (C[:, ls] - mean) * rstd
        xh[sec, m, :, ls] = xhat.astype(BF)
        zz[m, 2 * sec, :, ls] = (xhat * pr[sec, 10:11, ls] + pr[sec, 11:12, ls]).astype(BF)
        return carry

    lax.fori_loop(0, D // LANE, norm, 0)


def fold(value):
    return jnp.sum(value.reshape(ROWS // CELL, CELL, LANE), axis=0)


def front_backward(sec, m, msk, pr, U, T, gfull, xh, rs, sgp, out, sent):
    zero = jnp.zeros((ROWS, LANE), F32)

    def sums(i, carry):
        s1, s2 = carry
        ls = lanes(i)
        dz = T[:, ls]
        xhat = xh[sec, m, :, ls].astype(F32)
        both = xhat * dz
        sgp[sec, 10, :, ls] += fold(both)
        sgp[sec, 11, :, ls] += fold(dz)
        gain = pr[sec, 10:11, ls]
        return s1 + dz * gain, s2 + both * gain

    s1, s2 = lax.fori_loop(0, D // LANE, sums, (zero, zero))
    m1 = jnp.sum(s1, axis=-1, keepdims=True) * (1.0 / D)
    m2 = jnp.sum(s2, axis=-1, keepdims=True) * (1.0 / D)

    def back(i, carry):
        ls = lanes(i)
        xhat = xh[sec, m, :, ls].astype(F32)
        inner = T[:, ls] * pr[sec, 10:11, ls] - m1 - xhat * m2
        gc = gfull(i)[...].astype(F32) + rs[sec, m] * inner
        xh[sec, m, :, ls] = gc.astype(BF)
        gh = halves(gc)
        U[0, 1 : GRID + 1, :, ls] = gh[0]
        U[1, 1 : GRID + 1, :, ls] = gh[1]
        moved = shifts(U[0, :, :, ls], U[1, :, :, ls])
        taps = pr[sec, :, ls]
        mask = halves(msk[m])
        du = []
        for wc in range(SIDE):
            acc = jnp.zeros((GRID, CELL, LANE), F32)
            for a in range(3):
                for b in range(3):
                    tap = 3 * a + b
                    acc = acc + moved[wc][2 - b][2 - a : 2 - a + GRID] * taps[tap : tap + 1, :][None]
            du.append((gh[wc] + mask[wc] * acc).reshape(HALF, LANE))
        out(i)[...] = jnp.concatenate(du, axis=0).astype(BF)
        return carry

    lax.fori_loop(0, D // LANE // 2, back, 0)
    sent(0)
    lax.fori_loop(D // LANE // 2, D // LANE, back, 0)
    sent(1)


def front_sums(sec, m, ubuf, msk, U, xh, sgp):
    def part(i, carry):
        ls = lanes(i)
        gc = xh[sec, m, :, ls].astype(F32)
        sgp[sec, 9, :, ls] += fold(gc)
        gh = halves(gc)
        U[0, 1 : GRID + 1, :, ls] = gh[0]
        U[1, 1 : GRID + 1, :, ls] = gh[1]
        moved = shifts(U[0, :, :, ls], U[1, :, :, ls])
        um = halves(ubuf[sec, m, :, ls].astype(F32) * msk[m])
        for a in range(3):
            for b in range(3):
                kg = jnp.zeros((CELL, LANE), F32)
                for wc in range(SIDE):
                    kg = kg + jnp.sum(moved[wc][2 - b][2 - a : 2 - a + GRID] * um[wc], axis=0)
                sgp[sec, 3 * a + b, :, ls] += kg
        return carry

    lax.fori_loop(0, D // LANE, part, 0)


def spread_heads(value, head_of_lane):
    parts = [jnp.where(head_of_lane == h, value, 0.0) for h in range(PACK)]
    return jnp.concatenate(parts, axis=0).astype(BF)


def gather_heads(value, rows, head_of_lane):
    out = jnp.zeros((rows, GROUP), F32)
    for h in range(PACK):
        out = jnp.where(head_of_lane == h, value[h * rows : (h + 1) * rows], out)
    return out


def unit_slices(unit):
    pair, group = unit // NGROUP, lax.rem(unit, NGROUP)
    rows = [pl.ds(pl.multiple_of((2 * pair + w) * WROWS, 8), WROWS) for w in range(2)]
    cols = [pl.ds(pl.multiple_of(part * D + group * GROUP, LANE), GROUP) for part in range(3)]
    return rows, cols


def window_parts(m, i, qkv):
    rows, cols = unit_slices(i)
    head_of_lane = lax.broadcasted_iota(jnp.int32, (WROWS, GROUP), 1) // HEAD
    q = [qkv[m, r, cols[0]].astype(BF) for r in rows]
    kd = [spread_heads(qkv[m, r, cols[1]], head_of_lane) for r in rows]
    vd = [spread_heads(qkv[m, r, cols[2]], head_of_lane) for r in rows]
    return rows, cols, head_of_lane, q, kd, vd


def window_forward(m, qkv, pw, T):
    def unit(i, carry):
        rows, cols, head_of_lane, q, kd, vd = window_parts(m, i, qkv)
        s = [(dot(b, a, 1, 1) * SCALE).reshape(PACK, WROWS, WROWS) for a, b in zip(q, kd)]
        key = lax.broadcasted_iota(jnp.int32, s[0].shape, 1)
        real = lax.rem(key, CELL) < WIN
        s = [jnp.where(real, x, -1e30) for x in s]
        p = [jnp.exp(x - jnp.max(x, axis=1, keepdims=True)) for x in s]
        p = [x * (1.0 / jnp.sum(x, axis=1, keepdims=True)) for x in p]
        p = [x.reshape(PACK * WROWS, WROWS) for x in p]
        for w in range(2):
            pw[m, 2 * i + w, :, 0:WROWS] = p[w]
        out = [dot(x.astype(BF), v, 0, 0) for x, v in zip(p, vd)]
        for w in range(2):
            T[rows[w], cols[0]] = out[w]
        return carry

    lax.fori_loop(0, UNITS // 2, unit, 0)


def window_backward(m, qkv, pw, T):
    def unit(i, carry):
        rows, cols, head_of_lane, q, kd, vd = window_parts(m, i, qkv)
        g = [T[r, cols[0]].astype(BF) for r in rows]
        p = [pw[m, 2 * i + w, :, 0:WROWS].reshape(PACK, WROWS, WROWS) for w in range(2)]
        dp = [dot(v, x, 1, 1).reshape(PACK, WROWS, WROWS) for v, x in zip(vd, g)]
        ds = [x * (y - jnp.sum(x * y, axis=1, keepdims=True)) for x, y in zip(p, dp)]
        ds = [x.reshape(PACK * WROWS, WROWS).astype(BF) for x in ds]
        pb = [x.reshape(PACK * WROWS, WROWS).astype(BF) for x in p]
        dv = [gather_heads(dot(x, y), WROWS, head_of_lane) for x, y in zip(pb, g)]
        dk = [gather_heads(dot(x, y), WROWS, head_of_lane) * SCALE for x, y in zip(ds, q)]
        dq = [dot(x, y, 0, 0) * SCALE for x, y in zip(ds, kd)]
        for w in range(2):
            qkv[m, rows[w], cols[0]] = dq[w]
            qkv[m, rows[w], cols[1]] = dk[w]
            qkv[m, rows[w], cols[2]] = dv[w]
        return carry

    lax.fori_loop(0, UNITS // 2, unit, 0)


def group_slices(group):
    return [pl.ds(pl.multiple_of(part * D + group * GROUP, LANE), GROUP) for part in range(3)]


def channel_forward(m, qkv, pw, zz, msk):
    def unit(i, carry):
        cols = group_slices(i)
        mask = msk[m][:, :1]
        q = qkv[m, :, cols[0]].astype(BF)
        k = (qkv[m, :, cols[1]] * mask).astype(BF)
        v = qkv[m, :, cols[2]].astype(BF)
        s = dot(q, k, 0, 0) * SCALE
        same = (lax.broadcasted_iota(jnp.int32, s.shape, 0) // HEAD) == (lax.broadcasted_iota(jnp.int32, s.shape, 1) // HEAD)
        s = jnp.where(same, s, -1e30)
        p = jnp.exp(s - jnp.max(s, axis=1, keepdims=True))
        p = p * (1.0 / jnp.sum(p, axis=1, keepdims=True))
        for k in range(GROUP // LANE):
            pw[m, 2 * i + k, 0:GROUP, :] = p[:, k * LANE : (k + 1) * LANE]
        zz[m, 1, :, cols[0]] = dot(v, p.astype(BF), 1, 1).astype(BF)
        return carry

    lax.fori_loop(0, NGROUP, unit, 0, unroll=True)


def channel_backward(m, qkv, pw, T, rr, msk):
    def unit(i, carry):
        cols = group_slices(i)
        mask = msk[m][:, :1]
        q = qkv[m, :, cols[0]].astype(BF)
        k = (qkv[m, :, cols[1]] * mask).astype(BF)
        v = qkv[m, :, cols[2]].astype(BF)
        g = T[:, cols[0]].astype(BF)
        p = jnp.concatenate([pw[m, 2 * i + k, 0:GROUP, :] for k in range(GROUP // LANE)], axis=1)
        dp = dot(g, v, 0, 0)
        ds = (p * (dp - jnp.sum(p * dp, axis=1, keepdims=True))).astype(BF)
        rr[m, 0, :, cols[0]] = (dot(k, ds, 1, 1) * SCALE).astype(BF)
        rr[m, 0, :, cols[1]] = (dot(q, ds) * (SCALE * mask)).astype(BF)
        rr[m, 0, :, cols[2]] = (dot(g, p.astype(BF))).astype(BF)
        return carry

    lax.fori_loop(0, NGROUP, unit, 0, unroll=True)


RING = 8
COLS = FF // RING
WIDE = FF // 12 * 8 // RING
REST = FF // 6 // RING
FIFTH, SIXTH = FF // 6 * 4, FF // 6 * 5
EARLY = 2


def relay_kernel(
    wrows, wcols, img, cot, kern, bias, gain, move, first, second,
    act, ing, out1, out2, outs,
    wf, w2, pr, msk, flat, ubuf, gin, gout, zz, xh, rs, qkv, ab, rr, pw, U, C, T, sgp, sgs, sgm,
    rL, rR, rA, rG, xA, xG, buf, acc, got,
    wl, ws, wr, pl_, usem, gsem, us, gs, ss, rsem, es, er, sgsem, ssem, rcem, osem, sms, smr, xs, xr, ys, yr, bs, br, hs, hr, free,
):
    n = RING
    s = lax.axis_index("section")
    dp = lax.axis_index("dp")
    stage, c = s // 2, lax.rem(s, 2)
    mate = (dp, stage * 2 + (1 - c))
    opposite = (dp, (1 - stage) * 2 + c)
    lender, helper = s == 1, s == 3
    early = stage == 0

    spot = lax.rem(dp, n)
    base = dp - spot
    me = jnp.where(lax.rem(spot, 2) == 0, spot // 2, n - 1 - spot // 2)

    def place(pos):
        pos = lax.rem(pos + 2 * n, n)
        return (base + jnp.where(pos < n // 2, 2 * pos, 2 * (n - 1 - pos) + 1), s)

    nexts = (place(me + 1), place(me - 1))
    rounds = n.bit_length() - 1
    partners = []
    for r in range(rounds):
        bit = 1 << r
        partners.append((jnp.where(lax.rem(spot // bit, 2) == 0, dp + bit, dp - bit), s))

    barrier = pltpu.get_barrier_semaphore()
    peers = [mate, opposite, *nexts, *partners]
    for peer in peers:
        pl.semaphore_signal(barrier, inc=1, device_id=peer, device_id_type=MESH)
    pl.semaphore_wait(barrier, len(peers))

    def remote(src, dst, send, recv, peer):
        return pltpu.make_async_remote_copy(
            src_ref=src, dst_ref=dst, send_sem=send, recv_sem=recv, device_id=peer, device_id_type=MESH
        )

    half = second.shape[0]

    def weight_parts(k):
        parts = []
        for i in range(4):
            parts.append((first.at[:, pl.ds(i * D, D)], wf.at[k, :, pl.ds(i * D, D)]))
        parts.append((second, w2.at[pl.ds(k * half, half), :]))
        return parts

    def weight_copies(k):
        local = [pltpu.make_async_copy(a, b, wl.at[i]) for i, (a, b) in enumerate(weight_parts(k))]
        sent = [remote(a, b, ws.at[i], wr.at[i], mate) for i, (a, b) in enumerate(weight_parts(k))]
        return local, sent

    def params_copy(k):
        return remote(pr.at[k], pr.at[k], ws.at[5], wr.at[5], mate)

    pr[c, 0:9, :] = kern[...].astype(F32)
    pr[c, 9:10, :] = bias[...].astype(F32)
    pr[c, 10:11, :] = gain[...].astype(F32)
    pr[c, 11:12, :] = move[...].astype(F32)
    params_copy(c).start()
    for k in range(2):

        @pl.when(c == k)
        def _():
            local, sent = weight_copies(k)
            for i in range(5):
                local[i].start()
                sent[i].start()

    def wait_weight(k, i):
        if i < 5:

            @pl.when(c == k)
            def _():
                weight_copies(k)[0][i].wait()

        @pl.when(c != k)
        def _():
            (weight_copies(k)[1][i] if i < 5 else params_copy(k)).wait_recv()

    raw = flat.at[0]
    img_out = remote(img, raw, pl_.at[0], pl_.at[1], opposite)
    cot_out = remote(cot, raw, pl_.at[0], pl_.at[1], opposite)

    def pad(src, dst):
        blank = jnp.zeros((CELL - WIN, D), F32)
        for r in range(GRID):
            line = src[r].astype(F32)
            for wc in range(SIDE):
                cells = jnp.concatenate([line[wc * WIN : (wc + 1) * WIN], blank], axis=0)
                C[pl.ds(wc * HALF + r * CELL, CELL), :] = cells
        dst[...] = C[...].astype(BF)

    def unpad(dst):
        for r in range(GRID):
            sides = [C[pl.ds(wc * HALF + r * CELL, CELL), :][:WIN] for wc in range(SIDE)]
            dst[r] = jnp.concatenate(sides, axis=0).astype(BF)

    @pl.when(early)
    def _():
        cot_out.start()
        pad(img, ubuf.at[0, 0])

    @pl.when(jnp.logical_not(early))
    def _():
        img_out.start()
        pad(cot, gin.at[1])

    index = lax.broadcasted_iota(jnp.int32, (ROWS, LANE), 0)
    cell = lax.rem(index, CELL)
    row = lax.rem(index, HALF) // CELL
    column = (index // HALF) * WIN + cell
    for m in range(2):
        inside = (row < WIN * wrows[c + 2 * m]) & (column < WIN * wcols[c + 2 * m]) & (cell < WIN)
        msk[m] = jnp.where(inside, 1.0, 0.0)

    @pl.when(jnp.logical_not(early))
    def _():
        cot_out.wait_recv()
        pad(raw, gin.at[0])
        for m in range(2):
            for l in range(D // LANE):
                cols = pl.ds(l * LANE, LANE)
                gin[m, :, cols] = (gin[m, :, cols].astype(F32) * msk[m]).astype(BF)

    for wc in range(SIDE):
        U[wc, 0] = jnp.zeros((CELL, D), F32)
        U[wc, GRID + 1] = jnp.zeros((CELL, D), F32)
    sgp[...] = jnp.zeros(sgp.shape, F32)

    def hop(m, dst, send, recv):
        sides = [pl.ds(i * D // 2, D // 2) for i in range(2)]
        return [
            remote(gout.at[m, :, cols], dst.at[:, cols], send.at[m, i], recv.at[m, i], opposite)
            for i, cols in enumerate(sides)
        ]

    def u_hop(m):
        return hop(m, ubuf.at[0, m], us, usem)

    def g_hop(m):
        return hop(m, gin.at[m], gs, gsem)

    def factor_copies(k, m):
        if k == 0:
            parts = [
                ("F", zz.at[m, 0], rL.at[m, 0]),
                ("F", zz.at[m, 1], rL.at[m, 1]),
                ("G", rr.at[m, 0, :, pl.ds(3 * D, D)], rR.at[m, :, pl.ds(3 * D, D)]),
                ("A", rr.at[m, 0, :, pl.ds(0, 3 * D)], rR.at[m, :, pl.ds(0, 3 * D)]),
            ]
        else:
            parts = [
                ("F", zz.at[m, 2], rL.at[m, 0]),
                ("F", ab.at[m], rA.at[m]),
                ("M", gin.at[m], rG.at[m]),
            ]
            for i in range(3):
                cols = pl.ds(i * (FF // 3), FF // 3)
                parts.append((f"M{i}", rr.at[m, 1, :, cols], rR.at[m, :, cols]))
        return [(w, remote(a, b, ss.at[m, i], rsem.at[m, i], mate)) for i, (w, a, b) in enumerate(parts)]

    def start_factors(m, which):
        for k in range(2):

            @pl.when(c != k)
            def _():
                for when, copy in factor_copies(k, m):
                    if when == which:
                        copy.start()

    def wait_factors(which):
        for k in range(2):

            @pl.when(c == k)
            def _():
                for m in range(2):
                    for when, copy in factor_copies(k, m):
                        if when[0] in which:
                            copy.wait_recv()

    def shard(k):
        return lax.rem(k + 4 * n, n)

    def sign(h):
        return 1 if h == 0 else -1

    def home(h, t):
        return shard(me + sign(h) - sign(h) * t)

    def products(terms):
        total = None
        for a, b in terms:
            part = dot(a[...], b[...], 0, 0)
            total = part if total is None else total + part
        return total

    def pick(total, j):
        return jnp.where(lax.rem(j, 2) == 1, total[REST:], total[:REST])

    def tile(sub, h, j):
        side = pl.ds(h * COLS, COLS)
        if sub == 0:
            last = jnp.where(j >= (3 * n) // 4, 1, 0)
            own = jnp.where(c == 1, 2, last)
            other = jnp.where(c == 1, 0, last)
            cols = lanes(j, COLS)
            terms = [(zz.at[m, own, :, side], rr.at[m, c, :, cols]) for m in range(2)]
            terms += [(rL.at[m, other, :, side], rR.at[m, :, cols]) for m in range(2)]
        elif sub == 1:
            cols = lanes(j, WIDE)
            terms = [(ab.at[m, :, cols], gin.at[m, :, side]) for m in range(2)]
            terms += [(rA.at[m, :, cols], rG.at[m, :, side]) for m in range(2)]
        else:
            start = (FIFTH if sub == 2 else SIXTH) + j // 2 * 2 * REST
            cols = pl.ds(pl.multiple_of(start, LANE), 2 * REST)
            terms = [(ab.at[m, :, cols], gin.at[m, :, side]) for m in range(2)]
            terms += [(rA.at[m, :, cols], rG.at[m, :, side]) for m in range(2)]
            own = pick(products(terms), j)
            if sub == 2:
                return own
            cols = lanes(j // 2, 2 * REST)
            terms = [(xA.at[m, :, cols], gout.at[m, :, side]) for m in range(2)]
            terms += [(xA.at[2 + m, :, cols], xG.at[m, :, side]) for m in range(2)]
            return jnp.concatenate([own, pick(products(terms), j)], axis=0)
        return products(terms)

    sizes = (COLS, WIDE, REST, 2 * REST)
    parts = [pl.ds(sum(sizes[:i]), size) for i, size in enumerate(sizes)]
    odd = c == 1
    active = (None, odd, odd, helper)

    def where_active(sub, run):
        if active[sub] is None:
            run()
        else:
            pl.when(active[sub])(run)


    def gathered(sub, h, j):
        if sub == 0:
            return wf.at[0, pl.ds(h * COLS, COLS), lanes(j, COLS)]
        if sub == 3:
            rows = pl.ds(pl.multiple_of(lax.rem(j, n // 2) * sizes[3], 16), sizes[3])
            return wf.at[1, rows, lanes(2 * (j // (n // 2)) + h, COLS)]
        first_row = 0 if sub == 1 else FIFTH
        return w2.at[pl.ds(pl.multiple_of(first_row + j * sizes[sub], 16), sizes[sub]), pl.ds(h * COLS, COLS)]

    def scatter(h, t, sub):
        src, dst = buf.at[h, t, parts[sub], :], buf.at[h, t + 1, parts[sub], :]
        return remote(src, dst, ssem.at[h, t, sub], rcem.at[h, t + 1, sub], nexts[h])

    def spread(h, t, sub, j):
        ref = gathered(sub, h, j)
        return remote(ref, ref, ssem.at[h, n - 1 + t, sub], rcem.at[h, n + t, sub], nexts[h])

    half_shards = n * 3 // 4

    def write(h, j, sub, part=0):
        src, side = gathered(sub, h, j), pl.ds(h * COLS, COLS)
        if sub == 0:
            dst = out1.at[side, lanes(j, COLS)]
        elif sub == 1:
            dst = out2.at[pl.ds(pl.multiple_of((j - half_shards) * WIDE, 16), WIDE), side]
        else:
            first_row = (FIFTH if sub == 2 else SIXTH) - FF // 2
            dst = out2.at[pl.ds(pl.multiple_of(first_row + j * REST, 16), REST), side]
            src = src.at[pl.ds(part * REST, REST), :]
        if part == 1:
            return remote(src, dst, bs.at[h, j], br.at[h, j], opposite)
        return pltpu.make_async_copy(src, dst, osem.at[h, j, sub])

    def hand_over(h, j):
        dst = out2.at[pl.ds(pl.multiple_of(j * WIDE, 16), WIDE), pl.ds(h * COLS, COLS)]
        return remote(gathered(1, h, j), dst, hs.at[h, j], hr.at[h, j], mate)

    def deliver(h, j, sub):
        if sub == 1:

            @pl.when(j < half_shards)
            def _():
                hand_over(h, j).start()

            @pl.when(j >= half_shards)
            def _():
                write(h, j, sub).start()

        else:
            write(h, j, sub).start()
            if sub == 3:
                write(h, j, sub, 1).start()

    def lend(m):
        cols = pl.ds(SIXTH, FF - SIXTH)
        return (
            remote(ab.at[m, :, cols], xA.at[m], xs.at[m], xr.at[m], opposite),
            remote(rA.at[m, :, cols], xA.at[2 + m], xs.at[2 + m], xr.at[2 + m], opposite),
        )

    def share(m):
        return remote(gout.at[m], xG.at[m], ys.at[m], yr.at[m], mate)

    def reduce_event(sub, h, e):
        total = tile(sub, h, shard(me - sign(h) * e))

        @pl.when(e == 0)
        def _():
            buf[h, 0, parts[sub], :] = total.astype(BF)
            scatter(h, 0, sub).start()

        @pl.when((e > 0) & (e < n - 1))
        def _():
            scatter(h, e - 1, sub).wait_recv()
            buf[h, e, parts[sub], :] = (total + buf[h, e, parts[sub], :].astype(F32)).astype(BF)
            scatter(h, e, sub).start()

        @pl.when(e == n - 1)
        def _():
            j = home(h, 0)
            scatter(h, n - 2, sub).wait_recv()
            gathered(sub, h, j)[...] = (total + buf[h, n - 1, parts[sub], :].astype(F32)).astype(BF)
            pl.semaphore_wait(free.at[h, sub], 1)
            spread(h, 0, sub, j).start()
            deliver(h, j, sub)

    def event(sub, e):
        for h in range(2):

            @pl.when(e < n)
            def _():
                reduce_event(sub, h, e)

            @pl.when((e >= n) & (e < 2 * n - 1))
            def _():
                t = e - (n - 1)
                j = home(h, t)
                spread(h, t - 1, sub, j).wait_recv()

                @pl.when(t < n - 1)
                def _():
                    spread(h, t, sub, j).start()

                deliver(h, j, sub)

    def early_event(e):
        @pl.when(odd)
        def _():
            for sub in range(3):
                event(sub, e)

    def small(r):
        return remote(acc.at[r], got.at[r], sms.at[r], smr.at[r], partners[r])

    def forward(m, p):
        @pl.when(jnp.logical_not(early))
        def _():
            for copy in u_hop(m):
                copy.wait_recv()

        @pl.when(early & (m == 1))
        def _():
            img_out.wait_recv()
            pad(raw, ubuf.at[0, 1])

        once = p == 0

        def first_time(k, i):
            @pl.when(once)
            def _():
                wait_weight(k, i)

        first_time(0, 5)
        front_forward(0, m, ubuf, msk, pr, U, C, zz, xh, rs)
        for i in range(3):
            first_time(0, i)
            qkv[m, :, pl.ds(i * D, D)] = dot(zz[m, 0], wf[0, :, pl.ds(i * D, D)])

        @pl.when(early)
        def _():
            window_forward(m, qkv, pw, T)
            zz[m, 1] = T[...].astype(BF)

        @pl.when(jnp.logical_not(early))
        def _():
            channel_forward(m, qkv, pw, zz, msk)

        first_time(0, 3)
        ubuf[1, m] = (C[...] + dot(zz[m, 1], wf[0, :, pl.ds(3 * D, D)])).astype(BF)

        first_time(1, 5)
        front_forward(1, m, ubuf, msk, pr, U, C, zz, xh, rs)
        for i in range(4):
            first_time(1, i)
        first_time(0, 4)
        first_time(1, 4)

        total, before = C[...], None
        for t in range(FF // FTILE):
            cols = pl.ds(t * FTILE, FTILE)
            h = dot(zz[m, 2], wf[1, :, cols])
            if t > 0:
                total = total + dot(before, w2[pl.ds((t - 1) * FTILE, FTILE), :])
            a, d = gelu_parts(h)
            before = a.astype(BF)
            ab[m, :, cols] = before
            rr[m, 1, :, cols] = d.astype(BF)
        for i in range(2):
            cols = pl.ds(i * D // 2, D // 2)
            part = total[:, i * D // 2 : (i + 1) * D // 2]
            gout[m, :, cols] = (part + dot(before, w2[pl.ds(FF - FTILE, FTILE), cols])).astype(BF)

            @pl.when(early)
            def _():
                u_hop(m)[i].start()


        @pl.when(jnp.logical_not(early))
        def _():
            for l in range(D // LANE):
                cols = pl.ds(l * LANE, LANE)
                C[:, cols] = gout[m, :, cols].astype(F32) * msk[m]
            unpad(flat.at[m])

        @pl.when(jnp.logical_not(early) & (m == 0))
        def _():
            remote(flat.at[0], act, es.at[0], er.at[0], opposite).start()

        @pl.when(jnp.logical_not(early) & (m == 1))
        def _():
            pltpu.make_async_copy(flat.at[1], act, es.at[0]).start()

        start_factors(m, "F")

        @pl.when(early & (m == 1))
        def _():
            wait_factors("F")

        @pl.when(lender & (m == 1))
        def _():
            for i in range(2):
                for copy in lend(i):
                    copy.start()

    def backward(m):
        @pl.when(early)
        def _():
            for copy in g_hop(m):
                copy.wait_recv()

        start_factors(m, "M")
        for t in range(FF // FTILE):
            cols = pl.ds(t * FTILE, FTILE)
            da = dot(gin[m], w2[cols, :], 1, 1)
            rr[m, 1, :, cols] = (da * rr[m, 1, :, cols].astype(F32)).astype(BF)
            if t % 2 == 1:
                start_factors(m, f"M{t // 2}")
        T[...] = dot(rr[m, 1], wf[1], 1, 1)
        last = pl.ds(3 * D, D)

        @pl.when(early)
        def _():
            for copy in u_hop(m):
                copy.wait_send()

        def tail_lanes(i):
            return rr.at[m, 0, :, pl.ds(pl.multiple_of(3 * D + i * LANE, LANE), LANE)]

        def nothing(half):
            pass

        front_backward(1, m, msk, pr, U, T, lambda i: gin.at[m, :, lanes(i)], xh, rs, sgp, tail_lanes, nothing)
        start_factors(m, "G")

        @pl.when(m == 1)
        def _():
            @pl.when(jnp.logical_not(early))
            def _():
                wait_factors("F")

            wait_factors("M")
            early_event(0)

        T[...] = dot(rr[m, 0, :, last], wf[0, :, last], 1, 1)

        @pl.when(early)
        def _():
            window_backward(m, qkv, pw, T)
            for i in range(3):
                cols = pl.ds(i * D, D)
                rr[m, 0, :, cols] = qkv[m, :, cols].astype(BF)

        @pl.when(jnp.logical_not(early))
        def _():
            channel_backward(m, qkv, pw, T, rr, msk)

        start_factors(m, "A")

        @pl.when(m == 1)
        def _():
            for e in range(1, EARLY):
                early_event(e)

        T[...] = dot(rr[m, 0, :, pl.ds(0, 3 * D)], wf[0, :, pl.ds(0, 3 * D)], 1, 1)
        def send_half(half):
            @pl.when(jnp.logical_not(early))
            def _():
                g_hop(m)[half].start()

        front_backward(
            0, m, msk, pr, U, T, tail_lanes, xh, rs, sgp, lambda i: gout.at[m, :, lanes(i)], send_half
        )

        @pl.when(s == 2)
        def _():
            share(m).start()

        @pl.when(early)
        def _():
            C[...] = gout[m].astype(F32)
            unpad(flat.at[m])

        @pl.when(early & (m == 0))
        def _():
            pltpu.make_async_copy(flat.at[0], ing, es.at[1]).start()

        @pl.when(early & (m == 1))
        def _():
            remote(flat.at[1], ing, es.at[1], er.at[1], opposite).start()

    def phase(p, carry):
        m = jnp.where(early, lax.rem(p, 2), p // 2)
        ahead = jnp.where(early, p < 2, lax.rem(p, 2) == 0)

        @pl.when(ahead)
        def _():
            forward(m, p)

        @pl.when(jnp.logical_not(ahead))
        def _():
            backward(m)

        return carry

    lax.fori_loop(0, 4, phase, 0)

    for h in range(2):
        for sub in range(4):

            def ready():
                pl.semaphore_signal(free.at[h, sub], inc=1, device_id=nexts[1 - h], device_id_type=MESH)

            where_active(sub, ready)

    give = remote(sgs.at[1 - c], sgm, sgsem.at[0], sgsem.at[1], mate)

    def small_sums():
        for sec in range(2):
            for j in range(12):
                sgs[sec, j : j + 1, :] = jnp.sum(sgp[sec, j], axis=0, keepdims=True)
            sgs[sec, 12:16, :] = jnp.zeros((4, D), F32)
        give.start()

    wait_factors("GA")

    @pl.when(helper)
    def _():
        for m in range(2):
            for copy in lend(m):
                copy.wait_recv()
            share(m).wait_recv()

    def ring_step(t, carry):
        event(0, t + jnp.where(odd, EARLY, 0))
        where_active(1, lambda: event(1, t + EARLY))
        where_active(2, lambda: event(2, t + EARLY))
        where_active(3, lambda: event(3, t))
        @pl.when((t >= 1) & (t < 5))
        def _():
            front_sums((t - 1) // 2, lax.rem(t - 1, 2), ubuf, msk, U, xh, sgp)

        pl.when(t == 5)(small_sums)
        for r in range(rounds + 1):

            @pl.when(t == 6 + 2 * r)
            def _():
                if r == 0:
                    give.wait_recv()
                    acc[0] = sgs[c] + sgm[...]
                else:
                    small(r - 1).wait_recv()
                    acc[r] = acc[r - 1] + got[r - 1]
                if r < rounds:
                    small(r).start()

        return carry

    lax.fori_loop(0, 2 * n - 1, ring_step, 0)
    outs[...] = acc[rounds]

    for k in range(2):

        @pl.when(c == k)
        def _():
            for copy in weight_copies(k)[1]:
                copy.wait_send()
            params_copy(k).wait_send()
            for m in range(2):
                for _when, copy in factor_copies(1 - k, m):
                    copy.wait_send()

    give.wait_send()
    for r in range(rounds):
        small(r).wait_send()

    def drain(t, carry):
        for h in range(2):
            for sub in range(4):

                def sent():
                    scatter(h, t, sub).wait_send()
                    spread(h, t, sub, home(h, t)).wait_send()

                where_active(sub, sent)

        return carry

    lax.fori_loop(0, n - 1, drain, 0)

    def written(j, carry):
        for h in range(2):
            write(h, j, 0).wait()

            @pl.when(odd)
            def _():
                write(h, j, 2).wait()

                @pl.when(j < half_shards)
                def _():
                    hand_over(h, j).wait_send()

                @pl.when(j >= half_shards)
                def _():
                    write(h, j, 1).wait()

            @pl.when(jnp.logical_not(odd) & (j < half_shards))
            def _():
                hand_over(h, j).wait_recv()

            @pl.when(helper)
            def _():
                write(h, j, 3).wait()
                write(h, j, 3, 1).wait_send()

            @pl.when(lender)
            def _():
                write(h, j, 3, 1).wait_recv()

        return carry

    lax.fori_loop(0, n, written, 0)

    @pl.when(lender)
    def _():
        for m in range(2):
            for copy in lend(m):
                copy.wait_send()

    @pl.when(s == 2)
    def _():
        for m in range(2):
            share(m).wait_send()

    @pl.when(early)
    def _():
        cot_out.wait_send()
        pltpu.make_async_copy(flat.at[0], ing, es.at[1]).wait()
        remote(flat.at[1], ing, es.at[1], er.at[1], opposite).wait_send()
        remote(flat.at[0], act, es.at[0], er.at[0], opposite).wait_recv()

    @pl.when(jnp.logical_not(early))
    def _():
        img_out.wait_send()
        for m in range(2):
            for copy in g_hop(m):
                copy.wait_send()
        remote(flat.at[0], act, es.at[0], er.at[0], opposite).wait_send()
        pltpu.make_async_copy(flat.at[1], act, es.at[0]).wait()
        remote(flat.at[1], ing, es.at[1], er.at[1], opposite).wait_recv()


def relay(wrows, wcols, img, cot, kern, bias, gain, move, first, second):
    shape = jax.ShapeDtypeStruct
    vmem = pl.BlockSpec(memory_space=pltpu.VMEM)
    anywhere = pl.BlockSpec(memory_space=pl.ANY)
    dma = pltpu.SemaphoreType.DMA
    smem = pl.BlockSpec(memory_space=pltpu.SMEM)
    image = (ROWS, D)
    slot = img.shape
    rounds = RING.bit_length() - 1
    return pl.pallas_call(
        relay_kernel,
        out_shape=[
            shape(slot, BF),
            shape(slot, BF),
            shape((D, FF), BF),
            shape((FF // 2, D), BF),
            shape((16, D), F32),
        ],
        in_specs=[smem] * 2 + [vmem] * 6 + [anywhere] * 2,
        out_specs=[anywhere] * 4 + [vmem],
        scratch_shapes=[
            pltpu.VMEM((2, D, FF), BF),
            pltpu.VMEM((FF, D), BF),
            pltpu.VMEM((2, 16, D), F32),
            pltpu.VMEM((2, ROWS, LANE), F32),
            pltpu.VMEM((2,) + slot, BF),
            pltpu.VMEM((2, 2) + image, BF),
            pltpu.VMEM((2,) + image, BF),
            pltpu.VMEM((2,) + image, BF),
            pltpu.VMEM((2, 3) + image, BF),
            pltpu.VMEM((2, 2) + image, BF),
            pltpu.VMEM((2, 2, ROWS, LANE), F32),
            pltpu.VMEM((2, ROWS, 3 * D), F32),
            pltpu.VMEM((2, ROWS, FF), BF),
            pltpu.VMEM((2, 2, ROWS, FF), BF),
            pltpu.VMEM((2, UNITS, PACK * WROWS, LANE), F32),
            pltpu.VMEM((SIDE, GRID + 2, CELL, D), F32),
            pltpu.VMEM(image, F32),
            pltpu.VMEM(image, F32),
            pltpu.VMEM((2, 12, CELL, D), F32),
            pltpu.VMEM((2, 16, D), F32),
            pltpu.VMEM((16, D), F32),
            pltpu.VMEM((2, 2) + image, BF),
            pltpu.VMEM((2, ROWS, FF), BF),
            pltpu.VMEM((2, ROWS, FF), BF),
            pltpu.VMEM((2,) + image, BF),
            pltpu.VMEM((4, ROWS, FF - SIXTH), BF),
            pltpu.VMEM((2,) + image, BF),
            pltpu.VMEM((2, RING, COLS + WIDE + 3 * REST, COLS), BF),
            pltpu.VMEM((rounds + 1, 16, D), F32),
            pltpu.VMEM((rounds, 16, D), F32),
            dma((5,)),
            dma((6,)),
            dma((6,)),
            dma((2,)),
            dma((2, 2)),
            dma((2, 2)),
            dma((2, 2)),
            dma((2, 2)),
            dma((2, 6)),
            dma((2, 6)),
            dma((2,)),
            dma((2,)),
            dma((2,)),
            dma((2, 2 * RING, 4)),
            dma((2, 2 * RING, 4)),
            dma((2, RING, 4)),
            dma((rounds,)),
            dma((rounds,)),
            dma((4,)),
            dma((4,)),
            dma((2,)),
            dma((2,)),
            dma((2, RING)),
            dma((2, RING)),
            dma((2, RING)),
            dma((2, RING)),
            pltpu.SemaphoreType.REGULAR((2, 4)),
        ],
        name="relay",
        compiler_params=pltpu.CompilerParams(
            collective_id=1, has_side_effects=True, vmem_limit_bytes=63 * 2**20
        ),
    )(wrows, wcols, img, cot, kern, bias, gain, move, first, second)


def finish_kernel(
    out1, out2, act, ing, outs, first, second, acts, ings, kern, bias, gain, move,
    raw1, raw2, full1, full2, acted, graded, wide, small, kernels, rsem, wsem,
):
    steps = rsem.shape[0] - 3

    loads = [
        pltpu.make_async_copy(act, acted, rsem.at[steps]),
        pltpu.make_async_copy(ing, graded, rsem.at[steps + 1]),
        pltpu.make_async_copy(outs, small, rsem.at[steps + 2]),
    ]
    for copy in loads:
        copy.start()
    reads, writes = [], []
    for i in range(steps):
        pair = ((out1, raw1, full1, first), (out2, raw2, full2, second))[i % 2]
        src, raw, full, dst = pair
        half = steps // 2
        rows = pl.ds(i // 2 * (src.shape[0] // half), src.shape[0] // half)
        reads.append((pltpu.make_async_copy(src.at[rows, :], raw.at[rows, :], rsem.at[i]), raw, full, rows))
        writes.append(pltpu.make_async_copy(full.at[rows, :], dst.at[rows, :], wsem.at[i]))
    for copy, *_ in reads:
        copy.start()
    for (copy, raw, full, rows), back in zip(reads, writes):
        copy.wait()
        full[rows, :] = raw[rows, :].astype(F32)
        back.start()
    for copy in loads:
        copy.wait()
    for k in range(9):
        kernels[k] = small[k : k + 1, :]
    for r in range(GRID):
        line = graded[r].astype(F32)
        for k in range(GRID):
            wide[r, k] = line[k : k + 1, :]
    last = [
        pltpu.make_async_copy(acted, acts, wsem.at[steps]),
        pltpu.make_async_copy(wide, ings, wsem.at[steps + 1]),
        pltpu.make_async_copy(kernels, kern, wsem.at[steps + 2]),
    ]
    for i, dst in enumerate((bias, gain, move)):
        last.append(pltpu.make_async_copy(small.at[pl.ds(9 + i, 1), :], dst, wsem.at[steps + 3 + i]))
    for copy in last:
        copy.start()
    for copy in writes + last:
        copy.wait()


def finish(out1, out2, act, ing, outs):
    shape = jax.ShapeDtypeStruct
    slot = act.shape
    anywhere = pl.BlockSpec(memory_space=pl.ANY)
    line = (1, D)
    spread = slot[:2] + line
    steps = 16
    return pl.pallas_call(
        finish_kernel,
        out_shape=[
            shape(out1.shape, F32),
            shape(out2.shape, F32),
            shape(slot, BF),
            shape(spread, F32),
            shape((9,) + line, F32),
            shape(line, F32),
            shape(line, F32),
            shape(line, F32),
        ],
        in_specs=[anywhere] * 5,
        out_specs=[anywhere] * 8,
        scratch_shapes=[
            pltpu.VMEM(out1.shape, out1.dtype),
            pltpu.VMEM(out2.shape, out2.dtype),
            pltpu.VMEM(out1.shape, F32),
            pltpu.VMEM(out2.shape, F32),
            pltpu.VMEM(slot, BF),
            pltpu.VMEM(slot, BF),
            pltpu.VMEM(spread, F32),
            pltpu.VMEM(outs.shape, F32),
            pltpu.VMEM((9,) + line, F32),
            pltpu.SemaphoreType.DMA((steps + 3,)),
            pltpu.SemaphoreType.DMA((steps + 6,)),
        ],
        name="finish",
        compiler_params=pltpu.CompilerParams(vmem_limit_bytes=60 * 2**20),
    )(out1, out2, act, ing, outs)


def per_device(
    images, cotangent, window_rows, window_cols, pos_kernel, pos_bias, norm_gain, norm_shift, first_weight, second_weight
):
    act, ing, out1, out2, outs = relay(
        window_rows, window_cols, images[0], cotangent[0], pos_kernel[0], pos_bias, norm_gain, norm_shift,
        first_weight[0], second_weight,
    )
    if lax.axis_size("dp") > RING:
        out1, out2, outs = lax.psum((out1.astype(F32) / RING, out2.astype(F32) / RING, outs / RING), "dp")
    out1, out2, act, ing, kern, bias, gain, move = finish(out1, out2, act, ing, outs)
    return (
        act[None],
        ing.transpose(2, 0, 1, 3),
        out1[None],
        out2,
        kern.transpose(1, 0, 2),
        bias,
        gain,
        move,
    )


def solution(mesh):
    in_specs = (
        P(("dp", "section"), None, None, None),
        P(("dp", "section"), None, None, None),
        P("dp"),
        P("dp"),
        P("section", None, None),
        P("section", None),
        P("section", None),
        P("section", None),
        P("section", None, None),
        P("section", None),
    )
    out_specs = (
        P(("dp", "section"), None, None, None),
        P(("dp", "section"), None, None, None),
        P("section", None, None),
        P("section", None),
        P("section", None, None),
        P("section", None),
        P("section", None),
        P("section", None),
    )
    return jax.shard_map(per_device, mesh=mesh, in_specs=in_specs, out_specs=out_specs, check_vma=False)
```

```python
from functools import partial

import jax
import jax.numpy as jnp
from jax import lax
from jax.experimental import pallas as pl
from jax.experimental.pallas import tpu as pltpu
from jax.sharding import PartitionSpec as P

D = 768
FF = 3072
HEADS = 24
HEAD = 32
WIN = 7
SIDE = 2
GRID = SIDE * WIN
CELL = 8
WROWS = WIN * CELL
HALF = GRID * CELL
ROWS = SIDE * HALF
GROUP = 256
PACK = GROUP // HEAD
NGROUP = D // GROUP
UNITS = NGROUP * SIDE * SIDE
LANE = 128
FTILE = 512
EPS = 1e-05
SCALE = HEAD ** (-0.5)
BF = jnp.bfloat16
F32 = jnp.float32
MESH = pl.DeviceIdType.MESH


def dot(a, b, ca=1, cb=0):
    return lax.dot_general(a, b, (((ca,), (cb,)), ((), ())), preferred_element_type=F32)


def lanes(index, width=LANE):
    return pl.ds(pl.multiple_of(index * width, width), width)


def halves(value):
    return value.reshape(SIDE, GRID, CELL, value.shape[-1])


def shifts(left, right):
    column = lax.broadcasted_iota(jnp.int32, left.shape, 1)
    before0 = pltpu.roll(left, 1, 1)
    after0 = jnp.where(column == WIN - 1, pltpu.roll(right, CELL - 2, 1), pltpu.roll(left, CELL - 1, 1))
    before1 = jnp.where(column == 0, pltpu.roll(left, 2, 1), pltpu.roll(right, 1, 1))
    after1 = pltpu.roll(right, CELL - 1, 1)
    return ((before0, left, after0), (before1, right, after1))


def gelu_parts(h):
    expo = jnp.exp(h * h * -0.5)
    t = 1.0 / (1.0 + (0.3275911 * 0.7071067811865476) * jnp.abs(h))
    poly = t * (0.127414796 + t * (-0.142248368 + t * (0.7107068705 + t * (-0.7265760135 + t * 0.5307027145))))
    tail = poly * expo
    phi = jnp.where(h >= 0, 1.0 - tail, tail)
    return h * phi, phi + h * expo * 0.3989422804014327


def front_forward(sec, m, ubuf, msk, pr, U, C, zz, xh, rs):
    zero = jnp.zeros((ROWS, LANE), F32)

    def conv(i, total):
        ls = lanes(i)
        u = ubuf[sec, m, :, ls].astype(F32)
        masked = halves(u * msk[m])
        U[0, 1 : GRID + 1, :, ls] = masked[0]
        U[1, 1 : GRID + 1, :, ls] = masked[1]
        moved = shifts(U[0, :, :, ls], U[1, :, :, ls])
        taps = pr[sec, :, ls]
        uh = halves(u)
        sums = []
        for wc in range(SIDE):
            acc = uh[wc] + taps[9:10, :][None]
            for a in range(3):
                for b in range(3):
                    acc = acc + moved[wc][b][a : a + GRID] * taps[3 * a + b : 3 * a + b + 1, :][None]
            acc = acc.reshape(HALF, LANE)
            C[pl.ds(wc * HALF, HALF), ls] = acc
            sums.append(acc)
        return total + jnp.concatenate(sums, axis=0)

    mean = jnp.sum(lax.fori_loop(0, D // LANE, conv, zero), axis=-1, keepdims=True) * (1.0 / D)

    def spread(i, total):
        centred = C[:, lanes(i)] - mean
        return total + centred * centred

    var = jnp.sum(lax.fori_loop(0, D // LANE, spread, zero), axis=-1, keepdims=True) * (1.0 / D)
    rstd = lax.rsqrt(var + EPS)
    rs[sec, m] = jnp.broadcast_to(rstd, (ROWS, LANE))

    def norm(i, carry):
        ls = lanes(i)
        xhat = (C[:, ls] - mean) * rstd
        xh[sec, m, :, ls] = xhat.astype(BF)
        zz[m, 2 * sec, :, ls] = (xhat * pr[sec, 10:11, ls] + pr[sec, 11:12, ls]).astype(BF)
        return carry

    lax.fori_loop(0, D // LANE, norm, 0)


def fold(value):
    return jnp.sum(value.reshape(ROWS // CELL, CELL, LANE), axis=0)


def front_backward(sec, m, msk, pr, U, T, gfull, xh, rs, sgp, out, sent):
    zero = jnp.zeros((ROWS, LANE), F32)

    def sums(i, carry):
        s1, s2 = carry
        ls = lanes(i)
        dz = T[:, ls]
        xhat = xh[sec, m, :, ls].astype(F32)
        both = xhat * dz
        sgp[sec, 10, :, ls] += fold(both)
        sgp[sec, 11, :, ls] += fold(dz)
        gain = pr[sec, 10:11, ls]
        return s1 + dz * gain, s2 + both * gain

    s1, s2 = lax.fori_loop(0, D // LANE, sums, (zero, zero))
    m1 = jnp.sum(s1, axis=-1, keepdims=True) * (1.0 / D)
    m2 = jnp.sum(s2, axis=-1, keepdims=True) * (1.0 / D)

    def back(i, carry):
        ls = lanes(i)
        xhat = xh[sec, m, :, ls].astype(F32)
        inner = T[:, ls] * pr[sec, 10:11, ls] - m1 - xhat * m2
        gc = gfull(i)[...].astype(F32) + rs[sec, m] * inner
        xh[sec, m, :, ls] = gc.astype(BF)
        gh = halves(gc)
        U[0, 1 : GRID + 1, :, ls] = gh[0]
        U[1, 1 : GRID + 1, :, ls] = gh[1]
        moved = shifts(U[0, :, :, ls], U[1, :, :, ls])
        taps = pr[sec, :, ls]
        mask = halves(msk[m])
        du = []
        for wc in range(SIDE):
            acc = jnp.zeros((GRID, CELL, LANE), F32)
            for a in range(3):
                for b in range(3):
                    tap = 3 * a + b
                    acc = acc + moved[wc][2 - b][2 - a : 2 - a + GRID] * taps[tap : tap + 1, :][None]
            du.append((gh[wc] + mask[wc] * acc).reshape(HALF, LANE))
        out(i)[...] = jnp.concatenate(du, axis=0).astype(BF)
        return carry

    lax.fori_loop(0, D // LANE // 2, back, 0)
    sent(0)
    lax.fori_loop(D // LANE // 2, D // LANE, back, 0)
    sent(1)


def front_sums(sec, m, ubuf, msk, U, xh, sgp):
    def part(i, carry):
        ls = lanes(i)
        gc = xh[sec, m, :, ls].astype(F32)
        sgp[sec, 9, :, ls] += fold(gc)
        gh = halves(gc)
        U[0, 1 : GRID + 1, :, ls] = gh[0]
        U[1, 1 : GRID + 1, :, ls] = gh[1]
        moved = shifts(U[0, :, :, ls], U[1, :, :, ls])
        um = halves(ubuf[sec, m, :, ls].astype(F32) * msk[m])
        for a in range(3):
            for b in range(3):
                kg = jnp.zeros((CELL, LANE), F32)
                for wc in range(SIDE):
                    kg = kg + jnp.sum(moved[wc][2 - b][2 - a : 2 - a + GRID] * um[wc], axis=0)
                sgp[sec, 3 * a + b, :, ls] += kg
        return carry

    lax.fori_loop(0, D // LANE, part, 0)


def spread_heads(value, head_of_lane):
    parts = [jnp.where(head_of_lane == h, value, 0.0) for h in range(PACK)]
    return jnp.concatenate(parts, axis=0).astype(BF)


def gather_heads(value, rows, head_of_lane):
    out = jnp.zeros((rows, GROUP), F32)
    for h in range(PACK):
        out = jnp.where(head_of_lane == h, value[h * rows : (h + 1) * rows], out)
    return out


def unit_slices(unit):
    pair, group = unit // NGROUP, lax.rem(unit, NGROUP)
    rows = [pl.ds(pl.multiple_of((2 * pair + w) * WROWS, 8), WROWS) for w in range(2)]
    cols = [pl.ds(pl.multiple_of(part * D + group * GROUP, LANE), GROUP) for part in range(3)]
    return rows, cols


def window_parts(m, i, qkv):
    rows, cols = unit_slices(i)
    head_of_lane = lax.broadcasted_iota(jnp.int32, (WROWS, GROUP), 1) // HEAD
    q = [qkv[m, r, cols[0]].astype(BF) for r in rows]
    kd = [spread_heads(qkv[m, r, cols[1]], head_of_lane) for r in rows]
    vd = [spread_heads(qkv[m, r, cols[2]], head_of_lane) for r in rows]
    return rows, cols, head_of_lane, q, kd, vd


def window_forward(m, qkv, pw, T):
    def unit(i, carry):
        rows, cols, head_of_lane, q, kd, vd = window_parts(m, i, qkv)
        s = [(dot(b, a, 1, 1) * SCALE).reshape(PACK, WROWS, WROWS) for a, b in zip(q, kd)]
        key = lax.broadcasted_iota(jnp.int32, s[0].shape, 1)
        real = lax.rem(key, CELL) < WIN
        s = [jnp.where(real, x, -1e30) for x in s]
        p = [jnp.exp(x - jnp.max(x, axis=1, keepdims=True)) for x in s]
        p = [x * (1.0 / jnp.sum(x, axis=1, keepdims=True)) for x in p]
        p = [x.reshape(PACK * WROWS, WROWS) for x in p]
        for w in range(2):
            pw[m, 2 * i + w, :, 0:WROWS] = p[w]
        out = [dot(x.astype(BF), v, 0, 0) for x, v in zip(p, vd)]
        for w in range(2):
            T[rows[w], cols[0]] = out[w]
        return carry

    lax.fori_loop(0, UNITS // 2, unit, 0)


def window_backward(m, qkv, pw, T):
    def unit(i, carry):
        rows, cols, head_of_lane, q, kd, vd = window_parts(m, i, qkv)
        g = [T[r, cols[0]].astype(BF) for r in rows]
        p = [pw[m, 2 * i + w, :, 0:WROWS].reshape(PACK, WROWS, WROWS) for w in range(2)]
        dp = [dot(v, x, 1, 1).reshape(PACK, WROWS, WROWS) for v, x in zip(vd, g)]
        ds = [x * (y - jnp.sum(x * y, axis=1, keepdims=True)) for x, y in zip(p, dp)]
        ds = [x.reshape(PACK * WROWS, WROWS).astype(BF) for x in ds]
        pb = [x.reshape(PACK * WROWS, WROWS).astype(BF) for x in p]
        dv = [gather_heads(dot(x, y), WROWS, head_of_lane) for x, y in zip(pb, g)]
        dk = [gather_heads(dot(x, y), WROWS, head_of_lane) * SCALE for x, y in zip(ds, q)]
        dq = [dot(x, y, 0, 0) * SCALE for x, y in zip(ds, kd)]
        for w in range(2):
            qkv[m, rows[w], cols[0]] = dq[w]
            qkv[m, rows[w], cols[1]] = dk[w]
            qkv[m, rows[w], cols[2]] = dv[w]
        return carry

    lax.fori_loop(0, UNITS // 2, unit, 0)


def group_slices(group):
    return [pl.ds(pl.multiple_of(part * D + group * GROUP, LANE), GROUP) for part in range(3)]


def channel_forward(m, qkv, pw, zz, msk):
    def unit(i, carry):
        cols = group_slices(i)
        mask = msk[m][:, :1]
        q = qkv[m, :, cols[0]].astype(BF)
        k = (qkv[m, :, cols[1]] * mask).astype(BF)
        v = qkv[m, :, cols[2]].astype(BF)
        s = dot(q, k, 0, 0) * SCALE
        same = (lax.broadcasted_iota(jnp.int32, s.shape, 0) // HEAD) == (lax.broadcasted_iota(jnp.int32, s.shape, 1) // HEAD)
        s = jnp.where(same, s, -1e30)
        p = jnp.exp(s - jnp.max(s, axis=1, keepdims=True))
        p = p * (1.0 / jnp.sum(p, axis=1, keepdims=True))
        for k in range(GROUP // LANE):
            pw[m, 2 * i + k, 0:GROUP, :] = p[:, k * LANE : (k + 1) * LANE]
        zz[m, 1, :, cols[0]] = dot(v, p.astype(BF), 1, 1).astype(BF)
        return carry

    lax.fori_loop(0, NGROUP, unit, 0, unroll=True)


def channel_backward(m, qkv, pw, T, rr, msk):
    def unit(i, carry):
        cols = group_slices(i)
        mask = msk[m][:, :1]
        q = qkv[m, :, cols[0]].astype(BF)
        k = (qkv[m, :, cols[1]] * mask).astype(BF)
        v = qkv[m, :, cols[2]].astype(BF)
        g = T[:, cols[0]].astype(BF)
        p = jnp.concatenate([pw[m, 2 * i + k, 0:GROUP, :] for k in range(GROUP // LANE)], axis=1)
        dp = dot(g, v, 0, 0)
        ds = (p * (dp - jnp.sum(p * dp, axis=1, keepdims=True))).astype(BF)
        rr[m, 0, :, cols[0]] = (dot(k, ds, 1, 1) * SCALE).astype(BF)
        rr[m, 0, :, cols[1]] = (dot(q, ds) * (SCALE * mask)).astype(BF)
        rr[m, 0, :, cols[2]] = (dot(g, p.astype(BF))).astype(BF)
        return carry

    lax.fori_loop(0, NGROUP, unit, 0, unroll=True)


RING = 8
COLS = FF // RING
WIDE = FF // 12 * 8 // RING
REST = FF // 6 // RING
FIFTH, SIXTH = FF // 6 * 4, FF // 6 * 5
EARLY = 2


def relay_kernel(
    wrows, wcols, img, cot, kern, bias, gain, move, first, second,
    act, ing, out1, out2, outs,
    wf, w2, pr, msk, flat, ubuf, gin, gout, zz, xh, rs, qkv, ab, rr, pw, U, C, T, sgp, sgs, sgm,
    rL, rR, rA, rG, xA, xG, buf, acc, got,
    wl, ws, wr, pl_, usem, gsem, us, gs, ss, rsem, es, er, sgsem, ssem, rcem, osem, sms, smr, xs, xr, ys, yr, bs, br, hs, hr, free,
):
    n = RING
    s = lax.axis_index("section")
    dp = lax.axis_index("dp")
    stage, c = s // 2, lax.rem(s, 2)
    mate = (dp, stage * 2 + (1 - c))
    opposite = (dp, (1 - stage) * 2 + c)
    lender, helper = s == 1, s == 3
    early = stage == 0

    spot = lax.rem(dp, n)
    base = dp - spot
    me = jnp.where(lax.rem(spot, 2) == 0, spot // 2, n - 1 - spot // 2)

    def place(pos):
        pos = lax.rem(pos + 2 * n, n)
        return (base + jnp.where(pos < n // 2, 2 * pos, 2 * (n - 1 - pos) + 1), s)

    nexts = (place(me + 1), place(me - 1))
    rounds = n.bit_length() - 1
    partners = []
    for r in range(rounds):
        bit = 1 << r
        partners.append((jnp.where(lax.rem(spot // bit, 2) == 0, dp + bit, dp - bit), s))

    barrier = pltpu.get_barrier_semaphore()
    peers = [mate, opposite, *nexts, *partners]
    for peer in peers:
        pl.semaphore_signal(barrier, inc=1, device_id=peer, device_id_type=MESH)
    pl.semaphore_wait(barrier, len(peers))

    def remote(src, dst, send, recv, peer):
        return pltpu.make_async_remote_copy(
            src_ref=src, dst_ref=dst, send_sem=send, recv_sem=recv, device_id=peer, device_id_type=MESH
        )

    half = second.shape[0]

    def weight_parts(k):
        parts = []
        for i in range(4):
            parts.append((first.at[:, pl.ds(i * D, D)], wf.at[k, :, pl.ds(i * D, D)]))
        parts.append((second, w2.at[pl.ds(k * half, half), :]))
        return parts

    def weight_copies(k):
        local = [pltpu.make_async_copy(a, b, wl.at[i]) for i, (a, b) in enumerate(weight_parts(k))]
        sent = [remote(a, b, ws.at[i], wr.at[i], mate) for i, (a, b) in enumerate(weight_parts(k))]
        return local, sent

    def params_copy(k):
        return remote(pr.at[k], pr.at[k], ws.at[5], wr.at[5], mate)

    pr[c, 0:9, :] = kern[...].astype(F32)
    pr[c, 9:10, :] = bias[...].astype(F32)
    pr[c, 10:11, :] = gain[...].astype(F32)
    pr[c, 11:12, :] = move[...].astype(F32)
    params_copy(c).start()
    for k in range(2):

        @pl.when(c == k)
        def _():
            local, sent = weight_copies(k)
            for i in range(5):
                local[i].start()
                sent[i].start()

    def wait_weight(k, i):
        if i < 5:

            @pl.when(c == k)
            def _():
                weight_copies(k)[0][i].wait()

        @pl.when(c != k)
        def _():
            (weight_copies(k)[1][i] if i < 5 else params_copy(k)).wait_recv()

    raw = flat.at[0]
    img_out = remote(img, raw, pl_.at[0], pl_.at[1], opposite)
    cot_out = remote(cot, raw, pl_.at[0], pl_.at[1], opposite)

    def pad(src, dst):
        blank = jnp.zeros((CELL - WIN, D), F32)
        for r in range(GRID):
            line = src[r].astype(F32)
            for wc in range(SIDE):
                cells = jnp.concatenate([line[wc * WIN : (wc + 1) * WIN], blank], axis=0)
                C[pl.ds(wc * HALF + r * CELL, CELL), :] = cells
        dst[...] = C[...].astype(BF)

    def unpad(dst):
        for r in range(GRID):
            sides = [C[pl.ds(wc * HALF + r * CELL, CELL), :][:WIN] for wc in range(SIDE)]
            dst[r] = jnp.concatenate(sides, axis=0).astype(BF)

    @pl.when(early)
    def _():
        cot_out.start()
        pad(img, ubuf.at[0, 0])

    @pl.when(jnp.logical_not(early))
    def _():
        img_out.start()
        pad(cot, gin.at[1])

    index = lax.broadcasted_iota(jnp.int32, (ROWS, LANE), 0)
    cell = lax.rem(index, CELL)
    row = lax.rem(index, HALF) // CELL
    column = (index // HALF) * WIN + cell
    for m in range(2):
        inside = (row < WIN * wrows[c + 2 * m]) & (column < WIN * wcols[c + 2 * m]) & (cell < WIN)
        msk[m] = jnp.where(inside, 1.0, 0.0)

    @pl.when(jnp.logical_not(early))
    def _():
        cot_out.wait_recv()
        pad(raw, gin.at[0])
        for m in range(2):
            for l in range(D // LANE):
                cols = pl.ds(l * LANE, LANE)
                gin[m, :, cols] = (gin[m, :, cols].astype(F32) * msk[m]).astype(BF)

    for wc in range(SIDE):
        U[wc, 0] = jnp.zeros((CELL, D), F32)
        U[wc, GRID + 1] = jnp.zeros((CELL, D), F32)
    sgp[...] = jnp.zeros(sgp.shape, F32)

    def hop(m, dst, send, recv):
        sides = [pl.ds(i * D // 2, D // 2) for i in range(2)]
        return [
            remote(gout.at[m, :, cols], dst.at[:, cols], send.at[m, i], recv.at[m, i], opposite)
            for i, cols in enumerate(sides)
        ]

    def u_hop(m):
        return hop(m, ubuf.at[0, m], us, usem)

    def g_hop(m):
        return hop(m, gin.at[m], gs, gsem)

    def factor_copies(k, m):
        if k == 0:
            parts = [
                ("F", zz.at[m, 0], rL.at[m, 0]),
                ("F", zz.at[m, 1], rL.at[m, 1]),
                ("G", rr.at[m, 0, :, pl.ds(3 * D, D)], rR.at[m, :, pl.ds(3 * D, D)]),
                ("A", rr.at[m, 0, :, pl.ds(0, 3 * D)], rR.at[m, :, pl.ds(0, 3 * D)]),
            ]
        else:
            parts = [
                ("F", zz.at[m, 2], rL.at[m, 0]),
                ("F", ab.at[m], rA.at[m]),
                ("M", gin.at[m], rG.at[m]),
            ]
            for i in range(3):
                cols = pl.ds(i * (FF // 3), FF // 3)
                parts.append((f"H{i}", rr.at[m, 1, :, cols], rR.at[m, :, cols]))
        return [(w, remote(a, b, ss.at[m, i], rsem.at[m, i], mate)) for i, (w, a, b) in enumerate(parts)]

    def start_factors(m, which):
        for k in range(2):

            @pl.when(c != k)
            def _():
                for when, copy in factor_copies(k, m):
                    if when == which:
                        copy.start()

    def wait_factors(which):
        for k in range(2):

            @pl.when(c == k)
            def _():
                for m in range(2):
                    for when, copy in factor_copies(k, m):
                        if when[0] in which:
                            copy.wait_recv()

    def shard(k):
        return lax.rem(k + 4 * n, n)

    def sign(h):
        return 1 if h == 0 else -1

    def home(h, t):
        return shard(me + sign(h) - sign(h) * t)

    def products(terms):
        total = None
        for a, b in terms:
            part = dot(a[...], b[...], 0, 0)
            total = part if total is None else total + part
        return total

    def pick(total, j):
        return jnp.where(lax.rem(j, 2) == 1, total[REST:], total[:REST])

    def tile(sub, h, j):
        side = pl.ds(h * COLS, COLS)
        if sub in (0, 4):
            rows = first_rows(sub, h)
            last = jnp.where(j >= (3 * n) // 4, 1, 0)
            own = jnp.where(c == 1, 2, last)
            other = jnp.where(c == 1, 0, last)
            cols = lanes(j, COLS)
            terms = [(zz.at[m, own, :, rows], rr.at[m, c, :, cols]) for m in range(2)]
            terms += [(rL.at[m, other, :, rows], rR.at[m, :, cols]) for m in range(2)]
        elif sub == 1:
            cols = lanes(j, WIDE)
            terms = [(ab.at[m, :, cols], gin.at[m, :, side]) for m in range(2)]
            terms += [(rA.at[m, :, cols], rG.at[m, :, side]) for m in range(2)]
        else:
            start = (FIFTH if sub == 2 else SIXTH) + j // 2 * 2 * REST
            cols = pl.ds(pl.multiple_of(start, LANE), 2 * REST)
            terms = [(ab.at[m, :, cols], gin.at[m, :, side]) for m in range(2)]
            terms += [(rA.at[m, :, cols], rG.at[m, :, side]) for m in range(2)]
            own = pick(products(terms), j)
            if sub == 2:
                return own
            cols = lanes(j // 2, 2 * REST)
            terms = [(xA.at[m, :, cols], gout.at[m, :, side]) for m in range(2)]
            terms += [(xA.at[2 + m, :, cols], xG.at[m, :, side]) for m in range(2)]
            return jnp.concatenate([own, pick(products(terms), j)], axis=0)
        return products(terms)

    sizes = (COLS // 3 * 2, WIDE, REST, 2 * REST, COLS // 3)
    parts = [pl.ds(sum(sizes[:i]), size) for i, size in enumerate(sizes)]
    subs = range(len(sizes))
    odd = c == 1
    active = (None, odd, odd, helper, None)

    def first_rows(sub, h):
        return pl.ds(h * COLS + (0 if sub == 0 else sizes[0]), sizes[sub])

    def where_active(sub, run):
        if active[sub] is None:
            run()
        else:
            pl.when(active[sub])(run)


    def gathered(sub, h, j):
        if sub in (0, 4):
            return wf.at[0, first_rows(sub, h), lanes(j, COLS)]
        if sub == 3:
            rows = pl.ds(pl.multiple_of(lax.rem(j, n // 2) * sizes[3], 16), sizes[3])
            return wf.at[1, rows, lanes(2 * (j // (n // 2)) + h, COLS)]
        first_row = 0 if sub == 1 else FIFTH
        return w2.at[pl.ds(pl.multiple_of(first_row + j * sizes[sub], 16), sizes[sub]), pl.ds(h * COLS, COLS)]

    def scatter(h, t, sub):
        src, dst = buf.at[h, t, parts[sub], :], buf.at[h, t + 1, parts[sub], :]
        return remote(src, dst, ssem.at[h, t, sub], rcem.at[h, t + 1, sub], nexts[h])

    def spread(h, t, sub, j):
        ref = gathered(sub, h, j)
        return remote(ref, ref, ssem.at[h, n - 1 + t, sub], rcem.at[h, n + t, sub], nexts[h])

    half_shards = n * 3 // 4

    def write(h, j, sub, part=0):
        src, side = gathered(sub, h, j), pl.ds(h * COLS, COLS)
        if sub in (0, 4):
            dst = out1.at[first_rows(sub, h), lanes(j, COLS)]
        elif sub == 1:
            dst = out2.at[pl.ds(pl.multiple_of((j - half_shards) * WIDE, 16), WIDE), side]
        else:
            first_row = (FIFTH if sub == 2 else SIXTH) - FF // 2
            dst = out2.at[pl.ds(pl.multiple_of(first_row + j * REST, 16), REST), side]
            src = src.at[pl.ds(part * REST, REST), :]
        if part == 1:
            return remote(src, dst, bs.at[h, j], br.at[h, j], opposite)
        return pltpu.make_async_copy(src, dst, osem.at[h, j, sub])

    def hand_over(h, j):
        dst = out2.at[pl.ds(pl.multiple_of(j * WIDE, 16), WIDE), pl.ds(h * COLS, COLS)]
        return remote(gathered(1, h, j), dst, hs.at[h, j], hr.at[h, j], mate)

    def deliver(h, j, sub):
        if sub == 1:

            @pl.when(j < half_shards)
            def _():
                hand_over(h, j).start()

            @pl.when(j >= half_shards)
            def _():
                write(h, j, sub).start()

        else:
            write(h, j, sub).start()
            if sub == 3:
                write(h, j, sub, 1).start()

    def lend(m):
        cols = pl.ds(SIXTH, FF - SIXTH)
        return (
            remote(ab.at[m, :, cols], xA.at[m], xs.at[m], xr.at[m], opposite),
            remote(rA.at[m, :, cols], xA.at[2 + m], xs.at[2 + m], xr.at[2 + m], opposite),
        )

    def share(m):
        return remote(gout.at[m], xG.at[m], ys.at[m], yr.at[m], mate)

    def reduce_event(sub, h, e):
        total = tile(sub, h, shard(me - sign(h) * e))

        @pl.when(e == 0)
        def _():
            buf[h, 0, parts[sub], :] = total.astype(BF)
            scatter(h, 0, sub).start()

        @pl.when((e > 0) & (e < n - 1))
        def _():
            scatter(h, e - 1, sub).wait_recv()
            buf[h, e, parts[sub], :] = (total + buf[h, e, parts[sub], :].astype(F32)).astype(BF)
            scatter(h, e, sub).start()

        @pl.when(e == n - 1)
        def _():
            j = home(h, 0)
            scatter(h, n - 2, sub).wait_recv()
            gathered(sub, h, j)[...] = (total + buf[h, n - 1, parts[sub], :].astype(F32)).astype(BF)
            pl.semaphore_wait(free.at[h, sub], 1)
            spread(h, 0, sub, j).start()
            deliver(h, j, sub)

    def event(sub, e):
        for h in range(2):

            @pl.when(e < n)
            def _():
                reduce_event(sub, h, e)

            @pl.when((e >= n) & (e < 2 * n - 1))
            def _():
                t = e - (n - 1)
                j = home(h, t)
                spread(h, t - 1, sub, j).wait_recv()

                @pl.when(t < n - 1)
                def _():
                    spread(h, t, sub, j).start()

                deliver(h, j, sub)

    def early_event(e, which):
        @pl.when(odd)
        def _():
            for sub in which:
                event(sub, e)

    def small(r):
        return remote(acc.at[r], got.at[r], sms.at[r], smr.at[r], partners[r])

    def forward(m, p):
        @pl.when(jnp.logical_not(early))
        def _():
            for copy in u_hop(m):
                copy.wait_recv()

        @pl.when(early & (m == 1))
        def _():
            img_out.wait_recv()
            pad(raw, ubuf.at[0, 1])

        once = p == 0

        def first_time(k, i):
            @pl.when(once)
            def _():
                wait_weight(k, i)

        first_time(0, 5)
        front_forward(0, m, ubuf, msk, pr, U, C, zz, xh, rs)
        for i in range(3):
            first_time(0, i)
            qkv[m, :, pl.ds(i * D, D)] = dot(zz[m, 0], wf[0, :, pl.ds(i * D, D)])

        @pl.when(early)
        def _():
            window_forward(m, qkv, pw, T)
            zz[m, 1] = T[...].astype(BF)

        @pl.when(jnp.logical_not(early))
        def _():
            channel_forward(m, qkv, pw, zz, msk)

        first_time(0, 3)
        ubuf[1, m] = (C[...] + dot(zz[m, 1], wf[0, :, pl.ds(3 * D, D)])).astype(BF)

        first_time(1, 5)
        front_forward(1, m, ubuf, msk, pr, U, C, zz, xh, rs)
        for i in range(4):
            first_time(1, i)
        first_time(0, 4)
        first_time(1, 4)

        total, before = C[...], None
        for t in range(FF // FTILE):
            cols = pl.ds(t * FTILE, FTILE)
            h = dot(zz[m, 2], wf[1, :, cols])
            if t > 0:
                total = total + dot(before, w2[pl.ds((t - 1) * FTILE, FTILE), :])
            a, d = gelu_parts(h)
            before = a.astype(BF)
            ab[m, :, cols] = before
            rr[m, 1, :, cols] = d.astype(BF)
        for i in range(2):
            cols = pl.ds(i * D // 2, D // 2)
            part = total[:, i * D // 2 : (i + 1) * D // 2]
            gout[m, :, cols] = (part + dot(before, w2[pl.ds(FF - FTILE, FTILE), cols])).astype(BF)

            @pl.when(early)
            def _():
                u_hop(m)[i].start()


        @pl.when(jnp.logical_not(early))
        def _():
            for l in range(D // LANE):
                cols = pl.ds(l * LANE, LANE)
                C[:, cols] = gout[m, :, cols].astype(F32) * msk[m]
            unpad(flat.at[m])

        @pl.when(jnp.logical_not(early) & (m == 0))
        def _():
            remote(flat.at[0], act, es.at[0], er.at[0], opposite).start()

        @pl.when(jnp.logical_not(early) & (m == 1))
        def _():
            pltpu.make_async_copy(flat.at[1], act, es.at[0]).start()

        start_factors(m, "F")

        @pl.when(early & (m == 1))
        def _():
            wait_factors("F")

        @pl.when(lender & (m == 1))
        def _():
            for i in range(2):
                for copy in lend(i):
                    copy.start()

    def backward(m):
        @pl.when(early)
        def _():
            for copy in g_hop(m):
                copy.wait_recv()

        start_factors(m, "M")
        for t in range(FF // FTILE):
            cols = pl.ds(t * FTILE, FTILE)
            da = dot(gin[m], w2[cols, :], 1, 1)
            rr[m, 1, :, cols] = (da * rr[m, 1, :, cols].astype(F32)).astype(BF)
            if t % 2 == 1:
                start_factors(m, f"H{t // 2}")

        @pl.when(m == 1)
        def _():
            @pl.when(jnp.logical_not(early))
            def _():
                wait_factors("F")

            wait_factors("M")
            early_event(0, (1, 2))

        T[...] = dot(rr[m, 1], wf[1], 1, 1)

        @pl.when(m == 1)
        def _():
            wait_factors("H")
            early_event(0, (0, 4))

        last = pl.ds(3 * D, D)

        @pl.when(early)
        def _():
            for copy in u_hop(m):
                copy.wait_send()

        def tail_lanes(i):
            return rr.at[m, 0, :, pl.ds(pl.multiple_of(3 * D + i * LANE, LANE), LANE)]

        def nothing(half):
            pass

        front_backward(1, m, msk, pr, U, T, lambda i: gin.at[m, :, lanes(i)], xh, rs, sgp, tail_lanes, nothing)
        start_factors(m, "G")

        T[...] = dot(rr[m, 0, :, last], wf[0, :, last], 1, 1)

        @pl.when(early)
        def _():
            window_backward(m, qkv, pw, T)
            for i in range(3):
                cols = pl.ds(i * D, D)
                rr[m, 0, :, cols] = qkv[m, :, cols].astype(BF)

        @pl.when(jnp.logical_not(early))
        def _():
            channel_backward(m, qkv, pw, T, rr, msk)

        start_factors(m, "A")

        @pl.when(m == 1)
        def _():
            for e in range(1, EARLY):
                early_event(e, (1, 2, 0, 4))

        T[...] = dot(rr[m, 0, :, pl.ds(0, 3 * D)], wf[0, :, pl.ds(0, 3 * D)], 1, 1)
        def send_half(half):
            @pl.when(jnp.logical_not(early))
            def _():
                g_hop(m)[half].start()

        front_backward(
            0, m, msk, pr, U, T, tail_lanes, xh, rs, sgp, lambda i: gout.at[m, :, lanes(i)], send_half
        )

        @pl.when(s == 2)
        def _():
            share(m).start()

        @pl.when(early)
        def _():
            C[...] = gout[m].astype(F32)
            unpad(flat.at[m])

        @pl.when(early & (m == 0))
        def _():
            pltpu.make_async_copy(flat.at[0], ing, es.at[1]).start()

        @pl.when(early & (m == 1))
        def _():
            remote(flat.at[1], ing, es.at[1], er.at[1], opposite).start()

    def phase(p, carry):
        m = jnp.where(early, lax.rem(p, 2), p // 2)
        ahead = jnp.where(early, p < 2, lax.rem(p, 2) == 0)

        @pl.when(ahead)
        def _():
            forward(m, p)

        @pl.when(jnp.logical_not(ahead))
        def _():
            backward(m)

        return carry

    lax.fori_loop(0, 4, phase, 0)

    for h in range(2):
        for sub in subs:

            def ready():
                pl.semaphore_signal(free.at[h, sub], inc=1, device_id=nexts[1 - h], device_id_type=MESH)

            where_active(sub, ready)

    give = remote(sgs.at[1 - c], sgm, sgsem.at[0], sgsem.at[1], mate)

    def small_sums():
        for sec in range(2):
            for j in range(12):
                sgs[sec, j : j + 1, :] = jnp.sum(sgp[sec, j], axis=0, keepdims=True)
            sgs[sec, 12:16, :] = jnp.zeros((4, D), F32)
        give.start()

    wait_factors("GA")

    @pl.when(helper)
    def _():
        for m in range(2):
            for copy in lend(m):
                copy.wait_recv()
            share(m).wait_recv()

    def ring_step(t, carry):
        for sub in (0, 4):
            event(sub, t + jnp.where(odd, EARLY, 0))
        where_active(1, lambda: event(1, t + EARLY))
        where_active(2, lambda: event(2, t + EARLY))
        where_active(3, lambda: event(3, t))
        @pl.when((t >= 1) & (t < 5))
        def _():
            front_sums((t - 1) // 2, lax.rem(t - 1, 2), ubuf, msk, U, xh, sgp)

        pl.when(t == 5)(small_sums)
        for r in range(rounds + 1):

            @pl.when(t == 6 + 2 * r)
            def _():
                if r == 0:
                    give.wait_recv()
                    acc[0] = sgs[c] + sgm[...]
                else:
                    small(r - 1).wait_recv()
                    acc[r] = acc[r - 1] + got[r - 1]
                if r < rounds:
                    small(r).start()

        return carry

    lax.fori_loop(0, 2 * n - 1, ring_step, 0)
    outs[...] = acc[rounds]

    for k in range(2):

        @pl.when(c == k)
        def _():
            for copy in weight_copies(k)[1]:
                copy.wait_send()
            params_copy(k).wait_send()
            for m in range(2):
                for _when, copy in factor_copies(1 - k, m):
                    copy.wait_send()

    give.wait_send()
    for r in range(rounds):
        small(r).wait_send()

    def drain(t, carry):
        for h in range(2):
            for sub in subs:

                def sent():
                    scatter(h, t, sub).wait_send()
                    spread(h, t, sub, home(h, t)).wait_send()

                where_active(sub, sent)

        return carry

    lax.fori_loop(0, n - 1, drain, 0)

    def written(j, carry):
        for h in range(2):
            write(h, j, 0).wait()
            write(h, j, 4).wait()

            @pl.when(odd)
            def _():
                write(h, j, 2).wait()

                @pl.when(j < half_shards)
                def _():
                    hand_over(h, j).wait_send()

                @pl.when(j >= half_shards)
                def _():
                    write(h, j, 1).wait()

            @pl.when(jnp.logical_not(odd) & (j < half_shards))
            def _():
                hand_over(h, j).wait_recv()

            @pl.when(helper)
            def _():
                write(h, j, 3).wait()
                write(h, j, 3, 1).wait_send()

            @pl.when(lender)
            def _():
                write(h, j, 3, 1).wait_recv()

        return carry

    lax.fori_loop(0, n, written, 0)

    @pl.when(lender)
    def _():
        for m in range(2):
            for copy in lend(m):
                copy.wait_send()

    @pl.when(s == 2)
    def _():
        for m in range(2):
            share(m).wait_send()

    @pl.when(early)
    def _():
        cot_out.wait_send()
        pltpu.make_async_copy(flat.at[0], ing, es.at[1]).wait()
        remote(flat.at[1], ing, es.at[1], er.at[1], opposite).wait_send()
        remote(flat.at[0], act, es.at[0], er.at[0], opposite).wait_recv()

    @pl.when(jnp.logical_not(early))
    def _():
        img_out.wait_send()
        for m in range(2):
            for copy in g_hop(m):
                copy.wait_send()
        remote(flat.at[0], act, es.at[0], er.at[0], opposite).wait_send()
        pltpu.make_async_copy(flat.at[1], act, es.at[0]).wait()
        remote(flat.at[1], ing, es.at[1], er.at[1], opposite).wait_recv()


def relay(wrows, wcols, img, cot, kern, bias, gain, move, first, second):
    shape = jax.ShapeDtypeStruct
    vmem = pl.BlockSpec(memory_space=pltpu.VMEM)
    anywhere = pl.BlockSpec(memory_space=pl.ANY)
    dma = pltpu.SemaphoreType.DMA
    smem = pl.BlockSpec(memory_space=pltpu.SMEM)
    image = (ROWS, D)
    slot = img.shape
    rounds = RING.bit_length() - 1
    return pl.pallas_call(
        relay_kernel,
        out_shape=[
            shape(slot, BF),
            shape(slot, BF),
            shape((D, FF), BF),
            shape((FF // 2, D), BF),
            shape((16, D), F32),
        ],
        in_specs=[smem] * 2 + [vmem] * 6 + [anywhere] * 2,
        out_specs=[anywhere] * 4 + [vmem],
        scratch_shapes=[
            pltpu.VMEM((2, D, FF), BF),
            pltpu.VMEM((FF, D), BF),
            pltpu.VMEM((2, 16, D), F32),
            pltpu.VMEM((2, ROWS, LANE), F32),
            pltpu.VMEM((2,) + slot, BF),
            pltpu.VMEM((2, 2) + image, BF),
            pltpu.VMEM((2,) + image, BF),
            pltpu.VMEM((2,) + image, BF),
            pltpu.VMEM((2, 3) + image, BF),
            pltpu.VMEM((2, 2) + image, BF),
            pltpu.VMEM((2, 2, ROWS, LANE), F32),
            pltpu.VMEM((2, ROWS, 3 * D), F32),
            pltpu.VMEM((2, ROWS, FF), BF),
            pltpu.VMEM((2, 2, ROWS, FF), BF),
            pltpu.VMEM((2, UNITS, PACK * WROWS, LANE), F32),
            pltpu.VMEM((SIDE, GRID + 2, CELL, D), F32),
            pltpu.VMEM(image, F32),
            pltpu.VMEM(image, F32),
            pltpu.VMEM((2, 12, CELL, D), F32),
            pltpu.VMEM((2, 16, D), F32),
            pltpu.VMEM((16, D), F32),
            pltpu.VMEM((2, 2) + image, BF),
            pltpu.VMEM((2, ROWS, FF), BF),
            pltpu.VMEM((2, ROWS, FF), BF),
            pltpu.VMEM((2,) + image, BF),
            pltpu.VMEM((4, ROWS, FF - SIXTH), BF),
            pltpu.VMEM((2,) + image, BF),
            pltpu.VMEM((2, RING, COLS + WIDE + 3 * REST, COLS), BF),
            pltpu.VMEM((rounds + 1, 16, D), F32),
            pltpu.VMEM((rounds, 16, D), F32),
            dma((5,)),
            dma((6,)),
            dma((6,)),
            dma((2,)),
            dma((2, 2)),
            dma((2, 2)),
            dma((2, 2)),
            dma((2, 2)),
            dma((2, 6)),
            dma((2, 6)),
            dma((2,)),
            dma((2,)),
            dma((2,)),
            dma((2, 2 * RING, 5)),
            dma((2, 2 * RING, 5)),
            dma((2, RING, 5)),
            dma((rounds,)),
            dma((rounds,)),
            dma((4,)),
            dma((4,)),
            dma((2,)),
            dma((2,)),
            dma((2, RING)),
            dma((2, RING)),
            dma((2, RING)),
            dma((2, RING)),
            pltpu.SemaphoreType.REGULAR((2, 5)),
        ],
        name="relay",
        compiler_params=pltpu.CompilerParams(
            collective_id=1, has_side_effects=True, vmem_limit_bytes=63 * 2**20
        ),
    )(wrows, wcols, img, cot, kern, bias, gain, move, first, second)


def finish_kernel(
    out1, out2, act, ing, outs, first, second, acts, ings, kern, bias, gain, move,
    raw1, raw2, full1, full2, acted, graded, wide, small, kernels, rsem, wsem,
):
    steps = rsem.shape[0] - 3

    loads = [
        pltpu.make_async_copy(act, acted, rsem.at[steps]),
        pltpu.make_async_copy(ing, graded, rsem.at[steps + 1]),
        pltpu.make_async_copy(outs, small, rsem.at[steps + 2]),
    ]
    for copy in loads:
        copy.start()
    reads, writes = [], []
    for i in range(steps):
        pair = ((out1, raw1, full1, first), (out2, raw2, full2, second))[i % 2]
        src, raw, full, dst = pair
        half = steps // 2
        rows = pl.ds(i // 2 * (src.shape[0] // half), src.shape[0] // half)
        reads.append((pltpu.make_async_copy(src.at[rows, :], raw.at[rows, :], rsem.at[i]), raw, full, rows))
        writes.append(pltpu.make_async_copy(full.at[rows, :], dst.at[rows, :], wsem.at[i]))
    for copy, *_ in reads:
        copy.start()
    for (copy, raw, full, rows), back in zip(reads, writes):
        copy.wait()
        full[rows, :] = raw[rows, :].astype(F32)
        back.start()
    for copy in loads:
        copy.wait()
    for k in range(9):
        kernels[k] = small[k : k + 1, :]
    for r in range(GRID):
        line = graded[r].astype(F32)
        for k in range(GRID):
            wide[r, k] = line[k : k + 1, :]
    last = [
        pltpu.make_async_copy(acted, acts, wsem.at[steps]),
        pltpu.make_async_copy(wide, ings, wsem.at[steps + 1]),
        pltpu.make_async_copy(kernels, kern, wsem.at[steps + 2]),
    ]
    for i, dst in enumerate((bias, gain, move)):
        last.append(pltpu.make_async_copy(small.at[pl.ds(9 + i, 1), :], dst, wsem.at[steps + 3 + i]))
    for copy in last:
        copy.start()
    for copy in writes + last:
        copy.wait()


def finish(out1, out2, act, ing, outs):
    shape = jax.ShapeDtypeStruct
    slot = act.shape
    anywhere = pl.BlockSpec(memory_space=pl.ANY)
    line = (1, D)
    spread = slot[:2] + line
    steps = 16
    return pl.pallas_call(
        finish_kernel,
        out_shape=[
            shape(out1.shape, F32),
            shape(out2.shape, F32),
            shape(slot, BF),
            shape(spread, F32),
            shape((9,) + line, F32),
            shape(line, F32),
            shape(line, F32),
            shape(line, F32),
        ],
        in_specs=[anywhere] * 5,
        out_specs=[anywhere] * 8,
        scratch_shapes=[
            pltpu.VMEM(out1.shape, out1.dtype),
            pltpu.VMEM(out2.shape, out2.dtype),
            pltpu.VMEM(out1.shape, F32),
            pltpu.VMEM(out2.shape, F32),
            pltpu.VMEM(slot, BF),
            pltpu.VMEM(slot, BF),
            pltpu.VMEM(spread, F32),
            pltpu.VMEM(outs.shape, F32),
            pltpu.VMEM((9,) + line, F32),
            pltpu.SemaphoreType.DMA((steps + 3,)),
            pltpu.SemaphoreType.DMA((steps + 6,)),
        ],
        name="finish",
        compiler_params=pltpu.CompilerParams(vmem_limit_bytes=60 * 2**20),
    )(out1, out2, act, ing, outs)


def per_device(
    images, cotangent, window_rows, window_cols, pos_kernel, pos_bias, norm_gain, norm_shift, first_weight, second_weight
):
    act, ing, out1, out2, outs = relay(
        window_rows, window_cols, images[0], cotangent[0], pos_kernel[0], pos_bias, norm_gain, norm_shift,
        first_weight[0], second_weight,
    )
    if lax.axis_size("dp") > RING:
        out1, out2, outs = lax.psum((out1.astype(F32) / RING, out2.astype(F32) / RING, outs / RING), "dp")
    out1, out2, act, ing, kern, bias, gain, move = finish(out1, out2, act, ing, outs)
    return (
        act[None],
        ing.transpose(2, 0, 1, 3),
        out1[None],
        out2,
        kern.transpose(1, 0, 2),
        bias,
        gain,
        move,
    )


def solution(mesh):
    in_specs = (
        P(("dp", "section"), None, None, None),
        P(("dp", "section"), None, None, None),
        P("dp"),
        P("dp"),
        P("section", None, None),
        P("section", None),
        P("section", None),
        P("section", None),
        P("section", None, None),
        P("section", None),
    )
    out_specs = (
        P(("dp", "section"), None, None, None),
        P(("dp", "section"), None, None, None),
        P("section", None, None),
        P("section", None),
        P("section", None, None),
        P("section", None),
        P("section", None),
        P("section", None),
    )
    return jax.shard_map(per_device, mesh=mesh, in_specs=in_specs, out_specs=out_specs, check_vma=False)
```

```python
from functools import partial

import jax
import jax.numpy as jnp
from jax import lax
from jax.experimental import pallas as pl
from jax.experimental.pallas import tpu as pltpu
from jax.sharding import PartitionSpec as P

D = 768
FF = 3072
HEADS = 24
HEAD = 32
WIN = 7
SIDE = 2
GRID = SIDE * WIN
CELL = 8
WROWS = WIN * CELL
HALF = GRID * CELL
ROWS = SIDE * HALF
GROUP = 256
PACK = GROUP // HEAD
NGROUP = D // GROUP
UNITS = NGROUP * SIDE * SIDE
LANE = 128
FTILE = 512
EPS = 1e-05
SCALE = HEAD ** (-0.5)
BF = jnp.bfloat16
F32 = jnp.float32
MESH = pl.DeviceIdType.MESH


def dot(a, b, ca=1, cb=0):
    return lax.dot_general(a, b, (((ca,), (cb,)), ((), ())), preferred_element_type=F32)


def lanes(index, width=LANE):
    return pl.ds(pl.multiple_of(index * width, width), width)


def halves(value):
    return value.reshape(SIDE, GRID, CELL, value.shape[-1])


def shifts(left, right):
    column = lax.broadcasted_iota(jnp.int32, left.shape, 1)
    before0 = pltpu.roll(left, 1, 1)
    after0 = jnp.where(column == WIN - 1, pltpu.roll(right, CELL - 2, 1), pltpu.roll(left, CELL - 1, 1))
    before1 = jnp.where(column == 0, pltpu.roll(left, 2, 1), pltpu.roll(right, 1, 1))
    after1 = pltpu.roll(right, CELL - 1, 1)
    return ((before0, left, after0), (before1, right, after1))


def gelu_parts(h):
    expo = jnp.exp(h * h * -0.5)
    t = 1.0 / (1.0 + (0.3275911 * 0.7071067811865476) * jnp.abs(h))
    poly = t * (0.127414796 + t * (-0.142248368 + t * (0.7107068705 + t * (-0.7265760135 + t * 0.5307027145))))
    tail = poly * expo
    phi = jnp.where(h >= 0, 1.0 - tail, tail)
    return h * phi, phi + h * expo * 0.3989422804014327


def front_forward(sec, m, ubuf, msk, pr, U, C, zz, xh, rs):
    zero = jnp.zeros((ROWS, LANE), F32)

    def conv(i, total):
        ls = lanes(i)
        u = ubuf[sec, m, :, ls].astype(F32)
        masked = halves(u * msk[m])
        U[0, 1 : GRID + 1, :, ls] = masked[0]
        U[1, 1 : GRID + 1, :, ls] = masked[1]
        moved = shifts(U[0, :, :, ls], U[1, :, :, ls])
        taps = pr[sec, :, ls]
        uh = halves(u)
        sums = []
        for wc in range(SIDE):
            acc = uh[wc] + taps[9:10, :][None]
            for a in range(3):
                for b in range(3):
                    acc = acc + moved[wc][b][a : a + GRID] * taps[3 * a + b : 3 * a + b + 1, :][None]
            acc = acc.reshape(HALF, LANE)
            C[pl.ds(wc * HALF, HALF), ls] = acc
            sums.append(acc)
        return total + jnp.concatenate(sums, axis=0)

    mean = jnp.sum(lax.fori_loop(0, D // LANE, conv, zero), axis=-1, keepdims=True) * (1.0 / D)

    def spread(i, total):
        centred = C[:, lanes(i)] - mean
        return total + centred * centred

    var = jnp.sum(lax.fori_loop(0, D // LANE, spread, zero), axis=-1, keepdims=True) * (1.0 / D)
    rstd = lax.rsqrt(var + EPS)
    rs[sec, m] = jnp.broadcast_to(rstd, (ROWS, LANE))

    def norm(i, carry):
        ls = lanes(i)
        xhat = (C[:, ls] - mean) * rstd
        xh[sec, m, :, ls] = xhat.astype(BF)
        zz[m, 2 * sec, :, ls] = (xhat * pr[sec, 10:11, ls] + pr[sec, 11:12, ls]).astype(BF)
        return carry

    lax.fori_loop(0, D // LANE, norm, 0)


def fold(value):
    return jnp.sum(value.reshape(ROWS // CELL, CELL, LANE), axis=0)


def front_backward(sec, m, msk, pr, U, T, gfull, xh, rs, sgp, out, sent):
    zero = jnp.zeros((ROWS, LANE), F32)

    def sums(i, carry):
        s1, s2 = carry
        ls = lanes(i)
        dz = T[:, ls]
        xhat = xh[sec, m, :, ls].astype(F32)
        both = xhat * dz
        sgp[sec, 10, :, ls] += fold(both)
        sgp[sec, 11, :, ls] += fold(dz)
        gain = pr[sec, 10:11, ls]
        return s1 + dz * gain, s2 + both * gain

    s1, s2 = lax.fori_loop(0, D // LANE, sums, (zero, zero))
    m1 = jnp.sum(s1, axis=-1, keepdims=True) * (1.0 / D)
    m2 = jnp.sum(s2, axis=-1, keepdims=True) * (1.0 / D)

    def back(i, carry):
        ls = lanes(i)
        xhat = xh[sec, m, :, ls].astype(F32)
        inner = T[:, ls] * pr[sec, 10:11, ls] - m1 - xhat * m2
        gc = gfull(i)[...].astype(F32) + rs[sec, m] * inner
        xh[sec, m, :, ls] = gc.astype(BF)
        gh = halves(gc)
        U[0, 1 : GRID + 1, :, ls] = gh[0]
        U[1, 1 : GRID + 1, :, ls] = gh[1]
        moved = shifts(U[0, :, :, ls], U[1, :, :, ls])
        taps = pr[sec, :, ls]
        mask = halves(msk[m])
        du = []
        for wc in range(SIDE):
            acc = jnp.zeros((GRID, CELL, LANE), F32)
            for a in range(3):
                for b in range(3):
                    tap = 3 * a + b
                    acc = acc + moved[wc][2 - b][2 - a : 2 - a + GRID] * taps[tap : tap + 1, :][None]
            du.append((gh[wc] + mask[wc] * acc).reshape(HALF, LANE))
        out(i)[...] = jnp.concatenate(du, axis=0).astype(BF)
        return carry

    lax.fori_loop(0, D // LANE // 2, back, 0)
    sent(0)
    lax.fori_loop(D // LANE // 2, D // LANE, back, 0)
    sent(1)


def front_sums(sec, m, ubuf, msk, U, xh, sgp):
    def part(i, carry):
        ls = lanes(i)
        gc = xh[sec, m, :, ls].astype(F32)
        sgp[sec, 9, :, ls] += fold(gc)
        gh = halves(gc)
        U[0, 1 : GRID + 1, :, ls] = gh[0]
        U[1, 1 : GRID + 1, :, ls] = gh[1]
        moved = shifts(U[0, :, :, ls], U[1, :, :, ls])
        um = halves(ubuf[sec, m, :, ls].astype(F32) * msk[m])
        for a in range(3):
            for b in range(3):
                kg = jnp.zeros((CELL, LANE), F32)
                for wc in range(SIDE):
                    kg = kg + jnp.sum(moved[wc][2 - b][2 - a : 2 - a + GRID] * um[wc], axis=0)
                sgp[sec, 3 * a + b, :, ls] += kg
        return carry

    lax.fori_loop(0, D // LANE, part, 0)


def spread_heads(value, head_of_lane):
    parts = [jnp.where(head_of_lane == h, value, 0.0) for h in range(PACK)]
    return jnp.concatenate(parts, axis=0).astype(BF)


def gather_heads(value, rows, head_of_lane):
    out = jnp.zeros((rows, GROUP), F32)
    for h in range(PACK):
        out = jnp.where(head_of_lane == h, value[h * rows : (h + 1) * rows], out)
    return out


def unit_slices(unit):
    pair, group = unit // NGROUP, lax.rem(unit, NGROUP)
    rows = [pl.ds(pl.multiple_of((2 * pair + w) * WROWS, 8), WROWS) for w in range(2)]
    cols = [pl.ds(pl.multiple_of(part * D + group * GROUP, LANE), GROUP) for part in range(3)]
    return rows, cols


def window_parts(m, i, qkv):
    rows, cols = unit_slices(i)
    head_of_lane = lax.broadcasted_iota(jnp.int32, (WROWS, GROUP), 1) // HEAD
    q = [qkv[m, r, cols[0]].astype(BF) for r in rows]
    kd = [spread_heads(qkv[m, r, cols[1]], head_of_lane) for r in rows]
    vd = [spread_heads(qkv[m, r, cols[2]], head_of_lane) for r in rows]
    return rows, cols, head_of_lane, q, kd, vd


def window_forward(m, qkv, pw, T):
    def unit(i, carry):
        rows, cols, head_of_lane, q, kd, vd = window_parts(m, i, qkv)
        s = [(dot(b, a, 1, 1) * SCALE).reshape(PACK, WROWS, WROWS) for a, b in zip(q, kd)]
        key = lax.broadcasted_iota(jnp.int32, s[0].shape, 1)
        real = lax.rem(key, CELL) < WIN
        s = [jnp.where(real, x, -1e30) for x in s]
        p = [jnp.exp(x - jnp.max(x, axis=1, keepdims=True)) for x in s]
        p = [x * (1.0 / jnp.sum(x, axis=1, keepdims=True)) for x in p]
        p = [x.reshape(PACK * WROWS, WROWS) for x in p]
        for w in range(2):
            pw[m, 2 * i + w, :, 0:WROWS] = p[w]
        out = [dot(x.astype(BF), v, 0, 0) for x, v in zip(p, vd)]
        for w in range(2):
            T[rows[w], cols[0]] = out[w]
        return carry

    lax.fori_loop(0, UNITS // 2, unit, 0)


def window_backward(m, qkv, pw, T):
    def unit(i, carry):
        rows, cols, head_of_lane, q, kd, vd = window_parts(m, i, qkv)
        g = [T[r, cols[0]].astype(BF) for r in rows]
        p = [pw[m, 2 * i + w, :, 0:WROWS].reshape(PACK, WROWS, WROWS) for w in range(2)]
        dp = [dot(v, x, 1, 1).reshape(PACK, WROWS, WROWS) for v, x in zip(vd, g)]
        ds = [x * (y - jnp.sum(x * y, axis=1, keepdims=True)) for x, y in zip(p, dp)]
        ds = [x.reshape(PACK * WROWS, WROWS).astype(BF) for x in ds]
        pb = [x.reshape(PACK * WROWS, WROWS).astype(BF) for x in p]
        dv = [gather_heads(dot(x, y), WROWS, head_of_lane) for x, y in zip(pb, g)]
        dk = [gather_heads(dot(x, y), WROWS, head_of_lane) * SCALE for x, y in zip(ds, q)]
        dq = [dot(x, y, 0, 0) * SCALE for x, y in zip(ds, kd)]
        for w in range(2):
            qkv[m, rows[w], cols[0]] = dq[w]
            qkv[m, rows[w], cols[1]] = dk[w]
            qkv[m, rows[w], cols[2]] = dv[w]
        return carry

    lax.fori_loop(0, UNITS // 2, unit, 0)


def group_slices(group):
    return [pl.ds(pl.multiple_of(part * D + group * GROUP, LANE), GROUP) for part in range(3)]


def channel_forward(m, qkv, pw, zz, msk):
    def unit(i, carry):
        cols = group_slices(i)
        mask = msk[m][:, :1]
        q = qkv[m, :, cols[0]].astype(BF)
        k = (qkv[m, :, cols[1]] * mask).astype(BF)
        v = qkv[m, :, cols[2]].astype(BF)
        s = dot(q, k, 0, 0) * SCALE
        same = (lax.broadcasted_iota(jnp.int32, s.shape, 0) // HEAD) == (lax.broadcasted_iota(jnp.int32, s.shape, 1) // HEAD)
        s = jnp.where(same, s, -1e30)
        p = jnp.exp(s - jnp.max(s, axis=1, keepdims=True))
        p = p * (1.0 / jnp.sum(p, axis=1, keepdims=True))
        for k in range(GROUP // LANE):
            pw[m, 2 * i + k, 0:GROUP, :] = p[:, k * LANE : (k + 1) * LANE]
        zz[m, 1, :, cols[0]] = dot(v, p.astype(BF), 1, 1).astype(BF)
        return carry

    lax.fori_loop(0, NGROUP, unit, 0, unroll=True)


def channel_backward(m, qkv, pw, T, rr, msk):
    def unit(i, carry):
        cols = group_slices(i)
        mask = msk[m][:, :1]
        q = qkv[m, :, cols[0]].astype(BF)
        k = (qkv[m, :, cols[1]] * mask).astype(BF)
        v = qkv[m, :, cols[2]].astype(BF)
        g = T[:, cols[0]].astype(BF)
        p = jnp.concatenate([pw[m, 2 * i + k, 0:GROUP, :] for k in range(GROUP // LANE)], axis=1)
        dp = dot(g, v, 0, 0)
        ds = (p * (dp - jnp.sum(p * dp, axis=1, keepdims=True))).astype(BF)
        rr[m, 0, :, cols[0]] = (dot(k, ds, 1, 1) * SCALE).astype(BF)
        rr[m, 0, :, cols[1]] = (dot(q, ds) * (SCALE * mask)).astype(BF)
        rr[m, 0, :, cols[2]] = (dot(g, p.astype(BF))).astype(BF)
        return carry

    lax.fori_loop(0, NGROUP, unit, 0, unroll=True)


RING = 8
COLS = FF // RING
WIDE = FF // 12 * 8 // RING
REST = FF // 3 // RING
THIRD = FF // 3 * 2
EARLY = 2


def relay_kernel(
    wrows, wcols, img, cot, kern, bias, gain, move, first, second,
    act, ing, out1, out2, outs,
    wf, w2, pr, msk, flat, ubuf, gin, gout, zz, xh, rs, qkv, ab, rr, pw, U, C, T, sgp, sgs, sgm,
    rL, rR, rA, rG, xA, xG, buf, acc, got,
    wl, ws, wr, pl_, usem, gsem, us, gs, ss, rsem, es, er, sgsem, ssem, rcem, osem, sms, smr, xs, xr, ys, yr, bs, br, hs, hr, free,
):
    n = RING
    s = lax.axis_index("section")
    dp = lax.axis_index("dp")
    stage, c = s // 2, lax.rem(s, 2)
    mate = (dp, stage * 2 + (1 - c))
    opposite = (dp, (1 - stage) * 2 + c)
    diagonal = (dp, 3 - s)
    lender, helper = s == 1, s == 2
    early = stage == 0

    spot = lax.rem(dp, n)
    base = dp - spot
    me = jnp.where(lax.rem(spot, 2) == 0, spot // 2, n - 1 - spot // 2)

    def place(pos):
        pos = lax.rem(pos + 2 * n, n)
        return (base + jnp.where(pos < n // 2, 2 * pos, 2 * (n - 1 - pos) + 1), s)

    nexts = (place(me + 1), place(me - 1))
    rounds = n.bit_length() - 1
    partners = []
    for r in range(rounds):
        bit = 1 << r
        partners.append((jnp.where(lax.rem(spot // bit, 2) == 0, dp + bit, dp - bit), s))

    barrier = pltpu.get_barrier_semaphore()
    peers = [mate, opposite, diagonal, *nexts, *partners]
    for peer in peers:
        pl.semaphore_signal(barrier, inc=1, device_id=peer, device_id_type=MESH)
    pl.semaphore_wait(barrier, len(peers))

    def remote(src, dst, send, recv, peer):
        return pltpu.make_async_remote_copy(
            src_ref=src, dst_ref=dst, send_sem=send, recv_sem=recv, device_id=peer, device_id_type=MESH
        )

    half = second.shape[0]

    def weight_parts(k):
        parts = []
        for i in range(4):
            parts.append((first.at[:, pl.ds(i * D, D)], wf.at[k, :, pl.ds(i * D, D)]))
        parts.append((second, w2.at[pl.ds(k * half, half), :]))
        return parts

    def weight_copies(k):
        local = [pltpu.make_async_copy(a, b, wl.at[i]) for i, (a, b) in enumerate(weight_parts(k))]
        sent = [remote(a, b, ws.at[i], wr.at[i], mate) for i, (a, b) in enumerate(weight_parts(k))]
        return local, sent

    def params_copy(k):
        return remote(pr.at[k], pr.at[k], ws.at[5], wr.at[5], mate)

    pr[c, 0:9, :] = kern[...].astype(F32)
    pr[c, 9:10, :] = bias[...].astype(F32)
    pr[c, 10:11, :] = gain[...].astype(F32)
    pr[c, 11:12, :] = move[...].astype(F32)
    params_copy(c).start()
    for k in range(2):

        @pl.when(c == k)
        def _():
            local, sent = weight_copies(k)
            for i in range(5):
                local[i].start()
                sent[i].start()

    def wait_weight(k, i):
        if i < 5:

            @pl.when(c == k)
            def _():
                weight_copies(k)[0][i].wait()

        @pl.when(c != k)
        def _():
            (weight_copies(k)[1][i] if i < 5 else params_copy(k)).wait_recv()

    raw = flat.at[0]
    img_out = remote(img, raw, pl_.at[0], pl_.at[1], opposite)
    cot_out = remote(cot, raw, pl_.at[0], pl_.at[1], opposite)

    def pad(src, dst):
        blank = jnp.zeros((CELL - WIN, D), F32)
        for r in range(GRID):
            line = src[r].astype(F32)
            for wc in range(SIDE):
                cells = jnp.concatenate([line[wc * WIN : (wc + 1) * WIN], blank], axis=0)
                C[pl.ds(wc * HALF + r * CELL, CELL), :] = cells
        dst[...] = C[...].astype(BF)

    def unpad(dst):
        for r in range(GRID):
            sides = [C[pl.ds(wc * HALF + r * CELL, CELL), :][:WIN] for wc in range(SIDE)]
            dst[r] = jnp.concatenate(sides, axis=0).astype(BF)

    @pl.when(early)
    def _():
        cot_out.start()
        pad(img, ubuf.at[0, 0])

    @pl.when(jnp.logical_not(early))
    def _():
        img_out.start()
        pad(cot, gin.at[1])

    index = lax.broadcasted_iota(jnp.int32, (ROWS, LANE), 0)
    cell = lax.rem(index, CELL)
    row = lax.rem(index, HALF) // CELL
    column = (index // HALF) * WIN + cell
    for m in range(2):
        inside = (row < WIN * wrows[c + 2 * m]) & (column < WIN * wcols[c + 2 * m]) & (cell < WIN)
        msk[m] = jnp.where(inside, 1.0, 0.0)

    @pl.when(jnp.logical_not(early))
    def _():
        cot_out.wait_recv()
        pad(raw, gin.at[0])
        for m in range(2):
            for l in range(D // LANE):
                cols = pl.ds(l * LANE, LANE)
                gin[m, :, cols] = (gin[m, :, cols].astype(F32) * msk[m]).astype(BF)

    for wc in range(SIDE):
        U[wc, 0] = jnp.zeros((CELL, D), F32)
        U[wc, GRID + 1] = jnp.zeros((CELL, D), F32)
    sgp[...] = jnp.zeros(sgp.shape, F32)

    def hop(m, dst, send, recv):
        sides = [pl.ds(i * D // 2, D // 2) for i in range(2)]
        return [
            remote(gout.at[m, :, cols], dst.at[:, cols], send.at[m, i], recv.at[m, i], opposite)
            for i, cols in enumerate(sides)
        ]

    def u_hop(m):
        return hop(m, ubuf.at[0, m], us, usem)

    def g_hop(m):
        return hop(m, gin.at[m], gs, gsem)

    def factor_copies(k, m):
        if k == 0:
            parts = [
                ("F", zz.at[m, 0], rL.at[m, 0]),
                ("F", zz.at[m, 1], rL.at[m, 1]),
                ("G", rr.at[m, 0, :, pl.ds(3 * D, D)], rR.at[m, :, pl.ds(3 * D, D)]),
                ("A", rr.at[m, 0, :, pl.ds(0, 3 * D)], rR.at[m, :, pl.ds(0, 3 * D)]),
            ]
        else:
            parts = [
                ("F", zz.at[m, 2], rL.at[m, 0]),
                ("F", ab.at[m], rA.at[m]),
                ("M", gin.at[m], rG.at[m]),
            ]
            for i in range(3):
                cols = pl.ds(i * (FF // 3), FF // 3)
                parts.append((f"H{i}", rr.at[m, 1, :, cols], rR.at[m, :, cols]))
        return [(w, remote(a, b, ss.at[m, i], rsem.at[m, i], mate)) for i, (w, a, b) in enumerate(parts)]

    def start_factors(m, which):
        for k in range(2):

            @pl.when(c != k)
            def _():
                for when, copy in factor_copies(k, m):
                    if when == which:
                        copy.start()

    def wait_factors(which):
        for k in range(2):

            @pl.when(c == k)
            def _():
                for m in range(2):
                    for when, copy in factor_copies(k, m):
                        if when[0] in which:
                            copy.wait_recv()

    def shard(k):
        return lax.rem(k + 4 * n, n)

    def sign(h):
        return 1 if h == 0 else -1

    def home(h, t):
        return shard(me + sign(h) - sign(h) * t)

    def products(terms):
        total = None
        for a, b in terms:
            part = dot(a[...], b[...], 0, 0)
            total = part if total is None else total + part
        return total

    def tile(sub, h, j):
        side = pl.ds(h * COLS, COLS)
        if sub in (0, 4):
            rows = first_rows(sub, h)
            last = jnp.where(j >= (3 * n) // 4, 1, 0)
            own = jnp.where(c == 1, 2, last)
            other = jnp.where(c == 1, 0, last)
            cols = lanes(j, COLS)
            terms = [(zz.at[m, own, :, rows], rr.at[m, c, :, cols]) for m in range(2)]
            terms += [(rL.at[m, other, :, rows], rR.at[m, :, cols]) for m in range(2)]
        elif sub == 3:
            cols = lanes(j, REST)
            terms = [(xA.at[m, :, cols], xG.at[m, :, side]) for m in range(2)]
            terms += [(xA.at[2 + m, :, cols], gout.at[m, :, side]) for m in range(2)]
        else:
            cols = lanes(j, WIDE) if sub == 1 else pl.ds(pl.multiple_of(THIRD + j * REST, LANE), REST)
            terms = [(ab.at[m, :, cols], gin.at[m, :, side]) for m in range(2)]
            terms += [(rA.at[m, :, cols], rG.at[m, :, side]) for m in range(2)]
        return products(terms)

    sizes = (COLS // 3 * 2, WIDE, REST, REST, COLS // 3)
    starts = (0, COLS, COLS + WIDE, COLS + WIDE, COLS // 3 * 2)
    parts = [pl.ds(start, size) for start, size in zip(starts, sizes)]
    subs = range(len(sizes))
    odd = c == 1
    active = (None, odd, s == 3, helper, None)

    def first_rows(sub, h):
        return pl.ds(h * COLS + (0 if sub == 0 else sizes[0]), sizes[sub])

    def where_active(sub, run):
        if active[sub] is None:
            run()
        else:
            pl.when(active[sub])(run)


    def gathered(sub, h, j):
        if sub in (0, 4):
            return wf.at[0, first_rows(sub, h), lanes(j, COLS)]
        first_row = 0 if sub == 1 else THIRD
        return w2.at[pl.ds(pl.multiple_of(first_row + j * sizes[sub], 16), sizes[sub]), pl.ds(h * COLS, COLS)]

    def scatter(h, t, sub):
        src, dst = buf.at[h, t, parts[sub], :], buf.at[h, t + 1, parts[sub], :]
        return remote(src, dst, ssem.at[h, t, sub], rcem.at[h, t + 1, sub], nexts[h])

    def spread(h, t, sub, j):
        ref = gathered(sub, h, j)
        return remote(ref, ref, ssem.at[h, n - 1 + t, sub], rcem.at[h, n + t, sub], nexts[h])

    half_shards = n * 3 // 4

    def write(h, j, sub):
        src, side = gathered(sub, h, j), pl.ds(h * COLS, COLS)
        if sub in (0, 4):
            dst = out1.at[first_rows(sub, h), lanes(j, COLS)]
        elif sub == 1:
            dst = out2.at[pl.ds(pl.multiple_of((j - half_shards) * WIDE, 16), WIDE), side]
        else:
            dst = out2.at[pl.ds(pl.multiple_of(THIRD - FF // 2 + j * REST, 16), REST), side]
        if sub == 3:
            return remote(src, dst, bs.at[h, j], br.at[h, j], diagonal)
        return pltpu.make_async_copy(src, dst, osem.at[h, j, sub])

    def hand_over(h, j):
        dst = out2.at[pl.ds(pl.multiple_of(j * WIDE, 16), WIDE), pl.ds(h * COLS, COLS)]
        return remote(gathered(1, h, j), dst, hs.at[h, j], hr.at[h, j], mate)

    def deliver(h, j, sub):
        if sub == 1:

            @pl.when(j < half_shards)
            def _():
                hand_over(h, j).start()

            @pl.when(j >= half_shards)
            def _():
                write(h, j, sub).start()

        else:
            write(h, j, sub).start()

    def lend(m):
        cols = pl.ds(THIRD, FF - THIRD)
        return (
            remote(ab.at[m, :, cols], xA.at[m], xs.at[m], xr.at[m], diagonal),
            remote(rA.at[m, :, cols], xA.at[2 + m], xs.at[2 + m], xr.at[2 + m], diagonal),
        )

    def share(m):
        return remote(gout.at[m], xG.at[m], ys.at[m], yr.at[m], mate)

    def reduce_event(sub, h, e):
        total = tile(sub, h, shard(me - sign(h) * e))

        @pl.when(e == 0)
        def _():
            buf[h, 0, parts[sub], :] = total.astype(BF)
            scatter(h, 0, sub).start()

        @pl.when((e > 0) & (e < n - 1))
        def _():
            scatter(h, e - 1, sub).wait_recv()
            buf[h, e, parts[sub], :] = (total + buf[h, e, parts[sub], :].astype(F32)).astype(BF)
            scatter(h, e, sub).start()

        @pl.when(e == n - 1)
        def _():
            j = home(h, 0)
            scatter(h, n - 2, sub).wait_recv()
            gathered(sub, h, j)[...] = (total + buf[h, n - 1, parts[sub], :].astype(F32)).astype(BF)
            pl.semaphore_wait(free.at[h, sub], 1)
            spread(h, 0, sub, j).start()
            deliver(h, j, sub)

    def event(sub, e):
        for h in range(2):

            @pl.when(e < n)
            def _():
                reduce_event(sub, h, e)

            @pl.when((e >= n) & (e < 2 * n - 1))
            def _():
                t = e - (n - 1)
                j = home(h, t)
                spread(h, t - 1, sub, j).wait_recv()

                @pl.when(t < n - 1)
                def _():
                    spread(h, t, sub, j).start()

                deliver(h, j, sub)

    def early_event(e, which):
        @pl.when(odd)
        def _():
            for sub in which:
                where_active(sub, lambda: event(sub, e))

    def small(r):
        return remote(acc.at[r], got.at[r], sms.at[r], smr.at[r], partners[r])

    def forward(m, p):
        @pl.when(jnp.logical_not(early))
        def _():
            for copy in u_hop(m):
                copy.wait_recv()

        @pl.when(early & (m == 1))
        def _():
            img_out.wait_recv()
            pad(raw, ubuf.at[0, 1])

        once = p == 0

        def first_time(k, i):
            @pl.when(once)
            def _():
                wait_weight(k, i)

        first_time(0, 5)
        front_forward(0, m, ubuf, msk, pr, U, C, zz, xh, rs)
        for i in range(3):
            first_time(0, i)
            qkv[m, :, pl.ds(i * D, D)] = dot(zz[m, 0], wf[0, :, pl.ds(i * D, D)])

        @pl.when(early)
        def _():
            window_forward(m, qkv, pw, T)
            zz[m, 1] = T[...].astype(BF)

        @pl.when(jnp.logical_not(early))
        def _():
            channel_forward(m, qkv, pw, zz, msk)

        first_time(0, 3)
        ubuf[1, m] = (C[...] + dot(zz[m, 1], wf[0, :, pl.ds(3 * D, D)])).astype(BF)

        first_time(1, 5)
        front_forward(1, m, ubuf, msk, pr, U, C, zz, xh, rs)
        for i in range(4):
            first_time(1, i)
        first_time(0, 4)
        first_time(1, 4)

        total, before = C[...], None
        for t in range(FF // FTILE):
            cols = pl.ds(t * FTILE, FTILE)
            h = dot(zz[m, 2], wf[1, :, cols])
            if t > 0:
                total = total + dot(before, w2[pl.ds((t - 1) * FTILE, FTILE), :])
            a, d = gelu_parts(h)
            before = a.astype(BF)
            ab[m, :, cols] = before
            rr[m, 1, :, cols] = d.astype(BF)
        for i in range(2):
            cols = pl.ds(i * D // 2, D // 2)
            part = total[:, i * D // 2 : (i + 1) * D // 2]
            gout[m, :, cols] = (part + dot(before, w2[pl.ds(FF - FTILE, FTILE), cols])).astype(BF)

            @pl.when(early)
            def _():
                u_hop(m)[i].start()


        @pl.when(jnp.logical_not(early))
        def _():
            for l in range(D // LANE):
                cols = pl.ds(l * LANE, LANE)
                C[:, cols] = gout[m, :, cols].astype(F32) * msk[m]
            unpad(flat.at[m])

        @pl.when(jnp.logical_not(early) & (m == 0))
        def _():
            remote(flat.at[0], act, es.at[0], er.at[0], opposite).start()

        @pl.when(jnp.logical_not(early) & (m == 1))
        def _():
            pltpu.make_async_copy(flat.at[1], act, es.at[0]).start()

        start_factors(m, "F")

        @pl.when(early & (m == 1))
        def _():
            wait_factors("F")

        @pl.when(lender & (m == 1))
        def _():
            for i in range(2):
                for copy in lend(i):
                    copy.start()

    def backward(m):
        @pl.when(early)
        def _():
            for copy in g_hop(m):
                copy.wait_recv()

        start_factors(m, "M")
        for t in range(FF // FTILE):
            cols = pl.ds(t * FTILE, FTILE)
            da = dot(gin[m], w2[cols, :], 1, 1)
            rr[m, 1, :, cols] = (da * rr[m, 1, :, cols].astype(F32)).astype(BF)
            if t % 2 == 1:
                start_factors(m, f"H{t // 2}")

        @pl.when(m == 1)
        def _():
            @pl.when(jnp.logical_not(early))
            def _():
                wait_factors("F")

            wait_factors("M")
            early_event(0, (1, 2))

        T[...] = dot(rr[m, 1], wf[1], 1, 1)

        @pl.when(m == 1)
        def _():
            wait_factors("H")
            early_event(0, (0, 4))

        last = pl.ds(3 * D, D)

        @pl.when(early)
        def _():
            for copy in u_hop(m):
                copy.wait_send()

        def tail_lanes(i):
            return rr.at[m, 0, :, pl.ds(pl.multiple_of(3 * D + i * LANE, LANE), LANE)]

        def nothing(half):
            pass

        front_backward(1, m, msk, pr, U, T, lambda i: gin.at[m, :, lanes(i)], xh, rs, sgp, tail_lanes, nothing)
        start_factors(m, "G")

        T[...] = dot(rr[m, 0, :, last], wf[0, :, last], 1, 1)

        @pl.when(early)
        def _():
            window_backward(m, qkv, pw, T)
            for i in range(3):
                cols = pl.ds(i * D, D)
                rr[m, 0, :, cols] = qkv[m, :, cols].astype(BF)

        @pl.when(jnp.logical_not(early))
        def _():
            channel_backward(m, qkv, pw, T, rr, msk)

        start_factors(m, "A")

        @pl.when(m == 1)
        def _():
            for e in range(1, EARLY):
                early_event(e, (1, 2, 0, 4))

        T[...] = dot(rr[m, 0, :, pl.ds(0, 3 * D)], wf[0, :, pl.ds(0, 3 * D)], 1, 1)
        def send_half(half):
            @pl.when(jnp.logical_not(early))
            def _():
                g_hop(m)[half].start()

        front_backward(
            0, m, msk, pr, U, T, tail_lanes, xh, rs, sgp, lambda i: gout.at[m, :, lanes(i)], send_half
        )

        @pl.when(s == 3)
        def _():
            share(m).start()

        @pl.when(early)
        def _():
            C[...] = gout[m].astype(F32)
            unpad(flat.at[m])

        @pl.when(early & (m == 0))
        def _():
            pltpu.make_async_copy(flat.at[0], ing, es.at[1]).start()

        @pl.when(early & (m == 1))
        def _():
            remote(flat.at[1], ing, es.at[1], er.at[1], opposite).start()

    def phase(p, carry):
        m = jnp.where(early, lax.rem(p, 2), p // 2)
        ahead = jnp.where(early, p < 2, lax.rem(p, 2) == 0)

        @pl.when(ahead)
        def _():
            forward(m, p)

        @pl.when(jnp.logical_not(ahead))
        def _():
            backward(m)

        return carry

    lax.fori_loop(0, 4, phase, 0)

    for h in range(2):
        for sub in subs:

            def ready():
                pl.semaphore_signal(free.at[h, sub], inc=1, device_id=nexts[1 - h], device_id_type=MESH)

            where_active(sub, ready)

    give = remote(sgs.at[1 - c], sgm, sgsem.at[0], sgsem.at[1], mate)

    def small_sums():
        for sec in range(2):
            for j in range(12):
                sgs[sec, j : j + 1, :] = jnp.sum(sgp[sec, j], axis=0, keepdims=True)
            sgs[sec, 12:16, :] = jnp.zeros((4, D), F32)
        give.start()

    wait_factors("GA")

    @pl.when(helper)
    def _():
        for m in range(2):
            for copy in lend(m):
                copy.wait_recv()
            share(m).wait_recv()

    def ring_step(t, carry):
        for sub in (0, 4):
            event(sub, t + jnp.where(odd, EARLY, 0))
        where_active(1, lambda: event(1, t + EARLY))
        where_active(2, lambda: event(2, t + EARLY))
        where_active(3, lambda: event(3, t))
        @pl.when((t >= 1) & (t < 5))
        def _():
            front_sums((t - 1) // 2, lax.rem(t - 1, 2), ubuf, msk, U, xh, sgp)

        pl.when(t == 5)(small_sums)
        for r in range(rounds + 1):

            @pl.when(t == 6 + 2 * r)
            def _():
                if r == 0:
                    give.wait_recv()
                    acc[0] = sgs[c] + sgm[...]
                else:
                    small(r - 1).wait_recv()
                    acc[r] = acc[r - 1] + got[r - 1]
                if r < rounds:
                    small(r).start()

        return carry

    lax.fori_loop(0, 2 * n - 1, ring_step, 0)
    outs[...] = acc[rounds]

    for k in range(2):

        @pl.when(c == k)
        def _():
            for copy in weight_copies(k)[1]:
                copy.wait_send()
            params_copy(k).wait_send()
            for m in range(2):
                for _when, copy in factor_copies(1 - k, m):
                    copy.wait_send()

    give.wait_send()
    for r in range(rounds):
        small(r).wait_send()

    def drain(t, carry):
        for h in range(2):
            for sub in subs:

                def sent():
                    scatter(h, t, sub).wait_send()
                    spread(h, t, sub, home(h, t)).wait_send()

                where_active(sub, sent)

        return carry

    lax.fori_loop(0, n - 1, drain, 0)

    def written(j, carry):
        for h in range(2):
            write(h, j, 0).wait()
            write(h, j, 4).wait()

            @pl.when(odd)
            def _():
                where_active(2, lambda: write(h, j, 2).wait())

                @pl.when(j < half_shards)
                def _():
                    hand_over(h, j).wait_send()

                @pl.when(j >= half_shards)
                def _():
                    write(h, j, 1).wait()

            @pl.when(jnp.logical_not(odd) & (j < half_shards))
            def _():
                hand_over(h, j).wait_recv()

            @pl.when(helper)
            def _():
                write(h, j, 3).wait_send()

            @pl.when(lender)
            def _():
                write(h, j, 3).wait_recv()

        return carry

    lax.fori_loop(0, n, written, 0)

    @pl.when(lender)
    def _():
        for m in range(2):
            for copy in lend(m):
                copy.wait_send()

    @pl.when(s == 3)
    def _():
        for m in range(2):
            share(m).wait_send()

    @pl.when(early)
    def _():
        cot_out.wait_send()
        pltpu.make_async_copy(flat.at[0], ing, es.at[1]).wait()
        remote(flat.at[1], ing, es.at[1], er.at[1], opposite).wait_send()
        remote(flat.at[0], act, es.at[0], er.at[0], opposite).wait_recv()

    @pl.when(jnp.logical_not(early))
    def _():
        img_out.wait_send()
        for m in range(2):
            for copy in g_hop(m):
                copy.wait_send()
        remote(flat.at[0], act, es.at[0], er.at[0], opposite).wait_send()
        pltpu.make_async_copy(flat.at[1], act, es.at[0]).wait()
        remote(flat.at[1], ing, es.at[1], er.at[1], opposite).wait_recv()


def relay(wrows, wcols, img, cot, kern, bias, gain, move, first, second):
    shape = jax.ShapeDtypeStruct
    vmem = pl.BlockSpec(memory_space=pltpu.VMEM)
    anywhere = pl.BlockSpec(memory_space=pl.ANY)
    dma = pltpu.SemaphoreType.DMA
    smem = pl.BlockSpec(memory_space=pltpu.SMEM)
    image = (ROWS, D)
    slot = img.shape
    rounds = RING.bit_length() - 1
    return pl.pallas_call(
        relay_kernel,
        out_shape=[
            shape(slot, BF),
            shape(slot, BF),
            shape((D, FF), BF),
            shape((FF // 2, D), BF),
            shape((16, D), F32),
        ],
        in_specs=[smem] * 2 + [vmem] * 6 + [anywhere] * 2,
        out_specs=[anywhere] * 4 + [vmem],
        scratch_shapes=[
            pltpu.VMEM((2, D, FF), BF),
            pltpu.VMEM((FF, D), BF),
            pltpu.VMEM((2, 16, D), F32),
            pltpu.VMEM((2, ROWS, LANE), F32),
            pltpu.VMEM((2,) + slot, BF),
            pltpu.VMEM((2, 2) + image, BF),
            pltpu.VMEM((2,) + image, BF),
            pltpu.VMEM((2,) + image, BF),
            pltpu.VMEM((2, 3) + image, BF),
            pltpu.VMEM((2, 2) + image, BF),
            pltpu.VMEM((2, 2, ROWS, LANE), F32),
            pltpu.VMEM((2, ROWS, 3 * D), F32),
            pltpu.VMEM((2, ROWS, FF), BF),
            pltpu.VMEM((2, 2, ROWS, FF), BF),
            pltpu.VMEM((2, UNITS, PACK * WROWS, LANE), F32),
            pltpu.VMEM((SIDE, GRID + 2, CELL, D), F32),
            pltpu.VMEM(image, F32),
            pltpu.VMEM(image, F32),
            pltpu.VMEM((2, 12, CELL, D), F32),
            pltpu.VMEM((2, 16, D), F32),
            pltpu.VMEM((16, D), F32),
            pltpu.VMEM((2, 2) + image, BF),
            pltpu.VMEM((2, ROWS, FF), BF),
            pltpu.VMEM((2, ROWS, FF), BF),
            pltpu.VMEM((2,) + image, BF),
            pltpu.VMEM((4, ROWS, FF - THIRD), BF),
            pltpu.VMEM((2,) + image, BF),
            pltpu.VMEM((2, RING, COLS + WIDE + REST, COLS), BF),
            pltpu.VMEM((rounds + 1, 16, D), F32),
            pltpu.VMEM((rounds, 16, D), F32),
            dma((5,)),
            dma((6,)),
            dma((6,)),
            dma((2,)),
            dma((2, 2)),
            dma((2, 2)),
            dma((2, 2)),
            dma((2, 2)),
            dma((2, 6)),
            dma((2, 6)),
            dma((2,)),
            dma((2,)),
            dma((2,)),
            dma((2, 2 * RING, 5)),
            dma((2, 2 * RING, 5)),
            dma((2, RING, 5)),
            dma((rounds,)),
            dma((rounds,)),
            dma((4,)),
            dma((4,)),
            dma((2,)),
            dma((2,)),
            dma((2, RING)),
            dma((2, RING)),
            dma((2, RING)),
            dma((2, RING)),
            pltpu.SemaphoreType.REGULAR((2, 5)),
        ],
        name="relay",
        compiler_params=pltpu.CompilerParams(
            collective_id=1, has_side_effects=True, vmem_limit_bytes=63 * 2**20
        ),
    )(wrows, wcols, img, cot, kern, bias, gain, move, first, second)


def finish_kernel(
    out1, out2, act, ing, outs, first, second, acts, ings, kern, bias, gain, move,
    raw1, raw2, full1, full2, acted, graded, wide, small, kernels, rsem, wsem,
):
    steps = rsem.shape[0] - 3

    loads = [
        pltpu.make_async_copy(act, acted, rsem.at[steps]),
        pltpu.make_async_copy(ing, graded, rsem.at[steps + 1]),
        pltpu.make_async_copy(outs, small, rsem.at[steps + 2]),
    ]
    for copy in loads:
        copy.start()
    reads, writes = [], []
    for i in range(steps):
        pair = ((out1, raw1, full1, first), (out2, raw2, full2, second))[i % 2]
        src, raw, full, dst = pair
        half = steps // 2
        rows = pl.ds(i // 2 * (src.shape[0] // half), src.shape[0] // half)
        reads.append((pltpu.make_async_copy(src.at[rows, :], raw.at[rows, :], rsem.at[i]), raw, full, rows))
        writes.append(pltpu.make_async_copy(full.at[rows, :], dst.at[rows, :], wsem.at[i]))
    for copy, *_ in reads:
        copy.start()
    for (copy, raw, full, rows), back in zip(reads, writes):
        copy.wait()
        full[rows, :] = raw[rows, :].astype(F32)
        back.start()
    for copy in loads:
        copy.wait()
    for k in range(9):
        kernels[k] = small[k : k + 1, :]
    for r in range(GRID):
        line = graded[r].astype(F32)
        for k in range(GRID):
            wide[r, k] = line[k : k + 1, :]
    last = [
        pltpu.make_async_copy(acted, acts, wsem.at[steps]),
        pltpu.make_async_copy(wide, ings, wsem.at[steps + 1]),
        pltpu.make_async_copy(kernels, kern, wsem.at[steps + 2]),
    ]
    for i, dst in enumerate((bias, gain, move)):
        last.append(pltpu.make_async_copy(small.at[pl.ds(9 + i, 1), :], dst, wsem.at[steps + 3 + i]))
    for copy in last:
        copy.start()
    for copy in writes + last:
        copy.wait()


def finish(out1, out2, act, ing, outs):
    shape = jax.ShapeDtypeStruct
    slot = act.shape
    anywhere = pl.BlockSpec(memory_space=pl.ANY)
    line = (1, D)
    spread = slot[:2] + line
    steps = 16
    return pl.pallas_call(
        finish_kernel,
        out_shape=[
            shape(out1.shape, F32),
            shape(out2.shape, F32),
            shape(slot, BF),
            shape(spread, F32),
            shape((9,) + line, F32),
            shape(line, F32),
            shape(line, F32),
            shape(line, F32),
        ],
        in_specs=[anywhere] * 5,
        out_specs=[anywhere] * 8,
        scratch_shapes=[
            pltpu.VMEM(out1.shape, out1.dtype),
            pltpu.VMEM(out2.shape, out2.dtype),
            pltpu.VMEM(out1.shape, F32),
            pltpu.VMEM(out2.shape, F32),
            pltpu.VMEM(slot, BF),
            pltpu.VMEM(slot, BF),
            pltpu.VMEM(spread, F32),
            pltpu.VMEM(outs.shape, F32),
            pltpu.VMEM((9,) + line, F32),
            pltpu.SemaphoreType.DMA((steps + 3,)),
            pltpu.SemaphoreType.DMA((steps + 6,)),
        ],
        name="finish",
        compiler_params=pltpu.CompilerParams(vmem_limit_bytes=60 * 2**20),
    )(out1, out2, act, ing, outs)


def per_device(
    images, cotangent, window_rows, window_cols, pos_kernel, pos_bias, norm_gain, norm_shift, first_weight, second_weight
):
    act, ing, out1, out2, outs = relay(
        window_rows, window_cols, images[0], cotangent[0], pos_kernel[0], pos_bias, norm_gain, norm_shift,
        first_weight[0], second_weight,
    )
    if lax.axis_size("dp") > RING:
        out1, out2, outs = lax.psum((out1.astype(F32) / RING, out2.astype(F32) / RING, outs / RING), "dp")
    out1, out2, act, ing, kern, bias, gain, move = finish(out1, out2, act, ing, outs)
    return (
        act[None],
        ing.transpose(2, 0, 1, 3),
        out1[None],
        out2,
        kern.transpose(1, 0, 2),
        bias,
        gain,
        move,
    )


def solution(mesh):
    in_specs = (
        P(("dp", "section"), None, None, None),
        P(("dp", "section"), None, None, None),
        P("dp"),
        P("dp"),
        P("section", None, None),
        P("section", None),
        P("section", None),
        P("section", None),
        P("section", None, None),
        P("section", None),
    )
    out_specs = (
        P(("dp", "section"), None, None, None),
        P(("dp", "section"), None, None, None),
        P("section", None, None),
        P("section", None),
        P("section", None, None),
        P("section", None),
        P("section", None),
        P("section", None),
    )
    return jax.shard_map(per_device, mesh=mesh, in_specs=in_specs, out_specs=out_specs, check_vma=False)
```

```python
from functools import partial

import jax
import jax.numpy as jnp
from jax import lax
from jax.experimental import pallas as pl
from jax.experimental.pallas import tpu as pltpu
from jax.sharding import PartitionSpec as P

D = 768
FF = 3072
HEADS = 24
HEAD = 32
WIN = 7
SIDE = 2
GRID = SIDE * WIN
CELL = 8
WROWS = WIN * CELL
HALF = GRID * CELL
ROWS = SIDE * HALF
GROUP = 256
PACK = GROUP // HEAD
NGROUP = D // GROUP
UNITS = NGROUP * SIDE * SIDE
LANE = 128
FTILE = 512
EPS = 1e-05
SCALE = HEAD ** (-0.5)
BF = jnp.bfloat16
F32 = jnp.float32
MESH = pl.DeviceIdType.MESH


def dot(a, b, ca=1, cb=0):
    return lax.dot_general(a, b, (((ca,), (cb,)), ((), ())), preferred_element_type=F32)


def lanes(index, width=LANE):
    return pl.ds(pl.multiple_of(index * width, width), width)


def halves(value):
    return value.reshape(SIDE, GRID, CELL, value.shape[-1])


def shifts(left, right):
    column = lax.broadcasted_iota(jnp.int32, left.shape, 1)
    before0 = pltpu.roll(left, 1, 1)
    after0 = jnp.where(column == WIN - 1, pltpu.roll(right, CELL - 2, 1), pltpu.roll(left, CELL - 1, 1))
    before1 = jnp.where(column == 0, pltpu.roll(left, 2, 1), pltpu.roll(right, 1, 1))
    after1 = pltpu.roll(right, CELL - 1, 1)
    return ((before0, left, after0), (before1, right, after1))


def gelu_parts(h):
    expo = jnp.exp(h * h * -0.5)
    t = 1.0 / (1.0 + (0.3275911 * 0.7071067811865476) * jnp.abs(h))
    poly = t * (0.127414796 + t * (-0.142248368 + t * (0.7107068705 + t * (-0.7265760135 + t * 0.5307027145))))
    tail = poly * expo
    phi = jnp.where(h >= 0, 1.0 - tail, tail)
    return h * phi, phi + h * expo * 0.3989422804014327


def front_forward(sec, m, ubuf, msk, pr, U, C, zz, xh, rs):
    zero = jnp.zeros((ROWS, LANE), F32)

    def conv(i, total):
        ls = lanes(i)
        u = ubuf[sec, m, :, ls].astype(F32)
        masked = halves(u * msk[m])
        U[0, 1 : GRID + 1, :, ls] = masked[0]
        U[1, 1 : GRID + 1, :, ls] = masked[1]
        moved = shifts(U[0, :, :, ls], U[1, :, :, ls])
        taps = pr[sec, :, ls]
        uh = halves(u)
        sums = []
        for wc in range(SIDE):
            acc = uh[wc] + taps[9:10, :][None]
            for a in range(3):
                for b in range(3):
                    acc = acc + moved[wc][b][a : a + GRID] * taps[3 * a + b : 3 * a + b + 1, :][None]
            acc = acc.reshape(HALF, LANE)
            C[pl.ds(wc * HALF, HALF), ls] = acc
            sums.append(acc)
        return total + jnp.concatenate(sums, axis=0)

    mean = jnp.sum(lax.fori_loop(0, D // LANE, conv, zero, unroll=True), axis=-1, keepdims=True) * (1.0 / D)

    def spread(i, total):
        centred = C[:, lanes(i)] - mean
        return total + centred * centred

    var = jnp.sum(lax.fori_loop(0, D // LANE, spread, zero, unroll=True), axis=-1, keepdims=True) * (1.0 / D)
    rstd = lax.rsqrt(var + EPS)
    rs[sec, m] = jnp.broadcast_to(rstd, (ROWS, LANE))

    def norm(i, carry):
        ls = lanes(i)
        xhat = (C[:, ls] - mean) * rstd
        xh[sec, m, :, ls] = xhat.astype(BF)
        zz[m, 2 * sec, :, ls] = (xhat * pr[sec, 10:11, ls] + pr[sec, 11:12, ls]).astype(BF)
        return carry

    lax.fori_loop(0, D // LANE, norm, 0, unroll=True)


def fold(value):
    return jnp.sum(value.reshape(ROWS // CELL, CELL, LANE), axis=0)


def front_backward(sec, m, msk, pr, U, T, gfull, xh, rs, sgp, out, sent):
    zero = jnp.zeros((ROWS, LANE), F32)

    def sums(i, carry):
        s1, s2 = carry
        ls = lanes(i)
        dz = T[:, ls]
        xhat = xh[sec, m, :, ls].astype(F32)
        both = xhat * dz
        sgp[sec, 10, :, ls] += fold(both)
        sgp[sec, 11, :, ls] += fold(dz)
        gain = pr[sec, 10:11, ls]
        return s1 + dz * gain, s2 + both * gain

    s1, s2 = lax.fori_loop(0, D // LANE, sums, (zero, zero), unroll=True)
    m1 = jnp.sum(s1, axis=-1, keepdims=True) * (1.0 / D)
    m2 = jnp.sum(s2, axis=-1, keepdims=True) * (1.0 / D)

    def back(i, carry):
        ls = lanes(i)
        xhat = xh[sec, m, :, ls].astype(F32)
        inner = T[:, ls] * pr[sec, 10:11, ls] - m1 - xhat * m2
        gc = gfull(i)[...].astype(F32) + rs[sec, m] * inner
        xh[sec, m, :, ls] = gc.astype(BF)
        gh = halves(gc)
        U[0, 1 : GRID + 1, :, ls] = gh[0]
        U[1, 1 : GRID + 1, :, ls] = gh[1]
        moved = shifts(U[0, :, :, ls], U[1, :, :, ls])
        taps = pr[sec, :, ls]
        mask = halves(msk[m])
        du = []
        for wc in range(SIDE):
            acc = jnp.zeros((GRID, CELL, LANE), F32)
            for a in range(3):
                for b in range(3):
                    tap = 3 * a + b
                    acc = acc + moved[wc][2 - b][2 - a : 2 - a + GRID] * taps[tap : tap + 1, :][None]
            du.append((gh[wc] + mask[wc] * acc).reshape(HALF, LANE))
        out(i)[...] = jnp.concatenate(du, axis=0).astype(BF)
        return carry

    lax.fori_loop(0, D // LANE // 2, back, 0, unroll=True)
    sent(0)
    lax.fori_loop(D // LANE // 2, D // LANE, back, 0, unroll=True)
    sent(1)


def front_sums(sec, m, ubuf, msk, U, xh, sgp):
    def part(i, carry):
        ls = lanes(i)
        gc = xh[sec, m, :, ls].astype(F32)
        sgp[sec, 9, :, ls] += fold(gc)
        gh = halves(gc)
        U[0, 1 : GRID + 1, :, ls] = gh[0]
        U[1, 1 : GRID + 1, :, ls] = gh[1]
        moved = shifts(U[0, :, :, ls], U[1, :, :, ls])
        um = halves(ubuf[sec, m, :, ls].astype(F32) * msk[m])
        for a in range(3):
            for b in range(3):
                kg = jnp.zeros((CELL, LANE), F32)
                for wc in range(SIDE):
                    kg = kg + jnp.sum(moved[wc][2 - b][2 - a : 2 - a + GRID] * um[wc], axis=0)
                sgp[sec, 3 * a + b, :, ls] += kg
        return carry

    lax.fori_loop(0, D // LANE, part, 0)


def spread_heads(value, head_of_lane):
    parts = [jnp.where(head_of_lane == h, value, 0.0) for h in range(PACK)]
    return jnp.concatenate(parts, axis=0).astype(BF)


def gather_heads(value, rows, head_of_lane):
    out = jnp.zeros((rows, GROUP), F32)
    for h in range(PACK):
        out = jnp.where(head_of_lane == h, value[h * rows : (h + 1) * rows], out)
    return out


def unit_slices(unit):
    pair, group = unit // NGROUP, lax.rem(unit, NGROUP)
    rows = [pl.ds(pl.multiple_of((2 * pair + w) * WROWS, 8), WROWS) for w in range(2)]
    cols = [pl.ds(pl.multiple_of(part * D + group * GROUP, LANE), GROUP) for part in range(3)]
    return rows, cols


def window_parts(m, i, qkv):
    rows, cols = unit_slices(i)
    head_of_lane = lax.broadcasted_iota(jnp.int32, (WROWS, GROUP), 1) // HEAD
    q = [qkv[m, r, cols[0]].astype(BF) for r in rows]
    kd = [spread_heads(qkv[m, r, cols[1]], head_of_lane) for r in rows]
    vd = [spread_heads(qkv[m, r, cols[2]], head_of_lane) for r in rows]
    return rows, cols, head_of_lane, q, kd, vd


def window_forward(m, qkv, pw, T):
    def unit(i, carry):
        rows, cols, head_of_lane, q, kd, vd = window_parts(m, i, qkv)
        s = [(dot(b, a, 1, 1) * SCALE).reshape(PACK, WROWS, WROWS) for a, b in zip(q, kd)]
        key = lax.broadcasted_iota(jnp.int32, s[0].shape, 1)
        real = lax.rem(key, CELL) < WIN
        s = [jnp.where(real, x, -1e30) for x in s]
        p = [jnp.exp(x - jnp.max(x, axis=1, keepdims=True)) for x in s]
        p = [x * (1.0 / jnp.sum(x, axis=1, keepdims=True)) for x in p]
        p = [x.reshape(PACK * WROWS, WROWS) for x in p]
        for w in range(2):
            pw[m, 2 * i + w, :, 0:WROWS] = p[w]
        out = [dot(x.astype(BF), v, 0, 0) for x, v in zip(p, vd)]
        for w in range(2):
            T[rows[w], cols[0]] = out[w]
        return carry

    lax.fori_loop(0, UNITS // 2, unit, 0, unroll=2)


def window_backward(m, qkv, pw, T):
    def unit(i, carry):
        rows, cols, head_of_lane, q, kd, vd = window_parts(m, i, qkv)
        g = [T[r, cols[0]].astype(BF) for r in rows]
        p = [pw[m, 2 * i + w, :, 0:WROWS].reshape(PACK, WROWS, WROWS) for w in range(2)]
        dp = [dot(v, x, 1, 1).reshape(PACK, WROWS, WROWS) for v, x in zip(vd, g)]
        ds = [x * (y - jnp.sum(x * y, axis=1, keepdims=True)) for x, y in zip(p, dp)]
        ds = [x.reshape(PACK * WROWS, WROWS).astype(BF) for x in ds]
        pb = [x.reshape(PACK * WROWS, WROWS).astype(BF) for x in p]
        dv = [gather_heads(dot(x, y), WROWS, head_of_lane) for x, y in zip(pb, g)]
        dk = [gather_heads(dot(x, y), WROWS, head_of_lane) * SCALE for x, y in zip(ds, q)]
        dq = [dot(x, y, 0, 0) * SCALE for x, y in zip(ds, kd)]
        for w in range(2):
            qkv[m, rows[w], cols[0]] = dq[w]
            qkv[m, rows[w], cols[1]] = dk[w]
            qkv[m, rows[w], cols[2]] = dv[w]
        return carry

    lax.fori_loop(0, UNITS // 2, unit, 0)


def group_slices(group):
    return [pl.ds(pl.multiple_of(part * D + group * GROUP, LANE), GROUP) for part in range(3)]


def channel_forward(m, qkv, pw, zz, msk):
    def unit(i, carry):
        cols = group_slices(i)
        mask = msk[m][:, :1]
        q = qkv[m, :, cols[0]].astype(BF)
        k = (qkv[m, :, cols[1]] * mask).astype(BF)
        v = qkv[m, :, cols[2]].astype(BF)
        s = dot(q, k, 0, 0) * SCALE
        same = (lax.broadcasted_iota(jnp.int32, s.shape, 0) // HEAD) == (lax.broadcasted_iota(jnp.int32, s.shape, 1) // HEAD)
        s = jnp.where(same, s, -1e30)
        p = jnp.exp(s - jnp.max(s, axis=1, keepdims=True))
        p = p * (1.0 / jnp.sum(p, axis=1, keepdims=True))
        for k in range(GROUP // LANE):
            pw[m, 2 * i + k, 0:GROUP, :] = p[:, k * LANE : (k + 1) * LANE]
        zz[m, 1, :, cols[0]] = dot(v, p.astype(BF), 1, 1).astype(BF)
        return carry

    lax.fori_loop(0, NGROUP, unit, 0, unroll=True)


def channel_backward(m, qkv, pw, T, rr, msk):
    def unit(i, carry):
        cols = group_slices(i)
        mask = msk[m][:, :1]
        q = qkv[m, :, cols[0]].astype(BF)
        k = (qkv[m, :, cols[1]] * mask).astype(BF)
        v = qkv[m, :, cols[2]].astype(BF)
        g = T[:, cols[0]].astype(BF)
        p = jnp.concatenate([pw[m, 2 * i + k, 0:GROUP, :] for k in range(GROUP // LANE)], axis=1)
        dp = dot(g, v, 0, 0)
        ds = (p * (dp - jnp.sum(p * dp, axis=1, keepdims=True))).astype(BF)
        rr[m, 0, :, cols[0]] = (dot(k, ds, 1, 1) * SCALE).astype(BF)
        rr[m, 0, :, cols[1]] = (dot(q, ds) * (SCALE * mask)).astype(BF)
        rr[m, 0, :, cols[2]] = (dot(g, p.astype(BF))).astype(BF)
        return carry

    lax.fori_loop(0, NGROUP, unit, 0, unroll=True)


RING = 8
COLS = FF // RING
WIDE = FF // 12 * 8 // RING
REST = FF // 3 // RING
THIRD = FF // 3 * 2
LENT = RING * 3 // 4
EARLY = 2


def relay_kernel(
    wrows, wcols, img, cot, kern, bias, gain, move, first, second,
    act, ing, out1, out2, outs,
    wf, w2, pr, msk, flat, ubuf, gin, gout, zz, xh, rs, qkv, ab, rr, pw, U, C, T, sgp, sgs, sgm,
    rL, rR, rA, rG, xA, xG, buf, acc, got,
    wl, ws, wr, pl_, usem, gsem, us, gs, ss, rsem, es, er, sgsem, ssem, rcem, osem, sms, smr, xs, xr, ys, yr, bs, br, hs, hr, free,
):
    n = RING
    s = lax.axis_index("section")
    dp = lax.axis_index("dp")
    stage, c = s // 2, lax.rem(s, 2)
    mate = (dp, stage * 2 + (1 - c))
    opposite = (dp, (1 - stage) * 2 + c)
    diagonal = (dp, 3 - s)
    lender, helper = s == 1, s == 2
    early = stage == 0

    spot = lax.rem(dp, n)
    base = dp - spot
    me = jnp.where(lax.rem(spot, 2) == 0, spot // 2, n - 1 - spot // 2)

    def place(pos):
        pos = lax.rem(pos + 2 * n, n)
        return (base + jnp.where(pos < n // 2, 2 * pos, 2 * (n - 1 - pos) + 1), s)

    nexts = (place(me + 1), place(me - 1))
    rounds = n.bit_length() - 1
    partners = []
    for r in range(rounds):
        bit = 1 << r
        partners.append((jnp.where(lax.rem(spot // bit, 2) == 0, dp + bit, dp - bit), s))

    barrier = pltpu.get_barrier_semaphore()
    peers = [mate, opposite, diagonal, *nexts, *partners]
    for peer in peers:
        pl.semaphore_signal(barrier, inc=1, device_id=peer, device_id_type=MESH)
    pl.semaphore_wait(barrier, len(peers))

    def remote(src, dst, send, recv, peer):
        return pltpu.make_async_remote_copy(
            src_ref=src, dst_ref=dst, send_sem=send, recv_sem=recv, device_id=peer, device_id_type=MESH
        )

    half = second.shape[0]

    def weight_parts(k):
        parts = []
        for i in range(4):
            parts.append((first.at[:, pl.ds(i * D, D)], wf.at[k, :, pl.ds(i * D, D)]))
        parts.append((second, w2.at[pl.ds(k * half, half), :]))
        return parts

    def weight_copies(k):
        local = [pltpu.make_async_copy(a, b, wl.at[i]) for i, (a, b) in enumerate(weight_parts(k))]
        sent = [remote(a, b, ws.at[i], wr.at[i], mate) for i, (a, b) in enumerate(weight_parts(k))]
        return local, sent

    def params_copy(k):
        return remote(pr.at[k], pr.at[k], ws.at[5], wr.at[5], mate)

    pr[c, 0:9, :] = kern[...].astype(F32)
    pr[c, 9:10, :] = bias[...].astype(F32)
    pr[c, 10:11, :] = gain[...].astype(F32)
    pr[c, 11:12, :] = move[...].astype(F32)
    params_copy(c).start()
    for k in range(2):

        @pl.when(c == k)
        def _():
            local, sent = weight_copies(k)
            for i in range(5):
                local[i].start()
                sent[i].start()

    def wait_weight(k, i):
        if i < 5:

            @pl.when(c == k)
            def _():
                weight_copies(k)[0][i].wait()

        @pl.when(c != k)
        def _():
            (weight_copies(k)[1][i] if i < 5 else params_copy(k)).wait_recv()

    raw = flat.at[0]
    img_out = remote(img, raw, pl_.at[0], pl_.at[1], opposite)
    cot_out = remote(cot, raw, pl_.at[0], pl_.at[1], opposite)

    def pad(src, dst):
        blank = jnp.zeros((CELL - WIN, D), F32)
        for r in range(GRID):
            line = src[r].astype(F32)
            for wc in range(SIDE):
                cells = jnp.concatenate([line[wc * WIN : (wc + 1) * WIN], blank], axis=0)
                C[pl.ds(wc * HALF + r * CELL, CELL), :] = cells
        dst[...] = C[...].astype(BF)

    def unpad(dst):
        for r in range(GRID):
            sides = [C[pl.ds(wc * HALF + r * CELL, CELL), :][:WIN] for wc in range(SIDE)]
            dst[r] = jnp.concatenate(sides, axis=0).astype(BF)

    @pl.when(early)
    def _():
        cot_out.start()
        pad(img, ubuf.at[0, 0])

    @pl.when(jnp.logical_not(early))
    def _():
        img_out.start()
        pad(cot, gin.at[1])

    index = lax.broadcasted_iota(jnp.int32, (ROWS, LANE), 0)
    cell = lax.rem(index, CELL)
    row = lax.rem(index, HALF) // CELL
    column = (index // HALF) * WIN + cell
    for m in range(2):
        inside = (row < WIN * wrows[c + 2 * m]) & (column < WIN * wcols[c + 2 * m]) & (cell < WIN)
        msk[m] = jnp.where(inside, 1.0, 0.0)

    @pl.when(jnp.logical_not(early))
    def _():
        cot_out.wait_recv()
        pad(raw, gin.at[0])
        for m in range(2):
            for l in range(D // LANE):
                cols = pl.ds(l * LANE, LANE)
                gin[m, :, cols] = (gin[m, :, cols].astype(F32) * msk[m]).astype(BF)

    for wc in range(SIDE):
        U[wc, 0] = jnp.zeros((CELL, D), F32)
        U[wc, GRID + 1] = jnp.zeros((CELL, D), F32)
    sgp[...] = jnp.zeros(sgp.shape, F32)

    def hop(m, dst, send, recv):
        sides = [pl.ds(i * D // 2, D // 2) for i in range(2)]
        return [
            remote(gout.at[m, :, cols], dst.at[:, cols], send.at[m, i], recv.at[m, i], opposite)
            for i, cols in enumerate(sides)
        ]

    def u_hop(m):
        return hop(m, ubuf.at[0, m], us, usem)

    def g_hop(m):
        return hop(m, gin.at[m], gs, gsem)

    def factor_copies(k, m):
        if k == 0:
            parts = [
                ("F0", zz.at[m, 0], rL.at[m, 0]),
                ("F1", zz.at[m, 1], rL.at[m, 1]),
                ("G", rr.at[m, 0, :, pl.ds(3 * D, D)], rR.at[m, :, pl.ds(3 * D, D)]),
                ("A", rr.at[m, 0, :, pl.ds(0, 3 * D)], rR.at[m, :, pl.ds(0, 3 * D)]),
            ]
        else:
            parts = [
                ("F2", zz.at[m, 2], rL.at[m, 0]),
                ("M", gin.at[m], rG.at[m]),
            ]
            for i in range(3):
                cols = pl.ds(i * (FF // 3), FF // 3)
                parts.append((f"X{i}", ab.at[m, :, cols], rA.at[m, :, cols]))
                parts.append((f"H{i}", rr.at[m, 1, :, cols], rR.at[m, :, cols]))
        return [(w, remote(a, b, ss.at[m, i], rsem.at[m, i], mate)) for i, (w, a, b) in enumerate(parts)]

    def start_factors(m, which):
        for k in range(2):

            @pl.when(c != k)
            def _():
                for when, copy in factor_copies(k, m):
                    if when == which:
                        copy.start()

    def wait_factors(which):
        for k in range(2):

            @pl.when(c == k)
            def _():
                for m in range(2):
                    for when, copy in factor_copies(k, m):
                        if when[0] in which:
                            copy.wait_recv()

    def shard(k):
        return lax.rem(k + 4 * n, n)

    def sign(h):
        return 1 if h == 0 else -1

    def home(h, t):
        return shard(me + sign(h) - sign(h) * t)

    def products(terms):
        total = None
        for a, b in terms:
            part = dot(a[...], b[...], 0, 0)
            total = part if total is None else total + part
        return total

    def tile(sub, h, j):
        side = pl.ds(h * COLS, COLS)
        if sub in (0, 4):
            rows = first_rows(sub, h)
            last = jnp.where(j >= (3 * n) // 4, 1, 0)
            own = jnp.where(c == 1, 2, last)
            other = jnp.where(c == 1, 0, last)
            cols = lanes(j, COLS)
            terms = [(zz.at[m, own, :, rows], rr.at[m, c, :, cols]) for m in range(2)]
            terms += [(rL.at[m, other, :, rows], rR.at[m, :, cols]) for m in range(2)]
        elif sub == 3:
            cols = lanes(j, REST)
            terms = [(xA.at[m, :, cols], xG.at[m, :, side]) for m in range(2)]
            terms += [(xA.at[2 + m, :, cols], gout.at[m, :, side]) for m in range(2)]
        else:
            cols = lanes(j, WIDE) if sub == 1 else pl.ds(pl.multiple_of(THIRD + j * REST, LANE), REST)
            terms = [(ab.at[m, :, cols], gin.at[m, :, side]) for m in range(2)]
            terms += [(rA.at[m, :, cols], rG.at[m, :, side]) for m in range(2)]
        return products(terms)

    sizes = (COLS // 3 * 2, WIDE, REST, REST, COLS // 3)
    starts = (0, COLS, COLS + WIDE, COLS + WIDE, COLS // 3 * 2)
    parts = [pl.ds(start, size) for start, size in zip(starts, sizes)]
    subs = range(len(sizes))
    odd = c == 1
    active = (None, odd, odd, helper, None)

    def where_live(sub, j, run):
        if sub == 2:
            pl.when(jnp.logical_not(lender) | (j >= LENT))(run)
        elif sub == 3:
            pl.when(j < LENT)(run)
        else:
            run()

    def first_rows(sub, h):
        return pl.ds(h * COLS + (0 if sub == 0 else sizes[0]), sizes[sub])

    def where_active(sub, run):
        if active[sub] is None:
            run()
        else:
            pl.when(active[sub])(run)


    def gathered(sub, h, j):
        if sub in (0, 4):
            return wf.at[0, first_rows(sub, h), lanes(j, COLS)]
        first_row = 0 if sub == 1 else THIRD
        return w2.at[pl.ds(pl.multiple_of(first_row + j * sizes[sub], 16), sizes[sub]), pl.ds(h * COLS, COLS)]

    def scatter(h, t, sub):
        src, dst = buf.at[h, t, parts[sub], :], buf.at[h, t + 1, parts[sub], :]
        return remote(src, dst, ssem.at[h, t, sub], rcem.at[h, t + 1, sub], nexts[h])

    def spread(h, t, sub, j):
        ref = gathered(sub, h, j)
        return remote(ref, ref, ssem.at[h, n - 1 + t, sub], rcem.at[h, n + t, sub], nexts[h])

    half_shards = n * 3 // 4

    def write(h, j, sub):
        src, side = gathered(sub, h, j), pl.ds(h * COLS, COLS)
        if sub in (0, 4):
            dst = out1.at[first_rows(sub, h), lanes(j, COLS)]
        elif sub == 1:
            dst = out2.at[pl.ds(pl.multiple_of((j - half_shards) * WIDE, 16), WIDE), side]
        else:
            dst = out2.at[pl.ds(pl.multiple_of(THIRD - FF // 2 + j * REST, 16), REST), side]
        if sub == 3:
            return remote(src, dst, bs.at[h, j], br.at[h, j], diagonal)
        return pltpu.make_async_copy(src, dst, osem.at[h, j, sub])

    def hand_over(h, j):
        dst = out2.at[pl.ds(pl.multiple_of(j * WIDE, 16), WIDE), pl.ds(h * COLS, COLS)]
        return remote(gathered(1, h, j), dst, hs.at[h, j], hr.at[h, j], mate)

    def deliver(h, j, sub):
        if sub == 1:

            @pl.when(j < half_shards)
            def _():
                hand_over(h, j).start()

            @pl.when(j >= half_shards)
            def _():
                write(h, j, sub).start()

        else:
            write(h, j, sub).start()

    def lend(m):
        cols = pl.ds(THIRD, LENT * REST)
        return (
            remote(ab.at[m, :, cols], xA.at[m], xs.at[m], xr.at[m], diagonal),
            remote(rA.at[m, :, cols], xA.at[2 + m], xs.at[2 + m], xr.at[2 + m], diagonal),
        )

    def share(m):
        return remote(gout.at[m], xG.at[m], ys.at[m], yr.at[m], mate)

    def reduce_event(sub, h, e):
        j = shard(me - sign(h) * e)

        @pl.when(e == n - 1)
        def _():
            pl.semaphore_wait(free.at[h, sub], 1)

        def run():
            total = tile(sub, h, j)

            @pl.when(e == 0)
            def _():
                buf[h, 0, parts[sub], :] = total.astype(BF)
                scatter(h, 0, sub).start()

            @pl.when((e > 0) & (e < n - 1))
            def _():
                scatter(h, e - 1, sub).wait_recv()
                buf[h, e, parts[sub], :] = (total + buf[h, e, parts[sub], :].astype(F32)).astype(BF)
                scatter(h, e, sub).start()

            @pl.when(e == n - 1)
            def _():
                scatter(h, n - 2, sub).wait_recv()
                gathered(sub, h, j)[...] = (total + buf[h, n - 1, parts[sub], :].astype(F32)).astype(BF)
                spread(h, 0, sub, j).start()
                deliver(h, j, sub)

        where_live(sub, j, run)

    def event(sub, e):
        for h in range(2):

            @pl.when(e < n)
            def _():
                reduce_event(sub, h, e)

            @pl.when((e >= n) & (e < 2 * n - 1))
            def _():
                t = e - (n - 1)
                j = home(h, t)

                def run():
                    spread(h, t - 1, sub, j).wait_recv()

                    @pl.when(t < n - 1)
                    def _():
                        spread(h, t, sub, j).start()

                    deliver(h, j, sub)

                where_live(sub, j, run)

    def early_event(e, which):
        @pl.when(odd)
        def _():
            for sub in which:
                where_active(sub, lambda: event(sub, e))

    def small(r):
        return remote(acc.at[r], got.at[r], sms.at[r], smr.at[r], partners[r])

    def forward(m, p):
        @pl.when(jnp.logical_not(early))
        def _():
            for copy in u_hop(m):
                copy.wait_recv()

        @pl.when(early & (m == 1))
        def _():
            img_out.wait_recv()
            pad(raw, ubuf.at[0, 1])

        once = p == 0

        def first_time(k, i):
            @pl.when(once)
            def _():
                wait_weight(k, i)

        first_time(0, 5)
        front_forward(0, m, ubuf, msk, pr, U, C, zz, xh, rs)
        start_factors(m, "F0")
        for i in range(3):
            first_time(0, i)
            qkv[m, :, pl.ds(i * D, D)] = dot(zz[m, 0], wf[0, :, pl.ds(i * D, D)])

        @pl.when(early)
        def _():
            window_forward(m, qkv, pw, T)
            zz[m, 1] = T[...].astype(BF)

        @pl.when(jnp.logical_not(early))
        def _():
            channel_forward(m, qkv, pw, zz, msk)

        start_factors(m, "F1")
        first_time(0, 3)
        ubuf[1, m] = (C[...] + dot(zz[m, 1], wf[0, :, pl.ds(3 * D, D)])).astype(BF)

        first_time(1, 5)
        front_forward(1, m, ubuf, msk, pr, U, C, zz, xh, rs)
        start_factors(m, "F2")
        for i in range(4):
            first_time(1, i)
        first_time(0, 4)
        first_time(1, 4)

        total, before = C[...], None
        for t in range(FF // FTILE):
            cols = pl.ds(t * FTILE, FTILE)
            h = dot(zz[m, 2], wf[1, :, cols])
            if t > 0:
                total = total + dot(before, w2[pl.ds((t - 1) * FTILE, FTILE), :])
            a, d = gelu_parts(h)
            before = a.astype(BF)
            ab[m, :, cols] = before
            rr[m, 1, :, cols] = d.astype(BF)
            if t % 2 == 1:
                start_factors(m, f"X{t // 2}")
        for i in range(2):
            cols = pl.ds(i * D // 2, D // 2)
            part = total[:, i * D // 2 : (i + 1) * D // 2]
            gout[m, :, cols] = (part + dot(before, w2[pl.ds(FF - FTILE, FTILE), cols])).astype(BF)

            @pl.when(early)
            def _():
                u_hop(m)[i].start()


        @pl.when(jnp.logical_not(early))
        def _():
            for l in range(D // LANE):
                cols = pl.ds(l * LANE, LANE)
                C[:, cols] = gout[m, :, cols].astype(F32) * msk[m]
            unpad(flat.at[m])

        @pl.when(jnp.logical_not(early) & (m == 0))
        def _():
            remote(flat.at[0], act, es.at[0], er.at[0], opposite).start()

        @pl.when(jnp.logical_not(early) & (m == 1))
        def _():
            pltpu.make_async_copy(flat.at[1], act, es.at[0]).start()

        @pl.when(early & (m == 1))
        def _():
            wait_factors("FX")

        @pl.when(lender & (m == 1))
        def _():
            for i in range(2):
                for copy in lend(i):
                    copy.start()

    def backward(m):
        @pl.when(early)
        def _():
            for copy in g_hop(m):
                copy.wait_recv()

        start_factors(m, "M")
        for t in range(FF // FTILE):
            cols = pl.ds(t * FTILE, FTILE)
            da = dot(gin[m], w2[cols, :], 1, 1)
            rr[m, 1, :, cols] = (da * rr[m, 1, :, cols].astype(F32)).astype(BF)
            if t % 2 == 1:
                start_factors(m, f"H{t // 2}")

        @pl.when(m == 1)
        def _():
            @pl.when(jnp.logical_not(early))
            def _():
                wait_factors("FX")

            wait_factors("M")
            early_event(0, (1, 2))

        T[...] = dot(rr[m, 1], wf[1], 1, 1)

        @pl.when(m == 1)
        def _():
            wait_factors("H")
            early_event(0, (0, 4))

        last = pl.ds(3 * D, D)

        @pl.when(early)
        def _():
            for copy in u_hop(m):
                copy.wait_send()

        def tail_lanes(i):
            return rr.at[m, 0, :, pl.ds(pl.multiple_of(3 * D + i * LANE, LANE), LANE)]

        def nothing(half):
            pass

        front_backward(1, m, msk, pr, U, T, lambda i: gin.at[m, :, lanes(i)], xh, rs, sgp, tail_lanes, nothing)
        start_factors(m, "G")

        T[...] = dot(rr[m, 0, :, last], wf[0, :, last], 1, 1)

        @pl.when(early)
        def _():
            window_backward(m, qkv, pw, T)
            for i in range(3):
                cols = pl.ds(i * D, D)
                rr[m, 0, :, cols] = qkv[m, :, cols].astype(BF)

        @pl.when(jnp.logical_not(early))
        def _():
            channel_backward(m, qkv, pw, T, rr, msk)

        start_factors(m, "A")

        @pl.when(m == 1)
        def _():
            for e in range(1, EARLY):
                early_event(e, (1, 2, 0, 4))

        T[...] = dot(rr[m, 0, :, pl.ds(0, 3 * D)], wf[0, :, pl.ds(0, 3 * D)], 1, 1)
        def send_half(half):
            @pl.when(jnp.logical_not(early))
            def _():
                g_hop(m)[half].start()

        front_backward(
            0, m, msk, pr, U, T, tail_lanes, xh, rs, sgp, lambda i: gout.at[m, :, lanes(i)], send_half
        )

        @pl.when(s == 3)
        def _():
            share(m).start()

        @pl.when(early)
        def _():
            C[...] = gout[m].astype(F32)
            unpad(flat.at[m])

        @pl.when(early & (m == 0))
        def _():
            pltpu.make_async_copy(flat.at[0], ing, es.at[1]).start()

        @pl.when(early & (m == 1))
        def _():
            remote(flat.at[1], ing, es.at[1], er.at[1], opposite).start()

    def phase(p, carry):
        m = jnp.where(early, lax.rem(p, 2), p // 2)
        ahead = jnp.where(early, p < 2, lax.rem(p, 2) == 0)

        @pl.when(ahead)
        def _():
            forward(m, p)

        @pl.when(jnp.logical_not(ahead))
        def _():
            backward(m)

        return carry

    lax.fori_loop(0, 4, phase, 0)

    for h in range(2):
        for sub in subs:

            def ready():
                pl.semaphore_signal(free.at[h, sub], inc=1, device_id=nexts[1 - h], device_id_type=MESH)

            where_active(sub, ready)

    give = remote(sgs.at[1 - c], sgm, sgsem.at[0], sgsem.at[1], mate)

    def small_sums():
        for sec in range(2):
            for j in range(12):
                sgs[sec, j : j + 1, :] = jnp.sum(sgp[sec, j], axis=0, keepdims=True)
            sgs[sec, 12:16, :] = jnp.zeros((4, D), F32)
        give.start()

    wait_factors("GA")

    @pl.when(helper)
    def _():
        for m in range(2):
            for copy in lend(m):
                copy.wait_recv()
            share(m).wait_recv()

    def ring_step(t, carry):
        for sub in (0, 4):
            event(sub, t + jnp.where(odd, EARLY, 0))
        where_active(1, lambda: event(1, t + EARLY))
        where_active(2, lambda: event(2, t + EARLY))
        where_active(3, lambda: event(3, t))
        @pl.when((t >= 1) & (t < 5))
        def _():
            front_sums((t - 1) // 2, lax.rem(t - 1, 2), ubuf, msk, U, xh, sgp)

        pl.when(t == 5)(small_sums)
        for r in range(rounds + 1):

            @pl.when(t == 6 + 2 * r)
            def _():
                if r == 0:
                    give.wait_recv()
                    acc[0] = sgs[c] + sgm[...]
                else:
                    small(r - 1).wait_recv()
                    acc[r] = acc[r - 1] + got[r - 1]
                if r < rounds:
                    small(r).start()

        return carry

    lax.fori_loop(0, 2 * n - 1, ring_step, 0)
    outs[...] = acc[rounds]

    for k in range(2):

        @pl.when(c == k)
        def _():
            for copy in weight_copies(k)[1]:
                copy.wait_send()
            params_copy(k).wait_send()
            for m in range(2):
                for _when, copy in factor_copies(1 - k, m):
                    copy.wait_send()

    give.wait_send()
    for r in range(rounds):
        small(r).wait_send()

    def drain(t, carry):
        for h in range(2):
            for sub in subs:

                def sent():
                    where_live(sub, shard(me - sign(h) * t), lambda: scatter(h, t, sub).wait_send())
                    where_live(sub, home(h, t), lambda: spread(h, t, sub, home(h, t)).wait_send())

                where_active(sub, sent)

        return carry

    lax.fori_loop(0, n - 1, drain, 0)

    def written(j, carry):
        for h in range(2):
            write(h, j, 0).wait()
            write(h, j, 4).wait()

            @pl.when(odd)
            def _():
                where_live(2, j, lambda: write(h, j, 2).wait())

                @pl.when(j < half_shards)
                def _():
                    hand_over(h, j).wait_send()

                @pl.when(j >= half_shards)
                def _():
                    write(h, j, 1).wait()

            @pl.when(jnp.logical_not(odd) & (j < half_shards))
            def _():
                hand_over(h, j).wait_recv()

            @pl.when(helper & (j < LENT))
            def _():
                write(h, j, 3).wait_send()

            @pl.when(lender & (j < LENT))
            def _():
                write(h, j, 3).wait_recv()

        return carry

    lax.fori_loop(0, n, written, 0)

    @pl.when(lender)
    def _():
        for m in range(2):
            for copy in lend(m):
                copy.wait_send()

    @pl.when(s == 3)
    def _():
        for m in range(2):
            share(m).wait_send()

    @pl.when(early)
    def _():
        cot_out.wait_send()
        pltpu.make_async_copy(flat.at[0], ing, es.at[1]).wait()
        remote(flat.at[1], ing, es.at[1], er.at[1], opposite).wait_send()
        remote(flat.at[0], act, es.at[0], er.at[0], opposite).wait_recv()

    @pl.when(jnp.logical_not(early))
    def _():
        img_out.wait_send()
        for m in range(2):
            for copy in g_hop(m):
                copy.wait_send()
        remote(flat.at[0], act, es.at[0], er.at[0], opposite).wait_send()
        pltpu.make_async_copy(flat.at[1], act, es.at[0]).wait()
        remote(flat.at[1], ing, es.at[1], er.at[1], opposite).wait_recv()


def relay(wrows, wcols, img, cot, kern, bias, gain, move, first, second):
    shape = jax.ShapeDtypeStruct
    vmem = pl.BlockSpec(memory_space=pltpu.VMEM)
    anywhere = pl.BlockSpec(memory_space=pl.ANY)
    dma = pltpu.SemaphoreType.DMA
    smem = pl.BlockSpec(memory_space=pltpu.SMEM)
    image = (ROWS, D)
    slot = img.shape
    rounds = RING.bit_length() - 1
    return pl.pallas_call(
        relay_kernel,
        out_shape=[
            shape(slot, BF),
            shape(slot, BF),
            shape((D, FF), BF),
            shape((FF // 2, D), BF),
            shape((16, D), F32),
        ],
        in_specs=[smem] * 2 + [vmem] * 6 + [anywhere] * 2,
        out_specs=[anywhere] * 4 + [vmem],
        scratch_shapes=[
            pltpu.VMEM((2, D, FF), BF),
            pltpu.VMEM((FF, D), BF),
            pltpu.VMEM((2, 16, D), F32),
            pltpu.VMEM((2, ROWS, LANE), F32),
            pltpu.VMEM((2,) + slot, BF),
            pltpu.VMEM((2, 2) + image, BF),
            pltpu.VMEM((2,) + image, BF),
            pltpu.VMEM((2,) + image, BF),
            pltpu.VMEM((2, 3) + image, BF),
            pltpu.VMEM((2, 2) + image, BF),
            pltpu.VMEM((2, 2, ROWS, LANE), F32),
            pltpu.VMEM((2, ROWS, 3 * D), F32),
            pltpu.VMEM((2, ROWS, FF), BF),
            pltpu.VMEM((2, 2, ROWS, FF), BF),
            pltpu.VMEM((2, UNITS, PACK * WROWS, LANE), F32),
            pltpu.VMEM((SIDE, GRID + 2, CELL, D), F32),
            pltpu.VMEM(image, F32),
            pltpu.VMEM(image, F32),
            pltpu.VMEM((2, 12, CELL, D), F32),
            pltpu.VMEM((2, 16, D), F32),
            pltpu.VMEM((16, D), F32),
            pltpu.VMEM((2, 2) + image, BF),
            pltpu.VMEM((2, ROWS, FF), BF),
            pltpu.VMEM((2, ROWS, FF), BF),
            pltpu.VMEM((2,) + image, BF),
            pltpu.VMEM((4, ROWS, LENT * REST), BF),
            pltpu.VMEM((2,) + image, BF),
            pltpu.VMEM((2, RING, COLS + WIDE + REST, COLS), BF),
            pltpu.VMEM((rounds + 1, 16, D), F32),
            pltpu.VMEM((rounds, 16, D), F32),
            dma((5,)),
            dma((6,)),
            dma((6,)),
            dma((2,)),
            dma((2, 2)),
            dma((2, 2)),
            dma((2, 2)),
            dma((2, 2)),
            dma((2, 8)),
            dma((2, 8)),
            dma((2,)),
            dma((2,)),
            dma((2,)),
            dma((2, 2 * RING, 5)),
            dma((2, 2 * RING, 5)),
            dma((2, RING, 5)),
            dma((rounds,)),
            dma((rounds,)),
            dma((4,)),
            dma((4,)),
            dma((2,)),
            dma((2,)),
            dma((2, RING)),
            dma((2, RING)),
            dma((2, RING)),
            dma((2, RING)),
            pltpu.SemaphoreType.REGULAR((2, 5)),
        ],
        name="relay",
        compiler_params=pltpu.CompilerParams(
            collective_id=1, has_side_effects=True, vmem_limit_bytes=63 * 2**20
        ),
    )(wrows, wcols, img, cot, kern, bias, gain, move, first, second)


def finish_kernel(
    out1, out2, act, ing, outs, first, second, acts, ings, kern, bias, gain, move,
    raw1, raw2, full1, full2, acted, graded, wide, small, kernels, rsem, wsem,
):
    steps = rsem.shape[0] - 3

    loads = [
        pltpu.make_async_copy(act, acted, rsem.at[steps]),
        pltpu.make_async_copy(ing, graded, rsem.at[steps + 1]),
        pltpu.make_async_copy(outs, small, rsem.at[steps + 2]),
    ]
    for copy in loads:
        copy.start()
    reads, writes = [], []
    for i in range(steps):
        pair = ((out1, raw1, full1, first), (out2, raw2, full2, second))[i % 2]
        src, raw, full, dst = pair
        half = steps // 2
        rows = pl.ds(i // 2 * (src.shape[0] // half), src.shape[0] // half)
        reads.append((pltpu.make_async_copy(src.at[rows, :], raw.at[rows, :], rsem.at[i]), raw, full, rows))
        writes.append(pltpu.make_async_copy(full.at[rows, :], dst.at[rows, :], wsem.at[i]))
    for copy, *_ in reads:
        copy.start()
    for (copy, raw, full, rows), back in zip(reads, writes):
        copy.wait()
        full[rows, :] = raw[rows, :].astype(F32)
        back.start()
    for copy in loads:
        copy.wait()
    for k in range(9):
        kernels[k] = small[k : k + 1, :]
    for r in range(GRID):
        line = graded[r].astype(F32)
        for k in range(GRID):
            wide[r, k] = line[k : k + 1, :]
    last = [
        pltpu.make_async_copy(acted, acts, wsem.at[steps]),
        pltpu.make_async_copy(wide, ings, wsem.at[steps + 1]),
        pltpu.make_async_copy(kernels, kern, wsem.at[steps + 2]),
    ]
    for i, dst in enumerate((bias, gain, move)):
        last.append(pltpu.make_async_copy(small.at[pl.ds(9 + i, 1), :], dst, wsem.at[steps + 3 + i]))
    for copy in last:
        copy.start()
    for copy in writes + last:
        copy.wait()


def finish(out1, out2, act, ing, outs):
    shape = jax.ShapeDtypeStruct
    slot = act.shape
    anywhere = pl.BlockSpec(memory_space=pl.ANY)
    line = (1, D)
    spread = slot[:2] + line
    steps = 16
    return pl.pallas_call(
        finish_kernel,
        out_shape=[
            shape(out1.shape, F32),
            shape(out2.shape, F32),
            shape(slot, BF),
            shape(spread, F32),
            shape((9,) + line, F32),
            shape(line, F32),
            shape(line, F32),
            shape(line, F32),
        ],
        in_specs=[anywhere] * 5,
        out_specs=[anywhere] * 8,
        scratch_shapes=[
            pltpu.VMEM(out1.shape, out1.dtype),
            pltpu.VMEM(out2.shape, out2.dtype),
            pltpu.VMEM(out1.shape, F32),
            pltpu.VMEM(out2.shape, F32),
            pltpu.VMEM(slot, BF),
            pltpu.VMEM(slot, BF),
            pltpu.VMEM(spread, F32),
            pltpu.VMEM(outs.shape, F32),
            pltpu.VMEM((9,) + line, F32),
            pltpu.SemaphoreType.DMA((steps + 3,)),
            pltpu.SemaphoreType.DMA((steps + 6,)),
        ],
        name="finish",
        compiler_params=pltpu.CompilerParams(vmem_limit_bytes=60 * 2**20),
    )(out1, out2, act, ing, outs)


def per_device(
    images, cotangent, window_rows, window_cols, pos_kernel, pos_bias, norm_gain, norm_shift, first_weight, second_weight
):
    act, ing, out1, out2, outs = relay(
        window_rows, window_cols, images[0], cotangent[0], pos_kernel[0], pos_bias, norm_gain, norm_shift,
        first_weight[0], second_weight,
    )
    if lax.axis_size("dp") > RING:
        out1, out2, outs = lax.psum((out1.astype(F32) / RING, out2.astype(F32) / RING, outs / RING), "dp")
    out1, out2, act, ing, kern, bias, gain, move = finish(out1, out2, act, ing, outs)
    return (
        act[None],
        ing.transpose(2, 0, 1, 3),
        out1[None],
        out2,
        kern.transpose(1, 0, 2),
        bias,
        gain,
        move,
    )


def solution(mesh):
    in_specs = (
        P(("dp", "section"), None, None, None),
        P(("dp", "section"), None, None, None),
        P("dp"),
        P("dp"),
        P("section", None, None),
        P("section", None),
        P("section", None),
        P("section", None),
        P("section", None, None),
        P("section", None),
    )
    out_specs = (
        P(("dp", "section"), None, None, None),
        P(("dp", "section"), None, None, None),
        P("section", None, None),
        P("section", None),
        P("section", None, None),
        P("section", None),
        P("section", None),
        P("section", None),
    )
    return jax.shard_map(per_device, mesh=mesh, in_specs=in_specs, out_specs=out_specs, check_vma=False)
```

```python
from functools import partial

import jax
import jax.numpy as jnp
from jax import lax
from jax.experimental import pallas as pl
from jax.experimental.pallas import tpu as pltpu
from jax.sharding import PartitionSpec as P

D = 768
FF = 3072
HEADS = 24
HEAD = 32
WIN = 7
SIDE = 2
GRID = SIDE * WIN
CELL = 8
WROWS = WIN * CELL
HALF = GRID * CELL
ROWS = SIDE * HALF
GROUP = 256
PACK = GROUP // HEAD
NGROUP = D // GROUP
UNITS = NGROUP * SIDE * SIDE
LANE = 128
FTILE = 512
EPS = 1e-05
SCALE = HEAD ** (-0.5)
BF = jnp.bfloat16
F32 = jnp.float32
MESH = pl.DeviceIdType.MESH


def dot(a, b, ca=1, cb=0):
    return lax.dot_general(a, b, (((ca,), (cb,)), ((), ())), preferred_element_type=F32)


def lanes(index, width=LANE):
    return pl.ds(pl.multiple_of(index * width, width), width)


def halves(value):
    return value.reshape(SIDE, GRID, CELL, value.shape[-1])


def shifts(left, right):
    column = lax.broadcasted_iota(jnp.int32, left.shape, 1)
    before0 = pltpu.roll(left, 1, 1)
    after0 = jnp.where(column == WIN - 1, pltpu.roll(right, CELL - 2, 1), pltpu.roll(left, CELL - 1, 1))
    before1 = jnp.where(column == 0, pltpu.roll(left, 2, 1), pltpu.roll(right, 1, 1))
    after1 = pltpu.roll(right, CELL - 1, 1)
    return ((before0, left, after0), (before1, right, after1))


def gelu_parts(h):
    expo = jnp.exp(h * h * -0.5)
    t = 1.0 / (1.0 + (0.3275911 * 0.7071067811865476) * jnp.abs(h))
    poly = t * (0.127414796 + t * (-0.142248368 + t * (0.7107068705 + t * (-0.7265760135 + t * 0.5307027145))))
    tail = poly * expo
    phi = jnp.where(h >= 0, 1.0 - tail, tail)
    return h * phi, phi + h * expo * 0.3989422804014327


def front_forward(sec, m, ubuf, msk, pr, U, C, zz, xh, rs):
    zero = jnp.zeros((ROWS, LANE), F32)

    def conv(i, total):
        ls = lanes(i)
        u = ubuf[sec, m, :, ls].astype(F32)
        masked = halves(u * msk[m])
        U[0, 1 : GRID + 1, :, ls] = masked[0]
        U[1, 1 : GRID + 1, :, ls] = masked[1]
        moved = shifts(U[0, :, :, ls], U[1, :, :, ls])
        taps = pr[sec, :, ls]
        uh = halves(u)
        sums = []
        for wc in range(SIDE):
            acc = uh[wc] + taps[9:10, :][None]
            for a in range(3):
                for b in range(3):
                    acc = acc + moved[wc][b][a : a + GRID] * taps[3 * a + b : 3 * a + b + 1, :][None]
            acc = acc.reshape(HALF, LANE)
            C[pl.ds(wc * HALF, HALF), ls] = acc
            sums.append(acc)
        return total + jnp.concatenate(sums, axis=0)

    mean = jnp.sum(lax.fori_loop(0, D // LANE, conv, zero, unroll=True), axis=-1, keepdims=True) * (1.0 / D)

    def spread(i, total):
        centred = C[:, lanes(i)] - mean
        return total + centred * centred

    var = jnp.sum(lax.fori_loop(0, D // LANE, spread, zero, unroll=True), axis=-1, keepdims=True) * (1.0 / D)
    rstd = lax.rsqrt(var + EPS)
    rs[sec, m] = jnp.broadcast_to(rstd, (ROWS, LANE))

    def norm(i, carry):
        ls = lanes(i)
        xhat = (C[:, ls] - mean) * rstd
        xh[sec, m, :, ls] = xhat.astype(BF)
        zz[m, 2 * sec, :, ls] = (xhat * pr[sec, 10:11, ls] + pr[sec, 11:12, ls]).astype(BF)
        return carry

    lax.fori_loop(0, D // LANE, norm, 0, unroll=True)


def fold(value):
    return jnp.sum(value.reshape(ROWS // CELL, CELL, LANE), axis=0)


def front_backward(sec, m, msk, pr, U, T, gfull, xh, rs, sgp, out, sent):
    zero = jnp.zeros((ROWS, LANE), F32)

    def sums(i, carry):
        s1, s2 = carry
        ls = lanes(i)
        dz = T[:, ls]
        xhat = xh[sec, m, :, ls].astype(F32)
        both = xhat * dz
        sgp[sec, 10, :, ls] += fold(both)
        sgp[sec, 11, :, ls] += fold(dz)
        gain = pr[sec, 10:11, ls]
        return s1 + dz * gain, s2 + both * gain

    s1, s2 = lax.fori_loop(0, D // LANE, sums, (zero, zero), unroll=True)
    m1 = jnp.sum(s1, axis=-1, keepdims=True) * (1.0 / D)
    m2 = jnp.sum(s2, axis=-1, keepdims=True) * (1.0 / D)

    def back(i, carry):
        ls = lanes(i)
        xhat = xh[sec, m, :, ls].astype(F32)
        inner = T[:, ls] * pr[sec, 10:11, ls] - m1 - xhat * m2
        gc = gfull(i)[...].astype(F32) + rs[sec, m] * inner
        xh[sec, m, :, ls] = gc.astype(BF)
        gh = halves(gc)
        U[0, 1 : GRID + 1, :, ls] = gh[0]
        U[1, 1 : GRID + 1, :, ls] = gh[1]
        moved = shifts(U[0, :, :, ls], U[1, :, :, ls])
        taps = pr[sec, :, ls]
        mask = halves(msk[m])
        du = []
        for wc in range(SIDE):
            acc = jnp.zeros((GRID, CELL, LANE), F32)
            for a in range(3):
                for b in range(3):
                    tap = 3 * a + b
                    acc = acc + moved[wc][2 - b][2 - a : 2 - a + GRID] * taps[tap : tap + 1, :][None]
            du.append((gh[wc] + mask[wc] * acc).reshape(HALF, LANE))
        out(i)[...] = jnp.concatenate(du, axis=0).astype(BF)
        return carry

    lax.fori_loop(0, D // LANE // 2, back, 0, unroll=True)
    sent(0)
    lax.fori_loop(D // LANE // 2, D // LANE, back, 0, unroll=True)
    sent(1)


def front_sums(sec, m, ubuf, msk, U, xh, sgp):
    def part(i, carry):
        ls = lanes(i)
        gc = xh[sec, m, :, ls].astype(F32)
        sgp[sec, 9, :, ls] += fold(gc)
        gh = halves(gc)
        U[0, 1 : GRID + 1, :, ls] = gh[0]
        U[1, 1 : GRID + 1, :, ls] = gh[1]
        moved = shifts(U[0, :, :, ls], U[1, :, :, ls])
        um = halves(ubuf[sec, m, :, ls].astype(F32) * msk[m])
        for a in range(3):
            for b in range(3):
                kg = jnp.zeros((CELL, LANE), F32)
                for wc in range(SIDE):
                    kg = kg + jnp.sum(moved[wc][2 - b][2 - a : 2 - a + GRID] * um[wc], axis=0)
                sgp[sec, 3 * a + b, :, ls] += kg
        return carry

    lax.fori_loop(0, D // LANE, part, 0)


def spread_heads(value, head_of_lane):
    parts = [jnp.where(head_of_lane == h, value, 0.0) for h in range(PACK)]
    return jnp.concatenate(parts, axis=0).astype(BF)


def gather_heads(value, rows, head_of_lane):
    out = jnp.zeros((rows, GROUP), F32)
    for h in range(PACK):
        out = jnp.where(head_of_lane == h, value[h * rows : (h + 1) * rows], out)
    return out


def unit_slices(unit):
    pair, group = unit // NGROUP, lax.rem(unit, NGROUP)
    rows = [pl.ds(pl.multiple_of((2 * pair + w) * WROWS, 8), WROWS) for w in range(2)]
    cols = [pl.ds(pl.multiple_of(part * D + group * GROUP, LANE), GROUP) for part in range(3)]
    return rows, cols


def window_parts(m, i, qkv):
    rows, cols = unit_slices(i)
    head_of_lane = lax.broadcasted_iota(jnp.int32, (WROWS, GROUP), 1) // HEAD
    q = [qkv[m, r, cols[0]].astype(BF) for r in rows]
    kd = [spread_heads(qkv[m, r, cols[1]], head_of_lane) for r in rows]
    vd = [spread_heads(qkv[m, r, cols[2]], head_of_lane) for r in rows]
    return rows, cols, head_of_lane, q, kd, vd


def window_forward(m, qkv, pw, T, group=None):
    def unit(i, carry):
        rows, cols, head_of_lane, q, kd, vd = window_parts(m, i, qkv)
        s = [(dot(b, a, 1, 1) * SCALE).reshape(PACK, WROWS, WROWS) for a, b in zip(q, kd)]
        key = lax.broadcasted_iota(jnp.int32, s[0].shape, 1)
        real = lax.rem(key, CELL) < WIN
        s = [jnp.where(real, x, -1e30) for x in s]
        p = [jnp.exp(x - jnp.max(x, axis=1, keepdims=True)) for x in s]
        p = [x * (1.0 / jnp.sum(x, axis=1, keepdims=True)) for x in p]
        p = [x.reshape(PACK * WROWS, WROWS) for x in p]
        for w in range(2):
            pw[m, 2 * i + w, :, 0:WROWS] = p[w]
        out = [dot(x.astype(BF), v, 0, 0) for x, v in zip(p, vd)]
        for w in range(2):
            T[rows[w], cols[0]] = out[w]
        return carry

    if group is None:
        lax.fori_loop(0, UNITS // 2, unit, 0, unroll=2)
    else:
        for pair in range(UNITS // 2 // NGROUP):
            unit(pair * NGROUP + group, 0)


def window_backward(m, qkv, pw, T):
    def unit(i, carry):
        rows, cols, head_of_lane, q, kd, vd = window_parts(m, i, qkv)
        g = [T[r, cols[0]].astype(BF) for r in rows]
        p = [pw[m, 2 * i + w, :, 0:WROWS].reshape(PACK, WROWS, WROWS) for w in range(2)]
        dp = [dot(v, x, 1, 1).reshape(PACK, WROWS, WROWS) for v, x in zip(vd, g)]
        ds = [x * (y - jnp.sum(x * y, axis=1, keepdims=True)) for x, y in zip(p, dp)]
        ds = [x.reshape(PACK * WROWS, WROWS).astype(BF) for x in ds]
        pb = [x.reshape(PACK * WROWS, WROWS).astype(BF) for x in p]
        dv = [gather_heads(dot(x, y), WROWS, head_of_lane) for x, y in zip(pb, g)]
        dk = [gather_heads(dot(x, y), WROWS, head_of_lane) * SCALE for x, y in zip(ds, q)]
        dq = [dot(x, y, 0, 0) * SCALE for x, y in zip(ds, kd)]
        for w in range(2):
            qkv[m, rows[w], cols[0]] = dq[w]
            qkv[m, rows[w], cols[1]] = dk[w]
            qkv[m, rows[w], cols[2]] = dv[w]
        return carry

    lax.fori_loop(0, UNITS // 2, unit, 0)


def group_slices(group):
    return [pl.ds(pl.multiple_of(part * D + group * GROUP, LANE), GROUP) for part in range(3)]


def channel_forward(m, qkv, pw, zz, msk):
    def unit(i, carry):
        cols = group_slices(i)
        mask = msk[m][:, :1]
        q = qkv[m, :, cols[0]].astype(BF)
        k = (qkv[m, :, cols[1]] * mask).astype(BF)
        v = qkv[m, :, cols[2]].astype(BF)
        s = dot(q, k, 0, 0) * SCALE
        same = (lax.broadcasted_iota(jnp.int32, s.shape, 0) // HEAD) == (lax.broadcasted_iota(jnp.int32, s.shape, 1) // HEAD)
        s = jnp.where(same, s, -1e30)
        p = jnp.exp(s - jnp.max(s, axis=1, keepdims=True))
        p = p * (1.0 / jnp.sum(p, axis=1, keepdims=True))
        for k in range(GROUP // LANE):
            pw[m, 2 * i + k, 0:GROUP, :] = p[:, k * LANE : (k + 1) * LANE]
        zz[m, 1, :, cols[0]] = dot(v, p.astype(BF), 1, 1).astype(BF)
        return carry

    lax.fori_loop(0, NGROUP, unit, 0, unroll=True)


def channel_backward(m, qkv, pw, T, rr, msk):
    def unit(i, carry):
        cols = group_slices(i)
        mask = msk[m][:, :1]
        q = qkv[m, :, cols[0]].astype(BF)
        k = (qkv[m, :, cols[1]] * mask).astype(BF)
        v = qkv[m, :, cols[2]].astype(BF)
        g = T[:, cols[0]].astype(BF)
        p = jnp.concatenate([pw[m, 2 * i + k, 0:GROUP, :] for k in range(GROUP // LANE)], axis=1)
        dp = dot(g, v, 0, 0)
        ds = (p * (dp - jnp.sum(p * dp, axis=1, keepdims=True))).astype(BF)
        rr[m, 0, :, cols[0]] = (dot(k, ds, 1, 1) * SCALE).astype(BF)
        rr[m, 0, :, cols[1]] = (dot(q, ds) * (SCALE * mask)).astype(BF)
        rr[m, 0, :, cols[2]] = (dot(g, p.astype(BF))).astype(BF)
        return carry

    lax.fori_loop(0, NGROUP, unit, 0, unroll=True)


RING = 8
COLS = FF // RING
WIDE = FF // 12 * 8 // RING
REST = FF // 3 // RING
THIRD = FF // 3 * 2
LENT = RING * 3 // 4
EARLY = 2


def relay_kernel(
    wrows, wcols, img, cot, kern, bias, gain, move, first, second,
    act, ing, out1, out2, outs,
    wf, w2, pr, msk, flat, ubuf, gin, gout, zz, xh, rs, qkv, ab, rr, pw, U, C, T, sgp, sgs, sgm,
    rL, rR, rA, rG, buf, acc, got,
    wl, ws, wr, pl_, usem, gsem, us, gs, ss, rsem, es, er, sgsem, ssem, rcem, osem, sms, smr, xs, xr, ys, yr, bs, br, hs, hr, free,
):
    n = RING
    s = lax.axis_index("section")
    dp = lax.axis_index("dp")
    stage, c = s // 2, lax.rem(s, 2)
    mate = (dp, stage * 2 + (1 - c))
    opposite = (dp, (1 - stage) * 2 + c)
    diagonal = (dp, 3 - s)
    lender, helper = s == 1, s == 2
    early = stage == 0

    spot = lax.rem(dp, n)
    base = dp - spot
    me = jnp.where(lax.rem(spot, 2) == 0, spot // 2, n - 1 - spot // 2)

    def place(pos):
        pos = lax.rem(pos + 2 * n, n)
        return (base + jnp.where(pos < n // 2, 2 * pos, 2 * (n - 1 - pos) + 1), s)

    nexts = (place(me + 1), place(me - 1))
    rounds = n.bit_length() - 1
    partners = []
    for r in range(rounds):
        bit = 1 << r
        partners.append((jnp.where(lax.rem(spot // bit, 2) == 0, dp + bit, dp - bit), s))

    barrier = pltpu.get_barrier_semaphore()
    peers = [mate, opposite, diagonal, *nexts, *partners]
    for peer in peers:
        pl.semaphore_signal(barrier, inc=1, device_id=peer, device_id_type=MESH)
    pl.semaphore_wait(barrier, len(peers))

    def remote(src, dst, send, recv, peer):
        return pltpu.make_async_remote_copy(
            src_ref=src, dst_ref=dst, send_sem=send, recv_sem=recv, device_id=peer, device_id_type=MESH
        )

    half = second.shape[0]

    def weight_parts(k):
        parts = []
        if k == 0:
            for group in range(NGROUP):
                for part in range(3):
                    cols = pl.ds(part * D + group * GROUP, GROUP)
                    parts.append((first.at[:, cols], wf.at[k, :, cols]))
            cols = pl.ds(3 * D, D)
            parts.append((first.at[:, cols], wf.at[k, :, cols]))
        else:
            for i in range(3):
                cols = pl.ds(i * (FF // 3), FF // 3)
                parts.append((first.at[:, cols], wf.at[k, :, cols]))
        third = half // 3
        for i in range(3):
            rows = pl.ds(i * third, third)
            parts.append((second.at[rows, :], w2.at[pl.ds(k * half + i * third, third), :]))
        return parts

    names = (
        [f"qkv{group}" for group in range(NGROUP) for _ in range(3)] + ["out"] + [f"low{i}" for i in range(3)],
        ["in"] * 3 + [f"high{i}" for i in range(3)],
    )

    def weight_copies(k):
        local = [pltpu.make_async_copy(a, b, wl.at[i]) for i, (a, b) in enumerate(weight_parts(k))]
        sent = [remote(a, b, ws.at[i], wr.at[i], mate) for i, (a, b) in enumerate(weight_parts(k))]
        return local, sent

    def params_copy(k):
        return remote(pr.at[k], pr.at[k], ws.at[13], wr.at[13], mate)

    pr[c, 0:9, :] = kern[...].astype(F32)
    pr[c, 9:10, :] = bias[...].astype(F32)
    pr[c, 10:11, :] = gain[...].astype(F32)
    pr[c, 11:12, :] = move[...].astype(F32)
    params_copy(c).start()
    for k in range(2):

        @pl.when(c == k)
        def _():
            local, sent = weight_copies(k)
            for here, there in zip(local, sent):
                here.start()
                there.start()

    def wait_weights(*wanted):
        for k in range(2):

            @pl.when(c == k)
            def _():
                for name, copy in zip(names[k], weight_copies(k)[0]):
                    if name in wanted:
                        copy.wait()
                for name, copy in zip(names[1 - k], weight_copies(1 - k)[1]):
                    if name in wanted:
                        copy.wait_recv()

    def wait_params(k):
        @pl.when(c != k)
        def _():
            params_copy(k).wait_recv()

    raw = flat.at[0]
    img_out = remote(img, raw, pl_.at[0], pl_.at[1], opposite)
    cot_out = remote(cot, raw, pl_.at[0], pl_.at[1], opposite)

    def pad(src, dst):
        blank = jnp.zeros((CELL - WIN, D), F32)
        for r in range(GRID):
            line = src[r].astype(F32)
            for wc in range(SIDE):
                cells = jnp.concatenate([line[wc * WIN : (wc + 1) * WIN], blank], axis=0)
                C[pl.ds(wc * HALF + r * CELL, CELL), :] = cells
        dst[...] = C[...].astype(BF)

    def unpad(dst):
        for r in range(GRID):
            sides = [C[pl.ds(wc * HALF + r * CELL, CELL), :][:WIN] for wc in range(SIDE)]
            dst[r] = jnp.concatenate(sides, axis=0).astype(BF)

    @pl.when(early)
    def _():
        cot_out.start()
        pad(img, ubuf.at[0, 0])

    @pl.when(jnp.logical_not(early))
    def _():
        img_out.start()
        pad(cot, gin.at[1])

    index = lax.broadcasted_iota(jnp.int32, (ROWS, LANE), 0)
    cell = lax.rem(index, CELL)
    row = lax.rem(index, HALF) // CELL
    column = (index // HALF) * WIN + cell
    for m in range(2):
        inside = (row < WIN * wrows[c + 2 * m]) & (column < WIN * wcols[c + 2 * m]) & (cell < WIN)
        msk[m] = jnp.where(inside, 1.0, 0.0)

    @pl.when(jnp.logical_not(early))
    def _():
        cot_out.wait_recv()
        pad(raw, gin.at[0])
        for m in range(2):
            for l in range(D // LANE):
                cols = pl.ds(l * LANE, LANE)
                gin[m, :, cols] = (gin[m, :, cols].astype(F32) * msk[m]).astype(BF)

    for wc in range(SIDE):
        U[wc, 0] = jnp.zeros((CELL, D), F32)
        U[wc, GRID + 1] = jnp.zeros((CELL, D), F32)
    sgp[...] = jnp.zeros(sgp.shape, F32)

    def hop(m, dst, send, recv):
        sides = [pl.ds(i * D // 2, D // 2) for i in range(2)]
        return [
            remote(gout.at[m, :, cols], dst.at[:, cols], send.at[m, i], recv.at[m, i], opposite)
            for i, cols in enumerate(sides)
        ]

    def u_hop(m):
        return hop(m, ubuf.at[0, m], us, usem)

    def g_hop(m):
        return hop(m, gin.at[m], gs, gsem)

    def factor_copies(k, m):
        if k == 0:
            parts = [
                ("F0", zz.at[m, 0], rL.at[m, 0]),
                ("F1", zz.at[m, 1], rL.at[m, 1]),
                ("G", rr.at[m, 0, :, pl.ds(3 * D, D)], rR.at[m, :, pl.ds(3 * D, D)]),
                ("A", rr.at[m, 0, :, pl.ds(0, 3 * D)], rR.at[m, :, pl.ds(0, 3 * D)]),
            ]
        else:
            parts = [
                ("F2", zz.at[m, 2], rL.at[m, 0]),
                ("M", gin.at[m], rG.at[m]),
            ]
            parts.append(("X", ab.at[m], rA.at[m]))
            for i, cols in enumerate((pl.ds(0, FF // 3 * 2), pl.ds(FF // 3 * 2, FF // 3))):
                parts.append((f"H{i}", rr.at[m, 1, :, cols], rR.at[m, :, cols]))
        return [(w, remote(a, b, ss.at[m, i], rsem.at[m, i], mate)) for i, (w, a, b) in enumerate(parts)]

    def start_factors(m, which):
        for k in range(2):

            @pl.when(c != k)
            def _():
                for when, copy in factor_copies(k, m):
                    if when == which:
                        copy.start()

    def wait_factors(which):
        for k in range(2):

            @pl.when(c == k)
            def _():
                for m in range(2):
                    for when, copy in factor_copies(k, m):
                        if when[0] in which:
                            copy.wait_recv()

    def shard(k):
        return lax.rem(k + 4 * n, n)

    def sign(h):
        return 1 if h == 0 else -1

    def home(h, t):
        return shard(me + sign(h) - sign(h) * t)

    def products(terms):
        total = None
        for a, b in terms:
            part = dot(a[...], b[...], 0, 0)
            total = part if total is None else total + part
        return total

    def tile(sub, h, j):
        side = pl.ds(h * COLS, COLS)
        if sub in (0, 4):
            rows = first_rows(sub, h)
            last = jnp.where(j >= (3 * n) // 4, 1, 0)
            own = jnp.where(c == 1, 2, last)
            other = jnp.where(c == 1, 0, last)
            cols = lanes(j, COLS)
            terms = [(zz.at[m, own, :, rows], rr.at[m, c, :, cols]) for m in range(2)]
            terms += [(rL.at[m, other, :, rows], rR.at[m, :, cols]) for m in range(2)]
        elif sub == 3:
            cols = [pl.ds(pl.multiple_of(i * LENT * REST + j * REST, LANE), REST) for i in range(2)]
            terms = [(rA.at[m, :, cols[0]], rG.at[m, :, side]) for m in range(2)]
            terms += [(rA.at[m, :, cols[1]], gout.at[m, :, side]) for m in range(2)]
        else:
            cols = lanes(j, WIDE) if sub == 1 else pl.ds(pl.multiple_of(THIRD + j * REST, LANE), REST)
            terms = [(ab.at[m, :, cols], gin.at[m, :, side]) for m in range(2)]
            terms += [(rA.at[m, :, cols], rG.at[m, :, side]) for m in range(2)]
        return products(terms)

    sizes = (COLS // 3 * 2, WIDE, REST, REST, COLS // 3)
    starts = (0, COLS, COLS + WIDE, COLS + WIDE, COLS // 3 * 2)
    parts = [pl.ds(start, size) for start, size in zip(starts, sizes)]
    subs = range(len(sizes))
    odd = c == 1
    active = (None, odd, odd, helper, None)

    def where_live(sub, j, run):
        if sub == 2:
            pl.when(jnp.logical_not(lender) | (j >= LENT))(run)
        elif sub == 3:
            pl.when(j < LENT)(run)
        else:
            run()

    def first_rows(sub, h):
        return pl.ds(h * COLS + (0 if sub == 0 else sizes[0]), sizes[sub])

    def where_active(sub, run):
        if active[sub] is None:
            run()
        else:
            pl.when(active[sub])(run)


    def gathered(sub, h, j):
        if sub in (0, 4):
            return wf.at[0, first_rows(sub, h), lanes(j, COLS)]
        first_row = 0 if sub == 1 else THIRD
        return w2.at[pl.ds(pl.multiple_of(first_row + j * sizes[sub], 16), sizes[sub]), pl.ds(h * COLS, COLS)]

    def scatter(h, t, sub):
        src, dst = buf.at[h, t, parts[sub], :], buf.at[h, t + 1, parts[sub], :]
        return remote(src, dst, ssem.at[h, t, sub], rcem.at[h, t + 1, sub], nexts[h])

    def spread(h, t, sub, j):
        ref = gathered(sub, h, j)
        return remote(ref, ref, ssem.at[h, n - 1 + t, sub], rcem.at[h, n + t, sub], nexts[h])

    half_shards = n * 3 // 4

    def write(h, j, sub):
        src, side = gathered(sub, h, j), pl.ds(h * COLS, COLS)
        if sub in (0, 4):
            dst = out1.at[first_rows(sub, h), lanes(j, COLS)]
        elif sub == 1:
            dst = out2.at[pl.ds(pl.multiple_of((j - half_shards) * WIDE, 16), WIDE), side]
        else:
            dst = out2.at[pl.ds(pl.multiple_of(THIRD - FF // 2 + j * REST, 16), REST), side]
        if sub == 3:
            return remote(src, dst, bs.at[h, j], br.at[h, j], diagonal)
        return pltpu.make_async_copy(src, dst, osem.at[h, j, sub])

    def hand_over(h, j):
        dst = out2.at[pl.ds(pl.multiple_of(j * WIDE, 16), WIDE), pl.ds(h * COLS, COLS)]
        return remote(gathered(1, h, j), dst, hs.at[h, j], hr.at[h, j], mate)

    def deliver(h, j, sub):
        if sub == 1:

            @pl.when(j < half_shards)
            def _():
                hand_over(h, j).start()

            @pl.when(j >= half_shards)
            def _():
                write(h, j, sub).start()

        else:
            write(h, j, sub).start()

    def lend(m):
        cols, there = pl.ds(THIRD, LENT * REST), [rA.at[m, :, pl.ds(i * LENT * REST, LENT * REST)] for i in range(2)]
        return (
            remote(ab.at[m, :, cols], there[0], xs.at[m], xr.at[m], diagonal),
            remote(rA.at[m, :, cols], there[1], xs.at[2 + m], xr.at[2 + m], diagonal),
        )

    def share(m):
        return remote(gout.at[m], rG.at[m], ys.at[m], yr.at[m], mate)

    def reduce_event(sub, h, e):
        j = shard(me - sign(h) * e)

        @pl.when(e == n - 1)
        def _():
            pl.semaphore_wait(free.at[h, sub], 1)

        def run():
            total = tile(sub, h, j)

            @pl.when(e == 0)
            def _():
                buf[h, 0, parts[sub], :] = total.astype(BF)
                scatter(h, 0, sub).start()

            @pl.when((e > 0) & (e < n - 1))
            def _():
                scatter(h, e - 1, sub).wait_recv()
                buf[h, e, parts[sub], :] = (total + buf[h, e, parts[sub], :].astype(F32)).astype(BF)
                scatter(h, e, sub).start()

            @pl.when(e == n - 1)
            def _():
                scatter(h, n - 2, sub).wait_recv()
                gathered(sub, h, j)[...] = (total + buf[h, n - 1, parts[sub], :].astype(F32)).astype(BF)
                spread(h, 0, sub, j).start()
                deliver(h, j, sub)

        where_live(sub, j, run)

    def event(sub, e):
        for h in range(2):

            @pl.when(e < n)
            def _():
                reduce_event(sub, h, e)

            @pl.when((e >= n) & (e < 2 * n - 1))
            def _():
                t = e - (n - 1)
                j = home(h, t)

                def run():
                    spread(h, t - 1, sub, j).wait_recv()

                    @pl.when(t < n - 1)
                    def _():
                        spread(h, t, sub, j).start()

                    deliver(h, j, sub)

                where_live(sub, j, run)

    def early_event(e, which):
        @pl.when(odd)
        def _():
            for sub in which:
                where_active(sub, lambda: event(sub, e))

    def small(r):
        return remote(acc.at[r], got.at[r], sms.at[r], smr.at[r], partners[r])

    def mlp(m, order, wait):
        total, before, last = C[...], None, None
        for t in order:
            cols = pl.ds(t * FTILE, FTILE)
            h = dot(zz[m, 2], wf[1, :, cols])
            if last is not None:
                wait(last)
                total = total + dot(before, w2[pl.ds(last * FTILE, FTILE), :])
            a, d = gelu_parts(h)
            before, last = a.astype(BF), t
            ab[m, :, cols] = before
            rr[m, 1, :, cols] = d.astype(BF)
        wait(last)
        for i in range(2):
            cols = pl.ds(i * D // 2, D // 2)
            part = total[:, i * D // 2 : (i + 1) * D // 2]
            gout[m, :, cols] = (part + dot(before, w2[pl.ds(last * FTILE, FTILE), cols])).astype(BF)

            @pl.when(early)
            def _():
                u_hop(m)[i].start()

    def forward(m, p):
        @pl.when(jnp.logical_not(early))
        def _():
            for copy in u_hop(m):
                copy.wait_recv()

        @pl.when(early & (m == 1))
        def _():
            img_out.wait_recv()
            pad(raw, ubuf.at[0, 1])

        once = p == 0
        starting = early & once

        @pl.when(once)
        def _():
            wait_params(0)

        @pl.when(once & jnp.logical_not(early))
        def _():
            wait_params(1)
            wait_weights(*set(names[0] + names[1]))

        front_forward(0, m, ubuf, msk, pr, U, C, zz, xh, rs)
        start_factors(m, "F0")

        @pl.when(starting)
        def _():
            for group in range(NGROUP):
                wait_weights(f"qkv{group}")
                for part in range(3):
                    cols = pl.ds(part * D + group * GROUP, GROUP)
                    qkv[m, :, cols] = dot(zz[m, 0], wf[0, :, cols])
                window_forward(m, qkv, pw, T, group)
            zz[m, 1] = T[...].astype(BF)
            wait_weights("out")
            wait_params(1)

        @pl.when(jnp.logical_not(starting))
        def _():
            for i in range(3):
                qkv[m, :, pl.ds(i * D, D)] = dot(zz[m, 0], wf[0, :, pl.ds(i * D, D)])

        @pl.when(early & jnp.logical_not(once))
        def _():
            window_forward(m, qkv, pw, T)
            zz[m, 1] = T[...].astype(BF)

        @pl.when(jnp.logical_not(early))
        def _():
            channel_forward(m, qkv, pw, zz, msk)

        start_factors(m, "F1")
        ubuf[1, m] = (C[...] + dot(zz[m, 1], wf[0, :, pl.ds(3 * D, D)])).astype(BF)

        front_forward(1, m, ubuf, msk, pr, U, C, zz, xh, rs)
        start_factors(m, "F2")

        @pl.when(starting)
        def _():
            wait_weights("in")
            order = [i + 3 * k for i in range(3) for k in range(2)]
            mlp(m, order, lambda t: wait_weights(f"low{t}" if t < 3 else f"high{t - 3}"))

        @pl.when(jnp.logical_not(starting))
        def _():
            mlp(m, range(FF // FTILE), lambda t: None)

        start_factors(m, "X")

        @pl.when(jnp.logical_not(early))
        def _():
            for l in range(D // LANE):
                cols = pl.ds(l * LANE, LANE)
                C[:, cols] = gout[m, :, cols].astype(F32) * msk[m]
            unpad(flat.at[m])

        @pl.when(jnp.logical_not(early) & (m == 0))
        def _():
            remote(flat.at[0], act, es.at[0], er.at[0], opposite).start()

        @pl.when(jnp.logical_not(early) & (m == 1))
        def _():
            pltpu.make_async_copy(flat.at[1], act, es.at[0]).start()

        @pl.when(early & (m == 1))
        def _():
            wait_factors("FX")

        @pl.when(lender & (m == 1))
        def _():
            for i in range(2):
                for copy in lend(i):
                    copy.start()

    def backward(m):
        @pl.when(early)
        def _():
            for copy in g_hop(m):
                copy.wait_recv()

        start_factors(m, "M")
        for t in range(FF // FTILE):
            cols = pl.ds(t * FTILE, FTILE)
            da = dot(gin[m], w2[cols, :], 1, 1)
            rr[m, 1, :, cols] = (da * rr[m, 1, :, cols].astype(F32)).astype(BF)
            if t == FF // FTILE * 2 // 3 - 1:
                start_factors(m, "H0")

        start_factors(m, "H1")

        @pl.when(m == 1)
        def _():
            @pl.when(jnp.logical_not(early))
            def _():
                wait_factors("FX")

            wait_factors("M")
            early_event(0, (1, 2))

        T[...] = dot(rr[m, 1], wf[1], 1, 1)

        @pl.when(m == 1)
        def _():
            wait_factors("H")
            early_event(0, (0, 4))

        last = pl.ds(3 * D, D)

        @pl.when(early)
        def _():
            for copy in u_hop(m):
                copy.wait_send()

        def tail_lanes(i):
            return rr.at[m, 0, :, pl.ds(pl.multiple_of(3 * D + i * LANE, LANE), LANE)]

        def nothing(half):
            pass

        front_backward(1, m, msk, pr, U, T, lambda i: gin.at[m, :, lanes(i)], xh, rs, sgp, tail_lanes, nothing)
        start_factors(m, "G")

        T[...] = dot(rr[m, 0, :, last], wf[0, :, last], 1, 1)

        @pl.when(early)
        def _():
            window_backward(m, qkv, pw, T)
            for i in range(3):
                cols = pl.ds(i * D, D)
                rr[m, 0, :, cols] = qkv[m, :, cols].astype(BF)

        @pl.when(jnp.logical_not(early))
        def _():
            channel_backward(m, qkv, pw, T, rr, msk)

        start_factors(m, "A")

        @pl.when(m == 1)
        def _():
            for e in range(1, EARLY):
                early_event(e, (1, 2, 0, 4))

        T[...] = dot(rr[m, 0, :, pl.ds(0, 3 * D)], wf[0, :, pl.ds(0, 3 * D)], 1, 1)
        def send_half(half):
            @pl.when(jnp.logical_not(early))
            def _():
                g_hop(m)[half].start()

        front_backward(
            0, m, msk, pr, U, T, tail_lanes, xh, rs, sgp, lambda i: gout.at[m, :, lanes(i)], send_half
        )

        @pl.when(s == 3)
        def _():
            share(m).start()

        @pl.when(early)
        def _():
            C[...] = gout[m].astype(F32)
            unpad(flat.at[m])

        @pl.when(early & (m == 0))
        def _():
            pltpu.make_async_copy(flat.at[0], ing, es.at[1]).start()

        @pl.when(early & (m == 1))
        def _():
            remote(flat.at[1], ing, es.at[1], er.at[1], opposite).start()

    def phase(p, carry):
        m = jnp.where(early, lax.rem(p, 2), p // 2)
        ahead = jnp.where(early, p < 2, lax.rem(p, 2) == 0)

        @pl.when(ahead)
        def _():
            forward(m, p)

        @pl.when(jnp.logical_not(ahead))
        def _():
            backward(m)

        return carry

    lax.fori_loop(0, 4, phase, 0)

    for h in range(2):
        for sub in subs:

            def ready():
                pl.semaphore_signal(free.at[h, sub], inc=1, device_id=nexts[1 - h], device_id_type=MESH)

            where_active(sub, ready)

    give = remote(sgs.at[1 - c], sgm, sgsem.at[0], sgsem.at[1], mate)

    def small_sums():
        for sec in range(2):
            for j in range(12):
                sgs[sec, j : j + 1, :] = jnp.sum(sgp[sec, j], axis=0, keepdims=True)
            sgs[sec, 12:16, :] = jnp.zeros((4, D), F32)
        give.start()

    wait_factors("GA")

    @pl.when(helper)
    def _():
        for m in range(2):
            for copy in lend(m):
                copy.wait_recv()
            share(m).wait_recv()

    def ring_step(t, carry):
        for sub in (0, 4):
            event(sub, t + jnp.where(odd, EARLY, 0))
        where_active(1, lambda: event(1, t + EARLY))
        where_active(2, lambda: event(2, t + EARLY))
        where_active(3, lambda: event(3, t))
        @pl.when((t >= 1) & (t < 5))
        def _():
            front_sums((t - 1) // 2, lax.rem(t - 1, 2), ubuf, msk, U, xh, sgp)

        pl.when(t == 5)(small_sums)
        for r in range(rounds + 1):

            @pl.when(t == 6 + 2 * r)
            def _():
                if r == 0:
                    give.wait_recv()
                    acc[0] = sgs[c] + sgm[...]
                else:
                    small(r - 1).wait_recv()
                    acc[r] = acc[r - 1] + got[r - 1]
                if r < rounds:
                    small(r).start()

        return carry

    lax.fori_loop(0, 2 * n - 1, ring_step, 0)
    outs[...] = acc[rounds]

    for k in range(2):

        @pl.when(c == k)
        def _():
            for copy in weight_copies(k)[1]:
                copy.wait_send()
            params_copy(k).wait_send()
            for m in range(2):
                for _when, copy in factor_copies(1 - k, m):
                    copy.wait_send()

    give.wait_send()
    for r in range(rounds):
        small(r).wait_send()

    def drain(t, carry):
        for h in range(2):
            for sub in subs:

                def sent():
                    where_live(sub, shard(me - sign(h) * t), lambda: scatter(h, t, sub).wait_send())
                    where_live(sub, home(h, t), lambda: spread(h, t, sub, home(h, t)).wait_send())

                where_active(sub, sent)

        return carry

    lax.fori_loop(0, n - 1, drain, 0)

    def written(j, carry):
        for h in range(2):
            write(h, j, 0).wait()
            write(h, j, 4).wait()

            @pl.when(odd)
            def _():
                where_live(2, j, lambda: write(h, j, 2).wait())

                @pl.when(j < half_shards)
                def _():
                    hand_over(h, j).wait_send()

                @pl.when(j >= half_shards)
                def _():
                    write(h, j, 1).wait()

            @pl.when(jnp.logical_not(odd) & (j < half_shards))
            def _():
                hand_over(h, j).wait_recv()

            @pl.when(helper & (j < LENT))
            def _():
                write(h, j, 3).wait_send()

            @pl.when(lender & (j < LENT))
            def _():
                write(h, j, 3).wait_recv()

        return carry

    lax.fori_loop(0, n, written, 0)

    @pl.when(lender)
    def _():
        for m in range(2):
            for copy in lend(m):
                copy.wait_send()

    @pl.when(s == 3)
    def _():
        for m in range(2):
            share(m).wait_send()

    @pl.when(early)
    def _():
        cot_out.wait_send()
        pltpu.make_async_copy(flat.at[0], ing, es.at[1]).wait()
        remote(flat.at[1], ing, es.at[1], er.at[1], opposite).wait_send()
        remote(flat.at[0], act, es.at[0], er.at[0], opposite).wait_recv()

    @pl.when(jnp.logical_not(early))
    def _():
        img_out.wait_send()
        for m in range(2):
            for copy in g_hop(m):
                copy.wait_send()
        remote(flat.at[0], act, es.at[0], er.at[0], opposite).wait_send()
        pltpu.make_async_copy(flat.at[1], act, es.at[0]).wait()
        remote(flat.at[1], ing, es.at[1], er.at[1], opposite).wait_recv()


def relay(wrows, wcols, img, cot, kern, bias, gain, move, first, second):
    shape = jax.ShapeDtypeStruct
    vmem = pl.BlockSpec(memory_space=pltpu.VMEM)
    anywhere = pl.BlockSpec(memory_space=pl.ANY)
    dma = pltpu.SemaphoreType.DMA
    smem = pl.BlockSpec(memory_space=pltpu.SMEM)
    image = (ROWS, D)
    slot = img.shape
    rounds = RING.bit_length() - 1
    return pl.pallas_call(
        relay_kernel,
        out_shape=[
            shape(slot, BF),
            shape(slot, BF),
            shape((D, FF), BF),
            shape((FF // 2, D), BF),
            shape((16, D), F32),
        ],
        in_specs=[smem] * 2 + [vmem] * 6 + [anywhere] * 2,
        out_specs=[anywhere] * 4 + [vmem],
        scratch_shapes=[
            pltpu.VMEM((2, D, FF), BF),
            pltpu.VMEM((FF, D), BF),
            pltpu.VMEM((2, 16, D), F32),
            pltpu.VMEM((2, ROWS, LANE), F32),
            pltpu.VMEM((2,) + slot, BF),
            pltpu.VMEM((2, 2) + image, BF),
            pltpu.VMEM((2,) + image, BF),
            pltpu.VMEM((2,) + image, BF),
            pltpu.VMEM((2, 3) + image, BF),
            pltpu.VMEM((2, 2) + image, BF),
            pltpu.VMEM((2, 2, ROWS, LANE), F32),
            pltpu.VMEM((2, ROWS, 3 * D), F32),
            pltpu.VMEM((2, ROWS, FF), BF),
            pltpu.VMEM((2, 2, ROWS, FF), BF),
            pltpu.VMEM((2, UNITS, PACK * WROWS, LANE), F32),
            pltpu.VMEM((SIDE, GRID + 2, CELL, D), F32),
            pltpu.VMEM(image, F32),
            pltpu.VMEM(image, F32),
            pltpu.VMEM((2, 12, CELL, D), F32),
            pltpu.VMEM((2, 16, D), F32),
            pltpu.VMEM((16, D), F32),
            pltpu.VMEM((2, 2) + image, BF),
            pltpu.VMEM((2, ROWS, FF), BF),
            pltpu.VMEM((2, ROWS, FF), BF),
            pltpu.VMEM((2,) + image, BF),
            pltpu.VMEM((2, RING, COLS + WIDE + REST, COLS), BF),
            pltpu.VMEM((rounds + 1, 16, D), F32),
            pltpu.VMEM((rounds, 16, D), F32),
            dma((14,)),
            dma((14,)),
            dma((14,)),
            dma((2,)),
            dma((2, 2)),
            dma((2, 2)),
            dma((2, 2)),
            dma((2, 2)),
            dma((2, 8)),
            dma((2, 8)),
            dma((2,)),
            dma((2,)),
            dma((2,)),
            dma((2, 2 * RING, 5)),
            dma((2, 2 * RING, 5)),
            dma((2, RING, 5)),
            dma((rounds,)),
            dma((rounds,)),
            dma((4,)),
            dma((4,)),
            dma((2,)),
            dma((2,)),
            dma((2, RING)),
            dma((2, RING)),
            dma((2, RING)),
            dma((2, RING)),
            pltpu.SemaphoreType.REGULAR((2, 5)),
        ],
        name="relay",
        compiler_params=pltpu.CompilerParams(
            collective_id=1, has_side_effects=True, vmem_limit_bytes=63 * 2**20
        ),
    )(wrows, wcols, img, cot, kern, bias, gain, move, first, second)


def finish_kernel(
    out1, out2, act, ing, outs, first, second, acts, ings, kern, bias, gain, move,
    raw1, raw2, full1, full2, acted, graded, wide, small, kernels, rsem, wsem,
):
    steps = rsem.shape[0] - 3

    loads = [
        pltpu.make_async_copy(act, acted, rsem.at[steps]),
        pltpu.make_async_copy(ing, graded, rsem.at[steps + 1]),
        pltpu.make_async_copy(outs, small, rsem.at[steps + 2]),
    ]
    for copy in loads:
        copy.start()
    reads, writes = [], []
    for i in range(steps):
        pair = ((out1, raw1, full1, first), (out2, raw2, full2, second))[i % 2]
        src, raw, full, dst = pair
        half = steps // 2
        rows = pl.ds(i // 2 * (src.shape[0] // half), src.shape[0] // half)
        reads.append((pltpu.make_async_copy(src.at[rows, :], raw.at[rows, :], rsem.at[i]), raw, full, rows))
        writes.append(pltpu.make_async_copy(full.at[rows, :], dst.at[rows, :], wsem.at[i]))
    for copy, *_ in reads:
        copy.start()
    for (copy, raw, full, rows), back in zip(reads, writes):
        copy.wait()
        full[rows, :] = raw[rows, :].astype(F32)
        back.start()
    for copy in loads:
        copy.wait()
    for k in range(9):
        kernels[k] = small[k : k + 1, :]
    for r in range(GRID):
        line = graded[r].astype(F32)
        for k in range(GRID):
            wide[r, k] = line[k : k + 1, :]
    last = [
        pltpu.make_async_copy(acted, acts, wsem.at[steps]),
        pltpu.make_async_copy(wide, ings, wsem.at[steps + 1]),
        pltpu.make_async_copy(kernels, kern, wsem.at[steps + 2]),
    ]
    for i, dst in enumerate((bias, gain, move)):
        last.append(pltpu.make_async_copy(small.at[pl.ds(9 + i, 1), :], dst, wsem.at[steps + 3 + i]))
    for copy in last:
        copy.start()
    for copy in writes + last:
        copy.wait()


def finish(out1, out2, act, ing, outs):
    shape = jax.ShapeDtypeStruct
    slot = act.shape
    anywhere = pl.BlockSpec(memory_space=pl.ANY)
    line = (1, D)
    spread = slot[:2] + line
    steps = 16
    return pl.pallas_call(
        finish_kernel,
        out_shape=[
            shape(out1.shape, F32),
            shape(out2.shape, F32),
            shape(slot, BF),
            shape(spread, F32),
            shape((9,) + line, F32),
            shape(line, F32),
            shape(line, F32),
            shape(line, F32),
        ],
        in_specs=[anywhere] * 5,
        out_specs=[anywhere] * 8,
        scratch_shapes=[
            pltpu.VMEM(out1.shape, out1.dtype),
            pltpu.VMEM(out2.shape, out2.dtype),
            pltpu.VMEM(out1.shape, F32),
            pltpu.VMEM(out2.shape, F32),
            pltpu.VMEM(slot, BF),
            pltpu.VMEM(slot, BF),
            pltpu.VMEM(spread, F32),
            pltpu.VMEM(outs.shape, F32),
            pltpu.VMEM((9,) + line, F32),
            pltpu.SemaphoreType.DMA((steps + 3,)),
            pltpu.SemaphoreType.DMA((steps + 6,)),
        ],
        name="finish",
        compiler_params=pltpu.CompilerParams(vmem_limit_bytes=60 * 2**20),
    )(out1, out2, act, ing, outs)


def per_device(
    images, cotangent, window_rows, window_cols, pos_kernel, pos_bias, norm_gain, norm_shift, first_weight, second_weight
):
    act, ing, out1, out2, outs = relay(
        window_rows, window_cols, images[0], cotangent[0], pos_kernel[0], pos_bias, norm_gain, norm_shift,
        first_weight[0], second_weight,
    )
    if lax.axis_size("dp") > RING:
        out1, out2, outs = lax.psum((out1.astype(F32) / RING, out2.astype(F32) / RING, outs / RING), "dp")
    out1, out2, act, ing, kern, bias, gain, move = finish(out1, out2, act, ing, outs)
    return (
        act[None],
        ing.transpose(2, 0, 1, 3),
        out1[None],
        out2,
        kern.transpose(1, 0, 2),
        bias,
        gain,
        move,
    )


def solution(mesh):
    in_specs = (
        P(("dp", "section"), None, None, None),
        P(("dp", "section"), None, None, None),
        P("dp"),
        P("dp"),
        P("section", None, None),
        P("section", None),
        P("section", None),
        P("section", None),
        P("section", None, None),
        P("section", None),
    )
    out_specs = (
        P(("dp", "section"), None, None, None),
        P(("dp", "section"), None, None, None),
        P("section", None, None),
        P("section", None),
        P("section", None, None),
        P("section", None),
        P("section", None),
        P("section", None),
    )
    return jax.shard_map(per_device, mesh=mesh, in_specs=in_specs, out_specs=out_specs, check_vma=False)
```

```python
from functools import partial

import jax
import jax.numpy as jnp
from jax import lax
from jax.experimental import pallas as pl
from jax.experimental.pallas import tpu as pltpu
from jax.sharding import PartitionSpec as P

D = 768
FF = 3072
HEADS = 24
HEAD = 32
WIN = 7
SIDE = 2
GRID = SIDE * WIN
CELL = 8
WROWS = WIN * CELL
HALF = GRID * CELL
ROWS = SIDE * HALF
GROUP = 256
PACK = GROUP // HEAD
NGROUP = D // GROUP
UNITS = NGROUP * SIDE * SIDE
LANE = 128
FTILE = 512
EPS = 1e-05
SCALE = HEAD ** (-0.5)
BF = jnp.bfloat16
F32 = jnp.float32
MESH = pl.DeviceIdType.MESH


def dot(a, b, ca=1, cb=0):
    return lax.dot_general(a, b, (((ca,), (cb,)), ((), ())), preferred_element_type=F32)


def lanes(index, width=LANE):
    return pl.ds(pl.multiple_of(index * width, width), width)


def halves(value):
    return value.reshape(SIDE, GRID, CELL, value.shape[-1])


def shifts(left, right):
    column = lax.broadcasted_iota(jnp.int32, left.shape, 1)
    before0 = pltpu.roll(left, 1, 1)
    after0 = jnp.where(column == WIN - 1, pltpu.roll(right, CELL - 2, 1), pltpu.roll(left, CELL - 1, 1))
    before1 = jnp.where(column == 0, pltpu.roll(left, 2, 1), pltpu.roll(right, 1, 1))
    after1 = pltpu.roll(right, CELL - 1, 1)
    return ((before0, left, after0), (before1, right, after1))


def gelu_parts(h):
    expo = jnp.exp(h * h * -0.5)
    t = 1.0 / (1.0 + (0.3275911 * 0.7071067811865476) * jnp.abs(h))
    poly = t * (0.127414796 + t * (-0.142248368 + t * (0.7107068705 + t * (-0.7265760135 + t * 0.5307027145))))
    tail = poly * expo
    phi = jnp.where(h >= 0, 1.0 - tail, tail)
    return h * phi, phi + h * expo * 0.3989422804014327


def front_forward(sec, m, ubuf, msk, pr, U, C, zz, xh, rs):
    zero = jnp.zeros((ROWS, LANE), F32)

    def conv(i, total):
        ls = lanes(i)
        u = ubuf[sec, m, :, ls].astype(F32)
        masked = halves(u * msk[m])
        U[0, 1 : GRID + 1, :, ls] = masked[0]
        U[1, 1 : GRID + 1, :, ls] = masked[1]
        moved = shifts(U[0, :, :, ls], U[1, :, :, ls])
        taps = pr[sec, :, ls]
        uh = halves(u)
        sums = []
        for wc in range(SIDE):
            acc = uh[wc] + taps[9:10, :][None]
            for a in range(3):
                for b in range(3):
                    acc = acc + moved[wc][b][a : a + GRID] * taps[3 * a + b : 3 * a + b + 1, :][None]
            acc = acc.reshape(HALF, LANE)
            C[pl.ds(wc * HALF, HALF), ls] = acc
            sums.append(acc)
        return total + jnp.concatenate(sums, axis=0)

    mean = jnp.sum(lax.fori_loop(0, D // LANE, conv, zero, unroll=True), axis=-1, keepdims=True) * (1.0 / D)

    def spread(i, total):
        centred = C[:, lanes(i)] - mean
        return total + centred * centred

    var = jnp.sum(lax.fori_loop(0, D // LANE, spread, zero, unroll=True), axis=-1, keepdims=True) * (1.0 / D)
    rstd = lax.rsqrt(var + EPS)
    rs[sec, m] = jnp.broadcast_to(rstd, (ROWS, LANE))

    def norm(i, carry):
        ls = lanes(i)
        xhat = (C[:, ls] - mean) * rstd
        xh[sec, m, :, ls] = xhat.astype(BF)
        zz[m, 2 * sec, :, ls] = (xhat * pr[sec, 10:11, ls] + pr[sec, 11:12, ls]).astype(BF)
        return carry

    lax.fori_loop(0, D // LANE, norm, 0, unroll=True)


def fold(value):
    return jnp.sum(value.reshape(ROWS // CELL, CELL, LANE), axis=0)


def front_backward(sec, m, msk, pr, U, T, gfull, xh, rs, sgp, out, sent):
    zero = jnp.zeros((ROWS, LANE), F32)

    def sums(i, carry):
        s1, s2 = carry
        ls = lanes(i)
        dz = T[:, ls]
        xhat = xh[sec, m, :, ls].astype(F32)
        both = xhat * dz
        sgp[sec, 10, :, ls] += fold(both)
        sgp[sec, 11, :, ls] += fold(dz)
        gain = pr[sec, 10:11, ls]
        return s1 + dz * gain, s2 + both * gain

    s1, s2 = lax.fori_loop(0, D // LANE, sums, (zero, zero), unroll=True)
    m1 = jnp.sum(s1, axis=-1, keepdims=True) * (1.0 / D)
    m2 = jnp.sum(s2, axis=-1, keepdims=True) * (1.0 / D)

    def back(i, carry):
        ls = lanes(i)
        xhat = xh[sec, m, :, ls].astype(F32)
        inner = T[:, ls] * pr[sec, 10:11, ls] - m1 - xhat * m2
        gc = gfull(i)[...].astype(F32) + rs[sec, m] * inner
        xh[sec, m, :, ls] = gc.astype(BF)
        gh = halves(gc)
        U[0, 1 : GRID + 1, :, ls] = gh[0]
        U[1, 1 : GRID + 1, :, ls] = gh[1]
        moved = shifts(U[0, :, :, ls], U[1, :, :, ls])
        taps = pr[sec, :, ls]
        mask = halves(msk[m])
        du = []
        for wc in range(SIDE):
            acc = jnp.zeros((GRID, CELL, LANE), F32)
            for a in range(3):
                for b in range(3):
                    tap = 3 * a + b
                    acc = acc + moved[wc][2 - b][2 - a : 2 - a + GRID] * taps[tap : tap + 1, :][None]
            du.append((gh[wc] + mask[wc] * acc).reshape(HALF, LANE))
        out(i)[...] = jnp.concatenate(du, axis=0).astype(BF)
        return carry

    lax.fori_loop(0, D // LANE // 2, back, 0, unroll=True)
    sent(0)
    lax.fori_loop(D // LANE // 2, D // LANE, back, 0, unroll=True)
    sent(1)


def front_sums(sec, m, ubuf, msk, U, xh, sgp):
    def part(i, carry):
        ls = lanes(i)
        gc = xh[sec, m, :, ls].astype(F32)
        sgp[sec, 9, :, ls] += fold(gc)
        gh = halves(gc)
        U[0, 1 : GRID + 1, :, ls] = gh[0]
        U[1, 1 : GRID + 1, :, ls] = gh[1]
        moved = shifts(U[0, :, :, ls], U[1, :, :, ls])
        um = halves(ubuf[sec, m, :, ls].astype(F32) * msk[m])
        for a in range(3):
            for b in range(3):
                kg = jnp.zeros((CELL, LANE), F32)
                for wc in range(SIDE):
                    kg = kg + jnp.sum(moved[wc][2 - b][2 - a : 2 - a + GRID] * um[wc], axis=0)
                sgp[sec, 3 * a + b, :, ls] += kg
        return carry

    lax.fori_loop(0, D // LANE, part, 0)


def spread_heads(value, head_of_lane):
    parts = [jnp.where(head_of_lane == h, value, 0.0) for h in range(PACK)]
    return jnp.concatenate(parts, axis=0).astype(BF)


def gather_heads(value, rows, head_of_lane):
    out = jnp.zeros((rows, GROUP), F32)
    for h in range(PACK):
        out = jnp.where(head_of_lane == h, value[h * rows : (h + 1) * rows], out)
    return out


def unit_slices(unit):
    pair, group = unit // NGROUP, lax.rem(unit, NGROUP)
    rows = [pl.ds(pl.multiple_of((2 * pair + w) * WROWS, 8), WROWS) for w in range(2)]
    cols = [pl.ds(pl.multiple_of(part * D + group * GROUP, LANE), GROUP) for part in range(3)]
    return rows, cols


def window_parts(m, i, qkv):
    rows, cols = unit_slices(i)
    head_of_lane = lax.broadcasted_iota(jnp.int32, (WROWS, GROUP), 1) // HEAD
    q = [qkv[m, r, cols[0]].astype(BF) for r in rows]
    kd = [spread_heads(qkv[m, r, cols[1]], head_of_lane) for r in rows]
    vd = [spread_heads(qkv[m, r, cols[2]], head_of_lane) for r in rows]
    return rows, cols, head_of_lane, q, kd, vd


def window_forward(m, qkv, pw, T, group):
    def unit(i):
        rows, cols, head_of_lane, q, kd, vd = window_parts(m, i, qkv)
        s = [(dot(b, a, 1, 1) * SCALE).reshape(PACK, WROWS, WROWS) for a, b in zip(q, kd)]
        key = lax.broadcasted_iota(jnp.int32, s[0].shape, 1)
        real = lax.rem(key, CELL) < WIN
        s = [jnp.where(real, x, -1e30) for x in s]
        p = [jnp.exp(x - jnp.max(x, axis=1, keepdims=True)) for x in s]
        p = [x * (1.0 / jnp.sum(x, axis=1, keepdims=True)) for x in p]
        p = [x.reshape(PACK * WROWS, WROWS) for x in p]
        for w in range(2):
            pw[m, 2 * i + w, :, 0:WROWS] = p[w]
        out = [dot(x.astype(BF), v, 0, 0) for x, v in zip(p, vd)]
        for w in range(2):
            T[rows[w], cols[0]] = out[w]

    for pair in range(UNITS // 2 // NGROUP):
        unit(pair * NGROUP + group)


def window_backward(m, qkv, pw, T):
    def unit(i, carry):
        rows, cols, head_of_lane, q, kd, vd = window_parts(m, i, qkv)
        g = [T[r, cols[0]].astype(BF) for r in rows]
        p = [pw[m, 2 * i + w, :, 0:WROWS].reshape(PACK, WROWS, WROWS) for w in range(2)]
        dp = [dot(v, x, 1, 1).reshape(PACK, WROWS, WROWS) for v, x in zip(vd, g)]
        ds = [x * (y - jnp.sum(x * y, axis=1, keepdims=True)) for x, y in zip(p, dp)]
        ds = [x.reshape(PACK * WROWS, WROWS).astype(BF) for x in ds]
        pb = [x.reshape(PACK * WROWS, WROWS).astype(BF) for x in p]
        dv = [gather_heads(dot(x, y), WROWS, head_of_lane) for x, y in zip(pb, g)]
        dk = [gather_heads(dot(x, y), WROWS, head_of_lane) * SCALE for x, y in zip(ds, q)]
        dq = [dot(x, y, 0, 0) * SCALE for x, y in zip(ds, kd)]
        for w in range(2):
            qkv[m, rows[w], cols[0]] = dq[w]
            qkv[m, rows[w], cols[1]] = dk[w]
            qkv[m, rows[w], cols[2]] = dv[w]
        return carry

    lax.fori_loop(0, UNITS // 2, unit, 0)


def group_slices(group):
    return [pl.ds(pl.multiple_of(part * D + group * GROUP, LANE), GROUP) for part in range(3)]


def channel_forward(m, qkv, pw, zz, msk):
    def unit(i, carry):
        cols = group_slices(i)
        mask = msk[m][:, :1]
        q = qkv[m, :, cols[0]].astype(BF)
        k = (qkv[m, :, cols[1]] * mask).astype(BF)
        v = qkv[m, :, cols[2]].astype(BF)
        s = dot(q, k, 0, 0) * SCALE
        same = (lax.broadcasted_iota(jnp.int32, s.shape, 0) // HEAD) == (lax.broadcasted_iota(jnp.int32, s.shape, 1) // HEAD)
        s = jnp.where(same, s, -1e30)
        p = jnp.exp(s - jnp.max(s, axis=1, keepdims=True))
        p = p * (1.0 / jnp.sum(p, axis=1, keepdims=True))
        for k in range(GROUP // LANE):
            pw[m, 2 * i + k, 0:GROUP, :] = p[:, k * LANE : (k + 1) * LANE]
        zz[m, 1, :, cols[0]] = dot(v, p.astype(BF), 1, 1).astype(BF)
        return carry

    lax.fori_loop(0, NGROUP, unit, 0, unroll=True)


def channel_backward(m, qkv, pw, T, rr, msk):
    def unit(i, carry):
        cols = group_slices(i)
        mask = msk[m][:, :1]
        q = qkv[m, :, cols[0]].astype(BF)
        k = (qkv[m, :, cols[1]] * mask).astype(BF)
        v = qkv[m, :, cols[2]].astype(BF)
        g = T[:, cols[0]].astype(BF)
        p = jnp.concatenate([pw[m, 2 * i + k, 0:GROUP, :] for k in range(GROUP // LANE)], axis=1)
        dp = dot(g, v, 0, 0)
        ds = (p * (dp - jnp.sum(p * dp, axis=1, keepdims=True))).astype(BF)
        rr[m, 0, :, cols[0]] = (dot(k, ds, 1, 1) * SCALE).astype(BF)
        rr[m, 0, :, cols[1]] = (dot(q, ds) * (SCALE * mask)).astype(BF)
        rr[m, 0, :, cols[2]] = (dot(g, p.astype(BF))).astype(BF)
        return carry

    lax.fori_loop(0, NGROUP, unit, 0, unroll=True)


RING = 8
COLS = FF // RING
WIDE = FF // 12 * 8 // RING
REST = FF // 3 // RING
THIRD = FF // 3 * 2
LENT = RING * 3 // 4
EARLY = 2


def relay_kernel(
    wrows, wcols, img, cot, kern, bias, gain, move, first, second,
    act, ing, out1, out2, outs,
    wf, w2, pr, msk, flat, ubuf, gin, gout, zz, xh, rs, qkv, ab, rr, pw, U, C, T, sgp, sgs, sgm,
    rL, rR, rA, rG, buf, acc, got,
    wl, ws, wr, pl_, usem, gsem, us, gs, ss, rsem, es, er, sgsem, ssem, rcem, osem, sms, smr, xs, xr, ys, yr, bs, br, hs, hr, free,
):
    n = RING
    s = lax.axis_index("section")
    dp = lax.axis_index("dp")
    stage, c = s // 2, lax.rem(s, 2)
    mate = (dp, stage * 2 + (1 - c))
    opposite = (dp, (1 - stage) * 2 + c)
    diagonal = (dp, 3 - s)
    lender, helper = s == 1, s == 2
    early = stage == 0

    spot = lax.rem(dp, n)
    base = dp - spot
    me = jnp.where(lax.rem(spot, 2) == 0, spot // 2, n - 1 - spot // 2)

    def place(pos):
        pos = lax.rem(pos + 2 * n, n)
        return (base + jnp.where(pos < n // 2, 2 * pos, 2 * (n - 1 - pos) + 1), s)

    nexts = (place(me + 1), place(me - 1))
    rounds = n.bit_length() - 1
    partners = []
    for r in range(rounds):
        bit = 1 << r
        partners.append((jnp.where(lax.rem(spot // bit, 2) == 0, dp + bit, dp - bit), s))

    barrier = pltpu.get_barrier_semaphore()
    peers = [mate, opposite, diagonal, *nexts, *partners]
    for peer in peers:
        pl.semaphore_signal(barrier, inc=1, device_id=peer, device_id_type=MESH)
    pl.semaphore_wait(barrier, len(peers))

    def remote(src, dst, send, recv, peer):
        return pltpu.make_async_remote_copy(
            src_ref=src, dst_ref=dst, send_sem=send, recv_sem=recv, device_id=peer, device_id_type=MESH
        )

    half = second.shape[0]

    def group_part(group, part):
        cols = pl.ds(pl.multiple_of(part * D + group * GROUP, LANE), GROUP)
        return first.at[:, cols], wf.at[0, :, cols]

    def wait_group(group):
        for part in range(3):
            src, dst = group_part(group, part)
            i = group * 3 + part

            @pl.when(c == 0)
            def _():
                pltpu.make_async_copy(src, dst, wl.at[i]).wait()

            @pl.when(c == 1)
            def _():
                remote(src, dst, ws.at[i], wr.at[i], mate).wait_recv()

    def weight_parts(k):
        parts = []
        if k == 0:
            for group in range(NGROUP):
                for part in range(3):
                    parts.append(group_part(group, part))
            cols = pl.ds(3 * D, D)
            parts.append((first.at[:, cols], wf.at[k, :, cols]))
        else:
            for i in range(3):
                cols = pl.ds(i * (FF // 3), FF // 3)
                parts.append((first.at[:, cols], wf.at[k, :, cols]))
        third = half // 3
        for i in range(3):
            rows = pl.ds(i * third, third)
            parts.append((second.at[rows, :], w2.at[pl.ds(k * half + i * third, third), :]))
        return parts

    names = (
        [f"qkv{group}" for group in range(NGROUP) for _ in range(3)] + ["out"] + [f"low{i}" for i in range(3)],
        ["in"] * 3 + [f"high{i}" for i in range(3)],
    )

    def weight_copies(k):
        local = [pltpu.make_async_copy(a, b, wl.at[i]) for i, (a, b) in enumerate(weight_parts(k))]
        sent = [remote(a, b, ws.at[i], wr.at[i], mate) for i, (a, b) in enumerate(weight_parts(k))]
        return local, sent

    def params_copy(k):
        return remote(pr.at[k], pr.at[k], ws.at[13], wr.at[13], mate)

    pr[c, 0:9, :] = kern[...].astype(F32)
    pr[c, 9:10, :] = bias[...].astype(F32)
    pr[c, 10:11, :] = gain[...].astype(F32)
    pr[c, 11:12, :] = move[...].astype(F32)
    params_copy(c).start()
    for k in range(2):

        @pl.when(c == k)
        def _():
            local, sent = weight_copies(k)
            for here, there in zip(local, sent):
                here.start()
                there.start()

    def wait_weights(*wanted):
        for k in range(2):

            @pl.when(c == k)
            def _():
                for name, copy in zip(names[k], weight_copies(k)[0]):
                    if name in wanted:
                        copy.wait()
                for name, copy in zip(names[1 - k], weight_copies(1 - k)[1]):
                    if name in wanted:
                        copy.wait_recv()

    def wait_params(k):
        @pl.when(c != k)
        def _():
            params_copy(k).wait_recv()

    raw = flat.at[0]
    img_out = remote(img, raw, pl_.at[0], pl_.at[1], opposite)
    cot_out = remote(cot, raw, pl_.at[0], pl_.at[1], opposite)

    def pad(src, dst):
        blank = jnp.zeros((CELL - WIN, D), F32)
        for r in range(GRID):
            line = src[r].astype(F32)
            for wc in range(SIDE):
                cells = jnp.concatenate([line[wc * WIN : (wc + 1) * WIN], blank], axis=0)
                C[pl.ds(wc * HALF + r * CELL, CELL), :] = cells
        dst[...] = C[...].astype(BF)

    def unpad(dst):
        for r in range(GRID):
            sides = [C[pl.ds(wc * HALF + r * CELL, CELL), :][:WIN] for wc in range(SIDE)]
            dst[r] = jnp.concatenate(sides, axis=0).astype(BF)

    @pl.when(early)
    def _():
        cot_out.start()
        pad(img, ubuf.at[0, 0])

    @pl.when(jnp.logical_not(early))
    def _():
        img_out.start()
        pad(cot, gin.at[1])

    index = lax.broadcasted_iota(jnp.int32, (ROWS, LANE), 0)
    cell = lax.rem(index, CELL)
    row = lax.rem(index, HALF) // CELL
    column = (index // HALF) * WIN + cell
    for m in range(2):
        inside = (row < WIN * wrows[c + 2 * m]) & (column < WIN * wcols[c + 2 * m]) & (cell < WIN)
        msk[m] = jnp.where(inside, 1.0, 0.0)

    @pl.when(jnp.logical_not(early))
    def _():
        cot_out.wait_recv()
        pad(raw, gin.at[0])
        for m in range(2):
            for l in range(D // LANE):
                cols = pl.ds(l * LANE, LANE)
                gin[m, :, cols] = (gin[m, :, cols].astype(F32) * msk[m]).astype(BF)

    for wc in range(SIDE):
        U[wc, 0] = jnp.zeros((CELL, D), F32)
        U[wc, GRID + 1] = jnp.zeros((CELL, D), F32)
    sgp[...] = jnp.zeros(sgp.shape, F32)

    def hop(m, dst, send, recv):
        sides = [pl.ds(i * D // 2, D // 2) for i in range(2)]
        return [
            remote(gout.at[m, :, cols], dst.at[:, cols], send.at[m, i], recv.at[m, i], opposite)
            for i, cols in enumerate(sides)
        ]

    def u_hop(m):
        return hop(m, ubuf.at[0, m], us, usem)

    def g_hop(m):
        return hop(m, gin.at[m], gs, gsem)

    def factor_copies(k, m):
        if k == 0:
            parts = [
                ("F0", zz.at[m, 0], rL.at[m, 0]),
                ("F1", zz.at[m, 1], rL.at[m, 1]),
                ("G", rr.at[m, 0, :, pl.ds(3 * D, D)], rR.at[m, :, pl.ds(3 * D, D)]),
                ("A", rr.at[m, 0, :, pl.ds(0, 3 * D)], rR.at[m, :, pl.ds(0, 3 * D)]),
            ]
        else:
            parts = [
                ("F2", zz.at[m, 2], rL.at[m, 0]),
                ("M", gin.at[m], rG.at[m]),
            ]
            parts.append(("X", ab.at[m], rA.at[m]))
            for i, cols in enumerate((pl.ds(0, FF // 3 * 2), pl.ds(FF // 3 * 2, FF // 3))):
                parts.append((f"H{i}", rr.at[m, 1, :, cols], rR.at[m, :, cols]))
        return [(w, remote(a, b, ss.at[m, i], rsem.at[m, i], mate)) for i, (w, a, b) in enumerate(parts)]

    def start_factors(m, which):
        for k in range(2):

            @pl.when(c != k)
            def _():
                for when, copy in factor_copies(k, m):
                    if when == which:
                        copy.start()

    def wait_factors(which):
        for k in range(2):

            @pl.when(c == k)
            def _():
                for m in range(2):
                    for when, copy in factor_copies(k, m):
                        if when[0] in which:
                            copy.wait_recv()

    def shard(k):
        return lax.rem(k + 4 * n, n)

    def sign(h):
        return 1 if h == 0 else -1

    def home(h, t):
        return shard(me + sign(h) - sign(h) * t)

    def products(terms):
        total = None
        for a, b in terms:
            part = dot(a[...], b[...], 0, 0)
            total = part if total is None else total + part
        return total

    def tile(sub, h, j):
        side = pl.ds(h * COLS, COLS)
        if sub in (0, 4):
            rows = first_rows(sub, h)
            last = jnp.where(j >= (3 * n) // 4, 1, 0)
            own = jnp.where(c == 1, 2, last)
            other = jnp.where(c == 1, 0, last)
            cols = lanes(j, COLS)
            terms = [(zz.at[m, own, :, rows], rr.at[m, c, :, cols]) for m in range(2)]
            terms += [(rL.at[m, other, :, rows], rR.at[m, :, cols]) for m in range(2)]
        elif sub == 3:
            cols = [pl.ds(pl.multiple_of(i * LENT * REST + j * REST, LANE), REST) for i in range(2)]
            terms = [(rA.at[m, :, cols[0]], rG.at[m, :, side]) for m in range(2)]
            terms += [(rA.at[m, :, cols[1]], gout.at[m, :, side]) for m in range(2)]
        else:
            cols = lanes(j, WIDE) if sub == 1 else pl.ds(pl.multiple_of(THIRD + j * REST, LANE), REST)
            terms = [(ab.at[m, :, cols], gin.at[m, :, side]) for m in range(2)]
            terms += [(rA.at[m, :, cols], rG.at[m, :, side]) for m in range(2)]
        return products(terms)

    sizes = (COLS // 3 * 2, WIDE, REST, REST, COLS // 3)
    starts = (0, COLS, COLS + WIDE, COLS + WIDE, COLS // 3 * 2)
    parts = [pl.ds(start, size) for start, size in zip(starts, sizes)]
    subs = range(len(sizes))
    odd = c == 1
    active = (None, odd, odd, helper, None)

    def where_live(sub, j, run):
        if sub == 2:
            pl.when(jnp.logical_not(lender) | (j >= LENT))(run)
        elif sub == 3:
            pl.when(j < LENT)(run)
        else:
            run()

    def first_rows(sub, h):
        return pl.ds(h * COLS + (0 if sub == 0 else sizes[0]), sizes[sub])

    def where_active(sub, run):
        if active[sub] is None:
            run()
        else:
            pl.when(active[sub])(run)


    def gathered(sub, h, j):
        if sub in (0, 4):
            return wf.at[0, first_rows(sub, h), lanes(j, COLS)]
        first_row = 0 if sub == 1 else THIRD
        return w2.at[pl.ds(pl.multiple_of(first_row + j * sizes[sub], 16), sizes[sub]), pl.ds(h * COLS, COLS)]

    def scatter(h, t, sub):
        src, dst = buf.at[h, t, parts[sub], :], buf.at[h, t + 1, parts[sub], :]
        return remote(src, dst, ssem.at[h, t, sub], rcem.at[h, t + 1, sub], nexts[h])

    def spread(h, t, sub, j):
        ref = gathered(sub, h, j)
        return remote(ref, ref, ssem.at[h, n - 1 + t, sub], rcem.at[h, n + t, sub], nexts[h])

    half_shards = n * 3 // 4

    def write(h, j, sub):
        src, side = gathered(sub, h, j), pl.ds(h * COLS, COLS)
        if sub in (0, 4):
            dst = out1.at[first_rows(sub, h), lanes(j, COLS)]
        elif sub == 1:
            dst = out2.at[pl.ds(pl.multiple_of((j - half_shards) * WIDE, 16), WIDE), side]
        else:
            dst = out2.at[pl.ds(pl.multiple_of(THIRD - FF // 2 + j * REST, 16), REST), side]
        if sub == 3:
            return remote(src, dst, bs.at[h, j], br.at[h, j], diagonal)
        return pltpu.make_async_copy(src, dst, osem.at[h, j, sub])

    def hand_over(h, j):
        dst = out2.at[pl.ds(pl.multiple_of(j * WIDE, 16), WIDE), pl.ds(h * COLS, COLS)]
        return remote(gathered(1, h, j), dst, hs.at[h, j], hr.at[h, j], mate)

    def deliver(h, j, sub):
        if sub == 1:

            @pl.when(j < half_shards)
            def _():
                hand_over(h, j).start()

            @pl.when(j >= half_shards)
            def _():
                write(h, j, sub).start()

        else:
            write(h, j, sub).start()

    def lend(m):
        cols, there = pl.ds(THIRD, LENT * REST), [rA.at[m, :, pl.ds(i * LENT * REST, LENT * REST)] for i in range(2)]
        return (
            remote(ab.at[m, :, cols], there[0], xs.at[m], xr.at[m], diagonal),
            remote(rA.at[m, :, cols], there[1], xs.at[2 + m], xr.at[2 + m], diagonal),
        )

    def share(m):
        return remote(gout.at[m], rG.at[m], ys.at[m], yr.at[m], mate)

    def reduce_event(sub, h, e):
        j = shard(me - sign(h) * e)

        @pl.when(e == n - 1)
        def _():
            pl.semaphore_wait(free.at[h, sub], 1)

        def run():
            total = tile(sub, h, j)

            @pl.when(e == 0)
            def _():
                buf[h, 0, parts[sub], :] = total.astype(BF)
                scatter(h, 0, sub).start()

            @pl.when((e > 0) & (e < n - 1))
            def _():
                scatter(h, e - 1, sub).wait_recv()
                buf[h, e, parts[sub], :] = (total + buf[h, e, parts[sub], :].astype(F32)).astype(BF)
                scatter(h, e, sub).start()

            @pl.when(e == n - 1)
            def _():
                scatter(h, n - 2, sub).wait_recv()
                gathered(sub, h, j)[...] = (total + buf[h, n - 1, parts[sub], :].astype(F32)).astype(BF)
                spread(h, 0, sub, j).start()
                deliver(h, j, sub)

        where_live(sub, j, run)

    def event(sub, e):
        for h in range(2):

            @pl.when(e < n)
            def _():
                reduce_event(sub, h, e)

            @pl.when((e >= n) & (e < 2 * n - 1))
            def _():
                t = e - (n - 1)
                j = home(h, t)

                def run():
                    spread(h, t - 1, sub, j).wait_recv()

                    @pl.when(t < n - 1)
                    def _():
                        spread(h, t, sub, j).start()

                    deliver(h, j, sub)

                where_live(sub, j, run)

    def early_event(e, which):
        @pl.when(odd)
        def _():
            for sub in which:
                where_active(sub, lambda: event(sub, e))

    def small(r):
        return remote(acc.at[r], got.at[r], sms.at[r], smr.at[r], partners[r])

    def mlp(m, order, wait):
        total, before, last = C[...], None, None
        for t in order:
            cols = pl.ds(t * FTILE, FTILE)
            h = dot(zz[m, 2], wf[1, :, cols])
            if last is not None:
                wait(last)
                total = total + dot(before, w2[pl.ds(last * FTILE, FTILE), :])
            a, d = gelu_parts(h)
            before, last = a.astype(BF), t
            ab[m, :, cols] = before
            rr[m, 1, :, cols] = d.astype(BF)
        wait(last)
        for i in range(2):
            cols = pl.ds(i * D // 2, D // 2)
            part = total[:, i * D // 2 : (i + 1) * D // 2]
            gout[m, :, cols] = (part + dot(before, w2[pl.ds(last * FTILE, FTILE), cols])).astype(BF)

            @pl.when(early)
            def _():
                u_hop(m)[i].start()

    def forward(m, p):
        @pl.when(jnp.logical_not(early))
        def _():
            for copy in u_hop(m):
                copy.wait_recv()

        @pl.when(early & (m == 1))
        def _():
            img_out.wait_recv()
            pad(raw, ubuf.at[0, 1])

        once = p == 0
        starting = early & once

        @pl.when(once)
        def _():
            wait_params(0)

        @pl.when(once & jnp.logical_not(early))
        def _():
            wait_params(1)
            wait_weights(*set(names[0] + names[1]))

        front_forward(0, m, ubuf, msk, pr, U, C, zz, xh, rs)
        start_factors(m, "F0")

        @pl.when(early)
        def _():
            def head_group(group, carry):
                @pl.when(once)
                def _():
                    wait_group(group)

                for part in range(3):
                    cols = pl.ds(pl.multiple_of(part * D + group * GROUP, LANE), GROUP)
                    qkv[m, :, cols] = dot(zz[m, 0], wf[0, :, cols])
                window_forward(m, qkv, pw, T, group)
                return carry

            lax.fori_loop(0, NGROUP, head_group, 0)
            zz[m, 1] = T[...].astype(BF)

        @pl.when(starting)
        def _():
            wait_weights("out")
            wait_params(1)

        @pl.when(jnp.logical_not(early))
        def _():
            for i in range(3):
                qkv[m, :, pl.ds(i * D, D)] = dot(zz[m, 0], wf[0, :, pl.ds(i * D, D)])

        @pl.when(jnp.logical_not(early))
        def _():
            channel_forward(m, qkv, pw, zz, msk)

        start_factors(m, "F1")
        ubuf[1, m] = (C[...] + dot(zz[m, 1], wf[0, :, pl.ds(3 * D, D)])).astype(BF)

        front_forward(1, m, ubuf, msk, pr, U, C, zz, xh, rs)
        start_factors(m, "F2")

        @pl.when(starting)
        def _():
            wait_weights("in")
            order = [i + 3 * k for i in range(3) for k in range(2)]
            mlp(m, order, lambda t: wait_weights(f"low{t}" if t < 3 else f"high{t - 3}"))

        @pl.when(jnp.logical_not(starting))
        def _():
            mlp(m, range(FF // FTILE), lambda t: None)

        start_factors(m, "X")

        @pl.when(jnp.logical_not(early))
        def _():
            for l in range(D // LANE):
                cols = pl.ds(l * LANE, LANE)
                C[:, cols] = gout[m, :, cols].astype(F32) * msk[m]
            unpad(flat.at[m])

        @pl.when(jnp.logical_not(early) & (m == 0))
        def _():
            remote(flat.at[0], act, es.at[0], er.at[0], opposite).start()

        @pl.when(jnp.logical_not(early) & (m == 1))
        def _():
            pltpu.make_async_copy(flat.at[1], act, es.at[0]).start()

        @pl.when(early & (m == 1))
        def _():
            wait_factors("FX")

        @pl.when(lender & (m == 1))
        def _():
            for i in range(2):
                for copy in lend(i):
                    copy.start()

    def backward(m):
        @pl.when(early)
        def _():
            for copy in g_hop(m):
                copy.wait_recv()

        start_factors(m, "M")
        for t in range(FF // FTILE):
            cols = pl.ds(t * FTILE, FTILE)
            da = dot(gin[m], w2[cols, :], 1, 1)
            rr[m, 1, :, cols] = (da * rr[m, 1, :, cols].astype(F32)).astype(BF)
            if t == FF // FTILE * 2 // 3 - 1:
                start_factors(m, "H0")

        start_factors(m, "H1")

        @pl.when(m == 1)
        def _():
            @pl.when(jnp.logical_not(early))
            def _():
                wait_factors("FX")

            wait_factors("M")
            early_event(0, (1, 2))

        T[...] = dot(rr[m, 1], wf[1], 1, 1)

        @pl.when(m == 1)
        def _():
            wait_factors("H")
            early_event(0, (0, 4))

        last = pl.ds(3 * D, D)

        @pl.when(early)
        def _():
            for copy in u_hop(m):
                copy.wait_send()

        def tail_lanes(i):
            return rr.at[m, 0, :, pl.ds(pl.multiple_of(3 * D + i * LANE, LANE), LANE)]

        def nothing(half):
            pass

        front_backward(1, m, msk, pr, U, T, lambda i: gin.at[m, :, lanes(i)], xh, rs, sgp, tail_lanes, nothing)
        start_factors(m, "G")

        T[...] = dot(rr[m, 0, :, last], wf[0, :, last], 1, 1)

        @pl.when(early)
        def _():
            window_backward(m, qkv, pw, T)
            for i in range(3):
                cols = pl.ds(i * D, D)
                rr[m, 0, :, cols] = qkv[m, :, cols].astype(BF)

        @pl.when(jnp.logical_not(early))
        def _():
            channel_backward(m, qkv, pw, T, rr, msk)

        start_factors(m, "A")

        @pl.when(m == 1)
        def _():
            for e in range(1, EARLY):
                early_event(e, (1, 2, 0, 4))

        T[...] = dot(rr[m, 0, :, pl.ds(0, 3 * D)], wf[0, :, pl.ds(0, 3 * D)], 1, 1)
        def send_half(half):
            @pl.when(jnp.logical_not(early))
            def _():
                g_hop(m)[half].start()

        front_backward(
            0, m, msk, pr, U, T, tail_lanes, xh, rs, sgp, lambda i: gout.at[m, :, lanes(i)], send_half
        )

        @pl.when(s == 3)
        def _():
            share(m).start()

        @pl.when(early)
        def _():
            C[...] = gout[m].astype(F32)
            unpad(flat.at[m])

        @pl.when(early & (m == 0))
        def _():
            pltpu.make_async_copy(flat.at[0], ing, es.at[1]).start()

        @pl.when(early & (m == 1))
        def _():
            remote(flat.at[1], ing, es.at[1], er.at[1], opposite).start()

    def phase(p, carry):
        m = jnp.where(early, lax.rem(p, 2), p // 2)
        ahead = jnp.where(early, p < 2, lax.rem(p, 2) == 0)

        @pl.when(ahead)
        def _():
            forward(m, p)

        @pl.when(jnp.logical_not(ahead))
        def _():
            backward(m)

        return carry

    lax.fori_loop(0, 4, phase, 0)

    for h in range(2):
        for sub in subs:

            def ready():
                pl.semaphore_signal(free.at[h, sub], inc=1, device_id=nexts[1 - h], device_id_type=MESH)

            where_active(sub, ready)

    give = remote(sgs.at[1 - c], sgm, sgsem.at[0], sgsem.at[1], mate)

    def small_sums():
        for sec in range(2):
            for j in range(12):
                sgs[sec, j : j + 1, :] = jnp.sum(sgp[sec, j], axis=0, keepdims=True)
            sgs[sec, 12:16, :] = jnp.zeros((4, D), F32)
        give.start()

    wait_factors("GA")

    @pl.when(helper)
    def _():
        for m in range(2):
            for copy in lend(m):
                copy.wait_recv()
            share(m).wait_recv()

    def ring_step(t, carry):
        for sub in (0, 4):
            event(sub, t + jnp.where(odd, EARLY, 0))
        where_active(1, lambda: event(1, t + EARLY))
        where_active(2, lambda: event(2, t + EARLY))
        where_active(3, lambda: event(3, t))
        @pl.when((t >= 1) & (t < 5))
        def _():
            front_sums((t - 1) // 2, lax.rem(t - 1, 2), ubuf, msk, U, xh, sgp)

        pl.when(t == 5)(small_sums)
        for r in range(rounds + 1):

            @pl.when(t == 6 + 2 * r)
            def _():
                if r == 0:
                    give.wait_recv()
                    acc[0] = sgs[c] + sgm[...]
                else:
                    small(r - 1).wait_recv()
                    acc[r] = acc[r - 1] + got[r - 1]
                if r < rounds:
                    small(r).start()

        return carry

    lax.fori_loop(0, 2 * n - 1, ring_step, 0)
    outs[...] = acc[rounds]

    for k in range(2):

        @pl.when(c == k)
        def _():
            for copy in weight_copies(k)[1]:
                copy.wait_send()
            params_copy(k).wait_send()
            for m in range(2):
                for _when, copy in factor_copies(1 - k, m):
                    copy.wait_send()

    give.wait_send()
    for r in range(rounds):
        small(r).wait_send()

    def drain(t, carry):
        for h in range(2):
            for sub in subs:

                def sent():
                    where_live(sub, shard(me - sign(h) * t), lambda: scatter(h, t, sub).wait_send())
                    where_live(sub, home(h, t), lambda: spread(h, t, sub, home(h, t)).wait_send())

                where_active(sub, sent)

        return carry

    lax.fori_loop(0, n - 1, drain, 0)

    def written(j, carry):
        for h in range(2):
            write(h, j, 0).wait()
            write(h, j, 4).wait()

            @pl.when(odd)
            def _():
                where_live(2, j, lambda: write(h, j, 2).wait())

                @pl.when(j < half_shards)
                def _():
                    hand_over(h, j).wait_send()

                @pl.when(j >= half_shards)
                def _():
                    write(h, j, 1).wait()

            @pl.when(jnp.logical_not(odd) & (j < half_shards))
            def _():
                hand_over(h, j).wait_recv()

            @pl.when(helper & (j < LENT))
            def _():
                write(h, j, 3).wait_send()

            @pl.when(lender & (j < LENT))
            def _():
                write(h, j, 3).wait_recv()

        return carry

    lax.fori_loop(0, n, written, 0)

    @pl.when(lender)
    def _():
        for m in range(2):
            for copy in lend(m):
                copy.wait_send()

    @pl.when(s == 3)
    def _():
        for m in range(2):
            share(m).wait_send()

    @pl.when(early)
    def _():
        cot_out.wait_send()
        pltpu.make_async_copy(flat.at[0], ing, es.at[1]).wait()
        remote(flat.at[1], ing, es.at[1], er.at[1], opposite).wait_send()
        remote(flat.at[0], act, es.at[0], er.at[0], opposite).wait_recv()

    @pl.when(jnp.logical_not(early))
    def _():
        img_out.wait_send()
        for m in range(2):
            for copy in g_hop(m):
                copy.wait_send()
        remote(flat.at[0], act, es.at[0], er.at[0], opposite).wait_send()
        pltpu.make_async_copy(flat.at[1], act, es.at[0]).wait()
        remote(flat.at[1], ing, es.at[1], er.at[1], opposite).wait_recv()


def relay(wrows, wcols, img, cot, kern, bias, gain, move, first, second):
    shape = jax.ShapeDtypeStruct
    vmem = pl.BlockSpec(memory_space=pltpu.VMEM)
    anywhere = pl.BlockSpec(memory_space=pl.ANY)
    dma = pltpu.SemaphoreType.DMA
    smem = pl.BlockSpec(memory_space=pltpu.SMEM)
    image = (ROWS, D)
    slot = img.shape
    rounds = RING.bit_length() - 1
    return pl.pallas_call(
        relay_kernel,
        out_shape=[
            shape(slot, BF),
            shape(slot, BF),
            shape((D, FF), BF),
            shape((FF // 2, D), BF),
            shape((16, D), F32),
        ],
        in_specs=[smem] * 2 + [vmem] * 6 + [anywhere] * 2,
        out_specs=[anywhere] * 4 + [vmem],
        scratch_shapes=[
            pltpu.VMEM((2, D, FF), BF),
            pltpu.VMEM((FF, D), BF),
            pltpu.VMEM((2, 16, D), F32),
            pltpu.VMEM((2, ROWS, LANE), F32),
            pltpu.VMEM((2,) + slot, BF),
            pltpu.VMEM((2, 2) + image, BF),
            pltpu.VMEM((2,) + image, BF),
            pltpu.VMEM((2,) + image, BF),
            pltpu.VMEM((2, 3) + image, BF),
            pltpu.VMEM((2, 2) + image, BF),
            pltpu.VMEM((2, 2, ROWS, LANE), F32),
            pltpu.VMEM((2, ROWS, 3 * D), F32),
            pltpu.VMEM((2, ROWS, FF), BF),
            pltpu.VMEM((2, 2, ROWS, FF), BF),
            pltpu.VMEM((2, UNITS, PACK * WROWS, LANE), F32),
            pltpu.VMEM((SIDE, GRID + 2, CELL, D), F32),
            pltpu.VMEM(image, F32),
            pltpu.VMEM(image, F32),
            pltpu.VMEM((2, 12, CELL, D), F32),
            pltpu.VMEM((2, 16, D), F32),
            pltpu.VMEM((16, D), F32),
            pltpu.VMEM((2, 2) + image, BF),
            pltpu.VMEM((2, ROWS, FF), BF),
            pltpu.VMEM((2, ROWS, FF), BF),
            pltpu.VMEM((2,) + image, BF),
            pltpu.VMEM((2, RING, COLS + WIDE + REST, COLS), BF),
            pltpu.VMEM((rounds + 1, 16, D), F32),
            pltpu.VMEM((rounds, 16, D), F32),
            dma((14,)),
            dma((14,)),
            dma((14,)),
            dma((2,)),
            dma((2, 2)),
            dma((2, 2)),
            dma((2, 2)),
            dma((2, 2)),
            dma((2, 8)),
            dma((2, 8)),
            dma((2,)),
            dma((2,)),
            dma((2,)),
            dma((2, 2 * RING, 5)),
            dma((2, 2 * RING, 5)),
            dma((2, RING, 5)),
            dma((rounds,)),
            dma((rounds,)),
            dma((4,)),
            dma((4,)),
            dma((2,)),
            dma((2,)),
            dma((2, RING)),
            dma((2, RING)),
            dma((2, RING)),
            dma((2, RING)),
            pltpu.SemaphoreType.REGULAR((2, 5)),
        ],
        name="relay",
        compiler_params=pltpu.CompilerParams(
            collective_id=1, has_side_effects=True, vmem_limit_bytes=63 * 2**20
        ),
    )(wrows, wcols, img, cot, kern, bias, gain, move, first, second)


def finish_kernel(
    out1, out2, act, ing, outs, first, second, acts, ings, kern, bias, gain, move,
    raw1, raw2, full1, full2, acted, graded, wide, small, kernels, rsem, wsem,
):
    steps = rsem.shape[0] - 3

    loads = [
        pltpu.make_async_copy(act, acted, rsem.at[steps]),
        pltpu.make_async_copy(ing, graded, rsem.at[steps + 1]),
        pltpu.make_async_copy(outs, small, rsem.at[steps + 2]),
    ]
    for copy in loads:
        copy.start()
    reads, writes = [], []
    for i in range(steps):
        pair = ((out1, raw1, full1, first), (out2, raw2, full2, second))[i % 2]
        src, raw, full, dst = pair
        half = steps // 2
        rows = pl.ds(i // 2 * (src.shape[0] // half), src.shape[0] // half)
        reads.append((pltpu.make_async_copy(src.at[rows, :], raw.at[rows, :], rsem.at[i]), raw, full, rows))
        writes.append(pltpu.make_async_copy(full.at[rows, :], dst.at[rows, :], wsem.at[i]))
    for copy, *_ in reads:
        copy.start()
    for (copy, raw, full, rows), back in zip(reads, writes):
        copy.wait()
        full[rows, :] = raw[rows, :].astype(F32)
        back.start()
    for copy in loads:
        copy.wait()
    for k in range(9):
        kernels[k] = small[k : k + 1, :]
    for r in range(GRID):
        line = graded[r].astype(F32)
        for k in range(GRID):
            wide[r, k] = line[k : k + 1, :]
    last = [
        pltpu.make_async_copy(acted, acts, wsem.at[steps]),
        pltpu.make_async_copy(wide, ings, wsem.at[steps + 1]),
        pltpu.make_async_copy(kernels, kern, wsem.at[steps + 2]),
    ]
    for i, dst in enumerate((bias, gain, move)):
        last.append(pltpu.make_async_copy(small.at[pl.ds(9 + i, 1), :], dst, wsem.at[steps + 3 + i]))
    for copy in last:
        copy.start()
    for copy in writes + last:
        copy.wait()


def finish(out1, out2, act, ing, outs):
    shape = jax.ShapeDtypeStruct
    slot = act.shape
    anywhere = pl.BlockSpec(memory_space=pl.ANY)
    line = (1, D)
    spread = slot[:2] + line
    steps = 16
    return pl.pallas_call(
        finish_kernel,
        out_shape=[
            shape(out1.shape, F32),
            shape(out2.shape, F32),
            shape(slot, BF),
            shape(spread, F32),
            shape((9,) + line, F32),
            shape(line, F32),
            shape(line, F32),
            shape(line, F32),
        ],
        in_specs=[anywhere] * 5,
        out_specs=[anywhere] * 8,
        scratch_shapes=[
            pltpu.VMEM(out1.shape, out1.dtype),
            pltpu.VMEM(out2.shape, out2.dtype),
            pltpu.VMEM(out1.shape, F32),
            pltpu.VMEM(out2.shape, F32),
            pltpu.VMEM(slot, BF),
            pltpu.VMEM(slot, BF),
            pltpu.VMEM(spread, F32),
            pltpu.VMEM(outs.shape, F32),
            pltpu.VMEM((9,) + line, F32),
            pltpu.SemaphoreType.DMA((steps + 3,)),
            pltpu.SemaphoreType.DMA((steps + 6,)),
        ],
        name="finish",
        compiler_params=pltpu.CompilerParams(vmem_limit_bytes=60 * 2**20),
    )(out1, out2, act, ing, outs)


def per_device(
    images, cotangent, window_rows, window_cols, pos_kernel, pos_bias, norm_gain, norm_shift, first_weight, second_weight
):
    act, ing, out1, out2, outs = relay(
        window_rows, window_cols, images[0], cotangent[0], pos_kernel[0], pos_bias, norm_gain, norm_shift,
        first_weight[0], second_weight,
    )
    if lax.axis_size("dp") > RING:
        out1, out2, outs = lax.psum((out1.astype(F32) / RING, out2.astype(F32) / RING, outs / RING), "dp")
    out1, out2, act, ing, kern, bias, gain, move = finish(out1, out2, act, ing, outs)
    return (
        act[None],
        ing.transpose(2, 0, 1, 3),
        out1[None],
        out2,
        kern.transpose(1, 0, 2),
        bias,
        gain,
        move,
    )


def solution(mesh):
    in_specs = (
        P(("dp", "section"), None, None, None),
        P(("dp", "section"), None, None, None),
        P("dp"),
        P("dp"),
        P("section", None, None),
        P("section", None),
        P("section", None),
        P("section", None),
        P("section", None, None),
        P("section", None),
    )
    out_specs = (
        P(("dp", "section"), None, None, None),
        P(("dp", "section"), None, None, None),
        P("section", None, None),
        P("section", None),
        P("section", None, None),
        P("section", None),
        P("section", None),
        P("section", None),
    )
    return jax.shard_map(per_device, mesh=mesh, in_specs=in_specs, out_specs=out_specs, check_vma=False)
```

```python
from functools import partial

import jax
import jax.numpy as jnp
from jax import lax
from jax.experimental import pallas as pl
from jax.experimental.pallas import tpu as pltpu
from jax.sharding import PartitionSpec as P

D = 768
FF = 3072
HEADS = 24
HEAD = 32
WIN = 7
SIDE = 2
GRID = SIDE * WIN
CELL = 8
WROWS = WIN * CELL
HALF = GRID * CELL
ROWS = SIDE * HALF
GROUP = 256
PACK = GROUP // HEAD
NGROUP = D // GROUP
UNITS = NGROUP * SIDE * SIDE
LANE = 128
FTILE = 512
EPS = 1e-05
SCALE = HEAD ** (-0.5)
BF = jnp.bfloat16
F32 = jnp.float32
MESH = pl.DeviceIdType.MESH


def dot(a, b, ca=1, cb=0):
    return lax.dot_general(a, b, (((ca,), (cb,)), ((), ())), preferred_element_type=F32)


def lanes(index, width=LANE):
    return pl.ds(pl.multiple_of(index * width, width), width)


def halves(value):
    return value.reshape(SIDE, GRID, CELL, value.shape[-1])


def shifts(left, right):
    column = lax.broadcasted_iota(jnp.int32, left.shape, 1)
    before0 = pltpu.roll(left, 1, 1)
    after0 = jnp.where(column == WIN - 1, pltpu.roll(right, CELL - 2, 1), pltpu.roll(left, CELL - 1, 1))
    before1 = jnp.where(column == 0, pltpu.roll(left, 2, 1), pltpu.roll(right, 1, 1))
    after1 = pltpu.roll(right, CELL - 1, 1)
    return ((before0, left, after0), (before1, right, after1))


def gelu_parts(h):
    expo = jnp.exp(h * h * -0.5)
    t = 1.0 / (1.0 + (0.3275911 * 0.7071067811865476) * jnp.abs(h))
    poly = t * (0.127414796 + t * (-0.142248368 + t * (0.7107068705 + t * (-0.7265760135 + t * 0.5307027145))))
    tail = poly * expo
    phi = jnp.where(h >= 0, 1.0 - tail, tail)
    return h * phi, phi + h * expo * 0.3989422804014327


def front_forward(sec, m, ubuf, msk, pr, U, C, zz, xh, rs):
    zero = jnp.zeros((ROWS, LANE), F32)

    def conv(i, total):
        ls = lanes(i)
        u = ubuf[sec, m, :, ls].astype(F32)
        masked = halves(u * msk[m])
        U[0, 1 : GRID + 1, :, ls] = masked[0]
        U[1, 1 : GRID + 1, :, ls] = masked[1]
        moved = shifts(U[0, :, :, ls], U[1, :, :, ls])
        taps = pr[sec, :, ls]
        uh = halves(u)
        sums = []
        for wc in range(SIDE):
            acc = uh[wc] + taps[9:10, :][None]
            for a in range(3):
                for b in range(3):
                    acc = acc + moved[wc][b][a : a + GRID] * taps[3 * a + b : 3 * a + b + 1, :][None]
            acc = acc.reshape(HALF, LANE)
            C[pl.ds(wc * HALF, HALF), ls] = acc
            sums.append(acc)
        return total + jnp.concatenate(sums, axis=0)

    mean = jnp.sum(lax.fori_loop(0, D // LANE, conv, zero, unroll=True), axis=-1, keepdims=True) * (1.0 / D)

    def spread(i, total):
        centred = C[:, lanes(i)] - mean
        return total + centred * centred

    var = jnp.sum(lax.fori_loop(0, D // LANE, spread, zero, unroll=True), axis=-1, keepdims=True) * (1.0 / D)
    rstd = lax.rsqrt(var + EPS)
    rs[sec, m] = jnp.broadcast_to(rstd, (ROWS, LANE))

    def norm(i, carry):
        ls = lanes(i)
        xhat = (C[:, ls] - mean) * rstd
        xh[sec, m, :, ls] = xhat.astype(BF)
        zz[m, 2 * sec, :, ls] = (xhat * pr[sec, 10:11, ls] + pr[sec, 11:12, ls]).astype(BF)
        return carry

    lax.fori_loop(0, D // LANE, norm, 0, unroll=True)


def fold(value):
    return jnp.sum(value.reshape(ROWS // CELL, CELL, LANE), axis=0)


def front_backward(sec, m, msk, pr, U, T, gfull, xh, rs, sgp, out, sent):
    zero = jnp.zeros((ROWS, LANE), F32)

    def sums(i, carry):
        s1, s2 = carry
        ls = lanes(i)
        dz = T[:, ls]
        xhat = xh[sec, m, :, ls].astype(F32)
        both = xhat * dz
        sgp[sec, 10, :, ls] += fold(both)
        sgp[sec, 11, :, ls] += fold(dz)
        gain = pr[sec, 10:11, ls]
        return s1 + dz * gain, s2 + both * gain

    s1, s2 = lax.fori_loop(0, D // LANE, sums, (zero, zero), unroll=True)
    m1 = jnp.sum(s1, axis=-1, keepdims=True) * (1.0 / D)
    m2 = jnp.sum(s2, axis=-1, keepdims=True) * (1.0 / D)

    def back(i, carry):
        ls = lanes(i)
        xhat = xh[sec, m, :, ls].astype(F32)
        inner = T[:, ls] * pr[sec, 10:11, ls] - m1 - xhat * m2
        gc = gfull(i)[...].astype(F32) + rs[sec, m] * inner
        xh[sec, m, :, ls] = gc.astype(BF)
        gh = halves(gc)
        U[0, 1 : GRID + 1, :, ls] = gh[0]
        U[1, 1 : GRID + 1, :, ls] = gh[1]
        moved = shifts(U[0, :, :, ls], U[1, :, :, ls])
        taps = pr[sec, :, ls]
        mask = halves(msk[m])
        du = []
        for wc in range(SIDE):
            acc = jnp.zeros((GRID, CELL, LANE), F32)
            for a in range(3):
                for b in range(3):
                    tap = 3 * a + b
                    acc = acc + moved[wc][2 - b][2 - a : 2 - a + GRID] * taps[tap : tap + 1, :][None]
            du.append((gh[wc] + mask[wc] * acc).reshape(HALF, LANE))
        out(i)[...] = jnp.concatenate(du, axis=0).astype(BF)
        return carry

    lax.fori_loop(0, D // LANE // 2, back, 0, unroll=True)
    sent(0)
    lax.fori_loop(D // LANE // 2, D // LANE, back, 0, unroll=True)
    sent(1)


def front_sums(sec, m, ubuf, msk, U, xh, sgp):
    def part(i, carry):
        ls = lanes(i)
        gc = xh[sec, m, :, ls].astype(F32)
        sgp[sec, 9, :, ls] += fold(gc)
        gh = halves(gc)
        U[0, 1 : GRID + 1, :, ls] = gh[0]
        U[1, 1 : GRID + 1, :, ls] = gh[1]
        moved = shifts(U[0, :, :, ls], U[1, :, :, ls])
        um = halves(ubuf[sec, m, :, ls].astype(F32) * msk[m])
        for a in range(3):
            for b in range(3):
                kg = jnp.zeros((CELL, LANE), F32)
                for wc in range(SIDE):
                    kg = kg + jnp.sum(moved[wc][2 - b][2 - a : 2 - a + GRID] * um[wc], axis=0)
                sgp[sec, 3 * a + b, :, ls] += kg
        return carry

    lax.fori_loop(0, D // LANE, part, 0)


def spread_heads(value, head_of_lane):
    parts = [jnp.where(head_of_lane == h, value, 0.0) for h in range(PACK)]
    return jnp.concatenate(parts, axis=0).astype(BF)


def gather_heads(value, rows, head_of_lane):
    out = jnp.zeros((rows, GROUP), F32)
    for h in range(PACK):
        out = jnp.where(head_of_lane == h, value[h * rows : (h + 1) * rows], out)
    return out


def unit_slices(unit):
    pair, group = unit // NGROUP, lax.rem(unit, NGROUP)
    rows = [pl.ds(pl.multiple_of((2 * pair + w) * WROWS, 8), WROWS) for w in range(2)]
    cols = [pl.ds(pl.multiple_of(part * D + group * GROUP, LANE), GROUP) for part in range(3)]
    return rows, cols


def window_parts(m, i, qkv):
    rows, cols = unit_slices(i)
    head_of_lane = lax.broadcasted_iota(jnp.int32, (WROWS, GROUP), 1) // HEAD
    q = [qkv[m, r, cols[0]].astype(BF) for r in rows]
    kd = [spread_heads(qkv[m, r, cols[1]], head_of_lane) for r in rows]
    vd = [spread_heads(qkv[m, r, cols[2]], head_of_lane) for r in rows]
    return rows, cols, head_of_lane, q, kd, vd


def window_forward(m, qkv, pw, T, group):
    def unit(i):
        rows, cols, head_of_lane, q, kd, vd = window_parts(m, i, qkv)
        s = [(dot(b, a, 1, 1) * SCALE).reshape(PACK, WROWS, WROWS) for a, b in zip(q, kd)]
        key = lax.broadcasted_iota(jnp.int32, s[0].shape, 1)
        real = lax.rem(key, CELL) < WIN
        s = [jnp.where(real, x, -1e30) for x in s]
        p = [jnp.exp(x - jnp.max(x, axis=1, keepdims=True)) for x in s]
        p = [x * (1.0 / jnp.sum(x, axis=1, keepdims=True)) for x in p]
        p = [x.reshape(PACK * WROWS, WROWS) for x in p]
        for w in range(2):
            pw[m, 2 * i + w, :, 0:WROWS] = p[w]
        out = [dot(x.astype(BF), v, 0, 0) for x, v in zip(p, vd)]
        for w in range(2):
            T[rows[w], cols[0]] = out[w]

    for pair in range(UNITS // 2 // NGROUP):
        unit(pair * NGROUP + group)


def window_backward(m, qkv, pw, T):
    def unit(i, carry):
        rows, cols, head_of_lane, q, kd, vd = window_parts(m, i, qkv)
        g = [T[r, cols[0]].astype(BF) for r in rows]
        p = [pw[m, 2 * i + w, :, 0:WROWS].reshape(PACK, WROWS, WROWS) for w in range(2)]
        dp = [dot(v, x, 1, 1).reshape(PACK, WROWS, WROWS) for v, x in zip(vd, g)]
        ds = [x * (y - jnp.sum(x * y, axis=1, keepdims=True)) for x, y in zip(p, dp)]
        ds = [x.reshape(PACK * WROWS, WROWS).astype(BF) for x in ds]
        pb = [x.reshape(PACK * WROWS, WROWS).astype(BF) for x in p]
        dv = [gather_heads(dot(x, y), WROWS, head_of_lane) for x, y in zip(pb, g)]
        dk = [gather_heads(dot(x, y), WROWS, head_of_lane) * SCALE for x, y in zip(ds, q)]
        dq = [dot(x, y, 0, 0) * SCALE for x, y in zip(ds, kd)]
        for w in range(2):
            qkv[m, rows[w], cols[0]] = dq[w]
            qkv[m, rows[w], cols[1]] = dk[w]
            qkv[m, rows[w], cols[2]] = dv[w]
        return carry

    lax.fori_loop(0, UNITS // 2, unit, 0)


def group_slices(group):
    return [pl.ds(pl.multiple_of(part * D + group * GROUP, LANE), GROUP) for part in range(3)]


def channel_forward(m, qkv, pw, zz, msk):
    def unit(i, carry):
        cols = group_slices(i)
        mask = msk[m][:, :1]
        q = qkv[m, :, cols[0]].astype(BF)
        k = (qkv[m, :, cols[1]] * mask).astype(BF)
        v = qkv[m, :, cols[2]].astype(BF)
        s = dot(q, k, 0, 0) * SCALE
        same = (lax.broadcasted_iota(jnp.int32, s.shape, 0) // HEAD) == (lax.broadcasted_iota(jnp.int32, s.shape, 1) // HEAD)
        s = jnp.where(same, s, -1e30)
        p = jnp.exp(s - jnp.max(s, axis=1, keepdims=True))
        p = p * (1.0 / jnp.sum(p, axis=1, keepdims=True))
        for k in range(GROUP // LANE):
            pw[m, 2 * i + k, 0:GROUP, :] = p[:, k * LANE : (k + 1) * LANE]
        zz[m, 1, :, cols[0]] = dot(v, p.astype(BF), 1, 1).astype(BF)
        return carry

    lax.fori_loop(0, NGROUP, unit, 0, unroll=True)


def channel_backward(m, qkv, pw, T, rr, msk):
    def unit(i, carry):
        cols = group_slices(i)
        mask = msk[m][:, :1]
        q = qkv[m, :, cols[0]].astype(BF)
        k = (qkv[m, :, cols[1]] * mask).astype(BF)
        v = qkv[m, :, cols[2]].astype(BF)
        g = T[:, cols[0]].astype(BF)
        p = jnp.concatenate([pw[m, 2 * i + k, 0:GROUP, :] for k in range(GROUP // LANE)], axis=1)
        dp = dot(g, v, 0, 0)
        ds = (p * (dp - jnp.sum(p * dp, axis=1, keepdims=True))).astype(BF)
        rr[m, 0, :, cols[0]] = (dot(k, ds, 1, 1) * SCALE).astype(BF)
        rr[m, 0, :, cols[1]] = (dot(q, ds) * (SCALE * mask)).astype(BF)
        rr[m, 0, :, cols[2]] = (dot(g, p.astype(BF))).astype(BF)
        return carry

    lax.fori_loop(0, NGROUP, unit, 0, unroll=True)


RING = 8
COLS = FF // RING
WIDE = FF // 12 * 8 // RING
REST = FF // 3 // RING
THIRD = FF // 3 * 2
LENT = RING * 3 // 4
EARLY = 2


def relay_kernel(
    wrows, wcols, img, cot, kern, bias, gain, move, first, second,
    act, ing, out1, out2, outs,
    wf, w2, pr, msk, flat, ubuf, gin, gout, zz, xh, rs, qkv, ab, rr, pw, U, C, T, sgp, sgs, sgm,
    rL, rR, rA, rG, buf, acc, got,
    wl, ws, wr, pl_, usem, gsem, us, gs, ss, rsem, es, er, sgsem, ssem, rcem, osem, sms, smr, xs, xr, ys, yr, bs, br, hs, hr, free,
):
    n = RING
    s = lax.axis_index("section")
    dp = lax.axis_index("dp")
    stage, c = s // 2, lax.rem(s, 2)
    mate = (dp, stage * 2 + (1 - c))
    opposite = (dp, (1 - stage) * 2 + c)
    diagonal = (dp, 3 - s)
    lender, helper = s == 1, s == 2
    early = stage == 0

    spot = lax.rem(dp, n)
    base = dp - spot
    me = jnp.where(lax.rem(spot, 2) == 0, spot // 2, n - 1 - spot // 2)

    def place(pos):
        pos = lax.rem(pos + 2 * n, n)
        return (base + jnp.where(pos < n // 2, 2 * pos, 2 * (n - 1 - pos) + 1), s)

    nexts = (place(me + 1), place(me - 1))
    rounds = n.bit_length() - 1
    partners = []
    for r in range(rounds):
        bit = 1 << r
        partners.append((jnp.where(lax.rem(spot // bit, 2) == 0, dp + bit, dp - bit), s))

    barrier = pltpu.get_barrier_semaphore()
    peers = [mate, opposite, diagonal, *nexts, *partners]
    for peer in peers:
        pl.semaphore_signal(barrier, inc=1, device_id=peer, device_id_type=MESH)
    pl.semaphore_wait(barrier, len(peers))

    def remote(src, dst, send, recv, peer):
        return pltpu.make_async_remote_copy(
            src_ref=src, dst_ref=dst, send_sem=send, recv_sem=recv, device_id=peer, device_id_type=MESH
        )

    half = second.shape[0]

    def group_part(group, part):
        cols = pl.ds(pl.multiple_of(part * D + group * GROUP, LANE), GROUP)
        return first.at[:, cols], wf.at[0, :, cols]

    def wait_group(group):
        for part in range(3):
            src, dst = group_part(group, part)
            i = group * 3 + part

            @pl.when(c == 0)
            def _():
                pltpu.make_async_copy(src, dst, wl.at[i]).wait()

            @pl.when(c == 1)
            def _():
                remote(src, dst, ws.at[i], wr.at[i], mate).wait_recv()

    def weight_parts(k):
        parts = []
        if k == 0:
            for group in range(NGROUP):
                for part in range(3):
                    parts.append(group_part(group, part))
            cols = pl.ds(3 * D, D)
            parts.append((first.at[:, cols], wf.at[k, :, cols]))
        else:
            for i in range(3):
                cols = pl.ds(i * (FF // 3), FF // 3)
                parts.append((first.at[:, cols], wf.at[k, :, cols]))
        third = half // 3
        for i in range(3):
            rows = pl.ds(i * third, third)
            parts.append((second.at[rows, :], w2.at[pl.ds(k * half + i * third, third), :]))
        return parts

    names = (
        [f"qkv{group}" for group in range(NGROUP) for _ in range(3)] + ["out"] + [f"low{i}" for i in range(3)],
        ["in"] * 3 + [f"high{i}" for i in range(3)],
    )

    def weight_copies(k):
        local = [pltpu.make_async_copy(a, b, wl.at[i]) for i, (a, b) in enumerate(weight_parts(k))]
        sent = [remote(a, b, ws.at[i], wr.at[i], mate) for i, (a, b) in enumerate(weight_parts(k))]
        return local, sent

    def params_copy(k):
        return remote(pr.at[k], pr.at[k], ws.at[13], wr.at[13], mate)

    pr[c, 0:9, :] = kern[...].astype(F32)
    pr[c, 9:10, :] = bias[...].astype(F32)
    pr[c, 10:11, :] = gain[...].astype(F32)
    pr[c, 11:12, :] = move[...].astype(F32)
    params_copy(c).start()
    for k in range(2):

        @pl.when(c == k)
        def _():
            local, sent = weight_copies(k)
            for here, there in zip(local, sent):
                here.start()
                there.start()

    def wait_weights(*wanted):
        for k in range(2):

            @pl.when(c == k)
            def _():
                for name, copy in zip(names[k], weight_copies(k)[0]):
                    if name in wanted:
                        copy.wait()
                for name, copy in zip(names[1 - k], weight_copies(1 - k)[1]):
                    if name in wanted:
                        copy.wait_recv()

    def wait_params(k):
        @pl.when(c != k)
        def _():
            params_copy(k).wait_recv()

    raw = flat.at[0]
    img_out = remote(img, raw, pl_.at[0], pl_.at[1], opposite)
    cot_out = remote(cot, raw, pl_.at[0], pl_.at[1], opposite)

    def pad(src, dst):
        blank = jnp.zeros((CELL - WIN, D), F32)
        for r in range(GRID):
            line = src[r].astype(F32)
            for wc in range(SIDE):
                cells = jnp.concatenate([line[wc * WIN : (wc + 1) * WIN], blank], axis=0)
                C[pl.ds(wc * HALF + r * CELL, CELL), :] = cells
        dst[...] = C[...].astype(BF)

    def unpad(dst):
        for r in range(GRID):
            sides = [C[pl.ds(wc * HALF + r * CELL, CELL), :][:WIN] for wc in range(SIDE)]
            dst[r] = jnp.concatenate(sides, axis=0).astype(BF)

    @pl.when(early)
    def _():
        cot_out.start()
        pad(img, ubuf.at[0, 0])

    @pl.when(jnp.logical_not(early))
    def _():
        img_out.start()
        pad(cot, gin.at[1])

    index = lax.broadcasted_iota(jnp.int32, (ROWS, LANE), 0)
    cell = lax.rem(index, CELL)
    row = lax.rem(index, HALF) // CELL
    column = (index // HALF) * WIN + cell
    for m in range(2):
        inside = (row < WIN * wrows[c + 2 * m]) & (column < WIN * wcols[c + 2 * m]) & (cell < WIN)
        msk[m] = jnp.where(inside, 1.0, 0.0)

    @pl.when(jnp.logical_not(early))
    def _():
        cot_out.wait_recv()
        pad(raw, gin.at[0])
        for m in range(2):
            for l in range(D // LANE):
                cols = pl.ds(l * LANE, LANE)
                gin[m, :, cols] = (gin[m, :, cols].astype(F32) * msk[m]).astype(BF)

    for wc in range(SIDE):
        U[wc, 0] = jnp.zeros((CELL, D), F32)
        U[wc, GRID + 1] = jnp.zeros((CELL, D), F32)
    sgp[...] = jnp.zeros(sgp.shape, F32)

    def hop(m, dst, send, recv):
        sides = [pl.ds(i * D // 2, D // 2) for i in range(2)]
        return [
            remote(gout.at[m, :, cols], dst.at[:, cols], send.at[m, i], recv.at[m, i], opposite)
            for i, cols in enumerate(sides)
        ]

    def u_hop(m):
        return hop(m, ubuf.at[0, m], us, usem)

    def g_hop(m):
        return hop(m, gin.at[m], gs, gsem)

    def factor_copies(k, m):
        if k == 0:
            parts = [
                ("F", zz.at[m, 0], rL.at[m, 0]),
                ("F", zz.at[m, 1], rL.at[m, 1]),
                ("A", rr.at[m, 0, :, pl.ds(3 * D, D)], rR.at[m, :, pl.ds(3 * D, D)]),
                ("A", rr.at[m, 0, :, pl.ds(0, 3 * D)], rR.at[m, :, pl.ds(0, 3 * D)]),
            ]
        else:
            parts = [
                ("F", zz.at[m, 2], rL.at[m, 0]),
                ("M", gin.at[m], rG.at[m]),
            ]
            parts.append(("F", ab.at[m], rA.at[m]))
            for i, cols in enumerate((pl.ds(0, FF // 3 * 2), pl.ds(FF // 3 * 2, FF // 3))):
                parts.append((f"H{i}", rr.at[m, 1, :, cols], rR.at[m, :, cols]))
        return [(w, remote(a, b, ss.at[m, i], rsem.at[m, i], mate)) for i, (w, a, b) in enumerate(parts)]

    def start_factors(m, which):
        for k in range(2):

            @pl.when(c != k)
            def _():
                for when, copy in factor_copies(k, m):
                    if when == which:
                        copy.start()

    def wait_factors(which):
        for k in range(2):

            @pl.when(c == k)
            def _():
                for m in range(2):
                    for when, copy in factor_copies(k, m):
                        if when[0] in which:
                            copy.wait_recv()

    def shard(k):
        return lax.rem(k + 4 * n, n)

    def sign(h):
        return 1 if h == 0 else -1

    def home(h, t):
        return shard(me + sign(h) - sign(h) * t)

    def products(terms):
        total = None
        for a, b in terms:
            part = dot(a[...], b[...], 0, 0)
            total = part if total is None else total + part
        return total

    def tile(sub, h, j):
        side = pl.ds(h * COLS, COLS)
        if sub in (0, 4):
            rows = first_rows(sub, h)
            last = jnp.where(j >= (3 * n) // 4, 1, 0)
            own = jnp.where(c == 1, 2, last)
            other = jnp.where(c == 1, 0, last)
            cols = lanes(j, COLS)
            terms = [(zz.at[m, own, :, rows], rr.at[m, c, :, cols]) for m in range(2)]
            terms += [(rL.at[m, other, :, rows], rR.at[m, :, cols]) for m in range(2)]
        elif sub == 3:
            cols = [pl.ds(pl.multiple_of(i * LENT * REST + j * REST, LANE), REST) for i in range(2)]
            terms = [(rA.at[m, :, cols[0]], rG.at[m, :, side]) for m in range(2)]
            terms += [(rA.at[m, :, cols[1]], gout.at[m, :, side]) for m in range(2)]
        else:
            cols = lanes(j, WIDE) if sub == 1 else pl.ds(pl.multiple_of(THIRD + j * REST, LANE), REST)
            terms = [(ab.at[m, :, cols], gin.at[m, :, side]) for m in range(2)]
            terms += [(rA.at[m, :, cols], rG.at[m, :, side]) for m in range(2)]
        return products(terms)

    sizes = (COLS // 3 * 2, WIDE, REST, REST, COLS // 3)
    starts = (0, COLS, COLS + WIDE, COLS + WIDE, COLS // 3 * 2)
    parts = [pl.ds(start, size) for start, size in zip(starts, sizes)]
    subs = range(len(sizes))
    odd = c == 1
    active = (None, odd, odd, helper, None)

    def where_live(sub, j, run):
        if sub == 2:
            pl.when(jnp.logical_not(lender) | (j >= LENT))(run)
        elif sub == 3:
            pl.when(j < LENT)(run)
        else:
            run()

    def first_rows(sub, h):
        return pl.ds(h * COLS + (0 if sub == 0 else sizes[0]), sizes[sub])

    def where_active(sub, run):
        if active[sub] is None:
            run()
        else:
            pl.when(active[sub])(run)


    def gathered(sub, h, j):
        if sub in (0, 4):
            return wf.at[0, first_rows(sub, h), lanes(j, COLS)]
        first_row = 0 if sub == 1 else THIRD
        return w2.at[pl.ds(pl.multiple_of(first_row + j * sizes[sub], 16), sizes[sub]), pl.ds(h * COLS, COLS)]

    def scatter(h, t, sub):
        src, dst = buf.at[h, t, parts[sub], :], buf.at[h, t + 1, parts[sub], :]
        return remote(src, dst, ssem.at[h, t, sub], rcem.at[h, t + 1, sub], nexts[h])

    def spread(h, t, sub, j):
        ref = gathered(sub, h, j)
        return remote(ref, ref, ssem.at[h, n - 1 + t, sub], rcem.at[h, n + t, sub], nexts[h])

    half_shards = n * 3 // 4

    def write(h, j, sub):
        src, side = gathered(sub, h, j), pl.ds(h * COLS, COLS)
        if sub in (0, 4):
            dst = out1.at[first_rows(sub, h), lanes(j, COLS)]
        elif sub == 1:
            dst = out2.at[pl.ds(pl.multiple_of((j - half_shards) * WIDE, 16), WIDE), side]
        else:
            dst = out2.at[pl.ds(pl.multiple_of(THIRD - FF // 2 + j * REST, 16), REST), side]
        if sub == 3:
            return remote(src, dst, bs.at[h, j], br.at[h, j], diagonal)
        return pltpu.make_async_copy(src, dst, osem.at[h, j, sub])

    def hand_over(h, j):
        dst = out2.at[pl.ds(pl.multiple_of(j * WIDE, 16), WIDE), pl.ds(h * COLS, COLS)]
        return remote(gathered(1, h, j), dst, hs.at[h, j], hr.at[h, j], mate)

    def deliver(h, j, sub):
        if sub == 1:

            @pl.when(j < half_shards)
            def _():
                hand_over(h, j).start()

            @pl.when(j >= half_shards)
            def _():
                write(h, j, sub).start()

        else:
            write(h, j, sub).start()

    def lend(m):
        cols, there = pl.ds(THIRD, LENT * REST), [rA.at[m, :, pl.ds(i * LENT * REST, LENT * REST)] for i in range(2)]
        return (
            remote(ab.at[m, :, cols], there[0], xs.at[m], xr.at[m], diagonal),
            remote(rA.at[m, :, cols], there[1], xs.at[2 + m], xr.at[2 + m], diagonal),
        )

    def share(m):
        return remote(gout.at[m], rG.at[m], ys.at[m], yr.at[m], mate)

    def reduce_event(sub, h, e):
        j = shard(me - sign(h) * e)

        @pl.when(e == n - 1)
        def _():
            pl.semaphore_wait(free.at[h, sub], 1)

        def run():
            total = tile(sub, h, j)

            @pl.when(e == 0)
            def _():
                buf[h, 0, parts[sub], :] = total.astype(BF)
                scatter(h, 0, sub).start()

            @pl.when((e > 0) & (e < n - 1))
            def _():
                scatter(h, e - 1, sub).wait_recv()
                buf[h, e, parts[sub], :] = (total + buf[h, e, parts[sub], :].astype(F32)).astype(BF)
                scatter(h, e, sub).start()

            @pl.when(e == n - 1)
            def _():
                scatter(h, n - 2, sub).wait_recv()
                gathered(sub, h, j)[...] = (total + buf[h, n - 1, parts[sub], :].astype(F32)).astype(BF)
                spread(h, 0, sub, j).start()
                deliver(h, j, sub)

        where_live(sub, j, run)

    def event(sub, e):
        for h in range(2):

            @pl.when(e < n)
            def _():
                reduce_event(sub, h, e)

            @pl.when((e >= n) & (e < 2 * n - 1))
            def _():
                t = e - (n - 1)
                j = home(h, t)

                def run():
                    spread(h, t - 1, sub, j).wait_recv()

                    @pl.when(t < n - 1)
                    def _():
                        spread(h, t, sub, j).start()

                    deliver(h, j, sub)

                where_live(sub, j, run)

    def early_event(e, which):
        @pl.when(odd)
        def _():
            for sub in which:
                where_active(sub, lambda: event(sub, e))

    def small(r):
        return remote(acc.at[r], got.at[r], sms.at[r], smr.at[r], partners[r])

    def mlp(m, order, wait):
        total, before, last = C[...], None, None
        for t in order:
            cols = pl.ds(t * FTILE, FTILE)
            h = dot(zz[m, 2], wf[1, :, cols])
            if last is not None:
                wait(last)
                total = total + dot(before, w2[pl.ds(last * FTILE, FTILE), :])
            a, d = gelu_parts(h)
            before, last = a.astype(BF), t
            ab[m, :, cols] = before
            rr[m, 1, :, cols] = d.astype(BF)
        wait(last)
        for i in range(2):
            cols = pl.ds(i * D // 2, D // 2)
            part = total[:, i * D // 2 : (i + 1) * D // 2]
            gout[jnp.where(early, m, 2 + m), :, cols] = (part + dot(before, w2[pl.ds(last * FTILE, FTILE), cols])).astype(BF)

            @pl.when(early)
            def _():
                u_hop(m)[i].start()

    def give_results(m):
        @pl.when(early)
        def _():
            C[...] = gout[m].astype(F32)

        @pl.when(jnp.logical_not(early))
        def _():
            for l in range(D // LANE):
                cols = pl.ds(l * LANE, LANE)
                C[:, cols] = gout[2 + m, :, cols].astype(F32) * msk[m]

        unpad(flat.at[m])

        @pl.when(early & (m == 0))
        def _():
            pltpu.make_async_copy(flat.at[0], ing, es.at[1]).start()

        @pl.when(early & (m == 1))
        def _():
            remote(flat.at[1], ing, es.at[1], er.at[1], opposite).start()

        @pl.when(jnp.logical_not(early) & (m == 0))
        def _():
            remote(flat.at[0], act, es.at[0], er.at[0], opposite).start()

        @pl.when(jnp.logical_not(early) & (m == 1))
        def _():
            pltpu.make_async_copy(flat.at[1], act, es.at[0]).start()

    def forward(m, p):
        @pl.when(jnp.logical_not(early))
        def _():
            for copy in u_hop(m):
                copy.wait_recv()

        @pl.when(early & (m == 1))
        def _():
            img_out.wait_recv()
            pad(raw, ubuf.at[0, 1])

        once = p == 0
        starting = early & once

        @pl.when(once)
        def _():
            wait_params(0)

        @pl.when(once & jnp.logical_not(early))
        def _():
            wait_params(1)
            wait_weights(*set(names[0] + names[1]))

        front_forward(0, m, ubuf, msk, pr, U, C, zz, xh, rs)

        @pl.when(early)
        def _():
            def head_group(group, carry):
                @pl.when(once)
                def _():
                    wait_group(group)

                for part in range(3):
                    cols = pl.ds(pl.multiple_of(part * D + group * GROUP, LANE), GROUP)
                    qkv[m, :, cols] = dot(zz[m, 0], wf[0, :, cols])
                window_forward(m, qkv, pw, T, group)
                return carry

            lax.fori_loop(0, NGROUP, head_group, 0)
            zz[m, 1] = T[...].astype(BF)

        @pl.when(starting)
        def _():
            wait_weights("out")
            wait_params(1)

        @pl.when(jnp.logical_not(early))
        def _():
            for i in range(3):
                qkv[m, :, pl.ds(i * D, D)] = dot(zz[m, 0], wf[0, :, pl.ds(i * D, D)])

        @pl.when(jnp.logical_not(early))
        def _():
            channel_forward(m, qkv, pw, zz, msk)

        ubuf[1, m] = (C[...] + dot(zz[m, 1], wf[0, :, pl.ds(3 * D, D)])).astype(BF)

        front_forward(1, m, ubuf, msk, pr, U, C, zz, xh, rs)

        @pl.when(starting)
        def _():
            wait_weights("in")
            order = [i + 3 * k for i in range(3) for k in range(2)]
            mlp(m, order, lambda t: wait_weights(f"low{t}" if t < 3 else f"high{t - 3}"))

        @pl.when(jnp.logical_not(starting))
        def _():
            mlp(m, range(FF // FTILE), lambda t: None)

        start_factors(m, "F")

        @pl.when(early & (m == 1))
        def _():
            wait_factors("F")

        @pl.when(lender & (m == 1))
        def _():
            for i in range(2):
                for copy in lend(i):
                    copy.start()

    def backward(m):
        @pl.when(early)
        def _():
            for copy in g_hop(m):
                copy.wait_recv()
            start_factors(m, "M")

        for t in range(FF // FTILE):
            cols = pl.ds(t * FTILE, FTILE)
            da = dot(gin[m], w2[cols, :], 1, 1)
            rr[m, 1, :, cols] = (da * rr[m, 1, :, cols].astype(F32)).astype(BF)
            if t == FF // FTILE * 2 // 3 - 1:
                start_factors(m, "H0")

        start_factors(m, "H1")

        @pl.when(m == 1)
        def _():
            @pl.when(jnp.logical_not(early))
            def _():
                wait_factors("F")

            wait_factors("M")
            early_event(0, (1, 2))

        T[...] = dot(rr[m, 1], wf[1], 1, 1)

        @pl.when(m == 1)
        def _():
            wait_factors("H")
            early_event(0, (0, 4))

        last = pl.ds(3 * D, D)

        @pl.when(early)
        def _():
            for copy in u_hop(m):
                copy.wait_send()

        def tail_lanes(i):
            return rr.at[m, 0, :, pl.ds(pl.multiple_of(3 * D + i * LANE, LANE), LANE)]

        def nothing(half):
            pass

        front_backward(1, m, msk, pr, U, T, lambda i: gin.at[m, :, lanes(i)], xh, rs, sgp, tail_lanes, nothing)

        T[...] = dot(rr[m, 0, :, last], wf[0, :, last], 1, 1)

        @pl.when(early)
        def _():
            window_backward(m, qkv, pw, T)
            for i in range(3):
                cols = pl.ds(i * D, D)
                rr[m, 0, :, cols] = qkv[m, :, cols].astype(BF)

        @pl.when(jnp.logical_not(early))
        def _():
            channel_backward(m, qkv, pw, T, rr, msk)

        start_factors(m, "A")

        @pl.when(m == 1)
        def _():
            for e in range(1, EARLY):
                early_event(e, (1, 2, 0, 4))

        T[...] = dot(rr[m, 0, :, pl.ds(0, 3 * D)], wf[0, :, pl.ds(0, 3 * D)], 1, 1)
        def send_half(half):
            @pl.when(jnp.logical_not(early))
            def _():
                g_hop(m)[half].start()

        front_backward(
            0, m, msk, pr, U, T, tail_lanes, xh, rs, sgp, lambda i: gout.at[m, :, lanes(i)], send_half
        )

        @pl.when(s == 3)
        def _():
            share(m).start()

    @pl.when(jnp.logical_not(early))
    def _():
        for m in range(2):
            start_factors(m, "M")

    def phase(p, carry):
        m = jnp.where(early, lax.rem(p, 2), p // 2)
        ahead = jnp.where(early, p < 2, lax.rem(p, 2) == 0)

        @pl.when(ahead)
        def _():
            forward(m, p)

        @pl.when(jnp.logical_not(ahead))
        def _():
            backward(m)

        return carry

    lax.fori_loop(0, 4, phase, 0)

    for h in range(2):
        for sub in subs:

            def ready():
                pl.semaphore_signal(free.at[h, sub], inc=1, device_id=nexts[1 - h], device_id_type=MESH)

            where_active(sub, ready)

    give = remote(sgs.at[1 - c], sgm, sgsem.at[0], sgsem.at[1], mate)

    def small_sums():
        for sec in range(2):
            for j in range(12):
                sgs[sec, j : j + 1, :] = jnp.sum(sgp[sec, j], axis=0, keepdims=True)
            sgs[sec, 12:16, :] = jnp.zeros((4, D), F32)
        give.start()

    wait_factors("A")

    @pl.when(helper)
    def _():
        for m in range(2):
            for copy in lend(m):
                copy.wait_recv()
            share(m).wait_recv()

    def ring_step(t, carry):
        for sub in (0, 4):
            event(sub, t + jnp.where(odd, EARLY, 0))
        where_active(1, lambda: event(1, t + EARLY))
        where_active(2, lambda: event(2, t + EARLY))
        where_active(3, lambda: event(3, t))
        @pl.when((t >= 1) & (t < 5))
        def _():
            front_sums((t - 1) // 2, lax.rem(t - 1, 2), ubuf, msk, U, xh, sgp)

        pl.when(t == 5)(small_sums)

        @pl.when((t >= 6) & (t < 8))
        def _():
            give_results(t - 6)

        for r in range(rounds + 1):

            @pl.when(t == 6 + 2 * r)
            def _():
                if r == 0:
                    give.wait_recv()
                    acc[0] = sgs[c] + sgm[...]
                else:
                    small(r - 1).wait_recv()
                    acc[r] = acc[r - 1] + got[r - 1]
                if r < rounds:
                    small(r).start()

        return carry

    lax.fori_loop(0, 2 * n - 1, ring_step, 0)
    outs[...] = acc[rounds]

    for k in range(2):

        @pl.when(c == k)
        def _():
            for copy in weight_copies(k)[1]:
                copy.wait_send()
            params_copy(k).wait_send()
            for m in range(2):
                for _when, copy in factor_copies(1 - k, m):
                    copy.wait_send()

    give.wait_send()
    for r in range(rounds):
        small(r).wait_send()

    def drain(t, carry):
        for h in range(2):
            for sub in subs:

                def sent():
                    where_live(sub, shard(me - sign(h) * t), lambda: scatter(h, t, sub).wait_send())
                    where_live(sub, home(h, t), lambda: spread(h, t, sub, home(h, t)).wait_send())

                where_active(sub, sent)

        return carry

    lax.fori_loop(0, n - 1, drain, 0)

    def written(j, carry):
        for h in range(2):
            write(h, j, 0).wait()
            write(h, j, 4).wait()

            @pl.when(odd)
            def _():
                where_live(2, j, lambda: write(h, j, 2).wait())

                @pl.when(j < half_shards)
                def _():
                    hand_over(h, j).wait_send()

                @pl.when(j >= half_shards)
                def _():
                    write(h, j, 1).wait()

            @pl.when(jnp.logical_not(odd) & (j < half_shards))
            def _():
                hand_over(h, j).wait_recv()

            @pl.when(helper & (j < LENT))
            def _():
                write(h, j, 3).wait_send()

            @pl.when(lender & (j < LENT))
            def _():
                write(h, j, 3).wait_recv()

        return carry

    lax.fori_loop(0, n, written, 0)

    @pl.when(lender)
    def _():
        for m in range(2):
            for copy in lend(m):
                copy.wait_send()

    @pl.when(s == 3)
    def _():
        for m in range(2):
            share(m).wait_send()

    @pl.when(early)
    def _():
        cot_out.wait_send()
        pltpu.make_async_copy(flat.at[0], ing, es.at[1]).wait()
        remote(flat.at[1], ing, es.at[1], er.at[1], opposite).wait_send()
        remote(flat.at[0], act, es.at[0], er.at[0], opposite).wait_recv()

    @pl.when(jnp.logical_not(early))
    def _():
        img_out.wait_send()
        for m in range(2):
            for copy in g_hop(m):
                copy.wait_send()
        remote(flat.at[0], act, es.at[0], er.at[0], opposite).wait_send()
        pltpu.make_async_copy(flat.at[1], act, es.at[0]).wait()
        remote(flat.at[1], ing, es.at[1], er.at[1], opposite).wait_recv()


def relay(wrows, wcols, img, cot, kern, bias, gain, move, first, second):
    shape = jax.ShapeDtypeStruct
    vmem = pl.BlockSpec(memory_space=pltpu.VMEM)
    anywhere = pl.BlockSpec(memory_space=pl.ANY)
    dma = pltpu.SemaphoreType.DMA
    smem = pl.BlockSpec(memory_space=pltpu.SMEM)
    image = (ROWS, D)
    slot = img.shape
    rounds = RING.bit_length() - 1
    return pl.pallas_call(
        relay_kernel,
        out_shape=[
            shape(slot, BF),
            shape(slot, BF),
            shape((D, FF), BF),
            shape((FF // 2, D), BF),
            shape((16, D), F32),
        ],
        in_specs=[smem] * 2 + [vmem] * 6 + [anywhere] * 2,
        out_specs=[anywhere] * 4 + [vmem],
        scratch_shapes=[
            pltpu.VMEM((2, D, FF), BF),
            pltpu.VMEM((FF, D), BF),
            pltpu.VMEM((2, 16, D), F32),
            pltpu.VMEM((2, ROWS, LANE), F32),
            pltpu.VMEM((2,) + slot, BF),
            pltpu.VMEM((2, 2) + image, BF),
            pltpu.VMEM((2,) + image, BF),
            pltpu.VMEM((4,) + image, BF),
            pltpu.VMEM((2, 3) + image, BF),
            pltpu.VMEM((2, 2) + image, BF),
            pltpu.VMEM((2, 2, ROWS, LANE), F32),
            pltpu.VMEM((2, ROWS, 3 * D), F32),
            pltpu.VMEM((2, ROWS, FF), BF),
            pltpu.VMEM((2, 2, ROWS, FF), BF),
            pltpu.VMEM((2, UNITS, PACK * WROWS, LANE), F32),
            pltpu.VMEM((SIDE, GRID + 2, CELL, D), F32),
            pltpu.VMEM(image, F32),
            pltpu.VMEM(image, F32),
            pltpu.VMEM((2, 12, CELL, D), F32),
            pltpu.VMEM((2, 16, D), F32),
            pltpu.VMEM((16, D), F32),
            pltpu.VMEM((2, 2) + image, BF),
            pltpu.VMEM((2, ROWS, FF), BF),
            pltpu.VMEM((2, ROWS, FF), BF),
            pltpu.VMEM((2,) + image, BF),
            pltpu.VMEM((2, RING, COLS + WIDE + REST, COLS), BF),
            pltpu.VMEM((rounds + 1, 16, D), F32),
            pltpu.VMEM((rounds, 16, D), F32),
            dma((14,)),
            dma((14,)),
            dma((14,)),
            dma((2,)),
            dma((2, 2)),
            dma((2, 2)),
            dma((2, 2)),
            dma((2, 2)),
            dma((2, 8)),
            dma((2, 8)),
            dma((2,)),
            dma((2,)),
            dma((2,)),
            dma((2, 2 * RING, 5)),
            dma((2, 2 * RING, 5)),
            dma((2, RING, 5)),
            dma((rounds,)),
            dma((rounds,)),
            dma((4,)),
            dma((4,)),
            dma((2,)),
            dma((2,)),
            dma((2, RING)),
            dma((2, RING)),
            dma((2, RING)),
            dma((2, RING)),
            pltpu.SemaphoreType.REGULAR((2, 5)),
        ],
        name="relay",
        compiler_params=pltpu.CompilerParams(
            collective_id=1, has_side_effects=True, vmem_limit_bytes=63 * 2**20
        ),
    )(wrows, wcols, img, cot, kern, bias, gain, move, first, second)


def finish_kernel(
    out1, out2, act, ing, outs, first, second, acts, ings, kern, bias, gain, move,
    raw1, raw2, full1, full2, acted, graded, wide, small, kernels, rsem, wsem,
):
    steps = rsem.shape[0] - 3

    loads = [
        pltpu.make_async_copy(act, acted, rsem.at[steps]),
        pltpu.make_async_copy(ing, graded, rsem.at[steps + 1]),
        pltpu.make_async_copy(outs, small, rsem.at[steps + 2]),
    ]
    for copy in loads:
        copy.start()
    reads, writes = [], []
    for i in range(steps):
        pair = ((out1, raw1, full1, first), (out2, raw2, full2, second))[i % 2]
        src, raw, full, dst = pair
        half = steps // 2
        rows = pl.ds(i // 2 * (src.shape[0] // half), src.shape[0] // half)
        reads.append((pltpu.make_async_copy(src.at[rows, :], raw.at[rows, :], rsem.at[i]), raw, full, rows))
        writes.append(pltpu.make_async_copy(full.at[rows, :], dst.at[rows, :], wsem.at[i]))
    for copy, *_ in reads:
        copy.start()
    for (copy, raw, full, rows), back in zip(reads, writes):
        copy.wait()
        full[rows, :] = raw[rows, :].astype(F32)
        back.start()
    for copy in loads:
        copy.wait()
    for k in range(9):
        kernels[k] = small[k : k + 1, :]
    for r in range(GRID):
        line = graded[r].astype(F32)
        for k in range(GRID):
            wide[r, k] = line[k : k + 1, :]
    last = [
        pltpu.make_async_copy(acted, acts, wsem.at[steps]),
        pltpu.make_async_copy(wide, ings, wsem.at[steps + 1]),
        pltpu.make_async_copy(kernels, kern, wsem.at[steps + 2]),
    ]
    for i, dst in enumerate((bias, gain, move)):
        last.append(pltpu.make_async_copy(small.at[pl.ds(9 + i, 1), :], dst, wsem.at[steps + 3 + i]))
    for copy in last:
        copy.start()
    for copy in writes + last:
        copy.wait()


def finish(out1, out2, act, ing, outs):
    shape = jax.ShapeDtypeStruct
    slot = act.shape
    anywhere = pl.BlockSpec(memory_space=pl.ANY)
    line = (1, D)
    spread = slot[:2] + line
    steps = 16
    return pl.pallas_call(
        finish_kernel,
        out_shape=[
            shape(out1.shape, F32),
            shape(out2.shape, F32),
            shape(slot, BF),
            shape(spread, F32),
            shape((9,) + line, F32),
            shape(line, F32),
            shape(line, F32),
            shape(line, F32),
        ],
        in_specs=[anywhere] * 5,
        out_specs=[anywhere] * 8,
        scratch_shapes=[
            pltpu.VMEM(out1.shape, out1.dtype),
            pltpu.VMEM(out2.shape, out2.dtype),
            pltpu.VMEM(out1.shape, F32),
            pltpu.VMEM(out2.shape, F32),
            pltpu.VMEM(slot, BF),
            pltpu.VMEM(slot, BF),
            pltpu.VMEM(spread, F32),
            pltpu.VMEM(outs.shape, F32),
            pltpu.VMEM((9,) + line, F32),
            pltpu.SemaphoreType.DMA((steps + 3,)),
            pltpu.SemaphoreType.DMA((steps + 6,)),
        ],
        name="finish",
        compiler_params=pltpu.CompilerParams(vmem_limit_bytes=60 * 2**20),
    )(out1, out2, act, ing, outs)


def per_device(
    images, cotangent, window_rows, window_cols, pos_kernel, pos_bias, norm_gain, norm_shift, first_weight, second_weight
):
    act, ing, out1, out2, outs = relay(
        window_rows, window_cols, images[0], cotangent[0], pos_kernel[0], pos_bias, norm_gain, norm_shift,
        first_weight[0], second_weight,
    )
    if lax.axis_size("dp") > RING:
        out1, out2, outs = lax.psum((out1.astype(F32) / RING, out2.astype(F32) / RING, outs / RING), "dp")
    out1, out2, act, ing, kern, bias, gain, move = finish(out1, out2, act, ing, outs)
    return (
        act[None],
        ing.transpose(2, 0, 1, 3),
        out1[None],
        out2,
        kern.transpose(1, 0, 2),
        bias,
        gain,
        move,
    )


def solution(mesh):
    in_specs = (
        P(("dp", "section"), None, None, None),
        P(("dp", "section"), None, None, None),
        P("dp"),
        P("dp"),
        P("section", None, None),
        P("section", None),
        P("section", None),
        P("section", None),
        P("section", None, None),
        P("section", None),
    )
    out_specs = (
        P(("dp", "section"), None, None, None),
        P(("dp", "section"), None, None, None),
        P("section", None, None),
        P("section", None),
        P("section", None, None),
        P("section", None),
        P("section", None),
        P("section", None),
    )
    return jax.shard_map(per_device, mesh=mesh, in_specs=in_specs, out_specs=out_specs, check_vma=False)
```

```python
from functools import partial

import jax
import jax.numpy as jnp
from jax import lax
from jax.experimental import pallas as pl
from jax.experimental.pallas import tpu as pltpu
from jax.sharding import PartitionSpec as P

D = 768
FF = 3072
HEADS = 24
HEAD = 32
WIN = 7
SIDE = 2
GRID = SIDE * WIN
CELL = 8
WROWS = WIN * CELL
HALF = GRID * CELL
ROWS = SIDE * HALF
GROUP = 256
PACK = GROUP // HEAD
NGROUP = D // GROUP
UNITS = NGROUP * SIDE * SIDE
LANE = 128
FTILE = 512
EPS = 1e-05
SCALE = HEAD ** (-0.5)
BF = jnp.bfloat16
F32 = jnp.float32
MESH = pl.DeviceIdType.MESH


def dot(a, b, ca=1, cb=0):
    return lax.dot_general(a, b, (((ca,), (cb,)), ((), ())), preferred_element_type=F32)


def lanes(index, width=LANE):
    return pl.ds(pl.multiple_of(index * width, width), width)


def halves(value):
    return value.reshape(SIDE, GRID, CELL, value.shape[-1])


def shifts(left, right):
    column = lax.broadcasted_iota(jnp.int32, left.shape, 1)
    before0 = pltpu.roll(left, 1, 1)
    after0 = jnp.where(column == WIN - 1, pltpu.roll(right, CELL - 2, 1), pltpu.roll(left, CELL - 1, 1))
    before1 = jnp.where(column == 0, pltpu.roll(left, 2, 1), pltpu.roll(right, 1, 1))
    after1 = pltpu.roll(right, CELL - 1, 1)
    return ((before0, left, after0), (before1, right, after1))


def gelu_parts(h):
    expo = jnp.exp(h * h * -0.5)
    t = 1.0 / (1.0 + (0.3275911 * 0.7071067811865476) * jnp.abs(h))
    poly = t * (0.127414796 + t * (-0.142248368 + t * (0.7107068705 + t * (-0.7265760135 + t * 0.5307027145))))
    tail = poly * expo
    phi = jnp.where(h >= 0, 1.0 - tail, tail)
    return h * phi, phi + h * expo * 0.3989422804014327


def front_forward(sec, m, ubuf, msk, pr, U, C, zz, xh, rs):
    zero = jnp.zeros((ROWS, LANE), F32)

    def conv(i, total):
        ls = lanes(i)
        u = ubuf[sec, m, :, ls].astype(F32)
        masked = halves(u * msk[m])
        U[0, 1 : GRID + 1, :, ls] = masked[0]
        U[1, 1 : GRID + 1, :, ls] = masked[1]
        moved = shifts(U[0, :, :, ls], U[1, :, :, ls])
        taps = pr[sec, :, ls]
        uh = halves(u)
        sums = []
        for wc in range(SIDE):
            acc = uh[wc] + taps[9:10, :][None]
            for a in range(3):
                for b in range(3):
                    acc = acc + moved[wc][b][a : a + GRID] * taps[3 * a + b : 3 * a + b + 1, :][None]
            acc = acc.reshape(HALF, LANE)
            C[pl.ds(wc * HALF, HALF), ls] = acc
            sums.append(acc)
        return total + jnp.concatenate(sums, axis=0)

    mean = jnp.sum(lax.fori_loop(0, D // LANE, conv, zero, unroll=True), axis=-1, keepdims=True) * (1.0 / D)

    def spread(i, total):
        centred = C[:, lanes(i)] - mean
        return total + centred * centred

    var = jnp.sum(lax.fori_loop(0, D // LANE, spread, zero, unroll=True), axis=-1, keepdims=True) * (1.0 / D)
    rstd = lax.rsqrt(var + EPS)
    rs[sec, m] = jnp.broadcast_to(rstd, (ROWS, LANE))

    def norm(i, carry):
        ls = lanes(i)
        xhat = (C[:, ls] - mean) * rstd
        xh[sec, m, :, ls] = xhat.astype(BF)
        zz[m, 2 * sec, :, ls] = (xhat * pr[sec, 10:11, ls] + pr[sec, 11:12, ls]).astype(BF)
        return carry

    lax.fori_loop(0, D // LANE, norm, 0, unroll=True)


def fold(value):
    return jnp.sum(value.reshape(ROWS // CELL, CELL, LANE), axis=0)


def front_backward(sec, m, msk, pr, U, T, gfull, xh, rs, sgp, out, sent):
    zero = jnp.zeros((ROWS, LANE), F32)

    def sums(i, carry):
        s1, s2 = carry
        ls = lanes(i)
        dz = T[:, ls]
        xhat = xh[sec, m, :, ls].astype(F32)
        both = xhat * dz
        sgp[sec, 10, :, ls] += fold(both)
        sgp[sec, 11, :, ls] += fold(dz)
        gain = pr[sec, 10:11, ls]
        return s1 + dz * gain, s2 + both * gain

    s1, s2 = lax.fori_loop(0, D // LANE, sums, (zero, zero), unroll=True)
    m1 = jnp.sum(s1, axis=-1, keepdims=True) * (1.0 / D)
    m2 = jnp.sum(s2, axis=-1, keepdims=True) * (1.0 / D)

    def back(i, carry):
        ls = lanes(i)
        xhat = xh[sec, m, :, ls].astype(F32)
        inner = T[:, ls] * pr[sec, 10:11, ls] - m1 - xhat * m2
        gc = gfull(i)[...].astype(F32) + rs[sec, m] * inner
        xh[sec, m, :, ls] = gc.astype(BF)
        gh = halves(gc)
        U[0, 1 : GRID + 1, :, ls] = gh[0]
        U[1, 1 : GRID + 1, :, ls] = gh[1]
        moved = shifts(U[0, :, :, ls], U[1, :, :, ls])
        taps = pr[sec, :, ls]
        mask = halves(msk[m])
        du = []
        for wc in range(SIDE):
            acc = jnp.zeros((GRID, CELL, LANE), F32)
            for a in range(3):
                for b in range(3):
                    tap = 3 * a + b
                    acc = acc + moved[wc][2 - b][2 - a : 2 - a + GRID] * taps[tap : tap + 1, :][None]
            du.append((gh[wc] + mask[wc] * acc).reshape(HALF, LANE))
        out(i)[...] = jnp.concatenate(du, axis=0).astype(BF)
        return carry

    lax.fori_loop(0, D // LANE // 2, back, 0, unroll=True)
    sent(0)
    lax.fori_loop(D // LANE // 2, D // LANE, back, 0, unroll=True)
    sent(1)


def front_sums(sec, m, ubuf, msk, U, xh, sgp):
    def part(i, carry):
        ls = lanes(i)
        gc = xh[sec, m, :, ls].astype(F32)
        sgp[sec, 9, :, ls] += fold(gc)
        gh = halves(gc)
        U[0, 1 : GRID + 1, :, ls] = gh[0]
        U[1, 1 : GRID + 1, :, ls] = gh[1]
        moved = shifts(U[0, :, :, ls], U[1, :, :, ls])
        um = halves(ubuf[sec, m, :, ls].astype(F32) * msk[m])
        for a in range(3):
            for b in range(3):
                kg = jnp.zeros((CELL, LANE), F32)
                for wc in range(SIDE):
                    kg = kg + jnp.sum(moved[wc][2 - b][2 - a : 2 - a + GRID] * um[wc], axis=0)
                sgp[sec, 3 * a + b, :, ls] += kg
        return carry

    lax.fori_loop(0, D // LANE, part, 0)


def spread_heads(value, head_of_lane):
    parts = [jnp.where(head_of_lane == h, value, 0.0) for h in range(PACK)]
    return jnp.concatenate(parts, axis=0).astype(BF)


def gather_heads(value, rows, head_of_lane):
    out = jnp.zeros((rows, GROUP), F32)
    for h in range(PACK):
        out = jnp.where(head_of_lane == h, value[h * rows : (h + 1) * rows], out)
    return out


def unit_slices(unit):
    pair, group = unit // NGROUP, lax.rem(unit, NGROUP)
    rows = [pl.ds(pl.multiple_of((2 * pair + w) * WROWS, 8), WROWS) for w in range(2)]
    cols = [pl.ds(pl.multiple_of(part * D + group * GROUP, LANE), GROUP) for part in range(3)]
    return rows, cols


def window_parts(m, i, qkv):
    rows, cols = unit_slices(i)
    head_of_lane = lax.broadcasted_iota(jnp.int32, (WROWS, GROUP), 1) // HEAD
    q = [qkv[m, r, cols[0]].astype(BF) for r in rows]
    kd = [spread_heads(qkv[m, r, cols[1]], head_of_lane) for r in rows]
    vd = [spread_heads(qkv[m, r, cols[2]], head_of_lane) for r in rows]
    return rows, cols, head_of_lane, q, kd, vd


def window_forward(m, qkv, pw, T, group):
    def unit(i):
        rows, cols, head_of_lane, q, kd, vd = window_parts(m, i, qkv)
        s = [(dot(b, a, 1, 1) * SCALE).reshape(PACK, WROWS, WROWS) for a, b in zip(q, kd)]
        key = lax.broadcasted_iota(jnp.int32, s[0].shape, 1)
        real = lax.rem(key, CELL) < WIN
        s = [jnp.where(real, x, -1e30) for x in s]
        p = [jnp.exp(x - jnp.max(x, axis=1, keepdims=True)) for x in s]
        p = [x * (1.0 / jnp.sum(x, axis=1, keepdims=True)) for x in p]
        p = [x.reshape(PACK * WROWS, WROWS) for x in p]
        for w in range(2):
            pw[m, 2 * i + w, :, 0:WROWS] = p[w]
        out = [dot(x.astype(BF), v, 0, 0) for x, v in zip(p, vd)]
        for w in range(2):
            T[rows[w], cols[0]] = out[w]

    for pair in range(UNITS // 2 // NGROUP):
        unit(pair * NGROUP + group)


def window_backward(m, qkv, pw, T):
    def unit(i, carry):
        rows, cols, head_of_lane, q, kd, vd = window_parts(m, i, qkv)
        g = [T[r, cols[0]].astype(BF) for r in rows]
        p = [pw[m, 2 * i + w, :, 0:WROWS].reshape(PACK, WROWS, WROWS) for w in range(2)]
        dp = [dot(v, x, 1, 1).reshape(PACK, WROWS, WROWS) for v, x in zip(vd, g)]
        ds = [x * (y - jnp.sum(x * y, axis=1, keepdims=True)) for x, y in zip(p, dp)]
        ds = [x.reshape(PACK * WROWS, WROWS).astype(BF) for x in ds]
        pb = [x.reshape(PACK * WROWS, WROWS).astype(BF) for x in p]
        dv = [gather_heads(dot(x, y), WROWS, head_of_lane) for x, y in zip(pb, g)]
        dk = [gather_heads(dot(x, y), WROWS, head_of_lane) * SCALE for x, y in zip(ds, q)]
        dq = [dot(x, y, 0, 0) * SCALE for x, y in zip(ds, kd)]
        for w in range(2):
            qkv[m, rows[w], cols[0]] = dq[w]
            qkv[m, rows[w], cols[1]] = dk[w]
            qkv[m, rows[w], cols[2]] = dv[w]
        return carry

    lax.fori_loop(0, UNITS // 2, unit, 0)


def group_slices(group):
    return [pl.ds(pl.multiple_of(part * D + group * GROUP, LANE), GROUP) for part in range(3)]


def channel_forward(m, qkv, pw, zz, msk):
    def unit(i, carry):
        cols = group_slices(i)
        mask = msk[m][:, :1]
        q = qkv[m, :, cols[0]].astype(BF)
        k = (qkv[m, :, cols[1]] * mask).astype(BF)
        v = qkv[m, :, cols[2]].astype(BF)
        s = dot(q, k, 0, 0) * SCALE
        same = (lax.broadcasted_iota(jnp.int32, s.shape, 0) // HEAD) == (lax.broadcasted_iota(jnp.int32, s.shape, 1) // HEAD)
        s = jnp.where(same, s, -1e30)
        p = jnp.exp(s - jnp.max(s, axis=1, keepdims=True))
        p = p * (1.0 / jnp.sum(p, axis=1, keepdims=True))
        for k in range(GROUP // LANE):
            pw[m, 2 * i + k, 0:GROUP, :] = p[:, k * LANE : (k + 1) * LANE]
        zz[m, 1, :, cols[0]] = dot(v, p.astype(BF), 1, 1).astype(BF)
        return carry

    lax.fori_loop(0, NGROUP, unit, 0, unroll=True)


def channel_backward(m, qkv, pw, T, rr, msk):
    def unit(i, carry):
        cols = group_slices(i)
        mask = msk[m][:, :1]
        q = qkv[m, :, cols[0]].astype(BF)
        k = (qkv[m, :, cols[1]] * mask).astype(BF)
        v = qkv[m, :, cols[2]].astype(BF)
        g = T[:, cols[0]].astype(BF)
        p = jnp.concatenate([pw[m, 2 * i + k, 0:GROUP, :] for k in range(GROUP // LANE)], axis=1)
        dp = dot(g, v, 0, 0)
        ds = (p * (dp - jnp.sum(p * dp, axis=1, keepdims=True))).astype(BF)
        rr[m, 0, :, cols[0]] = (dot(k, ds, 1, 1) * SCALE).astype(BF)
        rr[m, 0, :, cols[1]] = (dot(q, ds) * (SCALE * mask)).astype(BF)
        rr[m, 0, :, cols[2]] = (dot(g, p.astype(BF))).astype(BF)
        return carry

    lax.fori_loop(0, NGROUP, unit, 0, unroll=True)


RING = 8
COLS = FF // RING
WIDE = FF // 12 * 8 // RING
REST = FF // 3 // RING
THIRD = FF // 3 * 2
LENT = RING * 3 // 4
EARLY = 2


def relay_kernel(
    wrows, wcols, img, cot, kern, bias, gain, move, first, second,
    act, ing, out1, out2, outs,
    wf, w2, pr, msk, flat, ubuf, gin, gout, zz, xh, rs, qkv, ab, rr, pw, U, C, T, sgp, sgs, sgm,
    rL, rR, rA, rG, buf, acc, going, got,
    wl, ws, wr, pl_, usem, gsem, us, gs, ss, rsem, es, er, sgsem, ssem, rcem, osem, sms, smr, xs, xr, ys, yr, bs, br, hs, hr, free,
):
    n = RING
    s = lax.axis_index("section")
    dp = lax.axis_index("dp")
    stage, c = s // 2, lax.rem(s, 2)
    mate = (dp, stage * 2 + (1 - c))
    opposite = (dp, (1 - stage) * 2 + c)
    diagonal = (dp, 3 - s)
    lender, helper = s == 1, s == 2
    early = stage == 0

    spot = lax.rem(dp, n)
    base = dp - spot
    me = jnp.where(lax.rem(spot, 2) == 0, spot // 2, n - 1 - spot // 2)

    def place(pos):
        pos = lax.rem(pos + 2 * n, n)
        return (base + jnp.where(pos < n // 2, 2 * pos, 2 * (n - 1 - pos) + 1), s)

    nexts = (place(me + 1), place(me - 1))
    rounds = n.bit_length() - 1
    partners = []
    for r in range(rounds):
        bit = 1 << r
        partners.append((jnp.where(lax.rem(spot // bit, 2) == 0, dp + bit, dp - bit), s))

    barrier = pltpu.get_barrier_semaphore()
    peers = [mate, opposite, diagonal, *nexts, *partners]
    for peer in peers:
        pl.semaphore_signal(barrier, inc=1, device_id=peer, device_id_type=MESH)
    pl.semaphore_wait(barrier, len(peers))

    def remote(src, dst, send, recv, peer):
        return pltpu.make_async_remote_copy(
            src_ref=src, dst_ref=dst, send_sem=send, recv_sem=recv, device_id=peer, device_id_type=MESH
        )

    half = second.shape[0]

    def group_part(group, part):
        cols = pl.ds(pl.multiple_of(part * D + group * GROUP, LANE), GROUP)
        return first.at[:, cols], wf.at[0, :, cols]

    def wait_group(group):
        for part in range(3):
            src, dst = group_part(group, part)
            i = group * 3 + part

            @pl.when(c == 0)
            def _():
                pltpu.make_async_copy(src, dst, wl.at[i]).wait()

            @pl.when(c == 1)
            def _():
                remote(src, dst, ws.at[i], wr.at[i], mate).wait_recv()

    def weight_parts(k):
        parts = []
        if k == 0:
            for group in range(NGROUP):
                for part in range(3):
                    parts.append(group_part(group, part))
            cols = pl.ds(3 * D, D)
            parts.append((first.at[:, cols], wf.at[k, :, cols]))
        else:
            for i in range(3):
                cols = pl.ds(i * (FF // 3), FF // 3)
                parts.append((first.at[:, cols], wf.at[k, :, cols]))
        third = half // 3
        for i in range(3):
            rows = pl.ds(i * third, third)
            parts.append((second.at[rows, :], w2.at[pl.ds(k * half + i * third, third), :]))
        return parts

    names = (
        [f"qkv{group}" for group in range(NGROUP) for _ in range(3)] + ["out"] + [f"low{i}" for i in range(3)],
        ["in"] * 3 + [f"high{i}" for i in range(3)],
    )

    def weight_copies(k):
        local = [pltpu.make_async_copy(a, b, wl.at[i]) for i, (a, b) in enumerate(weight_parts(k))]
        sent = [remote(a, b, ws.at[i], wr.at[i], mate) for i, (a, b) in enumerate(weight_parts(k))]
        return local, sent

    def params_copy(k):
        return remote(pr.at[k], pr.at[k], ws.at[13], wr.at[13], mate)

    pr[c, 0:9, :] = kern[...].astype(F32)
    pr[c, 9:10, :] = bias[...].astype(F32)
    pr[c, 10:11, :] = gain[...].astype(F32)
    pr[c, 11:12, :] = move[...].astype(F32)
    params_copy(c).start()
    for k in range(2):

        @pl.when(c == k)
        def _():
            local, sent = weight_copies(k)
            for here, there in zip(local, sent):
                here.start()
                there.start()

    def wait_weights(*wanted):
        for k in range(2):

            @pl.when(c == k)
            def _():
                for name, copy in zip(names[k], weight_copies(k)[0]):
                    if name in wanted:
                        copy.wait()
                for name, copy in zip(names[1 - k], weight_copies(1 - k)[1]):
                    if name in wanted:
                        copy.wait_recv()

    def wait_params(k):
        @pl.when(c != k)
        def _():
            params_copy(k).wait_recv()

    raw = flat.at[0]
    img_out = remote(img, raw, pl_.at[0], pl_.at[1], opposite)
    cot_out = remote(cot, raw, pl_.at[0], pl_.at[1], opposite)

    def pad(src, dst):
        blank = jnp.zeros((CELL - WIN, D), F32)
        for r in range(GRID):
            line = src[r].astype(F32)
            for wc in range(SIDE):
                cells = jnp.concatenate([line[wc * WIN : (wc + 1) * WIN], blank], axis=0)
                C[pl.ds(wc * HALF + r * CELL, CELL), :] = cells
        dst[...] = C[...].astype(BF)

    def unpad(dst):
        for r in range(GRID):
            sides = [C[pl.ds(wc * HALF + r * CELL, CELL), :][:WIN] for wc in range(SIDE)]
            dst[r] = jnp.concatenate(sides, axis=0).astype(BF)

    @pl.when(early)
    def _():
        cot_out.start()
        pad(img, ubuf.at[0, 0])

    @pl.when(jnp.logical_not(early))
    def _():
        img_out.start()
        pad(cot, gin.at[1])

    index = lax.broadcasted_iota(jnp.int32, (ROWS, LANE), 0)
    cell = lax.rem(index, CELL)
    row = lax.rem(index, HALF) // CELL
    column = (index // HALF) * WIN + cell
    for m in range(2):
        inside = (row < WIN * wrows[c + 2 * m]) & (column < WIN * wcols[c + 2 * m]) & (cell < WIN)
        msk[m] = jnp.where(inside, 1.0, 0.0)

    @pl.when(jnp.logical_not(early))
    def _():
        cot_out.wait_recv()
        pad(raw, gin.at[0])
        for m in range(2):
            for l in range(D // LANE):
                cols = pl.ds(l * LANE, LANE)
                gin[m, :, cols] = (gin[m, :, cols].astype(F32) * msk[m]).astype(BF)

    for wc in range(SIDE):
        U[wc, 0] = jnp.zeros((CELL, D), F32)
        U[wc, GRID + 1] = jnp.zeros((CELL, D), F32)
    sgp[...] = jnp.zeros(sgp.shape, F32)

    def hop(m, dst, send, recv):
        sides = [pl.ds(i * D // 2, D // 2) for i in range(2)]
        return [
            remote(gout.at[m, :, cols], dst.at[:, cols], send.at[m, i], recv.at[m, i], opposite)
            for i, cols in enumerate(sides)
        ]

    def u_hop(m):
        return hop(m, ubuf.at[0, m], us, usem)

    def g_hop(m):
        return hop(m, gin.at[m], gs, gsem)

    def factor_copies(k, m):
        if k == 0:
            parts = [
                ("F", zz.at[m, 0], rL.at[m, 0]),
                ("F", zz.at[m, 1], rL.at[m, 1]),
                ("G", rr.at[m, 0, :, pl.ds(3 * D, D)], rR.at[m, :, pl.ds(3 * D, D)]),
                ("A", rr.at[m, 0, :, pl.ds(0, 3 * D)], rR.at[m, :, pl.ds(0, 3 * D)]),
            ]
        else:
            parts = [
                ("X0", zz.at[m, 2], rL.at[m, 0]),
                ("M", gin.at[m], rG.at[m]),
            ]
            for i, cols in enumerate((pl.ds(0, FF // 3 * 2), pl.ds(FF // 3 * 2, FF // 3))):
                parts.append((f"X{i}", ab.at[m, :, cols], rA.at[m, :, cols]))
                parts.append((f"H{i}", rr.at[m, 1, :, cols], rR.at[m, :, cols]))
        return [(w, remote(a, b, ss.at[m, i], rsem.at[m, i], mate)) for i, (w, a, b) in enumerate(parts)]

    def start_factors(m, which):
        for k in range(2):

            @pl.when(c != k)
            def _():
                for when, copy in factor_copies(k, m):
                    if when == which:
                        copy.start()

    def wait_factors(which):
        for k in range(2):

            @pl.when(c == k)
            def _():
                for m in range(2):
                    for when, copy in factor_copies(k, m):
                        if when[0] in which:
                            copy.wait_recv()

    def shard(k):
        return lax.rem(k + 4 * n, n)

    def sign(h):
        return 1 if h == 0 else -1

    def home(h, t):
        return shard(me + sign(h) - sign(h) * t)

    def products(terms):
        total = None
        for a, b in terms:
            part = dot(a[...], b[...], 0, 0)
            total = part if total is None else total + part
        return total

    def tile(sub, h, j):
        side = pl.ds(h * COLS, COLS)
        if sub in (0, 4):
            rows = first_rows(sub, h)
            last = jnp.where(j >= (3 * n) // 4, 1, 0)
            own = jnp.where(c == 1, 2, last)
            other = jnp.where(c == 1, 0, last)
            cols = lanes(j, COLS)
            terms = [(zz.at[m, own, :, rows], rr.at[m, c, :, cols]) for m in range(2)]
            terms += [(rL.at[m, other, :, rows], rR.at[m, :, cols]) for m in range(2)]
        elif sub == 3:
            cols = [pl.ds(pl.multiple_of(i * LENT * REST + j * REST, LANE), REST) for i in range(2)]
            terms = [(rA.at[m, :, cols[0]], rG.at[m, :, side]) for m in range(2)]
            terms += [(rA.at[m, :, cols[1]], gout.at[m, :, side]) for m in range(2)]
        else:
            cols = lanes(j, WIDE) if sub == 1 else pl.ds(pl.multiple_of(THIRD + j * REST, LANE), REST)
            terms = [(ab.at[m, :, cols], gin.at[m, :, side]) for m in range(2)]
            terms += [(rA.at[m, :, cols], rG.at[m, :, side]) for m in range(2)]
        return products(terms)

    sizes = (COLS // 3 * 2, WIDE, REST, REST, COLS // 3)
    starts = (0, COLS, COLS + WIDE, COLS + WIDE, COLS // 3 * 2)
    parts = [pl.ds(start, size) for start, size in zip(starts, sizes)]
    subs = range(len(sizes))
    odd = c == 1
    active = (None, odd, odd, helper, None)

    def where_live(sub, j, run):
        if sub == 2:
            pl.when(jnp.logical_not(lender) | (j >= LENT))(run)
        elif sub == 3:
            pl.when(j < LENT)(run)
        else:
            run()

    def first_rows(sub, h):
        return pl.ds(h * COLS + (0 if sub == 0 else sizes[0]), sizes[sub])

    def where_active(sub, run):
        if active[sub] is None:
            run()
        else:
            pl.when(active[sub])(run)


    def gathered(sub, h, j):
        if sub in (0, 4):
            return wf.at[0, first_rows(sub, h), lanes(j, COLS)]
        first_row = 0 if sub == 1 else THIRD
        return w2.at[pl.ds(pl.multiple_of(first_row + j * sizes[sub], 16), sizes[sub]), pl.ds(h * COLS, COLS)]

    def scatter(h, t, sub):
        src, dst = buf.at[h, t, parts[sub], :], buf.at[h, t + 1, parts[sub], :]
        return remote(src, dst, ssem.at[h, t, sub], rcem.at[h, t + 1, sub], nexts[h])

    def spread(h, t, sub, j):
        ref = gathered(sub, h, j)
        return remote(ref, ref, ssem.at[h, n - 1 + t, sub], rcem.at[h, n + t, sub], nexts[h])

    half_shards = n * 3 // 4

    def write(h, j, sub):
        src, side = gathered(sub, h, j), pl.ds(h * COLS, COLS)
        if sub in (0, 4):
            dst = out1.at[first_rows(sub, h), lanes(j, COLS)]
        elif sub == 1:
            dst = out2.at[pl.ds(pl.multiple_of((j - half_shards) * WIDE, 16), WIDE), side]
        else:
            dst = out2.at[pl.ds(pl.multiple_of(THIRD - FF // 2 + j * REST, 16), REST), side]
        if sub == 3:
            return remote(src, dst, bs.at[h, j], br.at[h, j], diagonal)
        return pltpu.make_async_copy(src, dst, osem.at[h, j, sub])

    def hand_over(h, j):
        dst = out2.at[pl.ds(pl.multiple_of(j * WIDE, 16), WIDE), pl.ds(h * COLS, COLS)]
        return remote(gathered(1, h, j), dst, hs.at[h, j], hr.at[h, j], mate)

    def deliver(h, j, sub):
        if sub == 1:

            @pl.when(j < half_shards)
            def _():
                hand_over(h, j).start()

            @pl.when(j >= half_shards)
            def _():
                write(h, j, sub).start()

        else:
            write(h, j, sub).start()

    def lend(m):
        cols, there = pl.ds(THIRD, LENT * REST), [rA.at[m, :, pl.ds(i * LENT * REST, LENT * REST)] for i in range(2)]
        return (
            remote(ab.at[m, :, cols], there[0], xs.at[m], xr.at[m], diagonal),
            remote(rA.at[m, :, cols], there[1], xs.at[2 + m], xr.at[2 + m], diagonal),
        )

    def share(m):
        return remote(gout.at[m], rG.at[m], ys.at[m], yr.at[m], mate)

    def reduce_event(sub, h, e):
        j = shard(me - sign(h) * e)

        @pl.when(e == n - 1)
        def _():
            pl.semaphore_wait(free.at[h, sub], 1)

        def run():
            total = tile(sub, h, j)

            @pl.when(e == 0)
            def _():
                buf[h, 0, parts[sub], :] = total.astype(BF)
                scatter(h, 0, sub).start()

            @pl.when((e > 0) & (e < n - 1))
            def _():
                scatter(h, e - 1, sub).wait_recv()
                buf[h, e, parts[sub], :] = (total + buf[h, e, parts[sub], :].astype(F32)).astype(BF)
                scatter(h, e, sub).start()

            @pl.when(e == n - 1)
            def _():
                scatter(h, n - 2, sub).wait_recv()
                gathered(sub, h, j)[...] = (total + buf[h, n - 1, parts[sub], :].astype(F32)).astype(BF)
                spread(h, 0, sub, j).start()
                deliver(h, j, sub)

        where_live(sub, j, run)

    def event(sub, e):
        for h in range(2):

            @pl.when(e < n)
            def _():
                reduce_event(sub, h, e)

            @pl.when((e >= n) & (e < 2 * n - 1))
            def _():
                t = e - (n - 1)
                j = home(h, t)

                def run():
                    spread(h, t - 1, sub, j).wait_recv()

                    @pl.when(t < n - 1)
                    def _():
                        spread(h, t, sub, j).start()

                    deliver(h, j, sub)

                where_live(sub, j, run)

    def early_event(e, which):
        @pl.when(odd)
        def _():
            for sub in which:
                where_active(sub, lambda: event(sub, e))

    def small(r):
        return remote(going.at[r], got.at[r], sms.at[r], smr.at[r], partners[r])

    def mlp(m, order, wait):
        total, before, last = C[...], None, None
        for t in order:
            cols = pl.ds(t * FTILE, FTILE)
            h = dot(zz[m, 2], wf[1, :, cols])
            if last is not None:
                wait(last)
                total = total + dot(before, w2[pl.ds(last * FTILE, FTILE), :])
            a, d = gelu_parts(h)
            before, last = a.astype(BF), t
            ab[m, :, cols] = before
            rr[m, 1, :, cols] = d.astype(BF)
            if t == FF // FTILE * 2 // 3 - 1 and order == range(FF // FTILE):
                start_factors(m, "X0")
        wait(last)
        for i in range(2):
            cols = pl.ds(i * D // 2, D // 2)
            part = total[:, i * D // 2 : (i + 1) * D // 2]
            gout[jnp.where(early, m, 2 + m), :, cols] = (part + dot(before, w2[pl.ds(last * FTILE, FTILE), cols])).astype(BF)

            @pl.when(early)
            def _():
                u_hop(m)[i].start()

    def give_results(m):
        @pl.when(early)
        def _():
            C[...] = gout[m].astype(F32)

        @pl.when(jnp.logical_not(early))
        def _():
            for l in range(D // LANE):
                cols = pl.ds(l * LANE, LANE)
                C[:, cols] = gout[2 + m, :, cols].astype(F32) * msk[m]

        unpad(flat.at[m])

        @pl.when(early & (m == 0))
        def _():
            pltpu.make_async_copy(flat.at[0], ing, es.at[1]).start()

        @pl.when(early & (m == 1))
        def _():
            remote(flat.at[1], ing, es.at[1], er.at[1], opposite).start()

        @pl.when(jnp.logical_not(early) & (m == 0))
        def _():
            remote(flat.at[0], act, es.at[0], er.at[0], opposite).start()

        @pl.when(jnp.logical_not(early) & (m == 1))
        def _():
            pltpu.make_async_copy(flat.at[1], act, es.at[0]).start()

    def forward(m, p):
        @pl.when(jnp.logical_not(early))
        def _():
            for copy in u_hop(m):
                copy.wait_recv()

        @pl.when(early & (m == 1))
        def _():
            img_out.wait_recv()
            pad(raw, ubuf.at[0, 1])

        once = p == 0
        starting = early & once

        @pl.when(once)
        def _():
            wait_params(0)

        @pl.when(once & jnp.logical_not(early))
        def _():
            wait_params(1)
            wait_weights(*set(names[0] + names[1]))

        front_forward(0, m, ubuf, msk, pr, U, C, zz, xh, rs)

        @pl.when(early)
        def _():
            def head_group(group, carry):
                @pl.when(once)
                def _():
                    wait_group(group)

                for part in range(3):
                    cols = pl.ds(pl.multiple_of(part * D + group * GROUP, LANE), GROUP)
                    qkv[m, :, cols] = dot(zz[m, 0], wf[0, :, cols])
                window_forward(m, qkv, pw, T, group)
                return carry

            lax.fori_loop(0, NGROUP, head_group, 0)
            zz[m, 1] = T[...].astype(BF)

        @pl.when(starting)
        def _():
            wait_weights("out")
            wait_params(1)

        @pl.when(jnp.logical_not(early))
        def _():
            qkv[m] = dot(zz[m, 0], wf[0, :, pl.ds(0, 3 * D)])

        @pl.when(jnp.logical_not(early))
        def _():
            channel_forward(m, qkv, pw, zz, msk)

        ubuf[1, m] = (C[...] + dot(zz[m, 1], wf[0, :, pl.ds(3 * D, D)])).astype(BF)

        front_forward(1, m, ubuf, msk, pr, U, C, zz, xh, rs)

        @pl.when(starting)
        def _():
            wait_weights("in")
            order = [i + 3 * k for i in range(3) for k in range(2)]
            mlp(m, order, lambda t: wait_weights(f"low{t}" if t < 3 else f"high{t - 3}"))
            start_factors(m, "X0")

        @pl.when(jnp.logical_not(starting))
        def _():
            mlp(m, range(FF // FTILE), lambda t: None)

        start_factors(m, "F")
        start_factors(m, "X1")

        @pl.when(early & (m == 1))
        def _():
            wait_factors("FX")

        @pl.when(lender & (m == 1))
        def _():
            for i in range(2):
                for copy in lend(i):
                    copy.start()

    def backward(m):
        @pl.when(early)
        def _():
            for copy in g_hop(m):
                copy.wait_recv()
            start_factors(m, "M")

        for t in range(FF // FTILE):
            cols = pl.ds(t * FTILE, FTILE)
            da = dot(gin[m], w2[cols, :], 1, 1)
            rr[m, 1, :, cols] = (da * rr[m, 1, :, cols].astype(F32)).astype(BF)
            if t == FF // FTILE * 2 // 3 - 1:
                start_factors(m, "H0")

        start_factors(m, "H1")

        @pl.when(m == 1)
        def _():
            @pl.when(jnp.logical_not(early))
            def _():
                wait_factors("FX")

            wait_factors("M")
            early_event(0, (1, 2))

        T[...] = dot(rr[m, 1], wf[1], 1, 1)

        @pl.when(m == 1)
        def _():
            wait_factors("H")
            early_event(0, (0, 4))

        last = pl.ds(3 * D, D)

        @pl.when(early)
        def _():
            for copy in u_hop(m):
                copy.wait_send()

        def tail_lanes(i):
            return rr.at[m, 0, :, pl.ds(pl.multiple_of(3 * D + i * LANE, LANE), LANE)]

        def nothing(half):
            pass

        front_backward(1, m, msk, pr, U, T, lambda i: gin.at[m, :, lanes(i)], xh, rs, sgp, tail_lanes, nothing)

        start_factors(m, "G")
        T[...] = dot(rr[m, 0, :, last], wf[0, :, last], 1, 1)

        @pl.when(early)
        def _():
            window_backward(m, qkv, pw, T)
            for i in range(3):
                cols = pl.ds(i * D, D)
                rr[m, 0, :, cols] = qkv[m, :, cols].astype(BF)

        @pl.when(jnp.logical_not(early))
        def _():
            channel_backward(m, qkv, pw, T, rr, msk)

        start_factors(m, "A")

        @pl.when(m == 1)
        def _():
            for e in range(1, EARLY):
                early_event(e, (1, 2, 0, 4))

        T[...] = dot(rr[m, 0, :, pl.ds(0, 3 * D)], wf[0, :, pl.ds(0, 3 * D)], 1, 1)
        def send_half(half):
            @pl.when(jnp.logical_not(early))
            def _():
                g_hop(m)[half].start()

        front_backward(
            0, m, msk, pr, U, T, tail_lanes, xh, rs, sgp, lambda i: gout.at[m, :, lanes(i)], send_half
        )

        @pl.when(s == 3)
        def _():
            share(m).start()

    @pl.when(jnp.logical_not(early))
    def _():
        for m in range(2):
            start_factors(m, "M")

    def phase(p, carry):
        m = jnp.where(early, lax.rem(p, 2), p // 2)
        ahead = jnp.where(early, p < 2, lax.rem(p, 2) == 0)

        @pl.when(ahead)
        def _():
            forward(m, p)

        @pl.when(jnp.logical_not(ahead))
        def _():
            backward(m)

        return carry

    lax.fori_loop(0, 4, phase, 0)

    for h in range(2):
        for sub in subs:

            def ready():
                pl.semaphore_signal(free.at[h, sub], inc=1, device_id=nexts[1 - h], device_id_type=MESH)

            where_active(sub, ready)

    give = remote(sgs.at[1 - c], sgm, sgsem.at[0], sgsem.at[1], mate)

    def small_sums():
        for sec in range(2):
            for j in range(12):
                sgs[sec, j : j + 1, :] = jnp.sum(sgp[sec, j], axis=0, keepdims=True)
            sgs[sec, 12:16, :] = jnp.zeros((4, D), F32)
        give.start()

    wait_factors("GA")

    @pl.when(helper)
    def _():
        for m in range(2):
            for copy in lend(m):
                copy.wait_recv()
            share(m).wait_recv()

    def ring_step(t, carry):
        for sub in (0, 4):
            event(sub, t + jnp.where(odd, EARLY, 0))
        where_active(1, lambda: event(1, t + EARLY))
        where_active(2, lambda: event(2, t + EARLY))
        where_active(3, lambda: event(3, t))
        @pl.when((t >= 1) & (t < 5))
        def _():
            front_sums((t - 1) // 2, lax.rem(t - 1, 2), ubuf, msk, U, xh, sgp)

        pl.when(t == 5)(small_sums)

        @pl.when((t >= 6) & (t < 8))
        def _():
            give_results(t - 6)

        for r in range(rounds + 1):

            @pl.when(t == 6 + 2 * r)
            def _():
                if r == 0:
                    give.wait_recv()
                    acc[0] = sgs[c] + sgm[...]
                else:
                    small(r - 1).wait_recv()
                    acc[r] = going[r - 1].astype(F32) + got[r - 1].astype(F32)
                if r < rounds:
                    going[r] = acc[r].astype(BF)
                    small(r).start()

        return carry

    lax.fori_loop(0, 2 * n - 1, ring_step, 0)
    outs[...] = acc[rounds]

    for k in range(2):

        @pl.when(c == k)
        def _():
            for copy in weight_copies(k)[1]:
                copy.wait_send()
            params_copy(k).wait_send()
            for m in range(2):
                for _when, copy in factor_copies(1 - k, m):
                    copy.wait_send()

    give.wait_send()
    for r in range(rounds):
        small(r).wait_send()

    def drain(t, carry):
        for h in range(2):
            for sub in subs:

                def sent():
                    where_live(sub, shard(me - sign(h) * t), lambda: scatter(h, t, sub).wait_send())
                    where_live(sub, home(h, t), lambda: spread(h, t, sub, home(h, t)).wait_send())

                where_active(sub, sent)

        return carry

    lax.fori_loop(0, n - 1, drain, 0)

    def written(j, carry):
        for h in range(2):
            write(h, j, 0).wait()
            write(h, j, 4).wait()

            @pl.when(odd)
            def _():
                where_live(2, j, lambda: write(h, j, 2).wait())

                @pl.when(j < half_shards)
                def _():
                    hand_over(h, j).wait_send()

                @pl.when(j >= half_shards)
                def _():
                    write(h, j, 1).wait()

            @pl.when(jnp.logical_not(odd) & (j < half_shards))
            def _():
                hand_over(h, j).wait_recv()

            @pl.when(helper & (j < LENT))
            def _():
                write(h, j, 3).wait_send()

            @pl.when(lender & (j < LENT))
            def _():
                write(h, j, 3).wait_recv()

        return carry

    lax.fori_loop(0, n, written, 0)

    @pl.when(lender)
    def _():
        for m in range(2):
            for copy in lend(m):
                copy.wait_send()

    @pl.when(s == 3)
    def _():
        for m in range(2):
            share(m).wait_send()

    @pl.when(early)
    def _():
        cot_out.wait_send()
        pltpu.make_async_copy(flat.at[0], ing, es.at[1]).wait()
        remote(flat.at[1], ing, es.at[1], er.at[1], opposite).wait_send()
        remote(flat.at[0], act, es.at[0], er.at[0], opposite).wait_recv()

    @pl.when(jnp.logical_not(early))
    def _():
        img_out.wait_send()
        for m in range(2):
            for copy in g_hop(m):
                copy.wait_send()
        remote(flat.at[0], act, es.at[0], er.at[0], opposite).wait_send()
        pltpu.make_async_copy(flat.at[1], act, es.at[0]).wait()
        remote(flat.at[1], ing, es.at[1], er.at[1], opposite).wait_recv()


def relay(wrows, wcols, img, cot, kern, bias, gain, move, first, second):
    shape = jax.ShapeDtypeStruct
    vmem = pl.BlockSpec(memory_space=pltpu.VMEM)
    anywhere = pl.BlockSpec(memory_space=pl.ANY)
    dma = pltpu.SemaphoreType.DMA
    smem = pl.BlockSpec(memory_space=pltpu.SMEM)
    image = (ROWS, D)
    slot = img.shape
    rounds = RING.bit_length() - 1
    return pl.pallas_call(
        relay_kernel,
        out_shape=[
            shape(slot, BF),
            shape(slot, BF),
            shape((D, FF), BF),
            shape((FF // 2, D), BF),
            shape((16, D), F32),
        ],
        in_specs=[smem] * 2 + [vmem] * 6 + [anywhere] * 2,
        out_specs=[anywhere] * 4 + [vmem],
        scratch_shapes=[
            pltpu.VMEM((2, D, FF), BF),
            pltpu.VMEM((FF, D), BF),
            pltpu.VMEM((2, 16, D), F32),
            pltpu.VMEM((2, ROWS, LANE), F32),
            pltpu.VMEM((2,) + slot, BF),
            pltpu.VMEM((2, 2) + image, BF),
            pltpu.VMEM((2,) + image, BF),
            pltpu.VMEM((4,) + image, BF),
            pltpu.VMEM((2, 3) + image, BF),
            pltpu.VMEM((2, 2) + image, BF),
            pltpu.VMEM((2, 2, ROWS, LANE), F32),
            pltpu.VMEM((2, ROWS, 3 * D), F32),
            pltpu.VMEM((2, ROWS, FF), BF),
            pltpu.VMEM((2, 2, ROWS, FF), BF),
            pltpu.VMEM((2, UNITS, PACK * WROWS, LANE), F32),
            pltpu.VMEM((SIDE, GRID + 2, CELL, D), F32),
            pltpu.VMEM(image, F32),
            pltpu.VMEM(image, F32),
            pltpu.VMEM((2, 12, CELL, D), F32),
            pltpu.VMEM((2, 16, D), F32),
            pltpu.VMEM((16, D), F32),
            pltpu.VMEM((2, 2) + image, BF),
            pltpu.VMEM((2, ROWS, FF), BF),
            pltpu.VMEM((2, ROWS, FF), BF),
            pltpu.VMEM((2,) + image, BF),
            pltpu.VMEM((2, RING, COLS + WIDE + REST, COLS), BF),
            pltpu.VMEM((rounds + 1, 16, D), F32),
            pltpu.VMEM((rounds, 16, D), BF),
            pltpu.VMEM((rounds, 16, D), BF),
            dma((14,)),
            dma((14,)),
            dma((14,)),
            dma((2,)),
            dma((2, 2)),
            dma((2, 2)),
            dma((2, 2)),
            dma((2, 2)),
            dma((2, 8)),
            dma((2, 8)),
            dma((2,)),
            dma((2,)),
            dma((2,)),
            dma((2, 2 * RING, 5)),
            dma((2, 2 * RING, 5)),
            dma((2, RING, 5)),
            dma((rounds,)),
            dma((rounds,)),
            dma((4,)),
            dma((4,)),
            dma((2,)),
            dma((2,)),
            dma((2, RING)),
            dma((2, RING)),
            dma((2, RING)),
            dma((2, RING)),
            pltpu.SemaphoreType.REGULAR((2, 5)),
        ],
        name="relay",
        compiler_params=pltpu.CompilerParams(
            collective_id=1, has_side_effects=True, vmem_limit_bytes=63 * 2**20
        ),
    )(wrows, wcols, img, cot, kern, bias, gain, move, first, second)


def finish_kernel(
    out1, out2, act, ing, outs, first, second, acts, ings, kern, bias, gain, move,
    raw1, raw2, full1, full2, acted, graded, wide, small, kernels, rsem, wsem,
):
    steps = rsem.shape[0] - 3

    loads = [
        pltpu.make_async_copy(act, acted, rsem.at[steps]),
        pltpu.make_async_copy(ing, graded, rsem.at[steps + 1]),
        pltpu.make_async_copy(outs, small, rsem.at[steps + 2]),
    ]
    for copy in loads:
        copy.start()
    reads, writes = [], []
    for i in range(steps):
        pair = ((out1, raw1, full1, first), (out2, raw2, full2, second))[i % 2]
        src, raw, full, dst = pair
        half = steps // 2
        rows = pl.ds(i // 2 * (src.shape[0] // half), src.shape[0] // half)
        reads.append((pltpu.make_async_copy(src.at[rows, :], raw.at[rows, :], rsem.at[i]), raw, full, rows))
        writes.append(pltpu.make_async_copy(full.at[rows, :], dst.at[rows, :], wsem.at[i]))
    for copy, *_ in reads:
        copy.start()
    for (copy, raw, full, rows), back in zip(reads, writes):
        copy.wait()
        full[rows, :] = raw[rows, :].astype(F32)
        back.start()
    for copy in loads:
        copy.wait()
    for k in range(9):
        kernels[k] = small[k : k + 1, :]
    for r in range(GRID):
        line = graded[r].astype(F32)
        for k in range(GRID):
            wide[r, k] = line[k : k + 1, :]
    last = [
        pltpu.make_async_copy(acted, acts, wsem.at[steps]),
        pltpu.make_async_copy(wide, ings, wsem.at[steps + 1]),
        pltpu.make_async_copy(kernels, kern, wsem.at[steps + 2]),
    ]
    for i, dst in enumerate((bias, gain, move)):
        last.append(pltpu.make_async_copy(small.at[pl.ds(9 + i, 1), :], dst, wsem.at[steps + 3 + i]))
    for copy in last:
        copy.start()
    for copy in writes + last:
        copy.wait()


def finish(out1, out2, act, ing, outs):
    shape = jax.ShapeDtypeStruct
    slot = act.shape
    anywhere = pl.BlockSpec(memory_space=pl.ANY)
    line = (1, D)
    spread = slot[:2] + line
    steps = 16
    return pl.pallas_call(
        finish_kernel,
        out_shape=[
            shape(out1.shape, F32),
            shape(out2.shape, F32),
            shape(slot, BF),
            shape(spread, F32),
            shape((9,) + line, F32),
            shape(line, F32),
            shape(line, F32),
            shape(line, F32),
        ],
        in_specs=[anywhere] * 5,
        out_specs=[anywhere] * 8,
        scratch_shapes=[
            pltpu.VMEM(out1.shape, out1.dtype),
            pltpu.VMEM(out2.shape, out2.dtype),
            pltpu.VMEM(out1.shape, F32),
            pltpu.VMEM(out2.shape, F32),
            pltpu.VMEM(slot, BF),
            pltpu.VMEM(slot, BF),
            pltpu.VMEM(spread, F32),
            pltpu.VMEM(outs.shape, F32),
            pltpu.VMEM((9,) + line, F32),
            pltpu.SemaphoreType.DMA((steps + 3,)),
            pltpu.SemaphoreType.DMA((steps + 6,)),
        ],
        name="finish",
        compiler_params=pltpu.CompilerParams(vmem_limit_bytes=60 * 2**20),
    )(out1, out2, act, ing, outs)


def per_device(
    images, cotangent, window_rows, window_cols, pos_kernel, pos_bias, norm_gain, norm_shift, first_weight, second_weight
):
    act, ing, out1, out2, outs = relay(
        window_rows, window_cols, images[0], cotangent[0], pos_kernel[0], pos_bias, norm_gain, norm_shift,
        first_weight[0], second_weight,
    )
    if lax.axis_size("dp") > RING:
        out1, out2, outs = lax.psum((out1.astype(F32) / RING, out2.astype(F32) / RING, outs / RING), "dp")
    out1, out2, act, ing, kern, bias, gain, move = finish(out1, out2, act, ing, outs)
    return (
        act[None],
        ing.transpose(2, 0, 1, 3),
        out1[None],
        out2,
        kern.transpose(1, 0, 2),
        bias,
        gain,
        move,
    )


def solution(mesh):
    in_specs = (
        P(("dp", "section"), None, None, None),
        P(("dp", "section"), None, None, None),
        P("dp"),
        P("dp"),
        P("section", None, None),
        P("section", None),
        P("section", None),
        P("section", None),
        P("section", None, None),
        P("section", None),
    )
    out_specs = (
        P(("dp", "section"), None, None, None),
        P(("dp", "section"), None, None, None),
        P("section", None, None),
        P("section", None),
        P("section", None, None),
        P("section", None),
        P("section", None),
        P("section", None),
    )
    return jax.shard_map(per_device, mesh=mesh, in_specs=in_specs, out_specs=out_specs, check_vma=False)
```

```python
from functools import partial

import jax
import jax.numpy as jnp
from jax import lax
from jax.experimental import pallas as pl
from jax.experimental.pallas import tpu as pltpu
from jax.sharding import PartitionSpec as P

D = 768
FF = 3072
HEADS = 24
HEAD = 32
WIN = 7
SIDE = 2
GRID = SIDE * WIN
CELL = 8
WROWS = WIN * CELL
HALF = GRID * CELL
ROWS = SIDE * HALF
GROUP = 256
PACK = GROUP // HEAD
NGROUP = D // GROUP
UNITS = NGROUP * SIDE * SIDE
LANE = 128
FTILE = 512
EPS = 1e-05
SCALE = HEAD ** (-0.5)
BF = jnp.bfloat16
F32 = jnp.float32
MESH = pl.DeviceIdType.MESH


def dot(a, b, ca=1, cb=0):
    return lax.dot_general(a, b, (((ca,), (cb,)), ((), ())), preferred_element_type=F32)


def lanes(index, width=LANE):
    return pl.ds(pl.multiple_of(index * width, width), width)


def halves(value):
    return value.reshape(SIDE, GRID, CELL, value.shape[-1])


def shifts(left, right):
    column = lax.broadcasted_iota(jnp.int32, left.shape, 1)
    before0 = pltpu.roll(left, 1, 1)
    after0 = jnp.where(column == WIN - 1, pltpu.roll(right, CELL - 2, 1), pltpu.roll(left, CELL - 1, 1))
    before1 = jnp.where(column == 0, pltpu.roll(left, 2, 1), pltpu.roll(right, 1, 1))
    after1 = pltpu.roll(right, CELL - 1, 1)
    return ((before0, left, after0), (before1, right, after1))


def gelu_parts(h):
    expo = jnp.exp(h * h * -0.5)
    t = 1.0 / (1.0 + (0.3275911 * 0.7071067811865476) * jnp.abs(h))
    poly = t * (0.127414796 + t * (-0.142248368 + t * (0.7107068705 + t * (-0.7265760135 + t * 0.5307027145))))
    tail = poly * expo
    phi = jnp.where(h >= 0, 1.0 - tail, tail)
    return h * phi, phi + h * expo * 0.3989422804014327


def front_forward(sec, m, ubuf, msk, pr, U, C, zz, xh, rs):
    zero = jnp.zeros((ROWS, LANE), F32)

    def conv(i, total):
        ls = lanes(i)
        u = ubuf[sec, m, :, ls].astype(F32)
        masked = halves(u * msk[m])
        U[0, 1 : GRID + 1, :, ls] = masked[0]
        U[1, 1 : GRID + 1, :, ls] = masked[1]
        moved = shifts(U[0, :, :, ls], U[1, :, :, ls])
        taps = pr[sec, :, ls]
        uh = halves(u)
        sums = []
        for wc in range(SIDE):
            acc = uh[wc] + taps[9:10, :][None]
            for a in range(3):
                for b in range(3):
                    acc = acc + moved[wc][b][a : a + GRID] * taps[3 * a + b : 3 * a + b + 1, :][None]
            acc = acc.reshape(HALF, LANE)
            C[pl.ds(wc * HALF, HALF), ls] = acc
            sums.append(acc)
        return total + jnp.concatenate(sums, axis=0)

    mean = jnp.sum(lax.fori_loop(0, D // LANE, conv, zero, unroll=True), axis=-1, keepdims=True) * (1.0 / D)

    def spread(i, total):
        centred = C[:, lanes(i)] - mean
        return total + centred * centred

    var = jnp.sum(lax.fori_loop(0, D // LANE, spread, zero, unroll=True), axis=-1, keepdims=True) * (1.0 / D)
    rstd = lax.rsqrt(var + EPS)
    rs[sec, m] = jnp.broadcast_to(rstd, (ROWS, LANE))

    def norm(i, carry):
        ls = lanes(i)
        xhat = (C[:, ls] - mean) * rstd
        xh[sec, m, :, ls] = xhat.astype(BF)
        zz[m, 2 * sec, :, ls] = (xhat * pr[sec, 10:11, ls] + pr[sec, 11:12, ls]).astype(BF)
        return carry

    lax.fori_loop(0, D // LANE, norm, 0, unroll=True)


def fold(value):
    return jnp.sum(value.reshape(ROWS // CELL, CELL, LANE), axis=0)


def front_backward(sec, m, msk, pr, U, T, gfull, xh, rs, sgp, out, sent):
    zero = jnp.zeros((ROWS, LANE), F32)

    def sums(i, carry):
        s1, s2 = carry
        ls = lanes(i)
        dz = T[:, ls]
        xhat = xh[sec, m, :, ls].astype(F32)
        both = xhat * dz
        sgp[sec, 10, :, ls] += fold(both)
        sgp[sec, 11, :, ls] += fold(dz)
        gain = pr[sec, 10:11, ls]
        return s1 + dz * gain, s2 + both * gain

    s1, s2 = lax.fori_loop(0, D // LANE, sums, (zero, zero), unroll=True)
    m1 = jnp.sum(s1, axis=-1, keepdims=True) * (1.0 / D)
    m2 = jnp.sum(s2, axis=-1, keepdims=True) * (1.0 / D)

    def back(i, carry):
        ls = lanes(i)
        xhat = xh[sec, m, :, ls].astype(F32)
        inner = T[:, ls] * pr[sec, 10:11, ls] - m1 - xhat * m2
        gc = gfull(i)[...].astype(F32) + rs[sec, m] * inner
        xh[sec, m, :, ls] = gc.astype(BF)
        gh = halves(gc)
        U[0, 1 : GRID + 1, :, ls] = gh[0]
        U[1, 1 : GRID + 1, :, ls] = gh[1]
        moved = shifts(U[0, :, :, ls], U[1, :, :, ls])
        taps = pr[sec, :, ls]
        mask = halves(msk[m])
        du = []
        for wc in range(SIDE):
            acc = jnp.zeros((GRID, CELL, LANE), F32)
            for a in range(3):
                for b in range(3):
                    tap = 3 * a + b
                    acc = acc + moved[wc][2 - b][2 - a : 2 - a + GRID] * taps[tap : tap + 1, :][None]
            du.append((gh[wc] + mask[wc] * acc).reshape(HALF, LANE))
        out(i)[...] = jnp.concatenate(du, axis=0).astype(BF)
        return carry

    lax.fori_loop(0, D // LANE // 2, back, 0, unroll=True)
    sent(0)
    lax.fori_loop(D // LANE // 2, D // LANE, back, 0, unroll=True)
    sent(1)


def front_sums(sec, m, ubuf, msk, U, xh, sgp):
    def part(i, carry):
        ls = lanes(i)
        gc = xh[sec, m, :, ls].astype(F32)
        sgp[sec, 9, :, ls] += fold(gc)
        gh = halves(gc)
        U[0, 1 : GRID + 1, :, ls] = gh[0]
        U[1, 1 : GRID + 1, :, ls] = gh[1]
        moved = shifts(U[0, :, :, ls], U[1, :, :, ls])
        um = halves(ubuf[sec, m, :, ls].astype(F32) * msk[m])
        for a in range(3):
            for b in range(3):
                kg = jnp.zeros((CELL, LANE), F32)
                for wc in range(SIDE):
                    kg = kg + jnp.sum(moved[wc][2 - b][2 - a : 2 - a + GRID] * um[wc], axis=0)
                sgp[sec, 3 * a + b, :, ls] += kg
        return carry

    lax.fori_loop(0, D // LANE, part, 0)


def spread_heads(value, head_of_lane):
    parts = [jnp.where(head_of_lane == h, value, 0.0) for h in range(PACK)]
    return jnp.concatenate(parts, axis=0).astype(BF)


def gather_heads(value, rows, head_of_lane):
    out = jnp.zeros((rows, GROUP), F32)
    for h in range(PACK):
        out = jnp.where(head_of_lane == h, value[h * rows : (h + 1) * rows], out)
    return out


def unit_slices(unit):
    pair, group = unit // NGROUP, lax.rem(unit, NGROUP)
    rows = [pl.ds(pl.multiple_of((2 * pair + w) * WROWS, 8), WROWS) for w in range(2)]
    cols = [pl.ds(pl.multiple_of(part * D + group * GROUP, LANE), GROUP) for part in range(3)]
    return rows, cols


def window_parts(m, i, qkv):
    rows, cols = unit_slices(i)
    head_of_lane = lax.broadcasted_iota(jnp.int32, (WROWS, GROUP), 1) // HEAD
    q = [qkv[m, r, cols[0]].astype(BF) for r in rows]
    kd = [spread_heads(qkv[m, r, cols[1]], head_of_lane) for r in rows]
    vd = [spread_heads(qkv[m, r, cols[2]], head_of_lane) for r in rows]
    return rows, cols, head_of_lane, q, kd, vd


def window_forward(m, qkv, pw, T, group):
    def unit(i):
        rows, cols, head_of_lane, q, kd, vd = window_parts(m, i, qkv)
        s = [(dot(b, a, 1, 1) * SCALE).reshape(PACK, WROWS, WROWS) for a, b in zip(q, kd)]
        key = lax.broadcasted_iota(jnp.int32, s[0].shape, 1)
        real = lax.rem(key, CELL) < WIN
        s = [jnp.where(real, x, -1e30) for x in s]
        p = [jnp.exp(x - jnp.max(x, axis=1, keepdims=True)) for x in s]
        p = [x * (1.0 / jnp.sum(x, axis=1, keepdims=True)) for x in p]
        p = [x.reshape(PACK * WROWS, WROWS) for x in p]
        for w in range(2):
            pw[m, 2 * i + w, :, 0:WROWS] = p[w]
        out = [dot(x.astype(BF), v, 0, 0) for x, v in zip(p, vd)]
        for w in range(2):
            T[rows[w], cols[0]] = out[w]

    for pair in range(UNITS // 2 // NGROUP):
        unit(pair * NGROUP + group)


def window_backward(m, qkv, pw, T):
    def unit(i, carry):
        rows, cols, head_of_lane, q, kd, vd = window_parts(m, i, qkv)
        g = [T[r, cols[0]].astype(BF) for r in rows]
        p = [pw[m, 2 * i + w, :, 0:WROWS].reshape(PACK, WROWS, WROWS) for w in range(2)]
        dp = [dot(v, x, 1, 1).reshape(PACK, WROWS, WROWS) for v, x in zip(vd, g)]
        ds = [x * (y - jnp.sum(x * y, axis=1, keepdims=True)) for x, y in zip(p, dp)]
        ds = [x.reshape(PACK * WROWS, WROWS).astype(BF) for x in ds]
        pb = [x.reshape(PACK * WROWS, WROWS).astype(BF) for x in p]
        dv = [gather_heads(dot(x, y), WROWS, head_of_lane) for x, y in zip(pb, g)]
        dk = [gather_heads(dot(x, y), WROWS, head_of_lane) * SCALE for x, y in zip(ds, q)]
        dq = [dot(x, y, 0, 0) * SCALE for x, y in zip(ds, kd)]
        for w in range(2):
            qkv[m, rows[w], cols[0]] = dq[w]
            qkv[m, rows[w], cols[1]] = dk[w]
            qkv[m, rows[w], cols[2]] = dv[w]
        return carry

    lax.fori_loop(0, UNITS // 2, unit, 0)


def group_slices(group):
    return [pl.ds(pl.multiple_of(part * D + group * GROUP, LANE), GROUP) for part in range(3)]


def channel_forward(m, qkv, pw, zz, msk):
    def unit(i, carry):
        cols = group_slices(i)
        mask = msk[m][:, :1]
        q = qkv[m, :, cols[0]].astype(BF)
        k = (qkv[m, :, cols[1]] * mask).astype(BF)
        v = qkv[m, :, cols[2]].astype(BF)
        s = dot(q, k, 0, 0) * SCALE
        same = (lax.broadcasted_iota(jnp.int32, s.shape, 0) // HEAD) == (lax.broadcasted_iota(jnp.int32, s.shape, 1) // HEAD)
        s = jnp.where(same, s, -1e30)
        p = jnp.exp(s - jnp.max(s, axis=1, keepdims=True))
        p = p * (1.0 / jnp.sum(p, axis=1, keepdims=True))
        for k in range(GROUP // LANE):
            pw[m, 2 * i + k, 0:GROUP, :] = p[:, k * LANE : (k + 1) * LANE]
        zz[m, 1, :, cols[0]] = dot(v, p.astype(BF), 1, 1).astype(BF)
        return carry

    lax.fori_loop(0, NGROUP, unit, 0, unroll=True)


def channel_backward(m, qkv, pw, T, rr, msk):
    def unit(i, carry):
        cols = group_slices(i)
        mask = msk[m][:, :1]
        q = qkv[m, :, cols[0]].astype(BF)
        k = (qkv[m, :, cols[1]] * mask).astype(BF)
        v = qkv[m, :, cols[2]].astype(BF)
        g = T[:, cols[0]].astype(BF)
        p = jnp.concatenate([pw[m, 2 * i + k, 0:GROUP, :] for k in range(GROUP // LANE)], axis=1)
        dp = dot(g, v, 0, 0)
        ds = (p * (dp - jnp.sum(p * dp, axis=1, keepdims=True))).astype(BF)
        rr[m, 0, :, cols[0]] = (dot(k, ds, 1, 1) * SCALE).astype(BF)
        rr[m, 0, :, cols[1]] = (dot(q, ds) * (SCALE * mask)).astype(BF)
        rr[m, 0, :, cols[2]] = (dot(g, p.astype(BF))).astype(BF)
        return carry

    lax.fori_loop(0, NGROUP, unit, 0, unroll=True)


RING = 8
COLS = FF // RING
WIDE = FF // 12 * 8 // RING
REST = FF // 3 // RING
THIRD = FF // 3 * 2
LENT = RING * 3 // 4


def relay_kernel(
    wrows, wcols, img, cot, kern, bias, gain, move, first, second,
    act, ing, out1, out2, outs,
    kern_in, line_in, rows_in, cols_in, isem, wf, w2, pr, msk, flat, ubuf, gin, gout, zz, xh, rs, qkv, ab, rr, pw, U, C, T, sgp, sgs, sgm,
    rL, rR, rA, rG, buf, acc, going, got,
    wl, ws, wr, pl_, usem, gsem, us, gs, ss, rsem, es, er, sgsem, ssem, rcem, osem, sms, smr, xs, xr, ys, yr, bs, br, hs, hr, free,
):
    n = RING
    s = lax.axis_index("section")
    dp = lax.axis_index("dp")
    stage, c = s // 2, lax.rem(s, 2)
    mate = (dp, stage * 2 + (1 - c))
    opposite = (dp, (1 - stage) * 2 + c)
    diagonal = (dp, 3 - s)
    lender, helper = s == 1, s == 2
    early = stage == 0

    spot = lax.rem(dp, n)
    base = dp - spot
    me = jnp.where(lax.rem(spot, 2) == 0, spot // 2, n - 1 - spot // 2)

    def place(pos):
        pos = lax.rem(pos + 2 * n, n)
        return (base + jnp.where(pos < n // 2, 2 * pos, 2 * (n - 1 - pos) + 1), s)

    nexts = (place(me + 1), place(me - 1))
    rounds = n.bit_length() - 1
    partners = []
    for r in range(rounds):
        bit = 1 << r
        partners.append((jnp.where(lax.rem(spot // bit, 2) == 0, dp + bit, dp - bit), s))

    barrier = pltpu.get_barrier_semaphore()
    peers = [mate, opposite, diagonal, *nexts, *partners]
    for peer in peers:
        pl.semaphore_signal(barrier, inc=1, device_id=peer, device_id_type=MESH)
    pl.semaphore_wait(barrier, len(peers))

    def remote(src, dst, send, recv, peer):
        return pltpu.make_async_remote_copy(
            src_ref=src, dst_ref=dst, send_sem=send, recv_sem=recv, device_id=peer, device_id_type=MESH
        )

    half = second.shape[0]

    def group_part(group, part):
        cols = pl.ds(pl.multiple_of(part * D + group * GROUP, LANE), GROUP)
        return first.at[:, cols], wf.at[0, :, cols]

    def wait_group(group):
        for part in range(3):
            src, dst = group_part(group, part)
            i = group * 3 + part

            @pl.when(c == 0)
            def _():
                pltpu.make_async_copy(src, dst, wl.at[i]).wait()

            @pl.when(c == 1)
            def _():
                remote(src, dst, ws.at[i], wr.at[i], mate).wait_recv()

    def weight_parts(k):
        parts = []
        if k == 0:
            for group in range(NGROUP):
                for part in range(3):
                    parts.append(group_part(group, part))
            cols = pl.ds(3 * D, D)
            parts.append((first.at[:, cols], wf.at[k, :, cols]))
        else:
            for i in range(3):
                cols = pl.ds(i * (FF // 3), FF // 3)
                parts.append((first.at[:, cols], wf.at[k, :, cols]))
        third = half // 3
        for i in range(3):
            rows = pl.ds(i * third, third)
            parts.append((second.at[rows, :], w2.at[pl.ds(k * half + i * third, third), :]))
        return parts

    names = (
        [f"qkv{group}" for group in range(NGROUP) for _ in range(3)] + ["out"] + [f"low{i}" for i in range(3)],
        ["in"] * 3 + [f"high{i}" for i in range(3)],
    )

    def weight_copies(k):
        local = [pltpu.make_async_copy(a, b, wl.at[i]) for i, (a, b) in enumerate(weight_parts(k))]
        sent = [remote(a, b, ws.at[i], wr.at[i], mate) for i, (a, b) in enumerate(weight_parts(k))]
        return local, sent

    def params_copy(k):
        return remote(pr.at[k], pr.at[k], ws.at[13], wr.at[13], mate)

    own = flat.at[1]
    small_inputs = [
        pltpu.make_async_copy(a, b, isem.at[i])
        for i, (a, b) in enumerate(
            ((kern, kern_in), (bias, line_in.at[0]), (gain, line_in.at[1]), (move, line_in.at[2]), (wrows, rows_in), (wcols, cols_in))
        )
    ]
    for copy in small_inputs:
        copy.start()
    img_in = pltpu.make_async_copy(img, own, isem.at[6])
    cot_in = pltpu.make_async_copy(cot, own, isem.at[6])

    @pl.when(early)
    def _():
        img_in.start()

    for k in range(2):

        @pl.when(c == k)
        def _():
            local, sent = weight_copies(k)
            for here, there in zip(local, sent):
                here.start()
                there.start()

    for copy in small_inputs:
        copy.wait()
    pr[c, 0:9, :] = kern_in[...].astype(F32)
    for i in range(3):
        pr[c, 9 + i : 10 + i, :] = line_in[i].astype(F32)
    params_copy(c).start()

    def wait_weights(*wanted):
        for k in range(2):

            @pl.when(c == k)
            def _():
                for name, copy in zip(names[k], weight_copies(k)[0]):
                    if name in wanted:
                        copy.wait()
                for name, copy in zip(names[1 - k], weight_copies(1 - k)[1]):
                    if name in wanted:
                        copy.wait_recv()

    def wait_params(k):
        @pl.when(c != k)
        def _():
            params_copy(k).wait_recv()

    raw = flat.at[0]
    img_out = remote(img, raw, pl_.at[0], pl_.at[1], opposite)
    cot_out = remote(cot, raw, pl_.at[0], pl_.at[1], opposite)

    def pad(src, dst):
        blank = jnp.zeros((CELL - WIN, D), F32)
        for r in range(GRID):
            line = src[r].astype(F32)
            for wc in range(SIDE):
                cells = jnp.concatenate([line[wc * WIN : (wc + 1) * WIN], blank], axis=0)
                C[pl.ds(wc * HALF + r * CELL, CELL), :] = cells
        dst[...] = C[...].astype(BF)

    def unpad(dst):
        for r in range(GRID):
            sides = [C[pl.ds(wc * HALF + r * CELL, CELL), :][:WIN] for wc in range(SIDE)]
            dst[r] = jnp.concatenate(sides, axis=0).astype(BF)

    @pl.when(early)
    def _():
        cot_out.start()
        img_in.wait()
        pad(own, ubuf.at[0, 0])

    @pl.when(jnp.logical_not(early))
    def _():
        img_out.start()
        cot_in.start()
        cot_in.wait()
        pad(own, gin.at[1])

    index = lax.broadcasted_iota(jnp.int32, (ROWS, LANE), 0)
    cell = lax.rem(index, CELL)
    row = lax.rem(index, HALF) // CELL
    column = (index // HALF) * WIN + cell
    for m in range(2):
        inside = (row < WIN * rows_in[c + 2 * m]) & (column < WIN * cols_in[c + 2 * m]) & (cell < WIN)
        msk[m] = jnp.where(inside, 1.0, 0.0)

    @pl.when(jnp.logical_not(early))
    def _():
        cot_out.wait_recv()
        pad(raw, gin.at[0])
        for m in range(2):
            for l in range(D // LANE):
                cols = pl.ds(l * LANE, LANE)
                gin[m, :, cols] = (gin[m, :, cols].astype(F32) * msk[m]).astype(BF)

    for wc in range(SIDE):
        U[wc, 0] = jnp.zeros((CELL, D), F32)
        U[wc, GRID + 1] = jnp.zeros((CELL, D), F32)
    sgp[...] = jnp.zeros(sgp.shape, F32)

    def hop(m, dst, send, recv):
        sides = [pl.ds(i * D // 2, D // 2) for i in range(2)]
        return [
            remote(gout.at[m, :, cols], dst.at[:, cols], send.at[m, i], recv.at[m, i], opposite)
            for i, cols in enumerate(sides)
        ]

    def u_hop(m):
        return hop(m, ubuf.at[0, m], us, usem)

    def g_hop(m):
        return hop(m, gin.at[m], gs, gsem)

    def factor_copies(k, m):
        if k == 0:
            parts = [
                ("F", zz.at[m, 0], rL.at[m, 0]),
                ("F", zz.at[m, 1], rL.at[m, 1]),
                ("G", rr.at[m, 0, :, pl.ds(3 * D, D)], rR.at[m, :, pl.ds(3 * D, D)]),
                ("A", rr.at[m, 0, :, pl.ds(0, 3 * D)], rR.at[m, :, pl.ds(0, 3 * D)]),
            ]
        else:
            parts = [
                ("X0", zz.at[m, 2], rL.at[m, 0]),
                ("M", gin.at[m], rG.at[m]),
            ]
            for i, cols in enumerate((pl.ds(0, FF // 3 * 2), pl.ds(FF // 3 * 2, FF // 3))):
                parts.append((f"X{i}", ab.at[m, :, cols], rA.at[m, :, cols]))
                parts.append((f"H{i}", rr.at[m, 1, :, cols], rR.at[m, :, cols]))
        return [(w, remote(a, b, ss.at[m, i], rsem.at[m, i], mate)) for i, (w, a, b) in enumerate(parts)]

    def start_factors(m, which):
        for k in range(2):

            @pl.when(c != k)
            def _():
                for when, copy in factor_copies(k, m):
                    if when == which:
                        copy.start()

    def wait_factors(which):
        for k in range(2):

            @pl.when(c == k)
            def _():
                for m in range(2):
                    for when, copy in factor_copies(k, m):
                        if when[0] in which:
                            copy.wait_recv()

    def shard(k):
        return lax.rem(k + 4 * n, n)

    def sign(h):
        return 1 if h == 0 else -1

    def home(h, t):
        return shard(me + sign(h) - sign(h) * t)

    def products(terms):
        total = None
        for a, b in terms:
            part = dot(a[...], b[...], 0, 0)
            total = part if total is None else total + part
        return total

    def tile(sub, h, j):
        side = pl.ds(h * COLS, COLS)
        if sub in (0, 4):
            rows = first_rows(sub, h)
            last = jnp.where(j >= (3 * n) // 4, 1, 0)
            own = jnp.where(c == 1, 2, last)
            other = jnp.where(c == 1, 0, last)
            cols = lanes(j, COLS)
            terms = [(zz.at[m, own, :, rows], rr.at[m, c, :, cols]) for m in range(2)]
            terms += [(rL.at[m, other, :, rows], rR.at[m, :, cols]) for m in range(2)]
        elif sub == 3:
            cols = [pl.ds(pl.multiple_of(i * LENT * REST + j * REST, LANE), REST) for i in range(2)]
            terms = [(rA.at[m, :, cols[0]], rG.at[m, :, side]) for m in range(2)]
            terms += [(rA.at[m, :, cols[1]], gout.at[m, :, side]) for m in range(2)]
        else:
            cols = lanes(j, WIDE) if sub == 1 else pl.ds(pl.multiple_of(THIRD + j * REST, LANE), REST)
            terms = [(ab.at[m, :, cols], gin.at[m, :, side]) for m in range(2)]
            terms += [(rA.at[m, :, cols], rG.at[m, :, side]) for m in range(2)]
        return products(terms)

    sizes = (COLS // 3 * 2, WIDE, REST, REST, COLS // 3)
    starts = (0, COLS, COLS + WIDE, COLS + WIDE, COLS // 3 * 2)
    parts = [pl.ds(start, size) for start, size in zip(starts, sizes)]
    subs = range(len(sizes))
    odd = c == 1
    active = (None, odd, odd, helper, None)

    def where_live(sub, j, run):
        if sub == 2:
            pl.when(jnp.logical_not(lender) | (j >= LENT))(run)
        elif sub == 3:
            pl.when(j < LENT)(run)
        else:
            run()

    def first_rows(sub, h):
        return pl.ds(h * COLS + (0 if sub == 0 else sizes[0]), sizes[sub])

    def where_active(sub, run):
        if active[sub] is None:
            run()
        else:
            pl.when(active[sub])(run)


    def gathered(sub, h, j):
        if sub in (0, 4):
            return wf.at[0, first_rows(sub, h), lanes(j, COLS)]
        first_row = 0 if sub == 1 else THIRD
        return w2.at[pl.ds(pl.multiple_of(first_row + j * sizes[sub], 16), sizes[sub]), pl.ds(h * COLS, COLS)]

    def scatter(h, t, sub):
        src, dst = buf.at[h, t, parts[sub], :], buf.at[h, t + 1, parts[sub], :]
        return remote(src, dst, ssem.at[h, t, sub], rcem.at[h, t + 1, sub], nexts[h])

    def spread(h, t, sub, j):
        ref = gathered(sub, h, j)
        return remote(ref, ref, ssem.at[h, n - 1 + t, sub], rcem.at[h, n + t, sub], nexts[h])

    half_shards = n * 3 // 4

    def write(h, j, sub):
        src, side = gathered(sub, h, j), pl.ds(h * COLS, COLS)
        if sub in (0, 4):
            dst = out1.at[first_rows(sub, h), lanes(j, COLS)]
        elif sub == 1:
            dst = out2.at[pl.ds(pl.multiple_of((j - half_shards) * WIDE, 16), WIDE), side]
        else:
            dst = out2.at[pl.ds(pl.multiple_of(THIRD - FF // 2 + j * REST, 16), REST), side]
        if sub == 3:
            return remote(src, dst, bs.at[h, j], br.at[h, j], diagonal)
        return pltpu.make_async_copy(src, dst, osem.at[h, j, sub])

    def hand_over(h, j):
        dst = out2.at[pl.ds(pl.multiple_of(j * WIDE, 16), WIDE), pl.ds(h * COLS, COLS)]
        return remote(gathered(1, h, j), dst, hs.at[h, j], hr.at[h, j], mate)

    def deliver(h, j, sub):
        if sub == 1:

            @pl.when(j < half_shards)
            def _():
                hand_over(h, j).start()

            @pl.when(j >= half_shards)
            def _():
                write(h, j, sub).start()

        else:
            write(h, j, sub).start()

    def lend(m):
        cols, there = pl.ds(THIRD, LENT * REST), [rA.at[m, :, pl.ds(i * LENT * REST, LENT * REST)] for i in range(2)]
        return (
            remote(ab.at[m, :, cols], there[0], xs.at[m], xr.at[m], diagonal),
            remote(rA.at[m, :, cols], there[1], xs.at[2 + m], xr.at[2 + m], diagonal),
        )

    def share(m):
        return remote(gout.at[m], rG.at[m], ys.at[m], yr.at[m], mate)

    def reduce_event(sub, h, e):
        j = shard(me - sign(h) * e)

        @pl.when(e == n - 1)
        def _():
            pl.semaphore_wait(free.at[h, sub], 1)

        def run():
            total = tile(sub, h, j)

            @pl.when(e == 0)
            def _():
                buf[h, 0, parts[sub], :] = total.astype(BF)
                scatter(h, 0, sub).start()

            @pl.when((e > 0) & (e < n - 1))
            def _():
                scatter(h, e - 1, sub).wait_recv()
                buf[h, e, parts[sub], :] = (total + buf[h, e, parts[sub], :].astype(F32)).astype(BF)
                scatter(h, e, sub).start()

            @pl.when(e == n - 1)
            def _():
                scatter(h, n - 2, sub).wait_recv()
                gathered(sub, h, j)[...] = (total + buf[h, n - 1, parts[sub], :].astype(F32)).astype(BF)
                spread(h, 0, sub, j).start()
                deliver(h, j, sub)

        where_live(sub, j, run)

    def event(sub, e):
        for h in range(2):

            @pl.when(e < n)
            def _():
                reduce_event(sub, h, e)

            @pl.when((e >= n) & (e < 2 * n - 1))
            def _():
                t = e - (n - 1)
                j = home(h, t)

                def run():
                    spread(h, t - 1, sub, j).wait_recv()

                    @pl.when(t < n - 1)
                    def _():
                        spread(h, t, sub, j).start()

                    deliver(h, j, sub)

                where_live(sub, j, run)

    lead = jnp.where(early, 1, 2)

    def early_event(e, which):
        @pl.when(odd)
        def _():
            for sub in which:
                where_active(sub, lambda: event(sub, e))

    def small(r):
        return remote(going.at[r], got.at[r], sms.at[r], smr.at[r], partners[r])

    def mlp(m, order, wait):
        total, before, last = C[...], None, None
        for t in order:
            cols = pl.ds(t * FTILE, FTILE)
            h = dot(zz[m, 2], wf[1, :, cols])
            if last is not None:
                wait(last)
                total = total + dot(before, w2[pl.ds(last * FTILE, FTILE), :])
            a, d = gelu_parts(h)
            before, last = a.astype(BF), t
            ab[m, :, cols] = before
            rr[m, 1, :, cols] = d.astype(BF)
            if t == FF // FTILE * 2 // 3 - 1 and order == range(FF // FTILE):
                start_factors(m, "X0")
        wait(last)
        for i in range(2):
            cols = pl.ds(i * D // 2, D // 2)
            part = total[:, i * D // 2 : (i + 1) * D // 2]
            gout[jnp.where(early, m, 2 + m), :, cols] = (part + dot(before, w2[pl.ds(last * FTILE, FTILE), cols])).astype(BF)

            @pl.when(early)
            def _():
                u_hop(m)[i].start()

    def give_results(m):
        @pl.when(early)
        def _():
            C[...] = gout[m].astype(F32)

        @pl.when(jnp.logical_not(early))
        def _():
            for l in range(D // LANE):
                cols = pl.ds(l * LANE, LANE)
                C[:, cols] = gout[2 + m, :, cols].astype(F32) * msk[m]

        unpad(flat.at[m])

        @pl.when(early & (m == 0))
        def _():
            pltpu.make_async_copy(flat.at[0], ing, es.at[1]).start()

        @pl.when(early & (m == 1))
        def _():
            remote(flat.at[1], ing, es.at[1], er.at[1], opposite).start()

        @pl.when(jnp.logical_not(early) & (m == 0))
        def _():
            remote(flat.at[0], act, es.at[0], er.at[0], opposite).start()

        @pl.when(jnp.logical_not(early) & (m == 1))
        def _():
            pltpu.make_async_copy(flat.at[1], act, es.at[0]).start()

    def forward(m, p):
        @pl.when(jnp.logical_not(early))
        def _():
            for copy in u_hop(m):
                copy.wait_recv()

        @pl.when(early & (m == 1))
        def _():
            img_out.wait_recv()
            pad(raw, ubuf.at[0, 1])

        once = p == 0
        starting = early & once

        @pl.when(once)
        def _():
            wait_params(0)

        @pl.when(once & jnp.logical_not(early))
        def _():
            wait_params(1)
            wait_weights(*set(names[0] + names[1]))

        front_forward(0, m, ubuf, msk, pr, U, C, zz, xh, rs)

        @pl.when(early)
        def _():
            def head_group(group, carry):
                @pl.when(once)
                def _():
                    wait_group(group)

                for part in range(3):
                    cols = pl.ds(pl.multiple_of(part * D + group * GROUP, LANE), GROUP)
                    qkv[m, :, cols] = dot(zz[m, 0], wf[0, :, cols])
                window_forward(m, qkv, pw, T, group)
                return carry

            lax.fori_loop(0, NGROUP, head_group, 0)
            zz[m, 1] = T[...].astype(BF)

        @pl.when(starting)
        def _():
            wait_weights("out")
            wait_params(1)

        @pl.when(jnp.logical_not(early))
        def _():
            qkv[m] = dot(zz[m, 0], wf[0, :, pl.ds(0, 3 * D)])

        @pl.when(jnp.logical_not(early))
        def _():
            channel_forward(m, qkv, pw, zz, msk)

        ubuf[1, m] = (C[...] + dot(zz[m, 1], wf[0, :, pl.ds(3 * D, D)])).astype(BF)

        front_forward(1, m, ubuf, msk, pr, U, C, zz, xh, rs)

        @pl.when(starting)
        def _():
            wait_weights("in")
            order = [i + 3 * k for i in range(3) for k in range(2)]
            mlp(m, order, lambda t: wait_weights(f"low{t}" if t < 3 else f"high{t - 3}"))
            start_factors(m, "X0")

        @pl.when(jnp.logical_not(starting))
        def _():
            mlp(m, range(FF // FTILE), lambda t: None)

        start_factors(m, "F")
        start_factors(m, "X1")

        @pl.when(early & (m == 1))
        def _():
            wait_factors("FX")

        @pl.when(lender & (m == 1))
        def _():
            for i in range(2):
                for copy in lend(i):
                    copy.start()

    def backward(m):
        @pl.when(early)
        def _():
            for copy in g_hop(m):
                copy.wait_recv()
            start_factors(m, "M")

        for t in range(FF // FTILE):
            cols = pl.ds(t * FTILE, FTILE)
            da = dot(gin[m], w2[cols, :], 1, 1)
            rr[m, 1, :, cols] = (da * rr[m, 1, :, cols].astype(F32)).astype(BF)
            if t == FF // FTILE * 2 // 3 - 1:
                start_factors(m, "H0")

        start_factors(m, "H1")

        @pl.when(m == 1)
        def _():
            @pl.when(jnp.logical_not(early))
            def _():
                wait_factors("FX")

            wait_factors("M")

            @pl.when(jnp.logical_not(early))
            def _():
                early_event(0, (1, 2))

        T[...] = dot(rr[m, 1], wf[1], 1, 1)

        @pl.when(m == 1)
        def _():
            wait_factors("H")
            early_event(0, (0, 4))

        last = pl.ds(3 * D, D)

        @pl.when(early)
        def _():
            for copy in u_hop(m):
                copy.wait_send()

        def tail_lanes(i):
            return rr.at[m, 0, :, pl.ds(pl.multiple_of(3 * D + i * LANE, LANE), LANE)]

        def nothing(half):
            pass

        front_backward(1, m, msk, pr, U, T, lambda i: gin.at[m, :, lanes(i)], xh, rs, sgp, tail_lanes, nothing)

        start_factors(m, "G")
        T[...] = dot(rr[m, 0, :, last], wf[0, :, last], 1, 1)

        @pl.when(early)
        def _():
            window_backward(m, qkv, pw, T)
            for i in range(3):
                cols = pl.ds(i * D, D)
                rr[m, 0, :, cols] = qkv[m, :, cols].astype(BF)

        @pl.when(jnp.logical_not(early))
        def _():
            channel_backward(m, qkv, pw, T, rr, msk)

        start_factors(m, "A")

        @pl.when(m == 1)
        def _():
            early_event(1, (0, 4))
            early_event(lead - 1, (1, 2))

        T[...] = dot(rr[m, 0, :, pl.ds(0, 3 * D)], wf[0, :, pl.ds(0, 3 * D)], 1, 1)
        def send_half(half):
            @pl.when(jnp.logical_not(early))
            def _():
                g_hop(m)[half].start()

        front_backward(
            0, m, msk, pr, U, T, tail_lanes, xh, rs, sgp, lambda i: gout.at[m, :, lanes(i)], send_half
        )

        @pl.when(s == 3)
        def _():
            share(m).start()

    @pl.when(jnp.logical_not(early))
    def _():
        for m in range(2):
            start_factors(m, "M")

    def phase(p, carry):
        m = jnp.where(early, lax.rem(p, 2), p // 2)
        ahead = jnp.where(early, p < 2, lax.rem(p, 2) == 0)

        @pl.when(ahead)
        def _():
            forward(m, p)

        @pl.when(jnp.logical_not(ahead))
        def _():
            backward(m)

        return carry

    lax.fori_loop(0, 4, phase, 0)

    for h in range(2):
        for sub in subs:

            def ready():
                pl.semaphore_signal(free.at[h, sub], inc=1, device_id=nexts[1 - h], device_id_type=MESH)

            where_active(sub, ready)

    give = remote(sgs.at[1 - c], sgm, sgsem.at[0], sgsem.at[1], mate)

    def small_sums():
        for sec in range(2):
            for j in range(12):
                sgs[sec, j : j + 1, :] = jnp.sum(sgp[sec, j], axis=0, keepdims=True)
            sgs[sec, 12:16, :] = jnp.zeros((4, D), F32)
        give.start()

    wait_factors("GA")

    @pl.when(helper)
    def _():
        for m in range(2):
            for copy in lend(m):
                copy.wait_recv()
            share(m).wait_recv()

    def ring_step(t, carry):
        for sub in (0, 4):
            event(sub, t + jnp.where(odd, 2, 0))
        where_active(1, lambda: event(1, t + lead))
        where_active(2, lambda: event(2, t + lead))
        where_active(3, lambda: event(3, t))
        @pl.when((t >= 1) & (t < 5))
        def _():
            front_sums((t - 1) // 2, lax.rem(t - 1, 2), ubuf, msk, U, xh, sgp)

        pl.when(t == 5)(small_sums)

        @pl.when((t >= 6) & (t < 8))
        def _():
            give_results(t - 6)

        for r in range(rounds + 1):

            @pl.when(t == 6 + 2 * r)
            def _():
                if r == 0:
                    give.wait_recv()
                    acc[0] = sgs[c] + sgm[...]
                else:
                    small(r - 1).wait_recv()
                    acc[r] = going[r - 1].astype(F32) + got[r - 1].astype(F32)
                if r < rounds:
                    going[r] = acc[r].astype(BF)
                    small(r).start()

        return carry

    lax.fori_loop(0, 2 * n - 1, ring_step, 0)
    outs[...] = acc[rounds]

    for k in range(2):

        @pl.when(c == k)
        def _():
            for copy in weight_copies(k)[1]:
                copy.wait_send()
            params_copy(k).wait_send()
            for m in range(2):
                for _when, copy in factor_copies(1 - k, m):
                    copy.wait_send()

    give.wait_send()
    for r in range(rounds):
        small(r).wait_send()

    def drain(t, carry):
        for h in range(2):
            for sub in subs:

                def sent():
                    where_live(sub, shard(me - sign(h) * t), lambda: scatter(h, t, sub).wait_send())
                    where_live(sub, home(h, t), lambda: spread(h, t, sub, home(h, t)).wait_send())

                where_active(sub, sent)

        return carry

    lax.fori_loop(0, n - 1, drain, 0)

    def written(j, carry):
        for h in range(2):
            write(h, j, 0).wait()
            write(h, j, 4).wait()

            @pl.when(odd)
            def _():
                where_live(2, j, lambda: write(h, j, 2).wait())

                @pl.when(j < half_shards)
                def _():
                    hand_over(h, j).wait_send()

                @pl.when(j >= half_shards)
                def _():
                    write(h, j, 1).wait()

            @pl.when(jnp.logical_not(odd) & (j < half_shards))
            def _():
                hand_over(h, j).wait_recv()

            @pl.when(helper & (j < LENT))
            def _():
                write(h, j, 3).wait_send()

            @pl.when(lender & (j < LENT))
            def _():
                write(h, j, 3).wait_recv()

        return carry

    lax.fori_loop(0, n, written, 0)

    @pl.when(lender)
    def _():
        for m in range(2):
            for copy in lend(m):
                copy.wait_send()

    @pl.when(s == 3)
    def _():
        for m in range(2):
            share(m).wait_send()

    @pl.when(early)
    def _():
        cot_out.wait_send()
        pltpu.make_async_copy(flat.at[0], ing, es.at[1]).wait()
        remote(flat.at[1], ing, es.at[1], er.at[1], opposite).wait_send()
        remote(flat.at[0], act, es.at[0], er.at[0], opposite).wait_recv()

    @pl.when(jnp.logical_not(early))
    def _():
        img_out.wait_send()
        for m in range(2):
            for copy in g_hop(m):
                copy.wait_send()
        remote(flat.at[0], act, es.at[0], er.at[0], opposite).wait_send()
        pltpu.make_async_copy(flat.at[1], act, es.at[0]).wait()
        remote(flat.at[1], ing, es.at[1], er.at[1], opposite).wait_recv()


def relay(wrows, wcols, img, cot, kern, bias, gain, move, first, second):
    shape = jax.ShapeDtypeStruct
    vmem = pl.BlockSpec(memory_space=pltpu.VMEM)
    anywhere = pl.BlockSpec(memory_space=pl.ANY)
    dma = pltpu.SemaphoreType.DMA
    image = (ROWS, D)
    slot = img.shape
    rounds = RING.bit_length() - 1
    return pl.pallas_call(
        relay_kernel,
        out_shape=[
            shape(slot, BF),
            shape(slot, BF),
            shape((D, FF), BF),
            shape((FF // 2, D), BF),
            shape((16, D), F32),
        ],
        in_specs=[anywhere] * 10,
        out_specs=[anywhere] * 4 + [vmem],
        scratch_shapes=[
            pltpu.VMEM(kern.shape, BF),
            pltpu.VMEM((3,) + bias.shape, BF),
            pltpu.SMEM(wrows.shape, jnp.int32),
            pltpu.SMEM(wcols.shape, jnp.int32),
            dma((7,)),
            pltpu.VMEM((2, D, FF), BF),
            pltpu.VMEM((FF, D), BF),
            pltpu.VMEM((2, 16, D), F32),
            pltpu.VMEM((2, ROWS, LANE), F32),
            pltpu.VMEM((2,) + slot, BF),
            pltpu.VMEM((2, 2) + image, BF),
            pltpu.VMEM((2,) + image, BF),
            pltpu.VMEM((4,) + image, BF),
            pltpu.VMEM((2, 3) + image, BF),
            pltpu.VMEM((2, 2) + image, BF),
            pltpu.VMEM((2, 2, ROWS, LANE), F32),
            pltpu.VMEM((2, ROWS, 3 * D), F32),
            pltpu.VMEM((2, ROWS, FF), BF),
            pltpu.VMEM((2, 2, ROWS, FF), BF),
            pltpu.VMEM((2, UNITS, PACK * WROWS, LANE), F32),
            pltpu.VMEM((SIDE, GRID + 2, CELL, D), F32),
            pltpu.VMEM(image, F32),
            pltpu.VMEM(image, F32),
            pltpu.VMEM((2, 12, CELL, D), F32),
            pltpu.VMEM((2, 16, D), F32),
            pltpu.VMEM((16, D), F32),
            pltpu.VMEM((2, 2) + image, BF),
            pltpu.VMEM((2, ROWS, FF), BF),
            pltpu.VMEM((2, ROWS, FF), BF),
            pltpu.VMEM((2,) + image, BF),
            pltpu.VMEM((2, RING, COLS + WIDE + REST, COLS), BF),
            pltpu.VMEM((rounds + 1, 16, D), F32),
            pltpu.VMEM((rounds, 16, D), BF),
            pltpu.VMEM((rounds, 16, D), BF),
            dma((14,)),
            dma((14,)),
            dma((14,)),
            dma((2,)),
            dma((2, 2)),
            dma((2, 2)),
            dma((2, 2)),
            dma((2, 2)),
            dma((2, 8)),
            dma((2, 8)),
            dma((2,)),
            dma((2,)),
            dma((2,)),
            dma((2, 2 * RING, 5)),
            dma((2, 2 * RING, 5)),
            dma((2, RING, 5)),
            dma((rounds,)),
            dma((rounds,)),
            dma((4,)),
            dma((4,)),
            dma((2,)),
            dma((2,)),
            dma((2, RING)),
            dma((2, RING)),
            dma((2, RING)),
            dma((2, RING)),
            pltpu.SemaphoreType.REGULAR((2, 5)),
        ],
        name="relay",
        compiler_params=pltpu.CompilerParams(
            collective_id=1, has_side_effects=True, vmem_limit_bytes=63 * 2**20
        ),
    )(wrows, wcols, img, cot, kern, bias, gain, move, first, second)


def finish_kernel(
    out1, out2, act, ing, outs, first, second, acts, ings, kern, bias, gain, move,
    raw1, raw2, full1, full2, acted, graded, wide, small, kernels, rsem, wsem,
):
    steps = rsem.shape[0] - 3

    loads = [
        pltpu.make_async_copy(act, acted, rsem.at[steps]),
        pltpu.make_async_copy(ing, graded, rsem.at[steps + 1]),
        pltpu.make_async_copy(outs, small, rsem.at[steps + 2]),
    ]
    for copy in loads:
        copy.start()
    reads, writes = [], []
    for i in range(steps):
        pair = ((out1, raw1, full1, first), (out2, raw2, full2, second))[i % 2]
        src, raw, full, dst = pair
        half = steps // 2
        rows = pl.ds(i // 2 * (src.shape[0] // half), src.shape[0] // half)
        reads.append((pltpu.make_async_copy(src.at[rows, :], raw.at[rows, :], rsem.at[i]), raw, full, rows))
        writes.append(pltpu.make_async_copy(full.at[rows, :], dst.at[rows, :], wsem.at[i]))
    for copy, *_ in reads:
        copy.start()
    for (copy, raw, full, rows), back in zip(reads, writes):
        copy.wait()
        full[rows, :] = raw[rows, :].astype(F32)
        back.start()
    for copy in loads:
        copy.wait()
    for k in range(9):
        kernels[k] = small[k : k + 1, :]
    for r in range(GRID):
        line = graded[r].astype(F32)
        for k in range(GRID):
            wide[r, k] = line[k : k + 1, :]
    last = [
        pltpu.make_async_copy(acted, acts, wsem.at[steps]),
        pltpu.make_async_copy(wide, ings, wsem.at[steps + 1]),
        pltpu.make_async_copy(kernels, kern, wsem.at[steps + 2]),
    ]
    for i, dst in enumerate((bias, gain, move)):
        last.append(pltpu.make_async_copy(small.at[pl.ds(9 + i, 1), :], dst, wsem.at[steps + 3 + i]))
    for copy in last:
        copy.start()
    for copy in writes + last:
        copy.wait()


def finish(out1, out2, act, ing, outs):
    shape = jax.ShapeDtypeStruct
    slot = act.shape
    anywhere = pl.BlockSpec(memory_space=pl.ANY)
    line = (1, D)
    spread = slot[:2] + line
    steps = 16
    return pl.pallas_call(
        finish_kernel,
        out_shape=[
            shape(out1.shape, F32),
            shape(out2.shape, F32),
            shape(slot, BF),
            shape(spread, F32),
            shape((9,) + line, F32),
            shape(line, F32),
            shape(line, F32),
            shape(line, F32),
        ],
        in_specs=[anywhere] * 5,
        out_specs=[anywhere] * 8,
        scratch_shapes=[
            pltpu.VMEM(out1.shape, out1.dtype),
            pltpu.VMEM(out2.shape, out2.dtype),
            pltpu.VMEM(out1.shape, F32),
            pltpu.VMEM(out2.shape, F32),
            pltpu.VMEM(slot, BF),
            pltpu.VMEM(slot, BF),
            pltpu.VMEM(spread, F32),
            pltpu.VMEM(outs.shape, F32),
            pltpu.VMEM((9,) + line, F32),
            pltpu.SemaphoreType.DMA((steps + 3,)),
            pltpu.SemaphoreType.DMA((steps + 6,)),
        ],
        name="finish",
        compiler_params=pltpu.CompilerParams(vmem_limit_bytes=60 * 2**20),
    )(out1, out2, act, ing, outs)


def per_device(
    images, cotangent, window_rows, window_cols, pos_kernel, pos_bias, norm_gain, norm_shift, first_weight, second_weight
):
    act, ing, out1, out2, outs = relay(
        window_rows, window_cols, images[0], cotangent[0], pos_kernel[0], pos_bias, norm_gain, norm_shift,
        first_weight[0], second_weight,
    )
    if lax.axis_size("dp") > RING:
        out1, out2, outs = lax.psum((out1.astype(F32) / RING, out2.astype(F32) / RING, outs / RING), "dp")
    out1, out2, act, ing, kern, bias, gain, move = finish(out1, out2, act, ing, outs)
    return (
        act[None],
        ing.transpose(2, 0, 1, 3),
        out1[None],
        out2,
        kern.transpose(1, 0, 2),
        bias,
        gain,
        move,
    )


def solution(mesh):
    in_specs = (
        P(("dp", "section"), None, None, None),
        P(("dp", "section"), None, None, None),
        P("dp"),
        P("dp"),
        P("section", None, None),
        P("section", None),
        P("section", None),
        P("section", None),
        P("section", None, None),
        P("section", None),
    )
    out_specs = (
        P(("dp", "section"), None, None, None),
        P(("dp", "section"), None, None, None),
        P("section", None, None),
        P("section", None),
        P("section", None, None),
        P("section", None),
        P("section", None),
        P("section", None),
    )
    return jax.shard_map(per_device, mesh=mesh, in_specs=in_specs, out_specs=out_specs, check_vma=False)
```

```python
from functools import partial

import jax
import jax.numpy as jnp
from jax import lax
from jax.experimental import pallas as pl
from jax.experimental.pallas import tpu as pltpu
from jax.sharding import PartitionSpec as P

D = 768
FF = 3072
HEADS = 24
HEAD = 32
WIN = 7
SIDE = 2
GRID = SIDE * WIN
CELL = 8
WROWS = WIN * CELL
HALF = GRID * CELL
ROWS = SIDE * HALF
GROUP = 256
PACK = GROUP // HEAD
NGROUP = D // GROUP
UNITS = NGROUP * SIDE * SIDE
LANE = 128
FTILE = 512
EPS = 1e-05
SCALE = HEAD ** (-0.5)
BF = jnp.bfloat16
F32 = jnp.float32
MESH = pl.DeviceIdType.MESH


def dot(a, b, ca=1, cb=0):
    return lax.dot_general(a, b, (((ca,), (cb,)), ((), ())), preferred_element_type=F32)


def lanes(index, width=LANE):
    return pl.ds(pl.multiple_of(index * width, width), width)


def halves(value):
    return value.reshape(SIDE, GRID, CELL, value.shape[-1])


def shifts(left, right):
    column = lax.broadcasted_iota(jnp.int32, left.shape, 1)
    before0 = pltpu.roll(left, 1, 1)
    after0 = jnp.where(column == WIN - 1, pltpu.roll(right, CELL - 2, 1), pltpu.roll(left, CELL - 1, 1))
    before1 = jnp.where(column == 0, pltpu.roll(left, 2, 1), pltpu.roll(right, 1, 1))
    after1 = pltpu.roll(right, CELL - 1, 1)
    return ((before0, left, after0), (before1, right, after1))


def gelu_parts(h):
    expo = jnp.exp(h * h * -0.5)
    t = 1.0 / (1.0 + (0.3275911 * 0.7071067811865476) * jnp.abs(h))
    poly = t * (0.127414796 + t * (-0.142248368 + t * (0.7107068705 + t * (-0.7265760135 + t * 0.5307027145))))
    tail = poly * expo
    phi = jnp.where(h >= 0, 1.0 - tail, tail)
    return h * phi, phi + h * expo * 0.3989422804014327


def front_forward(sec, m, ubuf, msk, pr, U, C, zz, xh, rs):
    zero = jnp.zeros((ROWS, LANE), F32)

    def conv(i, total):
        ls = lanes(i)
        u = ubuf[sec, m, :, ls].astype(F32)
        masked = halves(u * msk[m])
        U[0, 1 : GRID + 1, :, ls] = masked[0]
        U[1, 1 : GRID + 1, :, ls] = masked[1]
        moved = shifts(U[0, :, :, ls], U[1, :, :, ls])
        taps = pr[sec, :, ls]
        uh = halves(u)
        sums = []
        for wc in range(SIDE):
            acc = uh[wc] + taps[9:10, :][None]
            for a in range(3):
                for b in range(3):
                    acc = acc + moved[wc][b][a : a + GRID] * taps[3 * a + b : 3 * a + b + 1, :][None]
            acc = acc.reshape(HALF, LANE)
            C[pl.ds(wc * HALF, HALF), ls] = acc
            sums.append(acc)
        return total + jnp.concatenate(sums, axis=0)

    mean = jnp.sum(lax.fori_loop(0, D // LANE, conv, zero, unroll=True), axis=-1, keepdims=True) * (1.0 / D)

    def spread(i, total):
        centred = C[:, lanes(i)] - mean
        return total + centred * centred

    var = jnp.sum(lax.fori_loop(0, D // LANE, spread, zero, unroll=True), axis=-1, keepdims=True) * (1.0 / D)
    rstd = lax.rsqrt(var + EPS)
    rs[sec, m] = jnp.broadcast_to(rstd, (ROWS, LANE))

    def norm(i, carry):
        ls = lanes(i)
        xhat = (C[:, ls] - mean) * rstd
        xh[sec, m, :, ls] = xhat.astype(BF)
        zz[m, 2 * sec, :, ls] = (xhat * pr[sec, 10:11, ls] + pr[sec, 11:12, ls]).astype(BF)
        return carry

    lax.fori_loop(0, D // LANE, norm, 0, unroll=True)


def fold(value):
    return jnp.sum(value.reshape(ROWS // CELL, CELL, LANE), axis=0)


def front_backward(sec, m, msk, pr, U, T, gfull, xh, rs, sgp, out, sent):
    zero = jnp.zeros((ROWS, LANE), F32)

    def sums(i, carry):
        s1, s2 = carry
        ls = lanes(i)
        dz = T[:, ls]
        xhat = xh[sec, m, :, ls].astype(F32)
        both = xhat * dz
        sgp[sec, 10, :, ls] += fold(both)
        sgp[sec, 11, :, ls] += fold(dz)
        gain = pr[sec, 10:11, ls]
        return s1 + dz * gain, s2 + both * gain

    s1, s2 = lax.fori_loop(0, D // LANE, sums, (zero, zero), unroll=True)
    m1 = jnp.sum(s1, axis=-1, keepdims=True) * (1.0 / D)
    m2 = jnp.sum(s2, axis=-1, keepdims=True) * (1.0 / D)

    def back(i, carry):
        ls = lanes(i)
        xhat = xh[sec, m, :, ls].astype(F32)
        inner = T[:, ls] * pr[sec, 10:11, ls] - m1 - xhat * m2
        gc = gfull(i)[...].astype(F32) + rs[sec, m] * inner
        xh[sec, m, :, ls] = gc.astype(BF)
        gh = halves(gc)
        U[0, 1 : GRID + 1, :, ls] = gh[0]
        U[1, 1 : GRID + 1, :, ls] = gh[1]
        moved = shifts(U[0, :, :, ls], U[1, :, :, ls])
        taps = pr[sec, :, ls]
        mask = halves(msk[m])
        du = []
        for wc in range(SIDE):
            acc = jnp.zeros((GRID, CELL, LANE), F32)
            for a in range(3):
                for b in range(3):
                    tap = 3 * a + b
                    acc = acc + moved[wc][2 - b][2 - a : 2 - a + GRID] * taps[tap : tap + 1, :][None]
            du.append((gh[wc] + mask[wc] * acc).reshape(HALF, LANE))
        out(i)[...] = jnp.concatenate(du, axis=0).astype(BF)
        return carry

    lax.fori_loop(0, D // LANE // 2, back, 0, unroll=True)
    sent(0)
    lax.fori_loop(D // LANE // 2, D // LANE, back, 0, unroll=True)
    sent(1)


def front_sums(sec, m, ubuf, msk, U, xh, sgp):
    def part(i, carry):
        ls = lanes(i)
        gc = xh[sec, m, :, ls].astype(F32)
        sgp[sec, 9, :, ls] += fold(gc)
        gh = halves(gc)
        U[0, 1 : GRID + 1, :, ls] = gh[0]
        U[1, 1 : GRID + 1, :, ls] = gh[1]
        moved = shifts(U[0, :, :, ls], U[1, :, :, ls])
        um = halves(ubuf[sec, m, :, ls].astype(F32) * msk[m])
        for a in range(3):
            for b in range(3):
                kg = jnp.zeros((CELL, LANE), F32)
                for wc in range(SIDE):
                    kg = kg + jnp.sum(moved[wc][2 - b][2 - a : 2 - a + GRID] * um[wc], axis=0)
                sgp[sec, 3 * a + b, :, ls] += kg
        return carry

    lax.fori_loop(0, D // LANE, part, 0)


def spread_heads(value, head_of_lane):
    parts = [jnp.where(head_of_lane == h, value, 0.0) for h in range(PACK)]
    return jnp.concatenate(parts, axis=0).astype(BF)


def gather_heads(value, rows, head_of_lane):
    out = jnp.zeros((rows, GROUP), F32)
    for h in range(PACK):
        out = jnp.where(head_of_lane == h, value[h * rows : (h + 1) * rows], out)
    return out


def unit_slices(unit):
    pair, group = unit // NGROUP, lax.rem(unit, NGROUP)
    rows = [pl.ds(pl.multiple_of((2 * pair + w) * WROWS, 8), WROWS) for w in range(2)]
    cols = [pl.ds(pl.multiple_of(part * D + group * GROUP, LANE), GROUP) for part in range(3)]
    return rows, cols


def window_parts(m, i, qkv):
    rows, cols = unit_slices(i)
    head_of_lane = lax.broadcasted_iota(jnp.int32, (WROWS, GROUP), 1) // HEAD
    q = [qkv[m, r, cols[0]].astype(BF) for r in rows]
    kd = [spread_heads(qkv[m, r, cols[1]], head_of_lane) for r in rows]
    vd = [spread_heads(qkv[m, r, cols[2]], head_of_lane) for r in rows]
    return rows, cols, head_of_lane, q, kd, vd


def window_forward(m, qkv, pw, T, group):
    def unit(i):
        rows, cols, head_of_lane, q, kd, vd = window_parts(m, i, qkv)
        s = [(dot(b, a, 1, 1) * SCALE).reshape(PACK, WROWS, WROWS) for a, b in zip(q, kd)]
        key = lax.broadcasted_iota(jnp.int32, s[0].shape, 1)
        real = lax.rem(key, CELL) < WIN
        s = [jnp.where(real, x, -1e30) for x in s]
        p = [jnp.exp(x - jnp.max(x, axis=1, keepdims=True)) for x in s]
        p = [x * (1.0 / jnp.sum(x, axis=1, keepdims=True)) for x in p]
        p = [x.reshape(PACK * WROWS, WROWS) for x in p]
        for w in range(2):
            pw[m, 2 * i + w, :, 0:WROWS] = p[w]
        out = [dot(x.astype(BF), v, 0, 0) for x, v in zip(p, vd)]
        for w in range(2):
            T[rows[w], cols[0]] = out[w]

    for pair in range(UNITS // 2 // NGROUP):
        unit(pair * NGROUP + group)


def window_backward(m, qkv, pw, T):
    def unit(i, carry):
        rows, cols, head_of_lane, q, kd, vd = window_parts(m, i, qkv)
        g = [T[r, cols[0]].astype(BF) for r in rows]
        p = [pw[m, 2 * i + w, :, 0:WROWS].reshape(PACK, WROWS, WROWS) for w in range(2)]
        dp = [dot(v, x, 1, 1).reshape(PACK, WROWS, WROWS) for v, x in zip(vd, g)]
        ds = [x * (y - jnp.sum(x * y, axis=1, keepdims=True)) for x, y in zip(p, dp)]
        ds = [x.reshape(PACK * WROWS, WROWS).astype(BF) for x in ds]
        pb = [x.reshape(PACK * WROWS, WROWS).astype(BF) for x in p]
        dv = [gather_heads(dot(x, y), WROWS, head_of_lane) for x, y in zip(pb, g)]
        dk = [gather_heads(dot(x, y), WROWS, head_of_lane) * SCALE for x, y in zip(ds, q)]
        dq = [dot(x, y, 0, 0) * SCALE for x, y in zip(ds, kd)]
        for w in range(2):
            qkv[m, rows[w], cols[0]] = dq[w]
            qkv[m, rows[w], cols[1]] = dk[w]
            qkv[m, rows[w], cols[2]] = dv[w]
        return carry

    lax.fori_loop(0, UNITS // 2, unit, 0)


def group_slices(group):
    return [pl.ds(pl.multiple_of(part * D + group * GROUP, LANE), GROUP) for part in range(3)]


def channel_forward(m, qkv, pw, zz, msk):
    def unit(i, carry):
        cols = group_slices(i)
        mask = msk[m][:, :1]
        q = qkv[m, :, cols[0]].astype(BF)
        k = (qkv[m, :, cols[1]] * mask).astype(BF)
        v = qkv[m, :, cols[2]].astype(BF)
        s = dot(q, k, 0, 0) * SCALE
        same = (lax.broadcasted_iota(jnp.int32, s.shape, 0) // HEAD) == (lax.broadcasted_iota(jnp.int32, s.shape, 1) // HEAD)
        s = jnp.where(same, s, -1e30)
        p = jnp.exp(s - jnp.max(s, axis=1, keepdims=True))
        p = p * (1.0 / jnp.sum(p, axis=1, keepdims=True))
        for k in range(GROUP // LANE):
            pw[m, 2 * i + k, 0:GROUP, :] = p[:, k * LANE : (k + 1) * LANE]
        zz[m, 1, :, cols[0]] = dot(v, p.astype(BF), 1, 1).astype(BF)
        return carry

    lax.fori_loop(0, NGROUP, unit, 0, unroll=True)


def channel_backward(m, qkv, pw, T, rr, msk):
    def unit(i, carry):
        cols = group_slices(i)
        mask = msk[m][:, :1]
        q = qkv[m, :, cols[0]].astype(BF)
        k = (qkv[m, :, cols[1]] * mask).astype(BF)
        v = qkv[m, :, cols[2]].astype(BF)
        g = T[:, cols[0]].astype(BF)
        p = jnp.concatenate([pw[m, 2 * i + k, 0:GROUP, :] for k in range(GROUP // LANE)], axis=1)
        dp = dot(g, v, 0, 0)
        ds = (p * (dp - jnp.sum(p * dp, axis=1, keepdims=True))).astype(BF)
        rr[m, 0, :, cols[0]] = (dot(k, ds, 1, 1) * SCALE).astype(BF)
        rr[m, 0, :, cols[1]] = (dot(q, ds) * (SCALE * mask)).astype(BF)
        rr[m, 0, :, cols[2]] = (dot(g, p.astype(BF))).astype(BF)
        return carry

    lax.fori_loop(0, NGROUP, unit, 0, unroll=True)


RING = 8
COLS = FF // RING
WIDE = FF // 12 * 8 // RING
REST = FF // 3 // RING
THIRD = FF // 3 * 2
LENT = RING * 7 // 8
EARLY = 2


def relay_kernel(
    wrows, wcols, img, cot, kern, bias, gain, move, first, second,
    act, ing, out1, out2, outs,
    kern_in, line_in, rows_in, cols_in, isem, wf, w2, pr, msk, flat, ubuf, gin, gout, zz, xh, rs, qkv, ab, rr, pw, U, C, T, sgp, sgs, sgm,
    rL, rR, rA, rG, buf, acc, going, got,
    wl, ws, wr, pl_, usem, gsem, us, gs, ss, rsem, es, er, sgsem, ssem, rcem, osem, sms, smr, xs, xr, ys, yr, bs, br, hs, hr, free,
):
    n = RING
    s = lax.axis_index("section")
    dp = lax.axis_index("dp")
    stage, c = s // 2, lax.rem(s, 2)
    mate = (dp, stage * 2 + (1 - c))
    opposite = (dp, (1 - stage) * 2 + c)
    diagonal = (dp, 3 - s)
    lender, helper = s == 1, s == 2
    early = stage == 0

    spot = lax.rem(dp, n)
    base = dp - spot
    me = jnp.where(lax.rem(spot, 2) == 0, spot // 2, n - 1 - spot // 2)

    def place(pos):
        pos = lax.rem(pos + 2 * n, n)
        return (base + jnp.where(pos < n // 2, 2 * pos, 2 * (n - 1 - pos) + 1), s)

    nexts = (place(me + 1), place(me - 1))
    rounds = n.bit_length() - 1
    partners = []
    for r in range(rounds):
        bit = 1 << r
        partners.append((jnp.where(lax.rem(spot // bit, 2) == 0, dp + bit, dp - bit), s))

    barrier = pltpu.get_barrier_semaphore()
    peers = [mate, opposite, diagonal, *nexts, *partners]
    for peer in peers:
        pl.semaphore_signal(barrier, inc=1, device_id=peer, device_id_type=MESH)
    pl.semaphore_wait(barrier, len(peers))

    def remote(src, dst, send, recv, peer):
        return pltpu.make_async_remote_copy(
            src_ref=src, dst_ref=dst, send_sem=send, recv_sem=recv, device_id=peer, device_id_type=MESH
        )

    half = second.shape[0]

    def group_part(group, part):
        cols = pl.ds(pl.multiple_of(part * D + group * GROUP, LANE), GROUP)
        return first.at[:, cols], wf.at[0, :, cols]

    def wait_group(group):
        for part in range(3):
            src, dst = group_part(group, part)
            i = group * 3 + part

            @pl.when(c == 0)
            def _():
                pltpu.make_async_copy(src, dst, wl.at[i]).wait()

            @pl.when(c == 1)
            def _():
                remote(src, dst, ws.at[i], wr.at[i], mate).wait_recv()

    def weight_parts(k):
        parts = []
        if k == 0:
            for group in range(NGROUP):
                for part in range(3):
                    parts.append(group_part(group, part))
            cols = pl.ds(3 * D, D)
            parts.append((first.at[:, cols], wf.at[k, :, cols]))
        else:
            for i in range(3):
                cols = pl.ds(i * (FF // 3), FF // 3)
                parts.append((first.at[:, cols], wf.at[k, :, cols]))
        third = half // 3
        for i in range(3):
            rows = pl.ds(i * third, third)
            parts.append((second.at[rows, :], w2.at[pl.ds(k * half + i * third, third), :]))
        return parts

    names = (
        [f"qkv{group}" for group in range(NGROUP) for _ in range(3)] + ["out"] + [f"low{i}" for i in range(3)],
        ["in"] * 3 + [f"high{i}" for i in range(3)],
    )

    def weight_copies(k):
        local = [pltpu.make_async_copy(a, b, wl.at[i]) for i, (a, b) in enumerate(weight_parts(k))]
        sent = [remote(a, b, ws.at[i], wr.at[i], mate) for i, (a, b) in enumerate(weight_parts(k))]
        return local, sent

    def params_copy(k):
        return remote(pr.at[k], pr.at[k], ws.at[13], wr.at[13], mate)

    own = flat.at[1]
    small_inputs = [
        pltpu.make_async_copy(a, b, isem.at[i])
        for i, (a, b) in enumerate(
            ((kern, kern_in), (bias, line_in.at[0]), (gain, line_in.at[1]), (move, line_in.at[2]), (wrows, rows_in), (wcols, cols_in))
        )
    ]
    for copy in small_inputs:
        copy.start()
    img_in = pltpu.make_async_copy(img, own, isem.at[6])
    cot_in = pltpu.make_async_copy(cot, own, isem.at[6])

    @pl.when(early)
    def _():
        img_in.start()

    for k in range(2):

        @pl.when(c == k)
        def _():
            local, sent = weight_copies(k)
            for here, there in zip(local, sent):
                here.start()
                there.start()

    for copy in small_inputs:
        copy.wait()
    pr[c, 0:9, :] = kern_in[...].astype(F32)
    for i in range(3):
        pr[c, 9 + i : 10 + i, :] = line_in[i].astype(F32)
    params_copy(c).start()

    def wait_weights(*wanted):
        for k in range(2):

            @pl.when(c == k)
            def _():
                for name, copy in zip(names[k], weight_copies(k)[0]):
                    if name in wanted:
                        copy.wait()
                for name, copy in zip(names[1 - k], weight_copies(1 - k)[1]):
                    if name in wanted:
                        copy.wait_recv()

    def wait_params(k):
        @pl.when(c != k)
        def _():
            params_copy(k).wait_recv()

    raw = flat.at[0]
    img_out = remote(img, raw, pl_.at[0], pl_.at[1], opposite)
    cot_out = remote(cot, raw, pl_.at[0], pl_.at[1], opposite)

    def pad(src, dst):
        blank = jnp.zeros((CELL - WIN, D), F32)
        for r in range(GRID):
            line = src[r].astype(F32)
            for wc in range(SIDE):
                cells = jnp.concatenate([line[wc * WIN : (wc + 1) * WIN], blank], axis=0)
                C[pl.ds(wc * HALF + r * CELL, CELL), :] = cells
        dst[...] = C[...].astype(BF)

    def unpad(dst):
        for r in range(GRID):
            sides = [C[pl.ds(wc * HALF + r * CELL, CELL), :][:WIN] for wc in range(SIDE)]
            dst[r] = jnp.concatenate(sides, axis=0).astype(BF)

    @pl.when(early)
    def _():
        cot_out.start()
        img_in.wait()
        pad(own, ubuf.at[0, 0])

    @pl.when(jnp.logical_not(early))
    def _():
        img_out.start()
        cot_in.start()
        cot_in.wait()
        pad(own, gin.at[1])

    index = lax.broadcasted_iota(jnp.int32, (ROWS, LANE), 0)
    cell = lax.rem(index, CELL)
    row = lax.rem(index, HALF) // CELL
    column = (index // HALF) * WIN + cell
    for m in range(2):
        inside = (row < WIN * rows_in[c + 2 * m]) & (column < WIN * cols_in[c + 2 * m]) & (cell < WIN)
        msk[m] = jnp.where(inside, 1.0, 0.0)

    @pl.when(jnp.logical_not(early))
    def _():
        cot_out.wait_recv()
        pad(raw, gin.at[0])
        for m in range(2):
            for l in range(D // LANE):
                cols = pl.ds(l * LANE, LANE)
                gin[m, :, cols] = (gin[m, :, cols].astype(F32) * msk[m]).astype(BF)

    for wc in range(SIDE):
        U[wc, 0] = jnp.zeros((CELL, D), F32)
        U[wc, GRID + 1] = jnp.zeros((CELL, D), F32)
    sgp[...] = jnp.zeros(sgp.shape, F32)

    def hop(m, dst, send, recv):
        sides = [pl.ds(i * D // 2, D // 2) for i in range(2)]
        return [
            remote(gout.at[m, :, cols], dst.at[:, cols], send.at[m, i], recv.at[m, i], opposite)
            for i, cols in enumerate(sides)
        ]

    def u_hop(m):
        return hop(m, ubuf.at[0, m], us, usem)

    def g_hop(m):
        return hop(m, gin.at[m], gs, gsem)

    def factor_copies(k, m):
        if k == 0:
            parts = [
                ("F", zz.at[m, 0], rL.at[m, 0]),
                ("F", zz.at[m, 1], rL.at[m, 1]),
                ("G", rr.at[m, 0, :, pl.ds(3 * D, D)], rR.at[m, :, pl.ds(3 * D, D)]),
                ("A", rr.at[m, 0, :, pl.ds(0, 3 * D)], rR.at[m, :, pl.ds(0, 3 * D)]),
            ]
        else:
            parts = [
                ("X0", zz.at[m, 2], rL.at[m, 0]),
                ("M", gin.at[m], rG.at[m]),
            ]
            for i, cols in enumerate((pl.ds(0, FF // 3 * 2), pl.ds(FF // 3 * 2, FF // 3))):
                parts.append((f"X{i}", ab.at[m, :, cols], rA.at[m, :, cols]))
                parts.append((f"H{i}", rr.at[m, 1, :, cols], rR.at[m, :, cols]))
        return [(w, remote(a, b, ss.at[m, i], rsem.at[m, i], mate)) for i, (w, a, b) in enumerate(parts)]

    def start_factors(m, which):
        for k in range(2):

            @pl.when(c != k)
            def _():
                for when, copy in factor_copies(k, m):
                    if when == which:
                        copy.start()

    def wait_factors(which):
        for k in range(2):

            @pl.when(c == k)
            def _():
                for m in range(2):
                    for when, copy in factor_copies(k, m):
                        if when[0] in which:
                            copy.wait_recv()

    def shard(k):
        return lax.rem(k + 4 * n, n)

    def sign(h):
        return 1 if h == 0 else -1

    def home(h, t):
        return shard(me + sign(h) - sign(h) * t)

    def products(terms):
        total = None
        for a, b in terms:
            part = dot(a[...], b[...], 0, 0)
            total = part if total is None else total + part
        return total

    def tile(sub, h, j):
        side = pl.ds(h * COLS, COLS)
        if sub in (0, 4):
            rows = first_rows(sub, h)
            last = jnp.where(j >= (3 * n) // 4, 1, 0)
            own = jnp.where(c == 1, 2, last)
            other = jnp.where(c == 1, 0, last)
            cols = lanes(j, COLS)
            terms = [(zz.at[m, own, :, rows], rr.at[m, c, :, cols]) for m in range(2)]
            terms += [(rL.at[m, other, :, rows], rR.at[m, :, cols]) for m in range(2)]
        elif sub == 3:
            cols = [pl.ds(pl.multiple_of(i * LENT * REST + j * REST, LANE), REST) for i in range(2)]
            terms = [(rA.at[m, :, cols[0]], rG.at[m, :, side]) for m in range(2)]
            terms += [(rA.at[m, :, cols[1]], gout.at[m, :, side]) for m in range(2)]
        else:
            cols = lanes(j, WIDE) if sub == 1 else pl.ds(pl.multiple_of(THIRD + j * REST, LANE), REST)
            terms = [(ab.at[m, :, cols], gin.at[m, :, side]) for m in range(2)]
            terms += [(rA.at[m, :, cols], rG.at[m, :, side]) for m in range(2)]
        return products(terms)

    sizes = (COLS // 3 * 2, WIDE, REST, REST, COLS // 3)
    starts = (0, COLS, COLS + WIDE, COLS + WIDE, COLS // 3 * 2)
    parts = [pl.ds(start, size) for start, size in zip(starts, sizes)]
    subs = range(len(sizes))
    odd = c == 1
    active = (None, odd, odd, helper, None)

    def where_live(sub, j, run):
        if sub == 2:
            pl.when(jnp.logical_not(lender) | (j >= LENT))(run)
        elif sub == 3:
            pl.when(j < LENT)(run)
        else:
            run()

    def first_rows(sub, h):
        return pl.ds(h * COLS + (0 if sub == 0 else sizes[0]), sizes[sub])

    def where_active(sub, run):
        if active[sub] is None:
            run()
        else:
            pl.when(active[sub])(run)


    def gathered(sub, h, j):
        if sub in (0, 4):
            return wf.at[0, first_rows(sub, h), lanes(j, COLS)]
        first_row = 0 if sub == 1 else THIRD
        return w2.at[pl.ds(pl.multiple_of(first_row + j * sizes[sub], 16), sizes[sub]), pl.ds(h * COLS, COLS)]

    def scatter(h, t, sub):
        src, dst = buf.at[h, t, parts[sub], :], buf.at[h, t + 1, parts[sub], :]
        return remote(src, dst, ssem.at[h, t, sub], rcem.at[h, t + 1, sub], nexts[h])

    def spread(h, t, sub, j):
        ref = gathered(sub, h, j)
        return remote(ref, ref, ssem.at[h, n - 1 + t, sub], rcem.at[h, n + t, sub], nexts[h])

    half_shards = n * 3 // 4

    def write(h, j, sub):
        src, side = gathered(sub, h, j), pl.ds(h * COLS, COLS)
        if sub in (0, 4):
            dst = out1.at[first_rows(sub, h), lanes(j, COLS)]
        elif sub == 1:
            dst = out2.at[pl.ds(pl.multiple_of((j - half_shards) * WIDE, 16), WIDE), side]
        else:
            dst = out2.at[pl.ds(pl.multiple_of(THIRD - FF // 2 + j * REST, 16), REST), side]
        if sub == 3:
            return remote(src, dst, bs.at[h, j], br.at[h, j], diagonal)
        return pltpu.make_async_copy(src, dst, osem.at[h, j, sub])

    def hand_over(h, j):
        dst = out2.at[pl.ds(pl.multiple_of(j * WIDE, 16), WIDE), pl.ds(h * COLS, COLS)]
        return remote(gathered(1, h, j), dst, hs.at[h, j], hr.at[h, j], mate)

    def deliver(h, j, sub):
        if sub == 1:

            @pl.when(j < half_shards)
            def _():
                hand_over(h, j).start()

            @pl.when(j >= half_shards)
            def _():
                write(h, j, sub).start()

        else:
            write(h, j, sub).start()

    def lend(m):
        cols, there = pl.ds(THIRD, LENT * REST), [rA.at[m, :, pl.ds(i * LENT * REST, LENT * REST)] for i in range(2)]
        return (
            remote(ab.at[m, :, cols], there[0], xs.at[m], xr.at[m], diagonal),
            remote(rA.at[m, :, cols], there[1], xs.at[2 + m], xr.at[2 + m], diagonal),
        )

    def share(m):
        return remote(gout.at[m], rG.at[m], ys.at[m], yr.at[m], mate)

    def reduce_event(sub, h, e):
        j = shard(me - sign(h) * e)

        @pl.when(e == n - 1)
        def _():
            pl.semaphore_wait(free.at[h, sub], 1)

        def run():
            total = tile(sub, h, j)

            @pl.when(e == 0)
            def _():
                buf[h, 0, parts[sub], :] = total.astype(BF)
                scatter(h, 0, sub).start()

            @pl.when((e > 0) & (e < n - 1))
            def _():
                scatter(h, e - 1, sub).wait_recv()
                buf[h, e, parts[sub], :] = (total + buf[h, e, parts[sub], :].astype(F32)).astype(BF)
                scatter(h, e, sub).start()

            @pl.when(e == n - 1)
            def _():
                scatter(h, n - 2, sub).wait_recv()
                gathered(sub, h, j)[...] = (total + buf[h, n - 1, parts[sub], :].astype(F32)).astype(BF)
                spread(h, 0, sub, j).start()
                deliver(h, j, sub)

        where_live(sub, j, run)

    def event(sub, e):
        for h in range(2):

            @pl.when(e < n)
            def _():
                reduce_event(sub, h, e)

            @pl.when((e >= n) & (e < 2 * n - 1))
            def _():
                t = e - (n - 1)
                j = home(h, t)

                def run():
                    spread(h, t - 1, sub, j).wait_recv()

                    @pl.when(t < n - 1)
                    def _():
                        spread(h, t, sub, j).start()

                    deliver(h, j, sub)

                where_live(sub, j, run)

    def early_event(e, which):
        @pl.when(odd)
        def _():
            for sub in which:
                where_active(sub, lambda: event(sub, e))

    def small(r):
        return remote(going.at[r], got.at[r], sms.at[r], smr.at[r], partners[r])

    def mlp(m, order, wait):
        total, before, last = C[...], None, None
        for t in order:
            cols = pl.ds(t * FTILE, FTILE)
            h = dot(zz[m, 2], wf[1, :, cols])
            if last is not None:
                wait(last)
                total = total + dot(before, w2[pl.ds(last * FTILE, FTILE), :])
            a, d = gelu_parts(h)
            before, last = a.astype(BF), t
            ab[m, :, cols] = before
            rr[m, 1, :, cols] = d.astype(BF)
            if t == FF // FTILE * 2 // 3 - 1 and order == range(FF // FTILE):
                start_factors(m, "X0")
        wait(last)
        for i in range(2):
            cols = pl.ds(i * D // 2, D // 2)
            part = total[:, i * D // 2 : (i + 1) * D // 2]
            gout[jnp.where(early, m, 2 + m), :, cols] = (part + dot(before, w2[pl.ds(last * FTILE, FTILE), cols])).astype(BF)

            @pl.when(early)
            def _():
                u_hop(m)[i].start()

    def give_results(m):
        @pl.when(early)
        def _():
            C[...] = gout[m].astype(F32)

        @pl.when(jnp.logical_not(early))
        def _():
            for l in range(D // LANE):
                cols = pl.ds(l * LANE, LANE)
                C[:, cols] = gout[2 + m, :, cols].astype(F32) * msk[m]

        unpad(flat.at[m])

        @pl.when(early & (m == 0))
        def _():
            pltpu.make_async_copy(flat.at[0], ing, es.at[1]).start()

        @pl.when(early & (m == 1))
        def _():
            remote(flat.at[1], ing, es.at[1], er.at[1], opposite).start()

        @pl.when(jnp.logical_not(early) & (m == 0))
        def _():
            remote(flat.at[0], act, es.at[0], er.at[0], opposite).start()

        @pl.when(jnp.logical_not(early) & (m == 1))
        def _():
            pltpu.make_async_copy(flat.at[1], act, es.at[0]).start()

    def forward(m, p):
        @pl.when(jnp.logical_not(early))
        def _():
            for copy in u_hop(m):
                copy.wait_recv()

        @pl.when(early & (m == 1))
        def _():
            img_out.wait_recv()
            pad(raw, ubuf.at[0, 1])

        once = p == 0
        starting = early & once

        @pl.when(once)
        def _():
            wait_params(0)

        @pl.when(once & jnp.logical_not(early))
        def _():
            wait_params(1)
            wait_weights(*set(names[0] + names[1]))

        front_forward(0, m, ubuf, msk, pr, U, C, zz, xh, rs)

        @pl.when(early)
        def _():
            def head_group(group, carry):
                @pl.when(once)
                def _():
                    wait_group(group)

                for part in range(3):
                    cols = pl.ds(pl.multiple_of(part * D + group * GROUP, LANE), GROUP)
                    qkv[m, :, cols] = dot(zz[m, 0], wf[0, :, cols])
                window_forward(m, qkv, pw, T, group)
                return carry

            lax.fori_loop(0, NGROUP, head_group, 0)
            zz[m, 1] = T[...].astype(BF)

        @pl.when(starting)
        def _():
            wait_weights("out")
            wait_params(1)

        @pl.when(jnp.logical_not(early))
        def _():
            qkv[m] = dot(zz[m, 0], wf[0, :, pl.ds(0, 3 * D)])

        @pl.when(jnp.logical_not(early))
        def _():
            channel_forward(m, qkv, pw, zz, msk)

        ubuf[1, m] = (C[...] + dot(zz[m, 1], wf[0, :, pl.ds(3 * D, D)])).astype(BF)

        front_forward(1, m, ubuf, msk, pr, U, C, zz, xh, rs)

        @pl.when(starting)
        def _():
            wait_weights("in")
            order = [i + 3 * k for i in range(3) for k in range(2)]
            mlp(m, order, lambda t: wait_weights(f"low{t}" if t < 3 else f"high{t - 3}"))
            start_factors(m, "X0")

        @pl.when(jnp.logical_not(starting))
        def _():
            mlp(m, range(FF // FTILE), lambda t: None)

        start_factors(m, "F")
        start_factors(m, "X1")

        @pl.when(early & (m == 1))
        def _():
            wait_factors("FX")

        @pl.when(lender & (m == 1))
        def _():
            for i in range(2):
                for copy in lend(i):
                    copy.start()

    def backward(m):
        @pl.when(early)
        def _():
            for copy in g_hop(m):
                copy.wait_recv()
            start_factors(m, "M")

        for t in range(FF // FTILE):
            cols = pl.ds(t * FTILE, FTILE)
            da = dot(gin[m], w2[cols, :], 1, 1)
            rr[m, 1, :, cols] = (da * rr[m, 1, :, cols].astype(F32)).astype(BF)
            if t == FF // FTILE * 2 // 3 - 1:
                start_factors(m, "H0")

        start_factors(m, "H1")

        @pl.when(m == 1)
        def _():
            @pl.when(jnp.logical_not(early))
            def _():
                wait_factors("FX")

            wait_factors("M")
            early_event(0, (1, 2))

        T[...] = dot(rr[m, 1], wf[1], 1, 1)

        @pl.when(m == 1)
        def _():
            wait_factors("H")
            early_event(0, (0, 4))

        last = pl.ds(3 * D, D)

        @pl.when(early)
        def _():
            for copy in u_hop(m):
                copy.wait_send()

        def tail_lanes(i):
            return rr.at[m, 0, :, pl.ds(pl.multiple_of(3 * D + i * LANE, LANE), LANE)]

        def nothing(half):
            pass

        front_backward(1, m, msk, pr, U, T, lambda i: gin.at[m, :, lanes(i)], xh, rs, sgp, tail_lanes, nothing)

        start_factors(m, "G")
        T[...] = dot(rr[m, 0, :, last], wf[0, :, last], 1, 1)

        @pl.when(early)
        def _():
            window_backward(m, qkv, pw, T)
            for i in range(3):
                cols = pl.ds(i * D, D)
                rr[m, 0, :, cols] = qkv[m, :, cols].astype(BF)

        @pl.when(jnp.logical_not(early))
        def _():
            channel_backward(m, qkv, pw, T, rr, msk)

        start_factors(m, "A")

        @pl.when(m == 1)
        def _():
            early_event(1, (1, 2, 0, 4))

        T[...] = dot(rr[m, 0, :, pl.ds(0, 3 * D)], wf[0, :, pl.ds(0, 3 * D)], 1, 1)
        def send_half(half):
            @pl.when(jnp.logical_not(early))
            def _():
                g_hop(m)[half].start()

        front_backward(
            0, m, msk, pr, U, T, tail_lanes, xh, rs, sgp, lambda i: gout.at[m, :, lanes(i)], send_half
        )

        @pl.when(s == 3)
        def _():
            share(m).start()

    @pl.when(jnp.logical_not(early))
    def _():
        for m in range(2):
            start_factors(m, "M")

    def phase(p, carry):
        m = jnp.where(early, lax.rem(p, 2), p // 2)
        ahead = jnp.where(early, p < 2, lax.rem(p, 2) == 0)

        @pl.when(ahead)
        def _():
            forward(m, p)

        @pl.when(jnp.logical_not(ahead))
        def _():
            backward(m)

        return carry

    lax.fori_loop(0, 4, phase, 0)

    for h in range(2):
        for sub in subs:

            def ready():
                pl.semaphore_signal(free.at[h, sub], inc=1, device_id=nexts[1 - h], device_id_type=MESH)

            where_active(sub, ready)

    give = remote(sgs.at[1 - c], sgm, sgsem.at[0], sgsem.at[1], mate)

    def small_sums():
        for sec in range(2):
            for j in range(12):
                sgs[sec, j : j + 1, :] = jnp.sum(sgp[sec, j], axis=0, keepdims=True)
            sgs[sec, 12:16, :] = jnp.zeros((4, D), F32)
        give.start()

    wait_factors("GA")

    @pl.when(helper)
    def _():
        for m in range(2):
            for copy in lend(m):
                copy.wait_recv()
            share(m).wait_recv()

    def ring_step(t, carry):
        for sub in (0, 4):
            event(sub, t + jnp.where(odd, EARLY, 0))
        where_active(1, lambda: event(1, t + EARLY))
        where_active(2, lambda: event(2, t + EARLY))
        where_active(3, lambda: event(3, t))
        @pl.when((t >= 1) & (t < 5))
        def _():
            front_sums((t - 1) // 2, lax.rem(t - 1, 2), ubuf, msk, U, xh, sgp)

        pl.when(t == 5)(small_sums)

        @pl.when((t >= 6) & (t < 8))
        def _():
            give_results(t - 6)

        for r in range(rounds + 1):

            @pl.when(t == 6 + 2 * r)
            def _():
                if r == 0:
                    give.wait_recv()
                    acc[0] = sgs[c] + sgm[...]
                else:
                    small(r - 1).wait_recv()
                    acc[r] = going[r - 1].astype(F32) + got[r - 1].astype(F32)
                if r < rounds:
                    going[r] = acc[r].astype(BF)
                    small(r).start()

        return carry

    lax.fori_loop(0, 2 * n - 1, ring_step, 0)
    outs[...] = acc[rounds]

    for k in range(2):

        @pl.when(c == k)
        def _():
            for copy in weight_copies(k)[1]:
                copy.wait_send()
            params_copy(k).wait_send()
            for m in range(2):
                for _when, copy in factor_copies(1 - k, m):
                    copy.wait_send()

    give.wait_send()
    for r in range(rounds):
        small(r).wait_send()

    def drain(t, carry):
        for h in range(2):
            for sub in subs:

                def sent():
                    where_live(sub, shard(me - sign(h) * t), lambda: scatter(h, t, sub).wait_send())
                    where_live(sub, home(h, t), lambda: spread(h, t, sub, home(h, t)).wait_send())

                where_active(sub, sent)

        return carry

    lax.fori_loop(0, n - 1, drain, 0)

    def written(j, carry):
        for h in range(2):
            write(h, j, 0).wait()
            write(h, j, 4).wait()

            @pl.when(odd)
            def _():
                where_live(2, j, lambda: write(h, j, 2).wait())

                @pl.when(j < half_shards)
                def _():
                    hand_over(h, j).wait_send()

                @pl.when(j >= half_shards)
                def _():
                    write(h, j, 1).wait()

            @pl.when(jnp.logical_not(odd) & (j < half_shards))
            def _():
                hand_over(h, j).wait_recv()

            @pl.when(helper & (j < LENT))
            def _():
                write(h, j, 3).wait_send()

            @pl.when(lender & (j < LENT))
            def _():
                write(h, j, 3).wait_recv()

        return carry

    lax.fori_loop(0, n, written, 0)

    @pl.when(lender)
    def _():
        for m in range(2):
            for copy in lend(m):
                copy.wait_send()

    @pl.when(s == 3)
    def _():
        for m in range(2):
            share(m).wait_send()

    @pl.when(early)
    def _():
        cot_out.wait_send()
        pltpu.make_async_copy(flat.at[0], ing, es.at[1]).wait()
        remote(flat.at[1], ing, es.at[1], er.at[1], opposite).wait_send()
        remote(flat.at[0], act, es.at[0], er.at[0], opposite).wait_recv()

    @pl.when(jnp.logical_not(early))
    def _():
        img_out.wait_send()
        for m in range(2):
            for copy in g_hop(m):
                copy.wait_send()
        remote(flat.at[0], act, es.at[0], er.at[0], opposite).wait_send()
        pltpu.make_async_copy(flat.at[1], act, es.at[0]).wait()
        remote(flat.at[1], ing, es.at[1], er.at[1], opposite).wait_recv()


def relay(wrows, wcols, img, cot, kern, bias, gain, move, first, second):
    shape = jax.ShapeDtypeStruct
    vmem = pl.BlockSpec(memory_space=pltpu.VMEM)
    anywhere = pl.BlockSpec(memory_space=pl.ANY)
    dma = pltpu.SemaphoreType.DMA
    image = (ROWS, D)
    slot = img.shape
    rounds = RING.bit_length() - 1
    return pl.pallas_call(
        relay_kernel,
        out_shape=[
            shape(slot, BF),
            shape(slot, BF),
            shape((D, FF), BF),
            shape((FF // 2, D), BF),
            shape((16, D), F32),
        ],
        in_specs=[anywhere] * 10,
        out_specs=[anywhere] * 4 + [vmem],
        scratch_shapes=[
            pltpu.VMEM(kern.shape, BF),
            pltpu.VMEM((3,) + bias.shape, BF),
            pltpu.SMEM(wrows.shape, jnp.int32),
            pltpu.SMEM(wcols.shape, jnp.int32),
            dma((7,)),
            pltpu.VMEM((2, D, FF), BF),
            pltpu.VMEM((FF, D), BF),
            pltpu.VMEM((2, 16, D), F32),
            pltpu.VMEM((2, ROWS, LANE), F32),
            pltpu.VMEM((2,) + slot, BF),
            pltpu.VMEM((2, 2) + image, BF),
            pltpu.VMEM((2,) + image, BF),
            pltpu.VMEM((4,) + image, BF),
            pltpu.VMEM((2, 3) + image, BF),
            pltpu.VMEM((2, 2) + image, BF),
            pltpu.VMEM((2, 2, ROWS, LANE), F32),
            pltpu.VMEM((2, ROWS, 3 * D), F32),
            pltpu.VMEM((2, ROWS, FF), BF),
            pltpu.VMEM((2, 2, ROWS, FF), BF),
            pltpu.VMEM((2, UNITS, PACK * WROWS, LANE), F32),
            pltpu.VMEM((SIDE, GRID + 2, CELL, D), F32),
            pltpu.VMEM(image, F32),
            pltpu.VMEM(image, F32),
            pltpu.VMEM((2, 12, CELL, D), F32),
            pltpu.VMEM((2, 16, D), F32),
            pltpu.VMEM((16, D), F32),
            pltpu.VMEM((2, 2) + image, BF),
            pltpu.VMEM((2, ROWS, FF), BF),
            pltpu.VMEM((2, ROWS, FF), BF),
            pltpu.VMEM((2,) + image, BF),
            pltpu.VMEM((2, RING, COLS + WIDE + REST, COLS), BF),
            pltpu.VMEM((rounds + 1, 16, D), F32),
            pltpu.VMEM((rounds, 16, D), BF),
            pltpu.VMEM((rounds, 16, D), BF),
            dma((14,)),
            dma((14,)),
            dma((14,)),
            dma((2,)),
            dma((2, 2)),
            dma((2, 2)),
            dma((2, 2)),
            dma((2, 2)),
            dma((2, 8)),
            dma((2, 8)),
            dma((2,)),
            dma((2,)),
            dma((2,)),
            dma((2, 2 * RING, 5)),
            dma((2, 2 * RING, 5)),
            dma((2, RING, 5)),
            dma((rounds,)),
            dma((rounds,)),
            dma((4,)),
            dma((4,)),
            dma((2,)),
            dma((2,)),
            dma((2, RING)),
            dma((2, RING)),
            dma((2, RING)),
            dma((2, RING)),
            pltpu.SemaphoreType.REGULAR((2, 5)),
        ],
        name="relay",
        compiler_params=pltpu.CompilerParams(
            collective_id=1, has_side_effects=True, vmem_limit_bytes=63 * 2**20
        ),
    )(wrows, wcols, img, cot, kern, bias, gain, move, first, second)


def finish_kernel(
    out1, out2, act, ing, outs, first, second, acts, ings, kern, bias, gain, move,
    raw1, raw2, full1, full2, acted, graded, wide, small, kernels, rsem, wsem,
):
    steps = rsem.shape[0] - 3

    loads = [
        pltpu.make_async_copy(act, acted, rsem.at[steps]),
        pltpu.make_async_copy(ing, graded, rsem.at[steps + 1]),
        pltpu.make_async_copy(outs, small, rsem.at[steps + 2]),
    ]
    for copy in loads:
        copy.start()
    reads, writes = [], []
    for i in range(steps):
        pair = ((out1, raw1, full1, first), (out2, raw2, full2, second))[i % 2]
        src, raw, full, dst = pair
        half = steps // 2
        rows = pl.ds(i // 2 * (src.shape[0] // half), src.shape[0] // half)
        reads.append((pltpu.make_async_copy(src.at[rows, :], raw.at[rows, :], rsem.at[i]), raw, full, rows))
        writes.append(pltpu.make_async_copy(full.at[rows, :], dst.at[rows, :], wsem.at[i]))
    for copy, *_ in reads:
        copy.start()
    for (copy, raw, full, rows), back in zip(reads, writes):
        copy.wait()
        full[rows, :] = raw[rows, :].astype(F32)
        back.start()
    for copy in loads:
        copy.wait()
    for k in range(9):
        kernels[k] = small[k : k + 1, :]
    for r in range(GRID):
        line = graded[r].astype(F32)
        for k in range(GRID):
            wide[r, k] = line[k : k + 1, :]
    last = [
        pltpu.make_async_copy(acted, acts, wsem.at[steps]),
        pltpu.make_async_copy(wide, ings, wsem.at[steps + 1]),
        pltpu.make_async_copy(kernels, kern, wsem.at[steps + 2]),
    ]
    for i, dst in enumerate((bias, gain, move)):
        last.append(pltpu.make_async_copy(small.at[pl.ds(9 + i, 1), :], dst, wsem.at[steps + 3 + i]))
    for copy in last:
        copy.start()
    for copy in writes + last:
        copy.wait()


def finish(out1, out2, act, ing, outs):
    shape = jax.ShapeDtypeStruct
    slot = act.shape
    anywhere = pl.BlockSpec(memory_space=pl.ANY)
    line = (1, D)
    spread = slot[:2] + line
    steps = 16
    return pl.pallas_call(
        finish_kernel,
        out_shape=[
            shape(out1.shape, F32),
            shape(out2.shape, F32),
            shape(slot, BF),
            shape(spread, F32),
            shape((9,) + line, F32),
            shape(line, F32),
            shape(line, F32),
            shape(line, F32),
        ],
        in_specs=[anywhere] * 5,
        out_specs=[anywhere] * 8,
        scratch_shapes=[
            pltpu.VMEM(out1.shape, out1.dtype),
            pltpu.VMEM(out2.shape, out2.dtype),
            pltpu.VMEM(out1.shape, F32),
            pltpu.VMEM(out2.shape, F32),
            pltpu.VMEM(slot, BF),
            pltpu.VMEM(slot, BF),
            pltpu.VMEM(spread, F32),
            pltpu.VMEM(outs.shape, F32),
            pltpu.VMEM((9,) + line, F32),
            pltpu.SemaphoreType.DMA((steps + 3,)),
            pltpu.SemaphoreType.DMA((steps + 6,)),
        ],
        name="finish",
        compiler_params=pltpu.CompilerParams(vmem_limit_bytes=60 * 2**20),
    )(out1, out2, act, ing, outs)


def per_device(
    images, cotangent, window_rows, window_cols, pos_kernel, pos_bias, norm_gain, norm_shift, first_weight, second_weight
):
    act, ing, out1, out2, outs = relay(
        window_rows, window_cols, images[0], cotangent[0], pos_kernel[0], pos_bias, norm_gain, norm_shift,
        first_weight[0], second_weight,
    )
    if lax.axis_size("dp") > RING:
        out1, out2, outs = lax.psum((out1.astype(F32) / RING, out2.astype(F32) / RING, outs / RING), "dp")
    out1, out2, act, ing, kern, bias, gain, move = finish(out1, out2, act, ing, outs)
    return (
        act[None],
        ing.transpose(2, 0, 1, 3),
        out1[None],
        out2,
        kern.transpose(1, 0, 2),
        bias,
        gain,
        move,
    )


def solution(mesh):
    in_specs = (
        P(("dp", "section"), None, None, None),
        P(("dp", "section"), None, None, None),
        P("dp"),
        P("dp"),
        P("section", None, None),
        P("section", None),
        P("section", None),
        P("section", None),
        P("section", None, None),
        P("section", None),
    )
    out_specs = (
        P(("dp", "section"), None, None, None),
        P(("dp", "section"), None, None, None),
        P("section", None, None),
        P("section", None),
        P("section", None, None),
        P("section", None),
        P("section", None),
        P("section", None),
    )
    return jax.shard_map(per_device, mesh=mesh, in_specs=in_specs, out_specs=out_specs, check_vma=False)
```

```python
from functools import partial

import jax
import jax.numpy as jnp
from jax import lax
from jax.experimental import pallas as pl
from jax.experimental.pallas import tpu as pltpu
from jax.sharding import PartitionSpec as P

D = 768
FF = 3072
HEADS = 24
HEAD = 32
WIN = 7
SIDE = 2
GRID = SIDE * WIN
CELL = 8
WROWS = WIN * CELL
HALF = GRID * CELL
ROWS = SIDE * HALF
GROUP = 256
PACK = GROUP // HEAD
NGROUP = D // GROUP
UNITS = NGROUP * SIDE * SIDE
LANE = 128
FTILE = 512
EPS = 1e-05
SCALE = HEAD ** (-0.5)
BF = jnp.bfloat16
F32 = jnp.float32
MESH = pl.DeviceIdType.MESH


def dot(a, b, ca=1, cb=0):
    return lax.dot_general(a, b, (((ca,), (cb,)), ((), ())), preferred_element_type=F32)


def lanes(index, width=LANE):
    return pl.ds(pl.multiple_of(index * width, width), width)


def halves(value):
    return value.reshape(SIDE, GRID, CELL, value.shape[-1])


def shifts(left, right):
    column = lax.broadcasted_iota(jnp.int32, left.shape, 1)
    before0 = pltpu.roll(left, 1, 1)
    after0 = jnp.where(column == WIN - 1, pltpu.roll(right, CELL - 2, 1), pltpu.roll(left, CELL - 1, 1))
    before1 = jnp.where(column == 0, pltpu.roll(left, 2, 1), pltpu.roll(right, 1, 1))
    after1 = pltpu.roll(right, CELL - 1, 1)
    return ((before0, left, after0), (before1, right, after1))


def gelu_parts(h):
    expo = jnp.exp(h * h * -0.5)
    t = 1.0 / (1.0 + (0.3275911 * 0.7071067811865476) * jnp.abs(h))
    poly = t * (0.127414796 + t * (-0.142248368 + t * (0.7107068705 + t * (-0.7265760135 + t * 0.5307027145))))
    tail = poly * expo
    phi = jnp.where(h >= 0, 1.0 - tail, tail)
    return h * phi, phi + h * expo * 0.3989422804014327


def front_forward(sec, m, ubuf, msk, pr, U, C, zz, xh, rs):
    zero = jnp.zeros((ROWS, LANE), F32)

    def conv(i, total):
        ls = lanes(i)
        u = ubuf[sec, m, :, ls].astype(F32)
        masked = halves(u * msk[m])
        U[0, 1 : GRID + 1, :, ls] = masked[0]
        U[1, 1 : GRID + 1, :, ls] = masked[1]
        moved = shifts(U[0, :, :, ls], U[1, :, :, ls])
        taps = pr[sec, :, ls]
        uh = halves(u)
        sums = []
        for wc in range(SIDE):
            acc = uh[wc] + taps[9:10, :][None]
            for a in range(3):
                for b in range(3):
                    acc = acc + moved[wc][b][a : a + GRID] * taps[3 * a + b : 3 * a + b + 1, :][None]
            acc = acc.reshape(HALF, LANE)
            C[pl.ds(wc * HALF, HALF), ls] = acc
            sums.append(acc)
        return total + jnp.concatenate(sums, axis=0)

    mean = jnp.sum(lax.fori_loop(0, D // LANE, conv, zero, unroll=True), axis=-1, keepdims=True) * (1.0 / D)

    def spread(i, total):
        centred = C[:, lanes(i)] - mean
        return total + centred * centred

    var = jnp.sum(lax.fori_loop(0, D // LANE, spread, zero, unroll=True), axis=-1, keepdims=True) * (1.0 / D)
    rstd = lax.rsqrt(var + EPS)
    rs[sec, m] = jnp.broadcast_to(rstd, (ROWS, LANE))

    def norm(i, carry):
        ls = lanes(i)
        xhat = (C[:, ls] - mean) * rstd
        xh[sec, m, :, ls] = xhat.astype(BF)
        zz[m, 2 * sec, :, ls] = (xhat * pr[sec, 10:11, ls] + pr[sec, 11:12, ls]).astype(BF)
        return carry

    lax.fori_loop(0, D // LANE, norm, 0, unroll=True)


def fold(value):
    return jnp.sum(value.reshape(ROWS // CELL, CELL, LANE), axis=0)


def front_backward(sec, m, msk, pr, U, T, gfull, xh, rs, sgp, out, sent):
    zero = jnp.zeros((ROWS, LANE), F32)

    def sums(i, carry):
        s1, s2 = carry
        ls = lanes(i)
        dz = T[:, ls]
        xhat = xh[sec, m, :, ls].astype(F32)
        both = xhat * dz
        sgp[sec, 10, :, ls] += fold(both)
        sgp[sec, 11, :, ls] += fold(dz)
        gain = pr[sec, 10:11, ls]
        return s1 + dz * gain, s2 + both * gain

    s1, s2 = lax.fori_loop(0, D // LANE, sums, (zero, zero), unroll=True)
    m1 = jnp.sum(s1, axis=-1, keepdims=True) * (1.0 / D)
    m2 = jnp.sum(s2, axis=-1, keepdims=True) * (1.0 / D)

    def back(i, carry):
        ls = lanes(i)
        xhat = xh[sec, m, :, ls].astype(F32)
        inner = T[:, ls] * pr[sec, 10:11, ls] - m1 - xhat * m2
        gc = gfull(i)[...].astype(F32) + rs[sec, m] * inner
        xh[sec, m, :, ls] = gc.astype(BF)
        gh = halves(gc)
        U[0, 1 : GRID + 1, :, ls] = gh[0]
        U[1, 1 : GRID + 1, :, ls] = gh[1]
        moved = shifts(U[0, :, :, ls], U[1, :, :, ls])
        taps = pr[sec, :, ls]
        mask = halves(msk[m])
        du = []
        for wc in range(SIDE):
            acc = jnp.zeros((GRID, CELL, LANE), F32)
            for a in range(3):
                for b in range(3):
                    tap = 3 * a + b
                    acc = acc + moved[wc][2 - b][2 - a : 2 - a + GRID] * taps[tap : tap + 1, :][None]
            du.append((gh[wc] + mask[wc] * acc).reshape(HALF, LANE))
        out(i)[...] = jnp.concatenate(du, axis=0).astype(BF)
        return carry

    lax.fori_loop(0, D // LANE // 2, back, 0, unroll=True)
    sent(0)
    lax.fori_loop(D // LANE // 2, D // LANE, back, 0, unroll=True)
    sent(1)


def front_sums(sec, m, ubuf, msk, U, xh, sgp):
    def part(i, carry):
        ls = lanes(i)
        gc = xh[sec, m, :, ls].astype(F32)
        sgp[sec, 9, :, ls] += fold(gc)
        gh = halves(gc)
        U[0, 1 : GRID + 1, :, ls] = gh[0]
        U[1, 1 : GRID + 1, :, ls] = gh[1]
        moved = shifts(U[0, :, :, ls], U[1, :, :, ls])
        um = halves(ubuf[sec, m, :, ls].astype(F32) * msk[m])
        for a in range(3):
            for b in range(3):
                kg = jnp.zeros((CELL, LANE), F32)
                for wc in range(SIDE):
                    kg = kg + jnp.sum(moved[wc][2 - b][2 - a : 2 - a + GRID] * um[wc], axis=0)
                sgp[sec, 3 * a + b, :, ls] += kg
        return carry

    lax.fori_loop(0, D // LANE, part, 0)


def spread_heads(value, head_of_lane):
    parts = [jnp.where(head_of_lane == h, value, 0.0) for h in range(PACK)]
    return jnp.concatenate(parts, axis=0).astype(BF)


def gather_heads(value, rows, head_of_lane):
    out = jnp.zeros((rows, GROUP), F32)
    for h in range(PACK):
        out = jnp.where(head_of_lane == h, value[h * rows : (h + 1) * rows], out)
    return out


def unit_slices(unit):
    pair, group = unit // NGROUP, lax.rem(unit, NGROUP)
    rows = [pl.ds(pl.multiple_of((2 * pair + w) * WROWS, 8), WROWS) for w in range(2)]
    cols = [pl.ds(pl.multiple_of(part * D + group * GROUP, LANE), GROUP) for part in range(3)]
    return rows, cols


def window_parts(m, i, qkv):
    rows, cols = unit_slices(i)
    head_of_lane = lax.broadcasted_iota(jnp.int32, (WROWS, GROUP), 1) // HEAD
    q = [qkv[m, r, cols[0]].astype(BF) for r in rows]
    kd = [spread_heads(qkv[m, r, cols[1]], head_of_lane) for r in rows]
    vd = [spread_heads(qkv[m, r, cols[2]], head_of_lane) for r in rows]
    return rows, cols, head_of_lane, q, kd, vd


def window_forward(m, qkv, pw, T, group):
    def unit(i):
        rows, cols, head_of_lane, q, kd, vd = window_parts(m, i, qkv)
        s = [(dot(b, a, 1, 1) * SCALE).reshape(PACK, WROWS, WROWS) for a, b in zip(q, kd)]
        key = lax.broadcasted_iota(jnp.int32, s[0].shape, 1)
        real = lax.rem(key, CELL) < WIN
        s = [jnp.where(real, x, -1e30) for x in s]
        p = [jnp.exp(x - jnp.max(x, axis=1, keepdims=True)) for x in s]
        p = [x * (1.0 / jnp.sum(x, axis=1, keepdims=True)) for x in p]
        p = [x.reshape(PACK * WROWS, WROWS) for x in p]
        for w in range(2):
            pw[m, 2 * i + w, :, 0:WROWS] = p[w]
        out = [dot(x.astype(BF), v, 0, 0) for x, v in zip(p, vd)]
        for w in range(2):
            T[rows[w], cols[0]] = out[w]

    for pair in range(UNITS // 2 // NGROUP):
        unit(pair * NGROUP + group)


def window_backward(m, qkv, pw, T):
    def unit(i, carry):
        rows, cols, head_of_lane, q, kd, vd = window_parts(m, i, qkv)
        g = [T[r, cols[0]].astype(BF) for r in rows]
        p = [pw[m, 2 * i + w, :, 0:WROWS].reshape(PACK, WROWS, WROWS) for w in range(2)]
        dp = [dot(v, x, 1, 1).reshape(PACK, WROWS, WROWS) for v, x in zip(vd, g)]
        ds = [x * (y - jnp.sum(x * y, axis=1, keepdims=True)) for x, y in zip(p, dp)]
        ds = [x.reshape(PACK * WROWS, WROWS).astype(BF) for x in ds]
        pb = [x.reshape(PACK * WROWS, WROWS).astype(BF) for x in p]
        dv = [gather_heads(dot(x, y), WROWS, head_of_lane) for x, y in zip(pb, g)]
        dk = [gather_heads(dot(x, y), WROWS, head_of_lane) * SCALE for x, y in zip(ds, q)]
        dq = [dot(x, y, 0, 0) * SCALE for x, y in zip(ds, kd)]
        for w in range(2):
            qkv[m, rows[w], cols[0]] = dq[w]
            qkv[m, rows[w], cols[1]] = dk[w]
            qkv[m, rows[w], cols[2]] = dv[w]
        return carry

    lax.fori_loop(0, UNITS // 2, unit, 0)


def group_slices(group):
    return [pl.ds(pl.multiple_of(part * D + group * GROUP, LANE), GROUP) for part in range(3)]


def channel_forward(m, qkv, pw, zz, msk):
    def unit(i, carry):
        cols = group_slices(i)
        mask = msk[m][:, :1]
        q = qkv[m, :, cols[0]].astype(BF)
        k = (qkv[m, :, cols[1]] * mask).astype(BF)
        v = qkv[m, :, cols[2]].astype(BF)
        s = dot(q, k, 0, 0) * SCALE
        same = (lax.broadcasted_iota(jnp.int32, s.shape, 0) // HEAD) == (lax.broadcasted_iota(jnp.int32, s.shape, 1) // HEAD)
        s = jnp.where(same, s, -1e30)
        p = jnp.exp(s - jnp.max(s, axis=1, keepdims=True))
        p = p * (1.0 / jnp.sum(p, axis=1, keepdims=True))
        for k in range(GROUP // LANE):
            pw[m, 2 * i + k, 0:GROUP, :] = p[:, k * LANE : (k + 1) * LANE]
        zz[m, 1, :, cols[0]] = dot(v, p.astype(BF), 1, 1).astype(BF)
        return carry

    lax.fori_loop(0, NGROUP, unit, 0, unroll=True)


def channel_backward(m, qkv, pw, T, rr, msk):
    def unit(i, carry):
        cols = group_slices(i)
        mask = msk[m][:, :1]
        q = qkv[m, :, cols[0]].astype(BF)
        k = (qkv[m, :, cols[1]] * mask).astype(BF)
        v = qkv[m, :, cols[2]].astype(BF)
        g = T[:, cols[0]].astype(BF)
        p = jnp.concatenate([pw[m, 2 * i + k, 0:GROUP, :] for k in range(GROUP // LANE)], axis=1)
        dp = dot(g, v, 0, 0)
        ds = (p * (dp - jnp.sum(p * dp, axis=1, keepdims=True))).astype(BF)
        rr[m, 0, :, cols[0]] = (dot(k, ds, 1, 1) * SCALE).astype(BF)
        rr[m, 0, :, cols[1]] = (dot(q, ds) * (SCALE * mask)).astype(BF)
        rr[m, 0, :, cols[2]] = (dot(g, p.astype(BF))).astype(BF)
        return carry

    lax.fori_loop(0, NGROUP, unit, 0, unroll=True)


RING = 8
COLS = FF // RING
WIDE = FF // 12 * 8 // RING
REST = FF // 3 // RING
THIRD = FF // 3 * 2
LENT = RING * 7 // 8
EARLY = 2


def relay_kernel(
    wrows, wcols, img, cot, kern, bias, gain, move, first, second,
    act, ing, out1, out2, outs,
    kern_in, line_in, rows_in, cols_in, isem, wf, w2, pr, msk, flat, ubuf, gin, gout, zz, xh, rs, qkv, ab, rr, pw, U, C, T, sgp, sgs, sgm,
    rL, rR, rA, rG, buf, acc, going, got,
    wl, ws, wr, pl_, usem, gsem, us, gs, ss, rsem, es, er, sgsem, ssem, rcem, osem, sms, smr, xs, xr, ys, yr, bs, br, hs, hr, free,
):
    n = RING
    s = lax.axis_index("section")
    dp = lax.axis_index("dp")
    stage, c = s // 2, lax.rem(s, 2)
    mate = (dp, stage * 2 + (1 - c))
    opposite = (dp, (1 - stage) * 2 + c)
    diagonal = (dp, 3 - s)
    lender, helper = s == 1, s == 2
    early = stage == 0

    spot = lax.rem(dp, n)
    base = dp - spot
    me = jnp.where(lax.rem(spot, 2) == 0, spot // 2, n - 1 - spot // 2)

    def place(pos):
        pos = lax.rem(pos + 2 * n, n)
        return (base + jnp.where(pos < n // 2, 2 * pos, 2 * (n - 1 - pos) + 1), s)

    nexts = (place(me + 1), place(me - 1))
    rounds = n.bit_length() - 1
    partners = []
    for r in range(rounds):
        bit = 1 << r
        partners.append((jnp.where(lax.rem(spot // bit, 2) == 0, dp + bit, dp - bit), s))

    barrier = pltpu.get_barrier_semaphore()
    peers = [mate, opposite, diagonal, *nexts, *partners]
    for peer in peers:
        pl.semaphore_signal(barrier, inc=1, device_id=peer, device_id_type=MESH)

    def remote(src, dst, send, recv, peer):
        return pltpu.make_async_remote_copy(
            src_ref=src, dst_ref=dst, send_sem=send, recv_sem=recv, device_id=peer, device_id_type=MESH
        )

    half = second.shape[0]

    def group_part(group, part):
        cols = pl.ds(pl.multiple_of(part * D + group * GROUP, LANE), GROUP)
        return first.at[:, cols], wf.at[0, :, cols]

    def wait_group(group):
        for part in range(3):
            src, dst = group_part(group, part)
            i = group * 3 + part

            @pl.when(c == 0)
            def _():
                pltpu.make_async_copy(src, dst, wl.at[i]).wait()

            @pl.when(c == 1)
            def _():
                remote(src, dst, ws.at[i], wr.at[i], mate).wait_recv()

    def weight_parts(k):
        parts = []
        if k == 0:
            for group in range(NGROUP):
                for part in range(3):
                    parts.append(group_part(group, part))
            cols = pl.ds(3 * D, D)
            parts.append((first.at[:, cols], wf.at[k, :, cols]))
        else:
            for i in range(3):
                cols = pl.ds(i * (FF // 3), FF // 3)
                parts.append((first.at[:, cols], wf.at[k, :, cols]))
        third = half // 3
        for i in range(3):
            rows = pl.ds(i * third, third)
            parts.append((second.at[rows, :], w2.at[pl.ds(k * half + i * third, third), :]))
        return parts

    names = (
        [f"qkv{group}" for group in range(NGROUP) for _ in range(3)] + ["out"] + [f"low{i}" for i in range(3)],
        ["in"] * 3 + [f"high{i}" for i in range(3)],
    )

    def weight_copies(k):
        local = [pltpu.make_async_copy(a, b, wl.at[i]) for i, (a, b) in enumerate(weight_parts(k))]
        sent = [remote(a, b, ws.at[i], wr.at[i], mate) for i, (a, b) in enumerate(weight_parts(k))]
        return local, sent

    def params_copy(k):
        return remote(pr.at[k], pr.at[k], ws.at[13], wr.at[13], mate)

    own = flat.at[1]
    small_inputs = [
        pltpu.make_async_copy(a, b, isem.at[i])
        for i, (a, b) in enumerate(
            ((kern, kern_in), (bias, line_in.at[0]), (gain, line_in.at[1]), (move, line_in.at[2]), (wrows, rows_in), (wcols, cols_in))
        )
    ]
    for copy in small_inputs:
        copy.start()
    img_in = pltpu.make_async_copy(img, own, isem.at[6])
    cot_in = pltpu.make_async_copy(cot, own, isem.at[6])

    @pl.when(early)
    def _():
        img_in.start()

    for k in range(2):

        @pl.when(c == k)
        def _():
            for copy in weight_copies(k)[0]:
                copy.start()

    pl.semaphore_wait(barrier, len(peers))
    for k in range(2):

        @pl.when(c == k)
        def _():
            for copy in weight_copies(k)[1]:
                copy.start()

    for copy in small_inputs:
        copy.wait()
    pr[c, 0:9, :] = kern_in[...].astype(F32)
    for i in range(3):
        pr[c, 9 + i : 10 + i, :] = line_in[i].astype(F32)
    params_copy(c).start()

    def wait_weights(*wanted):
        for k in range(2):

            @pl.when(c == k)
            def _():
                for name, copy in zip(names[k], weight_copies(k)[0]):
                    if name in wanted:
                        copy.wait()
                for name, copy in zip(names[1 - k], weight_copies(1 - k)[1]):
                    if name in wanted:
                        copy.wait_recv()

    def wait_params(k):
        @pl.when(c != k)
        def _():
            params_copy(k).wait_recv()

    raw = flat.at[0]
    img_out = remote(img, raw, pl_.at[0], pl_.at[1], opposite)
    cot_out = remote(cot, raw, pl_.at[0], pl_.at[1], opposite)

    def pad(src, dst):
        blank = jnp.zeros((CELL - WIN, D), F32)
        for r in range(GRID):
            line = src[r].astype(F32)
            for wc in range(SIDE):
                cells = jnp.concatenate([line[wc * WIN : (wc + 1) * WIN], blank], axis=0)
                C[pl.ds(wc * HALF + r * CELL, CELL), :] = cells
        dst[...] = C[...].astype(BF)

    def unpad(dst):
        for r in range(GRID):
            sides = [C[pl.ds(wc * HALF + r * CELL, CELL), :][:WIN] for wc in range(SIDE)]
            dst[r] = jnp.concatenate(sides, axis=0).astype(BF)

    @pl.when(early)
    def _():
        cot_out.start()
        img_in.wait()
        pad(own, ubuf.at[0, 0])

    @pl.when(jnp.logical_not(early))
    def _():
        img_out.start()
        cot_in.start()
        cot_in.wait()
        pad(own, gin.at[1])

    index = lax.broadcasted_iota(jnp.int32, (ROWS, LANE), 0)
    cell = lax.rem(index, CELL)
    row = lax.rem(index, HALF) // CELL
    column = (index // HALF) * WIN + cell
    for m in range(2):
        inside = (row < WIN * rows_in[c + 2 * m]) & (column < WIN * cols_in[c + 2 * m]) & (cell < WIN)
        msk[m] = jnp.where(inside, 1.0, 0.0)

    @pl.when(jnp.logical_not(early))
    def _():
        cot_out.wait_recv()
        pad(raw, gin.at[0])
        for m in range(2):
            for l in range(D // LANE):
                cols = pl.ds(l * LANE, LANE)
                gin[m, :, cols] = (gin[m, :, cols].astype(F32) * msk[m]).astype(BF)

    for wc in range(SIDE):
        U[wc, 0] = jnp.zeros((CELL, D), F32)
        U[wc, GRID + 1] = jnp.zeros((CELL, D), F32)
    sgp[...] = jnp.zeros(sgp.shape, F32)

    def hop(m, dst, send, recv):
        sides = [pl.ds(i * D // 2, D // 2) for i in range(2)]
        return [
            remote(gout.at[m, :, cols], dst.at[:, cols], send.at[m, i], recv.at[m, i], opposite)
            for i, cols in enumerate(sides)
        ]

    def u_hop(m):
        return hop(m, ubuf.at[0, m], us, usem)

    def g_hop(m):
        return hop(m, gin.at[m], gs, gsem)

    def factor_copies(k, m):
        if k == 0:
            parts = [
                ("F", zz.at[m, 0], rL.at[m, 0]),
                ("F", zz.at[m, 1], rL.at[m, 1]),
                ("G", rr.at[m, 0, :, pl.ds(3 * D, D)], rR.at[m, :, pl.ds(3 * D, D)]),
                ("A", rr.at[m, 0, :, pl.ds(0, 3 * D)], rR.at[m, :, pl.ds(0, 3 * D)]),
            ]
        else:
            parts = [
                ("X0", zz.at[m, 2], rL.at[m, 0]),
                ("M", gin.at[m], rG.at[m]),
            ]
            for i, cols in enumerate((pl.ds(0, FF // 3 * 2), pl.ds(FF // 3 * 2, FF // 3))):
                parts.append((f"X{i}", ab.at[m, :, cols], rA.at[m, :, cols]))
                parts.append((f"H{i}", rr.at[m, 1, :, cols], rR.at[m, :, cols]))
        return [(w, remote(a, b, ss.at[m, i], rsem.at[m, i], mate)) for i, (w, a, b) in enumerate(parts)]

    def start_factors(m, which):
        for k in range(2):

            @pl.when(c != k)
            def _():
                for when, copy in factor_copies(k, m):
                    if when == which:
                        copy.start()

    def wait_factors(which):
        for k in range(2):

            @pl.when(c == k)
            def _():
                for m in range(2):
                    for when, copy in factor_copies(k, m):
                        if when[0] in which:
                            copy.wait_recv()

    def shard(k):
        return lax.rem(k + 4 * n, n)

    def sign(h):
        return 1 if h == 0 else -1

    def home(h, t):
        return shard(me + sign(h) - sign(h) * t)

    def products(terms):
        total = None
        for a, b in terms:
            part = dot(a[...], b[...], 0, 0)
            total = part if total is None else total + part
        return total

    def tile(sub, h, j):
        side = pl.ds(h * COLS, COLS)
        if sub in (0, 4):
            rows = first_rows(sub, h)
            last = jnp.where(j >= (3 * n) // 4, 1, 0)
            own = jnp.where(c == 1, 2, last)
            other = jnp.where(c == 1, 0, last)
            cols = lanes(j, COLS)
            terms = [(zz.at[m, own, :, rows], rr.at[m, c, :, cols]) for m in range(2)]
            terms += [(rL.at[m, other, :, rows], rR.at[m, :, cols]) for m in range(2)]
        elif sub == 3:
            cols = [pl.ds(pl.multiple_of(i * LENT * REST + j * REST, LANE), REST) for i in range(2)]
            terms = [(rA.at[m, :, cols[0]], rG.at[m, :, side]) for m in range(2)]
            terms += [(rA.at[m, :, cols[1]], gout.at[m, :, side]) for m in range(2)]
        else:
            cols = lanes(j, WIDE) if sub == 1 else pl.ds(pl.multiple_of(THIRD + j * REST, LANE), REST)
            terms = [(ab.at[m, :, cols], gin.at[m, :, side]) for m in range(2)]
            terms += [(rA.at[m, :, cols], rG.at[m, :, side]) for m in range(2)]
        return products(terms)

    sizes = (COLS // 3 * 2, WIDE, REST, REST, COLS // 3)
    starts = (0, COLS, COLS + WIDE, COLS + WIDE, COLS // 3 * 2)
    parts = [pl.ds(start, size) for start, size in zip(starts, sizes)]
    subs = range(len(sizes))
    odd = c == 1
    active = (None, odd, odd, helper, None)

    def where_live(sub, j, run):
        if sub == 2:
            pl.when(jnp.logical_not(lender) | (j >= LENT))(run)
        elif sub == 3:
            pl.when(j < LENT)(run)
        else:
            run()

    def first_rows(sub, h):
        return pl.ds(h * COLS + (0 if sub == 0 else sizes[0]), sizes[sub])

    def where_active(sub, run):
        if active[sub] is None:
            run()
        else:
            pl.when(active[sub])(run)


    def gathered(sub, h, j):
        if sub in (0, 4):
            return wf.at[0, first_rows(sub, h), lanes(j, COLS)]
        first_row = 0 if sub == 1 else THIRD
        return w2.at[pl.ds(pl.multiple_of(first_row + j * sizes[sub], 16), sizes[sub]), pl.ds(h * COLS, COLS)]

    def scatter(h, t, sub):
        src, dst = buf.at[h, t, parts[sub], :], buf.at[h, t + 1, parts[sub], :]
        return remote(src, dst, ssem.at[h, t, sub], rcem.at[h, t + 1, sub], nexts[h])

    def spread(h, t, sub, j):
        ref = gathered(sub, h, j)
        return remote(ref, ref, ssem.at[h, n - 1 + t, sub], rcem.at[h, n + t, sub], nexts[h])

    half_shards = n * 3 // 4

    def write(h, j, sub):
        src, side = gathered(sub, h, j), pl.ds(h * COLS, COLS)
        if sub in (0, 4):
            dst = out1.at[first_rows(sub, h), lanes(j, COLS)]
        elif sub == 1:
            dst = out2.at[pl.ds(pl.multiple_of((j - half_shards) * WIDE, 16), WIDE), side]
        else:
            dst = out2.at[pl.ds(pl.multiple_of(THIRD - FF // 2 + j * REST, 16), REST), side]
        if sub == 3:
            return remote(src, dst, bs.at[h, j], br.at[h, j], diagonal)
        return pltpu.make_async_copy(src, dst, osem.at[h, j, sub])

    def hand_over(h, j):
        dst = out2.at[pl.ds(pl.multiple_of(j * WIDE, 16), WIDE), pl.ds(h * COLS, COLS)]
        return remote(gathered(1, h, j), dst, hs.at[h, j], hr.at[h, j], mate)

    def deliver(h, j, sub):
        if sub == 1:

            @pl.when(j < half_shards)
            def _():
                hand_over(h, j).start()

            @pl.when(j >= half_shards)
            def _():
                write(h, j, sub).start()

        else:
            write(h, j, sub).start()

    def lend(m):
        cols, there = pl.ds(THIRD, LENT * REST), [rA.at[m, :, pl.ds(i * LENT * REST, LENT * REST)] for i in range(2)]
        return (
            remote(ab.at[m, :, cols], there[0], xs.at[m], xr.at[m], diagonal),
            remote(rA.at[m, :, cols], there[1], xs.at[2 + m], xr.at[2 + m], diagonal),
        )

    def share(m):
        return remote(gout.at[m], rG.at[m], ys.at[m], yr.at[m], mate)

    def reduce_event(sub, h, e):
        j = shard(me - sign(h) * e)

        @pl.when(e == n - 1)
        def _():
            pl.semaphore_wait(free.at[h, sub], 1)

        def run():
            total = tile(sub, h, j)

            @pl.when(e == 0)
            def _():
                buf[h, 0, parts[sub], :] = total.astype(BF)
                scatter(h, 0, sub).start()

            @pl.when((e > 0) & (e < n - 1))
            def _():
                scatter(h, e - 1, sub).wait_recv()
                buf[h, e, parts[sub], :] = (total + buf[h, e, parts[sub], :].astype(F32)).astype(BF)
                scatter(h, e, sub).start()

            @pl.when(e == n - 1)
            def _():
                scatter(h, n - 2, sub).wait_recv()
                gathered(sub, h, j)[...] = (total + buf[h, n - 1, parts[sub], :].astype(F32)).astype(BF)
                spread(h, 0, sub, j).start()
                deliver(h, j, sub)

        where_live(sub, j, run)

    def event(sub, e):
        for h in range(2):

            @pl.when(e < n)
            def _():
                reduce_event(sub, h, e)

            @pl.when((e >= n) & (e < 2 * n - 1))
            def _():
                t = e - (n - 1)
                j = home(h, t)

                def run():
                    spread(h, t - 1, sub, j).wait_recv()

                    @pl.when(t < n - 1)
                    def _():
                        spread(h, t, sub, j).start()

                    deliver(h, j, sub)

                where_live(sub, j, run)

    def early_event(e, which):
        @pl.when(odd)
        def _():
            for sub in which:
                where_active(sub, lambda: event(sub, e))

    def small(r):
        return remote(going.at[r], got.at[r], sms.at[r], smr.at[r], partners[r])

    def mlp(m, order, wait):
        total, before, last = C[...], None, None
        for t in order:
            cols = pl.ds(t * FTILE, FTILE)
            h = dot(zz[m, 2], wf[1, :, cols])
            if last is not None:
                wait(last)
                total = total + dot(before, w2[pl.ds(last * FTILE, FTILE), :])
            a, d = gelu_parts(h)
            before, last = a.astype(BF), t
            ab[m, :, cols] = before
            rr[m, 1, :, cols] = d.astype(BF)
            if t == FF // FTILE * 2 // 3 - 1 and order == range(FF // FTILE):
                start_factors(m, "X0")
        wait(last)
        for i in range(2):
            cols = pl.ds(i * D // 2, D // 2)
            part = total[:, i * D // 2 : (i + 1) * D // 2]
            gout[jnp.where(early, m, 2 + m), :, cols] = (part + dot(before, w2[pl.ds(last * FTILE, FTILE), cols])).astype(BF)

            @pl.when(early)
            def _():
                u_hop(m)[i].start()

    def give_results(m):
        @pl.when(early)
        def _():
            C[...] = gout[m].astype(F32)

        @pl.when(jnp.logical_not(early))
        def _():
            for l in range(D // LANE):
                cols = pl.ds(l * LANE, LANE)
                C[:, cols] = gout[2 + m, :, cols].astype(F32) * msk[m]

        unpad(flat.at[m])

        @pl.when(early & (m == 0))
        def _():
            pltpu.make_async_copy(flat.at[0], ing, es.at[1]).start()

        @pl.when(early & (m == 1))
        def _():
            remote(flat.at[1], ing, es.at[1], er.at[1], opposite).start()

        @pl.when(jnp.logical_not(early) & (m == 0))
        def _():
            remote(flat.at[0], act, es.at[0], er.at[0], opposite).start()

        @pl.when(jnp.logical_not(early) & (m == 1))
        def _():
            pltpu.make_async_copy(flat.at[1], act, es.at[0]).start()

    def forward(m, p):
        @pl.when(jnp.logical_not(early))
        def _():
            for copy in u_hop(m):
                copy.wait_recv()

        @pl.when(early & (m == 1))
        def _():
            img_out.wait_recv()
            pad(raw, ubuf.at[0, 1])

        once = p == 0
        starting = early & once

        @pl.when(once)
        def _():
            wait_params(0)

        @pl.when(once & jnp.logical_not(early))
        def _():
            wait_params(1)
            wait_weights(*set(names[0] + names[1]))

        front_forward(0, m, ubuf, msk, pr, U, C, zz, xh, rs)

        @pl.when(early)
        def _():
            def head_group(group, carry):
                @pl.when(once)
                def _():
                    wait_group(group)

                for part in range(3):
                    cols = pl.ds(pl.multiple_of(part * D + group * GROUP, LANE), GROUP)
                    qkv[m, :, cols] = dot(zz[m, 0], wf[0, :, cols])
                window_forward(m, qkv, pw, T, group)
                return carry

            lax.fori_loop(0, NGROUP, head_group, 0)
            zz[m, 1] = T[...].astype(BF)

        @pl.when(starting)
        def _():
            wait_weights("out")
            wait_params(1)

        @pl.when(jnp.logical_not(early))
        def _():
            qkv[m] = dot(zz[m, 0], wf[0, :, pl.ds(0, 3 * D)])

        @pl.when(jnp.logical_not(early))
        def _():
            channel_forward(m, qkv, pw, zz, msk)

        ubuf[1, m] = (C[...] + dot(zz[m, 1], wf[0, :, pl.ds(3 * D, D)])).astype(BF)

        front_forward(1, m, ubuf, msk, pr, U, C, zz, xh, rs)

        @pl.when(starting)
        def _():
            wait_weights("in")
            order = [i + 3 * k for i in range(3) for k in range(2)]
            mlp(m, order, lambda t: wait_weights(f"low{t}" if t < 3 else f"high{t - 3}"))
            start_factors(m, "X0")

        @pl.when(jnp.logical_not(starting))
        def _():
            mlp(m, range(FF // FTILE), lambda t: None)

        start_factors(m, "F")
        start_factors(m, "X1")

        @pl.when(early & (m == 1))
        def _():
            wait_factors("FX")

        @pl.when(lender & (m == 1))
        def _():
            for i in range(2):
                for copy in lend(i):
                    copy.start()

    def backward(m):
        @pl.when(early)
        def _():
            for copy in g_hop(m):
                copy.wait_recv()
            start_factors(m, "M")

        for t in range(FF // FTILE):
            cols = pl.ds(t * FTILE, FTILE)
            da = dot(gin[m], w2[cols, :], 1, 1)
            rr[m, 1, :, cols] = (da * rr[m, 1, :, cols].astype(F32)).astype(BF)
            if t == FF // FTILE * 2 // 3 - 1:
                start_factors(m, "H0")

        start_factors(m, "H1")

        @pl.when(m == 1)
        def _():
            @pl.when(jnp.logical_not(early))
            def _():
                wait_factors("FX")

            wait_factors("M")
            early_event(0, (1, 2))

        T[...] = dot(rr[m, 1], wf[1], 1, 1)

        @pl.when(m == 1)
        def _():
            wait_factors("H")
            early_event(0, (0, 4))

        last = pl.ds(3 * D, D)

        @pl.when(early)
        def _():
            for copy in u_hop(m):
                copy.wait_send()

        def tail_lanes(i):
            return rr.at[m, 0, :, pl.ds(pl.multiple_of(3 * D + i * LANE, LANE), LANE)]

        def nothing(half):
            pass

        front_backward(1, m, msk, pr, U, T, lambda i: gin.at[m, :, lanes(i)], xh, rs, sgp, tail_lanes, nothing)

        start_factors(m, "G")
        T[...] = dot(rr[m, 0, :, last], wf[0, :, last], 1, 1)

        @pl.when(early)
        def _():
            window_backward(m, qkv, pw, T)
            for i in range(3):
                cols = pl.ds(i * D, D)
                rr[m, 0, :, cols] = qkv[m, :, cols].astype(BF)

        @pl.when(jnp.logical_not(early))
        def _():
            channel_backward(m, qkv, pw, T, rr, msk)

        start_factors(m, "A")

        @pl.when(m == 1)
        def _():
            early_event(1, (1, 2, 0, 4))

        T[...] = dot(rr[m, 0, :, pl.ds(0, 3 * D)], wf[0, :, pl.ds(0, 3 * D)], 1, 1)
        def send_half(half):
            @pl.when(jnp.logical_not(early))
            def _():
                g_hop(m)[half].start()

        front_backward(
            0, m, msk, pr, U, T, tail_lanes, xh, rs, sgp, lambda i: gout.at[m, :, lanes(i)], send_half
        )

        @pl.when(s == 3)
        def _():
            share(m).start()

    @pl.when(jnp.logical_not(early))
    def _():
        for m in range(2):
            start_factors(m, "M")

    def phase(p, carry):
        m = jnp.where(early, lax.rem(p, 2), p // 2)
        ahead = jnp.where(early, p < 2, lax.rem(p, 2) == 0)

        @pl.when(ahead)
        def _():
            forward(m, p)

        @pl.when(jnp.logical_not(ahead))
        def _():
            backward(m)

        return carry

    lax.fori_loop(0, 4, phase, 0)

    for h in range(2):
        for sub in subs:

            def ready():
                pl.semaphore_signal(free.at[h, sub], inc=1, device_id=nexts[1 - h], device_id_type=MESH)

            where_active(sub, ready)

    give = remote(sgs.at[1 - c], sgm, sgsem.at[0], sgsem.at[1], mate)

    def small_sums():
        for sec in range(2):
            for j in range(12):
                sgs[sec, j : j + 1, :] = jnp.sum(sgp[sec, j], axis=0, keepdims=True)
            sgs[sec, 12:16, :] = jnp.zeros((4, D), F32)
        give.start()

    wait_factors("GA")

    @pl.when(helper)
    def _():
        for m in range(2):
            for copy in lend(m):
                copy.wait_recv()
            share(m).wait_recv()

    def ring_step(t, carry):
        for sub in (0, 4):
            event(sub, t + jnp.where(odd, EARLY, 0))
        where_active(1, lambda: event(1, t + EARLY))
        where_active(2, lambda: event(2, t + EARLY))
        where_active(3, lambda: event(3, t))
        @pl.when((t >= 1) & (t < 5))
        def _():
            front_sums((t - 1) // 2, lax.rem(t - 1, 2), ubuf, msk, U, xh, sgp)

        pl.when(t == 5)(small_sums)

        @pl.when((t >= 6) & (t < 8))
        def _():
            give_results(t - 6)

        for r in range(rounds + 1):

            @pl.when(t == 6 + 2 * r)
            def _():
                if r == 0:
                    give.wait_recv()
                    acc[0] = sgs[c] + sgm[...]
                else:
                    small(r - 1).wait_recv()
                    acc[r] = going[r - 1].astype(F32) + got[r - 1].astype(F32)
                if r < rounds:
                    going[r] = acc[r].astype(BF)
                    small(r).start()

        return carry

    lax.fori_loop(0, 2 * n - 1, ring_step, 0)
    outs[...] = acc[rounds]

    for k in range(2):

        @pl.when(c == k)
        def _():
            for copy in weight_copies(k)[1]:
                copy.wait_send()
            params_copy(k).wait_send()
            for m in range(2):
                for _when, copy in factor_copies(1 - k, m):
                    copy.wait_send()

    give.wait_send()
    for r in range(rounds):
        small(r).wait_send()

    def drain(t, carry):
        for h in range(2):
            for sub in subs:

                def sent():
                    where_live(sub, shard(me - sign(h) * t), lambda: scatter(h, t, sub).wait_send())
                    where_live(sub, home(h, t), lambda: spread(h, t, sub, home(h, t)).wait_send())

                where_active(sub, sent)

        return carry

    lax.fori_loop(0, n - 1, drain, 0)

    def written(j, carry):
        for h in range(2):
            write(h, j, 0).wait()
            write(h, j, 4).wait()

            @pl.when(odd)
            def _():
                where_live(2, j, lambda: write(h, j, 2).wait())

                @pl.when(j < half_shards)
                def _():
                    hand_over(h, j).wait_send()

                @pl.when(j >= half_shards)
                def _():
                    write(h, j, 1).wait()

            @pl.when(jnp.logical_not(odd) & (j < half_shards))
            def _():
                hand_over(h, j).wait_recv()

            @pl.when(helper & (j < LENT))
            def _():
                write(h, j, 3).wait_send()

            @pl.when(lender & (j < LENT))
            def _():
                write(h, j, 3).wait_recv()

        return carry

    lax.fori_loop(0, n, written, 0)

    @pl.when(lender)
    def _():
        for m in range(2):
            for copy in lend(m):
                copy.wait_send()

    @pl.when(s == 3)
    def _():
        for m in range(2):
            share(m).wait_send()

    @pl.when(early)
    def _():
        cot_out.wait_send()
        pltpu.make_async_copy(flat.at[0], ing, es.at[1]).wait()
        remote(flat.at[1], ing, es.at[1], er.at[1], opposite).wait_send()
        remote(flat.at[0], act, es.at[0], er.at[0], opposite).wait_recv()

    @pl.when(jnp.logical_not(early))
    def _():
        img_out.wait_send()
        for m in range(2):
            for copy in g_hop(m):
                copy.wait_send()
        remote(flat.at[0], act, es.at[0], er.at[0], opposite).wait_send()
        pltpu.make_async_copy(flat.at[1], act, es.at[0]).wait()
        remote(flat.at[1], ing, es.at[1], er.at[1], opposite).wait_recv()


def relay(wrows, wcols, img, cot, kern, bias, gain, move, first, second):
    shape = jax.ShapeDtypeStruct
    vmem = pl.BlockSpec(memory_space=pltpu.VMEM)
    anywhere = pl.BlockSpec(memory_space=pl.ANY)
    dma = pltpu.SemaphoreType.DMA
    image = (ROWS, D)
    slot = img.shape
    rounds = RING.bit_length() - 1
    return pl.pallas_call(
        relay_kernel,
        out_shape=[
            shape(slot, BF),
            shape(slot, BF),
            shape((D, FF), BF),
            shape((FF // 2, D), BF),
            shape((16, D), F32),
        ],
        in_specs=[anywhere] * 10,
        out_specs=[anywhere] * 4 + [vmem],
        scratch_shapes=[
            pltpu.VMEM(kern.shape, BF),
            pltpu.VMEM((3,) + bias.shape, BF),
            pltpu.SMEM(wrows.shape, jnp.int32),
            pltpu.SMEM(wcols.shape, jnp.int32),
            dma((7,)),
            pltpu.VMEM((2, D, FF), BF),
            pltpu.VMEM((FF, D), BF),
            pltpu.VMEM((2, 16, D), F32),
            pltpu.VMEM((2, ROWS, LANE), F32),
            pltpu.VMEM((2,) + slot, BF),
            pltpu.VMEM((2, 2) + image, BF),
            pltpu.VMEM((2,) + image, BF),
            pltpu.VMEM((4,) + image, BF),
            pltpu.VMEM((2, 3) + image, BF),
            pltpu.VMEM((2, 2) + image, BF),
            pltpu.VMEM((2, 2, ROWS, LANE), F32),
            pltpu.VMEM((2, ROWS, 3 * D), F32),
            pltpu.VMEM((2, ROWS, FF), BF),
            pltpu.VMEM((2, 2, ROWS, FF), BF),
            pltpu.VMEM((2, UNITS, PACK * WROWS, LANE), F32),
            pltpu.VMEM((SIDE, GRID + 2, CELL, D), F32),
            pltpu.VMEM(image, F32),
            pltpu.VMEM(image, F32),
            pltpu.VMEM((2, 12, CELL, D), F32),
            pltpu.VMEM((2, 16, D), F32),
            pltpu.VMEM((16, D), F32),
            pltpu.VMEM((2, 2) + image, BF),
            pltpu.VMEM((2, ROWS, FF), BF),
            pltpu.VMEM((2, ROWS, FF), BF),
            pltpu.VMEM((2,) + image, BF),
            pltpu.VMEM((2, RING, COLS + WIDE + REST, COLS), BF),
            pltpu.VMEM((rounds + 1, 16, D), F32),
            pltpu.VMEM((rounds, 16, D), BF),
            pltpu.VMEM((rounds, 16, D), BF),
            dma((14,)),
            dma((14,)),
            dma((14,)),
            dma((2,)),
            dma((2, 2)),
            dma((2, 2)),
            dma((2, 2)),
            dma((2, 2)),
            dma((2, 8)),
            dma((2, 8)),
            dma((2,)),
            dma((2,)),
            dma((2,)),
            dma((2, 2 * RING, 5)),
            dma((2, 2 * RING, 5)),
            dma((2, RING, 5)),
            dma((rounds,)),
            dma((rounds,)),
            dma((4,)),
            dma((4,)),
            dma((2,)),
            dma((2,)),
            dma((2, RING)),
            dma((2, RING)),
            dma((2, RING)),
            dma((2, RING)),
            pltpu.SemaphoreType.REGULAR((2, 5)),
        ],
        name="relay",
        compiler_params=pltpu.CompilerParams(
            collective_id=1, has_side_effects=True, vmem_limit_bytes=63 * 2**20
        ),
    )(wrows, wcols, img, cot, kern, bias, gain, move, first, second)


def finish_kernel(
    out1, out2, act, ing, outs, first, second, acts, ings, kern, bias, gain, move,
    raw1, raw2, full1, full2, acted, graded, wide, small, kernels, rsem, wsem,
):
    steps = rsem.shape[0] - 3

    loads = [
        pltpu.make_async_copy(act, acted, rsem.at[steps]),
        pltpu.make_async_copy(ing, graded, rsem.at[steps + 1]),
        pltpu.make_async_copy(outs, small, rsem.at[steps + 2]),
    ]
    for copy in loads:
        copy.start()
    reads, writes = [], []
    for i in range(steps):
        pair = ((out1, raw1, full1, first), (out2, raw2, full2, second))[i % 2]
        src, raw, full, dst = pair
        half = steps // 2
        rows = pl.ds(i // 2 * (src.shape[0] // half), src.shape[0] // half)
        reads.append((pltpu.make_async_copy(src.at[rows, :], raw.at[rows, :], rsem.at[i]), raw, full, rows))
        writes.append(pltpu.make_async_copy(full.at[rows, :], dst.at[rows, :], wsem.at[i]))
    for copy, *_ in reads:
        copy.start()
    for (copy, raw, full, rows), back in zip(reads, writes):
        copy.wait()
        full[rows, :] = raw[rows, :].astype(F32)
        back.start()
    for copy in loads:
        copy.wait()
    for k in range(9):
        kernels[k] = small[k : k + 1, :]
    for r in range(GRID):
        line = graded[r].astype(F32)
        for k in range(GRID):
            wide[r, k] = line[k : k + 1, :]
    last = [
        pltpu.make_async_copy(acted, acts, wsem.at[steps]),
        pltpu.make_async_copy(wide, ings, wsem.at[steps + 1]),
        pltpu.make_async_copy(kernels, kern, wsem.at[steps + 2]),
    ]
    for i, dst in enumerate((bias, gain, move)):
        last.append(pltpu.make_async_copy(small.at[pl.ds(9 + i, 1), :], dst, wsem.at[steps + 3 + i]))
    for copy in last:
        copy.start()
    for copy in writes + last:
        copy.wait()


def finish(out1, out2, act, ing, outs):
    shape = jax.ShapeDtypeStruct
    slot = act.shape
    anywhere = pl.BlockSpec(memory_space=pl.ANY)
    line = (1, D)
    spread = slot[:2] + line
    steps = 16
    return pl.pallas_call(
        finish_kernel,
        out_shape=[
            shape(out1.shape, F32),
            shape(out2.shape, F32),
            shape(slot, BF),
            shape(spread, F32),
            shape((9,) + line, F32),
            shape(line, F32),
            shape(line, F32),
            shape(line, F32),
        ],
        in_specs=[anywhere] * 5,
        out_specs=[anywhere] * 8,
        scratch_shapes=[
            pltpu.VMEM(out1.shape, out1.dtype),
            pltpu.VMEM(out2.shape, out2.dtype),
            pltpu.VMEM(out1.shape, F32),
            pltpu.VMEM(out2.shape, F32),
            pltpu.VMEM(slot, BF),
            pltpu.VMEM(slot, BF),
            pltpu.VMEM(spread, F32),
            pltpu.VMEM(outs.shape, F32),
            pltpu.VMEM((9,) + line, F32),
            pltpu.SemaphoreType.DMA((steps + 3,)),
            pltpu.SemaphoreType.DMA((steps + 6,)),
        ],
        name="finish",
        compiler_params=pltpu.CompilerParams(vmem_limit_bytes=60 * 2**20),
    )(out1, out2, act, ing, outs)


def per_device(
    images, cotangent, window_rows, window_cols, pos_kernel, pos_bias, norm_gain, norm_shift, first_weight, second_weight
):
    act, ing, out1, out2, outs = relay(
        window_rows, window_cols, images[0], cotangent[0], pos_kernel[0], pos_bias, norm_gain, norm_shift,
        first_weight[0], second_weight,
    )
    if lax.axis_size("dp") > RING:
        out1, out2, outs = lax.psum((out1.astype(F32) / RING, out2.astype(F32) / RING, outs / RING), "dp")
    out1, out2, act, ing, kern, bias, gain, move = finish(out1, out2, act, ing, outs)
    return (
        act[None],
        ing.transpose(2, 0, 1, 3),
        out1[None],
        out2,
        kern.transpose(1, 0, 2),
        bias,
        gain,
        move,
    )


def solution(mesh):
    in_specs = (
        P(("dp", "section"), None, None, None),
        P(("dp", "section"), None, None, None),
        P("dp"),
        P("dp"),
        P("section", None, None),
        P("section", None),
        P("section", None),
        P("section", None),
        P("section", None, None),
        P("section", None),
    )
    out_specs = (
        P(("dp", "section"), None, None, None),
        P(("dp", "section"), None, None, None),
        P("section", None, None),
        P("section", None),
        P("section", None, None),
        P("section", None),
        P("section", None),
        P("section", None),
    )
    return jax.shard_map(per_device, mesh=mesh, in_specs=in_specs, out_specs=out_specs, check_vma=False)
```

```python
from functools import partial

import jax
import jax.numpy as jnp
from jax import lax
from jax.experimental import pallas as pl
from jax.experimental.pallas import tpu as pltpu
from jax.sharding import PartitionSpec as P

D = 768
FF = 3072
HEADS = 24
HEAD = 32
WIN = 7
SIDE = 2
GRID = SIDE * WIN
CELL = 8
WROWS = WIN * CELL
HALF = GRID * CELL
ROWS = SIDE * HALF
GROUP = 256
PACK = GROUP // HEAD
NGROUP = D // GROUP
UNITS = NGROUP * SIDE * SIDE
LANE = 128
FTILE = 512
EPS = 1e-05
SCALE = HEAD ** (-0.5)
BF = jnp.bfloat16
F32 = jnp.float32
MESH = pl.DeviceIdType.MESH


def dot(a, b, ca=1, cb=0):
    return lax.dot_general(a, b, (((ca,), (cb,)), ((), ())), preferred_element_type=F32)


def lanes(index, width=LANE):
    return pl.ds(pl.multiple_of(index * width, width), width)


def halves(value):
    return value.reshape(SIDE, GRID, CELL, value.shape[-1])


def shifts(left, right):
    column = lax.broadcasted_iota(jnp.int32, left.shape, 1)
    before0 = pltpu.roll(left, 1, 1)
    after0 = jnp.where(column == WIN - 1, pltpu.roll(right, CELL - 2, 1), pltpu.roll(left, CELL - 1, 1))
    before1 = jnp.where(column == 0, pltpu.roll(left, 2, 1), pltpu.roll(right, 1, 1))
    after1 = pltpu.roll(right, CELL - 1, 1)
    return ((before0, left, after0), (before1, right, after1))


def gelu_parts(h):
    expo = jnp.exp(h * h * -0.5)
    t = 1.0 / (1.0 + (0.3275911 * 0.7071067811865476) * jnp.abs(h))
    poly = t * (0.127414796 + t * (-0.142248368 + t * (0.7107068705 + t * (-0.7265760135 + t * 0.5307027145))))
    tail = poly * expo
    phi = jnp.where(h >= 0, 1.0 - tail, tail)
    return h * phi, phi + h * expo * 0.3989422804014327


def front_forward(sec, m, ubuf, msk, pr, U, C, zz, xh, rs):
    zero = jnp.zeros((ROWS, LANE), F32)

    def conv(i, total):
        ls = lanes(i)
        u = ubuf[sec, m, :, ls].astype(F32)
        masked = halves(u * msk[m])
        U[0, 1 : GRID + 1, :, ls] = masked[0]
        U[1, 1 : GRID + 1, :, ls] = masked[1]
        moved = shifts(U[0, :, :, ls], U[1, :, :, ls])
        taps = pr[sec, :, ls]
        uh = halves(u)
        sums = []
        for wc in range(SIDE):
            acc = uh[wc] + taps[9:10, :][None]
            for a in range(3):
                for b in range(3):
                    acc = acc + moved[wc][b][a : a + GRID] * taps[3 * a + b : 3 * a + b + 1, :][None]
            acc = acc.reshape(HALF, LANE)
            C[pl.ds(wc * HALF, HALF), ls] = acc
            sums.append(acc)
        return total + jnp.concatenate(sums, axis=0)

    mean = jnp.sum(lax.fori_loop(0, D // LANE, conv, zero, unroll=True), axis=-1, keepdims=True) * (1.0 / D)

    def spread(i, total):
        centred = C[:, lanes(i)] - mean
        return total + centred * centred

    var = jnp.sum(lax.fori_loop(0, D // LANE, spread, zero, unroll=True), axis=-1, keepdims=True) * (1.0 / D)
    rstd = lax.rsqrt(var + EPS)
    rs[sec, m] = jnp.broadcast_to(rstd, (ROWS, LANE))

    def norm(i, carry):
        ls = lanes(i)
        xhat = (C[:, ls] - mean) * rstd
        xh[sec, m, :, ls] = xhat.astype(BF)
        zz[m, 2 * sec, :, ls] = (xhat * pr[sec, 10:11, ls] + pr[sec, 11:12, ls]).astype(BF)
        return carry

    lax.fori_loop(0, D // LANE, norm, 0, unroll=True)


def fold(value):
    return jnp.sum(value.reshape(ROWS // CELL, CELL, LANE), axis=0)


def front_backward(sec, m, msk, pr, U, T, gfull, xh, rs, sgp, out, sent):
    zero = jnp.zeros((ROWS, LANE), F32)

    def sums(i, carry):
        s1, s2 = carry
        ls = lanes(i)
        dz = T[:, ls]
        xhat = xh[sec, m, :, ls].astype(F32)
        both = xhat * dz
        sgp[sec, 10, :, ls] += fold(both)
        sgp[sec, 11, :, ls] += fold(dz)
        gain = pr[sec, 10:11, ls]
        return s1 + dz * gain, s2 + both * gain

    s1, s2 = lax.fori_loop(0, D // LANE, sums, (zero, zero), unroll=True)
    m1 = jnp.sum(s1, axis=-1, keepdims=True) * (1.0 / D)
    m2 = jnp.sum(s2, axis=-1, keepdims=True) * (1.0 / D)

    def back(i, carry):
        ls = lanes(i)
        xhat = xh[sec, m, :, ls].astype(F32)
        inner = T[:, ls] * pr[sec, 10:11, ls] - m1 - xhat * m2
        gc = gfull(i)[...].astype(F32) + rs[sec, m] * inner
        xh[sec, m, :, ls] = gc.astype(BF)
        gh = halves(gc)
        U[0, 1 : GRID + 1, :, ls] = gh[0]
        U[1, 1 : GRID + 1, :, ls] = gh[1]
        moved = shifts(U[0, :, :, ls], U[1, :, :, ls])
        taps = pr[sec, :, ls]
        mask = halves(msk[m])
        du = []
        for wc in range(SIDE):
            acc = jnp.zeros((GRID, CELL, LANE), F32)
            for a in range(3):
                for b in range(3):
                    tap = 3 * a + b
                    acc = acc + moved[wc][2 - b][2 - a : 2 - a + GRID] * taps[tap : tap + 1, :][None]
            du.append((gh[wc] + mask[wc] * acc).reshape(HALF, LANE))
        out(i)[...] = jnp.concatenate(du, axis=0).astype(BF)
        return carry

    lax.fori_loop(0, D // LANE // 2, back, 0, unroll=True)
    sent(0)
    lax.fori_loop(D // LANE // 2, D // LANE, back, 0, unroll=True)
    sent(1)


def front_sums(sec, m, ubuf, msk, U, xh, sgp):
    def part(i, carry):
        ls = lanes(i)
        gc = xh[sec, m, :, ls].astype(F32)
        sgp[sec, 9, :, ls] += fold(gc)
        gh = halves(gc)
        U[0, 1 : GRID + 1, :, ls] = gh[0]
        U[1, 1 : GRID + 1, :, ls] = gh[1]
        moved = shifts(U[0, :, :, ls], U[1, :, :, ls])
        um = halves(ubuf[sec, m, :, ls].astype(F32) * msk[m])
        for a in range(3):
            for b in range(3):
                kg = jnp.zeros((CELL, LANE), F32)
                for wc in range(SIDE):
                    kg = kg + jnp.sum(moved[wc][2 - b][2 - a : 2 - a + GRID] * um[wc], axis=0)
                sgp[sec, 3 * a + b, :, ls] += kg
        return carry

    lax.fori_loop(0, D // LANE, part, 0)


def spread_heads(value, head_of_lane):
    parts = [jnp.where(head_of_lane == h, value, 0.0) for h in range(PACK)]
    return jnp.concatenate(parts, axis=0).astype(BF)


def gather_heads(value, rows, head_of_lane):
    out = jnp.zeros((rows, GROUP), F32)
    for h in range(PACK):
        out = jnp.where(head_of_lane == h, value[h * rows : (h + 1) * rows], out)
    return out


def unit_slices(unit):
    pair, group = unit // NGROUP, lax.rem(unit, NGROUP)
    rows = [pl.ds(pl.multiple_of((2 * pair + w) * WROWS, 8), WROWS) for w in range(2)]
    cols = [pl.ds(pl.multiple_of(part * D + group * GROUP, LANE), GROUP) for part in range(3)]
    return rows, cols


def window_parts(m, i, qkv):
    rows, cols = unit_slices(i)
    head_of_lane = lax.broadcasted_iota(jnp.int32, (WROWS, GROUP), 1) // HEAD
    q = [qkv[m, r, cols[0]].astype(BF) for r in rows]
    kd = [spread_heads(qkv[m, r, cols[1]], head_of_lane) for r in rows]
    vd = [spread_heads(qkv[m, r, cols[2]], head_of_lane) for r in rows]
    return rows, cols, head_of_lane, q, kd, vd


def window_forward(m, qkv, pw, T, group):
    def unit(i):
        rows, cols, head_of_lane, q, kd, vd = window_parts(m, i, qkv)
        s = [(dot(b, a, 1, 1) * SCALE).reshape(PACK, WROWS, WROWS) for a, b in zip(q, kd)]
        key = lax.broadcasted_iota(jnp.int32, s[0].shape, 1)
        real = lax.rem(key, CELL) < WIN
        s = [jnp.where(real, x, -1e30) for x in s]
        p = [jnp.exp(x - jnp.max(x, axis=1, keepdims=True)) for x in s]
        p = [x * (1.0 / jnp.sum(x, axis=1, keepdims=True)) for x in p]
        p = [x.reshape(PACK * WROWS, WROWS) for x in p]
        for w in range(2):
            pw[m, 2 * i + w, :, 0:WROWS] = p[w]
        out = [dot(x.astype(BF), v, 0, 0) for x, v in zip(p, vd)]
        for w in range(2):
            T[rows[w], cols[0]] = out[w]

    for pair in range(UNITS // 2 // NGROUP):
        unit(pair * NGROUP + group)


def window_backward(m, qkv, pw, T):
    def unit(i, carry):
        rows, cols, head_of_lane, q, kd, vd = window_parts(m, i, qkv)
        g = [T[r, cols[0]].astype(BF) for r in rows]
        p = [pw[m, 2 * i + w, :, 0:WROWS].reshape(PACK, WROWS, WROWS) for w in range(2)]
        dp = [dot(v, x, 1, 1).reshape(PACK, WROWS, WROWS) for v, x in zip(vd, g)]
        ds = [x * (y - jnp.sum(x * y, axis=1, keepdims=True)) for x, y in zip(p, dp)]
        ds = [x.reshape(PACK * WROWS, WROWS).astype(BF) for x in ds]
        pb = [x.reshape(PACK * WROWS, WROWS).astype(BF) for x in p]
        dv = [gather_heads(dot(x, y), WROWS, head_of_lane) for x, y in zip(pb, g)]
        dk = [gather_heads(dot(x, y), WROWS, head_of_lane) * SCALE for x, y in zip(ds, q)]
        dq = [dot(x, y, 0, 0) * SCALE for x, y in zip(ds, kd)]
        for w in range(2):
            qkv[m, rows[w], cols[0]] = dq[w]
            qkv[m, rows[w], cols[1]] = dk[w]
            qkv[m, rows[w], cols[2]] = dv[w]
        return carry

    lax.fori_loop(0, UNITS // 2, unit, 0)


def group_slices(group):
    return [pl.ds(pl.multiple_of(part * D + group * GROUP, LANE), GROUP) for part in range(3)]


def channel_forward(m, qkv, pw, zz, msk):
    def unit(i, carry):
        cols = group_slices(i)
        mask = msk[m][:, :1]
        q = qkv[m, :, cols[0]].astype(BF)
        k = (qkv[m, :, cols[1]] * mask).astype(BF)
        v = qkv[m, :, cols[2]].astype(BF)
        s = dot(q, k, 0, 0) * SCALE
        same = (lax.broadcasted_iota(jnp.int32, s.shape, 0) // HEAD) == (lax.broadcasted_iota(jnp.int32, s.shape, 1) // HEAD)
        s = jnp.where(same, s, -1e30)
        p = jnp.exp(s - jnp.max(s, axis=1, keepdims=True))
        p = p * (1.0 / jnp.sum(p, axis=1, keepdims=True))
        for k in range(GROUP // LANE):
            pw[m, 2 * i + k, 0:GROUP, :] = p[:, k * LANE : (k + 1) * LANE]
        zz[m, 1, :, cols[0]] = dot(v, p.astype(BF), 1, 1).astype(BF)
        return carry

    lax.fori_loop(0, NGROUP, unit, 0, unroll=True)


def channel_backward(m, qkv, pw, T, rr, msk):
    def unit(i, carry):
        cols = group_slices(i)
        mask = msk[m][:, :1]
        q = qkv[m, :, cols[0]].astype(BF)
        k = (qkv[m, :, cols[1]] * mask).astype(BF)
        v = qkv[m, :, cols[2]].astype(BF)
        g = T[:, cols[0]].astype(BF)
        p = jnp.concatenate([pw[m, 2 * i + k, 0:GROUP, :] for k in range(GROUP // LANE)], axis=1)
        dp = dot(g, v, 0, 0)
        ds = (p * (dp - jnp.sum(p * dp, axis=1, keepdims=True))).astype(BF)
        rr[m, 0, :, cols[0]] = (dot(k, ds, 1, 1) * SCALE).astype(BF)
        rr[m, 0, :, cols[1]] = (dot(q, ds) * (SCALE * mask)).astype(BF)
        rr[m, 0, :, cols[2]] = (dot(g, p.astype(BF))).astype(BF)
        return carry

    lax.fori_loop(0, NGROUP, unit, 0, unroll=True)


RING = 8
COLS = FF // RING
WIDE = FF // 12 * 8 // RING
REST = FF // 3 // RING
THIRD = FF // 3 * 2
LENT = RING * 7 // 8
EARLY = 2


def relay_kernel(
    wrows, wcols, img, cot, kern, bias, gain, move, first, second,
    act, ing, out1, out2, outs,
    kern_in, line_in, rows_in, cols_in, isem, wf, w2, pr, msk, flat, ubuf, gin, gout, zz, xh, rs, qkv, ab, rr, pw, U, C, T, sgp, sgs, sgm,
    rL, rR, rA, rG, buf, acc, going, got,
    wl, ws, wr, pl_, usem, gsem, us, gs, ss, rsem, es, er, sgsem, ssem, rcem, osem, sms, smr, xs, xr, ys, yr, bs, br, hs, hr, free,
):
    n = RING
    s = lax.axis_index("section")
    dp = lax.axis_index("dp")
    stage, c = s // 2, lax.rem(s, 2)
    mate = (dp, stage * 2 + (1 - c))
    opposite = (dp, (1 - stage) * 2 + c)
    diagonal = (dp, 3 - s)
    lender, helper = s == 1, s == 2
    early = stage == 0

    spot = lax.rem(dp, n)
    base = dp - spot
    me = jnp.where(lax.rem(spot, 2) == 0, spot // 2, n - 1 - spot // 2)

    def place(pos):
        pos = lax.rem(pos + 2 * n, n)
        return (base + jnp.where(pos < n // 2, 2 * pos, 2 * (n - 1 - pos) + 1), s)

    nexts = (place(me + 1), place(me - 1))
    rounds = n.bit_length() - 1
    partners = []
    for r in range(rounds):
        bit = 1 << r
        partners.append((jnp.where(lax.rem(spot // bit, 2) == 0, dp + bit, dp - bit), s))

    barrier = pltpu.get_barrier_semaphore()
    peers = [mate, opposite, diagonal, *nexts, *partners]
    for peer in peers:
        pl.semaphore_signal(barrier, inc=1, device_id=peer, device_id_type=MESH)

    def remote(src, dst, send, recv, peer):
        return pltpu.make_async_remote_copy(
            src_ref=src, dst_ref=dst, send_sem=send, recv_sem=recv, device_id=peer, device_id_type=MESH
        )

    half = second.shape[0]

    def group_part(group, part):
        cols = pl.ds(pl.multiple_of(part * D + group * GROUP, LANE), GROUP)
        return first.at[:, cols], wf.at[0, :, cols]

    def wait_group(group):
        for part in range(3):
            src, dst = group_part(group, part)
            i = group * 3 + part

            @pl.when(c == 0)
            def _():
                pltpu.make_async_copy(src, dst, wl.at[i]).wait()

            @pl.when(c == 1)
            def _():
                remote(src, dst, ws.at[i], wr.at[i], mate).wait_recv()

    def weight_parts(k):
        parts = []
        if k == 0:
            for group in range(NGROUP):
                for part in range(3):
                    parts.append(group_part(group, part))
            cols = pl.ds(3 * D, D)
            parts.append((first.at[:, cols], wf.at[k, :, cols]))
        else:
            for i in range(3):
                cols = pl.ds(i * (FF // 3), FF // 3)
                parts.append((first.at[:, cols], wf.at[k, :, cols]))
        third = half // 3
        for i in range(3):
            rows = pl.ds(i * third, third)
            parts.append((second.at[rows, :], w2.at[pl.ds(k * half + i * third, third), :]))
        return parts

    names = (
        [f"qkv{group}" for group in range(NGROUP) for _ in range(3)] + ["out"] + [f"low{i}" for i in range(3)],
        ["in"] * 3 + [f"high{i}" for i in range(3)],
    )

    def weight_copies(k):
        local = [pltpu.make_async_copy(a, b, wl.at[i]) for i, (a, b) in enumerate(weight_parts(k))]
        sent = [remote(a, b, ws.at[i], wr.at[i], mate) for i, (a, b) in enumerate(weight_parts(k))]
        return local, sent

    def params_copy(k):
        return remote(pr.at[k], pr.at[k], ws.at[13], wr.at[13], mate)

    own = flat.at[1]
    small_inputs = [
        pltpu.make_async_copy(a, b, isem.at[i])
        for i, (a, b) in enumerate(
            ((kern, kern_in), (bias, line_in.at[0]), (gain, line_in.at[1]), (move, line_in.at[2]), (wrows, rows_in), (wcols, cols_in))
        )
    ]
    for copy in small_inputs:
        copy.start()
    img_in = pltpu.make_async_copy(img, own, isem.at[6])
    cot_in = pltpu.make_async_copy(cot, own, isem.at[6])

    @pl.when(early)
    def _():
        img_in.start()

    for k in range(2):

        @pl.when(c == k)
        def _():
            for copy in weight_copies(k)[0]:
                copy.start()

    pl.semaphore_wait(barrier, len(peers))
    for k in range(2):

        @pl.when(c == k)
        def _():
            for copy in weight_copies(k)[1]:
                copy.start()

    for copy in small_inputs:
        copy.wait()
    pr[c, 0:9, :] = kern_in[...].astype(F32)
    for i in range(3):
        pr[c, 9 + i : 10 + i, :] = line_in[i].astype(F32)
    params_copy(c).start()

    def wait_weights(*wanted):
        for k in range(2):

            @pl.when(c == k)
            def _():
                for name, copy in zip(names[k], weight_copies(k)[0]):
                    if name in wanted:
                        copy.wait()
                for name, copy in zip(names[1 - k], weight_copies(1 - k)[1]):
                    if name in wanted:
                        copy.wait_recv()

    def wait_params(k):
        @pl.when(c != k)
        def _():
            params_copy(k).wait_recv()

    raw = flat.at[0]
    img_out = remote(img, raw, pl_.at[0], pl_.at[1], opposite)
    cot_out = remote(cot, raw, pl_.at[0], pl_.at[1], opposite)

    def pad(src, dst):
        blank = jnp.zeros((CELL - WIN, D), F32)
        for r in range(GRID):
            line = src[r].astype(F32)
            for wc in range(SIDE):
                cells = jnp.concatenate([line[wc * WIN : (wc + 1) * WIN], blank], axis=0)
                C[pl.ds(wc * HALF + r * CELL, CELL), :] = cells
        dst[...] = C[...].astype(BF)

    def unpad(dst):
        for r in range(GRID):
            sides = [C[pl.ds(wc * HALF + r * CELL, CELL), :][:WIN] for wc in range(SIDE)]
            dst[r] = jnp.concatenate(sides, axis=0).astype(BF)

    @pl.when(early)
    def _():
        cot_out.start()
        img_in.wait()
        pad(own, ubuf.at[0, 0])

    @pl.when(jnp.logical_not(early))
    def _():
        img_out.start()
        cot_in.start()
        cot_in.wait()
        pad(own, gin.at[1])

    index = lax.broadcasted_iota(jnp.int32, (ROWS, LANE), 0)
    cell = lax.rem(index, CELL)
    row = lax.rem(index, HALF) // CELL
    column = (index // HALF) * WIN + cell
    for m in range(2):
        inside = (row < WIN * rows_in[c + 2 * m]) & (column < WIN * cols_in[c + 2 * m]) & (cell < WIN)
        msk[m] = jnp.where(inside, 1.0, 0.0)

    @pl.when(jnp.logical_not(early))
    def _():
        cot_out.wait_recv()
        pad(raw, gin.at[0])
        for m in range(2):
            for l in range(D // LANE):
                cols = pl.ds(l * LANE, LANE)
                gin[m, :, cols] = (gin[m, :, cols].astype(F32) * msk[m]).astype(BF)

    for wc in range(SIDE):
        U[wc, 0] = jnp.zeros((CELL, D), F32)
        U[wc, GRID + 1] = jnp.zeros((CELL, D), F32)
    sgp[...] = jnp.zeros(sgp.shape, F32)

    def hop(m, dst, send, recv):
        sides = [pl.ds(i * D // 2, D // 2) for i in range(2)]
        return [
            remote(gout.at[m, :, cols], dst.at[:, cols], send.at[m, i], recv.at[m, i], opposite)
            for i, cols in enumerate(sides)
        ]

    def u_hop(m):
        return hop(m, ubuf.at[0, m], us, usem)

    def g_hop(m):
        return hop(m, gin.at[m], gs, gsem)

    def factor_copies(k, m):
        if k == 0:
            parts = [
                ("F", zz.at[m, 0], rL.at[m, 0]),
                ("F", zz.at[m, 1], rL.at[m, 1]),
                ("G", rr.at[m, 0, :, pl.ds(3 * D, D)], rR.at[m, :, pl.ds(3 * D, D)]),
                ("A", rr.at[m, 0, :, pl.ds(0, 3 * D)], rR.at[m, :, pl.ds(0, 3 * D)]),
            ]
        else:
            parts = [
                ("X0", zz.at[m, 2], rL.at[m, 0]),
                ("M", gin.at[m], rG.at[m]),
            ]
            for i, cols in enumerate((pl.ds(0, FF // 3 * 2), pl.ds(FF // 3 * 2, FF // 3))):
                parts.append((f"X{i}", ab.at[m, :, cols], rA.at[m, :, cols]))
                parts.append((f"H{i}", rr.at[m, 1, :, cols], rR.at[m, :, cols]))
        return [(w, remote(a, b, ss.at[m, i], rsem.at[m, i], mate)) for i, (w, a, b) in enumerate(parts)]

    def start_factors(m, which):
        for k in range(2):

            @pl.when(c != k)
            def _():
                for when, copy in factor_copies(k, m):
                    if when == which:
                        copy.start()

    def wait_factors(which):
        for k in range(2):

            @pl.when(c == k)
            def _():
                for m in range(2):
                    for when, copy in factor_copies(k, m):
                        if when[0] in which:
                            copy.wait_recv()

    def shard(k):
        return lax.rem(k + 4 * n, n)

    def sign(h):
        return 1 if h == 0 else -1

    def home(h, t):
        return shard(me + sign(h) - sign(h) * t)

    def products(terms):
        total = None
        for a, b in terms:
            part = dot(a[...], b[...], 0, 0)
            total = part if total is None else total + part
        return total

    def tile(sub, h, j):
        side = pl.ds(h * COLS, COLS)
        if sub in (0, 4):
            rows = first_rows(sub, h)
            last = jnp.where(j >= (3 * n) // 4, 1, 0)
            own = jnp.where(c == 1, 2, last)
            other = jnp.where(c == 1, 0, last)
            cols = lanes(j, COLS)
            terms = [(zz.at[m, own, :, rows], rr.at[m, c, :, cols]) for m in range(2)]
            terms += [(rL.at[m, other, :, rows], rR.at[m, :, cols]) for m in range(2)]
        elif sub == 3:
            cols = [pl.ds(pl.multiple_of(i * LENT * REST + j * REST, LANE), REST) for i in range(2)]
            terms = [(rA.at[m, :, cols[0]], rG.at[m, :, side]) for m in range(2)]
            terms += [(rA.at[m, :, cols[1]], gout.at[m, :, side]) for m in range(2)]
        else:
            cols = lanes(j, WIDE) if sub == 1 else pl.ds(pl.multiple_of(THIRD + j * REST, LANE), REST)
            terms = [(ab.at[m, :, cols], gin.at[m, :, side]) for m in range(2)]
            terms += [(rA.at[m, :, cols], rG.at[m, :, side]) for m in range(2)]
        return products(terms)

    sizes = (COLS // 3 * 2, WIDE, REST, REST, COLS // 3)
    starts = (0, COLS, COLS + WIDE, COLS + WIDE, COLS // 3 * 2)
    parts = [pl.ds(start, size) for start, size in zip(starts, sizes)]
    subs = range(len(sizes))
    odd = c == 1
    active = (None, odd, odd, helper, None)

    def where_live(sub, h, j, run):
        if sub == 2:
            pl.when(jnp.logical_not(lender) | (j >= LENT - h))(run)
        elif sub == 3:
            pl.when(j < LENT - h)(run)
        else:
            run()

    def first_rows(sub, h):
        return pl.ds(h * COLS + (0 if sub == 0 else sizes[0]), sizes[sub])

    def where_active(sub, run):
        if active[sub] is None:
            run()
        else:
            pl.when(active[sub])(run)


    def gathered(sub, h, j):
        if sub in (0, 4):
            return wf.at[0, first_rows(sub, h), lanes(j, COLS)]
        first_row = 0 if sub == 1 else THIRD
        return w2.at[pl.ds(pl.multiple_of(first_row + j * sizes[sub], 16), sizes[sub]), pl.ds(h * COLS, COLS)]

    def scatter(h, t, sub):
        src, dst = buf.at[h, t, parts[sub], :], buf.at[h, t + 1, parts[sub], :]
        return remote(src, dst, ssem.at[h, t, sub], rcem.at[h, t + 1, sub], nexts[h])

    def spread(h, t, sub, j):
        ref = gathered(sub, h, j)
        return remote(ref, ref, ssem.at[h, n - 1 + t, sub], rcem.at[h, n + t, sub], nexts[h])

    half_shards = n * 3 // 4

    def write(h, j, sub):
        src, side = gathered(sub, h, j), pl.ds(h * COLS, COLS)
        if sub in (0, 4):
            dst = out1.at[first_rows(sub, h), lanes(j, COLS)]
        elif sub == 1:
            dst = out2.at[pl.ds(pl.multiple_of((j - half_shards) * WIDE, 16), WIDE), side]
        else:
            dst = out2.at[pl.ds(pl.multiple_of(THIRD - FF // 2 + j * REST, 16), REST), side]
        if sub == 3:
            return remote(src, dst, bs.at[h, j], br.at[h, j], diagonal)
        return pltpu.make_async_copy(src, dst, osem.at[h, j, sub])

    def hand_over(h, j):
        dst = out2.at[pl.ds(pl.multiple_of(j * WIDE, 16), WIDE), pl.ds(h * COLS, COLS)]
        return remote(gathered(1, h, j), dst, hs.at[h, j], hr.at[h, j], mate)

    def deliver(h, j, sub):
        if sub == 1:

            @pl.when(j < half_shards)
            def _():
                hand_over(h, j).start()

            @pl.when(j >= half_shards)
            def _():
                write(h, j, sub).start()

        else:
            write(h, j, sub).start()

    def lend(m):
        cols, there = pl.ds(THIRD, LENT * REST), [rA.at[m, :, pl.ds(i * LENT * REST, LENT * REST)] for i in range(2)]
        return (
            remote(ab.at[m, :, cols], there[0], xs.at[m], xr.at[m], diagonal),
            remote(rA.at[m, :, cols], there[1], xs.at[2 + m], xr.at[2 + m], diagonal),
        )

    def share(m):
        return remote(gout.at[m], rG.at[m], ys.at[m], yr.at[m], mate)

    def reduce_event(sub, h, e):
        j = shard(me - sign(h) * e)

        @pl.when(e == n - 1)
        def _():
            pl.semaphore_wait(free.at[h, sub], 1)

        def run():
            total = tile(sub, h, j)

            @pl.when(e == 0)
            def _():
                buf[h, 0, parts[sub], :] = total.astype(BF)
                scatter(h, 0, sub).start()

            @pl.when((e > 0) & (e < n - 1))
            def _():
                scatter(h, e - 1, sub).wait_recv()
                buf[h, e, parts[sub], :] = (total + buf[h, e, parts[sub], :].astype(F32)).astype(BF)
                scatter(h, e, sub).start()

            @pl.when(e == n - 1)
            def _():
                scatter(h, n - 2, sub).wait_recv()
                gathered(sub, h, j)[...] = (total + buf[h, n - 1, parts[sub], :].astype(F32)).astype(BF)
                spread(h, 0, sub, j).start()
                deliver(h, j, sub)

        where_live(sub, h, j, run)

    def event(sub, e):
        for h in range(2):

            @pl.when(e < n)
            def _():
                reduce_event(sub, h, e)

            @pl.when((e >= n) & (e < 2 * n - 1))
            def _():
                t = e - (n - 1)
                j = home(h, t)

                def run():
                    spread(h, t - 1, sub, j).wait_recv()

                    @pl.when(t < n - 1)
                    def _():
                        spread(h, t, sub, j).start()

                    deliver(h, j, sub)

                where_live(sub, h, j, run)

    def early_event(e, which):
        @pl.when(odd)
        def _():
            for sub in which:
                where_active(sub, lambda: event(sub, e))

    def small(r):
        return remote(going.at[r], got.at[r], sms.at[r], smr.at[r], partners[r])

    def mlp(m, order, wait):
        total, before, last = C[...], None, None
        for t in order:
            cols = pl.ds(t * FTILE, FTILE)
            h = dot(zz[m, 2], wf[1, :, cols])
            if last is not None:
                wait(last)
                total = total + dot(before, w2[pl.ds(last * FTILE, FTILE), :])
            a, d = gelu_parts(h)
            before, last = a.astype(BF), t
            ab[m, :, cols] = before
            rr[m, 1, :, cols] = d.astype(BF)
            if t == FF // FTILE * 2 // 3 - 1 and order == range(FF // FTILE):
                start_factors(m, "X0")
        wait(last)
        for i in range(2):
            cols = pl.ds(i * D // 2, D // 2)
            part = total[:, i * D // 2 : (i + 1) * D // 2]
            gout[jnp.where(early, m, 2 + m), :, cols] = (part + dot(before, w2[pl.ds(last * FTILE, FTILE), cols])).astype(BF)

            @pl.when(early)
            def _():
                u_hop(m)[i].start()

    def give_results(m):
        @pl.when(early)
        def _():
            C[...] = gout[m].astype(F32)

        @pl.when(jnp.logical_not(early))
        def _():
            for l in range(D // LANE):
                cols = pl.ds(l * LANE, LANE)
                C[:, cols] = gout[2 + m, :, cols].astype(F32) * msk[m]

        unpad(flat.at[m])

        @pl.when(early & (m == 0))
        def _():
            pltpu.make_async_copy(flat.at[0], ing, es.at[1]).start()

        @pl.when(early & (m == 1))
        def _():
            remote(flat.at[1], ing, es.at[1], er.at[1], opposite).start()

        @pl.when(jnp.logical_not(early) & (m == 0))
        def _():
            remote(flat.at[0], act, es.at[0], er.at[0], opposite).start()

        @pl.when(jnp.logical_not(early) & (m == 1))
        def _():
            pltpu.make_async_copy(flat.at[1], act, es.at[0]).start()

    def forward(m, p):
        @pl.when(jnp.logical_not(early))
        def _():
            for copy in u_hop(m):
                copy.wait_recv()

        @pl.when(early & (m == 1))
        def _():
            img_out.wait_recv()
            pad(raw, ubuf.at[0, 1])

        once = p == 0
        starting = early & once

        @pl.when(once)
        def _():
            wait_params(0)

        @pl.when(once & jnp.logical_not(early))
        def _():
            wait_params(1)
            wait_weights(*set(names[0] + names[1]))

        front_forward(0, m, ubuf, msk, pr, U, C, zz, xh, rs)

        @pl.when(early)
        def _():
            def head_group(group, carry):
                @pl.when(once)
                def _():
                    wait_group(group)

                for part in range(3):
                    cols = pl.ds(pl.multiple_of(part * D + group * GROUP, LANE), GROUP)
                    qkv[m, :, cols] = dot(zz[m, 0], wf[0, :, cols])
                window_forward(m, qkv, pw, T, group)
                return carry

            lax.fori_loop(0, NGROUP, head_group, 0)
            zz[m, 1] = T[...].astype(BF)

        @pl.when(starting)
        def _():
            wait_weights("out")
            wait_params(1)

        @pl.when(jnp.logical_not(early))
        def _():
            qkv[m] = dot(zz[m, 0], wf[0, :, pl.ds(0, 3 * D)])

        @pl.when(jnp.logical_not(early))
        def _():
            channel_forward(m, qkv, pw, zz, msk)

        ubuf[1, m] = (C[...] + dot(zz[m, 1], wf[0, :, pl.ds(3 * D, D)])).astype(BF)

        front_forward(1, m, ubuf, msk, pr, U, C, zz, xh, rs)

        @pl.when(starting)
        def _():
            wait_weights("in")
            order = [i + 3 * k for i in range(3) for k in range(2)]
            mlp(m, order, lambda t: wait_weights(f"low{t}" if t < 3 else f"high{t - 3}"))
            start_factors(m, "X0")

        @pl.when(jnp.logical_not(starting))
        def _():
            mlp(m, range(FF // FTILE), lambda t: None)

        start_factors(m, "F")
        start_factors(m, "X1")

        @pl.when(early & (m == 1))
        def _():
            wait_factors("FX")

        @pl.when(lender & (m == 1))
        def _():
            for i in range(2):
                for copy in lend(i):
                    copy.start()

    def backward(m):
        @pl.when(early)
        def _():
            for copy in g_hop(m):
                copy.wait_recv()
            start_factors(m, "M")

        for t in range(FF // FTILE):
            cols = pl.ds(t * FTILE, FTILE)
            da = dot(gin[m], w2[cols, :], 1, 1)
            rr[m, 1, :, cols] = (da * rr[m, 1, :, cols].astype(F32)).astype(BF)
            if t == FF // FTILE * 2 // 3 - 1:
                start_factors(m, "H0")

        start_factors(m, "H1")

        @pl.when(m == 1)
        def _():
            @pl.when(jnp.logical_not(early))
            def _():
                wait_factors("FX")

            wait_factors("M")
            early_event(0, (1, 2))

        T[...] = dot(rr[m, 1], wf[1], 1, 1)

        @pl.when(m == 1)
        def _():
            wait_factors("H")
            early_event(0, (0, 4))

        last = pl.ds(3 * D, D)

        @pl.when(early)
        def _():
            for copy in u_hop(m):
                copy.wait_send()

        def tail_lanes(i):
            return rr.at[m, 0, :, pl.ds(pl.multiple_of(3 * D + i * LANE, LANE), LANE)]

        def nothing(half):
            pass

        front_backward(1, m, msk, pr, U, T, lambda i: gin.at[m, :, lanes(i)], xh, rs, sgp, tail_lanes, nothing)

        start_factors(m, "G")
        T[...] = dot(rr[m, 0, :, last], wf[0, :, last], 1, 1)

        @pl.when(early)
        def _():
            window_backward(m, qkv, pw, T)
            for i in range(3):
                cols = pl.ds(i * D, D)
                rr[m, 0, :, cols] = qkv[m, :, cols].astype(BF)

        @pl.when(jnp.logical_not(early))
        def _():
            channel_backward(m, qkv, pw, T, rr, msk)

        start_factors(m, "A")

        @pl.when(m == 1)
        def _():
            early_event(1, (1, 2, 0, 4))

        T[...] = dot(rr[m, 0, :, pl.ds(0, 3 * D)], wf[0, :, pl.ds(0, 3 * D)], 1, 1)
        def send_half(half):
            @pl.when(jnp.logical_not(early))
            def _():
                g_hop(m)[half].start()

        front_backward(
            0, m, msk, pr, U, T, tail_lanes, xh, rs, sgp, lambda i: gout.at[m, :, lanes(i)], send_half
        )

        @pl.when(s == 3)
        def _():
            share(m).start()

    @pl.when(jnp.logical_not(early))
    def _():
        for m in range(2):
            start_factors(m, "M")

    def phase(p, carry):
        m = jnp.where(early, lax.rem(p, 2), p // 2)
        ahead = jnp.where(early, p < 2, lax.rem(p, 2) == 0)

        @pl.when(ahead)
        def _():
            forward(m, p)

        @pl.when(jnp.logical_not(ahead))
        def _():
            backward(m)

        return carry

    lax.fori_loop(0, 4, phase, 0)

    for h in range(2):
        for sub in subs:

            def ready():
                pl.semaphore_signal(free.at[h, sub], inc=1, device_id=nexts[1 - h], device_id_type=MESH)

            where_active(sub, ready)

    give = remote(sgs.at[1 - c], sgm, sgsem.at[0], sgsem.at[1], mate)

    def small_sums():
        for sec in range(2):
            for j in range(12):
                sgs[sec, j : j + 1, :] = jnp.sum(sgp[sec, j], axis=0, keepdims=True)
            sgs[sec, 12:16, :] = jnp.zeros((4, D), F32)
        give.start()

    wait_factors("GA")

    @pl.when(helper)
    def _():
        for m in range(2):
            for copy in lend(m):
                copy.wait_recv()
            share(m).wait_recv()

    def ring_step(t, carry):
        for sub in (0, 4):
            event(sub, t + jnp.where(odd, EARLY, 0))
        where_active(1, lambda: event(1, t + EARLY))
        where_active(2, lambda: event(2, t + EARLY))
        where_active(3, lambda: event(3, t))
        @pl.when((t >= 1) & (t < 5))
        def _():
            front_sums((t - 1) // 2, lax.rem(t - 1, 2), ubuf, msk, U, xh, sgp)

        pl.when(t == 5)(small_sums)

        @pl.when((t >= 6) & (t < 8))
        def _():
            give_results(t - 6)

        for r in range(rounds + 1):

            @pl.when(t == 6 + 2 * r)
            def _():
                if r == 0:
                    give.wait_recv()
                    acc[0] = sgs[c] + sgm[...]
                else:
                    small(r - 1).wait_recv()
                    acc[r] = going[r - 1].astype(F32) + got[r - 1].astype(F32)
                if r < rounds:
                    going[r] = acc[r].astype(BF)
                    small(r).start()

        return carry

    lax.fori_loop(0, 2 * n - 1, ring_step, 0)
    outs[...] = acc[rounds]

    for k in range(2):

        @pl.when(c == k)
        def _():
            for copy in weight_copies(k)[1]:
                copy.wait_send()
            params_copy(k).wait_send()
            for m in range(2):
                for _when, copy in factor_copies(1 - k, m):
                    copy.wait_send()

    give.wait_send()
    for r in range(rounds):
        small(r).wait_send()

    def drain(t, carry):
        for h in range(2):
            for sub in subs:

                def sent():
                    where_live(sub, h, shard(me - sign(h) * t), lambda: scatter(h, t, sub).wait_send())
                    where_live(sub, h, home(h, t), lambda: spread(h, t, sub, home(h, t)).wait_send())

                where_active(sub, sent)

        return carry

    lax.fori_loop(0, n - 1, drain, 0)

    def written(j, carry):
        for h in range(2):
            write(h, j, 0).wait()
            write(h, j, 4).wait()

            @pl.when(odd)
            def _():
                where_live(2, h, j, lambda: write(h, j, 2).wait())

                @pl.when(j < half_shards)
                def _():
                    hand_over(h, j).wait_send()

                @pl.when(j >= half_shards)
                def _():
                    write(h, j, 1).wait()

            @pl.when(jnp.logical_not(odd) & (j < half_shards))
            def _():
                hand_over(h, j).wait_recv()

            @pl.when(helper & (j < LENT - h))
            def _():
                write(h, j, 3).wait_send()

            @pl.when(lender & (j < LENT - h))
            def _():
                write(h, j, 3).wait_recv()

        return carry

    lax.fori_loop(0, n, written, 0)

    @pl.when(lender)
    def _():
        for m in range(2):
            for copy in lend(m):
                copy.wait_send()

    @pl.when(s == 3)
    def _():
        for m in range(2):
            share(m).wait_send()

    @pl.when(early)
    def _():
        cot_out.wait_send()
        pltpu.make_async_copy(flat.at[0], ing, es.at[1]).wait()
        remote(flat.at[1], ing, es.at[1], er.at[1], opposite).wait_send()
        remote(flat.at[0], act, es.at[0], er.at[0], opposite).wait_recv()

    @pl.when(jnp.logical_not(early))
    def _():
        img_out.wait_send()
        for m in range(2):
            for copy in g_hop(m):
                copy.wait_send()
        remote(flat.at[0], act, es.at[0], er.at[0], opposite).wait_send()
        pltpu.make_async_copy(flat.at[1], act, es.at[0]).wait()
        remote(flat.at[1], ing, es.at[1], er.at[1], opposite).wait_recv()


def relay(wrows, wcols, img, cot, kern, bias, gain, move, first, second):
    shape = jax.ShapeDtypeStruct
    vmem = pl.BlockSpec(memory_space=pltpu.VMEM)
    anywhere = pl.BlockSpec(memory_space=pl.ANY)
    dma = pltpu.SemaphoreType.DMA
    image = (ROWS, D)
    slot = img.shape
    rounds = RING.bit_length() - 1
    return pl.pallas_call(
        relay_kernel,
        out_shape=[
            shape(slot, BF),
            shape(slot, BF),
            shape((D, FF), BF),
            shape((FF // 2, D), BF),
            shape((16, D), F32),
        ],
        in_specs=[anywhere] * 10,
        out_specs=[anywhere] * 4 + [vmem],
        scratch_shapes=[
            pltpu.VMEM(kern.shape, BF),
            pltpu.VMEM((3,) + bias.shape, BF),
            pltpu.SMEM(wrows.shape, jnp.int32),
            pltpu.SMEM(wcols.shape, jnp.int32),
            dma((7,)),
            pltpu.VMEM((2, D, FF), BF),
            pltpu.VMEM((FF, D), BF),
            pltpu.VMEM((2, 16, D), F32),
            pltpu.VMEM((2, ROWS, LANE), F32),
            pltpu.VMEM((2,) + slot, BF),
            pltpu.VMEM((2, 2) + image, BF),
            pltpu.VMEM((2,) + image, BF),
            pltpu.VMEM((4,) + image, BF),
            pltpu.VMEM((2, 3) + image, BF),
            pltpu.VMEM((2, 2) + image, BF),
            pltpu.VMEM((2, 2, ROWS, LANE), F32),
            pltpu.VMEM((2, ROWS, 3 * D), F32),
            pltpu.VMEM((2, ROWS, FF), BF),
            pltpu.VMEM((2, 2, ROWS, FF), BF),
            pltpu.VMEM((2, UNITS, PACK * WROWS, LANE), F32),
            pltpu.VMEM((SIDE, GRID + 2, CELL, D), F32),
            pltpu.VMEM(image, F32),
            pltpu.VMEM(image, F32),
            pltpu.VMEM((2, 12, CELL, D), F32),
            pltpu.VMEM((2, 16, D), F32),
            pltpu.VMEM((16, D), F32),
            pltpu.VMEM((2, 2) + image, BF),
            pltpu.VMEM((2, ROWS, FF), BF),
            pltpu.VMEM((2, ROWS, FF), BF),
            pltpu.VMEM((2,) + image, BF),
            pltpu.VMEM((2, RING, COLS + WIDE + REST, COLS), BF),
            pltpu.VMEM((rounds + 1, 16, D), F32),
            pltpu.VMEM((rounds, 16, D), BF),
            pltpu.VMEM((rounds, 16, D), BF),
            dma((14,)),
            dma((14,)),
            dma((14,)),
            dma((2,)),
            dma((2, 2)),
            dma((2, 2)),
            dma((2, 2)),
            dma((2, 2)),
            dma((2, 8)),
            dma((2, 8)),
            dma((2,)),
            dma((2,)),
            dma((2,)),
            dma((2, 2 * RING, 5)),
            dma((2, 2 * RING, 5)),
            dma((2, RING, 5)),
            dma((rounds,)),
            dma((rounds,)),
            dma((4,)),
            dma((4,)),
            dma((2,)),
            dma((2,)),
            dma((2, RING)),
            dma((2, RING)),
            dma((2, RING)),
            dma((2, RING)),
            pltpu.SemaphoreType.REGULAR((2, 5)),
        ],
        name="relay",
        compiler_params=pltpu.CompilerParams(
            collective_id=1, has_side_effects=True, vmem_limit_bytes=63 * 2**20
        ),
    )(wrows, wcols, img, cot, kern, bias, gain, move, first, second)


def finish_kernel(
    out1, out2, act, ing, outs, first, second, acts, ings, kern, bias, gain, move,
    raw1, raw2, full1, full2, acted, graded, wide, small, kernels, rsem, wsem,
):
    steps = rsem.shape[0] - 3

    loads = [
        pltpu.make_async_copy(act, acted, rsem.at[steps]),
        pltpu.make_async_copy(ing, graded, rsem.at[steps + 1]),
        pltpu.make_async_copy(outs, small, rsem.at[steps + 2]),
    ]
    for copy in loads:
        copy.start()
    reads, writes = [], []
    for i in range(steps):
        pair = ((out1, raw1, full1, first), (out2, raw2, full2, second))[i % 2]
        src, raw, full, dst = pair
        half = steps // 2
        rows = pl.ds(i // 2 * (src.shape[0] // half), src.shape[0] // half)
        reads.append((pltpu.make_async_copy(src.at[rows, :], raw.at[rows, :], rsem.at[i]), raw, full, rows))
        writes.append(pltpu.make_async_copy(full.at[rows, :], dst.at[rows, :], wsem.at[i]))
    for copy, *_ in reads:
        copy.start()
    for (copy, raw, full, rows), back in zip(reads, writes):
        copy.wait()
        full[rows, :] = raw[rows, :].astype(F32)
        back.start()
    for copy in loads:
        copy.wait()
    for k in range(9):
        kernels[k] = small[k : k + 1, :]
    for r in range(GRID):
        line = graded[r].astype(F32)
        for k in range(GRID):
            wide[r, k] = line[k : k + 1, :]
    last = [
        pltpu.make_async_copy(acted, acts, wsem.at[steps]),
        pltpu.make_async_copy(wide, ings, wsem.at[steps + 1]),
        pltpu.make_async_copy(kernels, kern, wsem.at[steps + 2]),
    ]
    for i, dst in enumerate((bias, gain, move)):
        last.append(pltpu.make_async_copy(small.at[pl.ds(9 + i, 1), :], dst, wsem.at[steps + 3 + i]))
    for copy in last:
        copy.start()
    for copy in writes + last:
        copy.wait()


def finish(out1, out2, act, ing, outs):
    shape = jax.ShapeDtypeStruct
    slot = act.shape
    anywhere = pl.BlockSpec(memory_space=pl.ANY)
    line = (1, D)
    spread = slot[:2] + line
    steps = 16
    return pl.pallas_call(
        finish_kernel,
        out_shape=[
            shape(out1.shape, F32),
            shape(out2.shape, F32),
            shape(slot, BF),
            shape(spread, F32),
            shape((9,) + line, F32),
            shape(line, F32),
            shape(line, F32),
            shape(line, F32),
        ],
        in_specs=[anywhere] * 5,
        out_specs=[anywhere] * 8,
        scratch_shapes=[
            pltpu.VMEM(out1.shape, out1.dtype),
            pltpu.VMEM(out2.shape, out2.dtype),
            pltpu.VMEM(out1.shape, F32),
            pltpu.VMEM(out2.shape, F32),
            pltpu.VMEM(slot, BF),
            pltpu.VMEM(slot, BF),
            pltpu.VMEM(spread, F32),
            pltpu.VMEM(outs.shape, F32),
            pltpu.VMEM((9,) + line, F32),
            pltpu.SemaphoreType.DMA((steps + 3,)),
            pltpu.SemaphoreType.DMA((steps + 6,)),
        ],
        name="finish",
        compiler_params=pltpu.CompilerParams(vmem_limit_bytes=60 * 2**20),
    )(out1, out2, act, ing, outs)


def per_device(
    images, cotangent, window_rows, window_cols, pos_kernel, pos_bias, norm_gain, norm_shift, first_weight, second_weight
):
    act, ing, out1, out2, outs = relay(
        window_rows, window_cols, images[0], cotangent[0], pos_kernel[0], pos_bias, norm_gain, norm_shift,
        first_weight[0], second_weight,
    )
    if lax.axis_size("dp") > RING:
        out1, out2, outs = lax.psum((out1.astype(F32) / RING, out2.astype(F32) / RING, outs / RING), "dp")
    out1, out2, act, ing, kern, bias, gain, move = finish(out1, out2, act, ing, outs)
    return (
        act[None],
        ing.transpose(2, 0, 1, 3),
        out1[None],
        out2,
        kern.transpose(1, 0, 2),
        bias,
        gain,
        move,
    )


def solution(mesh):
    in_specs = (
        P(("dp", "section"), None, None, None),
        P(("dp", "section"), None, None, None),
        P("dp"),
        P("dp"),
        P("section", None, None),
        P("section", None),
        P("section", None),
        P("section", None),
        P("section", None, None),
        P("section", None),
    )
    out_specs = (
        P(("dp", "section"), None, None, None),
        P(("dp", "section"), None, None, None),
        P("section", None, None),
        P("section", None),
        P("section", None, None),
        P("section", None),
        P("section", None),
        P("section", None),
    )
    return jax.shard_map(per_device, mesh=mesh, in_specs=in_specs, out_specs=out_specs, check_vma=False)
```

```python
from functools import partial

import jax
import jax.numpy as jnp
from jax import lax
from jax.experimental import pallas as pl
from jax.experimental.pallas import tpu as pltpu
from jax.sharding import PartitionSpec as P

D = 768
FF = 3072
HEADS = 24
HEAD = 32
WIN = 7
SIDE = 2
GRID = SIDE * WIN
CELL = 8
WROWS = WIN * CELL
HALF = GRID * CELL
ROWS = SIDE * HALF
GROUP = 256
PACK = GROUP // HEAD
NGROUP = D // GROUP
UNITS = NGROUP * SIDE * SIDE
LANE = 128
FTILE = 512
EPS = 1e-05
SCALE = HEAD ** (-0.5)
BF = jnp.bfloat16
F32 = jnp.float32
MESH = pl.DeviceIdType.MESH


def dot(a, b, ca=1, cb=0):
    return lax.dot_general(a, b, (((ca,), (cb,)), ((), ())), preferred_element_type=F32)


def lanes(index, width=LANE):
    return pl.ds(pl.multiple_of(index * width, width), width)


def halves(value):
    return value.reshape(SIDE, GRID, CELL, value.shape[-1])


def shifts(left, right):
    column = lax.broadcasted_iota(jnp.int32, left.shape, 1)
    before0 = pltpu.roll(left, 1, 1)
    after0 = jnp.where(column == WIN - 1, pltpu.roll(right, CELL - 2, 1), pltpu.roll(left, CELL - 1, 1))
    before1 = jnp.where(column == 0, pltpu.roll(left, 2, 1), pltpu.roll(right, 1, 1))
    after1 = pltpu.roll(right, CELL - 1, 1)
    return ((before0, left, after0), (before1, right, after1))


def gelu_parts(h):
    expo = jnp.exp(h * h * -0.5)
    t = 1.0 / (1.0 + (0.3275911 * 0.7071067811865476) * jnp.abs(h))
    poly = t * (0.127414796 + t * (-0.142248368 + t * (0.7107068705 + t * (-0.7265760135 + t * 0.5307027145))))
    tail = poly * expo
    phi = jnp.where(h >= 0, 1.0 - tail, tail)
    return h * phi, phi + h * expo * 0.3989422804014327


def front_forward(sec, m, ubuf, msk, pr, U, C, zz, xh, rs):
    zero = jnp.zeros((ROWS, LANE), F32)

    def conv(i, total):
        ls = lanes(i)
        u = ubuf[sec, m, :, ls].astype(F32)
        masked = halves(u * msk[m])
        U[0, 1 : GRID + 1, :, ls] = masked[0]
        U[1, 1 : GRID + 1, :, ls] = masked[1]
        moved = shifts(U[0, :, :, ls], U[1, :, :, ls])
        taps = pr[sec, :, ls]
        uh = halves(u)
        sums = []
        for wc in range(SIDE):
            acc = uh[wc] + taps[9:10, :][None]
            for a in range(3):
                for b in range(3):
                    acc = acc + moved[wc][b][a : a + GRID] * taps[3 * a + b : 3 * a + b + 1, :][None]
            acc = acc.reshape(HALF, LANE)
            C[pl.ds(wc * HALF, HALF), ls] = acc
            sums.append(acc)
        return total + jnp.concatenate(sums, axis=0)

    mean = jnp.sum(lax.fori_loop(0, D // LANE, conv, zero, unroll=True), axis=-1, keepdims=True) * (1.0 / D)

    def spread(i, total):
        centred = C[:, lanes(i)] - mean
        return total + centred * centred

    var = jnp.sum(lax.fori_loop(0, D // LANE, spread, zero, unroll=True), axis=-1, keepdims=True) * (1.0 / D)
    rstd = lax.rsqrt(var + EPS)
    rs[sec, m] = jnp.broadcast_to(rstd, (ROWS, LANE))

    def norm(i, carry):
        ls = lanes(i)
        xhat = (C[:, ls] - mean) * rstd
        xh[sec, m, :, ls] = xhat.astype(BF)
        zz[m, 2 * sec, :, ls] = (xhat * pr[sec, 10:11, ls] + pr[sec, 11:12, ls]).astype(BF)
        return carry

    lax.fori_loop(0, D // LANE, norm, 0, unroll=True)


def fold(value):
    return jnp.sum(value.reshape(ROWS // CELL, CELL, LANE), axis=0)


def front_backward(sec, m, msk, pr, U, T, gfull, xh, rs, sgp, out, sent):
    zero = jnp.zeros((ROWS, LANE), F32)

    def sums(i, carry):
        s1, s2 = carry
        ls = lanes(i)
        dz = T[:, ls]
        xhat = xh[sec, m, :, ls].astype(F32)
        both = xhat * dz
        sgp[sec, 10, :, ls] += fold(both)
        sgp[sec, 11, :, ls] += fold(dz)
        gain = pr[sec, 10:11, ls]
        return s1 + dz * gain, s2 + both * gain

    s1, s2 = lax.fori_loop(0, D // LANE, sums, (zero, zero), unroll=True)
    m1 = jnp.sum(s1, axis=-1, keepdims=True) * (1.0 / D)
    m2 = jnp.sum(s2, axis=-1, keepdims=True) * (1.0 / D)

    def back(i, carry):
        ls = lanes(i)
        xhat = xh[sec, m, :, ls].astype(F32)
        inner = T[:, ls] * pr[sec, 10:11, ls] - m1 - xhat * m2
        gc = gfull(i)[...].astype(F32) + rs[sec, m] * inner
        xh[sec, m, :, ls] = gc.astype(BF)
        gh = halves(gc)
        U[0, 1 : GRID + 1, :, ls] = gh[0]
        U[1, 1 : GRID + 1, :, ls] = gh[1]
        moved = shifts(U[0, :, :, ls], U[1, :, :, ls])
        taps = pr[sec, :, ls]
        mask = halves(msk[m])
        du = []
        for wc in range(SIDE):
            acc = jnp.zeros((GRID, CELL, LANE), F32)
            for a in range(3):
                for b in range(3):
                    tap = 3 * a + b
                    acc = acc + moved[wc][2 - b][2 - a : 2 - a + GRID] * taps[tap : tap + 1, :][None]
            du.append((gh[wc] + mask[wc] * acc).reshape(HALF, LANE))
        out(i)[...] = jnp.concatenate(du, axis=0).astype(BF)
        return carry

    lax.fori_loop(0, D // LANE // 2, back, 0, unroll=True)
    sent(0)
    lax.fori_loop(D // LANE // 2, D // LANE, back, 0, unroll=True)
    sent(1)


def front_sums(sec, m, ubuf, msk, U, xh, sgp):
    def part(i, carry):
        ls = lanes(i)
        gc = xh[sec, m, :, ls].astype(F32)
        sgp[sec, 9, :, ls] += fold(gc)
        gh = halves(gc)
        U[0, 1 : GRID + 1, :, ls] = gh[0]
        U[1, 1 : GRID + 1, :, ls] = gh[1]
        moved = shifts(U[0, :, :, ls], U[1, :, :, ls])
        um = halves(ubuf[sec, m, :, ls].astype(F32) * msk[m])
        for a in range(3):
            for b in range(3):
                kg = jnp.zeros((CELL, LANE), F32)
                for wc in range(SIDE):
                    kg = kg + jnp.sum(moved[wc][2 - b][2 - a : 2 - a + GRID] * um[wc], axis=0)
                sgp[sec, 3 * a + b, :, ls] += kg
        return carry

    lax.fori_loop(0, D // LANE, part, 0)


def spread_heads(value, head_of_lane):
    parts = [jnp.where(head_of_lane == h, value, 0.0) for h in range(PACK)]
    return jnp.concatenate(parts, axis=0).astype(BF)


def gather_heads(value, rows, head_of_lane):
    out = jnp.zeros((rows, GROUP), F32)
    for h in range(PACK):
        out = jnp.where(head_of_lane == h, value[h * rows : (h + 1) * rows], out)
    return out


def unit_slices(unit):
    pair, group = unit // NGROUP, lax.rem(unit, NGROUP)
    rows = [pl.ds(pl.multiple_of((2 * pair + w) * WROWS, 8), WROWS) for w in range(2)]
    cols = [pl.ds(pl.multiple_of(part * D + group * GROUP, LANE), GROUP) for part in range(3)]
    return rows, cols


def window_parts(m, i, qkv):
    rows, cols = unit_slices(i)
    head_of_lane = lax.broadcasted_iota(jnp.int32, (WROWS, GROUP), 1) // HEAD
    q = [qkv[m, r, cols[0]].astype(BF) for r in rows]
    kd = [spread_heads(qkv[m, r, cols[1]], head_of_lane) for r in rows]
    vd = [spread_heads(qkv[m, r, cols[2]], head_of_lane) for r in rows]
    return rows, cols, head_of_lane, q, kd, vd


def window_forward(m, qkv, pw, T, group):
    def unit(i):
        rows, cols, head_of_lane, q, kd, vd = window_parts(m, i, qkv)
        s = [(dot(b, a, 1, 1) * SCALE).reshape(PACK, WROWS, WROWS) for a, b in zip(q, kd)]
        key = lax.broadcasted_iota(jnp.int32, s[0].shape, 1)
        real = lax.rem(key, CELL) < WIN
        s = [jnp.where(real, x, -1e30) for x in s]
        p = [jnp.exp(x - jnp.max(x, axis=1, keepdims=True)) for x in s]
        p = [x * (1.0 / jnp.sum(x, axis=1, keepdims=True)) for x in p]
        p = [x.reshape(PACK * WROWS, WROWS) for x in p]
        for w in range(2):
            pw[m, 2 * i + w, :, 0:WROWS] = p[w]
        out = [dot(x.astype(BF), v, 0, 0) for x, v in zip(p, vd)]
        for w in range(2):
            T[rows[w], cols[0]] = out[w]

    for pair in range(UNITS // 2 // NGROUP):
        unit(pair * NGROUP + group)


def window_backward(m, qkv, pw, T):
    def unit(i, carry):
        rows, cols, head_of_lane, q, kd, vd = window_parts(m, i, qkv)
        g = [T[r, cols[0]].astype(BF) for r in rows]
        p = [pw[m, 2 * i + w, :, 0:WROWS].reshape(PACK, WROWS, WROWS) for w in range(2)]
        dp = [dot(v, x, 1, 1).reshape(PACK, WROWS, WROWS) for v, x in zip(vd, g)]
        ds = [x * (y - jnp.sum(x * y, axis=1, keepdims=True)) for x, y in zip(p, dp)]
        ds = [x.reshape(PACK * WROWS, WROWS).astype(BF) for x in ds]
        pb = [x.reshape(PACK * WROWS, WROWS).astype(BF) for x in p]
        dv = [gather_heads(dot(x, y), WROWS, head_of_lane) for x, y in zip(pb, g)]
        dk = [gather_heads(dot(x, y), WROWS, head_of_lane) * SCALE for x, y in zip(ds, q)]
        dq = [dot(x, y, 0, 0) * SCALE for x, y in zip(ds, kd)]
        for w in range(2):
            qkv[m, rows[w], cols[0]] = dq[w]
            qkv[m, rows[w], cols[1]] = dk[w]
            qkv[m, rows[w], cols[2]] = dv[w]
        return carry

    lax.fori_loop(0, UNITS // 2, unit, 0)


def group_slices(group):
    return [pl.ds(pl.multiple_of(part * D + group * GROUP, LANE), GROUP) for part in range(3)]


def channel_forward(m, qkv, pw, zz, msk):
    def unit(i, carry):
        cols = group_slices(i)
        mask = msk[m][:, :1]
        q = qkv[m, :, cols[0]].astype(BF)
        k = (qkv[m, :, cols[1]] * mask).astype(BF)
        v = qkv[m, :, cols[2]].astype(BF)
        s = dot(q, k, 0, 0) * SCALE
        same = (lax.broadcasted_iota(jnp.int32, s.shape, 0) // HEAD) == (lax.broadcasted_iota(jnp.int32, s.shape, 1) // HEAD)
        s = jnp.where(same, s, -1e30)
        p = jnp.exp(s - jnp.max(s, axis=1, keepdims=True))
        p = p * (1.0 / jnp.sum(p, axis=1, keepdims=True))
        for k in range(GROUP // LANE):
            pw[m, 2 * i + k, 0:GROUP, :] = p[:, k * LANE : (k + 1) * LANE]
        zz[m, 1, :, cols[0]] = dot(v, p.astype(BF), 1, 1).astype(BF)
        return carry

    lax.fori_loop(0, NGROUP, unit, 0, unroll=True)


def channel_backward(m, qkv, pw, T, rr, msk):
    def unit(i, carry):
        cols = group_slices(i)
        mask = msk[m][:, :1]
        q = qkv[m, :, cols[0]].astype(BF)
        k = (qkv[m, :, cols[1]] * mask).astype(BF)
        v = qkv[m, :, cols[2]].astype(BF)
        g = T[:, cols[0]].astype(BF)
        p = jnp.concatenate([pw[m, 2 * i + k, 0:GROUP, :] for k in range(GROUP // LANE)], axis=1)
        dp = dot(g, v, 0, 0)
        ds = (p * (dp - jnp.sum(p * dp, axis=1, keepdims=True))).astype(BF)
        rr[m, 0, :, cols[0]] = (dot(k, ds, 1, 1) * SCALE).astype(BF)
        rr[m, 0, :, cols[1]] = (dot(q, ds) * (SCALE * mask)).astype(BF)
        rr[m, 0, :, cols[2]] = (dot(g, p.astype(BF))).astype(BF)
        return carry

    lax.fori_loop(0, NGROUP, unit, 0, unroll=True)


RING = 8
COLS = FF // RING
WIDE = FF // 12 * 8 // RING
REST = FF // 3 // RING
THIRD = FF // 3 * 2
LENT = RING * 7 // 8
EARLY = 2


def relay_kernel(
    wrows, wcols, img, cot, kern, bias, gain, move, first, second,
    act, ing, out1, out2, outs,
    kern_in, line_in, rows_in, cols_in, isem, wf, w2, pr, msk, flat, ubuf, gin, gout, zz, xh, rs, qkv, ab, rr, pw, U, C, T, sgp, sgs, sgm,
    rL, rR, rA, rG, buf, acc, going, got,
    wl, ws, wr, pl_, usem, gsem, us, gs, ss, rsem, es, er, sgsem, ssem, rcem, osem, sms, smr, xs, xr, ys, yr, bs, br, hs, hr, free,
):
    n = RING
    s = lax.axis_index("section")
    dp = lax.axis_index("dp")
    stage, c = s // 2, lax.rem(s, 2)
    mate = (dp, stage * 2 + (1 - c))
    opposite = (dp, (1 - stage) * 2 + c)
    diagonal = (dp, 3 - s)
    lender, helper = s == 1, s == 2
    early = stage == 0

    spot = lax.rem(dp, n)
    base = dp - spot
    me = jnp.where(lax.rem(spot, 2) == 0, spot // 2, n - 1 - spot // 2)

    def place(pos):
        pos = lax.rem(pos + 2 * n, n)
        return (base + jnp.where(pos < n // 2, 2 * pos, 2 * (n - 1 - pos) + 1), s)

    nexts = (place(me + 1), place(me - 1))
    rounds = n.bit_length() - 1
    partners = []
    for r in range(rounds):
        bit = 1 << r
        partners.append((jnp.where(lax.rem(spot // bit, 2) == 0, dp + bit, dp - bit), s))

    barrier = pltpu.get_barrier_semaphore()
    peers = [mate, opposite, diagonal, *nexts, *partners]
    for peer in peers:
        pl.semaphore_signal(barrier, inc=1, device_id=peer, device_id_type=MESH)
    pl.semaphore_wait(barrier, len(peers))

    def remote(src, dst, send, recv, peer):
        return pltpu.make_async_remote_copy(
            src_ref=src, dst_ref=dst, send_sem=send, recv_sem=recv, device_id=peer, device_id_type=MESH
        )

    half = second.shape[0]

    def group_part(group, part):
        cols = pl.ds(pl.multiple_of(part * D + group * GROUP, LANE), GROUP)
        return first.at[:, cols], wf.at[0, :, cols]

    def wait_group(group):
        for part in range(3):
            src, dst = group_part(group, part)
            i = group * 3 + part

            @pl.when(c == 0)
            def _():
                pltpu.make_async_copy(src, dst, wl.at[i]).wait()

            @pl.when(c == 1)
            def _():
                remote(src, dst, ws.at[i], wr.at[i], mate).wait_recv()

    def weight_parts(k):
        parts = []
        if k == 0:
            for group in range(NGROUP):
                for part in range(3):
                    parts.append(group_part(group, part))
            cols = pl.ds(3 * D, D)
            parts.append((first.at[:, cols], wf.at[k, :, cols]))
        else:
            for i in range(3):
                cols = pl.ds(i * (FF // 3), FF // 3)
                parts.append((first.at[:, cols], wf.at[k, :, cols]))
        third = half // 3
        for i in range(3):
            rows = pl.ds(i * third, third)
            parts.append((second.at[rows, :], w2.at[pl.ds(k * half + i * third, third), :]))
        return parts

    names = (
        [f"qkv{group}" for group in range(NGROUP) for _ in range(3)] + ["out"] + [f"low{i}" for i in range(3)],
        ["in"] * 3 + [f"high{i}" for i in range(3)],
    )

    def weight_copies(k):
        local = [pltpu.make_async_copy(a, b, wl.at[i]) for i, (a, b) in enumerate(weight_parts(k))]
        sent = [remote(a, b, ws.at[i], wr.at[i], mate) for i, (a, b) in enumerate(weight_parts(k))]
        return local, sent

    def params_copy(k):
        return remote(pr.at[k], pr.at[k], ws.at[13], wr.at[13], mate)

    own = flat.at[1]
    small_inputs = [
        pltpu.make_async_copy(a, b, isem.at[i])
        for i, (a, b) in enumerate(
            ((kern, kern_in), (bias, line_in.at[0]), (gain, line_in.at[1]), (move, line_in.at[2]), (wrows, rows_in), (wcols, cols_in))
        )
    ]
    for copy in small_inputs:
        copy.start()
    img_in = pltpu.make_async_copy(img, own, isem.at[6])
    cot_in = pltpu.make_async_copy(cot, own, isem.at[6])

    @pl.when(early)
    def _():
        img_in.start()

    for k in range(2):

        @pl.when(c == k)
        def _():
            local, sent = weight_copies(k)
            for here, there in zip(local, sent):
                here.start()
                there.start()

    for copy in small_inputs:
        copy.wait()
    pr[c, 0:9, :] = kern_in[...].astype(F32)
    for i in range(3):
        pr[c, 9 + i : 10 + i, :] = line_in[i].astype(F32)
    params_copy(c).start()

    def wait_weights(*wanted):
        for k in range(2):

            @pl.when(c == k)
            def _():
                for name, copy in zip(names[k], weight_copies(k)[0]):
                    if name in wanted:
                        copy.wait()
                for name, copy in zip(names[1 - k], weight_copies(1 - k)[1]):
                    if name in wanted:
                        copy.wait_recv()

    def wait_params(k):
        @pl.when(c != k)
        def _():
            params_copy(k).wait_recv()

    raw = flat.at[0]
    img_out = remote(img, raw, pl_.at[0], pl_.at[1], opposite)
    cot_out = remote(cot, raw, pl_.at[0], pl_.at[1], opposite)

    def pad(src, dst):
        blank = jnp.zeros((CELL - WIN, D), F32)
        for r in range(GRID):
            line = src[r].astype(F32)
            for wc in range(SIDE):
                cells = jnp.concatenate([line[wc * WIN : (wc + 1) * WIN], blank], axis=0)
                C[pl.ds(wc * HALF + r * CELL, CELL), :] = cells
        dst[...] = C[...].astype(BF)

    def unpad(dst):
        for r in range(GRID):
            sides = [C[pl.ds(wc * HALF + r * CELL, CELL), :][:WIN] for wc in range(SIDE)]
            dst[r] = jnp.concatenate(sides, axis=0).astype(BF)

    @pl.when(early)
    def _():
        cot_out.start()
        img_in.wait()
        pad(own, ubuf.at[0, 0])

    @pl.when(jnp.logical_not(early))
    def _():
        img_out.start()
        cot_in.start()
        cot_in.wait()
        pad(own, gin.at[1])

    index = lax.broadcasted_iota(jnp.int32, (ROWS, LANE), 0)
    cell = lax.rem(index, CELL)
    row = lax.rem(index, HALF) // CELL
    column = (index // HALF) * WIN + cell
    for m in range(2):
        inside = (row < WIN * rows_in[c + 2 * m]) & (column < WIN * cols_in[c + 2 * m]) & (cell < WIN)
        msk[m] = jnp.where(inside, 1.0, 0.0)

    @pl.when(jnp.logical_not(early))
    def _():
        cot_out.wait_recv()
        pad(raw, gin.at[0])
        for m in range(2):
            for l in range(D // LANE):
                cols = pl.ds(l * LANE, LANE)
                gin[m, :, cols] = (gin[m, :, cols].astype(F32) * msk[m]).astype(BF)

    for wc in range(SIDE):
        U[wc, 0] = jnp.zeros((CELL, D), F32)
        U[wc, GRID + 1] = jnp.zeros((CELL, D), F32)
    sgp[...] = jnp.zeros(sgp.shape, F32)

    def hop(m, dst, send, recv):
        sides = [pl.ds(i * D // 2, D // 2) for i in range(2)]
        return [
            remote(gout.at[m, :, cols], dst.at[:, cols], send.at[m, i], recv.at[m, i], opposite)
            for i, cols in enumerate(sides)
        ]

    def u_hop(m):
        return hop(m, ubuf.at[0, m], us, usem)

    def g_hop(m):
        return hop(m, gin.at[m], gs, gsem)

    def factor_copies(k, m):
        if k == 0:
            parts = [
                ("F", zz.at[m, 0], rL.at[m, 0]),
                ("F", zz.at[m, 1], rL.at[m, 1]),
                ("G", rr.at[m, 0, :, pl.ds(3 * D, D)], rR.at[m, :, pl.ds(3 * D, D)]),
                ("A", rr.at[m, 0, :, pl.ds(0, 3 * D)], rR.at[m, :, pl.ds(0, 3 * D)]),
            ]
        else:
            parts = [
                ("X0", zz.at[m, 2], rL.at[m, 0]),
                ("M", gin.at[m], rG.at[m]),
            ]
            for i, cols in enumerate((pl.ds(0, FF // 3 * 2), pl.ds(FF // 3 * 2, FF // 3))):
                parts.append((f"X{i}", ab.at[m, :, cols], rA.at[m, :, cols]))
                parts.append((f"H{i}", rr.at[m, 1, :, cols], rR.at[m, :, cols]))
        return [(w, remote(a, b, ss.at[m, i], rsem.at[m, i], mate)) for i, (w, a, b) in enumerate(parts)]

    def start_factors(m, which):
        for k in range(2):

            @pl.when(c != k)
            def _():
                for when, copy in factor_copies(k, m):
                    if when == which:
                        copy.start()

    def wait_factors(which):
        for k in range(2):

            @pl.when(c == k)
            def _():
                for m in range(2):
                    for when, copy in factor_copies(k, m):
                        if when[0] in which:
                            copy.wait_recv()

    def shard(k):
        return lax.rem(k + 4 * n, n)

    def sign(h):
        return 1 if h == 0 else -1

    def home(h, t):
        return shard(me + sign(h) - sign(h) * t)

    def products(terms):
        total = None
        for a, b in terms:
            part = dot(a[...], b[...], 0, 0)
            total = part if total is None else total + part
        return total

    def tile(sub, h, j):
        side = pl.ds(h * COLS, COLS)
        if sub in (0, 4):
            rows = first_rows(sub, h)
            last = jnp.where(j >= (3 * n) // 4, 1, 0)
            own = jnp.where(c == 1, 2, last)
            other = jnp.where(c == 1, 0, last)
            cols = lanes(j, COLS)
            terms = [(zz.at[m, own, :, rows], rr.at[m, c, :, cols]) for m in range(2)]
            terms += [(rL.at[m, other, :, rows], rR.at[m, :, cols]) for m in range(2)]
        elif sub == 3:
            cols = [pl.ds(pl.multiple_of(i * LENT * REST + j * REST, LANE), REST) for i in range(2)]
            terms = [(rA.at[m, :, cols[0]], rG.at[m, :, side]) for m in range(2)]
            terms += [(rA.at[m, :, cols[1]], gout.at[m, :, side]) for m in range(2)]
        else:
            cols = lanes(j, WIDE) if sub == 1 else pl.ds(pl.multiple_of(THIRD + j * REST, LANE), REST)
            terms = [(ab.at[m, :, cols], gin.at[m, :, side]) for m in range(2)]
            terms += [(rA.at[m, :, cols], rG.at[m, :, side]) for m in range(2)]
        return products(terms)

    sizes = (COLS // 3 * 2, WIDE, REST, REST, COLS // 3)
    starts = (0, COLS, COLS + WIDE, COLS + WIDE, COLS // 3 * 2)
    parts = [pl.ds(start, size) for start, size in zip(starts, sizes)]
    subs = range(len(sizes))
    odd = c == 1
    active = (None, odd, odd, helper, None)

    def where_live(sub, j, run):
        if sub == 2:
            pl.when(jnp.logical_not(lender) | (j >= LENT))(run)
        elif sub == 3:
            pl.when(j < LENT)(run)
        else:
            run()

    def first_rows(sub, h):
        return pl.ds(h * COLS + (0 if sub == 0 else sizes[0]), sizes[sub])

    def where_active(sub, run):
        if active[sub] is None:
            run()
        else:
            pl.when(active[sub])(run)


    def gathered(sub, h, j):
        if sub in (0, 4):
            return wf.at[0, first_rows(sub, h), lanes(j, COLS)]
        first_row = 0 if sub == 1 else THIRD
        return w2.at[pl.ds(pl.multiple_of(first_row + j * sizes[sub], 16), sizes[sub]), pl.ds(h * COLS, COLS)]

    def scatter(h, t, sub):
        src, dst = buf.at[h, t, parts[sub], :], buf.at[h, t + 1, parts[sub], :]
        return remote(src, dst, ssem.at[h, t, sub], rcem.at[h, t + 1, sub], nexts[h])

    def spread(h, t, sub, j):
        ref = gathered(sub, h, j)
        return remote(ref, ref, ssem.at[h, n - 1 + t, sub], rcem.at[h, n + t, sub], nexts[h])

    half_shards = n * 3 // 4

    def write(h, j, sub):
        src, side = gathered(sub, h, j), pl.ds(h * COLS, COLS)
        if sub in (0, 4):
            dst = out1.at[first_rows(sub, h), lanes(j, COLS)]
        elif sub == 1:
            dst = out2.at[pl.ds(pl.multiple_of((j - half_shards) * WIDE, 16), WIDE), side]
        else:
            dst = out2.at[pl.ds(pl.multiple_of(THIRD - FF // 2 + j * REST, 16), REST), side]
        if sub == 3:
            return remote(src, dst, bs.at[h, j], br.at[h, j], diagonal)
        return pltpu.make_async_copy(src, dst, osem.at[h, j, sub])

    def hand_over(h, j):
        dst = out2.at[pl.ds(pl.multiple_of(j * WIDE, 16), WIDE), pl.ds(h * COLS, COLS)]
        return remote(gathered(1, h, j), dst, hs.at[h, j], hr.at[h, j], mate)

    def deliver(h, j, sub):
        if sub == 1:

            @pl.when(j < half_shards)
            def _():
                hand_over(h, j).start()

            @pl.when(j >= half_shards)
            def _():
                write(h, j, sub).start()

        else:
            write(h, j, sub).start()

    def lend(m):
        cols, there = pl.ds(THIRD, LENT * REST), [rA.at[m, :, pl.ds(i * LENT * REST, LENT * REST)] for i in range(2)]
        return (
            remote(ab.at[m, :, cols], there[0], xs.at[m], xr.at[m], diagonal),
            remote(rA.at[m, :, cols], there[1], xs.at[2 + m], xr.at[2 + m], diagonal),
        )

    def share(m):
        return remote(gout.at[m], rG.at[m], ys.at[m], yr.at[m], mate)

    def reduce_event(sub, h, e):
        j = shard(me - sign(h) * e)

        @pl.when(e == n - 1)
        def _():
            pl.semaphore_wait(free.at[h, sub], 1)

        def run():
            total = tile(sub, h, j)

            @pl.when(e == 0)
            def _():
                buf[h, 0, parts[sub], :] = total.astype(BF)
                scatter(h, 0, sub).start()

            @pl.when((e > 0) & (e < n - 1))
            def _():
                scatter(h, e - 1, sub).wait_recv()
                buf[h, e, parts[sub], :] = (total + buf[h, e, parts[sub], :].astype(F32)).astype(BF)
                scatter(h, e, sub).start()

            @pl.when(e == n - 1)
            def _():
                scatter(h, n - 2, sub).wait_recv()
                gathered(sub, h, j)[...] = (total + buf[h, n - 1, parts[sub], :].astype(F32)).astype(BF)
                spread(h, 0, sub, j).start()
                deliver(h, j, sub)

        where_live(sub, j, run)

    def event(sub, e):
        for h in range(2):

            @pl.when(e < n)
            def _():
                reduce_event(sub, h, e)

            @pl.when((e >= n) & (e < 2 * n - 1))
            def _():
                t = e - (n - 1)
                j = home(h, t)

                def run():
                    spread(h, t - 1, sub, j).wait_recv()

                    @pl.when(t < n - 1)
                    def _():
                        spread(h, t, sub, j).start()

                    deliver(h, j, sub)

                where_live(sub, j, run)

    def settle(sub, e):
        for h in range(2):

            @pl.when((e >= 0) & (e < n - 1))
            def _():
                where_live(sub, shard(me - sign(h) * e), lambda: scatter(h, e, sub).wait_send())

            @pl.when((e >= n - 1) & (e < 2 * n - 1))
            def _():
                t = e - (n - 1)
                j = home(h, t)

                def run():
                    @pl.when(t < n - 1)
                    def _():
                        spread(h, t, sub, j).wait_send()

                    if sub == 1:

                        @pl.when(j < half_shards)
                        def _():
                            hand_over(h, j).wait_send()

                        @pl.when(j >= half_shards)
                        def _():
                            write(h, j, sub).wait()

                    elif sub == 3:
                        write(h, j, sub).wait_send()
                    else:
                        write(h, j, sub).wait()

                where_live(sub, j, run)

    def early_event(e, which):
        @pl.when(odd)
        def _():
            for sub in which:
                where_active(sub, lambda: event(sub, e))

    def small(r):
        return remote(going.at[r], got.at[r], sms.at[r], smr.at[r], partners[r])

    def mlp(m, order, wait):
        total, before, last = C[...], None, None
        for t in order:
            cols = pl.ds(t * FTILE, FTILE)
            h = dot(zz[m, 2], wf[1, :, cols])
            if last is not None:
                wait(last)
                total = total + dot(before, w2[pl.ds(last * FTILE, FTILE), :])
            a, d = gelu_parts(h)
            before, last = a.astype(BF), t
            ab[m, :, cols] = before
            rr[m, 1, :, cols] = d.astype(BF)
            if t == FF // FTILE * 2 // 3 - 1 and order == range(FF // FTILE):
                start_factors(m, "X0")
        wait(last)
        for i in range(2):
            cols = pl.ds(i * D // 2, D // 2)
            part = total[:, i * D // 2 : (i + 1) * D // 2]
            gout[jnp.where(early, m, 2 + m), :, cols] = (part + dot(before, w2[pl.ds(last * FTILE, FTILE), cols])).astype(BF)

            @pl.when(early)
            def _():
                u_hop(m)[i].start()

    def give_results(m):
        @pl.when(early)
        def _():
            C[...] = gout[m].astype(F32)

        @pl.when(jnp.logical_not(early))
        def _():
            for l in range(D // LANE):
                cols = pl.ds(l * LANE, LANE)
                C[:, cols] = gout[2 + m, :, cols].astype(F32) * msk[m]

        unpad(flat.at[m])

        @pl.when(early & (m == 0))
        def _():
            pltpu.make_async_copy(flat.at[0], ing, es.at[1]).start()

        @pl.when(early & (m == 1))
        def _():
            remote(flat.at[1], ing, es.at[1], er.at[1], opposite).start()

        @pl.when(jnp.logical_not(early) & (m == 0))
        def _():
            remote(flat.at[0], act, es.at[0], er.at[0], opposite).start()

        @pl.when(jnp.logical_not(early) & (m == 1))
        def _():
            pltpu.make_async_copy(flat.at[1], act, es.at[0]).start()

    def forward(m, p):
        @pl.when(jnp.logical_not(early))
        def _():
            for copy in u_hop(m):
                copy.wait_recv()

        @pl.when(early & (m == 1))
        def _():
            img_out.wait_recv()
            pad(raw, ubuf.at[0, 1])

        once = p == 0
        starting = early & once

        @pl.when(once)
        def _():
            wait_params(0)

        @pl.when(once & jnp.logical_not(early))
        def _():
            wait_params(1)
            wait_weights(*set(names[0] + names[1]))

        front_forward(0, m, ubuf, msk, pr, U, C, zz, xh, rs)

        @pl.when(early)
        def _():
            def head_group(group, carry):
                @pl.when(once)
                def _():
                    wait_group(group)

                for part in range(3):
                    cols = pl.ds(pl.multiple_of(part * D + group * GROUP, LANE), GROUP)
                    qkv[m, :, cols] = dot(zz[m, 0], wf[0, :, cols])
                window_forward(m, qkv, pw, T, group)
                return carry

            lax.fori_loop(0, NGROUP, head_group, 0)
            zz[m, 1] = T[...].astype(BF)

        @pl.when(starting)
        def _():
            wait_weights("out")
            wait_params(1)

        @pl.when(jnp.logical_not(early))
        def _():
            qkv[m] = dot(zz[m, 0], wf[0, :, pl.ds(0, 3 * D)])

        @pl.when(jnp.logical_not(early))
        def _():
            channel_forward(m, qkv, pw, zz, msk)

        ubuf[1, m] = (C[...] + dot(zz[m, 1], wf[0, :, pl.ds(3 * D, D)])).astype(BF)

        front_forward(1, m, ubuf, msk, pr, U, C, zz, xh, rs)

        @pl.when(starting)
        def _():
            wait_weights("in")
            order = [i + 3 * k for i in range(3) for k in range(2)]
            mlp(m, order, lambda t: wait_weights(f"low{t}" if t < 3 else f"high{t - 3}"))
            start_factors(m, "X0")

        @pl.when(jnp.logical_not(starting))
        def _():
            mlp(m, range(FF // FTILE), lambda t: None)

        start_factors(m, "F")
        start_factors(m, "X1")

        @pl.when(early & (m == 1))
        def _():
            wait_factors("FX")

        @pl.when(lender & (m == 1))
        def _():
            for i in range(2):
                for copy in lend(i):
                    copy.start()

    def backward(m):
        @pl.when(early)
        def _():
            for copy in g_hop(m):
                copy.wait_recv()
            start_factors(m, "M")

        for t in range(FF // FTILE):
            cols = pl.ds(t * FTILE, FTILE)
            da = dot(gin[m], w2[cols, :], 1, 1)
            rr[m, 1, :, cols] = (da * rr[m, 1, :, cols].astype(F32)).astype(BF)
            if t == FF // FTILE * 2 // 3 - 1:
                start_factors(m, "H0")

        start_factors(m, "H1")

        @pl.when(m == 1)
        def _():
            @pl.when(jnp.logical_not(early))
            def _():
                wait_factors("FX")

            wait_factors("M")
            early_event(0, (1, 2))

        T[...] = dot(rr[m, 1], wf[1], 1, 1)

        @pl.when(m == 1)
        def _():
            wait_factors("H")
            early_event(0, (0, 4))

        last = pl.ds(3 * D, D)

        @pl.when(early)
        def _():
            for copy in u_hop(m):
                copy.wait_send()

        def tail_lanes(i):
            return rr.at[m, 0, :, pl.ds(pl.multiple_of(3 * D + i * LANE, LANE), LANE)]

        def nothing(half):
            pass

        front_backward(1, m, msk, pr, U, T, lambda i: gin.at[m, :, lanes(i)], xh, rs, sgp, tail_lanes, nothing)

        start_factors(m, "G")
        T[...] = dot(rr[m, 0, :, last], wf[0, :, last], 1, 1)

        @pl.when(early)
        def _():
            window_backward(m, qkv, pw, T)
            for i in range(3):
                cols = pl.ds(i * D, D)
                rr[m, 0, :, cols] = qkv[m, :, cols].astype(BF)

        @pl.when(jnp.logical_not(early))
        def _():
            channel_backward(m, qkv, pw, T, rr, msk)

        start_factors(m, "A")

        @pl.when(m == 1)
        def _():
            early_event(1, (1, 2, 0, 4))

        T[...] = dot(rr[m, 0, :, pl.ds(0, 3 * D)], wf[0, :, pl.ds(0, 3 * D)], 1, 1)
        def send_half(half):
            @pl.when(jnp.logical_not(early))
            def _():
                g_hop(m)[half].start()

        front_backward(
            0, m, msk, pr, U, T, tail_lanes, xh, rs, sgp, lambda i: gout.at[m, :, lanes(i)], send_half
        )

        @pl.when(s == 3)
        def _():
            share(m).start()

    @pl.when(jnp.logical_not(early))
    def _():
        for m in range(2):
            start_factors(m, "M")

    def phase(p, carry):
        m = jnp.where(early, lax.rem(p, 2), p // 2)
        ahead = jnp.where(early, p < 2, lax.rem(p, 2) == 0)

        @pl.when(ahead)
        def _():
            forward(m, p)

        @pl.when(jnp.logical_not(ahead))
        def _():
            backward(m)

        return carry

    lax.fori_loop(0, 4, phase, 0)

    for h in range(2):
        for sub in subs:

            def ready():
                pl.semaphore_signal(free.at[h, sub], inc=1, device_id=nexts[1 - h], device_id_type=MESH)

            where_active(sub, ready)

    give = remote(sgs.at[1 - c], sgm, sgsem.at[0], sgsem.at[1], mate)

    def small_sums():
        for sec in range(2):
            for j in range(12):
                sgs[sec, j : j + 1, :] = jnp.sum(sgp[sec, j], axis=0, keepdims=True)
            sgs[sec, 12:16, :] = jnp.zeros((4, D), F32)
        give.start()

    wait_factors("GA")

    @pl.when(helper)
    def _():
        for m in range(2):
            for copy in lend(m):
                copy.wait_recv()
            share(m).wait_recv()

    def sent_before():
        for k in range(2):

            @pl.when(c == k)
            def _():
                for copy in weight_copies(k)[1]:
                    copy.wait_send()
                params_copy(k).wait_send()
                for m in range(2):
                    for _when, copy in factor_copies(1 - k, m):
                        copy.wait_send()

    def ring_step(t, carry):
        for sub in (0, 4, 1, 2, 3):
            e = t + (jnp.where(odd, EARLY, 0) if sub in (0, 4) else 0 if sub == 3 else EARLY)

            def both():
                event(sub, e)
                settle(sub, e - 2)

            where_active(sub, both)

        @pl.when((t >= 1) & (t < 5))
        def _():
            front_sums((t - 1) // 2, lax.rem(t - 1, 2), ubuf, msk, U, xh, sgp)

        pl.when(t == 5)(small_sums)
        pl.when(t == 8)(sent_before)

        @pl.when((t >= 6) & (t < 8))
        def _():
            give_results(t - 6)

        for r in range(rounds + 1):

            @pl.when(t == 6 + 2 * r)
            def _():
                if r == 0:
                    give.wait_recv()
                    acc[0] = sgs[c] + sgm[...]
                else:
                    small(r - 1).wait_recv()
                    acc[r] = going[r - 1].astype(F32) + got[r - 1].astype(F32)
                if r < rounds:
                    going[r] = acc[r].astype(BF)
                    small(r).start()

        return carry

    lax.fori_loop(0, 2 * n + 1, ring_step, 0)
    outs[...] = acc[rounds]
    give.wait_send()
    for r in range(rounds):
        small(r).wait_send()


    def received(j, carry):
        for h in range(2):

            @pl.when(jnp.logical_not(odd) & (j < half_shards))
            def _():
                hand_over(h, j).wait_recv()

            @pl.when(lender & (j < LENT))
            def _():
                write(h, j, 3).wait_recv()

        return carry

    lax.fori_loop(0, n, received, 0)

    @pl.when(lender)
    def _():
        for m in range(2):
            for copy in lend(m):
                copy.wait_send()

    @pl.when(s == 3)
    def _():
        for m in range(2):
            share(m).wait_send()

    @pl.when(early)
    def _():
        cot_out.wait_send()
        pltpu.make_async_copy(flat.at[0], ing, es.at[1]).wait()
        remote(flat.at[1], ing, es.at[1], er.at[1], opposite).wait_send()
        remote(flat.at[0], act, es.at[0], er.at[0], opposite).wait_recv()

    @pl.when(jnp.logical_not(early))
    def _():
        img_out.wait_send()
        for m in range(2):
            for copy in g_hop(m):
                copy.wait_send()
        remote(flat.at[0], act, es.at[0], er.at[0], opposite).wait_send()
        pltpu.make_async_copy(flat.at[1], act, es.at[0]).wait()
        remote(flat.at[1], ing, es.at[1], er.at[1], opposite).wait_recv()


def relay(wrows, wcols, img, cot, kern, bias, gain, move, first, second):
    shape = jax.ShapeDtypeStruct
    vmem = pl.BlockSpec(memory_space=pltpu.VMEM)
    anywhere = pl.BlockSpec(memory_space=pl.ANY)
    dma = pltpu.SemaphoreType.DMA
    image = (ROWS, D)
    slot = img.shape
    rounds = RING.bit_length() - 1
    return pl.pallas_call(
        relay_kernel,
        out_shape=[
            shape(slot, BF),
            shape(slot, BF),
            shape((D, FF), BF),
            shape((FF // 2, D), BF),
            shape((16, D), F32),
        ],
        in_specs=[anywhere] * 10,
        out_specs=[anywhere] * 4 + [vmem],
        scratch_shapes=[
            pltpu.VMEM(kern.shape, BF),
            pltpu.VMEM((3,) + bias.shape, BF),
            pltpu.SMEM(wrows.shape, jnp.int32),
            pltpu.SMEM(wcols.shape, jnp.int32),
            dma((7,)),
            pltpu.VMEM((2, D, FF), BF),
            pltpu.VMEM((FF, D), BF),
            pltpu.VMEM((2, 16, D), F32),
            pltpu.VMEM((2, ROWS, LANE), F32),
            pltpu.VMEM((2,) + slot, BF),
            pltpu.VMEM((2, 2) + image, BF),
            pltpu.VMEM((2,) + image, BF),
            pltpu.VMEM((4,) + image, BF),
            pltpu.VMEM((2, 3) + image, BF),
            pltpu.VMEM((2, 2) + image, BF),
            pltpu.VMEM((2, 2, ROWS, LANE), F32),
            pltpu.VMEM((2, ROWS, 3 * D), F32),
            pltpu.VMEM((2, ROWS, FF), BF),
            pltpu.VMEM((2, 2, ROWS, FF), BF),
            pltpu.VMEM((2, UNITS, PACK * WROWS, LANE), F32),
            pltpu.VMEM((SIDE, GRID + 2, CELL, D), F32),
            pltpu.VMEM(image, F32),
            pltpu.VMEM(image, F32),
            pltpu.VMEM((2, 12, CELL, D), F32),
            pltpu.VMEM((2, 16, D), F32),
            pltpu.VMEM((16, D), F32),
            pltpu.VMEM((2, 2) + image, BF),
            pltpu.VMEM((2, ROWS, FF), BF),
            pltpu.VMEM((2, ROWS, FF), BF),
            pltpu.VMEM((2,) + image, BF),
            pltpu.VMEM((2, RING, COLS + WIDE + REST, COLS), BF),
            pltpu.VMEM((rounds + 1, 16, D), F32),
            pltpu.VMEM((rounds, 16, D), BF),
            pltpu.VMEM((rounds, 16, D), BF),
            dma((14,)),
            dma((14,)),
            dma((14,)),
            dma((2,)),
            dma((2, 2)),
            dma((2, 2)),
            dma((2, 2)),
            dma((2, 2)),
            dma((2, 8)),
            dma((2, 8)),
            dma((2,)),
            dma((2,)),
            dma((2,)),
            dma((2, 2 * RING, 5)),
            dma((2, 2 * RING, 5)),
            dma((2, RING, 5)),
            dma((rounds,)),
            dma((rounds,)),
            dma((4,)),
            dma((4,)),
            dma((2,)),
            dma((2,)),
            dma((2, RING)),
            dma((2, RING)),
            dma((2, RING)),
            dma((2, RING)),
            pltpu.SemaphoreType.REGULAR((2, 5)),
        ],
        name="relay",
        compiler_params=pltpu.CompilerParams(
            collective_id=1, has_side_effects=True, vmem_limit_bytes=63 * 2**20
        ),
    )(wrows, wcols, img, cot, kern, bias, gain, move, first, second)


def finish_kernel(
    out1, out2, act, ing, outs, first, second, acts, ings, kern, bias, gain, move,
    raw1, raw2, full1, full2, acted, graded, wide, small, kernels, rsem, wsem,
):
    steps = rsem.shape[0] - 3

    loads = [
        pltpu.make_async_copy(act, acted, rsem.at[steps]),
        pltpu.make_async_copy(ing, graded, rsem.at[steps + 1]),
        pltpu.make_async_copy(outs, small, rsem.at[steps + 2]),
    ]
    for copy in loads:
        copy.start()
    reads, writes = [], []
    for i in range(steps):
        pair = ((out1, raw1, full1, first), (out2, raw2, full2, second))[i % 2]
        src, raw, full, dst = pair
        half = steps // 2
        rows = pl.ds(i // 2 * (src.shape[0] // half), src.shape[0] // half)
        reads.append((pltpu.make_async_copy(src.at[rows, :], raw.at[rows, :], rsem.at[i]), raw, full, rows))
        writes.append(pltpu.make_async_copy(full.at[rows, :], dst.at[rows, :], wsem.at[i]))
    for copy, *_ in reads:
        copy.start()
    for (copy, raw, full, rows), back in zip(reads, writes):
        copy.wait()
        full[rows, :] = raw[rows, :].astype(F32)
        back.start()
    for copy in loads:
        copy.wait()
    for k in range(9):
        kernels[k] = small[k : k + 1, :]
    for r in range(GRID):
        line = graded[r].astype(F32)
        for k in range(GRID):
            wide[r, k] = line[k : k + 1, :]
    last = [
        pltpu.make_async_copy(acted, acts, wsem.at[steps]),
        pltpu.make_async_copy(wide, ings, wsem.at[steps + 1]),
        pltpu.make_async_copy(kernels, kern, wsem.at[steps + 2]),
    ]
    for i, dst in enumerate((bias, gain, move)):
        last.append(pltpu.make_async_copy(small.at[pl.ds(9 + i, 1), :], dst, wsem.at[steps + 3 + i]))
    for copy in last:
        copy.start()
    for copy in writes + last:
        copy.wait()


def finish(out1, out2, act, ing, outs):
    shape = jax.ShapeDtypeStruct
    slot = act.shape
    anywhere = pl.BlockSpec(memory_space=pl.ANY)
    line = (1, D)
    spread = slot[:2] + line
    steps = 16
    return pl.pallas_call(
        finish_kernel,
        out_shape=[
            shape(out1.shape, F32),
            shape(out2.shape, F32),
            shape(slot, BF),
            shape(spread, F32),
            shape((9,) + line, F32),
            shape(line, F32),
            shape(line, F32),
            shape(line, F32),
        ],
        in_specs=[anywhere] * 5,
        out_specs=[anywhere] * 8,
        scratch_shapes=[
            pltpu.VMEM(out1.shape, out1.dtype),
            pltpu.VMEM(out2.shape, out2.dtype),
            pltpu.VMEM(out1.shape, F32),
            pltpu.VMEM(out2.shape, F32),
            pltpu.VMEM(slot, BF),
            pltpu.VMEM(slot, BF),
            pltpu.VMEM(spread, F32),
            pltpu.VMEM(outs.shape, F32),
            pltpu.VMEM((9,) + line, F32),
            pltpu.SemaphoreType.DMA((steps + 3,)),
            pltpu.SemaphoreType.DMA((steps + 6,)),
        ],
        name="finish",
        compiler_params=pltpu.CompilerParams(vmem_limit_bytes=60 * 2**20),
    )(out1, out2, act, ing, outs)


def per_device(
    images, cotangent, window_rows, window_cols, pos_kernel, pos_bias, norm_gain, norm_shift, first_weight, second_weight
):
    act, ing, out1, out2, outs = relay(
        window_rows, window_cols, images[0], cotangent[0], pos_kernel[0], pos_bias, norm_gain, norm_shift,
        first_weight[0], second_weight,
    )
    if lax.axis_size("dp") > RING:
        out1, out2, outs = lax.psum((out1.astype(F32) / RING, out2.astype(F32) / RING, outs / RING), "dp")
    out1, out2, act, ing, kern, bias, gain, move = finish(out1, out2, act, ing, outs)
    return (
        act[None],
        ing.transpose(2, 0, 1, 3),
        out1[None],
        out2,
        kern.transpose(1, 0, 2),
        bias,
        gain,
        move,
    )


def solution(mesh):
    in_specs = (
        P(("dp", "section"), None, None, None),
        P(("dp", "section"), None, None, None),
        P("dp"),
        P("dp"),
        P("section", None, None),
        P("section", None),
        P("section", None),
        P("section", None),
        P("section", None, None),
        P("section", None),
    )
    out_specs = (
        P(("dp", "section"), None, None, None),
        P(("dp", "section"), None, None, None),
        P("section", None, None),
        P("section", None),
        P("section", None, None),
        P("section", None),
        P("section", None),
        P("section", None),
    )
    return jax.shard_map(per_device, mesh=mesh, in_specs=in_specs, out_specs=out_specs, check_vma=False)
```

```python
from functools import partial

import jax
import jax.numpy as jnp
from jax import lax
from jax.experimental import pallas as pl
from jax.experimental.pallas import tpu as pltpu
from jax.sharding import PartitionSpec as P

D = 768
FF = 3072
HEADS = 24
HEAD = 32
WIN = 7
SIDE = 2
GRID = SIDE * WIN
CELL = 8
WROWS = WIN * CELL
HALF = GRID * CELL
ROWS = SIDE * HALF
GROUP = 256
PACK = GROUP // HEAD
NGROUP = D // GROUP
UNITS = NGROUP * SIDE * SIDE
LANE = 128
FTILE = 512
EPS = 1e-05
SCALE = HEAD ** (-0.5)
BF = jnp.bfloat16
F32 = jnp.float32
MESH = pl.DeviceIdType.MESH


def dot(a, b, ca=1, cb=0):
    return lax.dot_general(a, b, (((ca,), (cb,)), ((), ())), preferred_element_type=F32)


def lanes(index, width=LANE):
    return pl.ds(pl.multiple_of(index * width, width), width)


def halves(value):
    return value.reshape(SIDE, GRID, CELL, value.shape[-1])


def shifts(left, right):
    column = lax.broadcasted_iota(jnp.int32, left.shape, 1)
    before0 = pltpu.roll(left, 1, 1)
    after0 = jnp.where(column == WIN - 1, pltpu.roll(right, CELL - 2, 1), pltpu.roll(left, CELL - 1, 1))
    before1 = jnp.where(column == 0, pltpu.roll(left, 2, 1), pltpu.roll(right, 1, 1))
    after1 = pltpu.roll(right, CELL - 1, 1)
    return ((before0, left, after0), (before1, right, after1))


def gelu_parts(h):
    expo = jnp.exp(h * h * -0.5)
    t = 1.0 / (1.0 + (0.3275911 * 0.7071067811865476) * jnp.abs(h))
    poly = t * (0.127414796 + t * (-0.142248368 + t * (0.7107068705 + t * (-0.7265760135 + t * 0.5307027145))))
    tail = poly * expo
    phi = jnp.where(h >= 0, 1.0 - tail, tail)
    return h * phi, phi + h * expo * 0.3989422804014327


def front_forward(sec, m, ubuf, msk, pr, U, C, zz, xh, rs):
    zero = jnp.zeros((ROWS, LANE), F32)

    def conv(i, total):
        ls = lanes(i)
        u = ubuf[sec, m, :, ls].astype(F32)
        masked = halves(u * msk[m])
        U[0, 1 : GRID + 1, :, ls] = masked[0]
        U[1, 1 : GRID + 1, :, ls] = masked[1]
        moved = shifts(U[0, :, :, ls], U[1, :, :, ls])
        taps = pr[sec, :, ls]
        uh = halves(u)
        sums = []
        for wc in range(SIDE):
            acc = uh[wc] + taps[9:10, :][None]
            for a in range(3):
                for b in range(3):
                    acc = acc + moved[wc][b][a : a + GRID] * taps[3 * a + b : 3 * a + b + 1, :][None]
            acc = acc.reshape(HALF, LANE)
            C[pl.ds(wc * HALF, HALF), ls] = acc
            sums.append(acc)
        return total + jnp.concatenate(sums, axis=0)

    mean = jnp.sum(lax.fori_loop(0, D // LANE, conv, zero, unroll=True), axis=-1, keepdims=True) * (1.0 / D)

    def spread(i, total):
        centred = C[:, lanes(i)] - mean
        return total + centred * centred

    var = jnp.sum(lax.fori_loop(0, D // LANE, spread, zero, unroll=True), axis=-1, keepdims=True) * (1.0 / D)
    rstd = lax.rsqrt(var + EPS)
    rs[sec, m] = jnp.broadcast_to(rstd, (ROWS, LANE))

    def norm(i, carry):
        ls = lanes(i)
        xhat = (C[:, ls] - mean) * rstd
        xh[sec, m, :, ls] = xhat.astype(BF)
        zz[m, 2 * sec, :, ls] = (xhat * pr[sec, 10:11, ls] + pr[sec, 11:12, ls]).astype(BF)
        return carry

    lax.fori_loop(0, D // LANE, norm, 0, unroll=True)


def fold(value):
    return jnp.sum(value.reshape(ROWS // CELL, CELL, LANE), axis=0)


def front_backward(sec, m, msk, pr, U, T, gfull, xh, rs, sgp, out, sent):
    zero = jnp.zeros((ROWS, LANE), F32)

    def sums(i, carry):
        s1, s2 = carry
        ls = lanes(i)
        dz = T[:, ls]
        xhat = xh[sec, m, :, ls].astype(F32)
        both = xhat * dz
        sgp[sec, 10, :, ls] += fold(both)
        sgp[sec, 11, :, ls] += fold(dz)
        gain = pr[sec, 10:11, ls]
        return s1 + dz * gain, s2 + both * gain

    s1, s2 = lax.fori_loop(0, D // LANE, sums, (zero, zero), unroll=True)
    m1 = jnp.sum(s1, axis=-1, keepdims=True) * (1.0 / D)
    m2 = jnp.sum(s2, axis=-1, keepdims=True) * (1.0 / D)

    def back(i, carry):
        ls = lanes(i)
        xhat = xh[sec, m, :, ls].astype(F32)
        inner = T[:, ls] * pr[sec, 10:11, ls] - m1 - xhat * m2
        gc = gfull(i)[...].astype(F32) + rs[sec, m] * inner
        xh[sec, m, :, ls] = gc.astype(BF)
        gh = halves(gc)
        U[0, 1 : GRID + 1, :, ls] = gh[0]
        U[1, 1 : GRID + 1, :, ls] = gh[1]
        moved = shifts(U[0, :, :, ls], U[1, :, :, ls])
        taps = pr[sec, :, ls]
        mask = halves(msk[m])
        du = []
        for wc in range(SIDE):
            acc = jnp.zeros((GRID, CELL, LANE), F32)
            for a in range(3):
                for b in range(3):
                    tap = 3 * a + b
                    acc = acc + moved[wc][2 - b][2 - a : 2 - a + GRID] * taps[tap : tap + 1, :][None]
            du.append((gh[wc] + mask[wc] * acc).reshape(HALF, LANE))
        out(i)[...] = jnp.concatenate(du, axis=0).astype(BF)
        return carry

    lax.fori_loop(0, D // LANE // 2, back, 0, unroll=True)
    sent(0)
    lax.fori_loop(D // LANE // 2, D // LANE, back, 0, unroll=True)
    sent(1)


def front_sums(sec, m, ubuf, msk, U, xh, sgp):
    def part(i, carry):
        ls = lanes(i)
        gc = xh[sec, m, :, ls].astype(F32)
        sgp[sec, 9, :, ls] += fold(gc)
        gh = halves(gc)
        U[0, 1 : GRID + 1, :, ls] = gh[0]
        U[1, 1 : GRID + 1, :, ls] = gh[1]
        moved = shifts(U[0, :, :, ls], U[1, :, :, ls])
        um = halves(ubuf[sec, m, :, ls].astype(F32) * msk[m])
        for a in range(3):
            for b in range(3):
                kg = jnp.zeros((CELL, LANE), F32)
                for wc in range(SIDE):
                    kg = kg + jnp.sum(moved[wc][2 - b][2 - a : 2 - a + GRID] * um[wc], axis=0)
                sgp[sec, 3 * a + b, :, ls] += kg
        return carry

    lax.fori_loop(0, D // LANE, part, 0)


def spread_heads(value, head_of_lane):
    parts = [jnp.where(head_of_lane == h, value, 0.0) for h in range(PACK)]
    return jnp.concatenate(parts, axis=0).astype(BF)


def gather_heads(value, rows, head_of_lane):
    out = jnp.zeros((rows, GROUP), F32)
    for h in range(PACK):
        out = jnp.where(head_of_lane == h, value[h * rows : (h + 1) * rows], out)
    return out


def unit_slices(unit):
    pair, group = unit // NGROUP, lax.rem(unit, NGROUP)
    rows = [pl.ds(pl.multiple_of((2 * pair + w) * WROWS, 8), WROWS) for w in range(2)]
    cols = [pl.ds(pl.multiple_of(part * D + group * GROUP, LANE), GROUP) for part in range(3)]
    return rows, cols


def window_parts(m, i, qkv):
    rows, cols = unit_slices(i)
    head_of_lane = lax.broadcasted_iota(jnp.int32, (WROWS, GROUP), 1) // HEAD
    q = [qkv[m, r, cols[0]].astype(BF) for r in rows]
    kd = [spread_heads(qkv[m, r, cols[1]], head_of_lane) for r in rows]
    vd = [spread_heads(qkv[m, r, cols[2]], head_of_lane) for r in rows]
    return rows, cols, head_of_lane, q, kd, vd


def window_forward(m, qkv, pw, T, group):
    def unit(i):
        rows, cols, head_of_lane, q, kd, vd = window_parts(m, i, qkv)
        s = [(dot(b, a, 1, 1) * SCALE).reshape(PACK, WROWS, WROWS) for a, b in zip(q, kd)]
        key = lax.broadcasted_iota(jnp.int32, s[0].shape, 1)
        real = lax.rem(key, CELL) < WIN
        s = [jnp.where(real, x, -1e30) for x in s]
        p = [jnp.exp(x - jnp.max(x, axis=1, keepdims=True)) for x in s]
        p = [x * (1.0 / jnp.sum(x, axis=1, keepdims=True)) for x in p]
        p = [x.reshape(PACK * WROWS, WROWS) for x in p]
        for w in range(2):
            pw[m, 2 * i + w, :, 0:WROWS] = p[w]
        out = [dot(x.astype(BF), v, 0, 0) for x, v in zip(p, vd)]
        for w in range(2):
            T[rows[w], cols[0]] = out[w]

    for pair in range(UNITS // 2 // NGROUP):
        unit(pair * NGROUP + group)


def window_backward(m, qkv, pw, T):
    def unit(i, carry):
        rows, cols, head_of_lane, q, kd, vd = window_parts(m, i, qkv)
        g = [T[r, cols[0]].astype(BF) for r in rows]
        p = [pw[m, 2 * i + w, :, 0:WROWS].reshape(PACK, WROWS, WROWS) for w in range(2)]
        dp = [dot(v, x, 1, 1).reshape(PACK, WROWS, WROWS) for v, x in zip(vd, g)]
        ds = [x * (y - jnp.sum(x * y, axis=1, keepdims=True)) for x, y in zip(p, dp)]
        ds = [x.reshape(PACK * WROWS, WROWS).astype(BF) for x in ds]
        pb = [x.reshape(PACK * WROWS, WROWS).astype(BF) for x in p]
        dv = [gather_heads(dot(x, y), WROWS, head_of_lane) for x, y in zip(pb, g)]
        dk = [gather_heads(dot(x, y), WROWS, head_of_lane) * SCALE for x, y in zip(ds, q)]
        dq = [dot(x, y, 0, 0) * SCALE for x, y in zip(ds, kd)]
        for w in range(2):
            qkv[m, rows[w], cols[0]] = dq[w]
            qkv[m, rows[w], cols[1]] = dk[w]
            qkv[m, rows[w], cols[2]] = dv[w]
        return carry

    lax.fori_loop(0, UNITS // 2, unit, 0)


def group_slices(group):
    return [pl.ds(pl.multiple_of(part * D + group * GROUP, LANE), GROUP) for part in range(3)]


def channel_forward(m, qkv, pw, zz, msk):
    def unit(i, carry):
        cols = group_slices(i)
        mask = msk[m][:, :1]
        q = qkv[m, :, cols[0]].astype(BF)
        k = (qkv[m, :, cols[1]] * mask).astype(BF)
        v = qkv[m, :, cols[2]].astype(BF)
        s = dot(q, k, 0, 0) * SCALE
        same = (lax.broadcasted_iota(jnp.int32, s.shape, 0) // HEAD) == (lax.broadcasted_iota(jnp.int32, s.shape, 1) // HEAD)
        s = jnp.where(same, s, -1e30)
        p = jnp.exp(s - jnp.max(s, axis=1, keepdims=True))
        p = p * (1.0 / jnp.sum(p, axis=1, keepdims=True))
        for k in range(GROUP // LANE):
            pw[m, 2 * i + k, 0:GROUP, :] = p[:, k * LANE : (k + 1) * LANE]
        zz[m, 1, :, cols[0]] = dot(v, p.astype(BF), 1, 1).astype(BF)
        return carry

    lax.fori_loop(0, NGROUP, unit, 0, unroll=True)


def channel_backward(m, qkv, pw, T, rr, msk):
    def unit(i, carry):
        cols = group_slices(i)
        mask = msk[m][:, :1]
        q = qkv[m, :, cols[0]].astype(BF)
        k = (qkv[m, :, cols[1]] * mask).astype(BF)
        v = qkv[m, :, cols[2]].astype(BF)
        g = T[:, cols[0]].astype(BF)
        p = jnp.concatenate([pw[m, 2 * i + k, 0:GROUP, :] for k in range(GROUP // LANE)], axis=1)
        dp = dot(g, v, 0, 0)
        ds = (p * (dp - jnp.sum(p * dp, axis=1, keepdims=True))).astype(BF)
        rr[m, 0, :, cols[0]] = (dot(k, ds, 1, 1) * SCALE).astype(BF)
        rr[m, 0, :, cols[1]] = (dot(q, ds) * (SCALE * mask)).astype(BF)
        rr[m, 0, :, cols[2]] = (dot(g, p.astype(BF))).astype(BF)
        return carry

    lax.fori_loop(0, NGROUP, unit, 0, unroll=True)


RING = 8
COLS = FF // RING
WIDE = FF // 12 * 8 // RING
REST = FF // 3 // RING
THIRD = FF // 3 * 2
LENT = RING * 7 // 8
EARLY = 2


def relay_kernel(
    wrows, wcols, img, cot, kern, bias, gain, move, first, second,
    act, ing, out1, out2, outs,
    kern_in, line_in, rows_in, cols_in, isem, wf, w2, pr, msk, flat, ubuf, gin, gout, zz, xh, rs, qkv, ab, rr, pw, U, C, T, sgp, sgs, sgm,
    rL, rR, rA, rG, buf, acc, going, got,
    wl, ws, wr, pl_, usem, gsem, us, gs, ss, rsem, es, er, sgsem, ssem, rcem, osem, sms, smr, xs, xr, ys, yr, bs, br, hs, hr, free,
):
    n = RING
    s = lax.axis_index("section")
    dp = lax.axis_index("dp")
    stage, c = s // 2, lax.rem(s, 2)
    mate = (dp, stage * 2 + (1 - c))
    opposite = (dp, (1 - stage) * 2 + c)
    diagonal = (dp, 3 - s)
    lender, helper = s == 1, s == 2
    early = stage == 0

    spot = lax.rem(dp, n)
    base = dp - spot
    me = jnp.where(lax.rem(spot, 2) == 0, spot // 2, n - 1 - spot // 2)

    def place(pos):
        pos = lax.rem(pos + 2 * n, n)
        return (base + jnp.where(pos < n // 2, 2 * pos, 2 * (n - 1 - pos) + 1), s)

    nexts = (place(me + 1), place(me - 1))
    rounds = n.bit_length() - 1
    partners = []
    for r in range(rounds):
        bit = 1 << r
        partners.append((jnp.where(lax.rem(spot // bit, 2) == 0, dp + bit, dp - bit), s))

    barrier = pltpu.get_barrier_semaphore()
    peers = [mate, opposite, diagonal, *nexts, *partners]
    for peer in peers:
        pl.semaphore_signal(barrier, inc=1, device_id=peer, device_id_type=MESH)

    def remote(src, dst, send, recv, peer):
        return pltpu.make_async_remote_copy(
            src_ref=src, dst_ref=dst, send_sem=send, recv_sem=recv, device_id=peer, device_id_type=MESH
        )

    half = second.shape[0]

    def group_part(group, part):
        cols = pl.ds(pl.multiple_of(part * D + group * GROUP, LANE), GROUP)
        return first.at[:, cols], wf.at[0, :, cols]

    def wait_group(group):
        for part in range(3):
            src, dst = group_part(group, part)
            i = group * 3 + part

            @pl.when(c == 0)
            def _():
                pltpu.make_async_copy(src, dst, wl.at[i]).wait()

            @pl.when(c == 1)
            def _():
                remote(src, dst, ws.at[i], wr.at[i], mate).wait_recv()

    def weight_parts(k):
        parts = []
        if k == 0:
            for group in range(NGROUP):
                for part in range(3):
                    parts.append(group_part(group, part))
            cols = pl.ds(3 * D, D)
            parts.append((first.at[:, cols], wf.at[k, :, cols]))
        else:
            for i in range(3):
                cols = pl.ds(i * (FF // 3), FF // 3)
                parts.append((first.at[:, cols], wf.at[k, :, cols]))
        third = half // 3
        for i in range(3):
            rows = pl.ds(i * third, third)
            parts.append((second.at[rows, :], w2.at[pl.ds(k * half + i * third, third), :]))
        return parts

    names = (
        [f"qkv{group}" for group in range(NGROUP) for _ in range(3)] + ["out"] + [f"low{i}" for i in range(3)],
        ["in"] * 3 + [f"high{i}" for i in range(3)],
    )

    def weight_copies(k):
        local = [pltpu.make_async_copy(a, b, wl.at[i]) for i, (a, b) in enumerate(weight_parts(k))]
        sent = [remote(a, b, ws.at[i], wr.at[i], mate) for i, (a, b) in enumerate(weight_parts(k))]
        return local, sent

    def params_copy(k):
        return remote(pr.at[k], pr.at[k], ws.at[13], wr.at[13], mate)

    own = flat.at[1]
    small_inputs = [
        pltpu.make_async_copy(a, b, isem.at[i])
        for i, (a, b) in enumerate(
            ((kern, kern_in), (bias, line_in.at[0]), (gain, line_in.at[1]), (move, line_in.at[2]), (wrows, rows_in), (wcols, cols_in))
        )
    ]
    for copy in small_inputs:
        copy.start()
    img_in = pltpu.make_async_copy(img, own, isem.at[6])
    cot_in = pltpu.make_async_copy(cot, own, isem.at[6])

    @pl.when(early)
    def _():
        img_in.start()

    for k in range(2):

        @pl.when(c == k)
        def _():
            for copy in weight_copies(k)[0]:
                copy.start()

    pl.semaphore_wait(barrier, len(peers))
    for k in range(2):

        @pl.when(c == k)
        def _():
            for copy in weight_copies(k)[1]:
                copy.start()

    for copy in small_inputs:
        copy.wait()
    pr[c, 0:9, :] = kern_in[...].astype(F32)
    for i in range(3):
        pr[c, 9 + i : 10 + i, :] = line_in[i].astype(F32)
    params_copy(c).start()

    def wait_weights(*wanted):
        for k in range(2):

            @pl.when(c == k)
            def _():
                for name, copy in zip(names[k], weight_copies(k)[0]):
                    if name in wanted:
                        copy.wait()
                for name, copy in zip(names[1 - k], weight_copies(1 - k)[1]):
                    if name in wanted:
                        copy.wait_recv()

    def wait_params(k):
        @pl.when(c != k)
        def _():
            params_copy(k).wait_recv()

    raw = flat.at[0]
    img_out = remote(img, raw, pl_.at[0], pl_.at[1], opposite)
    cot_out = remote(cot, raw, pl_.at[0], pl_.at[1], opposite)

    def pad(src, dst):
        blank = jnp.zeros((CELL - WIN, D), F32)
        for r in range(GRID):
            line = src[r].astype(F32)
            for wc in range(SIDE):
                cells = jnp.concatenate([line[wc * WIN : (wc + 1) * WIN], blank], axis=0)
                C[pl.ds(wc * HALF + r * CELL, CELL), :] = cells
        dst[...] = C[...].astype(BF)

    def unpad(dst):
        for r in range(GRID):
            sides = [C[pl.ds(wc * HALF + r * CELL, CELL), :][:WIN] for wc in range(SIDE)]
            dst[r] = jnp.concatenate(sides, axis=0).astype(BF)

    @pl.when(early)
    def _():
        cot_out.start()
        img_in.wait()
        pad(own, ubuf.at[0, 0])

    @pl.when(jnp.logical_not(early))
    def _():
        img_out.start()
        cot_in.start()
        cot_in.wait()
        pad(own, gin.at[1])

    index = lax.broadcasted_iota(jnp.int32, (ROWS, LANE), 0)
    cell = lax.rem(index, CELL)
    row = lax.rem(index, HALF) // CELL
    column = (index // HALF) * WIN + cell
    for m in range(2):
        inside = (row < WIN * rows_in[c + 2 * m]) & (column < WIN * cols_in[c + 2 * m]) & (cell < WIN)
        msk[m] = jnp.where(inside, 1.0, 0.0)

    @pl.when(jnp.logical_not(early))
    def _():
        cot_out.wait_recv()
        pad(raw, gin.at[0])
        for m in range(2):
            for l in range(D // LANE):
                cols = pl.ds(l * LANE, LANE)
                gin[m, :, cols] = (gin[m, :, cols].astype(F32) * msk[m]).astype(BF)

    for wc in range(SIDE):
        U[wc, 0] = jnp.zeros((CELL, D), F32)
        U[wc, GRID + 1] = jnp.zeros((CELL, D), F32)
    sgp[...] = jnp.zeros(sgp.shape, F32)

    def hop(m, dst, send, recv):
        sides = [pl.ds(i * D // 2, D // 2) for i in range(2)]
        return [
            remote(gout.at[m, :, cols], dst.at[:, cols], send.at[m, i], recv.at[m, i], opposite)
            for i, cols in enumerate(sides)
        ]

    def u_hop(m):
        return hop(m, ubuf.at[0, m], us, usem)

    def g_hop(m):
        return hop(m, gin.at[m], gs, gsem)

    def factor_copies(k, m):
        if k == 0:
            parts = [
                ("F", zz.at[m, 0], rL.at[m, 0]),
                ("F", zz.at[m, 1], rL.at[m, 1]),
                ("G", rr.at[m, 0, :, pl.ds(3 * D, D)], rR.at[m, :, pl.ds(3 * D, D)]),
                ("A", rr.at[m, 0, :, pl.ds(0, 3 * D)], rR.at[m, :, pl.ds(0, 3 * D)]),
            ]
        else:
            parts = [
                ("X0", zz.at[m, 2], rL.at[m, 0]),
                ("M", gin.at[m], rG.at[m]),
            ]
            for i, cols in enumerate((pl.ds(0, FF // 3 * 2), pl.ds(FF // 3 * 2, FF // 3))):
                parts.append((f"X{i}", ab.at[m, :, cols], rA.at[m, :, cols]))
                parts.append((f"H{i}", rr.at[m, 1, :, cols], rR.at[m, :, cols]))
        return [(w, remote(a, b, ss.at[m, i], rsem.at[m, i], mate)) for i, (w, a, b) in enumerate(parts)]

    def start_factors(m, which):
        for k in range(2):

            @pl.when(c != k)
            def _():
                for when, copy in factor_copies(k, m):
                    if when == which:
                        copy.start()

    def wait_factors(which):
        for k in range(2):

            @pl.when(c == k)
            def _():
                for m in range(2):
                    for when, copy in factor_copies(k, m):
                        if when[0] in which:
                            copy.wait_recv()

    def shard(k):
        return lax.rem(k + 4 * n, n)

    def sign(h):
        return 1 if h == 0 else -1

    def home(h, t):
        return shard(me + sign(h) - sign(h) * t)

    def products(terms):
        total = None
        for a, b in terms:
            part = dot(a[...], b[...], 0, 0)
            total = part if total is None else total + part
        return total

    def tile(sub, h, j):
        side = pl.ds(h * COLS, COLS)
        if sub in (0, 4):
            rows = first_rows(sub, h)
            last = jnp.where(j >= (3 * n) // 4, 1, 0)
            own = jnp.where(c == 1, 2, last)
            other = jnp.where(c == 1, 0, last)
            cols = lanes(j, COLS)
            terms = [(zz.at[m, own, :, rows], rr.at[m, c, :, cols]) for m in range(2)]
            terms += [(rL.at[m, other, :, rows], rR.at[m, :, cols]) for m in range(2)]
        elif sub == 3:
            cols = [pl.ds(pl.multiple_of(i * LENT * REST + j * REST, LANE), REST) for i in range(2)]
            terms = [(rA.at[m, :, cols[0]], rG.at[m, :, side]) for m in range(2)]
            terms += [(rA.at[m, :, cols[1]], gout.at[m, :, side]) for m in range(2)]
        else:
            cols = lanes(j, WIDE) if sub == 1 else pl.ds(pl.multiple_of(THIRD + j * REST, LANE), REST)
            terms = [(ab.at[m, :, cols], gin.at[m, :, side]) for m in range(2)]
            terms += [(rA.at[m, :, cols], rG.at[m, :, side]) for m in range(2)]
        return products(terms)

    sizes = (COLS // 3 * 2, WIDE, REST, REST, COLS // 3)
    starts = (0, COLS, COLS + WIDE, COLS + WIDE, COLS // 3 * 2)
    parts = [pl.ds(start, size) for start, size in zip(starts, sizes)]
    subs = range(len(sizes))
    odd = c == 1
    active = (None, odd, odd, helper, None)

    def where_live(sub, h, j, run):
        if sub == 2:
            pl.when(jnp.logical_not(lender) | (j >= LENT - h))(run)
        elif sub == 3:
            pl.when(j < LENT - h)(run)
        else:
            run()

    def first_rows(sub, h):
        return pl.ds(h * COLS + (0 if sub == 0 else sizes[0]), sizes[sub])

    def where_active(sub, run):
        if active[sub] is None:
            run()
        else:
            pl.when(active[sub])(run)


    def gathered(sub, h, j):
        if sub in (0, 4):
            return wf.at[0, first_rows(sub, h), lanes(j, COLS)]
        first_row = 0 if sub == 1 else THIRD
        return w2.at[pl.ds(pl.multiple_of(first_row + j * sizes[sub], 16), sizes[sub]), pl.ds(h * COLS, COLS)]

    def scatter(h, t, sub):
        src, dst = buf.at[h, t, parts[sub], :], buf.at[h, t + 1, parts[sub], :]
        return remote(src, dst, ssem.at[h, t, sub], rcem.at[h, t + 1, sub], nexts[h])

    def spread(h, t, sub, j):
        ref = gathered(sub, h, j)
        return remote(ref, ref, ssem.at[h, n - 1 + t, sub], rcem.at[h, n + t, sub], nexts[h])

    half_shards = n * 3 // 4

    def write(h, j, sub):
        src, side = gathered(sub, h, j), pl.ds(h * COLS, COLS)
        if sub in (0, 4):
            dst = out1.at[first_rows(sub, h), lanes(j, COLS)]
        elif sub == 1:
            dst = out2.at[pl.ds(pl.multiple_of((j - half_shards) * WIDE, 16), WIDE), side]
        else:
            dst = out2.at[pl.ds(pl.multiple_of(THIRD - FF // 2 + j * REST, 16), REST), side]
        if sub == 3:
            return remote(src, dst, bs.at[h, j], br.at[h, j], diagonal)
        return pltpu.make_async_copy(src, dst, osem.at[h, j, sub])

    def hand_over(h, j):
        dst = out2.at[pl.ds(pl.multiple_of(j * WIDE, 16), WIDE), pl.ds(h * COLS, COLS)]
        return remote(gathered(1, h, j), dst, hs.at[h, j], hr.at[h, j], mate)

    def deliver(h, j, sub):
        if sub == 1:

            @pl.when(j < half_shards)
            def _():
                hand_over(h, j).start()

            @pl.when(j >= half_shards)
            def _():
                write(h, j, sub).start()

        else:
            write(h, j, sub).start()

    def lend(m):
        cols, there = pl.ds(THIRD, LENT * REST), [rA.at[m, :, pl.ds(i * LENT * REST, LENT * REST)] for i in range(2)]
        return (
            remote(ab.at[m, :, cols], there[0], xs.at[m], xr.at[m], diagonal),
            remote(rA.at[m, :, cols], there[1], xs.at[2 + m], xr.at[2 + m], diagonal),
        )

    def share(m):
        return remote(gout.at[m], rG.at[m], ys.at[m], yr.at[m], mate)

    def reduce_event(sub, h, e):
        j = shard(me - sign(h) * e)

        @pl.when(e == n - 1)
        def _():
            pl.semaphore_wait(free.at[h, sub], 1)

        def run():
            total = tile(sub, h, j)

            @pl.when(e == 0)
            def _():
                buf[h, 0, parts[sub], :] = total.astype(BF)
                scatter(h, 0, sub).start()

            @pl.when((e > 0) & (e < n - 1))
            def _():
                scatter(h, e - 1, sub).wait_recv()
                buf[h, e, parts[sub], :] = (total + buf[h, e, parts[sub], :].astype(F32)).astype(BF)
                scatter(h, e, sub).start()

            @pl.when(e == n - 1)
            def _():
                scatter(h, n - 2, sub).wait_recv()
                gathered(sub, h, j)[...] = (total + buf[h, n - 1, parts[sub], :].astype(F32)).astype(BF)
                spread(h, 0, sub, j).start()
                deliver(h, j, sub)

        where_live(sub, h, j, run)

    def event(sub, e):
        for h in range(2):

            @pl.when(e < n)
            def _():
                reduce_event(sub, h, e)

            @pl.when((e >= n) & (e < 2 * n - 1))
            def _():
                t = e - (n - 1)
                j = home(h, t)

                def run():
                    spread(h, t - 1, sub, j).wait_recv()

                    @pl.when(t < n - 1)
                    def _():
                        spread(h, t, sub, j).start()

                    deliver(h, j, sub)

                where_live(sub, h, j, run)

    def early_event(e, which):
        @pl.when(odd)
        def _():
            for sub in which:
                where_active(sub, lambda: event(sub, e))

    def small(r):
        return remote(going.at[r], got.at[r], sms.at[r], smr.at[r], partners[r])

    def mlp(m, order, wait):
        total, before, last = C[...], None, None
        for t in order:
            cols = pl.ds(t * FTILE, FTILE)
            h = dot(zz[m, 2], wf[1, :, cols])
            if last is not None:
                wait(last)
                total = total + dot(before, w2[pl.ds(last * FTILE, FTILE), :])
            a, d = gelu_parts(h)
            before, last = a.astype(BF), t
            ab[m, :, cols] = before
            rr[m, 1, :, cols] = d.astype(BF)
            if t == FF // FTILE * 2 // 3 - 1 and order == range(FF // FTILE):
                start_factors(m, "X0")
        wait(last)
        total = total + dot(before, w2[pl.ds(last * FTILE, FTILE), :])
        gout[jnp.where(early, m, 2 + m)] = total.astype(BF)

        @pl.when(early)
        def _():
            for copy in u_hop(m):
                copy.start()

    def give_results(m):
        @pl.when(early)
        def _():
            C[...] = gout[m].astype(F32)

        @pl.when(jnp.logical_not(early))
        def _():
            for l in range(D // LANE):
                cols = pl.ds(l * LANE, LANE)
                C[:, cols] = gout[2 + m, :, cols].astype(F32) * msk[m]

        unpad(flat.at[m])

        @pl.when(early & (m == 0))
        def _():
            pltpu.make_async_copy(flat.at[0], ing, es.at[1]).start()

        @pl.when(early & (m == 1))
        def _():
            remote(flat.at[1], ing, es.at[1], er.at[1], opposite).start()

        @pl.when(jnp.logical_not(early) & (m == 0))
        def _():
            remote(flat.at[0], act, es.at[0], er.at[0], opposite).start()

        @pl.when(jnp.logical_not(early) & (m == 1))
        def _():
            pltpu.make_async_copy(flat.at[1], act, es.at[0]).start()

    def forward(m, p):
        @pl.when(jnp.logical_not(early))
        def _():
            for copy in u_hop(m):
                copy.wait_recv()

        @pl.when(early & (m == 1))
        def _():
            img_out.wait_recv()
            pad(raw, ubuf.at[0, 1])

        once = p == 0
        starting = early & once

        @pl.when(once)
        def _():
            wait_params(0)

        @pl.when(once & jnp.logical_not(early))
        def _():
            wait_params(1)
            wait_weights(*set(names[0] + names[1]))

        front_forward(0, m, ubuf, msk, pr, U, C, zz, xh, rs)

        @pl.when(early)
        def _():
            def head_group(group, carry):
                @pl.when(once)
                def _():
                    wait_group(group)

                for part in range(3):
                    cols = pl.ds(pl.multiple_of(part * D + group * GROUP, LANE), GROUP)
                    qkv[m, :, cols] = dot(zz[m, 0], wf[0, :, cols])
                window_forward(m, qkv, pw, T, group)
                return carry

            lax.fori_loop(0, NGROUP, head_group, 0)
            zz[m, 1] = T[...].astype(BF)

        @pl.when(starting)
        def _():
            wait_weights("out")
            wait_params(1)

        @pl.when(jnp.logical_not(early))
        def _():
            qkv[m] = dot(zz[m, 0], wf[0, :, pl.ds(0, 3 * D)])

        @pl.when(jnp.logical_not(early))
        def _():
            channel_forward(m, qkv, pw, zz, msk)

        ubuf[1, m] = (C[...] + dot(zz[m, 1], wf[0, :, pl.ds(3 * D, D)])).astype(BF)

        front_forward(1, m, ubuf, msk, pr, U, C, zz, xh, rs)

        @pl.when(starting)
        def _():
            wait_weights("in")
            order = [i + 3 * k for i in range(3) for k in range(2)]
            mlp(m, order, lambda t: wait_weights(f"low{t}" if t < 3 else f"high{t - 3}"))
            start_factors(m, "X0")

        @pl.when(jnp.logical_not(starting))
        def _():
            mlp(m, range(FF // FTILE), lambda t: None)

        start_factors(m, "F")
        start_factors(m, "X1")

        @pl.when(early & (m == 1))
        def _():
            wait_factors("FX")

        @pl.when(lender & (m == 1))
        def _():
            for i in range(2):
                for copy in lend(i):
                    copy.start()

    def backward(m):
        @pl.when(early)
        def _():
            for copy in g_hop(m):
                copy.wait_recv()
            start_factors(m, "M")

        for t in range(FF // FTILE):
            cols = pl.ds(t * FTILE, FTILE)
            da = dot(gin[m], w2[cols, :], 1, 1)
            rr[m, 1, :, cols] = (da * rr[m, 1, :, cols].astype(F32)).astype(BF)
            if t == FF // FTILE * 2 // 3 - 1:
                start_factors(m, "H0")

        start_factors(m, "H1")

        @pl.when(m == 1)
        def _():
            @pl.when(jnp.logical_not(early))
            def _():
                wait_factors("FX")

            wait_factors("M")
            early_event(0, (1, 2))

        T[...] = dot(rr[m, 1], wf[1], 1, 1)

        @pl.when(m == 1)
        def _():
            wait_factors("H")
            early_event(0, (0, 4))

        last = pl.ds(3 * D, D)

        @pl.when(early)
        def _():
            for copy in u_hop(m):
                copy.wait_send()

        def tail_lanes(i):
            return rr.at[m, 0, :, pl.ds(pl.multiple_of(3 * D + i * LANE, LANE), LANE)]

        def nothing(half):
            pass

        front_backward(1, m, msk, pr, U, T, lambda i: gin.at[m, :, lanes(i)], xh, rs, sgp, tail_lanes, nothing)

        start_factors(m, "G")
        T[...] = dot(rr[m, 0, :, last], wf[0, :, last], 1, 1)

        @pl.when(early)
        def _():
            window_backward(m, qkv, pw, T)
            for i in range(3):
                cols = pl.ds(i * D, D)
                rr[m, 0, :, cols] = qkv[m, :, cols].astype(BF)

        @pl.when(jnp.logical_not(early))
        def _():
            channel_backward(m, qkv, pw, T, rr, msk)

        start_factors(m, "A")

        @pl.when(m == 1)
        def _():
            early_event(1, (1, 2, 0, 4))

        T[...] = dot(rr[m, 0, :, pl.ds(0, 3 * D)], wf[0, :, pl.ds(0, 3 * D)], 1, 1)
        def send_half(half):
            @pl.when(jnp.logical_not(early))
            def _():
                g_hop(m)[half].start()

        front_backward(
            0, m, msk, pr, U, T, tail_lanes, xh, rs, sgp, lambda i: gout.at[m, :, lanes(i)], send_half
        )

        @pl.when(s == 3)
        def _():
            share(m).start()

    @pl.when(jnp.logical_not(early))
    def _():
        for m in range(2):
            start_factors(m, "M")

    def phase(p, carry):
        m = jnp.where(early, lax.rem(p, 2), p // 2)
        ahead = jnp.where(early, p < 2, lax.rem(p, 2) == 0)

        @pl.when(ahead)
        def _():
            forward(m, p)

        @pl.when(jnp.logical_not(ahead))
        def _():
            backward(m)

        return carry

    lax.fori_loop(0, 4, phase, 0)

    for h in range(2):
        for sub in subs:

            def ready():
                pl.semaphore_signal(free.at[h, sub], inc=1, device_id=nexts[1 - h], device_id_type=MESH)

            where_active(sub, ready)

    give = remote(sgs.at[1 - c], sgm, sgsem.at[0], sgsem.at[1], mate)

    def small_sums():
        for sec in range(2):
            for j in range(12):
                sgs[sec, j : j + 1, :] = jnp.sum(sgp[sec, j], axis=0, keepdims=True)
            sgs[sec, 12:16, :] = jnp.zeros((4, D), F32)
        give.start()

    wait_factors("GA")

    @pl.when(helper)
    def _():
        for m in range(2):
            for copy in lend(m):
                copy.wait_recv()
            share(m).wait_recv()

    def ring_step(t, carry):
        for sub in (0, 4):
            event(sub, t + jnp.where(odd, EARLY, 0))
        where_active(1, lambda: event(1, t + EARLY))
        where_active(2, lambda: event(2, t + EARLY))
        where_active(3, lambda: event(3, t))
        @pl.when((t >= 1) & (t < 5))
        def _():
            front_sums((t - 1) // 2, lax.rem(t - 1, 2), ubuf, msk, U, xh, sgp)

        pl.when(t == 5)(small_sums)

        @pl.when((t >= 6) & (t < 8))
        def _():
            give_results(t - 6)

        for r in range(rounds + 1):

            @pl.when(t == 6 + 2 * r)
            def _():
                if r == 0:
                    give.wait_recv()
                    acc[0] = sgs[c] + sgm[...]
                else:
                    small(r - 1).wait_recv()
                    acc[r] = going[r - 1].astype(F32) + got[r - 1].astype(F32)
                if r < rounds:
                    going[r] = acc[r].astype(BF)
                    small(r).start()

        return carry

    lax.fori_loop(0, 2 * n - 1, ring_step, 0)
    outs[...] = acc[rounds]

    for k in range(2):

        @pl.when(c == k)
        def _():
            for copy in weight_copies(k)[1]:
                copy.wait_send()
            params_copy(k).wait_send()
            for m in range(2):
                for _when, copy in factor_copies(1 - k, m):
                    copy.wait_send()

    give.wait_send()
    for r in range(rounds):
        small(r).wait_send()

    def drain(t, carry):
        for h in range(2):
            for sub in subs:

                def sent():
                    where_live(sub, h, shard(me - sign(h) * t), lambda: scatter(h, t, sub).wait_send())
                    where_live(sub, h, home(h, t), lambda: spread(h, t, sub, home(h, t)).wait_send())

                where_active(sub, sent)

        return carry

    lax.fori_loop(0, n - 1, drain, 0)

    def written(j, carry):
        for h in range(2):
            write(h, j, 0).wait()
            write(h, j, 4).wait()

            @pl.when(odd)
            def _():
                where_live(2, h, j, lambda: write(h, j, 2).wait())

                @pl.when(j < half_shards)
                def _():
                    hand_over(h, j).wait_send()

                @pl.when(j >= half_shards)
                def _():
                    write(h, j, 1).wait()

            @pl.when(jnp.logical_not(odd) & (j < half_shards))
            def _():
                hand_over(h, j).wait_recv()

            @pl.when(helper & (j < LENT - h))
            def _():
                write(h, j, 3).wait_send()

            @pl.when(lender & (j < LENT - h))
            def _():
                write(h, j, 3).wait_recv()

        return carry

    lax.fori_loop(0, n, written, 0)

    @pl.when(lender)
    def _():
        for m in range(2):
            for copy in lend(m):
                copy.wait_send()

    @pl.when(s == 3)
    def _():
        for m in range(2):
            share(m).wait_send()

    @pl.when(early)
    def _():
        cot_out.wait_send()
        pltpu.make_async_copy(flat.at[0], ing, es.at[1]).wait()
        remote(flat.at[1], ing, es.at[1], er.at[1], opposite).wait_send()
        remote(flat.at[0], act, es.at[0], er.at[0], opposite).wait_recv()

    @pl.when(jnp.logical_not(early))
    def _():
        img_out.wait_send()
        for m in range(2):
            for copy in g_hop(m):
                copy.wait_send()
        remote(flat.at[0], act, es.at[0], er.at[0], opposite).wait_send()
        pltpu.make_async_copy(flat.at[1], act, es.at[0]).wait()
        remote(flat.at[1], ing, es.at[1], er.at[1], opposite).wait_recv()


def relay(wrows, wcols, img, cot, kern, bias, gain, move, first, second):
    shape = jax.ShapeDtypeStruct
    vmem = pl.BlockSpec(memory_space=pltpu.VMEM)
    anywhere = pl.BlockSpec(memory_space=pl.ANY)
    dma = pltpu.SemaphoreType.DMA
    image = (ROWS, D)
    slot = img.shape
    rounds = RING.bit_length() - 1
    return pl.pallas_call(
        relay_kernel,
        out_shape=[
            shape(slot, BF),
            shape(slot, BF),
            shape((D, FF), BF),
            shape((FF // 2, D), BF),
            shape((16, D), F32),
        ],
        in_specs=[anywhere] * 10,
        out_specs=[anywhere] * 4 + [vmem],
        scratch_shapes=[
            pltpu.VMEM(kern.shape, BF),
            pltpu.VMEM((3,) + bias.shape, BF),
            pltpu.SMEM(wrows.shape, jnp.int32),
            pltpu.SMEM(wcols.shape, jnp.int32),
            dma((7,)),
            pltpu.VMEM((2, D, FF), BF),
            pltpu.VMEM((FF, D), BF),
            pltpu.VMEM((2, 16, D), F32),
            pltpu.VMEM((2, ROWS, LANE), F32),
            pltpu.VMEM((2,) + slot, BF),
            pltpu.VMEM((2, 2) + image, BF),
            pltpu.VMEM((2,) + image, BF),
            pltpu.VMEM((4,) + image, BF),
            pltpu.VMEM((2, 3) + image, BF),
            pltpu.VMEM((2, 2) + image, BF),
            pltpu.VMEM((2, 2, ROWS, LANE), F32),
            pltpu.VMEM((2, ROWS, 3 * D), F32),
            pltpu.VMEM((2, ROWS, FF), BF),
            pltpu.VMEM((2, 2, ROWS, FF), BF),
            pltpu.VMEM((2, UNITS, PACK * WROWS, LANE), F32),
            pltpu.VMEM((SIDE, GRID + 2, CELL, D), F32),
            pltpu.VMEM(image, F32),
            pltpu.VMEM(image, F32),
            pltpu.VMEM((2, 12, CELL, D), F32),
            pltpu.VMEM((2, 16, D), F32),
            pltpu.VMEM((16, D), F32),
            pltpu.VMEM((2, 2) + image, BF),
            pltpu.VMEM((2, ROWS, FF), BF),
            pltpu.VMEM((2, ROWS, FF), BF),
            pltpu.VMEM((2,) + image, BF),
            pltpu.VMEM((2, RING, COLS + WIDE + REST, COLS), BF),
            pltpu.VMEM((rounds + 1, 16, D), F32),
            pltpu.VMEM((rounds, 16, D), BF),
            pltpu.VMEM((rounds, 16, D), BF),
            dma((14,)),
            dma((14,)),
            dma((14,)),
            dma((2,)),
            dma((2, 2)),
            dma((2, 2)),
            dma((2, 2)),
            dma((2, 2)),
            dma((2, 8)),
            dma((2, 8)),
            dma((2,)),
            dma((2,)),
            dma((2,)),
            dma((2, 2 * RING, 5)),
            dma((2, 2 * RING, 5)),
            dma((2, RING, 5)),
            dma((rounds,)),
            dma((rounds,)),
            dma((4,)),
            dma((4,)),
            dma((2,)),
            dma((2,)),
            dma((2, RING)),
            dma((2, RING)),
            dma((2, RING)),
            dma((2, RING)),
            pltpu.SemaphoreType.REGULAR((2, 5)),
        ],
        name="relay",
        compiler_params=pltpu.CompilerParams(
            collective_id=1, has_side_effects=True, vmem_limit_bytes=63 * 2**20
        ),
    )(wrows, wcols, img, cot, kern, bias, gain, move, first, second)


def finish_kernel(
    out1, out2, act, ing, outs, first, second, acts, ings, kern, bias, gain, move,
    raw1, raw2, full1, full2, acted, graded, wide, small, kernels, rsem, wsem,
):
    steps = rsem.shape[0] - 3

    loads = [
        pltpu.make_async_copy(act, acted, rsem.at[steps]),
        pltpu.make_async_copy(ing, graded, rsem.at[steps + 1]),
        pltpu.make_async_copy(outs, small, rsem.at[steps + 2]),
    ]
    for copy in loads:
        copy.start()
    reads, writes = [], []
    for i in range(steps):
        pair = ((out1, raw1, full1, first), (out2, raw2, full2, second))[i % 2]
        src, raw, full, dst = pair
        half = steps // 2
        rows = pl.ds(i // 2 * (src.shape[0] // half), src.shape[0] // half)
        reads.append((pltpu.make_async_copy(src.at[rows, :], raw.at[rows, :], rsem.at[i]), raw, full, rows))
        writes.append(pltpu.make_async_copy(full.at[rows, :], dst.at[rows, :], wsem.at[i]))
    for copy, *_ in reads:
        copy.start()
    for (copy, raw, full, rows), back in zip(reads, writes):
        copy.wait()
        full[rows, :] = raw[rows, :].astype(F32)
        back.start()
    for copy in loads:
        copy.wait()
    for k in range(9):
        kernels[k] = small[k : k + 1, :]
    for r in range(GRID):
        line = graded[r].astype(F32)
        for k in range(GRID):
            wide[r, k] = line[k : k + 1, :]
    last = [
        pltpu.make_async_copy(acted, acts, wsem.at[steps]),
        pltpu.make_async_copy(wide, ings, wsem.at[steps + 1]),
        pltpu.make_async_copy(kernels, kern, wsem.at[steps + 2]),
    ]
    for i, dst in enumerate((bias, gain, move)):
        last.append(pltpu.make_async_copy(small.at[pl.ds(9 + i, 1), :], dst, wsem.at[steps + 3 + i]))
    for copy in last:
        copy.start()
    for copy in writes + last:
        copy.wait()


def finish(out1, out2, act, ing, outs):
    shape = jax.ShapeDtypeStruct
    slot = act.shape
    anywhere = pl.BlockSpec(memory_space=pl.ANY)
    line = (1, D)
    spread = slot[:2] + line
    steps = 8
    return pl.pallas_call(
        finish_kernel,
        out_shape=[
            shape(out1.shape, F32),
            shape(out2.shape, F32),
            shape(slot, BF),
            shape(spread, F32),
            shape((9,) + line, F32),
            shape(line, F32),
            shape(line, F32),
            shape(line, F32),
        ],
        in_specs=[anywhere] * 5,
        out_specs=[anywhere] * 8,
        scratch_shapes=[
            pltpu.VMEM(out1.shape, out1.dtype),
            pltpu.VMEM(out2.shape, out2.dtype),
            pltpu.VMEM(out1.shape, F32),
            pltpu.VMEM(out2.shape, F32),
            pltpu.VMEM(slot, BF),
            pltpu.VMEM(slot, BF),
            pltpu.VMEM(spread, F32),
            pltpu.VMEM(outs.shape, F32),
            pltpu.VMEM((9,) + line, F32),
            pltpu.SemaphoreType.DMA((steps + 3,)),
            pltpu.SemaphoreType.DMA((steps + 6,)),
        ],
        name="finish",
        compiler_params=pltpu.CompilerParams(vmem_limit_bytes=60 * 2**20),
    )(out1, out2, act, ing, outs)


def per_device(
    images, cotangent, window_rows, window_cols, pos_kernel, pos_bias, norm_gain, norm_shift, first_weight, second_weight
):
    act, ing, out1, out2, outs = relay(
        window_rows, window_cols, images[0], cotangent[0], pos_kernel[0], pos_bias, norm_gain, norm_shift,
        first_weight[0], second_weight,
    )
    if lax.axis_size("dp") > RING:
        out1, out2, outs = lax.psum((out1.astype(F32) / RING, out2.astype(F32) / RING, outs / RING), "dp")
    out1, out2, act, ing, kern, bias, gain, move = finish(out1, out2, act, ing, outs)
    return (
        act[None],
        ing.transpose(2, 0, 1, 3),
        out1[None],
        out2,
        kern.transpose(1, 0, 2),
        bias,
        gain,
        move,
    )


def solution(mesh):
    in_specs = (
        P(("dp", "section"), None, None, None),
        P(("dp", "section"), None, None, None),
        P("dp"),
        P("dp"),
        P("section", None, None),
        P("section", None),
        P("section", None),
        P("section", None),
        P("section", None, None),
        P("section", None),
    )
    out_specs = (
        P(("dp", "section"), None, None, None),
        P(("dp", "section"), None, None, None),
        P("section", None, None),
        P("section", None),
        P("section", None, None),
        P("section", None),
        P("section", None),
        P("section", None),
    )
    return jax.shard_map(per_device, mesh=mesh, in_specs=in_specs, out_specs=out_specs, check_vma=False)
```
